32 devices in a mesh: dp: 8 (over z, x), fsdp: 4 (over y, core).
Axes of the slice: x: 2, y: 2, z: 4, core: 2. Of those that a mesh axis runs over, the one named last changes fastest.
Arguments:
- hidden_in: bfloat16 [65536, 256], P(('dp', 'fsdp')), may hold values from -6 to 6
- lengths: int32 [128, 6], P(('dp', 'fsdp')), may hold values from 1 to 256, 512 in all within a row
- grad_out: bfloat16 [65536, 256], P(('dp', 'fsdp')), may hold values from -6 to 6
- attn_weight: bfloat16 [2, 256, 768], P(None, ('dp', 'fsdp')), may hold values from -0.375 to 0.375
- attn_bias: bfloat16 [2, 2, 256], P(None, None, ('dp', 'fsdp')), may hold values from -2 to 2
- out_weight: bfloat16 [2, 256, 256], P(None, ('dp', 'fsdp')), may hold values from -1.5 to 1.5
- ffn_in: bfloat16 [2, 256, 1024], P(None, ('dp', 'fsdp')), may hold values from -0.375 to 0.375
- ffn_in_bias: bfloat16 [2, 1024], P(None, ('dp', 'fsdp')), may hold values from -2 to 2
- ffn_out: bfloat16 [2, 1024, 256], P(None, ('dp', 'fsdp')), may hold values from -0.1875 to 0.1875
- norm_gain: bfloat16 [2, 2, 256], P(None, None, ('dp', 'fsdp')), may hold values from 0.5 to 1.5
- shifts: bfloat16 [2, 4, 256], P(None, None, ('dp', 'fsdp')), may hold values from -2 to 2
Outputs:
- hidden_out: bfloat16 [65536, 256], P(('dp', 'fsdp'))
- grad_in: bfloat16 [65536, 256], P(('dp', 'fsdp'))
- attn_weight_grad: float32 [2, 256, 768], P(None, ('dp', 'fsdp'))
- attn_bias_grad: float32 [2, 2, 256], P(None, None, ('dp', 'fsdp'))
- out_weight_grad: float32 [2, 256, 256], P(None, ('dp', 'fsdp'))
- ffn_in_grad: float32 [2, 256, 1024], P(None, ('dp', 'fsdp'))
- ffn_in_bias_grad: float32 [2, 1024], P(None, ('dp', 'fsdp'))
- ffn_out_grad: float32 [2, 1024, 256], P(None, ('dp', 'fsdp'))
- norm_gain_grad: float32 [2, 2, 256], P(None, None, ('dp', 'fsdp'))
- shifts_grad: float32 [2, 4, 256], P(None, None, ('dp', 'fsdp'))
The draws below stay inside these ranges and needn't reach their ends.
Inputs may be any that keep to these rules, and one draw needn't show every extreme that they name: `lengths`: every row's entries sum to 512 and its largest entry is 256; the last entry is the padding length.
All inputs are finite; a program needn't handle non-finite values.
Results may differ from the reference program's by a relative error of at most 0.014.
Values may be sent and summed in bfloat16 or wider, within the bound.
No kernel may reach another device: no remote copies, remote signals or barrier semaphores. Data moves between devices by JAX's collectives and lax.ppermute only.
A program may use at most 192 MiB of HBM per device.

```python
import math
import jax
import jax.numpy as jnp
import numpy as np
from jax import lax

D = 256
HEADS = 4
HD = 64
FF = 1024
SEQ = 512
SEGS = 6
LAYERS = 2
MOST = 256
ROWS = 128
TOKENS = 65536


def block_levels(key, extent, shards, low, high):
    factor_of, own = 1.0, jax.random.fold_in(key, 6)
    for dim, parts in shards:
        heights = jnp.exp(jax.random.uniform(jax.random.fold_in(own, dim), (parts,), jnp.float32, low / len(shards), high / len(shards)))
        factor_of = factor_of * jnp.repeat(heights, extent[dim] // parts).reshape([-1 if axis == dim else 1 for axis in range(len(extent))])
    return factor_of


def length_profile(count, total, reach, lean):
    loads = [(1 << 20) // math.isqrt(standing ** lean) + 1 for standing in range(2, count + 1)]
    rest, given = total - reach - (count - 1), [1] * (count - 1)
    while rest > 0:
        candidates = [i for i in range(count - 1) if given[i] < reach]
        mass, remaining = sum([loads[i] for i in candidates]), rest
        for i in candidates:
            addition = min(reach - given[i], max(1, remaining * loads[i] // mass), rest)
            given[i] = given[i] + addition
            rest = rest - addition
    return np.array([reach] + given)


def uneven(rng, amount, total, reach, lean):
    if amount == 2:
        one = jax.random.randint(rng, (), max(1, total - reach), min(reach, total - 1) + 1)
        return jnp.stack([one, total - one])
    sizes = jnp.asarray(length_profile(amount, total, reach, lean), jnp.int32)
    twos = (amount - 1) // 2
    source_of, taker = sizes[1:1 + 2 * twos:2], sizes[2:2 + 2 * twos:2]
    slack = jnp.minimum(source_of - 1, reach - taker)
    passed = jax.random.randint(jax.random.fold_in(rng, 1), (twos,), 0, 1 << 20) % (slack + 1)
    sizes = sizes.at[1:1 + 2 * twos:2].set(source_of - passed).at[2:2 + 2 * twos:2].set(taker + passed)
    return sizes[jax.random.permutation(jax.random.fold_in(rng, 2), amount)]


def bell_draw(stream_key, extent, scale, limit, cuts=(), held_as=jnp.bfloat16):
    drawn = jax.random.normal(stream_key, extent, jnp.float32) * scale
    if len(cuts) > 0:
        drawn = block_levels(stream_key, extent, cuts, -0.22, 0.18) * drawn
    return jnp.clip(drawn, min=-limit, max=limit).astype(held_as)


def setup_inputs(seed: int = 0) -> dict:
    streams_of = jax.random.split(jax.random.key(seed), 12)
    hidden_in = bell_draw(streams_of[0], (TOKENS, D), 1.0, 6.0, ((0, 32),))
    lengths = jax.vmap(lambda own: uneven(own, SEGS, SEQ, MOST, 1))(jax.random.split(streams_of[1], ROWS)).reshape((ROWS, SEGS)).astype(jnp.int32)
    grad_out = bell_draw(streams_of[2], (TOKENS, D), 1.0, 6.0, ((0, 32),))
    attn_weight = bell_draw(streams_of[3], (LAYERS, D, 3 * D), D ** -0.5, 0.375, ((1, 32),))
    attn_bias = bell_draw(streams_of[4], (LAYERS, 2, D), 0.3, 2.0, ((2, 32),))
    out_weight = bell_draw(streams_of[5], (LAYERS, D, D), (D // 16) ** -0.5, 1.5, ((1, 32),))
    ffn_in = bell_draw(streams_of[6], (LAYERS, D, FF), D ** -0.5, 0.375, ((1, 32),))
    ffn_in_bias = bell_draw(streams_of[7], (LAYERS, FF), 0.3, 2.0, ((1, 32),))
    ffn_out = bell_draw(streams_of[8], (LAYERS, FF, D), FF ** -0.5, 0.1875, ((1, 32),))
    norm_gain = jnp.clip(1.0 + 0.1 * jax.random.normal(streams_of[9], (LAYERS, 2, D), jnp.float32), 0.5, 1.5).astype(jnp.bfloat16)
    shifts = bell_draw(streams_of[10], (LAYERS, 4, D), 0.3, 2.0, ((2, 32),))
    return dict(hidden_in=hidden_in, lengths=lengths, grad_out=grad_out, attn_weight=attn_weight, attn_bias=attn_bias, out_weight=out_weight, ffn_in=ffn_in, ffn_in_bias=ffn_in_bias, ffn_out=ffn_out, norm_gain=norm_gain, shifts=shifts)


@jax.custom_vjp
def low(v):
    return lax.optimization_barrier(v.astype(jnp.bfloat16)).astype(jnp.float32)

@jax.custom_vjp
def low_back(v):
    return v

def low_keep(v):
    return (low(v), None)

def low_pass(kept, grad):
    return (grad,)

def back_keep(v):
    return (v, None)

def back_low(kept, grad):
    return (low(grad),)
low.defvjp(low_keep, low_pass)
low_back.defvjp(back_keep, back_low)
NEGATIVE = -1e+30
EPSILON = 1e-12
HIGHEST = lax.Precision.HIGHEST

def layer_norm(values, gains, offsets):
    centred = values - lax.optimization_barrier(jnp.mean(values, -1, keepdims=True))
    spread = lax.optimization_barrier(jnp.mean(centred * centred, -1, keepdims=True))
    return centred * lax.rsqrt(spread + EPSILON) * gains + offsets

def segment_ids(lengths):
    bounds = jnp.cumsum(lengths, -1).astype(jnp.int32)
    places = lax.iota(jnp.int32, SEQ)
    return lax.optimization_barrier(jnp.sum((places[None, :, None] >= bounds[:, None, :]).astype(jnp.int32), -1)).astype(jnp.int32)

def permitted(segment):
    places = lax.iota(jnp.int32, SEQ)
    shared = segment[:, None] == segment[None, :]
    unpadded = segment[None, :] != SEGS - 1
    return shared & unpadded | (places[:, None] == places[None, :])

def row_attention(packed):
    queries, key_rows, value_rows, segment = packed
    scores = low_back(jnp.einsum('qhd,khd->hqk', queries, key_rows, precision=HIGHEST) * HD ** (-0.5))
    scores = jnp.where(permitted(segment)[None], scores, NEGATIVE)
    highest = lax.optimization_barrier(jnp.max(scores, -1, keepdims=True))
    numerator = jnp.exp(scores - highest)
    probabilities = numerator / lax.optimization_barrier(jnp.sum(numerator, -1, keepdims=True))
    return jnp.einsum('hqk,khd->qhd', low(probabilities), value_rows, precision=HIGHEST)

def encoder_block(current, qkv_matrix, qv_biases, out_matrix, up_matrix, up_bias, down_matrix, gains, offsets, segment):
    current_low = low(current)
    biases = jnp.concatenate([qv_biases[0], jnp.zeros_like(qv_biases[0]), qv_biases[1]])
    projected = low(low_back(jnp.dot(current_low, qkv_matrix, precision=HIGHEST) + biases))
    head_rows = projected.reshape(ROWS, SEQ, 3, HEADS, HD)
    attended = lax.map(jax.checkpoint(row_attention), (head_rows[:, :, 0], head_rows[:, :, 1], head_rows[:, :, 2], segment))
    attended = low(low_back(attended.reshape(TOKENS, D)))
    branch = low_back(jnp.dot(attended, out_matrix, precision=HIGHEST) + offsets[0])
    normed = layer_norm(current + branch, gains[0], offsets[1])
    hidden_pre = low_back(jnp.dot(low(normed), up_matrix, precision=HIGHEST) + up_bias)
    activated = low(jax.nn.gelu(hidden_pre, approximate=False))
    ffn_result = low_back(jnp.dot(activated, down_matrix, precision=HIGHEST) + offsets[2])
    return layer_norm(normed + ffn_result, gains[1], offsets[3])

def reference(hidden_in, lengths, grad_out, attn_weight, attn_bias, out_weight, ffn_in, ffn_in_bias, ffn_out, norm_gain, shifts):
    segment = segment_ids(lengths)
    params = (attn_weight.astype(jnp.float32), attn_bias.astype(jnp.float32), out_weight.astype(jnp.float32), ffn_in.astype(jnp.float32), ffn_in_bias.astype(jnp.float32), ffn_out.astype(jnp.float32), norm_gain.astype(jnp.float32), shifts.astype(jnp.float32))

    def forward(current, qkv_all, bias_all, out_all, up_all, upbias_all, down_all, gain_all, offset_all):
        for layer_index in range(LAYERS):
            current = encoder_block(current, qkv_all[layer_index], bias_all[layer_index], out_all[layer_index], up_all[layer_index], upbias_all[layer_index], down_all[layer_index], gain_all[layer_index], offset_all[layer_index], segment)
        return current
    result, backward = jax.vjp(forward, hidden_in.astype(jnp.float32), *params)
    grads = backward(grad_out.astype(jnp.float32))
    return (result.astype(jnp.bfloat16), grads[0].astype(jnp.bfloat16), grads[1], grads[2], grads[3], grads[4], grads[5], grads[6], grads[7], grads[8])
```

```python
from functools import partial

import jax
import jax.numpy as jnp
from jax import lax
from jax.sharding import PartitionSpec as P

HEADS = 4
HD = 64
SEQ = 512


NEGATIVE = -1e30
EPSILON = 1e-12


def pack_layer(
    qkv_part, bias_part, out_part, up_part, upbias_part, down_part, gain_part, offset_part
):
    rows, width = out_part.shape
    blocks = lambda part: part.reshape(rows, -1, width).transpose(1, 0, 2).reshape(-1, width)
    small = jnp.concatenate([bias_part, gain_part, offset_part])
    small = jnp.pad(small, ((0, 0), (0, width - rows)))
    last = jnp.pad(upbias_part[None], ((0, 7), (0, width - upbias_part.shape[0])))
    return jnp.concatenate(
        [blocks(qkv_part), out_part, blocks(up_part), down_part, small, last]
    )


def unpack_layer(packed, rows, height):
    count, unused, width = packed.shape
    blocks = (
        lambda part: part.reshape(count, -1, rows, width)
        .transpose(0, 2, 1, 3)
        .reshape(count * rows, -1)
    )
    down_at = 8 * rows
    small_at = down_at + height
    small = packed[:, small_at : small_at + 8, :rows].transpose(1, 0, 2).reshape(8, -1)
    return (
        blocks(packed[:, : 3 * rows]),
        small[:2],
        packed[:, 3 * rows : 4 * rows].reshape(-1, width),
        blocks(packed[:, 4 * rows : 8 * rows]),
        packed[:, small_at + 8, :height].reshape(-1),
        packed[:, down_at:small_at].reshape(-1, width),
        small[2:4],
        small[4:8],
    )


def pack_grads(grads, rows, height):
    qkv_grad, bias_grad, out_grad, up_grad, upbias_grad, down_grad, gain_grad, offset_grad = grads
    width = out_grad.shape[1]
    count = width // rows
    blocks = (
        lambda grad: grad.reshape(count, rows, -1, width)
        .transpose(0, 2, 1, 3)
        .reshape(count, -1, width)
    )
    small = jnp.concatenate([bias_grad, gain_grad, offset_grad, upbias_grad.reshape(-1, width)])
    small = jnp.pad(small, ((0, -small.shape[0] % 16), (0, 0)))
    return jnp.concatenate(
        [
            blocks(qkv_grad),
            out_grad.reshape(count, rows, width),
            blocks(up_grad),
            down_grad.reshape(count, height, width),
            jnp.broadcast_to(small, (count,) + small.shape),
        ],
        1,
    )


def unpack_grads(packed, rows, height, place):
    width = packed.shape[1]
    blocks = (
        lambda part: part.reshape(-1, rows, width).transpose(1, 0, 2).reshape(rows, -1)
    )
    down_at = 8 * rows
    small_at = down_at + height
    small = lax.dynamic_slice(packed[small_at : small_at + 8], (0, place * rows), (8, rows))
    last = packed[small_at + 8 : small_at + 8 + (height * width // rows) // width].reshape(-1)
    last = lax.dynamic_slice(last, (place * height,), (height,))
    return (
        blocks(packed[: 3 * rows]),
        small[:2],
        packed[3 * rows : 4 * rows],
        blocks(packed[4 * rows : 8 * rows]),
        last,
        packed[down_at:small_at],
        small[2:4],
        small[4:8],
    )


def partners(size, mask):
    return [(source, source ^ mask) for source in range(size)]


def gather_direct(part, axis):
    size = lax.axis_size(axis)
    pieces = [part] + [lax.ppermute(part, axis, partners(size, mask)) for mask in range(1, size)]
    order = lax.axis_index(axis) ^ jnp.arange(size)
    return jnp.take(jnp.stack(pieces), order, axis=0)


def gather_doubling(part, axis):
    size = lax.axis_size(axis)
    place = lax.axis_index(axis)
    held = part[:, None]
    steps = []
    bit = 1
    while bit < size:
        steps.append(bit)
        bit *= 2
    for stage, bit in enumerate(reversed(steps)):
        other = lax.ppermute(held, axis, partners(size, bit))
        upper = (place & bit) != 0
        low = jnp.where(upper, other, held)
        high = jnp.where(upper, held, other)
        held = jnp.stack([low, high], 1 + stage)
    held = held.reshape((part.shape[0],) + (2,) * len(steps) + part.shape[1:])
    return held


def scatter_halving(parts, axis):
    size = lax.axis_size(axis)
    place = lax.axis_index(axis)
    bit = 1
    held = parts
    while bit < size:
        pairs = held.reshape(held.shape[0] // 2, 2, *held.shape[1:])
        upper = (place // bit) % 2
        keep = lax.dynamic_index_in_dim(pairs, upper, 1, keepdims=False)
        send = lax.dynamic_index_in_dim(pairs, 1 - upper, 1, keepdims=False)
        other = lax.ppermute(send, axis, partners(size, bit))
        held = (keep.astype(jnp.float32) + other.astype(jnp.float32)).astype(parts.dtype)
        bit *= 2
    return held[0]


def scatter_direct(parts, axis):
    size = lax.axis_size(axis)
    place = lax.axis_index(axis)
    total = lax.dynamic_index_in_dim(parts, place, 0, keepdims=False).astype(jnp.float32)
    for mask in range(1, size):
        send = lax.dynamic_index_in_dim(parts, place ^ mask, 0, keepdims=False)
        total = total + lax.ppermute(send, axis, partners(size, mask)).astype(jnp.float32)
    return total


def scatter_exchange(parts, axis):
    other = lax.all_to_all(parts, axis, 0, 0, tiled=True)
    return jnp.sum(other.astype(jnp.float32), 0)


def permitted(lengths):
    bounds = jnp.cumsum(lengths, -1)
    places = lax.iota(jnp.int32, SEQ)
    segment = jnp.sum((places[None, :, None] >= bounds[:, None, :]).astype(jnp.int32), -1)
    shared = segment[:, :, None] == segment[:, None, :]
    unpadded = segment[:, None, :] != lengths.shape[-1] - 1
    diagonal = places[:, None] == places[None, :]
    return shared & unpadded | diagonal[None]


def normalize(values, gains, offsets):
    centred = values - jnp.mean(values, -1, keepdims=True)
    inverse = lax.rsqrt(jnp.mean(centred * centred, -1, keepdims=True) + EPSILON)
    unit = centred * inverse
    return (unit * gains + offsets, unit, inverse)


def normalize_back(cotangent, unit, inverse, gains):
    scaled = cotangent * gains
    return inverse * (
        scaled
        - jnp.mean(scaled, -1, keepdims=True)
        - unit * jnp.mean(scaled * unit, -1, keepdims=True)
    )


def masked_scores(queries, key_rows, allowed_row):
    raw = jnp.einsum(
        "qhd,khd->hqk", queries, key_rows, preferred_element_type=jnp.float32
    ) * HD ** (-0.5)
    return jnp.where(allowed_row[None], raw, NEGATIVE)


def row_forward(packed):
    head_row, allowed_row = packed
    scores = masked_scores(head_row[:, 0], head_row[:, 1], allowed_row)
    highest = jnp.max(scores, -1, keepdims=True)
    numerator = jnp.exp(scores - highest)
    totals = jnp.sum(numerator, -1, keepdims=True)
    probabilities = (numerator / totals).astype(jnp.bfloat16)
    attended = jnp.einsum(
        "hqk,khd->qhd", probabilities, head_row[:, 2], preferred_element_type=jnp.float32
    )
    return (attended.reshape(head_row.shape[0], -1), highest[..., 0] + jnp.log(totals[..., 0]))


def row_backward(packed):
    head_row, grad_row, logsum_row, allowed_row = packed
    queries = head_row[:, 0]
    key_rows = head_row[:, 1]
    value_rows = head_row[:, 2]
    probabilities = jnp.exp(masked_scores(queries, key_rows, allowed_row) - logsum_row[:, :, None])
    grad_probs = jnp.einsum(
        "qhd,khd->hqk", grad_row, value_rows, preferred_element_type=jnp.float32
    )
    centre = jnp.sum(probabilities * grad_probs, -1, keepdims=True)
    grad_scores = (probabilities * (grad_probs - centre)).astype(jnp.bfloat16)
    scale = HD ** (-0.5)
    grad_query = (
        jnp.einsum("hqk,khd->qhd", grad_scores, key_rows, preferred_element_type=jnp.float32)
        * scale
    )
    grad_key = (
        jnp.einsum("hqk,qhd->khd", grad_scores, queries, preferred_element_type=jnp.float32) * scale
    )
    grad_value = jnp.einsum(
        "hqk,qhd->khd",
        probabilities.astype(jnp.bfloat16),
        grad_row,
        preferred_element_type=jnp.float32,
    )
    return jnp.stack([grad_query, grad_key, grad_value], 1).reshape(head_row.shape[0], -1)


def contract_rows(left, right):
    return lax.dot_general(
        left, right, (((0,), (0,)), ((), ())), preferred_element_type=jnp.float32
    )


def contract_cols(left, right):
    return lax.dot_general(
        left, right, (((1,), (1,)), ((), ())), preferred_element_type=jnp.float32
    )


def forward_layer(current, weights, allowed):
    qkv_matrix, qv_biases, out_matrix, up_matrix, up_bias, down_matrix, gains, offsets = weights
    current_low = current.astype(jnp.bfloat16)
    biases = jnp.concatenate([qv_biases[0], jnp.zeros_like(qv_biases[0]), qv_biases[1]]).astype(
        jnp.float32
    )
    projected = (
        jnp.dot(current_low, qkv_matrix, preferred_element_type=jnp.float32) + biases
    ).astype(jnp.bfloat16)
    head_rows = projected.reshape(allowed.shape[0], allowed.shape[1], 3, HEADS, HD)
    attended, logsum = lax.map(row_forward, (head_rows, allowed))
    attended = attended.reshape(current.shape[0], -1).astype(jnp.bfloat16)
    branch = jnp.dot(attended, out_matrix, preferred_element_type=jnp.float32) + offsets[0].astype(
        jnp.float32
    )
    normed, unit_first, inverse_first = normalize(
        current + branch, gains[0].astype(jnp.float32), offsets[1].astype(jnp.float32)
    )
    normed_low = normed.astype(jnp.bfloat16)
    hidden_pre = jnp.dot(
        normed_low, up_matrix, preferred_element_type=jnp.float32
    ) + up_bias.astype(jnp.float32)
    activated = jax.nn.gelu(hidden_pre, approximate=False).astype(jnp.bfloat16)
    ffn_result = jnp.dot(activated, down_matrix, preferred_element_type=jnp.float32) + offsets[
        2
    ].astype(jnp.float32)
    output, unit_second, inverse_second = normalize(
        normed + ffn_result, gains[1].astype(jnp.float32), offsets[3].astype(jnp.float32)
    )
    saved = (
        current_low,
        head_rows,
        logsum,
        attended,
        unit_first,
        inverse_first,
        normed_low,
        hidden_pre,
        activated,
        unit_second,
        inverse_second,
    )
    return (output, saved)


def backward_layer(cotangent, saved, weights, allowed):
    qkv_matrix, qv_biases, out_matrix, up_matrix, up_bias, down_matrix, gains, offsets = weights
    (
        current_low,
        head_rows,
        logsum,
        attended,
        unit_first,
        inverse_first,
        normed_low,
        hidden_pre,
        activated,
        unit_second,
        inverse_second,
    ) = saved
    width = out_matrix.shape[0]
    gain_second = jnp.sum(cotangent * unit_second, 0)
    offset_second = jnp.sum(cotangent, 0)
    grad_second = normalize_back(
        cotangent, unit_second, inverse_second, gains[1].astype(jnp.float32)
    )
    grad_ffn = grad_second.astype(jnp.bfloat16)
    offset_ffn = jnp.sum(grad_ffn, 0, dtype=jnp.float32)
    down_grad = contract_rows(activated, grad_ffn)
    grad_active = contract_cols(grad_ffn, down_matrix)
    unused, gelu_back = jax.vjp(partial(jax.nn.gelu, approximate=False), hidden_pre)
    grad_hidden = gelu_back(grad_active)[0].astype(jnp.bfloat16)
    upbias_grad = jnp.sum(grad_hidden, 0, dtype=jnp.float32)
    up_grad = contract_rows(normed_low, grad_hidden)
    grad_normed = grad_second + contract_cols(grad_hidden, up_matrix)
    gain_first = jnp.sum(grad_normed * unit_first, 0)
    offset_first = jnp.sum(grad_normed, 0)
    grad_first = normalize_back(
        grad_normed, unit_first, inverse_first, gains[0].astype(jnp.float32)
    )
    grad_branch = grad_first.astype(jnp.bfloat16)
    offset_branch = jnp.sum(grad_branch, 0, dtype=jnp.float32)
    out_grad = contract_rows(attended, grad_branch)
    grad_attended = contract_cols(grad_branch, out_matrix).astype(jnp.bfloat16)
    grad_attended = grad_attended.reshape(allowed.shape[0], allowed.shape[1], HEADS, HD)
    grad_projected = lax.map(row_backward, (head_rows, grad_attended, logsum, allowed))
    grad_projected = grad_projected.reshape(cotangent.shape[0], -1).astype(jnp.bfloat16)
    bias_grad = jnp.stack(
        [
            jnp.sum(grad_projected[:, :width], 0, dtype=jnp.float32),
            jnp.sum(grad_projected[:, 2 * width :], 0, dtype=jnp.float32),
        ]
    )
    qkv_grad = contract_rows(current_low, grad_projected)
    grad_input = grad_first + contract_cols(grad_projected, qkv_matrix)
    grads = (
        qkv_grad,
        bias_grad,
        out_grad,
        up_grad,
        upbias_grad,
        down_grad,
        jnp.stack([gain_first, gain_second]),
        jnp.stack([offset_branch, offset_first, offset_ffn, offset_second]),
    )
    return (grad_input, grads)


def local(
    hidden_in,
    lengths,
    grad_out,
    attn_weight,
    attn_bias,
    out_weight,
    ffn_in,
    ffn_in_bias,
    ffn_out,
    norm_gain,
    shifts,
):
    allowed = permitted(lengths)
    depth = attn_weight.shape[0]
    rows = out_weight.shape[1]
    height = ffn_out.shape[1]
    place = lax.axis_index(("dp", "fsdp"))
    packed = [
        pack_layer(
            attn_weight[layer_index],
            attn_bias[layer_index],
            out_weight[layer_index],
            ffn_in[layer_index],
            ffn_in_bias[layer_index],
            ffn_out[layer_index],
            norm_gain[layer_index],
            shifts[layer_index],
        )
        for layer_index in range(depth)
    ]
    fetched = []
    for layer_index in range(depth):
        if layer_index == 0:
            held = lax.all_gather(packed[layer_index], "dp", axis=0)
            held = lax.all_gather(held, "fsdp", axis=1)
        else:
            held = gather_direct(packed[layer_index], "dp")
            held = gather_doubling(held, "fsdp")
        held = held.reshape((-1,) + packed[layer_index].shape)
        fetched.append(unpack_layer(held, rows, height))
    current = hidden_in.astype(jnp.float32)
    saved_all = []
    for layer_index in range(depth):
        current, saved = forward_layer(current, fetched[layer_index], allowed)
        saved_all.append(saved)
    cotangent = grad_out.astype(jnp.float32)
    reduced = []
    first = lax.axis_size("dp")
    second = lax.axis_size("fsdp")
    for layer_index in reversed(range(depth)):
        cotangent, grads = backward_layer(
            cotangent, saved_all[layer_index], fetched[layer_index], allowed
        )
        sent = pack_grads(grads, rows, height).astype(jnp.bfloat16)
        sent = sent.reshape((first, second) + sent.shape[1:]).transpose(1, 0, 2, 3)
        if layer_index == 0:
            held = scatter_exchange(sent, "fsdp").astype(jnp.bfloat16)
            held = scatter_exchange(held, "dp")
        else:
            held = scatter_halving(sent, "fsdp")
            held = scatter_direct(held, "dp")
        reduced.insert(0, unpack_grads(held, rows, height, place))
    stacked = [jnp.stack([entry[member] for entry in reduced]) for member in range(8)]
    return (
        current.astype(jnp.bfloat16),
        cotangent.astype(jnp.bfloat16),
        stacked[0],
        stacked[1],
        stacked[2],
        stacked[3],
        stacked[4],
        stacked[5],
        stacked[6],
        stacked[7],
    )


def solution(mesh):
    placed = (
        P(("dp", "fsdp"), None),
        P(("dp", "fsdp"), None),
        P(("dp", "fsdp"), None),
        P(None, ("dp", "fsdp"), None),
        P(None, None, ("dp", "fsdp")),
        P(None, ("dp", "fsdp"), None),
        P(None, ("dp", "fsdp"), None),
        P(None, ("dp", "fsdp")),
        P(None, ("dp", "fsdp"), None),
        P(None, None, ("dp", "fsdp")),
        P(None, None, ("dp", "fsdp")),
    )
    return jax.shard_map(
        local,
        mesh=mesh,
        in_specs=placed,
        out_specs=(
            P(("dp", "fsdp"), None),
            P(("dp", "fsdp"), None),
            P(None, ("dp", "fsdp"), None),
            P(None, None, ("dp", "fsdp")),
            P(None, ("dp", "fsdp"), None),
            P(None, ("dp", "fsdp"), None),
            P(None, ("dp", "fsdp")),
            P(None, ("dp", "fsdp"), None),
            P(None, None, ("dp", "fsdp")),
            P(None, None, ("dp", "fsdp")),
        ),
        check_vma=False,
    )
```

```python
from functools import partial

import jax
import jax.numpy as jnp
from jax import lax
from jax.experimental import pallas as pl
from jax.experimental.pallas import tpu as pltpu
from jax.sharding import PartitionSpec as P

HEADS = 4
HD = 64
SEQ = 512
PAIR = 2 * HD
FAR = -(2.0**100)
FLOOR = -1e20
EPSILON = 1e-12
PIECE = 64
LOW = jnp.bfloat16
F32 = jnp.float32
MEMORY = 60 * 2**20


def dot_nn(left, right):
    return lax.dot_general(left, right, (((1,), (0,)), ((), ())), preferred_element_type=F32)


def dot_nt(left, right):
    return lax.dot_general(left, right, (((1,), (1,)), ((), ())), preferred_element_type=F32)


def dot_tn(left, right):
    return lax.dot_general(left, right, (((0,), (0,)), ((), ())), preferred_element_type=F32)


def pieces(total, size=PIECE):
    return [pl.ds(start, size) for start in range(0, total, size)]


def three_parts(values):
    first = values.astype(LOW).astype(F32)
    rest = values - first
    second = rest.astype(LOW).astype(F32)
    return first, second, rest - second


def gelu_parts(u):
    bell = jnp.exp(u * u * -0.5)
    t = 1.0 / (1.0 + (0.3275911 * 0.5**0.5) * jnp.abs(u))
    poly = t * (
        0.127414796
        + t * (-0.142248368 + t * (0.7107068705 + t * (-0.7265760135 + t * 0.5307027145)))
    )
    tail = poly * bell
    cumulative = jnp.where(u > 0, 1.0 - tail, tail)
    return u * cumulative, cumulative + u * bell * 0.3989422804014327


def lane_facts(rows):
    lane = lax.broadcasted_iota(jnp.int32, (rows, PAIR), 1)
    return lane < HD, lane % HD


def segments(lengths_ref, row, start, rows):
    places = lax.broadcasted_iota(jnp.int32, (rows, PAIR), 0) + start
    bound = jnp.int32(0)
    segment = jnp.zeros((rows, PAIR), jnp.int32)
    last = lengths_ref.shape[1] - 1
    for entry in range(last):
        bound = bound + lengths_ref[row, entry]
        segment = segment + (places >= bound).astype(jnp.int32)
    return segment, (segment == last).astype(F32), last


def attention_forward(row, lengths_ref, x, wq_ref, bias_ref, qa_ref, ka_ref, va_ref, ob_ref, s_ref, p_ref, m_ref, pad_ref, q_ref, aug_ref):
    width = HEADS * HD
    for block in range(3):
        for pair in range(HEADS // 2):
            at = block * width + pair * PAIR
            q_ref[block, pair] = dot_nn(x, wq_ref[:, at : at + PAIR]) + bias_ref[:, at : at + PAIR]
    for start in range(0, SEQ, PIECE):
        place = pl.ds(start, PIECE)
        low_half, slot = lane_facts(PIECE)
        segment, pad, last = segments(lengths_ref, row, start, PIECE)
        pad_ref[place] = pad
        aug_q = jnp.where(slot == segment, 1.0, 0.0)
        aug_ref[place] = aug_q
        seen = (slot == segment) & (slot != last)
        aug_k = jnp.where(slot <= last, jnp.where(seen, 0.0, FAR), jnp.where(slot <= last + 3, 1.0, 0.0))
        for pair in range(HEADS // 2):
            q = q_ref[0, pair, place] * HD**-0.5
            k = q_ref[1, pair, place]
            v = q_ref[2, pair, place]
            q_ref[0, pair, place] = q
            qa_ref[2 * pair, place] = jnp.where(low_half, q, aug_q).astype(LOW)
            qa_ref[2 * pair + 1, place] = jnp.where(low_half, aug_q, q).astype(LOW)
            ka_ref[2 * pair, place] = jnp.where(low_half, k, aug_k).astype(LOW)
            ka_ref[2 * pair + 1, place] = jnp.where(low_half, aug_k, k).astype(LOW)
            va_ref[2 * pair, place] = jnp.where(low_half, v, 1.0).astype(LOW)
            va_ref[2 * pair + 1, place] = jnp.where(low_half, 1.0, v).astype(LOW)
    half = SEQ // 2
    units = [(head, part) for head in range(HEADS) for part in range(2)]

    def scores(unit):
        head, part = units[unit]
        s_ref[unit % 2] = dot_nt(qa_ref[head, pl.ds(part * half, half)], ka_ref[head])

    def softmax(unit):
        head, part = units[unit]
        for start in range(0, half, PIECE):
            s = s_ref[unit % 2, pl.ds(start, PIECE)]
            highest = jnp.maximum(jnp.max(s, -1, keepdims=True), FLOOR)
            p_ref[unit % 2, pl.ds(start, PIECE)] = jnp.exp(s - highest).astype(LOW)
            m_ref[head % 2, pl.ds(part * half + start, PIECE)] = jnp.broadcast_to(highest, (PIECE, PAIR))

    def attend(unit):
        head, part = units[unit]
        return dot_nn(p_ref[unit % 2], va_ref[head])

    sums = {}
    scores(0)
    for unit in range(len(units)):
        if unit + 1 < len(units):
            scores(unit + 1)
        softmax(unit)
        head, part = units[unit]
        q_ref[1, head % 2, pl.ds(part * half, half)] = attend(unit)
        if head % 2 and part:
            pair = head // 2
            for start in range(0, SEQ, PIECE):
                place = pl.ds(start, PIECE)
                low_half, slot = lane_facts(PIECE)
                even = q_ref[1, 0, place]
                odd = q_ref[1, 1, place]
                pad = pad_ref[place]
                last = lengths_ref.shape[1] - 1
                total = jnp.where(low_half, odd, even) + pad
                top = jnp.where(low_half, odd_even(m_ref, 1, place), odd_even(m_ref, 0, place))
                spread = jnp.where(pad > 0, 0.0, top + jnp.log(total))
                first, second, third = three_parts(spread)
                aug = jnp.where(
                    slot == last + 1,
                    -first,
                    jnp.where(slot == last + 2, -second, jnp.where(slot == last + 3, -third, aug_ref[place])),
                )
                q = q_ref[0, pair, place]
                qa_ref[2 * pair, place] = jnp.where(low_half, q, aug).astype(LOW)
                qa_ref[2 * pair + 1, place] = jnp.where(low_half, aug, q).astype(LOW)
                v = q_ref[2, pair, place].astype(LOW).astype(F32)
                out = jnp.where(low_half, even, odd) / pltpu.roll(total, HD, 1) + pad * v
                ob_ref[place, pl.ds(pair * PAIR, PAIR)] = out.astype(LOW)


def odd_even(ref, which, place):
    return ref[which, place]


def normal(values):
    centred = values - jnp.mean(values, -1, keepdims=True)
    inverse = lax.rsqrt(jnp.mean(centred * centred, -1, keepdims=True) + EPSILON)
    return centred * inverse, inverse


def normal_back(cotangent, unit, inverse, gains):
    scaled = cotangent * gains
    return inverse * (
        scaled
        - jnp.mean(scaled, -1, keepdims=True)
        - unit * jnp.mean(scaled * unit, -1, keepdims=True)
    )


def dense_forward(x_ref, ob_ref, wo_ref, wi_ref, wf_ref, small_ref, bi_ref, n1_ref, n2_ref, inv_ref, yb_ref, gb_ref, gp_ref, z_ref, work_ref, u_ref):
    small = lambda index: small_ref[pl.ds(index, 1)]
    work_ref[...] = dot_nn(ob_ref[...], wo_ref[...])
    for place in pieces(SEQ):
        unit, inverse = normal(x_ref[place].astype(F32) + work_ref[place] + small(4))
        n1_ref[place] = unit
        inv_ref[place, pl.ds(0, HD)] = jnp.broadcast_to(inverse, (PIECE, HD))
        y = unit * small(2) + small(5)
        yb_ref[place] = y.astype(LOW)
        work_ref[place] = y + small(6)
    columns = 256
    count = wi_ref.shape[1] // columns

    def into(step):
        u_ref[step % 2] = dot_nn(yb_ref[...], wi_ref[:, pl.ds(step * columns, columns)])

    into(0)
    for step in range(count):
        if step + 1 < count:
            into(step + 1)
        lanes = pl.ds(step * columns, columns)
        for place in pieces(SEQ):
            g, slope = gelu_parts(u_ref[step % 2, place] + bi_ref[:, lanes])
            gb_ref[place, lanes] = g.astype(LOW)
            gp_ref[place, lanes] = slope.astype(LOW)
    work_ref[...] += dot_nn(gb_ref[...], wf_ref[...])
    for place in pieces(SEQ):
        unit, inverse = normal(work_ref[place])
        n2_ref[place] = unit
        inv_ref[place, pl.ds(HD, HD)] = jnp.broadcast_to(inverse, (PIECE, HD))
        z_ref[place] = (unit * small(3) + small(7)).astype(z_ref.dtype)


def fold(values):
    return jnp.sum(values.reshape(-1, 8, values.shape[-1]), 0)


def dense_backward(dz_ref, n1_ref, n2_ref, inv_ref, yb_ref, gb_ref, gp_ref, ob_ref, wo_ref, wi_ref, wf_ref, small_ref, dr_ref, dob_ref, gwo_ref, gwi_ref, gwf_ref, gsmall_ref, gbi_ref, low_ref, u_ref, du_ref):
    small = lambda index: small_ref[pl.ds(index, 1)]
    for place in pieces(SEQ):
        dz = dz_ref[place].astype(F32)
        unit = n2_ref[place]
        gsmall_ref[3] += fold(dz * unit)
        gsmall_ref[7] += fold(dz)
        dr = normal_back(dz, unit, inv_ref[place, pl.ds(HD, 1)], small(3))
        dr_ref[place] = dr
        df = dr.astype(LOW)
        low_ref[place] = df
        gsmall_ref[6] += fold(df.astype(F32))
    columns = 256
    count = wi_ref.shape[1] // columns

    def back(step):
        u_ref[step % 2] = dot_nt(low_ref[...], wf_ref[pl.ds(step * columns, columns)])

    back(0)
    for step in range(count):
        if step + 1 < count:
            back(step + 1)
        lanes = pl.ds(step * columns, columns)
        gwf_ref[:, lanes] += dot_tn(low_ref[...], gb_ref[:, lanes])
        for place in pieces(SEQ):
            du = (u_ref[step % 2, place] * gp_ref[place, lanes].astype(F32)).astype(LOW)
            du_ref[place, lanes] = du
            gbi_ref[:, lanes] += fold(du.astype(F32))
        gwi_ref[:, lanes] += dot_tn(yb_ref[...], du_ref[:, lanes])
    u_ref[0] = dot_nt(du_ref[...], wi_ref[...])
    for place in pieces(SEQ):
        dy = dr_ref[place] + u_ref[0, place]
        unit = n1_ref[place]
        gsmall_ref[2] += fold(dy * unit)
        gsmall_ref[5] += fold(dy)
        dr = normal_back(dy, unit, inv_ref[place, pl.ds(0, 1)], small(2))
        dr_ref[place] = dr
        da = dr.astype(LOW)
        low_ref[place] = da
        gsmall_ref[4] += fold(da.astype(F32))
    gwo_ref[...] += dot_tn(ob_ref[...], low_ref[...])
    dob_ref[...] = dot_nt(low_ref[...], wo_ref[...]).astype(LOW)


def attention_backward(row, lengths_ref, x, dob_ref, ob_ref, qa_ref, ka_ref, va_ref, wq_ref, dr_ref, dx_ref, gwq_ref, gbias_ref, da_ref, p_ref, ds_ref, s_ref, dqkv_ref, dq_ref, pad_ref):
    width = HEADS * HD
    half = SEQ // 2
    low_half, slot = lane_facts(PIECE)
    for start in range(0, SEQ, PIECE):
        place = pl.ds(start, PIECE)
        segment, pad, last = segments(lengths_ref, row, start, PIECE)
        pad_ref[place] = pad
        for pair in range(HEADS // 2):
            lanes = pl.ds(pair * PAIR, PAIR)
            dob = dob_ref[place, lanes].astype(F32)
            product = dob * ob_ref[place, lanes].astype(F32)
            even = jnp.sum(jnp.where(low_half, product, 0.0), -1, keepdims=True)
            odd = jnp.sum(jnp.where(low_half, 0.0, product), -1, keepdims=True)
            first, second, third = three_parts(jnp.where(low_half, odd, even))
            aug = jnp.where(
                slot == 0, -first, jnp.where(slot == 1, -second, jnp.where(slot == 2, -third, 0.0))
            )
            da_ref[2 * pair, place] = jnp.where(low_half, dob, aug).astype(LOW)
            da_ref[2 * pair + 1, place] = jnp.where(low_half, aug, dob).astype(LOW)
    units = [(head, part) for head in range(HEADS) for part in range(2)]

    def scores(unit):
        head, part = units[unit]
        keys = pl.ds(part * half, half)
        s_ref[0, unit % 2] = dot_nt(ka_ref[head, keys], qa_ref[head])
        s_ref[1, unit % 2] = dot_nt(va_ref[head, keys], da_ref[head])

    def weigh(unit):
        for place in pieces(half):
            p = jnp.exp(s_ref[0, unit % 2, place])
            p_ref[unit % 2, place] = p.astype(LOW)
            ds_ref[unit % 2, place] = (p * s_ref[1, unit % 2, place]).astype(LOW)

    scores(0)
    for unit in range(len(units)):
        if unit + 1 < len(units):
            scores(unit + 1)
        weigh(unit)
        head, part = units[unit]
        keys = pl.ds(part * half, half)
        side = head % 2
        dq_ref[1, side, keys] = dot_nn(ds_ref[unit % 2], qa_ref[head])
        dq_ref[2, side, keys] = dot_nn(p_ref[unit % 2], da_ref[head])
        dq = dot_tn(ds_ref[unit % 2], ka_ref[head, keys])
        if part:
            dq_ref[0, side] += dq
        else:
            dq_ref[0, side] = dq
        if side and part:
            pair = head // 2
            for start in range(0, SEQ, PIECE):
                place = pl.ds(start, PIECE)
                dq = jnp.where(low_half, dq_ref[0, 0, place], dq_ref[0, 1, place]) * HD**-0.5
                dk = jnp.where(low_half, dq_ref[1, 0, place], dq_ref[1, 1, place])
                dv = jnp.where(low_half, dq_ref[2, 0, place], dq_ref[2, 1, place])
                dv = dv + pad_ref[place] * dob_ref[place, pl.ds(pair * PAIR, PAIR)].astype(F32)
                for block, value in enumerate((dq, dk, dv)):
                    lanes = pl.ds(block * width + pair * PAIR, PAIR)
                    value = value.astype(LOW)
                    dqkv_ref[place, lanes] = value
                    if block != 1:
                        into = pl.ds(pair * PAIR, PAIR)
                        gbias_ref[block // 2, :, into] += fold(value.astype(F32))
    gwq_ref[...] += dot_tn(x, dqkv_ref[...])
    dx_ref[...] = (dr_ref[...] + dot_nt(dqkv_ref[...], wq_ref[...])).astype(dx_ref.dtype)


def shape_of(array):
    return jax.ShapeDtypeStruct(array.shape, array.dtype)


def by_row(shape):
    if len(shape) == 2:
        return pl.BlockSpec((SEQ, shape[1]), lambda row: (row, 0))
    return pl.BlockSpec((None,) + tuple(shape[1:]), lambda row: (row,) + (0,) * (len(shape) - 1))


def whole(shape):
    return pl.BlockSpec(tuple(shape), lambda row: (0,) * len(shape))


def run_rows(body, lengths, rowwise, fixed, row_outs, sums, scratch, cost):
    count = lengths.shape[0]

    def kernel(lengths_ref, *refs):
        row = pl.program_id(0)
        cuts = [len(rowwise), len(fixed), len(row_outs), len(sums), len(scratch)]
        groups = []
        at = 0
        for cut in cuts:
            groups.append(refs[at : at + cut])
            at += cut

        @pl.when(row == 0)
        def _():
            for ref in groups[3]:
                ref[...] = jnp.zeros(ref.shape, ref.dtype)

        body(row, lengths_ref, *groups)

    return pl.pallas_call(
        kernel,
        grid=(count,),
        in_specs=[pl.BlockSpec(memory_space=pltpu.SMEM)]
        + [by_row(array.shape) for array in rowwise]
        + [whole(array.shape) for array in fixed],
        out_specs=[by_row(struct.shape) for struct in row_outs]
        + [whole(struct.shape) for struct in sums],
        out_shape=list(row_outs) + list(sums),
        scratch_shapes=list(scratch),
        compiler_params=pltpu.CompilerParams(
            dimension_semantics=("arbitrary",), vmem_limit_bytes=MEMORY
        ),
        cost_estimate=pl.CostEstimate(flops=cost, bytes_accessed=8 * 2**20, transcendentals=0),
    )(lengths, *rowwise, *fixed)


def struct(shape, dtype):
    return jax.ShapeDtypeStruct(tuple(shape), dtype)


FORWARD_SCRATCH = lambda: [
    pltpu.VMEM((2, SEQ // 2, SEQ), F32),
    pltpu.VMEM((2, SEQ // 2, SEQ), LOW),
    pltpu.VMEM((2, SEQ, PAIR), F32),
    pltpu.VMEM((SEQ, PAIR), F32),
    pltpu.VMEM((3, HEADS // 2, SEQ, PAIR), F32),
    pltpu.VMEM((SEQ, PAIR), F32),
]
BACKWARD_SCRATCH = lambda: [
    pltpu.VMEM((HEADS, SEQ, PAIR), LOW),
    pltpu.VMEM((2, SEQ // 2, SEQ), LOW),
    pltpu.VMEM((2, SEQ // 2, SEQ), LOW),
    pltpu.VMEM((2, 2, SEQ // 2, SEQ), F32),
    pltpu.VMEM((SEQ, 3 * HEADS * HD), LOW),
    pltpu.VMEM((3, 2, SEQ, PAIR), F32),
    pltpu.VMEM((SEQ, PAIR), F32),
]


def attention_outs(rows, tokens, width):
    heads = (rows, HEADS, SEQ, PAIR)
    return [struct(heads, LOW)] * 3 + [struct((tokens, width), LOW)]


def dense_outs(tokens, width, hidden):
    return [
        struct((tokens, width), F32),
        struct((tokens, width), F32),
        struct((tokens, PAIR), F32),
        struct((tokens, width), LOW),
        struct((tokens, hidden), LOW),
        struct((tokens, hidden), LOW),
    ]


def dense_sums(width, hidden):
    return [
        struct((width, width), F32),
        struct((width, hidden), F32),
        struct((width, hidden), F32),
        struct((8, 8, width), F32),
        struct((8, hidden), F32),
    ]


def attention_sums(width):
    return [struct((width, 3 * width), F32), struct((2, 8, width), F32)]


def first_attention(lengths, x, wq, bias):
    rows, (tokens, width) = lengths.shape[0], x.shape

    def body(row, lengths_ref, rowwise, fixed, outs, sums, scratch):
        attention_forward(row, lengths_ref, rowwise[0][...], *fixed, *outs, *scratch)

    return run_rows(
        body, lengths, [x], [wq, bias], attention_outs(rows, tokens, width), [],
        FORWARD_SCRATCH(), 4 * 10**9,
    )


def dense_then_attention(lengths, x, ob, weights, wq, bias):
    rows, (tokens, width) = lengths.shape[0], x.shape
    hidden = weights[1].shape[1]
    dense = dense_outs(tokens, width, hidden)

    def body(row, lengths_ref, rowwise, fixed, outs, sums, scratch):
        kept, z_ref, attention = outs[:6], outs[6], outs[7:]
        dense_forward(*rowwise, *fixed[:5], *kept, z_ref, *scratch[:2])
        attention_forward(
            row, lengths_ref, z_ref[...].astype(LOW), *fixed[5:], *attention, *scratch[2:]
        )

    return run_rows(
        body, lengths, [x, ob], list(weights) + [wq, bias],
        dense + [struct((tokens, width), F32)] + attention_outs(rows, tokens, width), [],
        [pltpu.VMEM((SEQ, width), F32), pltpu.VMEM((2, SEQ, width), F32)] + FORWARD_SCRATCH(),
        10**10,
    )


def dense_both(lengths, x, ob, cotangent, weights):
    tokens, width = x.shape
    hidden = weights[1].shape[1]

    def body(row, lengths_ref, rowwise, fixed, outs, sums, scratch):
        x_ref, ob_ref, dz_ref = rowwise
        z_ref, dr_ref, dob_ref = outs
        kept, work, rest = scratch[:6], scratch[6], scratch[7:]
        low_ref, u_ref, du_ref = rest
        dense_forward(x_ref, ob_ref, *fixed, *kept, z_ref, work, u_ref)
        dense_backward(
            dz_ref, *kept, ob_ref, *fixed[:4], dr_ref, dob_ref, *sums, low_ref, u_ref, du_ref
        )

    kept = [pltpu.VMEM((SEQ,) + part.shape[1:], part.dtype) for part in dense_outs(tokens, width, hidden)]
    return run_rows(
        body, lengths, [x, ob, cotangent], list(weights),
        [struct((tokens, width), LOW), struct((tokens, width), F32), struct((tokens, width), LOW)],
        dense_sums(width, hidden),
        kept
        + [
            pltpu.VMEM((SEQ, width), F32),
            pltpu.VMEM((SEQ, width), LOW),
            pltpu.VMEM((2, SEQ, width), F32),
            pltpu.VMEM((SEQ, hidden), LOW),
        ],
        10**10,
    )


def attention_then_dense(lengths, upper, wq, lower, weights):
    tokens, width = upper[0].shape
    hidden = weights[1].shape[1]

    def body(row, lengths_ref, rowwise, fixed, outs, sums, scratch):
        up, low = rowwise[:7], rowwise[7:]
        dr_ref, dob_ref = outs
        dx_ref, low_ref, u_ref, du_ref = scratch[:4]
        attention_backward(
            row, lengths_ref, up[0][...].astype(LOW), *up[1:6], fixed[0], up[6], dx_ref,
            *sums[:2], *scratch[4:],
        )
        dense_backward(
            dx_ref, *low, *fixed[1:], dr_ref, dob_ref, *sums[2:], low_ref, u_ref, du_ref
        )

    return run_rows(
        body, lengths, list(upper) + list(lower), [wq] + list(weights[:4]),
        [struct((tokens, width), F32), struct((tokens, width), LOW)],
        attention_sums(width) + dense_sums(width, hidden),
        [
            pltpu.VMEM((SEQ, width), F32),
            pltpu.VMEM((SEQ, width), LOW),
            pltpu.VMEM((2, SEQ, width), F32),
            pltpu.VMEM((SEQ, hidden), LOW),
        ]
        + BACKWARD_SCRATCH(),
        15 * 10**9,
    )


def last_attention(lengths, upper, wq):
    tokens, width = upper[0].shape

    def body(row, lengths_ref, rowwise, fixed, outs, sums, scratch):
        attention_backward(
            row, lengths_ref, rowwise[0][...], *rowwise[1:6], fixed[0], rowwise[6], outs[0],
            *sums, *scratch,
        )

    return run_rows(
        body, lengths, list(upper), [wq], [struct((tokens, width), LOW)],
        attention_sums(width), BACKWARD_SCRATCH(), 8 * 10**9,
    )


def gather_exchange(part, axis):
    size = lax.axis_size(axis)
    return lax.all_to_all(jnp.broadcast_to(part[None], (size,) + part.shape), axis, 0, 0, tiled=True)


def scatter_exchange(parts, axis):
    return jnp.sum(lax.all_to_all(parts, axis, 0, 0, tiled=True).astype(F32), 0)


def columns_of(attn_bias, norm_gain, shifts, ffn_in_bias):
    rows = attn_bias.shape[1]
    return jnp.concatenate(
        [attn_bias.T, norm_gain.T, shifts.T, ffn_in_bias.reshape(-1, rows).T], 1
    )


def side_by_side(part, rows):
    width = part.shape[-1]
    return part.reshape(-1, rows, width).transpose(1, 0, 2).reshape(rows, -1)


def scatter_layout(parts, shared, rows, first, second):
    pieces_of = [part.reshape(first * second, rows, -1) for part in parts]
    pieces_of.append(
        jnp.broadcast_to(shared.reshape(1, rows, -1), (first * second, rows, shared.size // rows))
    )
    joined = jnp.concatenate([part.astype(LOW) for part in pieces_of], -1)
    return joined.reshape(first, second, rows, -1).transpose(1, 0, 2, 3)


def local(
    hidden_in,
    lengths,
    grad_out,
    attn_weight,
    attn_bias,
    out_weight,
    ffn_in,
    ffn_in_bias,
    ffn_out,
    norm_gain,
    shifts,
):
    depth, rows, width = out_weight.shape
    hidden = ffn_in.shape[2]
    first, second = lax.axis_size("dp"), lax.axis_size("fsdp")
    count = first * second
    small = jnp.concatenate(
        [columns_of(attn_bias[l], norm_gain[l], shifts[l], ffn_in_bias[l]) for l in range(depth)], 1
    )
    each = small.shape[1] // depth
    small = jnp.pad(small, ((0, 0), (0, 128 - small.shape[1])))
    urgent = jnp.concatenate([attn_weight[0], small], 1)
    urgent = gather_exchange(gather_exchange(urgent, "dp"), "fsdp")
    urgent = urgent.transpose(1, 0, 2, 3).reshape(width, -1)
    later = jnp.concatenate(
        [out_weight[0], ffn_in[0], side_by_side(ffn_out[0], rows)]
        + [attn_weight[1], out_weight[1], ffn_in[1], side_by_side(ffn_out[1], rows)],
        1,
    )
    later = lax.all_gather(later, ("dp", "fsdp"), axis=0, tiled=True)
    vectors = urgent[:, 3 * width :].T.astype(F32)
    wq, weights, biases = [], [], []
    at = 0
    for l in range(depth):
        mine = vectors[each * l : each * (l + 1)]
        if l == 0:
            wq.append(urgent[:, : 3 * width])
        else:
            wq.append(later[:, at : at + 3 * width])
            at += 3 * width
        biases.append(
            jnp.concatenate([mine[0], jnp.zeros_like(mine[0]), mine[1]]).reshape(1, -1)
        )
        wo = later[:, at : at + width]
        wi = later[:, at + width : at + width + hidden]
        wf = later[:, at + width + hidden : at + width + 2 * hidden]
        at += width + 2 * hidden
        wf = wf.reshape(count, rows, -1, width).transpose(0, 2, 1, 3).reshape(hidden, width)
        bi = mine[8:].reshape(-1, count, rows).transpose(1, 0, 2).reshape(1, hidden)
        weights.append((wo, wi, wf, mine[:8], bi))

    qa0, ka0, va0, ob0 = first_attention(lengths, hidden_in, wq[0], biases[0])
    n1, n2, inv, yb, gb, gp, z0, qa1, ka1, va1, ob1 = dense_then_attention(
        lengths, hidden_in, ob0, weights[0], wq[1], biases[1]
    )
    hidden_out, dr1, dob1, *sums1 = dense_both(lengths, z0, ob1, grad_out, weights[1])
    dr0, dob0, gwq1, gbias1, *sums0 = attention_then_dense(
        lengths, (z0, dob1, ob1, qa1, ka1, va1, dr1), wq[1], (n1, n2, inv, yb, gb, gp, ob0), weights[0]
    )
    grad_in, gwq0, gbias0 = last_attention(
        lengths, (hidden_in, dob0, ob0, qa0, ka0, va0, dr0), wq[0]
    )

    def dense_pieces(sums):
        gwo, gwi, gwf, gsmall, gbi = sums
        gwf = gwf.T.reshape(count, -1, rows, width).transpose(0, 2, 1, 3).reshape(width, hidden)
        shared = jnp.concatenate(
            [jnp.sum(gsmall, 1)[2:], jnp.sum(gbi, 0).reshape(-1, width)]
        )
        return [gwo, gwi, gwf], shared

    def scatter(parts, shared):
        sent = scatter_layout(parts, shared, rows, first, second)
        held = scatter_exchange(sent, "fsdp").astype(LOW)
        return scatter_exchange(held, "dp")

    parts1, shared1 = dense_pieces(sums1)
    parts0, shared0 = dense_pieces(sums0)
    tail1 = scatter(parts1, shared1)
    both = jnp.concatenate([shared0, jnp.sum(gbias1, 1)])
    middle = scatter([gwq1] + parts0, both)
    head0 = scatter([gwq0], jnp.sum(gbias0, 1))
    place = lax.axis_index(("dp", "fsdp"))

    def cut(held, sizes):
        found, at = [], 0
        for size in sizes:
            found.append(held[:, at : at + size])
            at += size
        return found, held[:, at:].reshape(-1, width)

    sizes = [width, hidden, hidden]
    (gwo1, gwi1, gwf1), shared1 = cut(tail1, sizes)
    (gwq1, gwo0, gwi0, gwf0), both = cut(middle, [3 * width] + sizes)
    (gwq0,), gbias0 = cut(head0, [3 * width])
    shared0, gbias1 = both[:-2], both[-2:]

    def own(values, height):
        return lax.dynamic_slice_in_dim(values, place * height, height, axis=-1)

    def stack_rows(values):
        return values.reshape(rows, -1, width).transpose(1, 0, 2).reshape(-1, width)

    return (
        hidden_out,
        grad_in,
        jnp.stack([gwq0, gwq1]),
        own(jnp.stack([gbias0, gbias1]), rows),
        jnp.stack([gwo0, gwo1]),
        jnp.stack([gwi0, gwi1]),
        own(jnp.stack([shared0[6:].reshape(-1), shared1[6:].reshape(-1)]), hidden // count),
        jnp.stack([stack_rows(gwf0), stack_rows(gwf1)]),
        own(jnp.stack([shared0[:2], shared1[:2]]), rows),
        own(jnp.stack([shared0[2:6], shared1[2:6]]), rows),
    )


def solution(mesh):
    placed = (
        P(("dp", "fsdp"), None),
        P(("dp", "fsdp"), None),
        P(("dp", "fsdp"), None),
        P(None, ("dp", "fsdp"), None),
        P(None, None, ("dp", "fsdp")),
        P(None, ("dp", "fsdp"), None),
        P(None, ("dp", "fsdp"), None),
        P(None, ("dp", "fsdp")),
        P(None, ("dp", "fsdp"), None),
        P(None, None, ("dp", "fsdp")),
        P(None, None, ("dp", "fsdp")),
    )
    return jax.shard_map(
        local,
        mesh=mesh,
        in_specs=placed,
        out_specs=(
            P(("dp", "fsdp"), None),
            P(("dp", "fsdp"), None),
            P(None, ("dp", "fsdp"), None),
            P(None, None, ("dp", "fsdp")),
            P(None, ("dp", "fsdp"), None),
            P(None, ("dp", "fsdp"), None),
            P(None, ("dp", "fsdp")),
            P(None, ("dp", "fsdp"), None),
            P(None, None, ("dp", "fsdp")),
            P(None, None, ("dp", "fsdp")),
        ),
        check_vma=False,
    )
```

```python
from functools import partial

import jax
import jax.numpy as jnp
from jax import lax
from jax.experimental import pallas as pl
from jax.experimental.pallas import tpu as pltpu
from jax.sharding import PartitionSpec as P

HEADS = 4
HD = 64
SEQ = 512
PAIR = 2 * HD
FAR = -(2.0**100)
FLOOR = -1e20
EPSILON = 1e-12
PIECE = 64
GROUPS = (4, 8, 8)
DEVICES = 32
LOW = jnp.bfloat16
F32 = jnp.float32
MEMORY = 60 * 2**20


def dot_nn(left, right):
    return lax.dot_general(left, right, (((1,), (0,)), ((), ())), preferred_element_type=F32)


def dot_nt(left, right):
    return lax.dot_general(left, right, (((1,), (1,)), ((), ())), preferred_element_type=F32)


def dot_tn(left, right):
    return lax.dot_general(left, right, (((0,), (0,)), ((), ())), preferred_element_type=F32)


def pieces(total, size=PIECE):
    return [pl.ds(start, size) for start in range(0, total, size)]


def three_parts(values):
    first = values.astype(LOW).astype(F32)
    rest = values - first
    second = rest.astype(LOW).astype(F32)
    return first, second, rest - second


def gelu_parts(u):
    bell = jnp.exp(u * u * -0.5)
    t = 1.0 / (1.0 + (0.3275911 * 0.5**0.5) * jnp.abs(u))
    poly = t * (
        0.127414796
        + t * (-0.142248368 + t * (0.7107068705 + t * (-0.7265760135 + t * 0.5307027145)))
    )
    tail = poly * bell
    cumulative = jnp.where(u > 0, 1.0 - tail, tail)
    return u * cumulative, cumulative + u * bell * 0.3989422804014327


def lane_facts(rows):
    lane = lax.broadcasted_iota(jnp.int32, (rows, PAIR), 1)
    return lane < HD, lane % HD


def segments(lengths_ref, row, start, rows):
    places = lax.broadcasted_iota(jnp.int32, (rows, PAIR), 0) + start
    bound = jnp.int32(0)
    segment = jnp.zeros((rows, PAIR), jnp.int32)
    last = lengths_ref.shape[1] - 1
    for entry in range(last):
        bound = bound + lengths_ref[row, entry]
        segment = segment + (places >= bound).astype(jnp.int32)
    return segment, (segment == last).astype(F32), last


def attention_forward(row, lengths_ref, x, wq_ref, bias_ref, qa_ref, ka_ref, va_ref, ob_ref, s_ref, p_ref, m_ref, pad_ref, q_ref, aug_ref):
    width = HEADS * HD
    for block in range(3):
        for pair in range(HEADS // 2):
            at = block * width + pair * PAIR
            q_ref[block, pair] = dot_nn(x, wq_ref[:, at : at + PAIR]) + bias_ref[:, at : at + PAIR]
    for start in range(0, SEQ, PIECE):
        place = pl.ds(start, PIECE)
        low_half, slot = lane_facts(PIECE)
        segment, pad, last = segments(lengths_ref, row, start, PIECE)
        pad_ref[place] = pad
        aug_q = jnp.where(slot == segment, 1.0, 0.0)
        aug_ref[place] = aug_q
        seen = (slot == segment) & (slot != last)
        aug_k = jnp.where(slot <= last, jnp.where(seen, 0.0, FAR), jnp.where(slot <= last + 3, 1.0, 0.0))
        for pair in range(HEADS // 2):
            q = q_ref[0, pair, place] * HD**-0.5
            k = q_ref[1, pair, place]
            v = q_ref[2, pair, place]
            q_ref[0, pair, place] = q
            qa_ref[2 * pair, place] = jnp.where(low_half, q, aug_q).astype(LOW)
            qa_ref[2 * pair + 1, place] = jnp.where(low_half, aug_q, q).astype(LOW)
            ka_ref[2 * pair, place] = jnp.where(low_half, k, aug_k).astype(LOW)
            ka_ref[2 * pair + 1, place] = jnp.where(low_half, aug_k, k).astype(LOW)
            va_ref[2 * pair, place] = jnp.where(low_half, v, 1.0).astype(LOW)
            va_ref[2 * pair + 1, place] = jnp.where(low_half, 1.0, v).astype(LOW)
    half = SEQ // 2
    units = [(head, part) for head in range(HEADS) for part in range(2)]

    def scores(unit):
        head, part = units[unit]
        s_ref[unit % 2] = dot_nt(qa_ref[head, pl.ds(part * half, half)], ka_ref[head])

    def softmax(unit):
        head, part = units[unit]
        for start in range(0, half, PIECE):
            s = s_ref[unit % 2, pl.ds(start, PIECE)]
            highest = jnp.maximum(jnp.max(s, -1, keepdims=True), FLOOR)
            p_ref[unit % 2, pl.ds(start, PIECE)] = jnp.exp(s - highest).astype(LOW)
            m_ref[head % 2, pl.ds(part * half + start, PIECE)] = jnp.broadcast_to(highest, (PIECE, PAIR))

    def attend(unit):
        head, part = units[unit]
        return dot_nn(p_ref[unit % 2], va_ref[head])

    sums = {}
    scores(0)
    for unit in range(len(units)):
        if unit + 1 < len(units):
            scores(unit + 1)
        softmax(unit)
        head, part = units[unit]
        q_ref[1, head % 2, pl.ds(part * half, half)] = attend(unit)
        if head % 2 and part:
            pair = head // 2
            for start in range(0, SEQ, PIECE):
                place = pl.ds(start, PIECE)
                low_half, slot = lane_facts(PIECE)
                even = q_ref[1, 0, place]
                odd = q_ref[1, 1, place]
                pad = pad_ref[place]
                last = lengths_ref.shape[1] - 1
                total = jnp.where(low_half, odd, even) + pad
                top = jnp.where(low_half, odd_even(m_ref, 1, place), odd_even(m_ref, 0, place))
                spread = jnp.where(pad > 0, 0.0, top + jnp.log(total))
                first, second, third = three_parts(spread)
                aug = jnp.where(
                    slot == last + 1,
                    -first,
                    jnp.where(slot == last + 2, -second, jnp.where(slot == last + 3, -third, aug_ref[place])),
                )
                q = q_ref[0, pair, place]
                qa_ref[2 * pair, place] = jnp.where(low_half, q, aug).astype(LOW)
                qa_ref[2 * pair + 1, place] = jnp.where(low_half, aug, q).astype(LOW)
                v = q_ref[2, pair, place].astype(LOW).astype(F32)
                out = jnp.where(low_half, even, odd) / pltpu.roll(total, HD, 1) + pad * v
                ob_ref[place, pl.ds(pair * PAIR, PAIR)] = out.astype(LOW)


def odd_even(ref, which, place):
    return ref[which, place]


def normal(values):
    centred = values - jnp.mean(values, -1, keepdims=True)
    inverse = lax.rsqrt(jnp.mean(centred * centred, -1, keepdims=True) + EPSILON)
    return centred * inverse, inverse


def normal_back(cotangent, unit, inverse, gains):
    scaled = cotangent * gains
    return inverse * (
        scaled
        - jnp.mean(scaled, -1, keepdims=True)
        - unit * jnp.mean(scaled * unit, -1, keepdims=True)
    )


def dense_forward(x_ref, ob_ref, wo_ref, wi_ref, wf_ref, small_ref, bi_ref, n1_ref, n2_ref, inv_ref, yb_ref, gb_ref, gp_ref, z_ref, work_ref, u_ref):
    small = lambda index: small_ref[pl.ds(index, 1)]
    work_ref[...] = dot_nn(ob_ref[...], wo_ref[...])
    for place in pieces(SEQ):
        unit, inverse = normal(x_ref[place].astype(F32) + work_ref[place] + small(4))
        n1_ref[place] = unit
        inv_ref[place, pl.ds(0, HD)] = jnp.broadcast_to(inverse, (PIECE, HD))
        y = unit * small(2) + small(5)
        yb_ref[place] = y.astype(LOW)
        work_ref[place] = y + small(6)
    columns = 256
    count = wi_ref.shape[1] // columns

    def into(step):
        u_ref[step % 2] = dot_nn(yb_ref[...], wi_ref[:, pl.ds(step * columns, columns)])

    into(0)
    for step in range(count):
        if step + 1 < count:
            into(step + 1)
        lanes = pl.ds(step * columns, columns)
        for place in pieces(SEQ):
            g, slope = gelu_parts(u_ref[step % 2, place] + bi_ref[:, lanes])
            gb_ref[place, lanes] = g.astype(LOW)
            gp_ref[place, lanes] = slope.astype(LOW)
    work_ref[...] += dot_nn(gb_ref[...], wf_ref[...])
    for place in pieces(SEQ):
        unit, inverse = normal(work_ref[place])
        n2_ref[place] = unit
        inv_ref[place, pl.ds(HD, HD)] = jnp.broadcast_to(inverse, (PIECE, HD))
        z_ref[place] = (unit * small(3) + small(7)).astype(z_ref.dtype)


def fold(values):
    return jnp.sum(values.reshape(-1, 8, values.shape[-1]), 0)


def dense_backward(dz_ref, n1_ref, n2_ref, inv_ref, yb_ref, gb_ref, gp_ref, ob_ref, wo_ref, wi_ref, wf_ref, small_ref, dr_ref, dob_ref, gwo_ref, gwi_ref, gwf_ref, gsmall_ref, gbi_ref, low_ref, u_ref, du_ref):
    small = lambda index: small_ref[pl.ds(index, 1)]
    for place in pieces(SEQ):
        dz = dz_ref[place].astype(F32)
        unit = n2_ref[place]
        gsmall_ref[3] += fold(dz * unit)
        gsmall_ref[7] += fold(dz)
        dr = normal_back(dz, unit, inv_ref[place, pl.ds(HD, 1)], small(3))
        dr_ref[place] = dr
        df = dr.astype(LOW)
        low_ref[place] = df
        gsmall_ref[6] += fold(df.astype(F32))
    columns = 256
    count = wi_ref.shape[1] // columns

    def back(step):
        u_ref[step % 2] = dot_nt(low_ref[...], wf_ref[pl.ds(step * columns, columns)])

    back(0)
    for step in range(count):
        if step + 1 < count:
            back(step + 1)
        lanes = pl.ds(step * columns, columns)
        gwf_ref[:, lanes] += dot_tn(low_ref[...], gb_ref[:, lanes])
        for place in pieces(SEQ):
            du = (u_ref[step % 2, place] * gp_ref[place, lanes].astype(F32)).astype(LOW)
            du_ref[place, lanes] = du
            gbi_ref[:, lanes] += fold(du.astype(F32))
        gwi_ref[:, lanes] += dot_tn(yb_ref[...], du_ref[:, lanes])
    u_ref[0] = dot_nt(du_ref[...], wi_ref[...])
    for place in pieces(SEQ):
        dy = dr_ref[place] + u_ref[0, place]
        unit = n1_ref[place]
        gsmall_ref[2] += fold(dy * unit)
        gsmall_ref[5] += fold(dy)
        dr = normal_back(dy, unit, inv_ref[place, pl.ds(0, 1)], small(2))
        dr_ref[place] = dr
        da = dr.astype(LOW)
        low_ref[place] = da
        gsmall_ref[4] += fold(da.astype(F32))
    gwo_ref[...] += dot_tn(ob_ref[...], low_ref[...])
    dob_ref[...] = dot_nt(low_ref[...], wo_ref[...]).astype(LOW)


def attention_backward(row, lengths_ref, x, dob_ref, ob_ref, qa_ref, ka_ref, va_ref, wq_ref, dr_ref, dx_ref, gwq_ref, gbias_ref, da_ref, p_ref, ds_ref, s_ref, dqkv_ref, dq_ref, pad_ref):
    width = HEADS * HD
    half = SEQ // 2
    low_half, slot = lane_facts(PIECE)
    for start in range(0, SEQ, PIECE):
        place = pl.ds(start, PIECE)
        segment, pad, last = segments(lengths_ref, row, start, PIECE)
        pad_ref[place] = pad
        for pair in range(HEADS // 2):
            lanes = pl.ds(pair * PAIR, PAIR)
            dob = dob_ref[place, lanes].astype(F32)
            product = dob * ob_ref[place, lanes].astype(F32)
            even = jnp.sum(jnp.where(low_half, product, 0.0), -1, keepdims=True)
            odd = jnp.sum(jnp.where(low_half, 0.0, product), -1, keepdims=True)
            first, second, third = three_parts(jnp.where(low_half, odd, even))
            aug = jnp.where(
                slot == 0, -first, jnp.where(slot == 1, -second, jnp.where(slot == 2, -third, 0.0))
            )
            da_ref[2 * pair, place] = jnp.where(low_half, dob, aug).astype(LOW)
            da_ref[2 * pair + 1, place] = jnp.where(low_half, aug, dob).astype(LOW)
    units = [(head, part) for head in range(HEADS) for part in range(2)]

    def scores(unit):
        head, part = units[unit]
        keys = pl.ds(part * half, half)
        s_ref[0, unit % 2] = dot_nt(ka_ref[head, keys], qa_ref[head])
        s_ref[1, unit % 2] = dot_nt(va_ref[head, keys], da_ref[head])

    def weigh(unit):
        for place in pieces(half):
            p = jnp.exp(s_ref[0, unit % 2, place])
            p_ref[unit % 2, place] = p.astype(LOW)
            ds_ref[unit % 2, place] = (p * s_ref[1, unit % 2, place]).astype(LOW)

    scores(0)
    for unit in range(len(units)):
        if unit + 1 < len(units):
            scores(unit + 1)
        weigh(unit)
        head, part = units[unit]
        keys = pl.ds(part * half, half)
        side = head % 2
        dq_ref[1, side, keys] = dot_nn(ds_ref[unit % 2], qa_ref[head])
        dq_ref[2, side, keys] = dot_nn(p_ref[unit % 2], da_ref[head])
        dq = dot_tn(ds_ref[unit % 2], ka_ref[head, keys])
        if part:
            dq_ref[0, side] += dq
        else:
            dq_ref[0, side] = dq
        if side and part:
            pair = head // 2
            for start in range(0, SEQ, PIECE):
                place = pl.ds(start, PIECE)
                dq = jnp.where(low_half, dq_ref[0, 0, place], dq_ref[0, 1, place]) * HD**-0.5
                dk = jnp.where(low_half, dq_ref[1, 0, place], dq_ref[1, 1, place])
                dv = jnp.where(low_half, dq_ref[2, 0, place], dq_ref[2, 1, place])
                dv = dv + pad_ref[place] * dob_ref[place, pl.ds(pair * PAIR, PAIR)].astype(F32)
                for block, value in enumerate((dq, dk, dv)):
                    lanes = pl.ds(block * width + pair * PAIR, PAIR)
                    value = value.astype(LOW)
                    dqkv_ref[place, lanes] = value
                    if block != 1:
                        into = pl.ds(pair * PAIR, PAIR)
                        gbias_ref[block // 2, :, into] += fold(value.astype(F32))
    gwq_ref[...] += dot_tn(x, dqkv_ref[...])
    dx_ref[...] = (dr_ref[...] + dot_nt(dqkv_ref[...], wq_ref[...])).astype(dx_ref.dtype)


def unpack_matrix(raw_ref, at, into_ref):
    width = into_ref.shape[0]
    for start in range(0, into_ref.shape[1], width):
        block = raw_ref[:, :, pl.ds(at + start, width)].astype(F32)
        block = block.reshape(GROUPS + (width,)).swapaxes(0, 1).reshape(width, width)
        into_ref[:, pl.ds(start, width)] = block.astype(LOW)


def unpack_stacked(raw_ref, at, into_ref):
    width = into_ref.shape[1]
    count = into_ref.shape[0] // width
    blocks = [
        raw_ref[:, :, pl.ds(at + step * width, width)].astype(F32).reshape(GROUPS + (width,))
        for step in range(count)
    ]
    outer, inner, rows = GROUPS
    for place in range(inner):
        part = jnp.stack([jnp.stack([block[f, place] for block in blocks]) for f in range(outer)])
        size = outer * count * rows
        into_ref[pl.ds(place * size, size)] = part.reshape(size, width).astype(LOW)


def sources(rows, columns):
    line = lax.broadcasted_iota(jnp.int32, (rows, columns), 0)
    outer, inner, height = GROUPS
    device = (line // height) % inner * outer + line // (inner * height)
    return device, line % height


def unpack_vectors(raw_ref, at, layer):
    outer, inner, rows = GROUPS
    total = outer * inner * rows
    raw = raw_ref[:, :, pl.ds(at, 128)].reshape(total, 128)
    lane = lax.broadcasted_iota(jnp.int32, (128, total), 0)
    column = lax.broadcasted_iota(jnp.int32, (128, total), 1)
    pick = jnp.where(lane == rows * layer + column % rows, 1.0, 0.0).astype(LOW)
    spread = dot_nn(raw, pick)
    device, unused = sources(total, total)
    column = lax.broadcasted_iota(jnp.int32, (total, total), 1)
    spread = jnp.where(column // rows == device, spread, 0.0)
    return jnp.sum(spread.reshape(outer * inner, rows, total), 0)


def unpack_hidden(raw_ref, at, layer, hidden):
    outer, inner, rows = GROUPS
    total = outer * inner * rows
    height = hidden // (outer * inner)
    raw = raw_ref[:, :, pl.ds(at, 128)].reshape(total, 128)
    lane = lax.broadcasted_iota(jnp.int32, (128, hidden), 0)
    column = lax.broadcasted_iota(jnp.int32, (128, hidden), 1)
    pick = jnp.where(lane == 2 * rows + column % height, 1.0, 0.0).astype(LOW)
    spread = dot_nn(raw, pick)
    device, within = sources(total, hidden)
    column = lax.broadcasted_iota(jnp.int32, (total, hidden), 1)
    spread = jnp.where((column // height == device) & (within == layer), spread, 0.0)
    return jnp.sum(spread, 0, keepdims=True)


def pack_matrix(sum_ref, sent_ref, at):
    width = sum_ref.shape[0]
    outer, inner, rows = GROUPS
    for start in range(0, sum_ref.shape[1], width):
        block = sum_ref[:, pl.ds(start, width)].reshape(inner, outer, rows, width)
        block = block.swapaxes(0, 1).reshape(outer, inner * rows, width)
        sent_ref[:, :, pl.ds(at + start, width)] = block.astype(LOW)


def pack_stacked(sum_ref, sent_ref, at):
    width = sum_ref.shape[0]
    outer, inner, rows = GROUPS
    count = sum_ref.shape[1] // width
    near = inner // count
    for step in range(count):
        block = sum_ref[:, pl.ds(step * width, width)].T
        block = block.reshape(near, outer, count, rows, width)
        for part in range(count):
            piece = jnp.stack([block[:, f, part] for f in range(outer)])
            piece = piece.reshape(outer, near * rows, width)
            sent_ref[:, pl.ds(step * near * rows, near * rows), pl.ds(at + part * width, width)] = (
                piece.astype(LOW)
            )


def pack_shared(block, sent_ref, at):
    outer, inner, rows = GROUPS
    columns = block.shape[1]
    block = jnp.broadcast_to(block[None], (outer * inner, rows, columns))
    sent_ref[:, :, pl.ds(at, columns)] = block.reshape(outer, inner * rows, columns).astype(LOW)


def pack_attention(gwq_ref, gbias_ref, sent_ref, at):
    pack_matrix(gwq_ref, sent_ref, at)
    width = gwq_ref.shape[0]
    line = lax.broadcasted_iota(jnp.int32, (8, width), 0)
    sums = [jnp.sum(gbias_ref[index], 0, keepdims=True) for index in range(2)]
    block = jnp.where(line == 0, sums[0], jnp.where(line == 1, sums[1], 0.0))
    pack_shared(block, sent_ref, at + 3 * width)


def pack_dense(gwo_ref, gwi_ref, gwf_ref, gsmall_ref, gbi_ref, sent_ref, at):
    width, hidden = gwi_ref.shape
    pack_matrix(gwo_ref, sent_ref, at)
    pack_matrix(gwi_ref, sent_ref, at + width)
    pack_stacked(gwf_ref, sent_ref, at + width + hidden)
    at = at + width + 2 * hidden
    pack_shared(jnp.sum(gsmall_ref[...], 1), sent_ref, at)
    line = jnp.sum(gbi_ref[...], 0, keepdims=True)
    size = hidden // 8
    block = jnp.concatenate([line[:, step * size : (step + 1) * size] for step in range(8)], 0)
    pack_shared(block, sent_ref, at + width)


def shape_of(array):
    return jax.ShapeDtypeStruct(array.shape, array.dtype)


def by_row(shape):
    if len(shape) == 2:
        return pl.BlockSpec((SEQ, shape[1]), lambda row: (row, 0))
    return pl.BlockSpec((None,) + tuple(shape[1:]), lambda row: (row,) + (0,) * (len(shape) - 1))


def whole(shape):
    return pl.BlockSpec(tuple(shape), lambda row: (0,) * len(shape))


def run_rows(body, lengths, rowwise, fixed, row_outs, sent, scratch, cost, setup, finish, after=()):
    count = lengths.shape[0]
    cuts = [len(rowwise), len(fixed), len(after), len(row_outs), len(sent), len(scratch)]

    def kernel(lengths_ref, *refs):
        row = pl.program_id(0)
        groups = []
        at = 0
        for cut in cuts:
            groups.append(refs[at : at + cut])
            at += cut
        rows_in, fixed_in, unused, rows_out, sent_out, work = groups

        @pl.when(row == 0)
        def _():
            setup(fixed_in, work)

        body(row, lengths_ref, rows_in, rows_out, work)

        if sent:

            @pl.when(row == count - 1)
            def _():
                finish(work, sent_out[0])

    return pl.pallas_call(
        kernel,
        grid=(count,),
        in_specs=[pl.BlockSpec(memory_space=pltpu.SMEM)]
        + [by_row(array.shape) for array in rowwise]
        + [whole(array.shape) for array in fixed]
        + [pl.BlockSpec(memory_space=pl.ANY) for array in after],
        out_specs=[by_row(part.shape) for part in row_outs] + [whole(part.shape) for part in sent],
        out_shape=list(row_outs) + list(sent),
        scratch_shapes=list(scratch),
        compiler_params=pltpu.CompilerParams(
            dimension_semantics=("arbitrary",), vmem_limit_bytes=MEMORY
        ),
        cost_estimate=pl.CostEstimate(flops=cost, bytes_accessed=8 * 2**20, transcendentals=0),
    )(lengths, *rowwise, *fixed, *after)


def struct(shape, dtype):
    return jax.ShapeDtypeStruct(tuple(shape), dtype)


FORWARD_SCRATCH = lambda: [
    pltpu.VMEM((2, SEQ // 2, SEQ), F32),
    pltpu.VMEM((2, SEQ // 2, SEQ), LOW),
    pltpu.VMEM((2, SEQ, PAIR), F32),
    pltpu.VMEM((SEQ, PAIR), F32),
    pltpu.VMEM((3, HEADS // 2, SEQ, PAIR), F32),
    pltpu.VMEM((SEQ, PAIR), F32),
]
BACKWARD_SCRATCH = lambda: [
    pltpu.VMEM((HEADS, SEQ, PAIR), LOW),
    pltpu.VMEM((2, SEQ // 2, SEQ), LOW),
    pltpu.VMEM((2, SEQ // 2, SEQ), LOW),
    pltpu.VMEM((2, 2, SEQ // 2, SEQ), F32),
    pltpu.VMEM((SEQ, 3 * HEADS * HD), LOW),
    pltpu.VMEM((3, 2, SEQ, PAIR), F32),
    pltpu.VMEM((SEQ, PAIR), F32),
]


def attention_outs(rows, tokens, width):
    heads = (rows, HEADS, SEQ, PAIR)
    return [struct(heads, LOW)] * 3 + [struct((tokens, width), LOW)]


def dense_outs(tokens, width, hidden):
    return [
        struct((tokens, width), F32),
        struct((tokens, width), F32),
        struct((tokens, PAIR), F32),
        struct((tokens, width), LOW),
        struct((tokens, hidden), LOW),
        struct((tokens, hidden), LOW),
    ]


def vmem(shape, dtype):
    return pltpu.VMEM(tuple(shape), dtype)


def attention_weights(width):
    return [vmem((width, 3 * width), LOW), vmem((1, 3 * width), F32)]


def dense_weights(width, hidden):
    return [
        vmem((width, width), LOW),
        vmem((width, hidden), LOW),
        vmem((hidden, width), LOW),
        vmem((8, width), F32),
        vmem((1, hidden), F32),
    ]


def dense_sums(width, hidden):
    return [
        vmem((width, width), F32),
        vmem((width, hidden), F32),
        vmem((width, hidden), F32),
        vmem((8, 8, width), F32),
        vmem((8, hidden), F32),
    ]


def attention_sums(width):
    return [vmem((width, 3 * width), F32), vmem((2, 8, width), F32)]


def dense_work(width, hidden):
    return [vmem((SEQ, width), LOW), vmem((2, SEQ, width), F32), vmem((SEQ, hidden), LOW)]


def set_attention(layer, urgent_ref, raw_ref, at, wq_ref, bias_ref):
    width = wq_ref.shape[0]
    unpack_matrix(raw_ref, at, wq_ref)
    vectors = unpack_vectors(urgent_ref, 3 * width, layer)
    bias_ref[:, :width] = vectors[0:1]
    bias_ref[:, width : 2 * width] = jnp.zeros((1, width), F32)
    bias_ref[:, 2 * width :] = vectors[1:2]


def set_dense(layer, urgent_ref, raw_ref, at, wo_ref, wi_ref, wf_ref, small_ref, bi_ref):
    width, hidden = wi_ref.shape
    unpack_matrix(raw_ref, at, wo_ref)
    unpack_matrix(raw_ref, at + width, wi_ref)
    unpack_stacked(raw_ref, at + width + hidden, wf_ref)
    small_ref[...] = unpack_vectors(urgent_ref, 3 * width, layer)
    bi_ref[...] = unpack_hidden(urgent_ref, 3 * width, layer, hidden)


def clear(refs):
    for ref in refs:
        ref[...] = jnp.zeros(ref.shape, ref.dtype)


def attention_kernel(layer, lengths, x, urgent, raw, at):
    rows, (tokens, width) = lengths.shape[0], x.shape

    def setup(fixed, work):
        set_attention(layer, fixed[0], fixed[-1], at, *work[:2])

    def body(row, lengths_ref, rowwise, outs, work):
        attention_forward(row, lengths_ref, rowwise[0][...].astype(LOW), *work[:2], *outs, *work[2:])

    fixed = [urgent] if raw is urgent else [urgent, raw]
    return run_rows(
        body, lengths, [x], fixed, attention_outs(rows, tokens, width), [],
        attention_weights(width) + FORWARD_SCRATCH(), 4 * 10**9, setup, None,
    )


def dense_kernel(layer, lengths, x, ob, urgent, raw, at, hidden):
    tokens, width = x.shape

    def setup(fixed, work):
        set_dense(layer, *fixed, at, *work[:5])

    def body(row, lengths_ref, rowwise, outs, work):
        dense_forward(*rowwise, *work[:5], *outs, *work[5:])

    return run_rows(
        body, lengths, [x, ob], [urgent, raw],
        dense_outs(tokens, width, hidden) + [struct((tokens, width), F32)], [],
        dense_weights(width, hidden) + [vmem((SEQ, width), F32), vmem((2, SEQ, width), F32)],
        5 * 10**9, setup, None,
    )


def turn_kernel(layer, lengths, x, ob, cotangent, urgent, raw, at, hidden):
    tokens, width = x.shape
    columns = width + 2 * hidden + width + hidden // 8

    def setup(fixed, work):
        set_dense(layer, *fixed, at, *work[:5])
        clear(work[5:10])

    def body(row, lengths_ref, rowwise, outs, work):
        x_ref, ob_ref, dz_ref = rowwise
        z_ref, dr_ref, dob_ref = outs
        weights, sums, kept = work[:5], work[5:10], work[10:16]
        work_ref, low_ref, u_ref, du_ref = work[16:]
        dense_forward(x_ref, ob_ref, *weights, *kept, z_ref, work_ref, u_ref)
        dense_backward(
            dz_ref, *kept, ob_ref, *weights[:4], dr_ref, dob_ref, *sums, low_ref, u_ref, du_ref
        )

    def finish(work, sent_ref):
        pack_dense(*work[5:10], sent_ref, 0)

    kept = [vmem((SEQ,) + part.shape[1:], part.dtype) for part in dense_outs(tokens, width, hidden)]
    return run_rows(
        body, lengths, [x, ob, cotangent], [urgent, raw],
        [struct((tokens, width), LOW), struct((tokens, width), F32), struct((tokens, width), LOW)],
        [struct((4, 64, columns), LOW)],
        dense_weights(width, hidden) + dense_sums(width, hidden) + kept
        + [vmem((SEQ, width), F32)] + dense_work(width, hidden),
        10**10, setup, finish,
    )


def middle_kernel(lengths, upper, lower, urgent, raw1, raw0, hidden, after):
    tokens, width = upper[0].shape
    columns = 4 * width + width + 2 * hidden + width + hidden // 8

    def setup(fixed, work):
        urgent_ref, raw1_ref, raw0_ref = fixed
        set_attention(1, urgent_ref, raw1_ref, 0, *work[:2])
        set_dense(0, urgent_ref, raw0_ref, 0, *work[2:7])
        clear(work[7:14])

    def body(row, lengths_ref, rowwise, outs, work):
        up, low = rowwise[:7], rowwise[7:]
        dr_ref, dob_ref = outs
        dx_ref, low_ref, u_ref, du_ref = work[14:18]
        attention_backward(
            row, lengths_ref, up[0][...].astype(LOW), *up[1:6], work[0], up[6], dx_ref,
            *work[7:9], *work[18:],
        )
        dense_backward(
            dx_ref, *low, *work[2:6], dr_ref, dob_ref, *work[9:14], low_ref, u_ref, du_ref
        )

    def finish(work, sent_ref):
        pack_attention(*work[7:9], sent_ref, 0)
        pack_dense(*work[9:14], sent_ref, 4 * width)

    return run_rows(
        body, lengths, list(upper) + list(lower), [urgent, raw1, raw0],
        [struct((tokens, width), F32), struct((tokens, width), LOW)],
        [struct((4, 64, columns), LOW)],
        attention_weights(width) + dense_weights(width, hidden)
        + attention_sums(width) + dense_sums(width, hidden)
        + [vmem((SEQ, width), F32)] + dense_work(width, hidden) + BACKWARD_SCRATCH(),
        15 * 10**9, setup, finish, after,
    )


def last_kernel(lengths, upper, urgent, after):
    tokens, width = upper[0].shape

    def setup(fixed, work):
        set_attention(0, fixed[0], fixed[0], 0, *work[:2])
        clear(work[2:4])

    def body(row, lengths_ref, rowwise, outs, work):
        attention_backward(
            row, lengths_ref, rowwise[0][...], *rowwise[1:6], work[0], rowwise[6], outs[0],
            *work[2:4], *work[4:],
        )

    def finish(work, sent_ref):
        pack_attention(*work[2:4], sent_ref, 0)

    return run_rows(
        body, lengths, list(upper), [urgent], [struct((tokens, width), LOW)],
        [struct((4, 64, 4 * width), LOW)],
        attention_weights(width) + attention_sums(width) + BACKWARD_SCRATCH(),
        8 * 10**9, setup, finish, after,
    )


def simple_call(kernel, out_shape, *operands, after=()):
    return pl.pallas_call(
        kernel,
        in_specs=[pl.BlockSpec(memory_space=pltpu.VMEM)] * len(operands)
        + [pl.BlockSpec(memory_space=pl.ANY)] * len(after),
        out_shape=out_shape,
        compiler_params=pltpu.CompilerParams(vmem_limit_bytes=MEMORY),
    )(*operands, *after)


def pack_parameters(attn_weight, small, out_weight, ffn_in, ffn_out):
    depth, rows, width = out_weight.shape
    copies = GROUPS[1]
    hidden = ffn_in.shape[2]
    columns = depth * (4 * width + 2 * hidden) + 128

    def kernel(wq_ref, small_ref, wo_ref, wi_ref, wf_ref, out_ref):
        def put(block, at):
            block = jnp.broadcast_to(block.astype(F32)[None], (copies,) + block.shape)
            block = block.reshape(copies * block.shape[1], block.shape[2])
            out_ref[:, pl.ds(at, block.shape[1])] = block.astype(LOW)

        put(wq_ref[0], 0)
        put(small_ref[...], 3 * width)
        at = 3 * width + 128
        for layer in range(depth):
            if layer:
                put(wq_ref[layer], at)
                at += 3 * width
            put(wo_ref[layer], at)
            put(wi_ref[layer], at + width)
            at += width + hidden
            down = wf_ref[layer].astype(F32)
            for step in range(hidden // width):
                put(down[step * rows : (step + 1) * rows], at)
                at += width

    return simple_call(
        kernel, struct((copies * rows, columns), LOW), attn_weight, small, out_weight, ffn_in, ffn_out
    )


def add_parts(received, after):
    def kernel(in_ref, *refs):
        columns = 256
        for start in range(0, in_ref.shape[2], columns):
            size = min(columns, in_ref.shape[2] - start)
            lanes = pl.ds(start, size)
            refs[-1][:, lanes] = jnp.sum(in_ref[:, :, lanes].astype(F32), 0).astype(LOW)

    return simple_call(kernel, struct(received.shape[1:], LOW), received, after=after)


def write_gradients(place, tail, middle, head, depth, width, hidden):
    rows = GROUPS[2]
    height = hidden // DEVICES

    def kernel(place_ref, tail_ref, middle_ref, head_ref, gwq_ref, gab_ref, gwo_ref, gwi_ref, gbi_ref, gwf_ref, gain_ref, shift_ref):
        spot = place_ref[0]

        def total(ref, at, columns):
            block = ref[:, pl.ds(at, columns)].astype(F32)
            return jnp.sum(block.reshape(-1, rows, columns), 0)

        def own(block, size):
            return pltpu.roll(block, block.shape[1] - spot * size, 1)

        for layer, ref, at in ((0, head_ref, 0), (1, middle_ref, 0)):
            gwq_ref[layer] = total(ref, at, 3 * width)
            gab_ref[layer] = own(total(ref, at + 3 * width, width), rows)[0:2, 0:rows]
        for layer, ref, at in ((0, middle_ref, 4 * width), (1, tail_ref, 0)):
            gwo_ref[layer] = total(ref, at, width)
            gwi_ref[layer] = total(ref, at + width, hidden)
            for step in range(hidden // width):
                gwf_ref[layer, pl.ds(step * rows, rows)] = total(
                    ref, at + width + hidden + step * width, width
                )
            at += width + 2 * hidden
            small = own(total(ref, at, width), rows)
            gain_ref[layer] = small[2:4, 0:rows]
            shift_ref[layer] = small[4:8, 0:rows]
            line = total(ref, at + width, hidden // 8)
            line = jnp.concatenate([line[step : step + 1] for step in range(8)], 1)
            gbi_ref[pl.ds(layer, 1)] = own(line, height)[:, 0:height]

    outs = [
        struct((depth, rows, 3 * width), F32),
        struct((depth, 2, rows), F32),
        struct((depth, rows, width), F32),
        struct((depth, rows, hidden), F32),
        struct((depth, height), F32),
        struct((depth, height, width), F32),
        struct((depth, 2, rows), F32),
        struct((depth, 4, rows), F32),
    ]
    return pl.pallas_call(
        kernel,
        in_specs=[pl.BlockSpec(memory_space=pltpu.SMEM)] + [pl.BlockSpec(memory_space=pltpu.VMEM)] * 3,
        out_shape=outs,
        compiler_params=pltpu.CompilerParams(vmem_limit_bytes=MEMORY),
    )(place, tail, middle, head)


def exchange(parts, axis):
    return lax.all_to_all(parts, axis, 0, 0, tiled=True)


def local(
    hidden_in,
    lengths,
    grad_out,
    attn_weight,
    attn_bias,
    out_weight,
    ffn_in,
    ffn_in_bias,
    ffn_out,
    norm_gain,
    shifts,
):
    depth, rows, width = out_weight.shape
    hidden = ffn_in.shape[2]
    first, second = lax.axis_size("dp"), lax.axis_size("fsdp")
    fits = (second, first, rows) == GROUPS
    urgent_size = 3 * width + 128
    later_size = width + 2 * hidden
    if fits:
        small = jnp.concatenate([attn_bias, norm_gain, shifts], 1)
        small = small.transpose(1, 0, 2).reshape(8, depth * rows)
        line = jnp.pad(ffn_in_bias, ((0, 8 - depth), (0, 0)))
        small = jnp.concatenate([small, line], 1)
        small = jnp.pad(small, ((0, 0), (0, 128 - small.shape[1])))
        packed = pack_parameters(attn_weight, small, out_weight, ffn_in, ffn_out)
        held = exchange(packed, "dp")
        urgent = held[:, :urgent_size]
        urgent = exchange(jnp.broadcast_to(urgent[None], (second,) + urgent.shape), "fsdp")
        raw0 = lax.all_gather(held[:, urgent_size : urgent_size + later_size], "fsdp")
        raw1 = lax.all_gather(held[:, urgent_size + later_size :], "fsdp")
    else:
        urgent, raw0, raw1 = gather_other(
            attn_weight, attn_bias, out_weight, ffn_in, ffn_in_bias, ffn_out, norm_gain, shifts
        )

    qa0, ka0, va0, ob0 = attention_kernel(0, lengths, hidden_in, urgent, urgent, 0)
    n1, n2, inv, yb, gb, gp, z0 = dense_kernel(0, lengths, hidden_in, ob0, urgent, raw0, 0, hidden)
    qa1, ka1, va1, ob1 = attention_kernel(1, lengths, z0, urgent, raw1, 0)
    hidden_out, dr1, dob1, sent_a = turn_kernel(
        1, lengths, z0, ob1, grad_out, urgent, raw1, 3 * width, hidden
    )
    dr0, dob0, sent_b = middle_kernel(
        lengths,
        (z0, dob1, ob1, qa1, ka1, va1, dr1),
        (n1, n2, inv, yb, gb, gp, ob0),
        urgent,
        raw1,
        raw0,
        hidden,
        (sent_a,),
    )
    grad_in, sent_c = last_kernel(
        lengths, (hidden_in, dob0, ob0, qa0, ka0, va0, dr0), urgent, (sent_b,)
    )
    if fits:
        tail = add_parts(exchange(sent_a, "fsdp"), (sent_b,))
        tail = exchange(tail, "dp")
        middle = add_parts(exchange(sent_b, "fsdp"), (sent_c,))
        middle = exchange(middle, "dp")
        head = add_parts(exchange(sent_c, "fsdp"), ())
        head = exchange(head, "dp")
        place = lax.axis_index(("dp", "fsdp")).astype(jnp.int32).reshape(1)
        grads = write_gradients(place, tail, middle, head, depth, width, hidden)
    else:
        grads = scatter_other(sent_a, sent_b, sent_c, rows, width, hidden)
    return (hidden_out, grad_in, *grads)


def gather_other(
    attn_weight, attn_bias, out_weight, ffn_in, ffn_in_bias, ffn_out, norm_gain, shifts
):
    axes = ("dp", "fsdp")
    gather = lambda part, axis: lax.all_gather(part, axes, axis=axis, tiled=True)
    depth, unused, width = out_weight.shape
    hidden = ffn_in.shape[2]
    outer, inner, rows = GROUPS
    vectors = gather(jnp.concatenate([attn_bias, norm_gain, shifts], 1), 2)
    line = gather(ffn_in_bias, 1)

    def order(natural):
        return (
            natural.reshape(inner, outer, rows, -1).swapaxes(0, 1).reshape(outer, inner * rows, -1)
        )

    def stacked(part):
        part = part.reshape(DEVICES, -1, rows, width)
        return order(part.swapaxes(1, 2).reshape(width, -1))

    small = vectors.reshape(depth, 8, DEVICES, rows).transpose(2, 1, 0, 3).reshape(width, -1)
    line = line.reshape(depth, DEVICES, -1).swapaxes(0, 1)
    line = jnp.pad(line, ((0, 0), (0, 8 - depth), (0, 0))).reshape(width, -1)
    small = jnp.concatenate([small, line], 1)
    small = jnp.pad(small, ((0, 0), (0, 128 - small.shape[1])))
    wq, wo, wi, wf = (gather(part, 1) for part in (attn_weight, out_weight, ffn_in, ffn_out))
    urgent = jnp.concatenate([order(wq[0]), order(small)], 2)
    raw0 = jnp.concatenate([order(wo[0]), order(wi[0]), stacked(wf[0])], 2)
    raw1 = jnp.concatenate([order(wq[1]), order(wo[1]), order(wi[1]), stacked(wf[1])], 2)
    return urgent, raw0, raw1


def scatter_other(sent_a, sent_b, sent_c, own_rows, width, hidden):
    outer, inner, rows = GROUPS
    axes = ("dp", "fsdp")

    def natural(part):
        return part.reshape(outer, inner, rows, -1).swapaxes(0, 1).reshape(width, -1).astype(F32)

    def cut(part, sizes):
        found, at = [], 0
        for size in sizes:
            found.append(part[:, at : at + size])
            at += size
        return found

    dense = [width, hidden, hidden, width, hidden // 8]
    attention = [3 * width, width]
    wq0, ab0 = cut(natural(sent_c), attention)
    wq1, ab1, wo0, wi0, wf0, small0, bi0 = cut(natural(sent_b), attention + dense)
    wo1, wi1, wf1, small1, bi1 = cut(natural(sent_a), dense)

    def stacked(part):
        part = part.reshape(DEVICES, rows, -1, width).swapaxes(1, 2)
        return part.reshape(hidden, width)

    def spread(parts, axis):
        return lax.psum_scatter(jnp.stack(parts), axes, scatter_dimension=axis, tiled=True)

    return (
        spread([wq0, wq1], 1),
        spread([ab0[:2], ab1[:2]], 2),
        spread([wo0, wo1], 1),
        spread([wi0, wi1], 1),
        spread([bi0[:8].reshape(-1), bi1[:8].reshape(-1)], 1),
        spread([stacked(wf0), stacked(wf1)], 1),
        spread([small0[2:4], small1[2:4]], 2),
        spread([small0[4:8], small1[4:8]], 2),
    )


def solution(mesh):
    placed = (
        P(("dp", "fsdp"), None),
        P(("dp", "fsdp"), None),
        P(("dp", "fsdp"), None),
        P(None, ("dp", "fsdp"), None),
        P(None, None, ("dp", "fsdp")),
        P(None, ("dp", "fsdp"), None),
        P(None, ("dp", "fsdp"), None),
        P(None, ("dp", "fsdp")),
        P(None, ("dp", "fsdp"), None),
        P(None, None, ("dp", "fsdp")),
        P(None, None, ("dp", "fsdp")),
    )
    return jax.shard_map(
        local,
        mesh=mesh,
        in_specs=placed,
        out_specs=(
            P(("dp", "fsdp"), None),
            P(("dp", "fsdp"), None),
            P(None, ("dp", "fsdp"), None),
            P(None, None, ("dp", "fsdp")),
            P(None, ("dp", "fsdp"), None),
            P(None, ("dp", "fsdp"), None),
            P(None, ("dp", "fsdp")),
            P(None, ("dp", "fsdp"), None),
            P(None, None, ("dp", "fsdp")),
            P(None, None, ("dp", "fsdp")),
        ),
        check_vma=False,
    )
```

```python
from functools import partial

import jax
import jax.numpy as jnp
from jax import lax
from jax.experimental import pallas as pl
from jax.experimental.pallas import tpu as pltpu
from jax.sharding import PartitionSpec as P

HEADS = 4
HD = 64
SEQ = 512
PAIR = 2 * HD
FAR = -(2.0**100)
FLOOR = -1e20
EPSILON = 1e-12
PIECE = 64
GROUPS = (4, 8, 8)
DEVICES = 32
LOW = jnp.bfloat16
F32 = jnp.float32
MEMORY = 60 * 2**20


def dot_nn(left, right):
    return lax.dot_general(left, right, (((1,), (0,)), ((), ())), preferred_element_type=F32)


def dot_nt(left, right):
    return lax.dot_general(left, right, (((1,), (1,)), ((), ())), preferred_element_type=F32)


def dot_tn(left, right):
    return lax.dot_general(left, right, (((0,), (0,)), ((), ())), preferred_element_type=F32)


def pieces(total, size=PIECE):
    return [pl.ds(start, size) for start in range(0, total, size)]


def three_parts(values):
    first = values.astype(LOW).astype(F32)
    rest = values - first
    second = rest.astype(LOW).astype(F32)
    return first, second, rest - second


def gelu_parts(u):
    bell = jnp.exp(u * u * -0.5)
    t = 1.0 / (1.0 + (0.3275911 * 0.5**0.5) * jnp.abs(u))
    poly = t * (
        0.127414796
        + t * (-0.142248368 + t * (0.7107068705 + t * (-0.7265760135 + t * 0.5307027145)))
    )
    tail = poly * bell
    cumulative = jnp.where(u > 0, 1.0 - tail, tail)
    return u * cumulative, cumulative + u * bell * 0.3989422804014327


def lane_facts(rows):
    lane = lax.broadcasted_iota(jnp.int32, (rows, PAIR), 1)
    return lane < HD, lane % HD


def segments(lengths_ref, row, start, rows):
    places = lax.broadcasted_iota(jnp.int32, (rows, PAIR), 0) + start
    bound = jnp.int32(0)
    segment = jnp.zeros((rows, PAIR), jnp.int32)
    last = lengths_ref.shape[1] - 1
    for entry in range(last):
        bound = bound + lengths_ref[row, entry]
        segment = segment + (places >= bound).astype(jnp.int32)
    return segment, (segment == last).astype(F32), last


def attention_forward(row, lengths_ref, x, wq_ref, bias_ref, qa_ref, ka_ref, va_ref, ob_ref, s_ref, p_ref, m_ref, pad_ref, q_ref, aug_ref):
    width = HEADS * HD
    for block in range(3):
        for pair in range(HEADS // 2):
            at = block * width + pair * PAIR
            q_ref[block, pair] = dot_nn(x, wq_ref[:, at : at + PAIR]) + bias_ref[:, at : at + PAIR]
    for start in range(0, SEQ, PIECE):
        place = pl.ds(start, PIECE)
        low_half, slot = lane_facts(PIECE)
        segment, pad, last = segments(lengths_ref, row, start, PIECE)
        pad_ref[place] = pad
        aug_q = jnp.where(slot == segment, 1.0, 0.0)
        aug_ref[place] = aug_q
        seen = (slot == segment) & (slot != last)
        aug_k = jnp.where(slot <= last, jnp.where(seen, 0.0, FAR), jnp.where(slot <= last + 3, 1.0, 0.0))
        for pair in range(HEADS // 2):
            q = q_ref[0, pair, place] * HD**-0.5
            k = q_ref[1, pair, place]
            v = q_ref[2, pair, place]
            q_ref[0, pair, place] = q
            qa_ref[2 * pair, place] = jnp.where(low_half, q, aug_q).astype(LOW)
            qa_ref[2 * pair + 1, place] = jnp.where(low_half, aug_q, q).astype(LOW)
            ka_ref[2 * pair, place] = jnp.where(low_half, k, aug_k).astype(LOW)
            ka_ref[2 * pair + 1, place] = jnp.where(low_half, aug_k, k).astype(LOW)
            va_ref[2 * pair, place] = jnp.where(low_half, v, 1.0).astype(LOW)
            va_ref[2 * pair + 1, place] = jnp.where(low_half, 1.0, v).astype(LOW)
    half = SEQ // 2
    units = [(head, part) for head in range(HEADS) for part in range(2)]

    def scores(unit):
        head, part = units[unit]
        s_ref[unit % 2] = dot_nt(qa_ref[head, pl.ds(part * half, half)], ka_ref[head])

    def softmax(unit):
        head, part = units[unit]
        for start in range(0, half, PIECE):
            s = s_ref[unit % 2, pl.ds(start, PIECE)]
            highest = jnp.maximum(jnp.max(s, -1, keepdims=True), FLOOR)
            p_ref[unit % 2, pl.ds(start, PIECE)] = jnp.exp(s - highest).astype(LOW)
            m_ref[head % 2, pl.ds(part * half + start, PIECE)] = jnp.broadcast_to(highest, (PIECE, PAIR))

    def attend(unit):
        head, part = units[unit]
        return dot_nn(p_ref[unit % 2], va_ref[head])

    sums = {}
    scores(0)
    for unit in range(len(units)):
        if unit + 1 < len(units):
            scores(unit + 1)
        softmax(unit)
        head, part = units[unit]
        q_ref[1, head % 2, pl.ds(part * half, half)] = attend(unit)
        if head % 2 and part:
            pair = head // 2
            for start in range(0, SEQ, PIECE):
                place = pl.ds(start, PIECE)
                low_half, slot = lane_facts(PIECE)
                even = q_ref[1, 0, place]
                odd = q_ref[1, 1, place]
                pad = pad_ref[place]
                last = lengths_ref.shape[1] - 1
                total = jnp.where(low_half, odd, even) + pad
                top = jnp.where(low_half, odd_even(m_ref, 1, place), odd_even(m_ref, 0, place))
                spread = jnp.where(pad > 0, 0.0, top + jnp.log(total))
                first, second, third = three_parts(spread)
                aug = jnp.where(
                    slot == last + 1,
                    -first,
                    jnp.where(slot == last + 2, -second, jnp.where(slot == last + 3, -third, aug_ref[place])),
                )
                q = q_ref[0, pair, place]
                qa_ref[2 * pair, place] = jnp.where(low_half, q, aug).astype(LOW)
                qa_ref[2 * pair + 1, place] = jnp.where(low_half, aug, q).astype(LOW)
                v = q_ref[2, pair, place].astype(LOW).astype(F32)
                out = jnp.where(low_half, even, odd) / pltpu.roll(total, HD, 1) + pad * v
                ob_ref[place, pl.ds(pair * PAIR, PAIR)] = out.astype(LOW)


def odd_even(ref, which, place):
    return ref[which, place]


def normal(values):
    centred = values - jnp.mean(values, -1, keepdims=True)
    inverse = lax.rsqrt(jnp.mean(centred * centred, -1, keepdims=True) + EPSILON)
    return centred * inverse, inverse


def normal_back(cotangent, unit, inverse, gains):
    scaled = cotangent * gains
    return inverse * (
        scaled
        - jnp.mean(scaled, -1, keepdims=True)
        - unit * jnp.mean(scaled * unit, -1, keepdims=True)
    )


def dense_forward(x_ref, ob_ref, wo_ref, wi_ref, wf_ref, small_ref, bi_ref, n1_ref, n2_ref, inv_ref, yb_ref, gb_ref, gp_ref, z_ref, work_ref, u_ref):
    small = lambda index: small_ref[pl.ds(index, 1)]
    work_ref[...] = dot_nn(ob_ref[...], wo_ref[...])
    for place in pieces(SEQ):
        unit, inverse = normal(x_ref[place].astype(F32) + work_ref[place] + small(4))
        n1_ref[place] = unit
        inv_ref[place, pl.ds(0, HD)] = jnp.broadcast_to(inverse, (PIECE, HD))
        y = unit * small(2) + small(5)
        yb_ref[place] = y.astype(LOW)
        work_ref[place] = y + small(6)
    columns = 256
    count = wi_ref.shape[1] // columns

    def into(step):
        u_ref[step % 2] = dot_nn(yb_ref[...], wi_ref[:, pl.ds(step * columns, columns)])

    into(0)
    for step in range(count):
        if step + 1 < count:
            into(step + 1)
        lanes = pl.ds(step * columns, columns)
        for place in pieces(SEQ):
            g, slope = gelu_parts(u_ref[step % 2, place] + bi_ref[:, lanes])
            gb_ref[place, lanes] = g.astype(LOW)
            gp_ref[place, lanes] = slope.astype(LOW)
    work_ref[...] += dot_nn(gb_ref[...], wf_ref[...])
    for place in pieces(SEQ):
        unit, inverse = normal(work_ref[place])
        n2_ref[place] = unit
        inv_ref[place, pl.ds(HD, HD)] = jnp.broadcast_to(inverse, (PIECE, HD))
        z_ref[place] = (unit * small(3) + small(7)).astype(z_ref.dtype)


def fold(values):
    return jnp.sum(values.reshape(-1, 8, values.shape[-1]), 0)


def dense_backward(dz_ref, n1_ref, n2_ref, inv_ref, yb_ref, gb_ref, gp_ref, ob_ref, wo_ref, wi_ref, wf_ref, small_ref, dr_ref, dob_ref, gwo_ref, gwi_ref, gwf_ref, gsmall_ref, gbi_ref, low_ref, u_ref, du_ref):
    small = lambda index: small_ref[pl.ds(index, 1)]
    for place in pieces(SEQ):
        dz = dz_ref[place].astype(F32)
        unit = n2_ref[place]
        gsmall_ref[3] += fold(dz * unit)
        gsmall_ref[7] += fold(dz)
        dr = normal_back(dz, unit, inv_ref[place, pl.ds(HD, 1)], small(3))
        dr_ref[place] = dr
        df = dr.astype(LOW)
        low_ref[place] = df
        gsmall_ref[6] += fold(df.astype(F32))
    columns = 256
    count = wi_ref.shape[1] // columns

    def back(step):
        u_ref[step % 2] = dot_nt(low_ref[...], wf_ref[pl.ds(step * columns, columns)])

    back(0)
    for step in range(count):
        if step + 1 < count:
            back(step + 1)
        lanes = pl.ds(step * columns, columns)
        gwf_ref[:, lanes] += dot_tn(low_ref[...], gb_ref[:, lanes])
        for place in pieces(SEQ):
            du = (u_ref[step % 2, place] * gp_ref[place, lanes].astype(F32)).astype(LOW)
            du_ref[place, lanes] = du
            gbi_ref[:, lanes] += fold(du.astype(F32))
        gwi_ref[:, lanes] += dot_tn(yb_ref[...], du_ref[:, lanes])
    u_ref[0] = dot_nt(du_ref[...], wi_ref[...])
    for place in pieces(SEQ):
        dy = dr_ref[place] + u_ref[0, place]
        unit = n1_ref[place]
        gsmall_ref[2] += fold(dy * unit)
        gsmall_ref[5] += fold(dy)
        dr = normal_back(dy, unit, inv_ref[place, pl.ds(0, 1)], small(2))
        dr_ref[place] = dr
        da = dr.astype(LOW)
        low_ref[place] = da
        gsmall_ref[4] += fold(da.astype(F32))
    gwo_ref[...] += dot_tn(ob_ref[...], low_ref[...])
    dob_ref[...] = dot_nt(low_ref[...], wo_ref[...]).astype(LOW)


def attention_backward(row, lengths_ref, x, dob_ref, ob_ref, qa_ref, ka_ref, va_ref, wq_ref, dr_ref, dx_ref, gwq_ref, gbias_ref, da_ref, p_ref, ds_ref, s_ref, dqkv_ref, dq_ref, pad_ref):
    width = HEADS * HD
    half = SEQ // 2
    low_half, slot = lane_facts(PIECE)
    for start in range(0, SEQ, PIECE):
        place = pl.ds(start, PIECE)
        segment, pad, last = segments(lengths_ref, row, start, PIECE)
        pad_ref[place] = pad
        for pair in range(HEADS // 2):
            lanes = pl.ds(pair * PAIR, PAIR)
            dob = dob_ref[place, lanes].astype(F32)
            product = dob * ob_ref[place, lanes].astype(F32)
            even = jnp.sum(jnp.where(low_half, product, 0.0), -1, keepdims=True)
            odd = jnp.sum(jnp.where(low_half, 0.0, product), -1, keepdims=True)
            first, second, third = three_parts(jnp.where(low_half, odd, even))
            aug = jnp.where(
                slot == 0, -first, jnp.where(slot == 1, -second, jnp.where(slot == 2, -third, 0.0))
            )
            da_ref[2 * pair, place] = jnp.where(low_half, dob, aug).astype(LOW)
            da_ref[2 * pair + 1, place] = jnp.where(low_half, aug, dob).astype(LOW)
    units = [(head, part) for head in range(HEADS) for part in range(2)]

    def scores(unit):
        head, part = units[unit]
        keys = pl.ds(part * half, half)
        s_ref[0, unit % 2] = dot_nt(ka_ref[head, keys], qa_ref[head])
        s_ref[1, unit % 2] = dot_nt(va_ref[head, keys], da_ref[head])

    def weigh(unit):
        for place in pieces(half):
            p = jnp.exp(s_ref[0, unit % 2, place])
            p_ref[unit % 2, place] = p.astype(LOW)
            ds_ref[unit % 2, place] = (p * s_ref[1, unit % 2, place]).astype(LOW)

    scores(0)
    for unit in range(len(units)):
        if unit + 1 < len(units):
            scores(unit + 1)
        weigh(unit)
        head, part = units[unit]
        keys = pl.ds(part * half, half)
        side = head % 2
        dq_ref[1, side, keys] = dot_nn(ds_ref[unit % 2], qa_ref[head])
        dq_ref[2, side, keys] = dot_nn(p_ref[unit % 2], da_ref[head])
        dq = dot_tn(ds_ref[unit % 2], ka_ref[head, keys])
        if part:
            dq_ref[0, side] += dq
        else:
            dq_ref[0, side] = dq
        if side and part:
            pair = head // 2
            for start in range(0, SEQ, PIECE):
                place = pl.ds(start, PIECE)
                dq = jnp.where(low_half, dq_ref[0, 0, place], dq_ref[0, 1, place]) * HD**-0.5
                dk = jnp.where(low_half, dq_ref[1, 0, place], dq_ref[1, 1, place])
                dv = jnp.where(low_half, dq_ref[2, 0, place], dq_ref[2, 1, place])
                dv = dv + pad_ref[place] * dob_ref[place, pl.ds(pair * PAIR, PAIR)].astype(F32)
                for block, value in enumerate((dq, dk, dv)):
                    lanes = pl.ds(block * width + pair * PAIR, PAIR)
                    value = value.astype(LOW)
                    dqkv_ref[place, lanes] = value
                    if block != 1:
                        into = pl.ds(pair * PAIR, PAIR)
                        gbias_ref[block // 2, :, into] += fold(value.astype(F32))
    gwq_ref[...] += dot_tn(x, dqkv_ref[...])
    dx_ref[...] = (dr_ref[...] + dot_nt(dqkv_ref[...], wq_ref[...])).astype(dx_ref.dtype)


def unpack_matrix(raw_ref, at, into_ref):
    width = into_ref.shape[0]
    for start in range(0, into_ref.shape[1], width):
        block = raw_ref[:, :, pl.ds(at + start, width)].astype(F32)
        block = block.reshape(GROUPS + (width,)).swapaxes(0, 1).reshape(width, width)
        into_ref[:, pl.ds(start, width)] = block.astype(LOW)


def unpack_stacked(raw_ref, at, into_ref):
    width = into_ref.shape[1]
    count = into_ref.shape[0] // width
    blocks = [
        raw_ref[:, :, pl.ds(at + step * width, width)].astype(F32).reshape(GROUPS + (width,))
        for step in range(count)
    ]
    outer, inner, rows = GROUPS
    for place in range(inner):
        part = jnp.stack([jnp.stack([block[f, place] for block in blocks]) for f in range(outer)])
        size = outer * count * rows
        into_ref[pl.ds(place * size, size)] = part.reshape(size, width).astype(LOW)


def sources(rows, columns):
    line = lax.broadcasted_iota(jnp.int32, (rows, columns), 0)
    outer, inner, height = GROUPS
    device = (line // height) % inner * outer + line // (inner * height)
    return device, line % height


def unpack_vectors(raw_ref, at, layer):
    outer, inner, rows = GROUPS
    total = outer * inner * rows
    raw = raw_ref[:, :, pl.ds(at, 128)].reshape(total, 128)
    lane = lax.broadcasted_iota(jnp.int32, (128, total), 0)
    column = lax.broadcasted_iota(jnp.int32, (128, total), 1)
    pick = jnp.where(lane == rows * layer + column % rows, 1.0, 0.0).astype(LOW)
    spread = dot_nn(raw, pick)
    device, unused = sources(total, total)
    column = lax.broadcasted_iota(jnp.int32, (total, total), 1)
    spread = jnp.where(column // rows == device, spread, 0.0)
    return jnp.sum(spread.reshape(outer * inner, rows, total), 0)


def unpack_hidden(raw_ref, at, layer, hidden):
    outer, inner, rows = GROUPS
    total = outer * inner * rows
    height = hidden // (outer * inner)
    raw = raw_ref[:, :, pl.ds(at, 128)].reshape(total, 128)
    lane = lax.broadcasted_iota(jnp.int32, (128, hidden), 0)
    column = lax.broadcasted_iota(jnp.int32, (128, hidden), 1)
    pick = jnp.where(lane == 2 * rows + column % height, 1.0, 0.0).astype(LOW)
    spread = dot_nn(raw, pick)
    device, within = sources(total, hidden)
    column = lax.broadcasted_iota(jnp.int32, (total, hidden), 1)
    spread = jnp.where((column // height == device) & (within == layer), spread, 0.0)
    return jnp.sum(spread, 0, keepdims=True)


def pack_matrix(sum_ref, sent_ref, at):
    width = sum_ref.shape[0]
    outer, inner, rows = GROUPS
    for start in range(0, sum_ref.shape[1], width):
        block = sum_ref[:, pl.ds(start, width)].reshape(inner, outer, rows, width)
        block = block.swapaxes(0, 1).reshape(outer, inner * rows, width)
        sent_ref[:, :, pl.ds(at + start, width)] = block.astype(LOW)


def pack_stacked(sum_ref, sent_ref, at):
    width = sum_ref.shape[0]
    outer, inner, rows = GROUPS
    count = sum_ref.shape[1] // width
    near = inner // count
    for step in range(count):
        block = sum_ref[:, pl.ds(step * width, width)].T
        block = block.reshape(near, outer, count, rows, width)
        for part in range(count):
            piece = jnp.stack([block[:, f, part] for f in range(outer)])
            piece = piece.reshape(outer, near * rows, width)
            sent_ref[:, pl.ds(step * near * rows, near * rows), pl.ds(at + part * width, width)] = (
                piece.astype(LOW)
            )


def pack_shared(block, sent_ref, at):
    outer, inner, rows = GROUPS
    columns = block.shape[1]
    block = jnp.broadcast_to(block[None], (outer * inner, rows, columns))
    sent_ref[:, :, pl.ds(at, columns)] = block.reshape(outer, inner * rows, columns).astype(LOW)


def pack_attention(gwq_ref, gbias_ref, sent_ref, at):
    pack_matrix(gwq_ref, sent_ref, at)
    width = gwq_ref.shape[0]
    line = lax.broadcasted_iota(jnp.int32, (8, width), 0)
    sums = [jnp.sum(gbias_ref[index], 0, keepdims=True) for index in range(2)]
    block = jnp.where(line == 0, sums[0], jnp.where(line == 1, sums[1], 0.0))
    pack_shared(block, sent_ref, at + 3 * width)


def pack_dense(gwo_ref, gwi_ref, gwf_ref, gsmall_ref, gbi_ref, sent_ref, at):
    width, hidden = gwi_ref.shape
    pack_matrix(gwo_ref, sent_ref, at)
    pack_matrix(gwi_ref, sent_ref, at + width)
    pack_stacked(gwf_ref, sent_ref, at + width + hidden)
    at = at + width + 2 * hidden
    pack_shared(jnp.sum(gsmall_ref[...], 1), sent_ref, at)
    line = jnp.sum(gbi_ref[...], 0, keepdims=True)
    size = hidden // 8
    block = jnp.concatenate([line[:, step * size : (step + 1) * size] for step in range(8)], 0)
    pack_shared(block, sent_ref, at + width)


def shape_of(array):
    return jax.ShapeDtypeStruct(array.shape, array.dtype)


def by_row(shape):
    if len(shape) == 2:
        return pl.BlockSpec((SEQ, shape[1]), lambda row: (row, 0))
    return pl.BlockSpec((None,) + tuple(shape[1:]), lambda row: (row,) + (0,) * (len(shape) - 1))


def whole(shape):
    return pl.BlockSpec(tuple(shape), lambda row: (0,) * len(shape))


def run_rows(body, lengths, rowwise, fixed, row_outs, sent, scratch, cost, setup, finish, after=()):
    count = lengths.shape[0]
    cuts = [len(rowwise), len(fixed), len(after), len(row_outs), len(sent), len(scratch)]

    def kernel(lengths_ref, *refs):
        row = pl.program_id(0)
        groups = []
        at = 0
        for cut in cuts:
            groups.append(refs[at : at + cut])
            at += cut
        rows_in, fixed_in, unused, rows_out, sent_out, work = groups

        @pl.when(row == 0)
        def _():
            setup(fixed_in, work)

        body(row, lengths_ref, rows_in, rows_out, work)

        if sent:

            @pl.when(row == count - 1)
            def _():
                finish(work, sent_out[0])

    return pl.pallas_call(
        kernel,
        grid=(count,),
        in_specs=[pl.BlockSpec(memory_space=pltpu.SMEM)]
        + [by_row(array.shape) for array in rowwise]
        + [whole(array.shape) for array in fixed]
        + [pl.BlockSpec(memory_space=pl.ANY) for array in after],
        out_specs=[by_row(part.shape) for part in row_outs] + [whole(part.shape) for part in sent],
        out_shape=list(row_outs) + list(sent),
        scratch_shapes=list(scratch),
        compiler_params=pltpu.CompilerParams(
            dimension_semantics=("arbitrary",), vmem_limit_bytes=MEMORY
        ),
        cost_estimate=pl.CostEstimate(flops=cost, bytes_accessed=8 * 2**20, transcendentals=0),
    )(lengths, *rowwise, *fixed, *after)


def struct(shape, dtype):
    return jax.ShapeDtypeStruct(tuple(shape), dtype)


FORWARD_SCRATCH = lambda: [
    pltpu.VMEM((2, SEQ // 2, SEQ), F32),
    pltpu.VMEM((2, SEQ // 2, SEQ), LOW),
    pltpu.VMEM((2, SEQ, PAIR), F32),
    pltpu.VMEM((SEQ, PAIR), F32),
    pltpu.VMEM((3, HEADS // 2, SEQ, PAIR), F32),
    pltpu.VMEM((SEQ, PAIR), F32),
]
BACKWARD_SCRATCH = lambda: [
    pltpu.VMEM((HEADS, SEQ, PAIR), LOW),
    pltpu.VMEM((2, SEQ // 2, SEQ), LOW),
    pltpu.VMEM((2, SEQ // 2, SEQ), LOW),
    pltpu.VMEM((2, 2, SEQ // 2, SEQ), F32),
    pltpu.VMEM((SEQ, 3 * HEADS * HD), LOW),
    pltpu.VMEM((3, 2, SEQ, PAIR), F32),
    pltpu.VMEM((SEQ, PAIR), F32),
]


def attention_outs(rows, tokens, width):
    heads = (rows, HEADS, SEQ, PAIR)
    return [struct(heads, LOW)] * 3 + [struct((tokens, width), LOW)]


def dense_outs(tokens, width, hidden):
    return [
        struct((tokens, width), F32),
        struct((tokens, width), F32),
        struct((tokens, PAIR), F32),
        struct((tokens, width), LOW),
        struct((tokens, hidden), LOW),
        struct((tokens, hidden), LOW),
    ]


def vmem(shape, dtype):
    return pltpu.VMEM(tuple(shape), dtype)


def attention_weights(width):
    return [vmem((width, 3 * width), LOW), vmem((1, 3 * width), F32)]


def dense_weights(width, hidden):
    return [
        vmem((width, width), LOW),
        vmem((width, hidden), LOW),
        vmem((hidden, width), LOW),
        vmem((8, width), F32),
        vmem((1, hidden), F32),
    ]


def dense_sums(width, hidden):
    return [
        vmem((width, width), F32),
        vmem((width, hidden), F32),
        vmem((width, hidden), F32),
        vmem((8, 8, width), F32),
        vmem((8, hidden), F32),
    ]


def attention_sums(width):
    return [vmem((width, 3 * width), F32), vmem((2, 8, width), F32)]


def dense_work(width, hidden):
    return [vmem((SEQ, width), LOW), vmem((2, SEQ, width), F32), vmem((SEQ, hidden), LOW)]


def set_attention(layer, urgent_ref, raw_ref, at, wq_ref, bias_ref):
    width = wq_ref.shape[0]
    unpack_matrix(raw_ref, at, wq_ref)
    vectors = unpack_vectors(urgent_ref, 3 * width, layer)
    bias_ref[:, :width] = vectors[0:1]
    bias_ref[:, width : 2 * width] = jnp.zeros((1, width), F32)
    bias_ref[:, 2 * width :] = vectors[1:2]


def set_dense(layer, urgent_ref, raw_ref, at, wo_ref, wi_ref, wf_ref, small_ref, bi_ref):
    width, hidden = wi_ref.shape
    unpack_matrix(raw_ref, at, wo_ref)
    unpack_matrix(raw_ref, at + width, wi_ref)
    unpack_stacked(raw_ref, at + width + hidden, wf_ref)
    small_ref[...] = unpack_vectors(urgent_ref, 3 * width, layer)
    bi_ref[...] = unpack_hidden(urgent_ref, 3 * width, layer, hidden)


def clear(refs):
    for ref in refs:
        ref[...] = jnp.zeros(ref.shape, ref.dtype)


def attention_kernel(layer, lengths, x, urgent, raw, at):
    rows, (tokens, width) = lengths.shape[0], x.shape

    def setup(fixed, work):
        set_attention(layer, fixed[0], fixed[-1], at, *work[:2])

    def body(row, lengths_ref, rowwise, outs, work):
        attention_forward(row, lengths_ref, rowwise[0][...].astype(LOW), *work[:2], *outs, *work[2:])

    fixed = [urgent] if raw is urgent else [urgent, raw]
    return run_rows(
        body, lengths, [x], fixed, attention_outs(rows, tokens, width), [],
        attention_weights(width) + FORWARD_SCRATCH(), 4 * 10**9, setup, None,
    )


def dense_kernel(layer, lengths, x, ob, urgent, raw, at, hidden):
    tokens, width = x.shape

    def setup(fixed, work):
        set_dense(layer, *fixed, at, *work[:5])

    def body(row, lengths_ref, rowwise, outs, work):
        dense_forward(*rowwise, *work[:5], *outs, *work[5:])

    return run_rows(
        body, lengths, [x, ob], [urgent, raw],
        dense_outs(tokens, width, hidden) + [struct((tokens, width), F32)], [],
        dense_weights(width, hidden) + [vmem((SEQ, width), F32), vmem((2, SEQ, width), F32)],
        5 * 10**9, setup, None,
    )


def turn_kernel(layer, lengths, x, ob, cotangent, urgent, raw, at, hidden):
    tokens, width = x.shape
    columns = width + 2 * hidden + width + hidden // 8

    def setup(fixed, work):
        set_dense(layer, *fixed, at, *work[:5])
        clear(work[5:10])

    def body(row, lengths_ref, rowwise, outs, work):
        x_ref, ob_ref, dz_ref = rowwise
        z_ref, dr_ref, dob_ref = outs
        weights, sums, kept = work[:5], work[5:10], work[10:16]
        work_ref, low_ref, u_ref, du_ref = work[16:]
        dense_forward(x_ref, ob_ref, *weights, *kept, z_ref, work_ref, u_ref)
        dense_backward(
            dz_ref, *kept, ob_ref, *weights[:4], dr_ref, dob_ref, *sums, low_ref, u_ref, du_ref
        )

    def finish(work, sent_ref):
        pack_dense(*work[5:10], sent_ref, 0)

    kept = [vmem((SEQ,) + part.shape[1:], part.dtype) for part in dense_outs(tokens, width, hidden)]
    return run_rows(
        body, lengths, [x, ob, cotangent], [urgent, raw],
        [struct((tokens, width), LOW), struct((tokens, width), F32), struct((tokens, width), LOW)],
        [struct((4, 64, columns), LOW)],
        dense_weights(width, hidden) + dense_sums(width, hidden) + kept
        + [vmem((SEQ, width), F32)] + dense_work(width, hidden),
        10**10, setup, finish,
    )


def middle_kernel(lengths, upper, lower, urgent, raw1, raw0, hidden, after):
    tokens, width = upper[0].shape
    columns = 4 * width + width + 2 * hidden + width + hidden // 8

    def setup(fixed, work):
        urgent_ref, raw1_ref, raw0_ref = fixed
        set_attention(1, urgent_ref, raw1_ref, 0, *work[:2])
        set_dense(0, urgent_ref, raw0_ref, 0, *work[2:7])
        clear(work[7:14])

    def body(row, lengths_ref, rowwise, outs, work):
        up, low = rowwise[:7], rowwise[7:]
        dr_ref, dob_ref = outs
        dx_ref, low_ref, u_ref, du_ref = work[14:18]
        attention_backward(
            row, lengths_ref, up[0][...].astype(LOW), *up[1:6], work[0], up[6], dx_ref,
            *work[7:9], *work[18:],
        )
        dense_backward(
            dx_ref, *low, *work[2:6], dr_ref, dob_ref, *work[9:14], low_ref, u_ref, du_ref
        )

    def finish(work, sent_ref):
        pack_attention(*work[7:9], sent_ref, 0)
        pack_dense(*work[9:14], sent_ref, 4 * width)

    return run_rows(
        body, lengths, list(upper) + list(lower), [urgent, raw1, raw0],
        [struct((tokens, width), F32), struct((tokens, width), LOW)],
        [struct((4, 64, columns), LOW)],
        attention_weights(width) + dense_weights(width, hidden)
        + attention_sums(width) + dense_sums(width, hidden)
        + [vmem((SEQ, width), F32)] + dense_work(width, hidden) + BACKWARD_SCRATCH(),
        15 * 10**9, setup, finish, after,
    )


def last_kernel(lengths, upper, urgent, after):
    tokens, width = upper[0].shape

    def setup(fixed, work):
        set_attention(0, fixed[0], fixed[0], 0, *work[:2])
        clear(work[2:4])

    def body(row, lengths_ref, rowwise, outs, work):
        attention_backward(
            row, lengths_ref, rowwise[0][...], *rowwise[1:6], work[0], rowwise[6], outs[0],
            *work[2:4], *work[4:],
        )

    def finish(work, sent_ref):
        pack_attention(*work[2:4], sent_ref, 0)

    return run_rows(
        body, lengths, list(upper), [urgent], [struct((tokens, width), LOW)],
        [struct((4, 64, 4 * width), LOW)],
        attention_weights(width) + attention_sums(width) + BACKWARD_SCRATCH(),
        8 * 10**9, setup, finish, after,
    )


def simple_call(kernel, out_shape, *operands, after=()):
    return pl.pallas_call(
        kernel,
        in_specs=[pl.BlockSpec(memory_space=pltpu.VMEM)] * len(operands)
        + [pl.BlockSpec(memory_space=pl.ANY)] * len(after),
        out_shape=out_shape,
        compiler_params=pltpu.CompilerParams(vmem_limit_bytes=MEMORY),
    )(*operands, *after)


def pack_parameters(
    attn_weight, attn_bias, out_weight, ffn_in, ffn_in_bias, ffn_out, norm_gain, shifts
):
    depth, rows, width = out_weight.shape
    copies = GROUPS[1]
    hidden = ffn_in.shape[2]
    urgent = 3 * width + 128
    columns = depth * (4 * width + 2 * hidden) + 128 - urgent
    height = ffn_in_bias.shape[1]

    def kernel(wq_ref, ab_ref, wo_ref, wi_ref, bi_ref, wf_ref, gain_ref, shift_ref, first_ref, rest_ref, small_ref):
        def put(ref, block, at):
            block = jnp.broadcast_to(block.astype(F32)[None], (copies,) + block.shape)
            block = block.reshape(copies * block.shape[1], block.shape[2])
            ref[:, pl.ds(at, block.shape[1])] = block.astype(LOW)

        small_ref[...] = jnp.zeros(small_ref.shape, F32)
        for layer in range(depth):
            lanes = pl.ds(rows * layer, rows)
            small_ref[0:2, lanes] = ab_ref[layer].astype(F32)
            small_ref[2:4, lanes] = gain_ref[layer].astype(F32)
            small_ref[4:8, lanes] = shift_ref[layer].astype(F32)
        small_ref[0:depth, pl.ds(2 * rows, height)] = bi_ref[...].astype(F32)
        put(first_ref, wq_ref[0], 0)
        put(first_ref, small_ref[...], 3 * width)
        at = 0
        for layer in range(depth):
            if layer:
                put(rest_ref, wq_ref[layer], at)
                at += 3 * width
            put(rest_ref, wo_ref[layer], at)
            put(rest_ref, wi_ref[layer], at + width)
            at += width + hidden
            down = wf_ref[layer].astype(F32)
            for step in range(hidden // width):
                put(rest_ref, down[step * rows : (step + 1) * rows], at)
                at += width

    return pl.pallas_call(
        kernel,
        in_specs=[pl.BlockSpec(memory_space=pltpu.VMEM)] * 8,
        out_shape=[struct((copies * rows, urgent), LOW), struct((copies * rows, columns), LOW)],
        scratch_shapes=[vmem((rows, 128), F32)],
        compiler_params=pltpu.CompilerParams(vmem_limit_bytes=MEMORY),
    )(attn_weight, attn_bias, out_weight, ffn_in, ffn_in_bias, ffn_out, norm_gain, shifts)


def add_parts(received, after=(), passed=None):
    extra = [] if passed is None else [passed]

    def kernel(in_ref, *refs):
        out_ref = refs[len(after) + len(extra)]
        columns = 256
        for start in range(0, in_ref.shape[2], columns):
            size = min(columns, in_ref.shape[2] - start)
            lanes = pl.ds(start, size)
            out_ref[:, lanes] = jnp.sum(in_ref[:, :, lanes].astype(F32), 0).astype(LOW)

    anywhere = pl.BlockSpec(memory_space=pl.ANY)
    found = pl.pallas_call(
        kernel,
        in_specs=[pl.BlockSpec(memory_space=pltpu.VMEM)] + [anywhere] * (len(extra) + len(after)),
        out_specs=[pl.BlockSpec(memory_space=pltpu.VMEM)] + [anywhere] * len(extra),
        out_shape=[struct(received.shape[1:], LOW)] + [shape_of(part) for part in extra],
        input_output_aliases={1: 1} if extra else {},
        compiler_params=pltpu.CompilerParams(vmem_limit_bytes=MEMORY),
    )(received, *extra, *after)
    return found if extra else found[0]


def write_gradients(place, tail, middle, head, depth, width, hidden):
    rows = GROUPS[2]
    height = hidden // DEVICES

    def kernel(place_ref, tail_ref, middle_ref, head_ref, gwq_ref, gab_ref, gwo_ref, gwi_ref, gbi_ref, gwf_ref, gain_ref, shift_ref):
        spot = place_ref[0]

        def total(ref, at, columns):
            block = ref[:, pl.ds(at, columns)].astype(F32)
            return jnp.sum(block.reshape(-1, rows, columns), 0)

        def own(block, size):
            return pltpu.roll(block, block.shape[1] - spot * size, 1)

        for layer, ref, at in ((0, head_ref, 0), (1, middle_ref, 0)):
            gwq_ref[layer] = total(ref, at, 3 * width)
            gab_ref[layer] = own(total(ref, at + 3 * width, width), rows)[0:2, 0:rows]
        for layer, ref, at in ((0, middle_ref, 4 * width), (1, tail_ref, 0)):
            gwo_ref[layer] = total(ref, at, width)
            gwi_ref[layer] = total(ref, at + width, hidden)
            for step in range(hidden // width):
                gwf_ref[layer, pl.ds(step * rows, rows)] = total(
                    ref, at + width + hidden + step * width, width
                )
            at += width + 2 * hidden
            small = own(total(ref, at, width), rows)
            gain_ref[layer] = small[2:4, 0:rows]
            shift_ref[layer] = small[4:8, 0:rows]
            line = total(ref, at + width, hidden // 8)
            line = jnp.concatenate([line[step : step + 1] for step in range(8)], 1)
            gbi_ref[pl.ds(layer, 1)] = own(line, height)[:, 0:height]

    outs = [
        struct((depth, rows, 3 * width), F32),
        struct((depth, 2, rows), F32),
        struct((depth, rows, width), F32),
        struct((depth, rows, hidden), F32),
        struct((depth, height), F32),
        struct((depth, height, width), F32),
        struct((depth, 2, rows), F32),
        struct((depth, 4, rows), F32),
    ]
    return pl.pallas_call(
        kernel,
        in_specs=[pl.BlockSpec(memory_space=pltpu.SMEM)] + [pl.BlockSpec(memory_space=pltpu.VMEM)] * 3,
        out_shape=outs,
        compiler_params=pltpu.CompilerParams(vmem_limit_bytes=MEMORY),
    )(place, tail, middle, head)


def exchange(parts, axis):
    return lax.all_to_all(parts, axis, 0, 0, tiled=True)


def local(
    hidden_in,
    lengths,
    grad_out,
    attn_weight,
    attn_bias,
    out_weight,
    ffn_in,
    ffn_in_bias,
    ffn_out,
    norm_gain,
    shifts,
):
    depth, rows, width = out_weight.shape
    hidden = ffn_in.shape[2]
    first, second = lax.axis_size("dp"), lax.axis_size("fsdp")
    fits = (second, first, rows) == GROUPS
    later_size = width + 2 * hidden
    if fits:
        urgent, later = pack_parameters(
            attn_weight, attn_bias, out_weight, ffn_in, ffn_in_bias, ffn_out, norm_gain, shifts
        )
        urgent = exchange(urgent, "dp")
        urgent = exchange(jnp.broadcast_to(urgent[None], (second,) + urgent.shape), "fsdp")
        later = exchange(later, "dp")
        raw0 = lax.all_gather(later[:, :later_size], "fsdp")
        raw1 = lax.all_gather(later[:, later_size:], "fsdp")
    else:
        urgent, raw0, raw1 = gather_other(
            attn_weight, attn_bias, out_weight, ffn_in, ffn_in_bias, ffn_out, norm_gain, shifts
        )

    qa0, ka0, va0, ob0 = attention_kernel(0, lengths, hidden_in, urgent, urgent, 0)
    n1, n2, inv, yb, gb, gp, z0 = dense_kernel(0, lengths, hidden_in, ob0, urgent, raw0, 0, hidden)
    qa1, ka1, va1, ob1 = attention_kernel(1, lengths, z0, urgent, raw1, 0)
    hidden_out, dr1, dob1, sent_a = turn_kernel(
        1, lengths, z0, ob1, grad_out, urgent, raw1, 3 * width, hidden
    )
    dr0, dob0, sent_b = middle_kernel(
        lengths,
        (z0, dob1, ob1, qa1, ka1, va1, dr1),
        (n1, n2, inv, yb, gb, gp, ob0),
        urgent,
        raw1,
        raw0,
        hidden,
        (sent_a,),
    )
    lower = (hidden_in, dob0, ob0, qa0, ka0, va0, dr0)
    if fits:
        tail = add_parts(exchange(sent_a, "fsdp"), (sent_b,))
        grad_in, sent_c = last_kernel(lengths, lower, urgent, (sent_b, tail))
        tail = exchange(tail, "dp")
        middle, sent_c = add_parts(exchange(sent_b, "fsdp"), (tail,), sent_c)
        middle = exchange(middle, "dp")
        head = add_parts(exchange(sent_c, "fsdp"))
        head = exchange(head, "dp")
        place = lax.axis_index(("dp", "fsdp")).astype(jnp.int32).reshape(1)
        grads = write_gradients(place, tail, middle, head, depth, width, hidden)
    else:
        grad_in, sent_c = last_kernel(lengths, lower, urgent, (sent_b,))
        grads = scatter_other(sent_a, sent_b, sent_c, rows, width, hidden)
    return (hidden_out, grad_in, *grads)


def gather_other(
    attn_weight, attn_bias, out_weight, ffn_in, ffn_in_bias, ffn_out, norm_gain, shifts
):
    axes = ("dp", "fsdp")
    gather = lambda part, axis: lax.all_gather(part, axes, axis=axis, tiled=True)
    depth, unused, width = out_weight.shape
    hidden = ffn_in.shape[2]
    outer, inner, rows = GROUPS
    vectors = gather(jnp.concatenate([attn_bias, norm_gain, shifts], 1), 2)
    line = gather(ffn_in_bias, 1)

    def order(natural):
        return (
            natural.reshape(inner, outer, rows, -1).swapaxes(0, 1).reshape(outer, inner * rows, -1)
        )

    def stacked(part):
        part = part.reshape(DEVICES, -1, rows, width)
        return order(part.swapaxes(1, 2).reshape(width, -1))

    small = vectors.reshape(depth, 8, DEVICES, rows).transpose(2, 1, 0, 3).reshape(width, -1)
    line = line.reshape(depth, DEVICES, -1).swapaxes(0, 1)
    line = jnp.pad(line, ((0, 0), (0, 8 - depth), (0, 0))).reshape(width, -1)
    small = jnp.concatenate([small, line], 1)
    small = jnp.pad(small, ((0, 0), (0, 128 - small.shape[1])))
    wq, wo, wi, wf = (gather(part, 1) for part in (attn_weight, out_weight, ffn_in, ffn_out))
    urgent = jnp.concatenate([order(wq[0]), order(small)], 2)
    raw0 = jnp.concatenate([order(wo[0]), order(wi[0]), stacked(wf[0])], 2)
    raw1 = jnp.concatenate([order(wq[1]), order(wo[1]), order(wi[1]), stacked(wf[1])], 2)
    return urgent, raw0, raw1


def scatter_other(sent_a, sent_b, sent_c, own_rows, width, hidden):
    outer, inner, rows = GROUPS
    axes = ("dp", "fsdp")

    def natural(part):
        return part.reshape(outer, inner, rows, -1).swapaxes(0, 1).reshape(width, -1).astype(F32)

    def cut(part, sizes):
        found, at = [], 0
        for size in sizes:
            found.append(part[:, at : at + size])
            at += size
        return found

    dense = [width, hidden, hidden, width, hidden // 8]
    attention = [3 * width, width]
    wq0, ab0 = cut(natural(sent_c), attention)
    wq1, ab1, wo0, wi0, wf0, small0, bi0 = cut(natural(sent_b), attention + dense)
    wo1, wi1, wf1, small1, bi1 = cut(natural(sent_a), dense)

    def stacked(part):
        part = part.reshape(DEVICES, rows, -1, width).swapaxes(1, 2)
        return part.reshape(hidden, width)

    def spread(parts, axis):
        return lax.psum_scatter(jnp.stack(parts), axes, scatter_dimension=axis, tiled=True)

    return (
        spread([wq0, wq1], 1),
        spread([ab0[:2], ab1[:2]], 2),
        spread([wo0, wo1], 1),
        spread([wi0, wi1], 1),
        spread([bi0[:8].reshape(-1), bi1[:8].reshape(-1)], 1),
        spread([stacked(wf0), stacked(wf1)], 1),
        spread([small0[2:4], small1[2:4]], 2),
        spread([small0[4:8], small1[4:8]], 2),
    )


def solution(mesh):
    placed = (
        P(("dp", "fsdp"), None),
        P(("dp", "fsdp"), None),
        P(("dp", "fsdp"), None),
        P(None, ("dp", "fsdp"), None),
        P(None, None, ("dp", "fsdp")),
        P(None, ("dp", "fsdp"), None),
        P(None, ("dp", "fsdp"), None),
        P(None, ("dp", "fsdp")),
        P(None, ("dp", "fsdp"), None),
        P(None, None, ("dp", "fsdp")),
        P(None, None, ("dp", "fsdp")),
    )
    return jax.shard_map(
        local,
        mesh=mesh,
        in_specs=placed,
        out_specs=(
            P(("dp", "fsdp"), None),
            P(("dp", "fsdp"), None),
            P(None, ("dp", "fsdp"), None),
            P(None, None, ("dp", "fsdp")),
            P(None, ("dp", "fsdp"), None),
            P(None, ("dp", "fsdp"), None),
            P(None, ("dp", "fsdp")),
            P(None, ("dp", "fsdp"), None),
            P(None, None, ("dp", "fsdp")),
            P(None, None, ("dp", "fsdp")),
        ),
        check_vma=False,
    )
```

```python
from functools import partial

import jax
import jax.numpy as jnp
from jax import lax
from jax.experimental import pallas as pl
from jax.experimental.pallas import tpu as pltpu
from jax.sharding import PartitionSpec as P

HEADS = 4
HD = 64
SEQ = 512
PAIR = 2 * HD
FAR = -(2.0**100)
FLOOR = -1e20
EPSILON = 1e-12
PIECE = 64
GROUPS = (4, 8, 8)
DEVICES = 32
LOW = jnp.bfloat16
F32 = jnp.float32
MEMORY = 60 * 2**20


def dot_nn(left, right):
    return lax.dot_general(left, right, (((1,), (0,)), ((), ())), preferred_element_type=F32)


def dot_nt(left, right):
    return lax.dot_general(left, right, (((1,), (1,)), ((), ())), preferred_element_type=F32)


def dot_tn(left, right):
    return lax.dot_general(left, right, (((0,), (0,)), ((), ())), preferred_element_type=F32)


def pieces(total, size=PIECE):
    return [pl.ds(start, size) for start in range(0, total, size)]


def three_parts(values):
    first = values.astype(LOW).astype(F32)
    rest = values - first
    second = rest.astype(LOW).astype(F32)
    return first, second, rest - second


def gelu_parts(u):
    bell = jnp.exp(u * u * -0.5)
    t = 1.0 / (1.0 + (0.3275911 * 0.5**0.5) * jnp.abs(u))
    poly = t * (
        0.127414796
        + t * (-0.142248368 + t * (0.7107068705 + t * (-0.7265760135 + t * 0.5307027145)))
    )
    tail = poly * bell
    cumulative = jnp.where(u > 0, 1.0 - tail, tail)
    return u * cumulative, cumulative + u * bell * 0.3989422804014327


def lane_facts(rows):
    lane = lax.broadcasted_iota(jnp.int32, (rows, PAIR), 1)
    return lane < HD, lane % HD


def segments(lengths_ref, row, start, rows):
    places = lax.broadcasted_iota(jnp.int32, (rows, PAIR), 0) + start
    bound = jnp.int32(0)
    segment = jnp.zeros((rows, PAIR), jnp.int32)
    last = lengths_ref.shape[1] - 1
    for entry in range(last):
        bound = bound + lengths_ref[row, entry]
        segment = segment + (places >= bound).astype(jnp.int32)
    return segment, (segment == last).astype(F32), last


def attention_forward(row, lengths_ref, x, wq_ref, bias_ref, qa_ref, ka_ref, va_ref, ob_ref, s_ref, p_ref, m_ref, pad_ref, q_ref, aug_ref):
    width = HEADS * HD
    for block in range(3):
        for pair in range(HEADS // 2):
            at = block * width + pair * PAIR
            q_ref[block, pair] = dot_nn(x, wq_ref[:, at : at + PAIR]) + bias_ref[:, at : at + PAIR]
    for start in range(0, SEQ, PIECE):
        place = pl.ds(start, PIECE)
        low_half, slot = lane_facts(PIECE)
        segment, pad, last = segments(lengths_ref, row, start, PIECE)
        pad_ref[place] = pad
        aug_q = jnp.where(slot == segment, 1.0, 0.0)
        aug_ref[place] = aug_q
        seen = (slot == segment) & (slot != last)
        aug_k = jnp.where(slot <= last, jnp.where(seen, 0.0, FAR), jnp.where(slot <= last + 3, 1.0, 0.0))
        for pair in range(HEADS // 2):
            q = q_ref[0, pair, place] * HD**-0.5
            k = q_ref[1, pair, place]
            v = q_ref[2, pair, place]
            q_ref[0, pair, place] = q
            qa_ref[2 * pair, place] = jnp.where(low_half, q, aug_q).astype(LOW)
            qa_ref[2 * pair + 1, place] = jnp.where(low_half, aug_q, q).astype(LOW)
            ka_ref[2 * pair, place] = jnp.where(low_half, k, aug_k).astype(LOW)
            ka_ref[2 * pair + 1, place] = jnp.where(low_half, aug_k, k).astype(LOW)
            va_ref[2 * pair, place] = jnp.where(low_half, v, 1.0).astype(LOW)
            va_ref[2 * pair + 1, place] = jnp.where(low_half, 1.0, v).astype(LOW)
    half = SEQ // 2
    units = [(head, part) for head in range(HEADS) for part in range(2)]

    def scores(unit):
        head, part = units[unit]
        s_ref[unit % 2] = dot_nt(qa_ref[head, pl.ds(part * half, half)], ka_ref[head])

    def softmax(unit):
        head, part = units[unit]
        for start in range(0, half, PIECE):
            s = s_ref[unit % 2, pl.ds(start, PIECE)]
            highest = jnp.maximum(jnp.max(s, -1, keepdims=True), FLOOR)
            p_ref[unit % 2, pl.ds(start, PIECE)] = jnp.exp(s - highest).astype(LOW)
            m_ref[head % 2, pl.ds(part * half + start, PIECE)] = jnp.broadcast_to(highest, (PIECE, PAIR))

    def attend(unit):
        head, part = units[unit]
        return dot_nn(p_ref[unit % 2], va_ref[head])

    sums = {}
    scores(0)
    for unit in range(len(units)):
        if unit + 1 < len(units):
            scores(unit + 1)
        softmax(unit)
        head, part = units[unit]
        q_ref[1, head % 2, pl.ds(part * half, half)] = attend(unit)
        if head % 2 and part:
            pair = head // 2
            for start in range(0, SEQ, PIECE):
                place = pl.ds(start, PIECE)
                low_half, slot = lane_facts(PIECE)
                even = q_ref[1, 0, place]
                odd = q_ref[1, 1, place]
                pad = pad_ref[place]
                last = lengths_ref.shape[1] - 1
                total = jnp.where(low_half, odd, even) + pad
                top = jnp.where(low_half, odd_even(m_ref, 1, place), odd_even(m_ref, 0, place))
                spread = jnp.where(pad > 0, 0.0, top + jnp.log(total))
                first, second, third = three_parts(spread)
                aug = jnp.where(
                    slot == last + 1,
                    -first,
                    jnp.where(slot == last + 2, -second, jnp.where(slot == last + 3, -third, aug_ref[place])),
                )
                q = q_ref[0, pair, place]
                qa_ref[2 * pair, place] = jnp.where(low_half, q, aug).astype(LOW)
                qa_ref[2 * pair + 1, place] = jnp.where(low_half, aug, q).astype(LOW)
                v = q_ref[2, pair, place].astype(LOW).astype(F32)
                out = jnp.where(low_half, even, odd) / pltpu.roll(total, HD, 1) + pad * v
                ob_ref[place, pl.ds(pair * PAIR, PAIR)] = out.astype(LOW)


def odd_even(ref, which, place):
    return ref[which, place]


def normal(values):
    centred = values - jnp.mean(values, -1, keepdims=True)
    inverse = lax.rsqrt(jnp.mean(centred * centred, -1, keepdims=True) + EPSILON)
    return centred * inverse, inverse


def normal_back(cotangent, unit, inverse, gains):
    scaled = cotangent * gains
    return inverse * (
        scaled
        - jnp.mean(scaled, -1, keepdims=True)
        - unit * jnp.mean(scaled * unit, -1, keepdims=True)
    )


def dense_forward(x_ref, ob_ref, wo_ref, wi_ref, wf_ref, small_ref, bi_ref, n1_ref, n2_ref, inv_ref, yb_ref, gb_ref, gp_ref, z_ref, work_ref, u_ref):
    small = lambda index: small_ref[pl.ds(index, 1)]
    work_ref[...] = dot_nn(ob_ref[...], wo_ref[...])
    for place in pieces(SEQ):
        unit, inverse = normal(x_ref[place].astype(F32) + work_ref[place] + small(4))
        n1_ref[place] = unit
        inv_ref[place, pl.ds(0, HD)] = jnp.broadcast_to(inverse, (PIECE, HD))
        y = unit * small(2) + small(5)
        yb_ref[place] = y.astype(LOW)
        work_ref[place] = y + small(6)
    columns = 256
    count = wi_ref.shape[1] // columns

    def into(step):
        u_ref[step % 2] = dot_nn(yb_ref[...], wi_ref[:, pl.ds(step * columns, columns)])

    into(0)
    for step in range(count):
        if step + 1 < count:
            into(step + 1)
        lanes = pl.ds(step * columns, columns)
        for place in pieces(SEQ):
            g, slope = gelu_parts(u_ref[step % 2, place] + bi_ref[:, lanes])
            gb_ref[place, lanes] = g.astype(LOW)
            gp_ref[place, lanes] = slope.astype(LOW)
    work_ref[...] += dot_nn(gb_ref[...], wf_ref[...])
    for place in pieces(SEQ):
        unit, inverse = normal(work_ref[place])
        n2_ref[place] = unit
        inv_ref[place, pl.ds(HD, HD)] = jnp.broadcast_to(inverse, (PIECE, HD))
        z_ref[place] = (unit * small(3) + small(7)).astype(z_ref.dtype)


def fold(values):
    return jnp.sum(values.reshape(-1, 8, values.shape[-1]), 0)


def dense_backward(dz_ref, n1_ref, n2_ref, inv_ref, yb_ref, gb_ref, gp_ref, ob_ref, wo_ref, wi_ref, wf_ref, small_ref, dr_ref, dob_ref, gwo_ref, gwi_ref, gwf_ref, gsmall_ref, gbi_ref, low_ref, u_ref, du_ref):
    small = lambda index: small_ref[pl.ds(index, 1)]
    for place in pieces(SEQ):
        dz = dz_ref[place].astype(F32)
        unit = n2_ref[place]
        gsmall_ref[3] += fold(dz * unit)
        gsmall_ref[7] += fold(dz)
        dr = normal_back(dz, unit, inv_ref[place, pl.ds(HD, 1)], small(3))
        dr_ref[place] = dr
        df = dr.astype(LOW)
        low_ref[place] = df
        gsmall_ref[6] += fold(df.astype(F32))
    columns = 256
    count = wi_ref.shape[1] // columns

    def back(step):
        u_ref[step % 2] = dot_nt(low_ref[...], wf_ref[pl.ds(step * columns, columns)])

    back(0)
    for step in range(count):
        if step + 1 < count:
            back(step + 1)
        lanes = pl.ds(step * columns, columns)
        gwf_ref[:, lanes] += dot_tn(low_ref[...], gb_ref[:, lanes])
        for place in pieces(SEQ):
            du = (u_ref[step % 2, place] * gp_ref[place, lanes].astype(F32)).astype(LOW)
            du_ref[place, lanes] = du
            gbi_ref[:, lanes] += fold(du.astype(F32))
        gwi_ref[:, lanes] += dot_tn(yb_ref[...], du_ref[:, lanes])
    u_ref[0] = dot_nt(du_ref[...], wi_ref[...])
    for place in pieces(SEQ):
        dy = dr_ref[place] + u_ref[0, place]
        unit = n1_ref[place]
        gsmall_ref[2] += fold(dy * unit)
        gsmall_ref[5] += fold(dy)
        dr = normal_back(dy, unit, inv_ref[place, pl.ds(0, 1)], small(2))
        dr_ref[place] = dr
        da = dr.astype(LOW)
        low_ref[place] = da
        gsmall_ref[4] += fold(da.astype(F32))
    gwo_ref[...] += dot_tn(ob_ref[...], low_ref[...])
    dob_ref[...] = dot_nt(low_ref[...], wo_ref[...]).astype(LOW)


def attention_backward(row, lengths_ref, x, dob_ref, ob_ref, qa_ref, ka_ref, va_ref, wq_ref, dr_ref, dx_ref, gwq_ref, gbias_ref, da_ref, p_ref, ds_ref, s_ref, dqkv_ref, dq_ref, pad_ref):
    width = HEADS * HD
    half = SEQ // 2
    low_half, slot = lane_facts(PIECE)
    for start in range(0, SEQ, PIECE):
        place = pl.ds(start, PIECE)
        segment, pad, last = segments(lengths_ref, row, start, PIECE)
        pad_ref[place] = pad
        for pair in range(HEADS // 2):
            lanes = pl.ds(pair * PAIR, PAIR)
            dob = dob_ref[place, lanes].astype(F32)
            product = dob * ob_ref[place, lanes].astype(F32)
            even = jnp.sum(jnp.where(low_half, product, 0.0), -1, keepdims=True)
            odd = jnp.sum(jnp.where(low_half, 0.0, product), -1, keepdims=True)
            first, second, third = three_parts(jnp.where(low_half, odd, even))
            aug = jnp.where(
                slot == 0, -first, jnp.where(slot == 1, -second, jnp.where(slot == 2, -third, 0.0))
            )
            da_ref[2 * pair, place] = jnp.where(low_half, dob, aug).astype(LOW)
            da_ref[2 * pair + 1, place] = jnp.where(low_half, aug, dob).astype(LOW)
    units = [(head, part) for head in range(HEADS) for part in range(2)]

    def scores(unit):
        head, part = units[unit]
        keys = pl.ds(part * half, half)
        s_ref[0, unit % 2] = dot_nt(ka_ref[head, keys], qa_ref[head])
        s_ref[1, unit % 2] = dot_nt(va_ref[head, keys], da_ref[head])

    def weigh(unit):
        for place in pieces(half):
            p = jnp.exp(s_ref[0, unit % 2, place])
            p_ref[unit % 2, place] = p.astype(LOW)
            ds_ref[unit % 2, place] = (p * s_ref[1, unit % 2, place]).astype(LOW)

    scores(0)
    for unit in range(len(units)):
        if unit + 1 < len(units):
            scores(unit + 1)
        weigh(unit)
        head, part = units[unit]
        keys = pl.ds(part * half, half)
        side = head % 2
        dq_ref[1, side, keys] = dot_nn(ds_ref[unit % 2], qa_ref[head])
        dq_ref[2, side, keys] = dot_nn(p_ref[unit % 2], da_ref[head])
        dq = dot_tn(ds_ref[unit % 2], ka_ref[head, keys])
        if part:
            dq_ref[0, side] += dq
        else:
            dq_ref[0, side] = dq
        if side and part:
            pair = head // 2
            for start in range(0, SEQ, PIECE):
                place = pl.ds(start, PIECE)
                dq = jnp.where(low_half, dq_ref[0, 0, place], dq_ref[0, 1, place]) * HD**-0.5
                dk = jnp.where(low_half, dq_ref[1, 0, place], dq_ref[1, 1, place])
                dv = jnp.where(low_half, dq_ref[2, 0, place], dq_ref[2, 1, place])
                dv = dv + pad_ref[place] * dob_ref[place, pl.ds(pair * PAIR, PAIR)].astype(F32)
                for block, value in enumerate((dq, dk, dv)):
                    lanes = pl.ds(block * width + pair * PAIR, PAIR)
                    value = value.astype(LOW)
                    dqkv_ref[place, lanes] = value
                    if block != 1:
                        into = pl.ds(pair * PAIR, PAIR)
                        gbias_ref[block // 2, :, into] += fold(value.astype(F32))
    gwq_ref[...] += dot_tn(x, dqkv_ref[...])
    dx_ref[...] = (dr_ref[...] + dot_nt(dqkv_ref[...], wq_ref[...])).astype(dx_ref.dtype)


def unpack_matrix(raw_ref, at, into_ref):
    width = into_ref.shape[0]
    for start in range(0, into_ref.shape[1], width):
        block = raw_ref[:, :, pl.ds(at + start, width)].astype(F32)
        block = block.reshape(GROUPS + (width,)).swapaxes(0, 1).reshape(width, width)
        into_ref[:, pl.ds(start, width)] = block.astype(LOW)


def unpack_stacked(raw_ref, at, into_ref):
    width = into_ref.shape[1]
    count = into_ref.shape[0] // width
    blocks = [
        raw_ref[:, :, pl.ds(at + step * width, width)].astype(F32).reshape(GROUPS + (width,))
        for step in range(count)
    ]
    outer, inner, rows = GROUPS
    for place in range(inner):
        part = jnp.stack([jnp.stack([block[f, place] for block in blocks]) for f in range(outer)])
        size = outer * count * rows
        into_ref[pl.ds(place * size, size)] = part.reshape(size, width).astype(LOW)


def sources(rows, columns):
    line = lax.broadcasted_iota(jnp.int32, (rows, columns), 0)
    outer, inner, height = GROUPS
    device = (line // height) % inner * outer + line // (inner * height)
    return device, line % height


def unpack_vectors(raw_ref, at, layer):
    outer, inner, rows = GROUPS
    total = outer * inner * rows
    raw = raw_ref[:, :, pl.ds(at, 128)].reshape(total, 128)
    lane = lax.broadcasted_iota(jnp.int32, (128, total), 0)
    column = lax.broadcasted_iota(jnp.int32, (128, total), 1)
    pick = jnp.where(lane == rows * layer + column % rows, 1.0, 0.0).astype(LOW)
    spread = dot_nn(raw, pick)
    device, unused = sources(total, total)
    column = lax.broadcasted_iota(jnp.int32, (total, total), 1)
    spread = jnp.where(column // rows == device, spread, 0.0)
    return jnp.sum(spread.reshape(outer * inner, rows, total), 0)


def unpack_hidden(raw_ref, at, layer, hidden):
    outer, inner, rows = GROUPS
    total = outer * inner * rows
    height = hidden // (outer * inner)
    raw = raw_ref[:, :, pl.ds(at, 128)].reshape(total, 128)
    lane = lax.broadcasted_iota(jnp.int32, (128, hidden), 0)
    column = lax.broadcasted_iota(jnp.int32, (128, hidden), 1)
    pick = jnp.where(lane == 2 * rows + column % height, 1.0, 0.0).astype(LOW)
    spread = dot_nn(raw, pick)
    device, within = sources(total, hidden)
    column = lax.broadcasted_iota(jnp.int32, (total, hidden), 1)
    spread = jnp.where((column // height == device) & (within == layer), spread, 0.0)
    return jnp.sum(spread, 0, keepdims=True)


def pack_matrix(sum_ref, sent_ref, at):
    width = sum_ref.shape[0]
    outer, inner, rows = GROUPS
    for start in range(0, sum_ref.shape[1], width):
        block = sum_ref[:, pl.ds(start, width)].reshape(inner, outer, rows, width)
        block = block.swapaxes(0, 1).reshape(outer, inner * rows, width)
        sent_ref[:, :, pl.ds(at + start, width)] = block.astype(LOW)


def pack_stacked(sum_ref, sent_ref, at):
    width = sum_ref.shape[0]
    outer, inner, rows = GROUPS
    count = sum_ref.shape[1] // width
    near = inner // count
    for step in range(count):
        block = sum_ref[:, pl.ds(step * width, width)].T
        block = block.reshape(near, outer, count, rows, width)
        for part in range(count):
            piece = jnp.stack([block[:, f, part] for f in range(outer)])
            piece = piece.reshape(outer, near * rows, width)
            sent_ref[:, pl.ds(step * near * rows, near * rows), pl.ds(at + part * width, width)] = (
                piece.astype(LOW)
            )


def pack_shared(block, sent_ref, at):
    outer, inner, rows = GROUPS
    columns = block.shape[1]
    block = jnp.broadcast_to(block[None], (outer * inner, rows, columns))
    sent_ref[:, :, pl.ds(at, columns)] = block.reshape(outer, inner * rows, columns).astype(LOW)


def pack_attention(gwq_ref, gbias_ref, sent_ref, at):
    pack_matrix(gwq_ref, sent_ref, at)
    width = gwq_ref.shape[0]
    line = lax.broadcasted_iota(jnp.int32, (8, width), 0)
    sums = [jnp.sum(gbias_ref[index], 0, keepdims=True) for index in range(2)]
    block = jnp.where(line == 0, sums[0], jnp.where(line == 1, sums[1], 0.0))
    pack_shared(block, sent_ref, at + 3 * width)


def pack_dense(gwo_ref, gwi_ref, gwf_ref, gsmall_ref, gbi_ref, sent_ref, at):
    width, hidden = gwi_ref.shape
    pack_matrix(gwo_ref, sent_ref, at)
    pack_matrix(gwi_ref, sent_ref, at + width)
    pack_stacked(gwf_ref, sent_ref, at + width + hidden)
    at = at + width + 2 * hidden
    pack_shared(jnp.sum(gsmall_ref[...], 1), sent_ref, at)
    line = jnp.sum(gbi_ref[...], 0, keepdims=True)
    size = hidden // 8
    block = jnp.concatenate([line[:, step * size : (step + 1) * size] for step in range(8)], 0)
    pack_shared(block, sent_ref, at + width)


def shape_of(array):
    return jax.ShapeDtypeStruct(array.shape, array.dtype)


def by_row(shape):
    if len(shape) == 2:
        return pl.BlockSpec((SEQ, shape[1]), lambda row: (row, 0))
    return pl.BlockSpec((None,) + tuple(shape[1:]), lambda row: (row,) + (0,) * (len(shape) - 1))


def whole(shape):
    return pl.BlockSpec(tuple(shape), lambda row: (0,) * len(shape))


def run_rows(body, lengths, rowwise, fixed, row_outs, sent, scratch, cost, setup, finish, after=()):
    count = lengths.shape[0]
    cuts = [len(rowwise), len(fixed), len(after), len(row_outs), len(sent), len(scratch)]

    def kernel(lengths_ref, *refs):
        row = pl.program_id(0)
        groups = []
        at = 0
        for cut in cuts:
            groups.append(refs[at : at + cut])
            at += cut
        rows_in, fixed_in, unused, rows_out, sent_out, work = groups

        @pl.when(row == 0)
        def _():
            setup(fixed_in, work)

        body(row, lengths_ref, rows_in, rows_out, work)

        if sent:

            @pl.when(row == count - 1)
            def _():
                finish(work, fixed_in, sent_out[0])

    return pl.pallas_call(
        kernel,
        grid=(count,),
        in_specs=[pl.BlockSpec(memory_space=pltpu.SMEM)]
        + [by_row(array.shape) for array in rowwise]
        + [whole(array.shape) for array in fixed]
        + [pl.BlockSpec(memory_space=pl.ANY) for array in after],
        out_specs=[by_row(part.shape) for part in row_outs] + [whole(part.shape) for part in sent],
        out_shape=list(row_outs) + list(sent),
        scratch_shapes=list(scratch),
        compiler_params=pltpu.CompilerParams(
            dimension_semantics=("arbitrary",), vmem_limit_bytes=MEMORY
        ),
        cost_estimate=pl.CostEstimate(flops=cost, bytes_accessed=8 * 2**20, transcendentals=0),
    )(lengths, *rowwise, *fixed, *after)


def struct(shape, dtype):
    return jax.ShapeDtypeStruct(tuple(shape), dtype)


FORWARD_SCRATCH = lambda: [
    pltpu.VMEM((2, SEQ // 2, SEQ), F32),
    pltpu.VMEM((2, SEQ // 2, SEQ), LOW),
    pltpu.VMEM((2, SEQ, PAIR), F32),
    pltpu.VMEM((SEQ, PAIR), F32),
    pltpu.VMEM((3, HEADS // 2, SEQ, PAIR), F32),
    pltpu.VMEM((SEQ, PAIR), F32),
]
BACKWARD_SCRATCH = lambda: [
    pltpu.VMEM((HEADS, SEQ, PAIR), LOW),
    pltpu.VMEM((2, SEQ // 2, SEQ), LOW),
    pltpu.VMEM((2, SEQ // 2, SEQ), LOW),
    pltpu.VMEM((2, 2, SEQ // 2, SEQ), F32),
    pltpu.VMEM((SEQ, 3 * HEADS * HD), LOW),
    pltpu.VMEM((3, 2, SEQ, PAIR), F32),
    pltpu.VMEM((SEQ, PAIR), F32),
]


def attention_outs(rows, tokens, width):
    heads = (rows, HEADS, SEQ, PAIR)
    return [struct(heads, LOW)] * 3 + [struct((tokens, width), LOW)]


def dense_outs(tokens, width, hidden):
    return [
        struct((tokens, width), F32),
        struct((tokens, width), F32),
        struct((tokens, PAIR), F32),
        struct((tokens, width), LOW),
        struct((tokens, hidden), LOW),
        struct((tokens, hidden), LOW),
    ]


def vmem(shape, dtype):
    return pltpu.VMEM(tuple(shape), dtype)


def attention_weights(width):
    return [vmem((width, 3 * width), LOW), vmem((1, 3 * width), F32)]


def dense_weights(width, hidden):
    return [
        vmem((width, width), LOW),
        vmem((width, hidden), LOW),
        vmem((hidden, width), LOW),
        vmem((8, width), F32),
        vmem((1, hidden), F32),
    ]


def dense_sums(width, hidden):
    return [
        vmem((width, width), F32),
        vmem((width, hidden), F32),
        vmem((width, hidden), F32),
        vmem((8, 8, width), F32),
        vmem((8, hidden), F32),
    ]


def attention_sums(width):
    return [vmem((width, 3 * width), F32), vmem((2, 8, width), F32)]


def dense_work(width, hidden):
    return [vmem((SEQ, width), LOW), vmem((2, SEQ, width), F32), vmem((SEQ, hidden), LOW)]


def set_attention(layer, urgent_ref, raw_ref, at, wq_ref, bias_ref):
    width = wq_ref.shape[0]
    unpack_matrix(raw_ref, at, wq_ref)
    vectors = unpack_vectors(urgent_ref, 3 * width, layer)
    bias_ref[:, :width] = vectors[0:1]
    bias_ref[:, width : 2 * width] = jnp.zeros((1, width), F32)
    bias_ref[:, 2 * width :] = vectors[1:2]


def set_dense(layer, urgent_ref, raw_ref, at, wo_ref, wi_ref, wf_ref, small_ref, bi_ref):
    width, hidden = wi_ref.shape
    unpack_matrix(raw_ref, at, wo_ref)
    unpack_matrix(raw_ref, at + width, wi_ref)
    unpack_stacked(raw_ref, at + width + hidden, wf_ref)
    small_ref[...] = unpack_vectors(urgent_ref, 3 * width, layer)
    bi_ref[...] = unpack_hidden(urgent_ref, 3 * width, layer, hidden)


def clear(refs):
    for ref in refs:
        ref[...] = jnp.zeros(ref.shape, ref.dtype)


def attention_kernel(layer, lengths, x, urgent, raw, at):
    rows, (tokens, width) = lengths.shape[0], x.shape

    def setup(fixed, work):
        set_attention(layer, fixed[0], fixed[-1], at, *work[:2])

    def body(row, lengths_ref, rowwise, outs, work):
        attention_forward(row, lengths_ref, rowwise[0][...].astype(LOW), *work[:2], *outs, *work[2:])

    fixed = [urgent] if raw is urgent else [urgent, raw]
    return run_rows(
        body, lengths, [x], fixed, attention_outs(rows, tokens, width), [],
        attention_weights(width) + FORWARD_SCRATCH(), 4 * 10**9, setup, None,
    )


def dense_kernel(layer, lengths, x, ob, urgent, raw, at, hidden, after):
    tokens, width = x.shape

    def setup(fixed, work):
        set_dense(layer, *fixed, at, *work[:5])

    def body(row, lengths_ref, rowwise, outs, work):
        dense_forward(*rowwise, *work[:5], *outs, *work[5:])

    return run_rows(
        body, lengths, [x, ob], [urgent, raw],
        dense_outs(tokens, width, hidden) + [struct((tokens, width), F32)], [],
        dense_weights(width, hidden) + [vmem((SEQ, width), F32), vmem((2, SEQ, width), F32)],
        5 * 10**9, setup, None, after,
    )


def turn_kernel(layer, lengths, x, ob, cotangent, urgent, raw, at, hidden):
    tokens, width = x.shape
    columns = width + 2 * hidden + width + hidden // 8

    def setup(fixed, work):
        set_dense(layer, *fixed, at, *work[:5])
        clear(work[5:10])

    def body(row, lengths_ref, rowwise, outs, work):
        x_ref, ob_ref, dz_ref = rowwise
        z_ref, dr_ref, dob_ref = outs
        weights, sums, kept = work[:5], work[5:10], work[10:16]
        work_ref, low_ref, u_ref, du_ref = work[16:]
        dense_forward(x_ref, ob_ref, *weights, *kept, z_ref, work_ref, u_ref)
        dense_backward(
            dz_ref, *kept, ob_ref, *weights[:4], dr_ref, dob_ref, *sums, low_ref, u_ref, du_ref
        )

    def finish(work, fixed, sent_ref):
        pack_dense(*work[5:10], sent_ref, 0)

    kept = [vmem((SEQ,) + part.shape[1:], part.dtype) for part in dense_outs(tokens, width, hidden)]
    return run_rows(
        body, lengths, [x, ob, cotangent], [urgent, raw],
        [struct((tokens, width), LOW), struct((tokens, width), F32), struct((tokens, width), LOW)],
        [struct((4, 64, columns), LOW)],
        dense_weights(width, hidden) + dense_sums(width, hidden) + kept
        + [vmem((SEQ, width), F32)] + dense_work(width, hidden),
        10**10, setup, finish,
    )


def attention_back_kernel(layer, lengths, upper, urgent, raw, dtype, after):
    tokens, width = upper[0].shape

    def setup(fixed, work):
        set_attention(layer, fixed[0], fixed[-1], 0, *work[:2])
        clear(work[2:4])

    def body(row, lengths_ref, rowwise, outs, work):
        attention_backward(
            row, lengths_ref, rowwise[0][...].astype(LOW), *rowwise[1:6], work[0], rowwise[6],
            outs[0], *work[2:4], *work[4:],
        )

    def finish(work, fixed, sent_ref):
        pack_attention(*work[2:4], sent_ref, 0)

    fixed = [urgent] if raw is urgent else [urgent, raw]
    return run_rows(
        body, lengths, list(upper), fixed, [struct((tokens, width), dtype)],
        [struct((4, 64, 4 * width), LOW)],
        attention_weights(width) + attention_sums(width) + BACKWARD_SCRATCH(),
        8 * 10**9, setup, finish, after,
    )


def dense_back_kernel(layer, lengths, dz, lower, urgent, raw, at, hidden, joined, after):
    tokens, width = dz.shape
    ahead = joined.shape[2]
    columns = ahead + width + 2 * hidden + width + hidden // 8

    def setup(fixed, work):
        set_dense(layer, *fixed[:2], at, *work[:5])
        clear(work[5:10])

    def body(row, lengths_ref, rowwise, outs, work):
        dense_backward(*rowwise, *work[:4], *outs, *work[5:])

    def finish(work, fixed, sent_ref):
        sent_ref[:, :, pl.ds(0, ahead)] = fixed[2][...]
        pack_dense(*work[5:10], sent_ref, ahead)

    return run_rows(
        body, lengths, [dz] + list(lower), [urgent, raw, joined],
        [struct((tokens, width), F32), struct((tokens, width), LOW)],
        [struct((4, 64, columns), LOW)],
        dense_weights(width, hidden) + dense_sums(width, hidden) + dense_work(width, hidden),
        7 * 10**9, setup, finish, after,
    )


def hold(array, after):
    def kernel(*refs):
        pass

    anywhere = pl.BlockSpec(memory_space=pl.ANY)
    return pl.pallas_call(
        kernel,
        in_specs=[anywhere] * (1 + len(after)),
        out_specs=anywhere,
        out_shape=shape_of(array),
        input_output_aliases={0: 0},
    )(array, *after)


def pack_parameters(
    attn_weight, attn_bias, out_weight, ffn_in, ffn_in_bias, ffn_out, norm_gain, shifts
):
    depth, rows, width = out_weight.shape
    copies = GROUPS[1]
    hidden = ffn_in.shape[2]
    early = 4 * width + 2 * hidden + 128
    columns = 4 * width + 2 * hidden
    height = ffn_in_bias.shape[1]

    def kernel(wq_ref, ab_ref, wo_ref, wi_ref, bi_ref, wf_ref, gain_ref, shift_ref, first_ref, rest_ref, small_ref):
        def put(ref, block, at):
            block = jnp.broadcast_to(block.astype(F32)[None], (copies,) + block.shape)
            block = block.reshape(copies * block.shape[1], block.shape[2])
            ref[:, pl.ds(at, block.shape[1])] = block.astype(LOW)

        small_ref[...] = jnp.zeros(small_ref.shape, F32)
        for layer in range(depth):
            lanes = pl.ds(rows * layer, rows)
            small_ref[0:2, lanes] = ab_ref[layer].astype(F32)
            small_ref[2:4, lanes] = gain_ref[layer].astype(F32)
            small_ref[4:8, lanes] = shift_ref[layer].astype(F32)
        small_ref[0:depth, pl.ds(2 * rows, height)] = bi_ref[...].astype(F32)
        put(first_ref, wq_ref[0], 0)
        put(first_ref, small_ref[...], 3 * width)
        for layer, ref, at in ((0, first_ref, 3 * width + 128), (1, rest_ref, 3 * width)):
            if layer:
                put(ref, wq_ref[layer], 0)
            put(ref, wo_ref[layer], at)
            put(ref, wi_ref[layer], at + width)
            at += width + hidden
            down = wf_ref[layer].astype(F32)
            for step in range(hidden // width):
                put(ref, down[step * rows : (step + 1) * rows], at)
                at += width

    return pl.pallas_call(
        kernel,
        in_specs=[pl.BlockSpec(memory_space=pltpu.VMEM)] * 8,
        out_shape=[struct((copies * rows, early), LOW), struct((copies * rows, columns), LOW)],
        scratch_shapes=[vmem((rows, 128), F32)],
        compiler_params=pltpu.CompilerParams(vmem_limit_bytes=MEMORY),
    )(attn_weight, attn_bias, out_weight, ffn_in, ffn_in_bias, ffn_out, norm_gain, shifts)


def add_parts(received, after=(), passed=None, joined=None):
    extra = [] if passed is None else [passed]
    inner = [] if joined is None else [joined]
    ahead = 0 if joined is None else joined.shape[1]
    rows, lanes_in = received.shape[1:]

    def kernel(in_ref, *refs):
        out_ref = refs[len(inner) + len(extra) + len(after)]
        if inner:
            out_ref[:, pl.ds(0, ahead)] = refs[0][...]
        columns = 256
        for start in range(0, lanes_in, columns):
            size = min(columns, lanes_in - start)
            total = jnp.sum(in_ref[:, :, pl.ds(start, size)].astype(F32), 0)
            out_ref[:, pl.ds(ahead + start, size)] = total.astype(LOW)

    anywhere = pl.BlockSpec(memory_space=pl.ANY)
    near = pl.BlockSpec(memory_space=pltpu.VMEM)
    found = pl.pallas_call(
        kernel,
        in_specs=[near] * (1 + len(inner)) + [anywhere] * (len(extra) + len(after)),
        out_specs=[near] + [anywhere] * len(extra),
        out_shape=[struct((rows, ahead + lanes_in), LOW)] + [shape_of(part) for part in extra],
        input_output_aliases={1 + len(inner): 1} if extra else {},
        compiler_params=pltpu.CompilerParams(vmem_limit_bytes=MEMORY),
    )(received, *inner, *extra, *after)
    return found if extra else found[0]


def write_gradients(place, tail, front, depth, width, hidden):
    rows = GROUPS[2]
    last = front.shape[1] - 4 * width
    height = hidden // DEVICES

    def kernel(place_ref, tail_ref, front_ref, gwq_ref, gab_ref, gwo_ref, gwi_ref, gbi_ref, gwf_ref, gain_ref, shift_ref):
        spot = place_ref[0]

        def total(ref, at, columns):
            block = ref[:, pl.ds(at, columns)].astype(F32)
            return jnp.sum(block.reshape(-1, rows, columns), 0)

        def own(block, size):
            return pltpu.roll(block, block.shape[1] - spot * size, 1)

        for layer, ref, at in ((0, front_ref, last), (1, front_ref, 0)):
            gwq_ref[layer] = total(ref, at, 3 * width)
            gab_ref[layer] = own(total(ref, at + 3 * width, width), rows)[0:2, 0:rows]
        for layer, ref, at in ((0, front_ref, 4 * width), (1, tail_ref, 0)):
            gwo_ref[layer] = total(ref, at, width)
            gwi_ref[layer] = total(ref, at + width, hidden)
            for step in range(hidden // width):
                gwf_ref[layer, pl.ds(step * rows, rows)] = total(
                    ref, at + width + hidden + step * width, width
                )
            at += width + 2 * hidden
            small = own(total(ref, at, width), rows)
            gain_ref[layer] = small[2:4, 0:rows]
            shift_ref[layer] = small[4:8, 0:rows]
            line = total(ref, at + width, hidden // 8)
            line = jnp.concatenate([line[step : step + 1] for step in range(8)], 1)
            gbi_ref[pl.ds(layer, 1)] = own(line, height)[:, 0:height]

    outs = [
        struct((depth, rows, 3 * width), F32),
        struct((depth, 2, rows), F32),
        struct((depth, rows, width), F32),
        struct((depth, rows, hidden), F32),
        struct((depth, height), F32),
        struct((depth, height, width), F32),
        struct((depth, 2, rows), F32),
        struct((depth, 4, rows), F32),
    ]
    return pl.pallas_call(
        kernel,
        in_specs=[pl.BlockSpec(memory_space=pltpu.SMEM)] + [pl.BlockSpec(memory_space=pltpu.VMEM)] * 2,
        out_shape=outs,
        compiler_params=pltpu.CompilerParams(vmem_limit_bytes=MEMORY),
    )(place, tail, front)


def exchange(parts, axis):
    return lax.all_to_all(parts, axis, 0, 0, tiled=True)


def local(
    hidden_in,
    lengths,
    grad_out,
    attn_weight,
    attn_bias,
    out_weight,
    ffn_in,
    ffn_in_bias,
    ffn_out,
    norm_gain,
    shifts,
):
    depth, rows, width = out_weight.shape
    hidden = ffn_in.shape[2]
    first, second = lax.axis_size("dp"), lax.axis_size("fsdp")
    fits = (second, first, rows) == GROUPS
    urgent_size = 3 * width + 128
    if fits:
        early, later = pack_parameters(
            attn_weight, attn_bias, out_weight, ffn_in, ffn_in_bias, ffn_out, norm_gain, shifts
        )
        early = exchange(early, "dp")
        urgent = early[:, :urgent_size]
        urgent = exchange(jnp.broadcast_to(urgent[None], (second,) + urgent.shape), "fsdp")
        raw0 = lax.all_gather(early[:, urgent_size:], "fsdp")
        later = exchange(hold(later, (urgent,)), "dp")
        raw1 = lax.all_gather(later, "fsdp")
        ready = (later,)
    else:
        urgent, raw0, raw1 = gather_other(
            attn_weight, attn_bias, out_weight, ffn_in, ffn_in_bias, ffn_out, norm_gain, shifts
        )
        ready = ()

    qa0, ka0, va0, ob0 = attention_kernel(0, lengths, hidden_in, urgent, urgent, 0)
    n1, n2, inv, yb, gb, gp, z0 = dense_kernel(
        0, lengths, hidden_in, ob0, urgent, raw0, 0, hidden, ready
    )
    qa1, ka1, va1, ob1 = attention_kernel(1, lengths, z0, urgent, raw1, 0)
    hidden_out, dr1, dob1, sent_a = turn_kernel(
        1, lengths, z0, ob1, grad_out, urgent, raw1, 3 * width, hidden
    )
    dx1, sent_q = attention_back_kernel(
        1, lengths, (z0, dob1, ob1, qa1, ka1, va1, dr1), urgent, raw1, F32, (sent_a,)
    )
    ready = ()
    if fits:
        tail = add_parts(exchange(sent_a, "fsdp"), (sent_q,))
        ready = (tail,)
    dr0, dob0, sent_b = dense_back_kernel(
        0, lengths, dx1, (n1, n2, inv, yb, gb, gp, ob0), urgent, raw0, 0, hidden, sent_q, ready
    )
    if fits:
        tail = exchange(tail, "dp")
        ready = (tail,)
    grad_in, sent_c = attention_back_kernel(
        0, lengths, (hidden_in, dob0, ob0, qa0, ka0, va0, dr0), urgent, urgent, LOW,
        (sent_b,) + ready,
    )
    if fits:
        front, sent_c = add_parts(exchange(sent_b, "fsdp"), (), sent_c)
        front = add_parts(exchange(sent_c, "fsdp"), (), None, front)
        front = exchange(front, "dp")
        place = lax.axis_index(("dp", "fsdp")).astype(jnp.int32).reshape(1)
        grads = write_gradients(place, tail, front, depth, width, hidden)
    else:
        grads = scatter_other(sent_a, sent_b, sent_c, rows, width, hidden)
    return (hidden_out, grad_in, *grads)


def gather_other(
    attn_weight, attn_bias, out_weight, ffn_in, ffn_in_bias, ffn_out, norm_gain, shifts
):
    axes = ("dp", "fsdp")
    gather = lambda part, axis: lax.all_gather(part, axes, axis=axis, tiled=True)
    depth, unused, width = out_weight.shape
    hidden = ffn_in.shape[2]
    outer, inner, rows = GROUPS
    vectors = gather(jnp.concatenate([attn_bias, norm_gain, shifts], 1), 2)
    line = gather(ffn_in_bias, 1)

    def order(natural):
        return (
            natural.reshape(inner, outer, rows, -1).swapaxes(0, 1).reshape(outer, inner * rows, -1)
        )

    def stacked(part):
        part = part.reshape(DEVICES, -1, rows, width)
        return order(part.swapaxes(1, 2).reshape(width, -1))

    small = vectors.reshape(depth, 8, DEVICES, rows).transpose(2, 1, 0, 3).reshape(width, -1)
    line = line.reshape(depth, DEVICES, -1).swapaxes(0, 1)
    line = jnp.pad(line, ((0, 0), (0, 8 - depth), (0, 0))).reshape(width, -1)
    small = jnp.concatenate([small, line], 1)
    small = jnp.pad(small, ((0, 0), (0, 128 - small.shape[1])))
    wq, wo, wi, wf = (gather(part, 1) for part in (attn_weight, out_weight, ffn_in, ffn_out))
    urgent = jnp.concatenate([order(wq[0]), order(small)], 2)
    raw0 = jnp.concatenate([order(wo[0]), order(wi[0]), stacked(wf[0])], 2)
    raw1 = jnp.concatenate([order(wq[1]), order(wo[1]), order(wi[1]), stacked(wf[1])], 2)
    return urgent, raw0, raw1


def scatter_other(sent_a, sent_b, sent_c, own_rows, width, hidden):
    outer, inner, rows = GROUPS
    axes = ("dp", "fsdp")

    def natural(part):
        return part.reshape(outer, inner, rows, -1).swapaxes(0, 1).reshape(width, -1).astype(F32)

    def cut(part, sizes):
        found, at = [], 0
        for size in sizes:
            found.append(part[:, at : at + size])
            at += size
        return found

    dense = [width, hidden, hidden, width, hidden // 8]
    attention = [3 * width, width]
    wq0, ab0 = cut(natural(sent_c), attention)
    wq1, ab1, wo0, wi0, wf0, small0, bi0 = cut(natural(sent_b), attention + dense)
    wo1, wi1, wf1, small1, bi1 = cut(natural(sent_a), dense)

    def stacked(part):
        part = part.reshape(DEVICES, rows, -1, width).swapaxes(1, 2)
        return part.reshape(hidden, width)

    def spread(parts, axis):
        return lax.psum_scatter(jnp.stack(parts), axes, scatter_dimension=axis, tiled=True)

    return (
        spread([wq0, wq1], 1),
        spread([ab0[:2], ab1[:2]], 2),
        spread([wo0, wo1], 1),
        spread([wi0, wi1], 1),
        spread([bi0[:8].reshape(-1), bi1[:8].reshape(-1)], 1),
        spread([stacked(wf0), stacked(wf1)], 1),
        spread([small0[2:4], small1[2:4]], 2),
        spread([small0[4:8], small1[4:8]], 2),
    )


def solution(mesh):
    placed = (
        P(("dp", "fsdp"), None),
        P(("dp", "fsdp"), None),
        P(("dp", "fsdp"), None),
        P(None, ("dp", "fsdp"), None),
        P(None, None, ("dp", "fsdp")),
        P(None, ("dp", "fsdp"), None),
        P(None, ("dp", "fsdp"), None),
        P(None, ("dp", "fsdp")),
        P(None, ("dp", "fsdp"), None),
        P(None, None, ("dp", "fsdp")),
        P(None, None, ("dp", "fsdp")),
    )
    return jax.shard_map(
        local,
        mesh=mesh,
        in_specs=placed,
        out_specs=(
            P(("dp", "fsdp"), None),
            P(("dp", "fsdp"), None),
            P(None, ("dp", "fsdp"), None),
            P(None, None, ("dp", "fsdp")),
            P(None, ("dp", "fsdp"), None),
            P(None, ("dp", "fsdp"), None),
            P(None, ("dp", "fsdp")),
            P(None, ("dp", "fsdp"), None),
            P(None, None, ("dp", "fsdp")),
            P(None, None, ("dp", "fsdp")),
        ),
        check_vma=False,
    )
```

```python
from functools import partial

import jax
import jax.numpy as jnp
from jax import lax
from jax.experimental import pallas as pl
from jax.experimental.pallas import tpu as pltpu
from jax.sharding import PartitionSpec as P

HEADS = 4
HD = 64
SEQ = 512
PAIR = 2 * HD
FAR = -(2.0**100)
FLOOR = -1e20
EPSILON = 1e-12
PIECE = 64
GROUPS = (4, 8, 8)
DEVICES = 32
LOW = jnp.bfloat16
F32 = jnp.float32
MEMORY = 60 * 2**20


def dot_nn(left, right):
    return lax.dot_general(left, right, (((1,), (0,)), ((), ())), preferred_element_type=F32)


def dot_nt(left, right):
    return lax.dot_general(left, right, (((1,), (1,)), ((), ())), preferred_element_type=F32)


def dot_tn(left, right):
    return lax.dot_general(left, right, (((0,), (0,)), ((), ())), preferred_element_type=F32)


def pieces(total, size=PIECE):
    return [pl.ds(start, size) for start in range(0, total, size)]


def three_parts(values):
    first = values.astype(LOW).astype(F32)
    rest = values - first
    second = rest.astype(LOW).astype(F32)
    return first, second, rest - second


CURVE = (
    7.97882253e-01,
    3.63445176e-02,
    -4.47304308e-05,
    -5.04138899e-05,
    3.10523303e-06,
    -6.66676088e-08,
)
BELL = -0.5 / 0.6931471805599453


def gelu_parts(u):
    square = u * u
    near = jnp.minimum(square, 31.36)
    curve = CURVE[-1]
    for factor in CURVE[-2::-1]:
        curve = curve * near + factor
    bent = jnp.tanh(u * curve)
    half = 0.5 * u
    slope = (0.5 + 0.5 * bent) + (u * 0.3989422804014327) * jnp.exp2(square * BELL)
    return half + half * bent, slope


def lane_facts(rows):
    lane = lax.broadcasted_iota(jnp.int32, (rows, PAIR), 1)
    return lane < HD, lane % HD


def segments(lengths_ref, row, start, rows):
    places = lax.broadcasted_iota(jnp.int32, (rows, PAIR), 0) + start
    bound = jnp.int32(0)
    segment = jnp.zeros((rows, PAIR), jnp.int32)
    last = lengths_ref.shape[1] - 1
    for entry in range(last):
        bound = bound + lengths_ref[row, entry]
        segment = segment + (places >= bound).astype(jnp.int32)
    return segment, (segment == last).astype(F32), last


def attention_forward(row, lengths_ref, x, wq_ref, bias_ref, qa_ref, ka_ref, va_ref, ob_ref, s_ref, p_ref, m_ref, pad_ref, q_ref, aug_ref):
    width = HEADS * HD
    for block in range(3):
        for pair in range(HEADS // 2):
            at = block * width + pair * PAIR
            q_ref[block, pair] = dot_nn(x, wq_ref[:, at : at + PAIR]) + bias_ref[:, at : at + PAIR]
    for start in range(0, SEQ, PIECE):
        place = pl.ds(start, PIECE)
        low_half, slot = lane_facts(PIECE)
        segment, pad, last = segments(lengths_ref, row, start, PIECE)
        pad_ref[place] = pad
        aug_q = jnp.where(slot == segment, 1.0, 0.0)
        aug_ref[place] = aug_q
        seen = (slot == segment) & (slot != last)
        aug_k = jnp.where(slot <= last, jnp.where(seen, 0.0, FAR), jnp.where(slot <= last + 3, 1.0, 0.0))
        for pair in range(HEADS // 2):
            q = q_ref[0, pair, place] * HD**-0.5
            k = q_ref[1, pair, place]
            v = q_ref[2, pair, place]
            q_ref[0, pair, place] = q
            qa_ref[2 * pair, place] = jnp.where(low_half, q, aug_q).astype(LOW)
            qa_ref[2 * pair + 1, place] = jnp.where(low_half, aug_q, q).astype(LOW)
            ka_ref[2 * pair, place] = jnp.where(low_half, k, aug_k).astype(LOW)
            ka_ref[2 * pair + 1, place] = jnp.where(low_half, aug_k, k).astype(LOW)
            va_ref[2 * pair, place] = jnp.where(low_half, v, 1.0).astype(LOW)
            va_ref[2 * pair + 1, place] = jnp.where(low_half, 1.0, v).astype(LOW)
    half = SEQ // 2
    units = [(head, part) for head in range(HEADS) for part in range(2)]

    def scores(unit):
        head, part = units[unit]
        s_ref[unit % 2] = dot_nt(qa_ref[head, pl.ds(part * half, half)], ka_ref[head])

    def softmax(unit):
        head, part = units[unit]
        for start in range(0, half, PIECE):
            s = s_ref[unit % 2, pl.ds(start, PIECE)]
            highest = jnp.maximum(jnp.max(s, -1, keepdims=True), FLOOR)
            p_ref[unit % 2, pl.ds(start, PIECE)] = jnp.exp(s - highest).astype(LOW)
            m_ref[head % 2, pl.ds(part * half + start, PIECE)] = jnp.broadcast_to(highest, (PIECE, PAIR))

    def attend(unit):
        head, part = units[unit]
        return dot_nn(p_ref[unit % 2], va_ref[head])

    sums = {}
    scores(0)
    for unit in range(len(units)):
        if unit + 1 < len(units):
            scores(unit + 1)
        softmax(unit)
        head, part = units[unit]
        q_ref[1, head % 2, pl.ds(part * half, half)] = attend(unit)
        if head % 2 and part:
            pair = head // 2
            for start in range(0, SEQ, PIECE):
                place = pl.ds(start, PIECE)
                low_half, slot = lane_facts(PIECE)
                even = q_ref[1, 0, place]
                odd = q_ref[1, 1, place]
                pad = pad_ref[place]
                last = lengths_ref.shape[1] - 1
                total = jnp.where(low_half, odd, even) + pad
                top = jnp.where(low_half, odd_even(m_ref, 1, place), odd_even(m_ref, 0, place))
                spread = jnp.where(pad > 0, 0.0, top + jnp.log(total))
                first, second, third = three_parts(spread)
                aug = jnp.where(
                    slot == last + 1,
                    -first,
                    jnp.where(slot == last + 2, -second, jnp.where(slot == last + 3, -third, aug_ref[place])),
                )
                q = q_ref[0, pair, place]
                qa_ref[2 * pair, place] = jnp.where(low_half, q, aug).astype(LOW)
                qa_ref[2 * pair + 1, place] = jnp.where(low_half, aug, q).astype(LOW)
                v = q_ref[2, pair, place].astype(LOW).astype(F32)
                out = jnp.where(low_half, even, odd) / pltpu.roll(total, HD, 1) + pad * v
                ob_ref[place, pl.ds(pair * PAIR, PAIR)] = out.astype(LOW)


def odd_even(ref, which, place):
    return ref[which, place]


def normal(values):
    centred = values - jnp.mean(values, -1, keepdims=True)
    inverse = lax.rsqrt(jnp.mean(centred * centred, -1, keepdims=True) + EPSILON)
    return centred * inverse, inverse


def normal_back(cotangent, unit, inverse, gains):
    scaled = cotangent * gains
    return inverse * (
        scaled
        - jnp.mean(scaled, -1, keepdims=True)
        - unit * jnp.mean(scaled * unit, -1, keepdims=True)
    )


def dense_forward(x_ref, ob_ref, wo_ref, wi_ref, wf_ref, small_ref, bi_ref, n1_ref, n2_ref, inv_ref, yb_ref, gb_ref, gp_ref, z_ref, work_ref, u_ref):
    small = lambda index: small_ref[pl.ds(index, 1)]
    work_ref[...] = dot_nn(ob_ref[...], wo_ref[...])
    for place in pieces(SEQ):
        unit, inverse = normal(x_ref[place].astype(F32) + work_ref[place] + small(4))
        n1_ref[place] = unit
        inv_ref[place, pl.ds(0, HD)] = jnp.broadcast_to(inverse, (PIECE, HD))
        y = unit * small(2) + small(5)
        yb_ref[place] = y.astype(LOW)
        work_ref[place] = y + small(6)
    columns = 256
    count = wi_ref.shape[1] // columns

    def into(step):
        u_ref[step % 2] = dot_nn(yb_ref[...], wi_ref[:, pl.ds(step * columns, columns)])

    into(0)
    for step in range(count):
        if step + 1 < count:
            into(step + 1)
        lanes = pl.ds(step * columns, columns)
        for place in pieces(SEQ):
            g, slope = gelu_parts(u_ref[step % 2, place] + bi_ref[:, lanes])
            gb_ref[place, lanes] = g.astype(LOW)
            gp_ref[place, lanes] = slope.astype(LOW)
    work_ref[...] += dot_nn(gb_ref[...], wf_ref[...])
    for place in pieces(SEQ):
        unit, inverse = normal(work_ref[place])
        n2_ref[place] = unit
        inv_ref[place, pl.ds(HD, HD)] = jnp.broadcast_to(inverse, (PIECE, HD))
        z_ref[place] = (unit * small(3) + small(7)).astype(z_ref.dtype)


def fold(values):
    return jnp.sum(values.reshape(-1, 8, values.shape[-1]), 0)


def dense_backward(dz_ref, n1_ref, n2_ref, inv_ref, yb_ref, gb_ref, gp_ref, ob_ref, wo_ref, wi_ref, wf_ref, small_ref, dr_ref, dob_ref, gwo_ref, gwi_ref, gwf_ref, gsmall_ref, gbi_ref, low_ref, u_ref, du_ref):
    small = lambda index: small_ref[pl.ds(index, 1)]
    for place in pieces(SEQ):
        dz = dz_ref[place].astype(F32)
        unit = n2_ref[place]
        gsmall_ref[3] += fold(dz * unit)
        gsmall_ref[7] += fold(dz)
        dr = normal_back(dz, unit, inv_ref[place, pl.ds(HD, 1)], small(3))
        dr_ref[place] = dr
        df = dr.astype(LOW)
        low_ref[place] = df
        gsmall_ref[6] += fold(df.astype(F32))
    columns = 256
    count = wi_ref.shape[1] // columns

    def back(step):
        u_ref[step % 2] = dot_nt(low_ref[...], wf_ref[pl.ds(step * columns, columns)])

    back(0)
    for step in range(count):
        if step + 1 < count:
            back(step + 1)
        lanes = pl.ds(step * columns, columns)
        gwf_ref[:, lanes] += dot_tn(low_ref[...], gb_ref[:, lanes])
        for place in pieces(SEQ):
            du = (u_ref[step % 2, place] * gp_ref[place, lanes].astype(F32)).astype(LOW)
            du_ref[place, lanes] = du
            gbi_ref[:, lanes] += fold(du.astype(F32))
        gwi_ref[:, lanes] += dot_tn(yb_ref[...], du_ref[:, lanes])
    u_ref[0] = dot_nt(du_ref[...], wi_ref[...])
    for place in pieces(SEQ):
        dy = dr_ref[place] + u_ref[0, place]
        unit = n1_ref[place]
        gsmall_ref[2] += fold(dy * unit)
        gsmall_ref[5] += fold(dy)
        dr = normal_back(dy, unit, inv_ref[place, pl.ds(0, 1)], small(2))
        dr_ref[place] = dr
        da = dr.astype(LOW)
        low_ref[place] = da
        gsmall_ref[4] += fold(da.astype(F32))
    gwo_ref[...] += dot_tn(ob_ref[...], low_ref[...])
    dob_ref[...] = dot_nt(low_ref[...], wo_ref[...]).astype(LOW)


def attention_backward(row, lengths_ref, x, dob_ref, ob_ref, qa_ref, ka_ref, va_ref, wq_ref, dr_ref, dx_ref, gwq_ref, gbias_ref, da_ref, p_ref, ds_ref, s_ref, dqkv_ref, dq_ref, pad_ref, kt_ref, dqt_ref):
    width = HEADS * HD
    half = SEQ // 2
    low_half, slot = lane_facts(PIECE)
    for start in range(0, SEQ, PIECE):
        place = pl.ds(start, PIECE)
        segment, pad, last = segments(lengths_ref, row, start, PIECE)
        pad_ref[place] = pad
        for pair in range(HEADS // 2):
            lanes = pl.ds(pair * PAIR, PAIR)
            dob = dob_ref[place, lanes].astype(F32)
            product = dob * ob_ref[place, lanes].astype(F32)
            even = jnp.sum(jnp.where(low_half, product, 0.0), -1, keepdims=True)
            odd = jnp.sum(jnp.where(low_half, 0.0, product), -1, keepdims=True)
            first, second, third = three_parts(jnp.where(low_half, odd, even))
            aug = jnp.where(
                slot == 0, -first, jnp.where(slot == 1, -second, jnp.where(slot == 2, -third, 0.0))
            )
            da_ref[2 * pair, place] = jnp.where(low_half, dob, aug).astype(LOW)
            da_ref[2 * pair + 1, place] = jnp.where(low_half, aug, dob).astype(LOW)
    for pair in range(HEADS // 2):
        low_half, unused = lane_facts(SEQ)
        keys = jnp.where(low_half, ka_ref[2 * pair].astype(F32), ka_ref[2 * pair + 1].astype(F32))
        kt_ref[pl.ds(pair * PAIR, PAIR)] = keys.T.astype(LOW)
    low_half, slot = lane_facts(PIECE)
    units = [(head, part) for head in range(HEADS) for part in range(2)]

    def scores(unit):
        head, part = units[unit]
        keys = pl.ds(part * half, half)
        s_ref[0, unit % 2] = dot_nt(ka_ref[head, keys], qa_ref[head])
        s_ref[1, unit % 2] = dot_nt(va_ref[head, keys], da_ref[head])

    def weigh(unit):
        for place in pieces(half):
            p = jnp.exp(s_ref[0, unit % 2, place])
            p_ref[unit % 2, place] = p.astype(LOW)
            ds_ref[unit % 2, place] = (p * s_ref[1, unit % 2, place]).astype(LOW)

    scores(0)
    for unit in range(len(units)):
        if unit + 1 < len(units):
            scores(unit + 1)
        weigh(unit)
        head, part = units[unit]
        keys = pl.ds(part * half, half)
        side = head % 2
        dq_ref[1, side, keys] = dot_nn(ds_ref[unit % 2], qa_ref[head])
        dq_ref[2, side, keys] = dot_nn(p_ref[unit % 2], da_ref[head])
        lines = pl.ds(side * HD, HD)
        dq = dot_nn(kt_ref[pl.ds(head * HD, HD), keys], ds_ref[unit % 2])
        if part:
            dqt_ref[lines] += dq
        else:
            dqt_ref[lines] = dq
        if side and part:
            pair = head // 2
            dq_ref[0, 0] = dqt_ref[...].T
            for start in range(0, SEQ, PIECE):
                place = pl.ds(start, PIECE)
                dq = dq_ref[0, 0, place] * HD**-0.5
                dk = jnp.where(low_half, dq_ref[1, 0, place], dq_ref[1, 1, place])
                dv = jnp.where(low_half, dq_ref[2, 0, place], dq_ref[2, 1, place])
                dv = dv + pad_ref[place] * dob_ref[place, pl.ds(pair * PAIR, PAIR)].astype(F32)
                for block, value in enumerate((dq, dk, dv)):
                    lanes = pl.ds(block * width + pair * PAIR, PAIR)
                    value = value.astype(LOW)
                    dqkv_ref[place, lanes] = value
                    if block != 1:
                        into = pl.ds(pair * PAIR, PAIR)
                        gbias_ref[block // 2, :, into] += fold(value.astype(F32))
    gwq_ref[...] += dot_tn(x, dqkv_ref[...])
    dx_ref[...] = (dr_ref[...] + dot_nt(dqkv_ref[...], wq_ref[...])).astype(dx_ref.dtype)


def unpack_matrix(raw_ref, at, into_ref):
    width = into_ref.shape[0]
    for start in range(0, into_ref.shape[1], width):
        block = raw_ref[:, :, pl.ds(at + start, width)].astype(F32)
        block = block.reshape(GROUPS + (width,)).swapaxes(0, 1).reshape(width, width)
        into_ref[:, pl.ds(start, width)] = block.astype(LOW)


def unpack_stacked(raw_ref, at, into_ref):
    width = into_ref.shape[1]
    count = into_ref.shape[0] // width
    blocks = [
        raw_ref[:, :, pl.ds(at + step * width, width)].astype(F32).reshape(GROUPS + (width,))
        for step in range(count)
    ]
    outer, inner, rows = GROUPS
    for place in range(inner):
        part = jnp.stack([jnp.stack([block[f, place] for block in blocks]) for f in range(outer)])
        size = outer * count * rows
        into_ref[pl.ds(place * size, size)] = part.reshape(size, width).astype(LOW)


def sources(rows, columns):
    line = lax.broadcasted_iota(jnp.int32, (rows, columns), 0)
    outer, inner, height = GROUPS
    device = (line // height) % inner * outer + line // (inner * height)
    return device, line % height


def unpack_vectors(raw_ref, at, layer):
    outer, inner, rows = GROUPS
    total = outer * inner * rows
    raw = raw_ref[:, :, pl.ds(at, 128)].reshape(total, 128)
    lane = lax.broadcasted_iota(jnp.int32, (128, total), 0)
    column = lax.broadcasted_iota(jnp.int32, (128, total), 1)
    pick = jnp.where(lane == rows * layer + column % rows, 1.0, 0.0).astype(LOW)
    spread = dot_nn(raw, pick)
    device, unused = sources(total, total)
    column = lax.broadcasted_iota(jnp.int32, (total, total), 1)
    spread = jnp.where(column // rows == device, spread, 0.0)
    return jnp.sum(spread.reshape(outer * inner, rows, total), 0)


def unpack_hidden(raw_ref, at, layer, hidden):
    outer, inner, rows = GROUPS
    total = outer * inner * rows
    height = hidden // (outer * inner)
    raw = raw_ref[:, :, pl.ds(at, 128)].reshape(total, 128)
    lane = lax.broadcasted_iota(jnp.int32, (128, hidden), 0)
    column = lax.broadcasted_iota(jnp.int32, (128, hidden), 1)
    pick = jnp.where(lane == 2 * rows + column % height, 1.0, 0.0).astype(LOW)
    spread = dot_nn(raw, pick)
    device, within = sources(total, hidden)
    column = lax.broadcasted_iota(jnp.int32, (total, hidden), 1)
    spread = jnp.where((column // height == device) & (within == layer), spread, 0.0)
    return jnp.sum(spread, 0, keepdims=True)


def pack_matrix(sum_ref, sent_ref, at):
    width = sum_ref.shape[0]
    outer, inner, rows = GROUPS
    for start in range(0, sum_ref.shape[1], width):
        block = sum_ref[:, pl.ds(start, width)].reshape(inner, outer, rows, width)
        block = block.swapaxes(0, 1).reshape(outer, inner * rows, width)
        sent_ref[:, :, pl.ds(at + start, width)] = block.astype(LOW)


def pack_stacked(sum_ref, sent_ref, at):
    width = sum_ref.shape[0]
    outer, inner, rows = GROUPS
    count = sum_ref.shape[1] // width
    near = inner // count
    for step in range(count):
        block = sum_ref[:, pl.ds(step * width, width)].T
        block = block.reshape(near, outer, count, rows, width)
        for part in range(count):
            piece = jnp.stack([block[:, f, part] for f in range(outer)])
            piece = piece.reshape(outer, near * rows, width)
            sent_ref[:, pl.ds(step * near * rows, near * rows), pl.ds(at + part * width, width)] = (
                piece.astype(LOW)
            )


def pack_shared(block, sent_ref, at):
    outer, inner, rows = GROUPS
    columns = block.shape[1]
    block = jnp.broadcast_to(block[None], (outer * inner, rows, columns))
    sent_ref[:, :, pl.ds(at, columns)] = block.reshape(outer, inner * rows, columns).astype(LOW)


def pack_attention(gwq_ref, gbias_ref, sent_ref, at):
    pack_matrix(gwq_ref, sent_ref, at)
    width = gwq_ref.shape[0]
    line = lax.broadcasted_iota(jnp.int32, (8, width), 0)
    sums = [jnp.sum(gbias_ref[index], 0, keepdims=True) for index in range(2)]
    block = jnp.where(line == 0, sums[0], jnp.where(line == 1, sums[1], 0.0))
    pack_shared(block, sent_ref, at + 3 * width)


def pack_dense(gwo_ref, gwi_ref, gwf_ref, gsmall_ref, gbi_ref, sent_ref, at):
    width, hidden = gwi_ref.shape
    pack_matrix(gwo_ref, sent_ref, at)
    pack_matrix(gwi_ref, sent_ref, at + width)
    pack_stacked(gwf_ref, sent_ref, at + width + hidden)
    at = at + width + 2 * hidden
    pack_shared(jnp.sum(gsmall_ref[...], 1), sent_ref, at)
    line = jnp.sum(gbi_ref[...], 0, keepdims=True)
    size = hidden // 8
    block = jnp.concatenate([line[:, step * size : (step + 1) * size] for step in range(8)], 0)
    pack_shared(block, sent_ref, at + width)


def shape_of(array):
    return jax.ShapeDtypeStruct(array.shape, array.dtype)


def by_row(shape):
    if len(shape) == 2:
        return pl.BlockSpec((SEQ, shape[1]), lambda row: (row, 0))
    return pl.BlockSpec((None,) + tuple(shape[1:]), lambda row: (row,) + (0,) * (len(shape) - 1))


def whole(shape):
    return pl.BlockSpec(tuple(shape), lambda row: (0,) * len(shape))


def run_rows(body, lengths, rowwise, fixed, row_outs, sent, scratch, cost, setup, finish, after=()):
    count = lengths.shape[0]
    cuts = [len(rowwise), len(fixed), len(after), len(row_outs), len(sent), len(scratch)]

    def kernel(lengths_ref, *refs):
        row = pl.program_id(0)
        groups = []
        at = 0
        for cut in cuts:
            groups.append(refs[at : at + cut])
            at += cut
        rows_in, fixed_in, unused, rows_out, sent_out, work = groups

        @pl.when(row == 0)
        def _():
            setup(fixed_in, work)

        body(row, lengths_ref, rows_in, rows_out, work)

        if sent:

            @pl.when(row == count - 1)
            def _():
                finish(work, fixed_in, sent_out[0])

    return pl.pallas_call(
        kernel,
        grid=(count,),
        in_specs=[pl.BlockSpec(memory_space=pltpu.SMEM)]
        + [by_row(array.shape) for array in rowwise]
        + [whole(array.shape) for array in fixed]
        + [pl.BlockSpec(memory_space=pl.ANY) for array in after],
        out_specs=[by_row(part.shape) for part in row_outs] + [whole(part.shape) for part in sent],
        out_shape=list(row_outs) + list(sent),
        scratch_shapes=list(scratch),
        compiler_params=pltpu.CompilerParams(
            dimension_semantics=("arbitrary",), vmem_limit_bytes=MEMORY
        ),
        cost_estimate=pl.CostEstimate(flops=cost, bytes_accessed=8 * 2**20, transcendentals=0),
    )(lengths, *rowwise, *fixed, *after)


def struct(shape, dtype):
    return jax.ShapeDtypeStruct(tuple(shape), dtype)


FORWARD_SCRATCH = lambda: [
    pltpu.VMEM((2, SEQ // 2, SEQ), F32),
    pltpu.VMEM((2, SEQ // 2, SEQ), LOW),
    pltpu.VMEM((2, SEQ, PAIR), F32),
    pltpu.VMEM((SEQ, PAIR), F32),
    pltpu.VMEM((3, HEADS // 2, SEQ, PAIR), F32),
    pltpu.VMEM((SEQ, PAIR), F32),
]
BACKWARD_SCRATCH = lambda: [
    pltpu.VMEM((HEADS, SEQ, PAIR), LOW),
    pltpu.VMEM((2, SEQ // 2, SEQ), LOW),
    pltpu.VMEM((2, SEQ // 2, SEQ), LOW),
    pltpu.VMEM((2, 2, SEQ // 2, SEQ), F32),
    pltpu.VMEM((SEQ, 3 * HEADS * HD), LOW),
    pltpu.VMEM((3, 2, SEQ, PAIR), F32),
    pltpu.VMEM((SEQ, PAIR), F32),
    pltpu.VMEM((HEADS * HD, SEQ), LOW),
    pltpu.VMEM((PAIR, SEQ), F32),
]


def attention_outs(rows, tokens, width):
    heads = (rows, HEADS, SEQ, PAIR)
    return [struct(heads, LOW)] * 3 + [struct((tokens, width), LOW)]


def dense_outs(tokens, width, hidden):
    return [
        struct((tokens, width), F32),
        struct((tokens, width), F32),
        struct((tokens, PAIR), F32),
        struct((tokens, width), LOW),
        struct((tokens, hidden), LOW),
        struct((tokens, hidden), LOW),
    ]


def vmem(shape, dtype):
    return pltpu.VMEM(tuple(shape), dtype)


def attention_weights(width):
    return [vmem((width, 3 * width), LOW), vmem((1, 3 * width), F32)]


def dense_weights(width, hidden):
    return [
        vmem((width, width), LOW),
        vmem((width, hidden), LOW),
        vmem((hidden, width), LOW),
        vmem((8, width), F32),
        vmem((1, hidden), F32),
    ]


def dense_sums(width, hidden):
    return [
        vmem((width, width), F32),
        vmem((width, hidden), F32),
        vmem((width, hidden), F32),
        vmem((8, 8, width), F32),
        vmem((8, hidden), F32),
    ]


def attention_sums(width):
    return [vmem((width, 3 * width), F32), vmem((2, 8, width), F32)]


def dense_work(width, hidden):
    return [vmem((SEQ, width), LOW), vmem((2, SEQ, width), F32), vmem((SEQ, hidden), LOW)]


def set_attention(layer, urgent_ref, raw_ref, at, wq_ref, bias_ref):
    width = wq_ref.shape[0]
    unpack_matrix(raw_ref, at, wq_ref)
    vectors = unpack_vectors(urgent_ref, 3 * width, layer)
    bias_ref[:, :width] = vectors[0:1]
    bias_ref[:, width : 2 * width] = jnp.zeros((1, width), F32)
    bias_ref[:, 2 * width :] = vectors[1:2]


def set_dense(layer, urgent_ref, raw_ref, at, wo_ref, wi_ref, wf_ref, small_ref, bi_ref):
    width, hidden = wi_ref.shape
    unpack_matrix(raw_ref, at, wo_ref)
    unpack_matrix(raw_ref, at + width, wi_ref)
    unpack_stacked(raw_ref, at + width + hidden, wf_ref)
    small_ref[...] = unpack_vectors(urgent_ref, 3 * width, layer)
    bi_ref[...] = unpack_hidden(urgent_ref, 3 * width, layer, hidden)


def clear(refs):
    for ref in refs:
        ref[...] = jnp.zeros(ref.shape, ref.dtype)


def attention_kernel(layer, lengths, x, urgent, raw, at):
    rows, (tokens, width) = lengths.shape[0], x.shape

    def setup(fixed, work):
        set_attention(layer, fixed[0], fixed[-1], at, *work[:2])

    def body(row, lengths_ref, rowwise, outs, work):
        attention_forward(row, lengths_ref, rowwise[0][...].astype(LOW), *work[:2], *outs, *work[2:])

    fixed = [urgent] if raw is urgent else [urgent, raw]
    return run_rows(
        body, lengths, [x], fixed, attention_outs(rows, tokens, width), [],
        attention_weights(width) + FORWARD_SCRATCH(), 4 * 10**9, setup, None,
    )


def dense_kernel(layer, lengths, x, ob, urgent, raw, at, hidden, after):
    tokens, width = x.shape

    def setup(fixed, work):
        set_dense(layer, *fixed, at, *work[:5])

    def body(row, lengths_ref, rowwise, outs, work):
        dense_forward(*rowwise, *work[:5], *outs, *work[5:])

    return run_rows(
        body, lengths, [x, ob], [urgent, raw],
        dense_outs(tokens, width, hidden) + [struct((tokens, width), F32)], [],
        dense_weights(width, hidden) + [vmem((SEQ, width), F32), vmem((2, SEQ, width), F32)],
        5 * 10**9, setup, None, after,
    )


def turn_kernel(layer, lengths, x, ob, cotangent, urgent, raw, at, hidden):
    tokens, width = x.shape
    columns = width + 2 * hidden + width + hidden // 8

    def setup(fixed, work):
        set_dense(layer, *fixed, at, *work[:5])
        clear(work[5:10])

    def body(row, lengths_ref, rowwise, outs, work):
        x_ref, ob_ref, dz_ref = rowwise
        z_ref, dr_ref, dob_ref = outs
        weights, sums, kept = work[:5], work[5:10], work[10:16]
        work_ref, low_ref, u_ref, du_ref = work[16:]
        dense_forward(x_ref, ob_ref, *weights, *kept, z_ref, work_ref, u_ref)
        dense_backward(
            dz_ref, *kept, ob_ref, *weights[:4], dr_ref, dob_ref, *sums, low_ref, u_ref, du_ref
        )

    def finish(work, fixed, sent_ref):
        pack_dense(*work[5:10], sent_ref, 0)

    kept = [vmem((SEQ,) + part.shape[1:], part.dtype) for part in dense_outs(tokens, width, hidden)]
    return run_rows(
        body, lengths, [x, ob, cotangent], [urgent, raw],
        [struct((tokens, width), LOW), struct((tokens, width), F32), struct((tokens, width), LOW)],
        [struct((4, 64, columns), LOW)],
        dense_weights(width, hidden) + dense_sums(width, hidden) + kept
        + [vmem((SEQ, width), F32)] + dense_work(width, hidden),
        10**10, setup, finish,
    )


def attention_back_kernel(layer, lengths, upper, urgent, raw, dtype, after):
    tokens, width = upper[0].shape

    def setup(fixed, work):
        set_attention(layer, fixed[0], fixed[-1], 0, *work[:2])
        clear(work[2:4])

    def body(row, lengths_ref, rowwise, outs, work):
        attention_backward(
            row, lengths_ref, rowwise[0][...].astype(LOW), *rowwise[1:6], work[0], rowwise[6],
            outs[0], *work[2:4], *work[4:],
        )

    def finish(work, fixed, sent_ref):
        pack_attention(*work[2:4], sent_ref, 0)

    fixed = [urgent] if raw is urgent else [urgent, raw]
    return run_rows(
        body, lengths, list(upper), fixed, [struct((tokens, width), dtype)],
        [struct((4, 64, 4 * width), LOW)],
        attention_weights(width) + attention_sums(width) + BACKWARD_SCRATCH(),
        8 * 10**9, setup, finish, after,
    )


def dense_back_kernel(layer, lengths, dz, lower, urgent, raw, at, hidden, joined, after):
    tokens, width = dz.shape
    ahead = joined.shape[2]
    columns = ahead + width + 2 * hidden + width + hidden // 8

    def setup(fixed, work):
        set_dense(layer, *fixed[:2], at, *work[:5])
        clear(work[5:10])

    def body(row, lengths_ref, rowwise, outs, work):
        dense_backward(*rowwise, *work[:4], *outs, *work[5:])

    def finish(work, fixed, sent_ref):
        sent_ref[:, :, pl.ds(0, ahead)] = fixed[2][...]
        pack_dense(*work[5:10], sent_ref, ahead)

    return run_rows(
        body, lengths, [dz] + list(lower), [urgent, raw, joined],
        [struct((tokens, width), F32), struct((tokens, width), LOW)],
        [struct((4, 64, columns), LOW)],
        dense_weights(width, hidden) + dense_sums(width, hidden) + dense_work(width, hidden),
        7 * 10**9, setup, finish, after,
    )


def hold(array, after):
    def kernel(*refs):
        pass

    anywhere = pl.BlockSpec(memory_space=pl.ANY)
    return pl.pallas_call(
        kernel,
        in_specs=[anywhere] * (1 + len(after)),
        out_specs=anywhere,
        out_shape=shape_of(array),
        input_output_aliases={0: 0},
    )(array, *after)


def pack_parameters(
    attn_weight, attn_bias, out_weight, ffn_in, ffn_in_bias, ffn_out, norm_gain, shifts
):
    depth, rows, width = out_weight.shape
    copies = GROUPS[1]
    hidden = ffn_in.shape[2]
    early = 4 * width + 2 * hidden + 128
    columns = 4 * width + 2 * hidden
    height = ffn_in_bias.shape[1]

    def kernel(wq_ref, ab_ref, wo_ref, wi_ref, bi_ref, wf_ref, gain_ref, shift_ref, first_ref, rest_ref, small_ref):
        def put(ref, block, at):
            block = jnp.broadcast_to(block.astype(F32)[None], (copies,) + block.shape)
            block = block.reshape(copies * block.shape[1], block.shape[2])
            ref[:, pl.ds(at, block.shape[1])] = block.astype(LOW)

        small_ref[...] = jnp.zeros(small_ref.shape, F32)
        for layer in range(depth):
            lanes = pl.ds(rows * layer, rows)
            small_ref[0:2, lanes] = ab_ref[layer].astype(F32)
            small_ref[2:4, lanes] = gain_ref[layer].astype(F32)
            small_ref[4:8, lanes] = shift_ref[layer].astype(F32)
        small_ref[0:depth, pl.ds(2 * rows, height)] = bi_ref[...].astype(F32)
        put(first_ref, wq_ref[0], 0)
        put(first_ref, small_ref[...], 3 * width)
        for layer, ref, at in ((0, first_ref, 3 * width + 128), (1, rest_ref, 3 * width)):
            if layer:
                put(ref, wq_ref[layer], 0)
            put(ref, wo_ref[layer], at)
            put(ref, wi_ref[layer], at + width)
            at += width + hidden
            down = wf_ref[layer].astype(F32)
            for step in range(hidden // width):
                put(ref, down[step * rows : (step + 1) * rows], at)
                at += width

    return pl.pallas_call(
        kernel,
        in_specs=[pl.BlockSpec(memory_space=pltpu.VMEM)] * 8,
        out_shape=[struct((copies * rows, early), LOW), struct((copies * rows, columns), LOW)],
        scratch_shapes=[vmem((rows, 128), F32)],
        compiler_params=pltpu.CompilerParams(vmem_limit_bytes=MEMORY),
    )(attn_weight, attn_bias, out_weight, ffn_in, ffn_in_bias, ffn_out, norm_gain, shifts)


def add_parts(received, after=(), passed=None, joined=None):
    extra = [] if passed is None else [passed]
    inner = [] if joined is None else [joined]
    ahead = 0 if joined is None else joined.shape[1]
    rows, lanes_in = received.shape[1:]

    def kernel(in_ref, *refs):
        out_ref = refs[len(inner) + len(extra) + len(after)]
        if inner:
            out_ref[:, pl.ds(0, ahead)] = refs[0][...]
        columns = 256
        for start in range(0, lanes_in, columns):
            size = min(columns, lanes_in - start)
            total = jnp.sum(in_ref[:, :, pl.ds(start, size)].astype(F32), 0)
            out_ref[:, pl.ds(ahead + start, size)] = total.astype(LOW)

    anywhere = pl.BlockSpec(memory_space=pl.ANY)
    near = pl.BlockSpec(memory_space=pltpu.VMEM)
    found = pl.pallas_call(
        kernel,
        in_specs=[near] * (1 + len(inner)) + [anywhere] * (len(extra) + len(after)),
        out_specs=[near] + [anywhere] * len(extra),
        out_shape=[struct((rows, ahead + lanes_in), LOW)] + [shape_of(part) for part in extra],
        input_output_aliases={1 + len(inner): 1} if extra else {},
        compiler_params=pltpu.CompilerParams(vmem_limit_bytes=MEMORY),
    )(received, *inner, *extra, *after)
    return found if extra else found[0]


def write_gradients(place, tail, front, depth, width, hidden):
    rows = GROUPS[2]
    last = front.shape[1] - 4 * width
    height = hidden // DEVICES

    def kernel(place_ref, tail_ref, front_ref, gwq_ref, gab_ref, gwo_ref, gwi_ref, gbi_ref, gwf_ref, gain_ref, shift_ref):
        spot = place_ref[0]

        def total(ref, at, columns):
            block = ref[:, pl.ds(at, columns)].astype(F32)
            return jnp.sum(block.reshape(-1, rows, columns), 0)

        def own(block, size):
            return pltpu.roll(block, block.shape[1] - spot * size, 1)

        for layer, ref, at in ((0, front_ref, last), (1, front_ref, 0)):
            gwq_ref[layer] = total(ref, at, 3 * width)
            gab_ref[layer] = own(total(ref, at + 3 * width, width), rows)[0:2, 0:rows]
        for layer, ref, at in ((0, front_ref, 4 * width), (1, tail_ref, 0)):
            gwo_ref[layer] = total(ref, at, width)
            gwi_ref[layer] = total(ref, at + width, hidden)
            for step in range(hidden // width):
                gwf_ref[layer, pl.ds(step * rows, rows)] = total(
                    ref, at + width + hidden + step * width, width
                )
            at += width + 2 * hidden
            small = own(total(ref, at, width), rows)
            gain_ref[layer] = small[2:4, 0:rows]
            shift_ref[layer] = small[4:8, 0:rows]
            line = total(ref, at + width, hidden // 8)
            line = jnp.concatenate([line[step : step + 1] for step in range(8)], 1)
            gbi_ref[pl.ds(layer, 1)] = own(line, height)[:, 0:height]

    outs = [
        struct((depth, rows, 3 * width), F32),
        struct((depth, 2, rows), F32),
        struct((depth, rows, width), F32),
        struct((depth, rows, hidden), F32),
        struct((depth, height), F32),
        struct((depth, height, width), F32),
        struct((depth, 2, rows), F32),
        struct((depth, 4, rows), F32),
    ]
    return pl.pallas_call(
        kernel,
        in_specs=[pl.BlockSpec(memory_space=pltpu.SMEM)] + [pl.BlockSpec(memory_space=pltpu.VMEM)] * 2,
        out_shape=outs,
        compiler_params=pltpu.CompilerParams(vmem_limit_bytes=MEMORY),
    )(place, tail, front)


def exchange(parts, axis):
    return lax.all_to_all(parts, axis, 0, 0, tiled=True)


def local(
    hidden_in,
    lengths,
    grad_out,
    attn_weight,
    attn_bias,
    out_weight,
    ffn_in,
    ffn_in_bias,
    ffn_out,
    norm_gain,
    shifts,
):
    depth, rows, width = out_weight.shape
    hidden = ffn_in.shape[2]
    first, second = lax.axis_size("dp"), lax.axis_size("fsdp")
    fits = (second, first, rows) == GROUPS
    urgent_size = 3 * width + 128
    if fits:
        early, later = pack_parameters(
            attn_weight, attn_bias, out_weight, ffn_in, ffn_in_bias, ffn_out, norm_gain, shifts
        )
        early = exchange(early, "dp")
        urgent = early[:, :urgent_size]
        urgent = exchange(jnp.broadcast_to(urgent[None], (second,) + urgent.shape), "fsdp")
        raw0 = lax.all_gather(early[:, urgent_size:], "fsdp")
        later = exchange(hold(later, (urgent,)), "dp")
    else:
        urgent, raw0, raw1 = gather_other(
            attn_weight, attn_bias, out_weight, ffn_in, ffn_in_bias, ffn_out, norm_gain, shifts
        )
        ready = ()

    qa0, ka0, va0, ob0 = attention_kernel(0, lengths, hidden_in, urgent, urgent, 0)
    if fits:
        later = hold(later, (ob0,))
        raw1 = lax.all_gather(later, "fsdp")
        ready = (later,)
    n1, n2, inv, yb, gb, gp, z0 = dense_kernel(
        0, lengths, hidden_in, ob0, urgent, raw0, 0, hidden, ready
    )
    qa1, ka1, va1, ob1 = attention_kernel(1, lengths, z0, urgent, raw1, 0)
    hidden_out, dr1, dob1, sent_a = turn_kernel(
        1, lengths, z0, ob1, grad_out, urgent, raw1, 3 * width, hidden
    )
    dx1, sent_q = attention_back_kernel(
        1, lengths, (z0, dob1, ob1, qa1, ka1, va1, dr1), urgent, raw1, F32, (sent_a,)
    )
    ready = ()
    if fits:
        tail = add_parts(exchange(sent_a, "fsdp"), (sent_q,))
        ready = (tail,)
    dr0, dob0, sent_b = dense_back_kernel(
        0, lengths, dx1, (n1, n2, inv, yb, gb, gp, ob0), urgent, raw0, 0, hidden, sent_q, ready
    )
    if fits:
        tail = exchange(tail, "dp")
        ready = (tail,)
    grad_in, sent_c = attention_back_kernel(
        0, lengths, (hidden_in, dob0, ob0, qa0, ka0, va0, dr0), urgent, urgent, LOW,
        (sent_b,) + ready,
    )
    if fits:
        front, sent_c = add_parts(exchange(sent_b, "fsdp"), (), sent_c)
        front = add_parts(exchange(sent_c, "fsdp"), (), None, front)
        front = exchange(front, "dp")
        place = lax.axis_index(("dp", "fsdp")).astype(jnp.int32).reshape(1)
        grads = write_gradients(place, tail, front, depth, width, hidden)
    else:
        grads = scatter_other(sent_a, sent_b, sent_c, rows, width, hidden)
    return (hidden_out, grad_in, *grads)


def gather_other(
    attn_weight, attn_bias, out_weight, ffn_in, ffn_in_bias, ffn_out, norm_gain, shifts
):
    axes = ("dp", "fsdp")
    gather = lambda part, axis: lax.all_gather(part, axes, axis=axis, tiled=True)
    depth, unused, width = out_weight.shape
    hidden = ffn_in.shape[2]
    outer, inner, rows = GROUPS
    vectors = gather(jnp.concatenate([attn_bias, norm_gain, shifts], 1), 2)
    line = gather(ffn_in_bias, 1)

    def order(natural):
        return (
            natural.reshape(inner, outer, rows, -1).swapaxes(0, 1).reshape(outer, inner * rows, -1)
        )

    def stacked(part):
        part = part.reshape(DEVICES, -1, rows, width)
        return order(part.swapaxes(1, 2).reshape(width, -1))

    small = vectors.reshape(depth, 8, DEVICES, rows).transpose(2, 1, 0, 3).reshape(width, -1)
    line = line.reshape(depth, DEVICES, -1).swapaxes(0, 1)
    line = jnp.pad(line, ((0, 0), (0, 8 - depth), (0, 0))).reshape(width, -1)
    small = jnp.concatenate([small, line], 1)
    small = jnp.pad(small, ((0, 0), (0, 128 - small.shape[1])))
    wq, wo, wi, wf = (gather(part, 1) for part in (attn_weight, out_weight, ffn_in, ffn_out))
    urgent = jnp.concatenate([order(wq[0]), order(small)], 2)
    raw0 = jnp.concatenate([order(wo[0]), order(wi[0]), stacked(wf[0])], 2)
    raw1 = jnp.concatenate([order(wq[1]), order(wo[1]), order(wi[1]), stacked(wf[1])], 2)
    return urgent, raw0, raw1


def scatter_other(sent_a, sent_b, sent_c, own_rows, width, hidden):
    outer, inner, rows = GROUPS
    axes = ("dp", "fsdp")

    def natural(part):
        return part.reshape(outer, inner, rows, -1).swapaxes(0, 1).reshape(width, -1).astype(F32)

    def cut(part, sizes):
        found, at = [], 0
        for size in sizes:
            found.append(part[:, at : at + size])
            at += size
        return found

    dense = [width, hidden, hidden, width, hidden // 8]
    attention = [3 * width, width]
    wq0, ab0 = cut(natural(sent_c), attention)
    wq1, ab1, wo0, wi0, wf0, small0, bi0 = cut(natural(sent_b), attention + dense)
    wo1, wi1, wf1, small1, bi1 = cut(natural(sent_a), dense)

    def stacked(part):
        part = part.reshape(DEVICES, rows, -1, width).swapaxes(1, 2)
        return part.reshape(hidden, width)

    def spread(parts, axis):
        return lax.psum_scatter(jnp.stack(parts), axes, scatter_dimension=axis, tiled=True)

    return (
        spread([wq0, wq1], 1),
        spread([ab0[:2], ab1[:2]], 2),
        spread([wo0, wo1], 1),
        spread([wi0, wi1], 1),
        spread([bi0[:8].reshape(-1), bi1[:8].reshape(-1)], 1),
        spread([stacked(wf0), stacked(wf1)], 1),
        spread([small0[2:4], small1[2:4]], 2),
        spread([small0[4:8], small1[4:8]], 2),
    )


def solution(mesh):
    placed = (
        P(("dp", "fsdp"), None),
        P(("dp", "fsdp"), None),
        P(("dp", "fsdp"), None),
        P(None, ("dp", "fsdp"), None),
        P(None, None, ("dp", "fsdp")),
        P(None, ("dp", "fsdp"), None),
        P(None, ("dp", "fsdp"), None),
        P(None, ("dp", "fsdp")),
        P(None, ("dp", "fsdp"), None),
        P(None, None, ("dp", "fsdp")),
        P(None, None, ("dp", "fsdp")),
    )
    return jax.shard_map(
        local,
        mesh=mesh,
        in_specs=placed,
        out_specs=(
            P(("dp", "fsdp"), None),
            P(("dp", "fsdp"), None),
            P(None, ("dp", "fsdp"), None),
            P(None, None, ("dp", "fsdp")),
            P(None, ("dp", "fsdp"), None),
            P(None, ("dp", "fsdp"), None),
            P(None, ("dp", "fsdp")),
            P(None, ("dp", "fsdp"), None),
            P(None, None, ("dp", "fsdp")),
            P(None, None, ("dp", "fsdp")),
        ),
        check_vma=False,
    )
```

```python
from functools import partial

import jax
import jax.numpy as jnp
from jax import lax
from jax.experimental import pallas as pl
from jax.experimental.pallas import tpu as pltpu
from jax.sharding import PartitionSpec as P

HEADS = 4
HD = 64
SEQ = 512
PAIR = 2 * HD
FAR = -(2.0**100)
FLOOR = -1e20
EPSILON = 1e-12
PIECE = 256
SMALL = 128
GROUPS = (4, 8, 8)
DEVICES = 32
LOW = jnp.bfloat16
F32 = jnp.float32
MEMORY = 60 * 2**20


def dot_nn(left, right):
    return lax.dot_general(left, right, (((1,), (0,)), ((), ())), preferred_element_type=F32)


def dot_nt(left, right):
    return lax.dot_general(left, right, (((1,), (1,)), ((), ())), preferred_element_type=F32)


def dot_tn(left, right):
    return lax.dot_general(left, right, (((0,), (0,)), ((), ())), preferred_element_type=F32)


def pieces(total, size=PIECE):
    return [pl.ds(start, size) for start in range(0, total, size)]


def three_parts(values):
    first = values.astype(LOW).astype(F32)
    rest = values - first
    second = rest.astype(LOW).astype(F32)
    return first, second, rest - second


CURVE = (
    7.97882253e-01,
    3.63445176e-02,
    -4.47304308e-05,
    -5.04138899e-05,
    3.10523303e-06,
    -6.66676088e-08,
)
BELL = -0.5 / 0.6931471805599453


def gelu_parts(u):
    square = u * u
    near = jnp.minimum(square, 31.36)
    curve = CURVE[-1]
    for factor in CURVE[-2::-1]:
        curve = curve * near + factor
    bent = jnp.tanh(u * curve)
    half = 0.5 * u
    slope = (0.5 + 0.5 * bent) + (u * 0.3989422804014327) * jnp.exp2(square * BELL)
    return half + half * bent, slope


def lane_facts(rows):
    lane = lax.broadcasted_iota(jnp.int32, (rows, PAIR), 1)
    return lane < HD, lane % HD


def segments(lengths_ref, row, start, rows):
    places = lax.broadcasted_iota(jnp.int32, (rows, PAIR), 0) + start
    bound = jnp.int32(0)
    segment = jnp.zeros((rows, PAIR), jnp.int32)
    last = lengths_ref.shape[1] - 1
    for entry in range(last):
        bound = bound + lengths_ref[row, entry]
        segment = segment + (places >= bound).astype(jnp.int32)
    return segment, (segment == last).astype(F32), last


def attention_forward(row, lengths_ref, x, wq_ref, bias_ref, qa_ref, ka_ref, va_ref, ob_ref, s_ref, p_ref, m_ref, pad_ref, q_ref, aug_ref):
    width = HEADS * HD
    for block in range(3):
        for pair in range(HEADS // 2):
            at = block * width + pair * PAIR
            q_ref[block, pair] = dot_nn(x, wq_ref[:, at : at + PAIR]) + bias_ref[:, at : at + PAIR]
    for start in range(0, SEQ, PIECE):
        place = pl.ds(start, PIECE)
        low_half, slot = lane_facts(PIECE)
        segment, pad, last = segments(lengths_ref, row, start, PIECE)
        pad_ref[place] = pad
        aug_q = jnp.where(slot == segment, 1.0, 0.0)
        aug_ref[place] = aug_q
        seen = (slot == segment) & (slot != last)
        aug_k = jnp.where(slot <= last, jnp.where(seen, 0.0, FAR), jnp.where(slot <= last + 3, 1.0, 0.0))
        for pair in range(HEADS // 2):
            q = q_ref[0, pair, place] * HD**-0.5
            k = q_ref[1, pair, place]
            v = q_ref[2, pair, place]
            q_ref[0, pair, place] = q
            qa_ref[2 * pair, place] = jnp.where(low_half, q, aug_q).astype(LOW)
            qa_ref[2 * pair + 1, place] = jnp.where(low_half, aug_q, q).astype(LOW)
            ka_ref[2 * pair, place] = jnp.where(low_half, k, aug_k).astype(LOW)
            ka_ref[2 * pair + 1, place] = jnp.where(low_half, aug_k, k).astype(LOW)
            va_ref[2 * pair, place] = jnp.where(low_half, v, 1.0).astype(LOW)
            va_ref[2 * pair + 1, place] = jnp.where(low_half, 1.0, v).astype(LOW)
    half = SEQ // 2
    units = [(head, part) for head in range(HEADS) for part in range(2)]

    def scores(unit):
        head, part = units[unit]
        s_ref[unit % 2] = dot_nt(qa_ref[head, pl.ds(part * half, half)], ka_ref[head])

    def softmax(unit):
        head, part = units[unit]
        highest = jnp.maximum(jnp.max(s_ref[unit % 2], -1, keepdims=True), FLOOR)
        m_ref[head % 2, pl.ds(part * half, half)] = jnp.broadcast_to(highest, (half, PAIR))
        for start in range(0, half, SMALL):
            place = pl.ds(start, SMALL)
            s = s_ref[unit % 2, place] - highest[start : start + SMALL]
            p_ref[unit % 2, place] = jnp.exp(s).astype(LOW)

    def attend(unit):
        head, part = units[unit]
        return dot_nn(p_ref[unit % 2], va_ref[head])

    sums = {}
    scores(0)
    for unit in range(len(units)):
        if unit + 1 < len(units):
            scores(unit + 1)
        softmax(unit)
        head, part = units[unit]
        q_ref[1, head % 2, pl.ds(part * half, half)] = attend(unit)
        if head % 2 and part:
            pair = head // 2
            for start in range(0, SEQ, PIECE):
                place = pl.ds(start, PIECE)
                low_half, slot = lane_facts(PIECE)
                even = q_ref[1, 0, place]
                odd = q_ref[1, 1, place]
                pad = pad_ref[place]
                last = lengths_ref.shape[1] - 1
                total = jnp.where(low_half, odd, even) + pad
                top = jnp.where(low_half, odd_even(m_ref, 1, place), odd_even(m_ref, 0, place))
                spread = jnp.where(pad > 0, 0.0, top + jnp.log(total))
                first, second, third = three_parts(spread)
                aug = jnp.where(
                    slot == last + 1,
                    -first,
                    jnp.where(slot == last + 2, -second, jnp.where(slot == last + 3, -third, aug_ref[place])),
                )
                q = q_ref[0, pair, place]
                qa_ref[2 * pair, place] = jnp.where(low_half, q, aug).astype(LOW)
                qa_ref[2 * pair + 1, place] = jnp.where(low_half, aug, q).astype(LOW)
                v = q_ref[2, pair, place].astype(LOW).astype(F32)
                out = jnp.where(low_half, even, odd) / pltpu.roll(total, HD, 1) + pad * v
                ob_ref[place, pl.ds(pair * PAIR, PAIR)] = out.astype(LOW)


def odd_even(ref, which, place):
    return ref[which, place]


def normal(values):
    centred = values - jnp.mean(values, -1, keepdims=True)
    inverse = lax.rsqrt(jnp.mean(centred * centred, -1, keepdims=True) + EPSILON)
    return centred * inverse, inverse


def normal_back(cotangent, unit, inverse, gains):
    scaled = cotangent * gains
    return inverse * (
        scaled
        - jnp.mean(scaled, -1, keepdims=True)
        - unit * jnp.mean(scaled * unit, -1, keepdims=True)
    )


def dense_forward(x_ref, ob_ref, wo_ref, wi_ref, wf_ref, small_ref, bi_ref, n1_ref, n2_ref, inv_ref, yb_ref, gb_ref, gp_ref, z_ref, work_ref, u_ref):
    small = lambda index: small_ref[pl.ds(index, 1)]
    work_ref[...] = dot_nn(ob_ref[...], wo_ref[...])
    for place in pieces(SEQ):
        unit, inverse = normal(x_ref[place].astype(F32) + work_ref[place] + small(4))
        n1_ref[place] = unit
        inv_ref[place, pl.ds(0, HD)] = jnp.broadcast_to(inverse, (PIECE, HD))
        y = unit * small(2) + small(5)
        yb_ref[place] = y.astype(LOW)
        work_ref[place] = y + small(6)
    columns = 256
    count = wi_ref.shape[1] // columns

    def into(step):
        u_ref[step % 2] = dot_nn(yb_ref[...], wi_ref[:, pl.ds(step * columns, columns)])

    into(0)
    for step in range(count):
        if step + 1 < count:
            into(step + 1)
        lanes = pl.ds(step * columns, columns)
        for place in pieces(SEQ, SMALL):
            g, slope = gelu_parts(u_ref[step % 2, place] + bi_ref[:, lanes])
            gb_ref[place, lanes] = g.astype(LOW)
            gp_ref[place, lanes] = slope.astype(LOW)
    work_ref[...] += dot_nn(gb_ref[...], wf_ref[...])
    for place in pieces(SEQ):
        unit, inverse = normal(work_ref[place])
        n2_ref[place] = unit
        inv_ref[place, pl.ds(HD, HD)] = jnp.broadcast_to(inverse, (PIECE, HD))
        z_ref[place] = (unit * small(3) + small(7)).astype(z_ref.dtype)


def fold(values):
    return jnp.sum(values.reshape(-1, 8, values.shape[-1]), 0)


def dense_backward(dz_ref, n1_ref, n2_ref, inv_ref, yb_ref, gb_ref, gp_ref, ob_ref, wo_ref, wi_ref, wf_ref, small_ref, dr_ref, dob_ref, gwo_ref, gwi_ref, gwf_ref, gsmall_ref, gbi_ref, low_ref, u_ref, du_ref):
    small = lambda index: small_ref[pl.ds(index, 1)]
    for place in pieces(SEQ):
        dz = dz_ref[place].astype(F32)
        unit = n2_ref[place]
        gsmall_ref[3] += fold(dz * unit)
        gsmall_ref[7] += fold(dz)
        dr = normal_back(dz, unit, inv_ref[place, pl.ds(HD, 1)], small(3))
        dr_ref[place] = dr
        df = dr.astype(LOW)
        low_ref[place] = df
        gsmall_ref[6] += fold(df.astype(F32))
    columns = 256
    count = wi_ref.shape[1] // columns

    def back(step):
        u_ref[step % 2] = dot_nt(low_ref[...], wf_ref[pl.ds(step * columns, columns)])

    back(0)
    for step in range(count):
        if step + 1 < count:
            back(step + 1)
        lanes = pl.ds(step * columns, columns)
        gwf_ref[:, lanes] += dot_tn(low_ref[...], gb_ref[:, lanes])
        for place in pieces(SEQ, SMALL):
            du = (u_ref[step % 2, place] * gp_ref[place, lanes].astype(F32)).astype(LOW)
            du_ref[place, lanes] = du
            gbi_ref[:, lanes] += fold(du.astype(F32))
        gwi_ref[:, lanes] += dot_tn(yb_ref[...], du_ref[:, lanes])
    u_ref[0] = dot_nt(du_ref[...], wi_ref[...])
    for place in pieces(SEQ):
        dy = dr_ref[place] + u_ref[0, place]
        unit = n1_ref[place]
        gsmall_ref[2] += fold(dy * unit)
        gsmall_ref[5] += fold(dy)
        dr = normal_back(dy, unit, inv_ref[place, pl.ds(0, 1)], small(2))
        dr_ref[place] = dr
        da = dr.astype(LOW)
        low_ref[place] = da
        gsmall_ref[4] += fold(da.astype(F32))
    gwo_ref[...] += dot_tn(ob_ref[...], low_ref[...])
    dob_ref[...] = dot_nt(low_ref[...], wo_ref[...]).astype(LOW)


def attention_backward(row, lengths_ref, x, dob_ref, ob_ref, qa_ref, ka_ref, va_ref, wq_ref, dr_ref, dx_ref, gwq_ref, gbias_ref, da_ref, p_ref, ds_ref, s_ref, dqkv_ref, dq_ref, pad_ref, kt_ref, dqt_ref):
    width = HEADS * HD
    half = SEQ // 2
    low_half, slot = lane_facts(PIECE)
    for start in range(0, SEQ, PIECE):
        place = pl.ds(start, PIECE)
        segment, pad, last = segments(lengths_ref, row, start, PIECE)
        pad_ref[place] = pad
        for pair in range(HEADS // 2):
            lanes = pl.ds(pair * PAIR, PAIR)
            dob = dob_ref[place, lanes].astype(F32)
            product = dob * ob_ref[place, lanes].astype(F32)
            even = jnp.sum(jnp.where(low_half, product, 0.0), -1, keepdims=True)
            odd = jnp.sum(jnp.where(low_half, 0.0, product), -1, keepdims=True)
            first, second, third = three_parts(jnp.where(low_half, odd, even))
            aug = jnp.where(
                slot == 0, -first, jnp.where(slot == 1, -second, jnp.where(slot == 2, -third, 0.0))
            )
            da_ref[2 * pair, place] = jnp.where(low_half, dob, aug).astype(LOW)
            da_ref[2 * pair + 1, place] = jnp.where(low_half, aug, dob).astype(LOW)
    for pair in range(HEADS // 2):
        low_half, unused = lane_facts(SEQ)
        keys = jnp.where(low_half, ka_ref[2 * pair].astype(F32), ka_ref[2 * pair + 1].astype(F32))
        kt_ref[pl.ds(pair * PAIR, PAIR)] = keys.T.astype(LOW)
    low_half, slot = lane_facts(PIECE)
    units = [(head, part) for head in range(HEADS) for part in range(2)]

    def scores(unit):
        head, part = units[unit]
        keys = pl.ds(part * half, half)
        s_ref[0, unit % 2] = dot_nt(ka_ref[head, keys], qa_ref[head])
        s_ref[1, unit % 2] = dot_nt(va_ref[head, keys], da_ref[head])

    def weigh(unit):
        for place in pieces(half, SMALL):
            p = jnp.exp(s_ref[0, unit % 2, place])
            p_ref[unit % 2, place] = p.astype(LOW)
            ds_ref[unit % 2, place] = (p * s_ref[1, unit % 2, place]).astype(LOW)

    scores(0)
    for unit in range(len(units)):
        if unit + 1 < len(units):
            scores(unit + 1)
        weigh(unit)
        head, part = units[unit]
        keys = pl.ds(part * half, half)
        side = head % 2
        dq_ref[1, side, keys] = dot_nn(ds_ref[unit % 2], qa_ref[head])
        dq_ref[2, side, keys] = dot_nn(p_ref[unit % 2], da_ref[head])
        lines = pl.ds(side * HD, HD)
        dq = dot_nn(kt_ref[pl.ds(head * HD, HD), keys], ds_ref[unit % 2])
        if part:
            dqt_ref[lines] += dq
        else:
            dqt_ref[lines] = dq
        if side and part:
            pair = head // 2
            dq_ref[0, 0] = dqt_ref[...].T
            for start in range(0, SEQ, PIECE):
                place = pl.ds(start, PIECE)
                dq = dq_ref[0, 0, place] * HD**-0.5
                dk = jnp.where(low_half, dq_ref[1, 0, place], dq_ref[1, 1, place])
                dv = jnp.where(low_half, dq_ref[2, 0, place], dq_ref[2, 1, place])
                dv = dv + pad_ref[place] * dob_ref[place, pl.ds(pair * PAIR, PAIR)].astype(F32)
                for block, value in enumerate((dq, dk, dv)):
                    lanes = pl.ds(block * width + pair * PAIR, PAIR)
                    value = value.astype(LOW)
                    dqkv_ref[place, lanes] = value
                    if block != 1:
                        into = pl.ds(pair * PAIR, PAIR)
                        gbias_ref[block // 2, :, into] += fold(value.astype(F32))
    gwq_ref[...] += dot_tn(x, dqkv_ref[...])
    dx_ref[...] = (dr_ref[...] + dot_nt(dqkv_ref[...], wq_ref[...])).astype(dx_ref.dtype)


def unpack_matrix(raw_ref, at, into_ref):
    width = into_ref.shape[0]
    for start in range(0, into_ref.shape[1], width):
        block = raw_ref[:, :, pl.ds(at + start, width)].astype(F32)
        block = block.reshape(GROUPS + (width,)).swapaxes(0, 1).reshape(width, width)
        into_ref[:, pl.ds(start, width)] = block.astype(LOW)


def unpack_stacked(raw_ref, at, into_ref):
    width = into_ref.shape[1]
    count = into_ref.shape[0] // width
    blocks = [
        raw_ref[:, :, pl.ds(at + step * width, width)].astype(F32).reshape(GROUPS + (width,))
        for step in range(count)
    ]
    outer, inner, rows = GROUPS
    for place in range(inner):
        part = jnp.stack([jnp.stack([block[f, place] for block in blocks]) for f in range(outer)])
        size = outer * count * rows
        into_ref[pl.ds(place * size, size)] = part.reshape(size, width).astype(LOW)


def sources(rows, columns):
    line = lax.broadcasted_iota(jnp.int32, (rows, columns), 0)
    outer, inner, height = GROUPS
    device = (line // height) % inner * outer + line // (inner * height)
    return device, line % height


def unpack_vectors(raw_ref, at, layer):
    outer, inner, rows = GROUPS
    total = outer * inner * rows
    raw = raw_ref[:, :, pl.ds(at, 128)].reshape(total, 128)
    lane = lax.broadcasted_iota(jnp.int32, (128, total), 0)
    column = lax.broadcasted_iota(jnp.int32, (128, total), 1)
    pick = jnp.where(lane == rows * layer + column % rows, 1.0, 0.0).astype(LOW)
    spread = dot_nn(raw, pick)
    device, unused = sources(total, total)
    column = lax.broadcasted_iota(jnp.int32, (total, total), 1)
    spread = jnp.where(column // rows == device, spread, 0.0)
    return jnp.sum(spread.reshape(outer * inner, rows, total), 0)


def unpack_hidden(raw_ref, at, layer, hidden):
    outer, inner, rows = GROUPS
    total = outer * inner * rows
    height = hidden // (outer * inner)
    raw = raw_ref[:, :, pl.ds(at, 128)].reshape(total, 128)
    lane = lax.broadcasted_iota(jnp.int32, (128, hidden), 0)
    column = lax.broadcasted_iota(jnp.int32, (128, hidden), 1)
    pick = jnp.where(lane == 2 * rows + column % height, 1.0, 0.0).astype(LOW)
    spread = dot_nn(raw, pick)
    device, within = sources(total, hidden)
    column = lax.broadcasted_iota(jnp.int32, (total, hidden), 1)
    spread = jnp.where((column // height == device) & (within == layer), spread, 0.0)
    return jnp.sum(spread, 0, keepdims=True)


def pack_matrix(sum_ref, sent_ref, at):
    width = sum_ref.shape[0]
    outer, inner, rows = GROUPS
    for start in range(0, sum_ref.shape[1], width):
        block = sum_ref[:, pl.ds(start, width)].reshape(inner, outer, rows, width)
        block = block.swapaxes(0, 1).reshape(outer, inner * rows, width)
        sent_ref[:, :, pl.ds(at + start, width)] = block.astype(LOW)


def pack_stacked(sum_ref, sent_ref, at):
    width = sum_ref.shape[0]
    outer, inner, rows = GROUPS
    count = sum_ref.shape[1] // width
    near = inner // count
    for step in range(count):
        block = sum_ref[:, pl.ds(step * width, width)].T
        block = block.reshape(near, outer, count, rows, width)
        for part in range(count):
            piece = jnp.stack([block[:, f, part] for f in range(outer)])
            piece = piece.reshape(outer, near * rows, width)
            sent_ref[:, pl.ds(step * near * rows, near * rows), pl.ds(at + part * width, width)] = (
                piece.astype(LOW)
            )


def pack_shared(block, sent_ref, at):
    outer, inner, rows = GROUPS
    columns = block.shape[1]
    block = jnp.broadcast_to(block[None], (outer * inner, rows, columns))
    sent_ref[:, :, pl.ds(at, columns)] = block.reshape(outer, inner * rows, columns).astype(LOW)


def pack_attention(gwq_ref, gbias_ref, sent_ref, at):
    pack_matrix(gwq_ref, sent_ref, at)
    width = gwq_ref.shape[0]
    line = lax.broadcasted_iota(jnp.int32, (8, width), 0)
    sums = [jnp.sum(gbias_ref[index], 0, keepdims=True) for index in range(2)]
    block = jnp.where(line == 0, sums[0], jnp.where(line == 1, sums[1], 0.0))
    pack_shared(block, sent_ref, at + 3 * width)


def pack_dense(gwo_ref, gwi_ref, gwf_ref, gsmall_ref, gbi_ref, sent_ref, at):
    width, hidden = gwi_ref.shape
    pack_matrix(gwo_ref, sent_ref, at)
    pack_matrix(gwi_ref, sent_ref, at + width)
    pack_stacked(gwf_ref, sent_ref, at + width + hidden)
    at = at + width + 2 * hidden
    pack_shared(jnp.sum(gsmall_ref[...], 1), sent_ref, at)
    line = jnp.sum(gbi_ref[...], 0, keepdims=True)
    size = hidden // 8
    block = jnp.concatenate([line[:, step * size : (step + 1) * size] for step in range(8)], 0)
    pack_shared(block, sent_ref, at + width)


def shape_of(array):
    return jax.ShapeDtypeStruct(array.shape, array.dtype)


def by_row(shape):
    if len(shape) == 2:
        return pl.BlockSpec((SEQ, shape[1]), lambda row: (row, 0))
    return pl.BlockSpec((None,) + tuple(shape[1:]), lambda row: (row,) + (0,) * (len(shape) - 1))


def whole(shape):
    return pl.BlockSpec(tuple(shape), lambda row: (0,) * len(shape))


def run_rows(body, lengths, rowwise, fixed, row_outs, sent, scratch, cost, setup, finish, after=()):
    count = lengths.shape[0]
    cuts = [len(rowwise), len(fixed), len(after), len(row_outs), len(sent), len(scratch)]

    def kernel(lengths_ref, *refs):
        row = pl.program_id(0)
        groups = []
        at = 0
        for cut in cuts:
            groups.append(refs[at : at + cut])
            at += cut
        rows_in, fixed_in, unused, rows_out, sent_out, work = groups

        @pl.when(row == 0)
        def _():
            setup(fixed_in, work)

        body(row, lengths_ref, rows_in, rows_out, work)

        if sent:

            @pl.when(row == count - 1)
            def _():
                finish(work, fixed_in, sent_out[0])

    return pl.pallas_call(
        kernel,
        grid=(count,),
        in_specs=[pl.BlockSpec(memory_space=pltpu.SMEM)]
        + [by_row(array.shape) for array in rowwise]
        + [whole(array.shape) for array in fixed]
        + [pl.BlockSpec(memory_space=pl.ANY) for array in after],
        out_specs=[by_row(part.shape) for part in row_outs] + [whole(part.shape) for part in sent],
        out_shape=list(row_outs) + list(sent),
        scratch_shapes=list(scratch),
        compiler_params=pltpu.CompilerParams(
            dimension_semantics=("arbitrary",), vmem_limit_bytes=MEMORY
        ),
        cost_estimate=pl.CostEstimate(flops=cost, bytes_accessed=8 * 2**20, transcendentals=0),
    )(lengths, *rowwise, *fixed, *after)


def struct(shape, dtype):
    return jax.ShapeDtypeStruct(tuple(shape), dtype)


FORWARD_SCRATCH = lambda: [
    pltpu.VMEM((2, SEQ // 2, SEQ), F32),
    pltpu.VMEM((2, SEQ // 2, SEQ), LOW),
    pltpu.VMEM((2, SEQ, PAIR), F32),
    pltpu.VMEM((SEQ, PAIR), F32),
    pltpu.VMEM((3, HEADS // 2, SEQ, PAIR), F32),
    pltpu.VMEM((SEQ, PAIR), F32),
]
BACKWARD_SCRATCH = lambda: [
    pltpu.VMEM((HEADS, SEQ, PAIR), LOW),
    pltpu.VMEM((2, SEQ // 2, SEQ), LOW),
    pltpu.VMEM((2, SEQ // 2, SEQ), LOW),
    pltpu.VMEM((2, 2, SEQ // 2, SEQ), F32),
    pltpu.VMEM((SEQ, 3 * HEADS * HD), LOW),
    pltpu.VMEM((3, 2, SEQ, PAIR), F32),
    pltpu.VMEM((SEQ, PAIR), F32),
    pltpu.VMEM((HEADS * HD, SEQ), LOW),
    pltpu.VMEM((PAIR, SEQ), F32),
]


def attention_outs(rows, tokens, width):
    heads = (rows, HEADS, SEQ, PAIR)
    return [struct(heads, LOW)] * 3 + [struct((tokens, width), LOW)]


def dense_outs(tokens, width, hidden):
    return [
        struct((tokens, width), F32),
        struct((tokens, width), F32),
        struct((tokens, PAIR), F32),
        struct((tokens, width), LOW),
        struct((tokens, hidden), LOW),
        struct((tokens, hidden), LOW),
    ]


def vmem(shape, dtype):
    return pltpu.VMEM(tuple(shape), dtype)


def attention_weights(width):
    return [vmem((width, 3 * width), LOW), vmem((1, 3 * width), F32)]


def dense_weights(width, hidden):
    return [
        vmem((width, width), LOW),
        vmem((width, hidden), LOW),
        vmem((hidden, width), LOW),
        vmem((8, width), F32),
        vmem((1, hidden), F32),
    ]


def dense_sums(width, hidden):
    return [
        vmem((width, width), F32),
        vmem((width, hidden), F32),
        vmem((width, hidden), F32),
        vmem((8, 8, width), F32),
        vmem((8, hidden), F32),
    ]


def attention_sums(width):
    return [vmem((width, 3 * width), F32), vmem((2, 8, width), F32)]


def dense_work(width, hidden):
    return [vmem((SEQ, width), LOW), vmem((2, SEQ, width), F32), vmem((SEQ, hidden), LOW)]


def set_attention(layer, urgent_ref, raw_ref, at, wq_ref, bias_ref):
    width = wq_ref.shape[0]
    unpack_matrix(raw_ref, at, wq_ref)
    vectors = unpack_vectors(urgent_ref, 3 * width, layer)
    bias_ref[:, :width] = vectors[0:1]
    bias_ref[:, width : 2 * width] = jnp.zeros((1, width), F32)
    bias_ref[:, 2 * width :] = vectors[1:2]


def set_dense(layer, urgent_ref, raw_ref, at, wo_ref, wi_ref, wf_ref, small_ref, bi_ref):
    width, hidden = wi_ref.shape
    unpack_matrix(raw_ref, at, wo_ref)
    unpack_matrix(raw_ref, at + width, wi_ref)
    unpack_stacked(raw_ref, at + width + hidden, wf_ref)
    small_ref[...] = unpack_vectors(urgent_ref, 3 * width, layer)
    bi_ref[...] = unpack_hidden(urgent_ref, 3 * width, layer, hidden)


def clear(refs):
    for ref in refs:
        ref[...] = jnp.zeros(ref.shape, ref.dtype)


def attention_kernel(layer, lengths, x, urgent, raw, at):
    rows, (tokens, width) = lengths.shape[0], x.shape

    def setup(fixed, work):
        set_attention(layer, fixed[0], fixed[-1], at, *work[:2])

    def body(row, lengths_ref, rowwise, outs, work):
        attention_forward(row, lengths_ref, rowwise[0][...].astype(LOW), *work[:2], *outs, *work[2:])

    fixed = [urgent] if raw is urgent else [urgent, raw]
    return run_rows(
        body, lengths, [x], fixed, attention_outs(rows, tokens, width), [],
        attention_weights(width) + FORWARD_SCRATCH(), 4 * 10**9, setup, None,
    )


def dense_kernel(layer, lengths, x, ob, urgent, raw, at, hidden, after):
    tokens, width = x.shape

    def setup(fixed, work):
        set_dense(layer, *fixed, at, *work[:5])

    def body(row, lengths_ref, rowwise, outs, work):
        dense_forward(*rowwise, *work[:5], *outs, *work[5:])

    return run_rows(
        body, lengths, [x, ob], [urgent, raw],
        dense_outs(tokens, width, hidden) + [struct((tokens, width), F32)], [],
        dense_weights(width, hidden) + [vmem((SEQ, width), F32), vmem((2, SEQ, width), F32)],
        5 * 10**9, setup, None, after,
    )


def turn_kernel(layer, lengths, x, ob, cotangent, urgent, raw, at, hidden):
    tokens, width = x.shape
    columns = width + 2 * hidden + width + hidden // 8

    def setup(fixed, work):
        set_dense(layer, *fixed, at, *work[:5])
        clear(work[5:10])

    def body(row, lengths_ref, rowwise, outs, work):
        x_ref, ob_ref, dz_ref = rowwise
        z_ref, dr_ref, dob_ref = outs
        weights, sums, kept = work[:5], work[5:10], work[10:16]
        work_ref, low_ref, u_ref, du_ref = work[16:]
        dense_forward(x_ref, ob_ref, *weights, *kept, z_ref, work_ref, u_ref)
        dense_backward(
            dz_ref, *kept, ob_ref, *weights[:4], dr_ref, dob_ref, *sums, low_ref, u_ref, du_ref
        )

    def finish(work, fixed, sent_ref):
        pack_dense(*work[5:10], sent_ref, 0)

    kept = [vmem((SEQ,) + part.shape[1:], part.dtype) for part in dense_outs(tokens, width, hidden)]
    return run_rows(
        body, lengths, [x, ob, cotangent], [urgent, raw],
        [struct((tokens, width), LOW), struct((tokens, width), F32), struct((tokens, width), LOW)],
        [struct((4, 64, columns), LOW)],
        dense_weights(width, hidden) + dense_sums(width, hidden) + kept
        + [vmem((SEQ, width), F32)] + dense_work(width, hidden),
        10**10, setup, finish,
    )


def attention_back_kernel(layer, lengths, upper, urgent, raw, dtype, after):
    tokens, width = upper[0].shape

    def setup(fixed, work):
        set_attention(layer, fixed[0], fixed[-1], 0, *work[:2])
        clear(work[2:4])

    def body(row, lengths_ref, rowwise, outs, work):
        attention_backward(
            row, lengths_ref, rowwise[0][...].astype(LOW), *rowwise[1:6], work[0], rowwise[6],
            outs[0], *work[2:4], *work[4:],
        )

    def finish(work, fixed, sent_ref):
        pack_attention(*work[2:4], sent_ref, 0)

    fixed = [urgent] if raw is urgent else [urgent, raw]
    return run_rows(
        body, lengths, list(upper), fixed, [struct((tokens, width), dtype)],
        [struct((4, 64, 4 * width), LOW)],
        attention_weights(width) + attention_sums(width) + BACKWARD_SCRATCH(),
        8 * 10**9, setup, finish, after,
    )


def dense_back_kernel(layer, lengths, dz, lower, urgent, raw, at, hidden, joined, after):
    tokens, width = dz.shape
    ahead = joined.shape[2]
    columns = ahead + width + 2 * hidden + width + hidden // 8

    def setup(fixed, work):
        set_dense(layer, *fixed[:2], at, *work[:5])
        clear(work[5:10])

    def body(row, lengths_ref, rowwise, outs, work):
        dense_backward(*rowwise, *work[:4], *outs, *work[5:])

    def finish(work, fixed, sent_ref):
        sent_ref[:, :, pl.ds(0, ahead)] = fixed[2][...]
        pack_dense(*work[5:10], sent_ref, ahead)

    return run_rows(
        body, lengths, [dz] + list(lower), [urgent, raw, joined],
        [struct((tokens, width), F32), struct((tokens, width), LOW)],
        [struct((4, 64, columns), LOW)],
        dense_weights(width, hidden) + dense_sums(width, hidden) + dense_work(width, hidden),
        7 * 10**9, setup, finish, after,
    )


def hold(array, after):
    def kernel(*refs):
        pass

    anywhere = pl.BlockSpec(memory_space=pl.ANY)
    return pl.pallas_call(
        kernel,
        in_specs=[anywhere] * (1 + len(after)),
        out_specs=anywhere,
        out_shape=shape_of(array),
        input_output_aliases={0: 0},
    )(array, *after)


def pack_parameters(
    attn_weight, attn_bias, out_weight, ffn_in, ffn_in_bias, ffn_out, norm_gain, shifts
):
    depth, rows, width = out_weight.shape
    copies = GROUPS[1]
    hidden = ffn_in.shape[2]
    early = 4 * width + 2 * hidden + 128
    columns = 4 * width + 2 * hidden
    height = ffn_in_bias.shape[1]

    def kernel(wq_ref, ab_ref, wo_ref, wi_ref, bi_ref, wf_ref, gain_ref, shift_ref, first_ref, rest_ref, small_ref):
        def put(ref, block, at):
            block = jnp.broadcast_to(block.astype(F32)[None], (copies,) + block.shape)
            block = block.reshape(copies * block.shape[1], block.shape[2])
            ref[:, pl.ds(at, block.shape[1])] = block.astype(LOW)

        small_ref[...] = jnp.zeros(small_ref.shape, F32)
        for layer in range(depth):
            lanes = pl.ds(rows * layer, rows)
            small_ref[0:2, lanes] = ab_ref[layer].astype(F32)
            small_ref[2:4, lanes] = gain_ref[layer].astype(F32)
            small_ref[4:8, lanes] = shift_ref[layer].astype(F32)
        small_ref[0:depth, pl.ds(2 * rows, height)] = bi_ref[...].astype(F32)
        put(first_ref, wq_ref[0], 0)
        put(first_ref, small_ref[...], 3 * width)
        for layer, ref, at in ((0, first_ref, 3 * width + 128), (1, rest_ref, 3 * width)):
            if layer:
                put(ref, wq_ref[layer], 0)
            put(ref, wo_ref[layer], at)
            put(ref, wi_ref[layer], at + width)
            at += width + hidden
            down = wf_ref[layer].astype(F32)
            for step in range(hidden // width):
                put(ref, down[step * rows : (step + 1) * rows], at)
                at += width

    return pl.pallas_call(
        kernel,
        in_specs=[pl.BlockSpec(memory_space=pltpu.VMEM)] * 8,
        out_shape=[struct((copies * rows, early), LOW), struct((copies * rows, columns), LOW)],
        scratch_shapes=[vmem((rows, 128), F32)],
        compiler_params=pltpu.CompilerParams(vmem_limit_bytes=MEMORY),
    )(attn_weight, attn_bias, out_weight, ffn_in, ffn_in_bias, ffn_out, norm_gain, shifts)


def add_parts(received, after=(), passed=None, joined=None):
    extra = [] if passed is None else [passed]
    inner = [] if joined is None else [joined]
    ahead = 0 if joined is None else joined.shape[1]
    rows, lanes_in = received.shape[1:]

    def kernel(in_ref, *refs):
        out_ref = refs[len(inner) + len(extra) + len(after)]
        if inner:
            out_ref[:, pl.ds(0, ahead)] = refs[0][...]
        columns = 256
        for start in range(0, lanes_in, columns):
            size = min(columns, lanes_in - start)
            total = jnp.sum(in_ref[:, :, pl.ds(start, size)].astype(F32), 0)
            out_ref[:, pl.ds(ahead + start, size)] = total.astype(LOW)

    anywhere = pl.BlockSpec(memory_space=pl.ANY)
    near = pl.BlockSpec(memory_space=pltpu.VMEM)
    found = pl.pallas_call(
        kernel,
        in_specs=[near] * (1 + len(inner)) + [anywhere] * (len(extra) + len(after)),
        out_specs=[near] + [anywhere] * len(extra),
        out_shape=[struct((rows, ahead + lanes_in), LOW)] + [shape_of(part) for part in extra],
        input_output_aliases={1 + len(inner): 1} if extra else {},
        compiler_params=pltpu.CompilerParams(vmem_limit_bytes=MEMORY),
    )(received, *inner, *extra, *after)
    return found if extra else found[0]


def write_gradients(place, tail, front, depth, width, hidden):
    rows = GROUPS[2]
    last = front.shape[1] - 4 * width
    height = hidden // DEVICES

    def kernel(place_ref, tail_ref, front_ref, gwq_ref, gab_ref, gwo_ref, gwi_ref, gbi_ref, gwf_ref, gain_ref, shift_ref):
        spot = place_ref[0]

        def total(ref, at, columns):
            block = ref[:, pl.ds(at, columns)].astype(F32)
            return jnp.sum(block.reshape(-1, rows, columns), 0)

        def own(block, size):
            return pltpu.roll(block, block.shape[1] - spot * size, 1)

        for layer, ref, at in ((0, front_ref, last), (1, front_ref, 0)):
            gwq_ref[layer] = total(ref, at, 3 * width)
            gab_ref[layer] = own(total(ref, at + 3 * width, width), rows)[0:2, 0:rows]
        for layer, ref, at in ((0, front_ref, 4 * width), (1, tail_ref, 0)):
            gwo_ref[layer] = total(ref, at, width)
            gwi_ref[layer] = total(ref, at + width, hidden)
            for step in range(hidden // width):
                gwf_ref[layer, pl.ds(step * rows, rows)] = total(
                    ref, at + width + hidden + step * width, width
                )
            at += width + 2 * hidden
            small = own(total(ref, at, width), rows)
            gain_ref[layer] = small[2:4, 0:rows]
            shift_ref[layer] = small[4:8, 0:rows]
            line = total(ref, at + width, hidden // 8)
            line = jnp.concatenate([line[step : step + 1] for step in range(8)], 1)
            gbi_ref[pl.ds(layer, 1)] = own(line, height)[:, 0:height]

    outs = [
        struct((depth, rows, 3 * width), F32),
        struct((depth, 2, rows), F32),
        struct((depth, rows, width), F32),
        struct((depth, rows, hidden), F32),
        struct((depth, height), F32),
        struct((depth, height, width), F32),
        struct((depth, 2, rows), F32),
        struct((depth, 4, rows), F32),
    ]
    return pl.pallas_call(
        kernel,
        in_specs=[pl.BlockSpec(memory_space=pltpu.SMEM)] + [pl.BlockSpec(memory_space=pltpu.VMEM)] * 2,
        out_shape=outs,
        compiler_params=pltpu.CompilerParams(vmem_limit_bytes=MEMORY),
    )(place, tail, front)


def exchange(parts, axis):
    return lax.all_to_all(parts, axis, 0, 0, tiled=True)


def local(
    hidden_in,
    lengths,
    grad_out,
    attn_weight,
    attn_bias,
    out_weight,
    ffn_in,
    ffn_in_bias,
    ffn_out,
    norm_gain,
    shifts,
):
    depth, rows, width = out_weight.shape
    hidden = ffn_in.shape[2]
    first, second = lax.axis_size("dp"), lax.axis_size("fsdp")
    fits = (second, first, rows) == GROUPS
    urgent_size = 3 * width + 128
    if fits:
        early, later = pack_parameters(
            attn_weight, attn_bias, out_weight, ffn_in, ffn_in_bias, ffn_out, norm_gain, shifts
        )
        early = exchange(early, "dp")
        urgent = early[:, :urgent_size]
        urgent = exchange(jnp.broadcast_to(urgent[None], (second,) + urgent.shape), "fsdp")
        raw0 = lax.all_gather(early[:, urgent_size:], "fsdp")
        later = exchange(hold(later, (urgent,)), "dp")
    else:
        urgent, raw0, raw1 = gather_other(
            attn_weight, attn_bias, out_weight, ffn_in, ffn_in_bias, ffn_out, norm_gain, shifts
        )
        ready = ()

    qa0, ka0, va0, ob0 = attention_kernel(0, lengths, hidden_in, urgent, urgent, 0)
    if fits:
        later = hold(later, (ob0,))
        raw1 = lax.all_gather(later, "fsdp")
        ready = (later,)
    n1, n2, inv, yb, gb, gp, z0 = dense_kernel(
        0, lengths, hidden_in, ob0, urgent, raw0, 0, hidden, ready
    )
    qa1, ka1, va1, ob1 = attention_kernel(1, lengths, z0, urgent, raw1, 0)
    hidden_out, dr1, dob1, sent_a = turn_kernel(
        1, lengths, z0, ob1, grad_out, urgent, raw1, 3 * width, hidden
    )
    dx1, sent_q = attention_back_kernel(
        1, lengths, (z0, dob1, ob1, qa1, ka1, va1, dr1), urgent, raw1, F32, (sent_a,)
    )
    ready = ()
    if fits:
        tail = add_parts(exchange(sent_a, "fsdp"), (sent_q,))
        ready = (tail,)
    dr0, dob0, sent_b = dense_back_kernel(
        0, lengths, dx1, (n1, n2, inv, yb, gb, gp, ob0), urgent, raw0, 0, hidden, sent_q, ready
    )
    if fits:
        tail = exchange(tail, "dp")
        ready = (tail,)
    grad_in, sent_c = attention_back_kernel(
        0, lengths, (hidden_in, dob0, ob0, qa0, ka0, va0, dr0), urgent, urgent, LOW,
        (sent_b,) + ready,
    )
    if fits:
        front, sent_c = add_parts(exchange(sent_b, "fsdp"), (), sent_c)
        front = add_parts(exchange(sent_c, "fsdp"), (), None, front)
        front = exchange(front, "dp")
        place = lax.axis_index(("dp", "fsdp")).astype(jnp.int32).reshape(1)
        grads = write_gradients(place, tail, front, depth, width, hidden)
    else:
        grads = scatter_other(sent_a, sent_b, sent_c, rows, width, hidden)
    return (hidden_out, grad_in, *grads)


def gather_other(
    attn_weight, attn_bias, out_weight, ffn_in, ffn_in_bias, ffn_out, norm_gain, shifts
):
    axes = ("dp", "fsdp")
    gather = lambda part, axis: lax.all_gather(part, axes, axis=axis, tiled=True)
    depth, unused, width = out_weight.shape
    hidden = ffn_in.shape[2]
    outer, inner, rows = GROUPS
    vectors = gather(jnp.concatenate([attn_bias, norm_gain, shifts], 1), 2)
    line = gather(ffn_in_bias, 1)

    def order(natural):
        return (
            natural.reshape(inner, outer, rows, -1).swapaxes(0, 1).reshape(outer, inner * rows, -1)
        )

    def stacked(part):
        part = part.reshape(DEVICES, -1, rows, width)
        return order(part.swapaxes(1, 2).reshape(width, -1))

    small = vectors.reshape(depth, 8, DEVICES, rows).transpose(2, 1, 0, 3).reshape(width, -1)
    line = line.reshape(depth, DEVICES, -1).swapaxes(0, 1)
    line = jnp.pad(line, ((0, 0), (0, 8 - depth), (0, 0))).reshape(width, -1)
    small = jnp.concatenate([small, line], 1)
    small = jnp.pad(small, ((0, 0), (0, 128 - small.shape[1])))
    wq, wo, wi, wf = (gather(part, 1) for part in (attn_weight, out_weight, ffn_in, ffn_out))
    urgent = jnp.concatenate([order(wq[0]), order(small)], 2)
    raw0 = jnp.concatenate([order(wo[0]), order(wi[0]), stacked(wf[0])], 2)
    raw1 = jnp.concatenate([order(wq[1]), order(wo[1]), order(wi[1]), stacked(wf[1])], 2)
    return urgent, raw0, raw1


def scatter_other(sent_a, sent_b, sent_c, own_rows, width, hidden):
    outer, inner, rows = GROUPS
    axes = ("dp", "fsdp")

    def natural(part):
        return part.reshape(outer, inner, rows, -1).swapaxes(0, 1).reshape(width, -1).astype(F32)

    def cut(part, sizes):
        found, at = [], 0
        for size in sizes:
            found.append(part[:, at : at + size])
            at += size
        return found

    dense = [width, hidden, hidden, width, hidden // 8]
    attention = [3 * width, width]
    wq0, ab0 = cut(natural(sent_c), attention)
    wq1, ab1, wo0, wi0, wf0, small0, bi0 = cut(natural(sent_b), attention + dense)
    wo1, wi1, wf1, small1, bi1 = cut(natural(sent_a), dense)

    def stacked(part):
        part = part.reshape(DEVICES, rows, -1, width).swapaxes(1, 2)
        return part.reshape(hidden, width)

    def spread(parts, axis):
        return lax.psum_scatter(jnp.stack(parts), axes, scatter_dimension=axis, tiled=True)

    return (
        spread([wq0, wq1], 1),
        spread([ab0[:2], ab1[:2]], 2),
        spread([wo0, wo1], 1),
        spread([wi0, wi1], 1),
        spread([bi0[:8].reshape(-1), bi1[:8].reshape(-1)], 1),
        spread([stacked(wf0), stacked(wf1)], 1),
        spread([small0[2:4], small1[2:4]], 2),
        spread([small0[4:8], small1[4:8]], 2),
    )


def solution(mesh):
    placed = (
        P(("dp", "fsdp"), None),
        P(("dp", "fsdp"), None),
        P(("dp", "fsdp"), None),
        P(None, ("dp", "fsdp"), None),
        P(None, None, ("dp", "fsdp")),
        P(None, ("dp", "fsdp"), None),
        P(None, ("dp", "fsdp"), None),
        P(None, ("dp", "fsdp")),
        P(None, ("dp", "fsdp"), None),
        P(None, None, ("dp", "fsdp")),
        P(None, None, ("dp", "fsdp")),
    )
    return jax.shard_map(
        local,
        mesh=mesh,
        in_specs=placed,
        out_specs=(
            P(("dp", "fsdp"), None),
            P(("dp", "fsdp"), None),
            P(None, ("dp", "fsdp"), None),
            P(None, None, ("dp", "fsdp")),
            P(None, ("dp", "fsdp"), None),
            P(None, ("dp", "fsdp"), None),
            P(None, ("dp", "fsdp")),
            P(None, ("dp", "fsdp"), None),
            P(None, None, ("dp", "fsdp")),
            P(None, None, ("dp", "fsdp")),
        ),
        check_vma=False,
    )
```

```python
from functools import partial

import jax
import jax.numpy as jnp
from jax import lax
from jax.experimental import pallas as pl
from jax.experimental.pallas import tpu as pltpu
from jax.sharding import PartitionSpec as P

HEADS = 4
HD = 64
SEQ = 512
PAIR = 2 * HD
FAR = -(2.0**100)
FLOOR = -1e20
EPSILON = 1e-12
PIECE = 256
SMALL = 128
GROUPS = (4, 8, 8)
DEVICES = 32
LOW = jnp.bfloat16
F32 = jnp.float32
MEMORY = 60 * 2**20


def dot_nn(left, right):
    return lax.dot_general(left, right, (((1,), (0,)), ((), ())), preferred_element_type=F32)


def dot_nt(left, right):
    return lax.dot_general(left, right, (((1,), (1,)), ((), ())), preferred_element_type=F32)


def dot_tn(left, right):
    return lax.dot_general(left, right, (((0,), (0,)), ((), ())), preferred_element_type=F32)


def pieces(total, size=PIECE):
    return [pl.ds(start, size) for start in range(0, total, size)]


def three_parts(values):
    first = values.astype(LOW).astype(F32)
    rest = values - first
    second = rest.astype(LOW).astype(F32)
    return first, second, rest - second


CURVE = (
    7.97882253e-01,
    3.63445176e-02,
    -4.47304308e-05,
    -5.04138899e-05,
    3.10523303e-06,
    -6.66676088e-08,
)
BELL = -0.5 / 0.6931471805599453


def gelu_parts(u):
    square = u * u
    near = jnp.minimum(square, 31.36)
    curve = CURVE[-1]
    for factor in CURVE[-2::-1]:
        curve = curve * near + factor
    bent = jnp.tanh(u * curve)
    half = 0.5 * u
    slope = (0.5 + 0.5 * bent) + (u * 0.3989422804014327) * jnp.exp2(square * BELL)
    return half + half * bent, slope


def lane_facts():
    lane = lax.broadcasted_iota(jnp.int32, (1, PAIR), 1)
    return lane < HD, lane & (HD - 1)


def segments(lengths_ref, row, start, rows):
    places = lax.broadcasted_iota(jnp.int32, (rows, 1), 0) + start
    bound = jnp.int32(0)
    segment = jnp.zeros((rows, 1), jnp.int32)
    last = lengths_ref.shape[1] - 1
    for entry in range(last):
        bound = bound + lengths_ref[row, entry]
        segment = segment + (places >= bound).astype(jnp.int32)
    return segment, (segment == last).astype(F32), last


def attention_forward(row, lengths_ref, x, wq_ref, bias_ref, qa_ref, ka_ref, va_ref, ob_ref, s_ref, p_ref, m_ref, pad_ref, q_ref, aug_ref):
    width = HEADS * HD
    for block in range(3):
        for pair in range(HEADS // 2):
            at = block * width + pair * PAIR
            q_ref[block, pair] = dot_nn(x, wq_ref[:, at : at + PAIR]) + bias_ref[:, at : at + PAIR]
    for start in range(0, SEQ, PIECE):
        place = pl.ds(start, PIECE)
        low_half, slot = lane_facts()
        segment, pad, last = segments(lengths_ref, row, start, PIECE)
        pad_ref[place] = jnp.broadcast_to(pad, (PIECE, PAIR))
        aug_q = jnp.where(slot == segment, 1.0, 0.0)
        aug_ref[place] = aug_q
        seen = (slot == segment) & (slot != last)
        aug_k = jnp.where(seen, 0.0, jnp.where(slot <= last, FAR, jnp.where(slot <= last + 3, 1.0, 0.0)))
        for pair in range(HEADS // 2):
            q = q_ref[0, pair, place] * HD**-0.5
            k = q_ref[1, pair, place]
            v = q_ref[2, pair, place]
            q_ref[0, pair, place] = q
            qa_ref[2 * pair, place] = jnp.where(low_half, q, aug_q).astype(LOW)
            qa_ref[2 * pair + 1, place] = jnp.where(low_half, aug_q, q).astype(LOW)
            ka_ref[2 * pair, place] = jnp.where(low_half, k, aug_k).astype(LOW)
            ka_ref[2 * pair + 1, place] = jnp.where(low_half, aug_k, k).astype(LOW)
            va_ref[2 * pair, place] = jnp.where(low_half, v, 1.0).astype(LOW)
            va_ref[2 * pair + 1, place] = jnp.where(low_half, 1.0, v).astype(LOW)
    half = SEQ // 2
    units = [(head, part) for head in range(HEADS) for part in range(2)]

    def scores(unit):
        head, part = units[unit]
        s_ref[unit % 2] = dot_nt(qa_ref[head, pl.ds(part * half, half)], ka_ref[head])

    def softmax(unit):
        head, part = units[unit]
        highest = jnp.maximum(jnp.max(s_ref[unit % 2], -1, keepdims=True), FLOOR)
        m_ref[head % 2, pl.ds(part * half, half)] = jnp.broadcast_to(highest, (half, PAIR))
        for start in range(0, half, SMALL):
            place = pl.ds(start, SMALL)
            s = s_ref[unit % 2, place] - highest[start : start + SMALL]
            p_ref[unit % 2, place] = jnp.exp(s).astype(LOW)

    def attend(unit):
        head, part = units[unit]
        return dot_nn(p_ref[unit % 2], va_ref[head])

    sums = {}
    scores(0)
    for unit in range(len(units)):
        if unit + 1 < len(units):
            scores(unit + 1)
        softmax(unit)
        head, part = units[unit]
        q_ref[1, head % 2, pl.ds(part * half, half)] = attend(unit)
        if head % 2 and part:
            pair = head // 2
            for start in range(0, SEQ, PIECE):
                place = pl.ds(start, PIECE)
                low_half, slot = lane_facts()
                even = q_ref[1, 0, place]
                odd = q_ref[1, 1, place]
                pad = pad_ref[place]
                last = lengths_ref.shape[1] - 1
                total = jnp.where(low_half, odd, even) + pad
                top = jnp.where(low_half, odd_even(m_ref, 1, place), odd_even(m_ref, 0, place))
                spread = jnp.where(pad > 0, 0.0, top + jnp.log(total))
                first, second, third = three_parts(spread)
                aug = jnp.where(
                    slot == last + 1,
                    -first,
                    jnp.where(slot == last + 2, -second, jnp.where(slot == last + 3, -third, aug_ref[place])),
                )
                q = q_ref[0, pair, place]
                qa_ref[2 * pair, place] = jnp.where(low_half, q, aug).astype(LOW)
                qa_ref[2 * pair + 1, place] = jnp.where(low_half, aug, q).astype(LOW)
                v = q_ref[2, pair, place].astype(LOW).astype(F32)
                out = jnp.where(low_half, even, odd) / pltpu.roll(total, HD, 1) + pad * v
                ob_ref[place, pl.ds(pair * PAIR, PAIR)] = out.astype(LOW)


def odd_even(ref, which, place):
    return ref[which, place]


def normal(values):
    centred = values - jnp.mean(values, -1, keepdims=True)
    inverse = lax.rsqrt(jnp.mean(centred * centred, -1, keepdims=True) + EPSILON)
    return centred * inverse, inverse


def normal_back(cotangent, unit, inverse, gains):
    scaled = cotangent * gains
    return inverse * (
        scaled
        - jnp.mean(scaled, -1, keepdims=True)
        - unit * jnp.mean(scaled * unit, -1, keepdims=True)
    )


def dense_forward(x_ref, ob_ref, wo_ref, wi_ref, wf_ref, small_ref, bi_ref, n1_ref, n2_ref, inv_ref, yb_ref, gb_ref, gp_ref, z_ref, work_ref, u_ref):
    small = lambda index: small_ref[pl.ds(index, 1)]
    work_ref[...] = dot_nn(ob_ref[...], wo_ref[...])
    for place in pieces(SEQ):
        unit, inverse = normal(x_ref[place].astype(F32) + work_ref[place] + small(4))
        n1_ref[place] = unit
        inv_ref[place, pl.ds(0, HD)] = jnp.broadcast_to(inverse, (PIECE, HD))
        y = unit * small(2) + small(5)
        yb_ref[place] = y.astype(LOW)
        work_ref[place] = y + small(6)
    columns = 256
    count = wi_ref.shape[1] // columns

    def into(step):
        u_ref[step % 2] = dot_nn(yb_ref[...], wi_ref[:, pl.ds(step * columns, columns)])

    into(0)
    for step in range(count):
        if step + 1 < count:
            into(step + 1)
        lanes = pl.ds(step * columns, columns)
        for place in pieces(SEQ, SMALL):
            g, slope = gelu_parts(u_ref[step % 2, place] + bi_ref[:, lanes])
            gb_ref[place, lanes] = g.astype(LOW)
            gp_ref[place, lanes] = slope.astype(LOW)
    work_ref[...] += dot_nn(gb_ref[...], wf_ref[...])
    for place in pieces(SEQ):
        unit, inverse = normal(work_ref[place])
        n2_ref[place] = unit
        inv_ref[place, pl.ds(HD, HD)] = jnp.broadcast_to(inverse, (PIECE, HD))
        z_ref[place] = (unit * small(3) + small(7)).astype(z_ref.dtype)


def fold(values):
    return jnp.sum(values.reshape(-1, 8, values.shape[-1]), 0)


def dense_backward(dz_ref, n1_ref, n2_ref, inv_ref, yb_ref, gb_ref, gp_ref, ob_ref, wo_ref, wi_ref, wf_ref, small_ref, dr_ref, dob_ref, gwo_ref, gwi_ref, gwf_ref, gsmall_ref, gbi_ref, low_ref, u_ref, du_ref):
    small = lambda index: small_ref[pl.ds(index, 1)]
    for place in pieces(SEQ):
        dz = dz_ref[place].astype(F32)
        unit = n2_ref[place]
        gsmall_ref[3] += fold(dz * unit)
        gsmall_ref[7] += fold(dz)
        dr = normal_back(dz, unit, inv_ref[place, pl.ds(HD, 1)], small(3))
        dr_ref[place] = dr
        df = dr.astype(LOW)
        low_ref[place] = df
        gsmall_ref[6] += fold(df.astype(F32))
    columns = 256
    count = wi_ref.shape[1] // columns

    def back(step):
        u_ref[step % 2] = dot_nt(low_ref[...], wf_ref[pl.ds(step * columns, columns)])

    back(0)
    for step in range(count):
        if step + 1 < count:
            back(step + 1)
        lanes = pl.ds(step * columns, columns)
        gwf_ref[:, lanes] += dot_tn(low_ref[...], gb_ref[:, lanes])
        for place in pieces(SEQ, SMALL):
            du = (u_ref[step % 2, place] * gp_ref[place, lanes].astype(F32)).astype(LOW)
            du_ref[place, lanes] = du
            gbi_ref[:, lanes] += fold(du.astype(F32))
        gwi_ref[:, lanes] += dot_tn(yb_ref[...], du_ref[:, lanes])
    u_ref[0] = dot_nt(du_ref[...], wi_ref[...])
    for place in pieces(SEQ):
        dy = dr_ref[place] + u_ref[0, place]
        unit = n1_ref[place]
        gsmall_ref[2] += fold(dy * unit)
        gsmall_ref[5] += fold(dy)
        dr = normal_back(dy, unit, inv_ref[place, pl.ds(0, 1)], small(2))
        dr_ref[place] = dr
        da = dr.astype(LOW)
        low_ref[place] = da
        gsmall_ref[4] += fold(da.astype(F32))
    gwo_ref[...] += dot_tn(ob_ref[...], low_ref[...])
    dob_ref[...] = dot_nt(low_ref[...], wo_ref[...]).astype(LOW)


def attention_backward(row, lengths_ref, x, dob_ref, ob_ref, qa_ref, ka_ref, va_ref, wq_ref, dr_ref, dx_ref, gwq_ref, gbias_ref, da_ref, p_ref, ds_ref, s_ref, dqkv_ref, dq_ref, pad_ref, kt_ref, dqt_ref):
    width = HEADS * HD
    half = SEQ // 2
    low_half, slot = lane_facts()
    for start in range(0, SEQ, PIECE):
        place = pl.ds(start, PIECE)
        segment, pad, last = segments(lengths_ref, row, start, PIECE)
        pad_ref[place] = jnp.broadcast_to(pad, (PIECE, PAIR))
        for pair in range(HEADS // 2):
            lanes = pl.ds(pair * PAIR, PAIR)
            dob = dob_ref[place, lanes].astype(F32)
            product = dob * ob_ref[place, lanes].astype(F32)
            even = jnp.sum(jnp.where(low_half, product, 0.0), -1, keepdims=True)
            odd = jnp.sum(jnp.where(low_half, 0.0, product), -1, keepdims=True)
            first, second, third = three_parts(jnp.where(low_half, odd, even))
            aug = jnp.where(
                slot == 0, -first, jnp.where(slot == 1, -second, jnp.where(slot == 2, -third, 0.0))
            )
            da_ref[2 * pair, place] = jnp.where(low_half, dob, aug).astype(LOW)
            da_ref[2 * pair + 1, place] = jnp.where(low_half, aug, dob).astype(LOW)
    for pair in range(HEADS // 2):
        low_half, unused = lane_facts()
        keys = jnp.where(low_half, ka_ref[2 * pair].astype(F32), ka_ref[2 * pair + 1].astype(F32))
        kt_ref[pl.ds(pair * PAIR, PAIR)] = keys.T.astype(LOW)
    low_half, slot = lane_facts()
    units = [(head, part) for head in range(HEADS) for part in range(2)]

    def scores(unit):
        head, part = units[unit]
        keys = pl.ds(part * half, half)
        s_ref[0, unit % 2] = dot_nt(ka_ref[head, keys], qa_ref[head])
        s_ref[1, unit % 2] = dot_nt(va_ref[head, keys], da_ref[head])

    def weigh(unit):
        for place in pieces(half, SMALL):
            p = jnp.exp(s_ref[0, unit % 2, place])
            p_ref[unit % 2, place] = p.astype(LOW)
            ds_ref[unit % 2, place] = (p * s_ref[1, unit % 2, place]).astype(LOW)

    scores(0)
    for unit in range(len(units)):
        if unit + 1 < len(units):
            scores(unit + 1)
        weigh(unit)
        head, part = units[unit]
        keys = pl.ds(part * half, half)
        side = head % 2
        dq_ref[1, side, keys] = dot_nn(ds_ref[unit % 2], qa_ref[head])
        dq_ref[2, side, keys] = dot_nn(p_ref[unit % 2], da_ref[head])
        lines = pl.ds(side * HD, HD)
        dq = dot_nn(kt_ref[pl.ds(head * HD, HD), keys], ds_ref[unit % 2])
        if part:
            dqt_ref[lines] += dq
        else:
            dqt_ref[lines] = dq
        if side and part:
            pair = head // 2
            dq_ref[0, 0] = dqt_ref[...].T
            for start in range(0, SEQ, PIECE):
                place = pl.ds(start, PIECE)
                dq = dq_ref[0, 0, place] * HD**-0.5
                dk = jnp.where(low_half, dq_ref[1, 0, place], dq_ref[1, 1, place])
                dv = jnp.where(low_half, dq_ref[2, 0, place], dq_ref[2, 1, place])
                dv = dv + pad_ref[place] * dob_ref[place, pl.ds(pair * PAIR, PAIR)].astype(F32)
                for block, value in enumerate((dq, dk, dv)):
                    lanes = pl.ds(block * width + pair * PAIR, PAIR)
                    value = value.astype(LOW)
                    dqkv_ref[place, lanes] = value
                    if block != 1:
                        into = pl.ds(pair * PAIR, PAIR)
                        gbias_ref[block // 2, :, into] += fold(value.astype(F32))
    gwq_ref[...] += dot_tn(x, dqkv_ref[...])
    dx_ref[...] = (dr_ref[...] + dot_nt(dqkv_ref[...], wq_ref[...])).astype(dx_ref.dtype)


def unpack_matrix(raw_ref, at, into_ref):
    width = into_ref.shape[0]
    for start in range(0, into_ref.shape[1], width):
        block = raw_ref[:, :, pl.ds(at + start, width)].astype(F32)
        block = block.reshape(GROUPS + (width,)).swapaxes(0, 1).reshape(width, width)
        into_ref[:, pl.ds(start, width)] = block.astype(LOW)


def unpack_stacked(raw_ref, at, into_ref):
    width = into_ref.shape[1]
    count = into_ref.shape[0] // width
    blocks = [
        raw_ref[:, :, pl.ds(at + step * width, width)].astype(F32).reshape(GROUPS + (width,))
        for step in range(count)
    ]
    outer, inner, rows = GROUPS
    for place in range(inner):
        part = jnp.stack([jnp.stack([block[f, place] for block in blocks]) for f in range(outer)])
        size = outer * count * rows
        into_ref[pl.ds(place * size, size)] = part.reshape(size, width).astype(LOW)


def counter(shape, axis):
    return lax.broadcasted_iota(jnp.int32, shape, axis)


def split_by(values, size):
    return lax.shift_right_logical(values, size.bit_length() - 1), values & (size - 1)


def sources(rows):
    outer, inner, height = GROUPS
    group, within = split_by(counter((rows, 1), 0), height)
    far, near = split_by(group, inner)
    return near * outer + far, within


def unpack_vectors(raw_ref, at, layer):
    outer, inner, rows = GROUPS
    total = outer * inner * rows
    raw = raw_ref[:, :, pl.ds(at, 128)].reshape(total, 128)
    owner, place = split_by(counter((1, total), 1), rows)
    pick = jnp.where(counter((128, 1), 0) == rows * layer + place, 1.0, 0.0).astype(LOW)
    device, unused = sources(total)
    spread = jnp.where(owner == device, dot_nn(raw, pick), 0.0)
    return jnp.sum(spread.reshape(outer * inner, rows, total), 0)


def unpack_hidden(raw_ref, at, layer, hidden):
    outer, inner, rows = GROUPS
    total = outer * inner * rows
    raw = raw_ref[:, :, pl.ds(at, 128)].reshape(total, 128)
    owner, place = split_by(counter((1, hidden), 1), hidden // (outer * inner))
    pick = jnp.where(counter((128, 1), 0) == 2 * rows + place, 1.0, 0.0).astype(LOW)
    device, within = sources(total)
    device = jnp.where(within == layer, device, -1)
    spread = jnp.where(owner == device, dot_nn(raw, pick), 0.0)
    return jnp.sum(spread, 0, keepdims=True)


def pack_matrix(sum_ref, sent_ref, at):
    width = sum_ref.shape[0]
    outer, inner, rows = GROUPS
    for start in range(0, sum_ref.shape[1], width):
        block = sum_ref[:, pl.ds(start, width)].reshape(inner, outer, rows, width)
        block = block.swapaxes(0, 1).reshape(outer, inner * rows, width)
        sent_ref[:, :, pl.ds(at + start, width)] = block.astype(LOW)


def pack_stacked(sum_ref, sent_ref, at):
    width = sum_ref.shape[0]
    outer, inner, rows = GROUPS
    count = sum_ref.shape[1] // width
    near = inner // count
    for step in range(count):
        block = sum_ref[:, pl.ds(step * width, width)].T
        block = block.reshape(near, outer, count, rows, width)
        for part in range(count):
            piece = jnp.stack([block[:, f, part] for f in range(outer)])
            piece = piece.reshape(outer, near * rows, width)
            sent_ref[:, pl.ds(step * near * rows, near * rows), pl.ds(at + part * width, width)] = (
                piece.astype(LOW)
            )


def pack_shared(block, sent_ref, at):
    outer, inner, rows = GROUPS
    columns = block.shape[1]
    block = jnp.broadcast_to(block[None], (outer * inner, rows, columns))
    sent_ref[:, :, pl.ds(at, columns)] = block.reshape(outer, inner * rows, columns).astype(LOW)


def pack_attention(gwq_ref, gbias_ref, sent_ref, at):
    pack_matrix(gwq_ref, sent_ref, at)
    width = gwq_ref.shape[0]
    line = lax.broadcasted_iota(jnp.int32, (8, width), 0)
    sums = [jnp.sum(gbias_ref[index], 0, keepdims=True) for index in range(2)]
    block = jnp.where(line == 0, sums[0], jnp.where(line == 1, sums[1], 0.0))
    pack_shared(block, sent_ref, at + 3 * width)


def pack_dense(gwo_ref, gwi_ref, gwf_ref, gsmall_ref, gbi_ref, sent_ref, at):
    width, hidden = gwi_ref.shape
    pack_matrix(gwo_ref, sent_ref, at)
    pack_matrix(gwi_ref, sent_ref, at + width)
    pack_stacked(gwf_ref, sent_ref, at + width + hidden)
    at = at + width + 2 * hidden
    pack_shared(jnp.sum(gsmall_ref[...], 1), sent_ref, at)
    line = jnp.sum(gbi_ref[...], 0, keepdims=True)
    size = hidden // 8
    block = jnp.concatenate([line[:, step * size : (step + 1) * size] for step in range(8)], 0)
    pack_shared(block, sent_ref, at + width)


def shape_of(array):
    return jax.ShapeDtypeStruct(array.shape, array.dtype)


def by_row(shape):
    if len(shape) == 2:
        return pl.BlockSpec((SEQ, shape[1]), lambda row: (row, 0))
    return pl.BlockSpec((None,) + tuple(shape[1:]), lambda row: (row,) + (0,) * (len(shape) - 1))


def whole(shape):
    return pl.BlockSpec(tuple(shape), lambda row: (0,) * len(shape))


def run_rows(body, lengths, rowwise, fixed, row_outs, sent, scratch, cost, setup, finish, after=()):
    count = lengths.shape[0]
    cuts = [len(rowwise), len(fixed), len(after), len(row_outs), len(sent), len(scratch)]

    def kernel(lengths_ref, *refs):
        row = pl.program_id(0)
        groups = []
        at = 0
        for cut in cuts:
            groups.append(refs[at : at + cut])
            at += cut
        rows_in, fixed_in, unused, rows_out, sent_out, work = groups

        @pl.when(row == 0)
        def _():
            setup(fixed_in, work)

        body(row, lengths_ref, rows_in, rows_out, work)

        if sent:

            @pl.when(row == count - 1)
            def _():
                finish(work, fixed_in, sent_out[0])

    return pl.pallas_call(
        kernel,
        grid=(count,),
        in_specs=[pl.BlockSpec(memory_space=pltpu.SMEM)]
        + [by_row(array.shape) for array in rowwise]
        + [whole(array.shape) for array in fixed]
        + [pl.BlockSpec(memory_space=pl.ANY) for array in after],
        out_specs=[by_row(part.shape) for part in row_outs] + [whole(part.shape) for part in sent],
        out_shape=list(row_outs) + list(sent),
        scratch_shapes=list(scratch),
        compiler_params=pltpu.CompilerParams(
            dimension_semantics=("arbitrary",), vmem_limit_bytes=MEMORY
        ),
        cost_estimate=pl.CostEstimate(flops=cost, bytes_accessed=8 * 2**20, transcendentals=0),
    )(lengths, *rowwise, *fixed, *after)


def struct(shape, dtype):
    return jax.ShapeDtypeStruct(tuple(shape), dtype)


FORWARD_SCRATCH = lambda: [
    pltpu.VMEM((2, SEQ // 2, SEQ), F32),
    pltpu.VMEM((2, SEQ // 2, SEQ), LOW),
    pltpu.VMEM((2, SEQ, PAIR), F32),
    pltpu.VMEM((SEQ, PAIR), F32),
    pltpu.VMEM((3, HEADS // 2, SEQ, PAIR), F32),
    pltpu.VMEM((SEQ, PAIR), F32),
]
BACKWARD_SCRATCH = lambda: [
    pltpu.VMEM((HEADS, SEQ, PAIR), LOW),
    pltpu.VMEM((2, SEQ // 2, SEQ), LOW),
    pltpu.VMEM((2, SEQ // 2, SEQ), LOW),
    pltpu.VMEM((2, 2, SEQ // 2, SEQ), F32),
    pltpu.VMEM((SEQ, 3 * HEADS * HD), LOW),
    pltpu.VMEM((3, 2, SEQ, PAIR), F32),
    pltpu.VMEM((SEQ, PAIR), F32),
    pltpu.VMEM((HEADS * HD, SEQ), LOW),
    pltpu.VMEM((PAIR, SEQ), F32),
]


def attention_outs(rows, tokens, width):
    heads = (rows, HEADS, SEQ, PAIR)
    return [struct(heads, LOW)] * 3 + [struct((tokens, width), LOW)]


def dense_outs(tokens, width, hidden):
    return [
        struct((tokens, width), F32),
        struct((tokens, width), F32),
        struct((tokens, PAIR), F32),
        struct((tokens, width), LOW),
        struct((tokens, hidden), LOW),
        struct((tokens, hidden), LOW),
    ]


def vmem(shape, dtype):
    return pltpu.VMEM(tuple(shape), dtype)


def attention_weights(width):
    return [vmem((width, 3 * width), LOW), vmem((1, 3 * width), F32)]


def dense_weights(width, hidden):
    return [
        vmem((width, width), LOW),
        vmem((width, hidden), LOW),
        vmem((hidden, width), LOW),
        vmem((8, width), F32),
        vmem((1, hidden), F32),
    ]


def dense_sums(width, hidden):
    return [
        vmem((width, width), F32),
        vmem((width, hidden), F32),
        vmem((width, hidden), F32),
        vmem((8, 8, width), F32),
        vmem((8, hidden), F32),
    ]


def attention_sums(width):
    return [vmem((width, 3 * width), F32), vmem((2, 8, width), F32)]


def dense_work(width, hidden):
    return [vmem((SEQ, width), LOW), vmem((2, SEQ, width), F32), vmem((SEQ, hidden), LOW)]


def set_attention(layer, urgent_ref, raw_ref, at, wq_ref, bias_ref):
    width = wq_ref.shape[0]
    unpack_matrix(raw_ref, at, wq_ref)
    vectors = unpack_vectors(urgent_ref, 3 * width, layer)
    bias_ref[:, :width] = vectors[0:1]
    bias_ref[:, width : 2 * width] = jnp.zeros((1, width), F32)
    bias_ref[:, 2 * width :] = vectors[1:2]


def set_dense(layer, urgent_ref, raw_ref, at, wo_ref, wi_ref, wf_ref, small_ref, bi_ref):
    width, hidden = wi_ref.shape
    unpack_matrix(raw_ref, at, wo_ref)
    unpack_matrix(raw_ref, at + width, wi_ref)
    unpack_stacked(raw_ref, at + width + hidden, wf_ref)
    small_ref[...] = unpack_vectors(urgent_ref, 3 * width, layer)
    bi_ref[...] = unpack_hidden(urgent_ref, 3 * width, layer, hidden)


def clear(refs):
    for ref in refs:
        ref[...] = jnp.zeros(ref.shape, ref.dtype)


def attention_kernel(layer, lengths, x, urgent, raw, at):
    rows, (tokens, width) = lengths.shape[0], x.shape

    def setup(fixed, work):
        set_attention(layer, fixed[0], fixed[-1], at, *work[:2])

    def body(row, lengths_ref, rowwise, outs, work):
        attention_forward(row, lengths_ref, rowwise[0][...].astype(LOW), *work[:2], *outs, *work[2:])

    fixed = [urgent] if raw is urgent else [urgent, raw]
    return run_rows(
        body, lengths, [x], fixed, attention_outs(rows, tokens, width), [],
        attention_weights(width) + FORWARD_SCRATCH(), 4 * 10**9, setup, None,
    )


def dense_kernel(layer, lengths, x, ob, urgent, raw, at, hidden, after):
    tokens, width = x.shape

    def setup(fixed, work):
        set_dense(layer, *fixed, at, *work[:5])

    def body(row, lengths_ref, rowwise, outs, work):
        dense_forward(*rowwise, *work[:5], *outs, *work[5:])

    return run_rows(
        body, lengths, [x, ob], [urgent, raw],
        dense_outs(tokens, width, hidden) + [struct((tokens, width), F32)], [],
        dense_weights(width, hidden) + [vmem((SEQ, width), F32), vmem((2, SEQ, width), F32)],
        5 * 10**9, setup, None, after,
    )


def turn_kernel(layer, lengths, x, ob, cotangent, urgent, raw, at, hidden):
    tokens, width = x.shape
    columns = width + 2 * hidden + width + hidden // 8

    def setup(fixed, work):
        set_dense(layer, *fixed, at, *work[:5])
        clear(work[5:10])

    def body(row, lengths_ref, rowwise, outs, work):
        x_ref, ob_ref, dz_ref = rowwise
        z_ref, dr_ref, dob_ref = outs
        weights, sums, kept = work[:5], work[5:10], work[10:16]
        work_ref, low_ref, u_ref, du_ref = work[16:]
        dense_forward(x_ref, ob_ref, *weights, *kept, z_ref, work_ref, u_ref)
        dense_backward(
            dz_ref, *kept, ob_ref, *weights[:4], dr_ref, dob_ref, *sums, low_ref, u_ref, du_ref
        )

    def finish(work, fixed, sent_ref):
        pack_dense(*work[5:10], sent_ref, 0)

    kept = [vmem((SEQ,) + part.shape[1:], part.dtype) for part in dense_outs(tokens, width, hidden)]
    return run_rows(
        body, lengths, [x, ob, cotangent], [urgent, raw],
        [struct((tokens, width), LOW), struct((tokens, width), F32), struct((tokens, width), LOW)],
        [struct((4, 64, columns), LOW)],
        dense_weights(width, hidden) + dense_sums(width, hidden) + kept
        + [vmem((SEQ, width), F32)] + dense_work(width, hidden),
        10**10, setup, finish,
    )


def attention_back_kernel(layer, lengths, upper, urgent, raw, dtype, after):
    tokens, width = upper[0].shape

    def setup(fixed, work):
        set_attention(layer, fixed[0], fixed[-1], 0, *work[:2])
        clear(work[2:4])

    def body(row, lengths_ref, rowwise, outs, work):
        attention_backward(
            row, lengths_ref, rowwise[0][...].astype(LOW), *rowwise[1:6], work[0], rowwise[6],
            outs[0], *work[2:4], *work[4:],
        )

    def finish(work, fixed, sent_ref):
        pack_attention(*work[2:4], sent_ref, 0)

    fixed = [urgent] if raw is urgent else [urgent, raw]
    return run_rows(
        body, lengths, list(upper), fixed, [struct((tokens, width), dtype)],
        [struct((4, 64, 4 * width), LOW)],
        attention_weights(width) + attention_sums(width) + BACKWARD_SCRATCH(),
        8 * 10**9, setup, finish, after,
    )


def dense_back_kernel(layer, lengths, dz, lower, urgent, raw, at, hidden, joined, after):
    tokens, width = dz.shape
    ahead = joined.shape[2]
    columns = ahead + width + 2 * hidden + width + hidden // 8

    def setup(fixed, work):
        set_dense(layer, *fixed[:2], at, *work[:5])
        clear(work[5:10])

    def body(row, lengths_ref, rowwise, outs, work):
        dense_backward(*rowwise, *work[:4], *outs, *work[5:])

    def finish(work, fixed, sent_ref):
        sent_ref[:, :, pl.ds(0, ahead)] = fixed[2][...]
        pack_dense(*work[5:10], sent_ref, ahead)

    return run_rows(
        body, lengths, [dz] + list(lower), [urgent, raw, joined],
        [struct((tokens, width), F32), struct((tokens, width), LOW)],
        [struct((4, 64, columns), LOW)],
        dense_weights(width, hidden) + dense_sums(width, hidden) + dense_work(width, hidden),
        7 * 10**9, setup, finish, after,
    )


def hold(array, after):
    def kernel(*refs):
        pass

    anywhere = pl.BlockSpec(memory_space=pl.ANY)
    return pl.pallas_call(
        kernel,
        in_specs=[anywhere] * (1 + len(after)),
        out_specs=anywhere,
        out_shape=shape_of(array),
        input_output_aliases={0: 0},
    )(array, *after)


def pack_parameters(
    attn_weight, attn_bias, out_weight, ffn_in, ffn_in_bias, ffn_out, norm_gain, shifts
):
    depth, rows, width = out_weight.shape
    copies = GROUPS[1]
    hidden = ffn_in.shape[2]
    early = 4 * width + 2 * hidden + 128
    columns = 4 * width + 2 * hidden
    height = ffn_in_bias.shape[1]

    def kernel(wq_ref, ab_ref, wo_ref, wi_ref, bi_ref, wf_ref, gain_ref, shift_ref, first_ref, rest_ref, small_ref):
        def put(ref, block, at):
            block = jnp.broadcast_to(block.astype(F32)[None], (copies,) + block.shape)
            block = block.reshape(copies * block.shape[1], block.shape[2])
            ref[:, pl.ds(at, block.shape[1])] = block.astype(LOW)

        small_ref[...] = jnp.zeros(small_ref.shape, F32)
        for layer in range(depth):
            lanes = pl.ds(rows * layer, rows)
            small_ref[0:2, lanes] = ab_ref[layer].astype(F32)
            small_ref[2:4, lanes] = gain_ref[layer].astype(F32)
            small_ref[4:8, lanes] = shift_ref[layer].astype(F32)
        small_ref[0:depth, pl.ds(2 * rows, height)] = bi_ref[...].astype(F32)
        put(first_ref, wq_ref[0], 0)
        put(first_ref, small_ref[...], 3 * width)
        for layer, ref, at in ((0, first_ref, 3 * width + 128), (1, rest_ref, 3 * width)):
            if layer:
                put(ref, wq_ref[layer], 0)
            put(ref, wo_ref[layer], at)
            put(ref, wi_ref[layer], at + width)
            at += width + hidden
            down = wf_ref[layer].astype(F32)
            for step in range(hidden // width):
                put(ref, down[step * rows : (step + 1) * rows], at)
                at += width

    return pl.pallas_call(
        kernel,
        in_specs=[pl.BlockSpec(memory_space=pltpu.VMEM)] * 8,
        out_shape=[struct((copies * rows, early), LOW), struct((copies * rows, columns), LOW)],
        scratch_shapes=[vmem((rows, 128), F32)],
        compiler_params=pltpu.CompilerParams(vmem_limit_bytes=MEMORY),
    )(attn_weight, attn_bias, out_weight, ffn_in, ffn_in_bias, ffn_out, norm_gain, shifts)


def add_parts(received, after=(), passed=None, joined=None):
    extra = [] if passed is None else [passed]
    inner = [] if joined is None else [joined]
    ahead = 0 if joined is None else joined.shape[1]
    rows, lanes_in = received.shape[1:]

    def kernel(in_ref, *refs):
        out_ref = refs[len(inner) + len(extra) + len(after)]
        if inner:
            out_ref[:, pl.ds(0, ahead)] = refs[0][...]
        columns = 256
        for start in range(0, lanes_in, columns):
            size = min(columns, lanes_in - start)
            total = jnp.sum(in_ref[:, :, pl.ds(start, size)].astype(F32), 0)
            out_ref[:, pl.ds(ahead + start, size)] = total.astype(LOW)

    anywhere = pl.BlockSpec(memory_space=pl.ANY)
    near = pl.BlockSpec(memory_space=pltpu.VMEM)
    found = pl.pallas_call(
        kernel,
        in_specs=[near] * (1 + len(inner)) + [anywhere] * (len(extra) + len(after)),
        out_specs=[near] + [anywhere] * len(extra),
        out_shape=[struct((rows, ahead + lanes_in), LOW)] + [shape_of(part) for part in extra],
        input_output_aliases={1 + len(inner): 1} if extra else {},
        compiler_params=pltpu.CompilerParams(vmem_limit_bytes=MEMORY),
    )(received, *inner, *extra, *after)
    return found if extra else found[0]


def write_gradients(place, tail, front, depth, width, hidden):
    rows = GROUPS[2]
    last = front.shape[1] - 4 * width
    height = hidden // DEVICES

    def kernel(place_ref, tail_ref, front_ref, gwq_ref, gab_ref, gwo_ref, gwi_ref, gbi_ref, gwf_ref, gain_ref, shift_ref):
        spot = place_ref[0]

        def total(ref, at, columns):
            block = ref[:, pl.ds(at, columns)].astype(F32)
            return jnp.sum(block.reshape(-1, rows, columns), 0)

        def own(block, size):
            return pltpu.roll(block, block.shape[1] - spot * size, 1)

        for layer, ref, at in ((0, front_ref, last), (1, front_ref, 0)):
            gwq_ref[layer] = total(ref, at, 3 * width)
            gab_ref[layer] = own(total(ref, at + 3 * width, width), rows)[0:2, 0:rows]
        for layer, ref, at in ((0, front_ref, 4 * width), (1, tail_ref, 0)):
            gwo_ref[layer] = total(ref, at, width)
            gwi_ref[layer] = total(ref, at + width, hidden)
            for step in range(hidden // width):
                gwf_ref[layer, pl.ds(step * rows, rows)] = total(
                    ref, at + width + hidden + step * width, width
                )
            at += width + 2 * hidden
            small = own(total(ref, at, width), rows)
            gain_ref[layer] = small[2:4, 0:rows]
            shift_ref[layer] = small[4:8, 0:rows]
            line = total(ref, at + width, hidden // 8)
            line = jnp.concatenate([line[step : step + 1] for step in range(8)], 1)
            gbi_ref[pl.ds(layer, 1)] = own(line, height)[:, 0:height]

    outs = [
        struct((depth, rows, 3 * width), F32),
        struct((depth, 2, rows), F32),
        struct((depth, rows, width), F32),
        struct((depth, rows, hidden), F32),
        struct((depth, height), F32),
        struct((depth, height, width), F32),
        struct((depth, 2, rows), F32),
        struct((depth, 4, rows), F32),
    ]
    return pl.pallas_call(
        kernel,
        in_specs=[pl.BlockSpec(memory_space=pltpu.SMEM)] + [pl.BlockSpec(memory_space=pltpu.VMEM)] * 2,
        out_shape=outs,
        compiler_params=pltpu.CompilerParams(vmem_limit_bytes=MEMORY),
    )(place, tail, front)


def exchange(parts, axis):
    return lax.all_to_all(parts, axis, 0, 0, tiled=True)


def local(
    hidden_in,
    lengths,
    grad_out,
    attn_weight,
    attn_bias,
    out_weight,
    ffn_in,
    ffn_in_bias,
    ffn_out,
    norm_gain,
    shifts,
):
    depth, rows, width = out_weight.shape
    hidden = ffn_in.shape[2]
    first, second = lax.axis_size("dp"), lax.axis_size("fsdp")
    fits = (second, first, rows) == GROUPS
    urgent_size = 3 * width + 128
    if fits:
        early, later = pack_parameters(
            attn_weight, attn_bias, out_weight, ffn_in, ffn_in_bias, ffn_out, norm_gain, shifts
        )
        early = exchange(early, "dp")
        urgent = early[:, :urgent_size]
        urgent = exchange(jnp.broadcast_to(urgent[None], (second,) + urgent.shape), "fsdp")
        raw0 = lax.all_gather(early[:, urgent_size:], "fsdp")
        later = exchange(hold(later, (urgent,)), "dp")
    else:
        urgent, raw0, raw1 = gather_other(
            attn_weight, attn_bias, out_weight, ffn_in, ffn_in_bias, ffn_out, norm_gain, shifts
        )
        ready = ()

    qa0, ka0, va0, ob0 = attention_kernel(0, lengths, hidden_in, urgent, urgent, 0)
    if fits:
        later = hold(later, (ob0,))
        raw1 = lax.all_gather(later, "fsdp")
        ready = (later,)
    n1, n2, inv, yb, gb, gp, z0 = dense_kernel(
        0, lengths, hidden_in, ob0, urgent, raw0, 0, hidden, ready
    )
    qa1, ka1, va1, ob1 = attention_kernel(1, lengths, z0, urgent, raw1, 0)
    hidden_out, dr1, dob1, sent_a = turn_kernel(
        1, lengths, z0, ob1, grad_out, urgent, raw1, 3 * width, hidden
    )
    dx1, sent_q = attention_back_kernel(
        1, lengths, (z0, dob1, ob1, qa1, ka1, va1, dr1), urgent, raw1, F32, (sent_a,)
    )
    ready = ()
    if fits:
        tail = add_parts(exchange(sent_a, "fsdp"), (sent_q,))
        ready = (tail,)
    dr0, dob0, sent_b = dense_back_kernel(
        0, lengths, dx1, (n1, n2, inv, yb, gb, gp, ob0), urgent, raw0, 0, hidden, sent_q, ready
    )
    if fits:
        tail = exchange(tail, "dp")
        ready = (tail,)
    grad_in, sent_c = attention_back_kernel(
        0, lengths, (hidden_in, dob0, ob0, qa0, ka0, va0, dr0), urgent, urgent, LOW,
        (sent_b,) + ready,
    )
    if fits:
        front, sent_c = add_parts(exchange(sent_b, "fsdp"), (), sent_c)
        front = add_parts(exchange(sent_c, "fsdp"), (), None, front)
        front = exchange(front, "dp")
        place = lax.axis_index(("dp", "fsdp")).astype(jnp.int32).reshape(1)
        grads = write_gradients(place, tail, front, depth, width, hidden)
    else:
        grads = scatter_other(sent_a, sent_b, sent_c, rows, width, hidden)
    return (hidden_out, grad_in, *grads)


def gather_other(
    attn_weight, attn_bias, out_weight, ffn_in, ffn_in_bias, ffn_out, norm_gain, shifts
):
    axes = ("dp", "fsdp")
    gather = lambda part, axis: lax.all_gather(part, axes, axis=axis, tiled=True)
    depth, unused, width = out_weight.shape
    hidden = ffn_in.shape[2]
    outer, inner, rows = GROUPS
    vectors = gather(jnp.concatenate([attn_bias, norm_gain, shifts], 1), 2)
    line = gather(ffn_in_bias, 1)

    def order(natural):
        return (
            natural.reshape(inner, outer, rows, -1).swapaxes(0, 1).reshape(outer, inner * rows, -1)
        )

    def stacked(part):
        part = part.reshape(DEVICES, -1, rows, width)
        return order(part.swapaxes(1, 2).reshape(width, -1))

    small = vectors.reshape(depth, 8, DEVICES, rows).transpose(2, 1, 0, 3).reshape(width, -1)
    line = line.reshape(depth, DEVICES, -1).swapaxes(0, 1)
    line = jnp.pad(line, ((0, 0), (0, 8 - depth), (0, 0))).reshape(width, -1)
    small = jnp.concatenate([small, line], 1)
    small = jnp.pad(small, ((0, 0), (0, 128 - small.shape[1])))
    wq, wo, wi, wf = (gather(part, 1) for part in (attn_weight, out_weight, ffn_in, ffn_out))
    urgent = jnp.concatenate([order(wq[0]), order(small)], 2)
    raw0 = jnp.concatenate([order(wo[0]), order(wi[0]), stacked(wf[0])], 2)
    raw1 = jnp.concatenate([order(wq[1]), order(wo[1]), order(wi[1]), stacked(wf[1])], 2)
    return urgent, raw0, raw1


def scatter_other(sent_a, sent_b, sent_c, own_rows, width, hidden):
    outer, inner, rows = GROUPS
    axes = ("dp", "fsdp")

    def natural(part):
        return part.reshape(outer, inner, rows, -1).swapaxes(0, 1).reshape(width, -1).astype(F32)

    def cut(part, sizes):
        found, at = [], 0
        for size in sizes:
            found.append(part[:, at : at + size])
            at += size
        return found

    dense = [width, hidden, hidden, width, hidden // 8]
    attention = [3 * width, width]
    wq0, ab0 = cut(natural(sent_c), attention)
    wq1, ab1, wo0, wi0, wf0, small0, bi0 = cut(natural(sent_b), attention + dense)
    wo1, wi1, wf1, small1, bi1 = cut(natural(sent_a), dense)

    def stacked(part):
        part = part.reshape(DEVICES, rows, -1, width).swapaxes(1, 2)
        return part.reshape(hidden, width)

    def spread(parts, axis):
        return lax.psum_scatter(jnp.stack(parts), axes, scatter_dimension=axis, tiled=True)

    return (
        spread([wq0, wq1], 1),
        spread([ab0[:2], ab1[:2]], 2),
        spread([wo0, wo1], 1),
        spread([wi0, wi1], 1),
        spread([bi0[:8].reshape(-1), bi1[:8].reshape(-1)], 1),
        spread([stacked(wf0), stacked(wf1)], 1),
        spread([small0[2:4], small1[2:4]], 2),
        spread([small0[4:8], small1[4:8]], 2),
    )


def solution(mesh):
    placed = (
        P(("dp", "fsdp"), None),
        P(("dp", "fsdp"), None),
        P(("dp", "fsdp"), None),
        P(None, ("dp", "fsdp"), None),
        P(None, None, ("dp", "fsdp")),
        P(None, ("dp", "fsdp"), None),
        P(None, ("dp", "fsdp"), None),
        P(None, ("dp", "fsdp")),
        P(None, ("dp", "fsdp"), None),
        P(None, None, ("dp", "fsdp")),
        P(None, None, ("dp", "fsdp")),
    )
    return jax.shard_map(
        local,
        mesh=mesh,
        in_specs=placed,
        out_specs=(
            P(("dp", "fsdp"), None),
            P(("dp", "fsdp"), None),
            P(None, ("dp", "fsdp"), None),
            P(None, None, ("dp", "fsdp")),
            P(None, ("dp", "fsdp"), None),
            P(None, ("dp", "fsdp"), None),
            P(None, ("dp", "fsdp")),
            P(None, ("dp", "fsdp"), None),
            P(None, None, ("dp", "fsdp")),
            P(None, None, ("dp", "fsdp")),
        ),
        check_vma=False,
    )
```

```python
from functools import partial

import jax
import jax.numpy as jnp
from jax import lax
from jax.experimental import pallas as pl
from jax.experimental.pallas import tpu as pltpu
from jax.sharding import PartitionSpec as P

HEADS = 4
HD = 64
SEQ = 512
PAIR = 2 * HD
FAR = -(2.0**100)
FLOOR = -1e20
EPSILON = 1e-12
PIECE = 256
SMALL = 128
GROUPS = (4, 8, 8)
DEVICES = 32
LOW = jnp.bfloat16
F32 = jnp.float32
MEMORY = 60 * 2**20


def dot_nn(left, right):
    return lax.dot_general(left, right, (((1,), (0,)), ((), ())), preferred_element_type=F32)


def dot_nt(left, right):
    return lax.dot_general(left, right, (((1,), (1,)), ((), ())), preferred_element_type=F32)


def dot_tn(left, right):
    return lax.dot_general(left, right, (((0,), (0,)), ((), ())), preferred_element_type=F32)


def pieces(total, size=PIECE):
    return [pl.ds(start, size) for start in range(0, total, size)]


def three_parts(values):
    first = values.astype(LOW).astype(F32)
    rest = values - first
    second = rest.astype(LOW).astype(F32)
    return first, second, rest - second


CURVE = (
    7.97882253e-01,
    3.63445176e-02,
    -4.47304308e-05,
    -5.04138899e-05,
    3.10523303e-06,
    -6.66676088e-08,
)
BELL = -0.5 / 0.6931471805599453


def gelu_parts(u):
    square = u * u
    near = jnp.minimum(square, 31.36)
    curve = CURVE[-1]
    for factor in CURVE[-2::-1]:
        curve = curve * near + factor
    bent = jnp.tanh(u * curve)
    half = 0.5 * u
    slope = (0.5 + 0.5 * bent) + (u * 0.3989422804014327) * jnp.exp2(square * BELL)
    return half + half * bent, slope


def lane_facts():
    lane = lax.broadcasted_iota(jnp.int32, (1, PAIR), 1)
    return lane < HD, lane & (HD - 1)


def segments(lengths_ref, row, start, rows):
    places = lax.broadcasted_iota(jnp.int32, (rows, 1), 0) + start
    bound = jnp.int32(0)
    segment = jnp.zeros((rows, 1), jnp.int32)
    last = lengths_ref.shape[1] - 1
    for entry in range(last):
        bound = bound + lengths_ref[row, entry]
        segment = segment + (places >= bound).astype(jnp.int32)
    return segment, (segment == last).astype(F32), last


def attention_forward(row, lengths_ref, x, wq_ref, bias_ref, qa_ref, ka_ref, va_ref, ob_ref, s_ref, p_ref, m_ref, pad_ref, q_ref, aug_ref):
    width = HEADS * HD
    for block in range(3):
        for pair in range(HEADS // 2):
            at = block * width + pair * PAIR
            q_ref[block, pair] = dot_nn(x, wq_ref[:, at : at + PAIR]) + bias_ref[:, at : at + PAIR]
    for start in range(0, SEQ, PIECE):
        place = pl.ds(start, PIECE)
        low_half, slot = lane_facts()
        segment, pad, last = segments(lengths_ref, row, start, PIECE)
        pad_ref[place] = jnp.broadcast_to(pad, (PIECE, PAIR))
        aug_q = jnp.where(slot == segment, 1.0, 0.0)
        aug_ref[place] = aug_q
        seen = (slot == segment) & (slot != last)
        aug_k = jnp.where(seen, 0.0, jnp.where(slot <= last, FAR, jnp.where(slot <= last + 3, 1.0, 0.0)))
        for pair in range(HEADS // 2):
            q = q_ref[0, pair, place] * HD**-0.5
            k = q_ref[1, pair, place]
            v = q_ref[2, pair, place]
            q_ref[0, pair, place] = q
            qa_ref[2 * pair, place] = jnp.where(low_half, q, aug_q).astype(LOW)
            qa_ref[2 * pair + 1, place] = jnp.where(low_half, aug_q, q).astype(LOW)
            ka_ref[2 * pair, place] = jnp.where(low_half, k, aug_k).astype(LOW)
            ka_ref[2 * pair + 1, place] = jnp.where(low_half, aug_k, k).astype(LOW)
            va_ref[2 * pair, place] = jnp.where(low_half, v, 1.0).astype(LOW)
            va_ref[2 * pair + 1, place] = jnp.where(low_half, 1.0, v).astype(LOW)
    half = SEQ // 2
    units = [(head, part) for head in range(HEADS) for part in range(2)]

    def scores(unit):
        head, part = units[unit]
        s_ref[unit % 2] = dot_nt(qa_ref[head, pl.ds(part * half, half)], ka_ref[head])

    def softmax(unit):
        head, part = units[unit]
        highest = jnp.maximum(jnp.max(s_ref[unit % 2], -1, keepdims=True), FLOOR)
        m_ref[head % 2, pl.ds(part * half, half)] = jnp.broadcast_to(highest, (half, PAIR))
        for start in range(0, half, SMALL):
            place = pl.ds(start, SMALL)
            s = s_ref[unit % 2, place] - highest[start : start + SMALL]
            p_ref[unit % 2, place] = jnp.exp(s).astype(LOW)

    def attend(unit):
        head, part = units[unit]
        return dot_nn(p_ref[unit % 2], va_ref[head])

    sums = {}
    scores(0)
    for unit in range(len(units)):
        if unit + 1 < len(units):
            scores(unit + 1)
        softmax(unit)
        head, part = units[unit]
        q_ref[1, head % 2, pl.ds(part * half, half)] = attend(unit)
        if head % 2 and part:
            pair = head // 2
            for start in range(0, SEQ, PIECE):
                place = pl.ds(start, PIECE)
                low_half, slot = lane_facts()
                even = q_ref[1, 0, place]
                odd = q_ref[1, 1, place]
                pad = pad_ref[place]
                last = lengths_ref.shape[1] - 1
                total = jnp.where(low_half, odd, even) + pad
                top = jnp.where(low_half, odd_even(m_ref, 1, place), odd_even(m_ref, 0, place))
                spread = jnp.where(pad > 0, 0.0, top + jnp.log(total))
                first, second, third = three_parts(spread)
                aug = jnp.where(
                    slot == last + 1,
                    -first,
                    jnp.where(slot == last + 2, -second, jnp.where(slot == last + 3, -third, aug_ref[place])),
                )
                q = q_ref[0, pair, place]
                qa_ref[2 * pair, place] = jnp.where(low_half, q, aug).astype(LOW)
                qa_ref[2 * pair + 1, place] = jnp.where(low_half, aug, q).astype(LOW)
                v = q_ref[2, pair, place].astype(LOW).astype(F32)
                out = jnp.where(low_half, even, odd) / pltpu.roll(total, HD, 1) + pad * v
                ob_ref[place, pl.ds(pair * PAIR, PAIR)] = out.astype(LOW)


def odd_even(ref, which, place):
    return ref[which, place]


def normal(values):
    centred = values - jnp.mean(values, -1, keepdims=True)
    inverse = lax.rsqrt(jnp.mean(centred * centred, -1, keepdims=True) + EPSILON)
    return centred * inverse, inverse


def normal_back(cotangent, unit, inverse, gains):
    scaled = cotangent * gains
    return inverse * (
        scaled
        - jnp.mean(scaled, -1, keepdims=True)
        - unit * jnp.mean(scaled * unit, -1, keepdims=True)
    )


def dense_forward(x_ref, ob_ref, wo_ref, wi_ref, wf_ref, small_ref, bi_ref, n1_ref, n2_ref, inv_ref, yb_ref, gb_ref, gp_ref, z_ref, work_ref, u_ref):
    small = lambda index: small_ref[pl.ds(index, 1)]
    work_ref[...] = dot_nn(ob_ref[...], wo_ref[...])
    for place in pieces(SEQ):
        unit, inverse = normal(x_ref[place].astype(F32) + work_ref[place] + small(4))
        n1_ref[place] = unit
        inv_ref[place, pl.ds(0, HD)] = jnp.broadcast_to(inverse, (PIECE, HD))
        y = unit * small(2) + small(5)
        yb_ref[place] = y.astype(LOW)
        work_ref[place] = y + small(6)
    columns = 256
    count = wi_ref.shape[1] // columns

    def into(step):
        u_ref[step % 2] = dot_nn(yb_ref[...], wi_ref[:, pl.ds(step * columns, columns)])

    into(0)
    for step in range(count):
        if step + 1 < count:
            into(step + 1)
        lanes = pl.ds(step * columns, columns)
        for place in pieces(SEQ, SMALL):
            g, slope = gelu_parts(u_ref[step % 2, place] + bi_ref[:, lanes])
            gb_ref[place, lanes] = g.astype(LOW)
            gp_ref[place, lanes] = slope.astype(LOW)
    work_ref[...] += dot_nn(gb_ref[...], wf_ref[...])
    for place in pieces(SEQ):
        unit, inverse = normal(work_ref[place])
        n2_ref[place] = unit
        inv_ref[place, pl.ds(HD, HD)] = jnp.broadcast_to(inverse, (PIECE, HD))
        z_ref[place] = (unit * small(3) + small(7)).astype(z_ref.dtype)


def fold(values):
    return jnp.sum(values.reshape(-1, 8, values.shape[-1]), 0)


def dense_backward(dz_ref, n1_ref, n2_ref, inv_ref, yb_ref, gb_ref, gp_ref, ob_ref, wo_ref, wi_ref, wf_ref, small_ref, dr_ref, dob_ref, gwo_ref, gwi_ref, gwf_ref, gsmall_ref, gbi_ref, low_ref, u_ref, du_ref):
    small = lambda index: small_ref[pl.ds(index, 1)]
    for place in pieces(SEQ):
        dz = dz_ref[place].astype(F32)
        unit = n2_ref[place]
        gsmall_ref[3] += fold(dz * unit)
        gsmall_ref[7] += fold(dz)
        dr = normal_back(dz, unit, inv_ref[place, pl.ds(HD, 1)], small(3))
        dr_ref[place] = dr
        df = dr.astype(LOW)
        low_ref[place] = df
        gsmall_ref[6] += fold(df.astype(F32))
    columns = 256
    count = wi_ref.shape[1] // columns

    def back(step):
        u_ref[step % 2] = dot_nt(low_ref[...], wf_ref[pl.ds(step * columns, columns)])

    back(0)
    for step in range(count):
        if step + 1 < count:
            back(step + 1)
        lanes = pl.ds(step * columns, columns)
        gwf_ref[:, lanes] += dot_tn(low_ref[...], gb_ref[:, lanes])
        for place in pieces(SEQ, SMALL):
            du = (u_ref[step % 2, place] * gp_ref[place, lanes].astype(F32)).astype(LOW)
            du_ref[place, lanes] = du
            gbi_ref[:, lanes] += fold(du.astype(F32))
        gwi_ref[:, lanes] += dot_tn(yb_ref[...], du_ref[:, lanes])
    u_ref[0] = dot_nt(du_ref[...], wi_ref[...])
    for place in pieces(SEQ):
        dy = dr_ref[place] + u_ref[0, place]
        unit = n1_ref[place]
        gsmall_ref[2] += fold(dy * unit)
        gsmall_ref[5] += fold(dy)
        dr = normal_back(dy, unit, inv_ref[place, pl.ds(0, 1)], small(2))
        dr_ref[place] = dr
        da = dr.astype(LOW)
        low_ref[place] = da
        gsmall_ref[4] += fold(da.astype(F32))
    gwo_ref[...] += dot_tn(ob_ref[...], low_ref[...])
    dob_ref[...] = dot_nt(low_ref[...], wo_ref[...]).astype(LOW)


def attention_backward(row, lengths_ref, x, dob_ref, ob_ref, qa_ref, ka_ref, va_ref, wq_ref, dr_ref, dx_ref, gwq_ref, gbias_ref, da_ref, p_ref, ds_ref, s_ref, dqkv_ref, dq_ref, pad_ref, kt_ref, dqt_ref):
    width = HEADS * HD
    half = SEQ // 2
    low_half, slot = lane_facts()
    for start in range(0, SEQ, PIECE):
        place = pl.ds(start, PIECE)
        segment, pad, last = segments(lengths_ref, row, start, PIECE)
        pad_ref[place] = jnp.broadcast_to(pad, (PIECE, PAIR))
        for pair in range(HEADS // 2):
            lanes = pl.ds(pair * PAIR, PAIR)
            dob = dob_ref[place, lanes].astype(F32)
            product = dob * ob_ref[place, lanes].astype(F32)
            even = jnp.sum(jnp.where(low_half, product, 0.0), -1, keepdims=True)
            odd = jnp.sum(jnp.where(low_half, 0.0, product), -1, keepdims=True)
            first, second, third = three_parts(jnp.where(low_half, odd, even))
            aug = jnp.where(
                slot == 0, -first, jnp.where(slot == 1, -second, jnp.where(slot == 2, -third, 0.0))
            )
            da_ref[2 * pair, place] = jnp.where(low_half, dob, aug).astype(LOW)
            da_ref[2 * pair + 1, place] = jnp.where(low_half, aug, dob).astype(LOW)
    for pair in range(HEADS // 2):
        low_half, unused = lane_facts()
        keys = jnp.where(low_half, ka_ref[2 * pair].astype(F32), ka_ref[2 * pair + 1].astype(F32))
        kt_ref[pl.ds(pair * PAIR, PAIR)] = keys.T.astype(LOW)
    low_half, slot = lane_facts()
    units = [(head, part) for head in range(HEADS) for part in range(2)]

    def scores(unit):
        head, part = units[unit]
        keys = pl.ds(part * half, half)
        s_ref[0, unit % 2] = dot_nt(ka_ref[head, keys], qa_ref[head])
        s_ref[1, unit % 2] = dot_nt(va_ref[head, keys], da_ref[head])

    def weigh(unit):
        for place in pieces(half, SMALL):
            p = jnp.exp(s_ref[0, unit % 2, place])
            p_ref[unit % 2, place] = p.astype(LOW)
            ds_ref[unit % 2, place] = (p * s_ref[1, unit % 2, place]).astype(LOW)

    scores(0)
    for unit in range(len(units)):
        if unit + 1 < len(units):
            scores(unit + 1)
        weigh(unit)
        head, part = units[unit]
        keys = pl.ds(part * half, half)
        side = head % 2
        dq_ref[1, side, keys] = dot_nn(ds_ref[unit % 2], qa_ref[head])
        dq_ref[2, side, keys] = dot_nn(p_ref[unit % 2], da_ref[head])
        lines = pl.ds(side * HD, HD)
        dq = dot_nn(kt_ref[pl.ds(head * HD, HD), keys], ds_ref[unit % 2])
        if part:
            dqt_ref[lines] += dq
        else:
            dqt_ref[lines] = dq
        if side and part:
            pair = head // 2
            dq_ref[0, 0] = dqt_ref[...].T
            for start in range(0, SEQ, PIECE):
                place = pl.ds(start, PIECE)
                dq = dq_ref[0, 0, place] * HD**-0.5
                dk = jnp.where(low_half, dq_ref[1, 0, place], dq_ref[1, 1, place])
                dv = jnp.where(low_half, dq_ref[2, 0, place], dq_ref[2, 1, place])
                dv = dv + pad_ref[place] * dob_ref[place, pl.ds(pair * PAIR, PAIR)].astype(F32)
                for block, value in enumerate((dq, dk, dv)):
                    lanes = pl.ds(block * width + pair * PAIR, PAIR)
                    value = value.astype(LOW)
                    dqkv_ref[place, lanes] = value
                    if block != 1:
                        into = pl.ds(pair * PAIR, PAIR)
                        gbias_ref[block // 2, :, into] += fold(value.astype(F32))
    gwq_ref[...] += dot_tn(x, dqkv_ref[...])
    dx_ref[...] = (dr_ref[...] + dot_nt(dqkv_ref[...], wq_ref[...])).astype(dx_ref.dtype)


def unpack_matrix(raw_ref, at, into_ref):
    width = into_ref.shape[0]
    for start in range(0, into_ref.shape[1], width):
        block = raw_ref[:, :, pl.ds(at + start, width)].astype(F32)
        block = block.reshape(GROUPS + (width,)).swapaxes(0, 1).reshape(width, width)
        into_ref[:, pl.ds(start, width)] = block.astype(LOW)


def unpack_stacked(raw_ref, at, into_ref):
    width = into_ref.shape[1]
    count = into_ref.shape[0] // width
    blocks = [
        raw_ref[:, :, pl.ds(at + step * width, width)].astype(F32).reshape(GROUPS + (width,))
        for step in range(count)
    ]
    outer, inner, rows = GROUPS
    for place in range(inner):
        part = jnp.stack([jnp.stack([block[f, place] for block in blocks]) for f in range(outer)])
        size = outer * count * rows
        into_ref[pl.ds(place * size, size)] = part.reshape(size, width).astype(LOW)


def counter(shape, axis):
    return lax.broadcasted_iota(jnp.int32, shape, axis)


def split_by(values, size):
    return lax.shift_right_logical(values, size.bit_length() - 1), values & (size - 1)


def sources(rows):
    outer, inner, height = GROUPS
    group, within = split_by(counter((rows, 1), 0), height)
    far, near = split_by(group, inner)
    return near * outer + far, within


def unpack_vectors(raw_ref, at, layer):
    outer, inner, rows = GROUPS
    total = outer * inner * rows
    raw = raw_ref[:, :, pl.ds(at, 128)].reshape(total, 128)
    owner, place = split_by(counter((1, total), 1), rows)
    pick = jnp.where(counter((128, 1), 0) == rows * layer + place, 1.0, 0.0).astype(LOW)
    device, unused = sources(total)
    spread = jnp.where(owner == device, dot_nn(raw, pick), 0.0)
    return jnp.sum(spread.reshape(outer * inner, rows, total), 0)


def unpack_hidden(raw_ref, at, layer, hidden):
    outer, inner, rows = GROUPS
    total = outer * inner * rows
    raw = raw_ref[:, :, pl.ds(at, 128)].reshape(total, 128)
    owner, place = split_by(counter((1, hidden), 1), hidden // (outer * inner))
    pick = jnp.where(counter((128, 1), 0) == 2 * rows + place, 1.0, 0.0).astype(LOW)
    device, within = sources(total)
    device = jnp.where(within == layer, device, -1)
    spread = jnp.where(owner == device, dot_nn(raw, pick), 0.0)
    return jnp.sum(spread, 0, keepdims=True)


def pack_matrix(sum_ref, sent_ref, at):
    width = sum_ref.shape[0]
    outer, inner, rows = GROUPS
    for start in range(0, sum_ref.shape[1], width):
        block = sum_ref[:, pl.ds(start, width)].reshape(inner, outer, rows, width)
        block = block.swapaxes(0, 1).reshape(outer, inner * rows, width)
        sent_ref[:, :, pl.ds(at + start, width)] = block.astype(LOW)


def pack_stacked(sum_ref, sent_ref, at):
    width = sum_ref.shape[0]
    outer, inner, rows = GROUPS
    count = sum_ref.shape[1] // width
    near = inner // count
    for step in range(count):
        block = sum_ref[:, pl.ds(step * width, width)].T
        block = block.reshape(near, outer, count, rows, width)
        for part in range(count):
            piece = jnp.stack([block[:, f, part] for f in range(outer)])
            piece = piece.reshape(outer, near * rows, width)
            sent_ref[:, pl.ds(step * near * rows, near * rows), pl.ds(at + part * width, width)] = (
                piece.astype(LOW)
            )


def pack_shared(block, sent_ref, at):
    outer, inner, rows = GROUPS
    columns = block.shape[1]
    block = jnp.broadcast_to(block[None], (outer * inner, rows, columns))
    sent_ref[:, :, pl.ds(at, columns)] = block.reshape(outer, inner * rows, columns).astype(LOW)


def pack_attention(gwq_ref, gbias_ref, sent_ref, at):
    pack_matrix(gwq_ref, sent_ref, at)
    width = gwq_ref.shape[0]
    line = lax.broadcasted_iota(jnp.int32, (8, width), 0)
    sums = [jnp.sum(gbias_ref[index], 0, keepdims=True) for index in range(2)]
    block = jnp.where(line == 0, sums[0], jnp.where(line == 1, sums[1], 0.0))
    pack_shared(block, sent_ref, at + 3 * width)


def pack_dense(gwo_ref, gwi_ref, gwf_ref, gsmall_ref, gbi_ref, sent_ref, at):
    width, hidden = gwi_ref.shape
    pack_matrix(gwo_ref, sent_ref, at)
    pack_matrix(gwi_ref, sent_ref, at + width)
    pack_stacked(gwf_ref, sent_ref, at + width + hidden)
    at = at + width + 2 * hidden
    pack_shared(jnp.sum(gsmall_ref[...], 1), sent_ref, at)
    line = jnp.sum(gbi_ref[...], 0, keepdims=True)
    size = hidden // 8
    block = jnp.concatenate([line[:, step * size : (step + 1) * size] for step in range(8)], 0)
    pack_shared(block, sent_ref, at + width)


def shape_of(array):
    return jax.ShapeDtypeStruct(array.shape, array.dtype)


def by_row(shape):
    if len(shape) == 2:
        return pl.BlockSpec((SEQ, shape[1]), lambda row: (row, 0))
    return pl.BlockSpec((None,) + tuple(shape[1:]), lambda row: (row,) + (0,) * (len(shape) - 1))


def whole(shape):
    return pl.BlockSpec(tuple(shape), lambda row: (0,) * len(shape))


def run_rows(
    body, lengths, rowwise, fixed, row_outs, sent, scratch, cost, setup, finish, after=(), scalars=()
):
    count = lengths.shape[0]
    cuts = [len(scalars), len(rowwise), len(fixed), len(after), len(row_outs), len(sent), len(scratch)]

    def kernel(lengths_ref, *refs):
        row = pl.program_id(0)
        groups = []
        at = 0
        for cut in cuts:
            groups.append(refs[at : at + cut])
            at += cut
        numbers, rows_in, fixed_in, unused, rows_out, sent_out, work = groups

        @pl.when(row == 0)
        def _():
            setup(numbers, fixed_in, sent_out, work)

        body(row, lengths_ref, rows_in, rows_out, work)

        if finish:

            @pl.when(row == count - 1)
            def _():
                finish(work, fixed_in, sent_out[0])

    return pl.pallas_call(
        kernel,
        grid=(count,),
        in_specs=[pl.BlockSpec(memory_space=pltpu.SMEM)] * (1 + len(scalars))
        + [by_row(array.shape) for array in rowwise]
        + [whole(array.shape) for array in fixed]
        + [pl.BlockSpec(memory_space=pl.ANY) for array in after],
        out_specs=[by_row(part.shape) for part in row_outs] + [whole(part.shape) for part in sent],
        out_shape=list(row_outs) + list(sent),
        scratch_shapes=list(scratch),
        compiler_params=pltpu.CompilerParams(
            dimension_semantics=("arbitrary",), vmem_limit_bytes=MEMORY
        ),
        cost_estimate=pl.CostEstimate(flops=cost, bytes_accessed=8 * 2**20, transcendentals=0),
    )(lengths, *scalars, *rowwise, *fixed, *after)


def struct(shape, dtype):
    return jax.ShapeDtypeStruct(tuple(shape), dtype)


FORWARD_SCRATCH = lambda: [
    pltpu.VMEM((2, SEQ // 2, SEQ), F32),
    pltpu.VMEM((2, SEQ // 2, SEQ), LOW),
    pltpu.VMEM((2, SEQ, PAIR), F32),
    pltpu.VMEM((SEQ, PAIR), F32),
    pltpu.VMEM((3, HEADS // 2, SEQ, PAIR), F32),
    pltpu.VMEM((SEQ, PAIR), F32),
]
BACKWARD_SCRATCH = lambda: [
    pltpu.VMEM((HEADS, SEQ, PAIR), LOW),
    pltpu.VMEM((2, SEQ // 2, SEQ), LOW),
    pltpu.VMEM((2, SEQ // 2, SEQ), LOW),
    pltpu.VMEM((2, 2, SEQ // 2, SEQ), F32),
    pltpu.VMEM((SEQ, 3 * HEADS * HD), LOW),
    pltpu.VMEM((3, 2, SEQ, PAIR), F32),
    pltpu.VMEM((SEQ, PAIR), F32),
    pltpu.VMEM((HEADS * HD, SEQ), LOW),
    pltpu.VMEM((PAIR, SEQ), F32),
]


def attention_outs(rows, tokens, width):
    heads = (rows, HEADS, SEQ, PAIR)
    return [struct(heads, LOW)] * 3 + [struct((tokens, width), LOW)]


def dense_outs(tokens, width, hidden):
    return [
        struct((tokens, width), F32),
        struct((tokens, width), F32),
        struct((tokens, PAIR), F32),
        struct((tokens, width), LOW),
        struct((tokens, hidden), LOW),
        struct((tokens, hidden), LOW),
    ]


def vmem(shape, dtype):
    return pltpu.VMEM(tuple(shape), dtype)


def attention_weights(width):
    return [vmem((width, 3 * width), LOW), vmem((1, 3 * width), F32)]


def dense_weights(width, hidden):
    return [
        vmem((width, width), LOW),
        vmem((width, hidden), LOW),
        vmem((hidden, width), LOW),
        vmem((8, width), F32),
        vmem((1, hidden), F32),
    ]


def dense_sums(width, hidden):
    return [
        vmem((width, width), F32),
        vmem((width, hidden), F32),
        vmem((width, hidden), F32),
        vmem((8, 8, width), F32),
        vmem((8, hidden), F32),
    ]


def attention_sums(width):
    return [vmem((width, 3 * width), F32), vmem((2, 8, width), F32)]


def dense_work(width, hidden):
    return [vmem((SEQ, width), LOW), vmem((2, SEQ, width), F32), vmem((SEQ, hidden), LOW)]


def set_attention(layer, urgent_ref, raw_ref, at, wq_ref, bias_ref):
    width = wq_ref.shape[0]
    unpack_matrix(raw_ref, at, wq_ref)
    vectors = unpack_vectors(urgent_ref, 3 * width, layer)
    bias_ref[:, :width] = vectors[0:1]
    bias_ref[:, width : 2 * width] = jnp.zeros((1, width), F32)
    bias_ref[:, 2 * width :] = vectors[1:2]


def set_dense(layer, urgent_ref, raw_ref, at, wo_ref, wi_ref, wf_ref, small_ref, bi_ref):
    width, hidden = wi_ref.shape
    unpack_matrix(raw_ref, at, wo_ref)
    unpack_matrix(raw_ref, at + width, wi_ref)
    unpack_stacked(raw_ref, at + width + hidden, wf_ref)
    small_ref[...] = unpack_vectors(urgent_ref, 3 * width, layer)
    bi_ref[...] = unpack_hidden(urgent_ref, 3 * width, layer, hidden)


def clear(refs):
    for ref in refs:
        ref[...] = jnp.zeros(ref.shape, ref.dtype)


def first_kernel(lengths, x, place, parts):
    rows, (tokens, width) = lengths.shape[0], x.shape

    def setup(numbers, fixed, sent, work):
        for step, part in enumerate(fixed):
            sent[0][numbers[0][0] ^ step] = part[...]
        set_attention(0, sent[0], sent[0], 0, *work[:2])

    def body(row, lengths_ref, rowwise, outs, work):
        attention_forward(row, lengths_ref, rowwise[0][...], *work[:2], *outs, *work[2:])

    return run_rows(
        body, lengths, [x], list(parts), attention_outs(rows, tokens, width),
        [struct((len(parts),) + parts[0].shape, LOW)],
        attention_weights(width) + FORWARD_SCRATCH(), 4 * 10**9, setup, None, (), [place],
    )


def attention_kernel(layer, lengths, x, urgent, raw, at):
    rows, (tokens, width) = lengths.shape[0], x.shape

    def setup(numbers, fixed, sent, work):
        set_attention(layer, *fixed, at, *work[:2])

    def body(row, lengths_ref, rowwise, outs, work):
        attention_forward(row, lengths_ref, rowwise[0][...].astype(LOW), *work[:2], *outs, *work[2:])

    return run_rows(
        body, lengths, [x], [urgent, raw], attention_outs(rows, tokens, width), [],
        attention_weights(width) + FORWARD_SCRATCH(), 4 * 10**9, setup, None,
    )


def dense_kernel(layer, lengths, x, ob, urgent, raw, at, hidden, after):
    tokens, width = x.shape

    def setup(numbers, fixed, sent, work):
        set_dense(layer, *fixed, at, *work[:5])

    def body(row, lengths_ref, rowwise, outs, work):
        dense_forward(*rowwise, *work[:5], *outs, *work[5:])

    return run_rows(
        body, lengths, [x, ob], [urgent, raw],
        dense_outs(tokens, width, hidden) + [struct((tokens, width), F32)], [],
        dense_weights(width, hidden) + [vmem((SEQ, width), F32), vmem((2, SEQ, width), F32)],
        5 * 10**9, setup, None, after,
    )


def turn_kernel(layer, lengths, x, ob, cotangent, urgent, raw, at, hidden):
    tokens, width = x.shape
    columns = width + 2 * hidden + width + hidden // 8

    def setup(numbers, fixed, sent, work):
        set_dense(layer, *fixed, at, *work[:5])
        clear(work[5:10])

    def body(row, lengths_ref, rowwise, outs, work):
        x_ref, ob_ref, dz_ref = rowwise
        z_ref, dr_ref, dob_ref = outs
        weights, sums, kept = work[:5], work[5:10], work[10:16]
        work_ref, low_ref, u_ref, du_ref = work[16:]
        dense_forward(x_ref, ob_ref, *weights, *kept, z_ref, work_ref, u_ref)
        dense_backward(
            dz_ref, *kept, ob_ref, *weights[:4], dr_ref, dob_ref, *sums, low_ref, u_ref, du_ref
        )

    def finish(work, fixed, sent_ref):
        pack_dense(*work[5:10], sent_ref, 0)

    kept = [vmem((SEQ,) + part.shape[1:], part.dtype) for part in dense_outs(tokens, width, hidden)]
    return run_rows(
        body, lengths, [x, ob, cotangent], [urgent, raw],
        [struct((tokens, width), LOW), struct((tokens, width), F32), struct((tokens, width), LOW)],
        [struct((4, 64, columns), LOW)],
        dense_weights(width, hidden) + dense_sums(width, hidden) + kept
        + [vmem((SEQ, width), F32)] + dense_work(width, hidden),
        10**10, setup, finish,
    )


def middle_kernel(lengths, upper, lower, urgent, raw1, raw0, hidden, after):
    tokens, width = upper[0].shape
    columns = 4 * width + width + 2 * hidden + width + hidden // 8

    def setup(numbers, fixed, sent, work):
        urgent_ref, raw1_ref, raw0_ref = fixed
        set_attention(1, urgent_ref, raw1_ref, 0, *work[:2])
        set_dense(0, urgent_ref, raw0_ref, 0, *work[2:7])
        clear(work[7:14])

    def body(row, lengths_ref, rowwise, outs, work):
        up, low = rowwise[:7], rowwise[7:]
        dr_ref, dob_ref = outs
        dx_ref, low_ref, u_ref, du_ref = work[14:18]
        attention_backward(
            row, lengths_ref, up[0][...].astype(LOW), *up[1:6], work[0], up[6], dx_ref,
            *work[7:9], *work[18:],
        )
        dense_backward(
            dx_ref, *low, *work[2:6], dr_ref, dob_ref, *work[9:14], low_ref, u_ref, du_ref
        )

    def finish(work, fixed, sent_ref):
        pack_attention(*work[7:9], sent_ref, 0)
        pack_dense(*work[9:14], sent_ref, 4 * width)

    return run_rows(
        body, lengths, list(upper) + list(lower), [urgent, raw1, raw0],
        [struct((tokens, width), F32), struct((tokens, width), LOW)],
        [struct((4, 64, columns), LOW)],
        attention_weights(width) + dense_weights(width, hidden)
        + attention_sums(width) + dense_sums(width, hidden)
        + [vmem((SEQ, width), F32)] + dense_work(width, hidden) + BACKWARD_SCRATCH(),
        15 * 10**9, setup, finish, after,
    )


def last_kernel(lengths, upper, urgent, after):
    tokens, width = upper[0].shape

    def setup(numbers, fixed, sent, work):
        set_attention(0, fixed[0], fixed[0], 0, *work[:2])
        clear(work[2:4])

    def body(row, lengths_ref, rowwise, outs, work):
        attention_backward(
            row, lengths_ref, rowwise[0][...], *rowwise[1:6], work[0], rowwise[6], outs[0],
            *work[2:4], *work[4:],
        )

    def finish(work, fixed, sent_ref):
        pack_attention(*work[2:4], sent_ref, 0)

    return run_rows(
        body, lengths, list(upper), [urgent], [struct((tokens, width), LOW)],
        [struct((4, 64, 4 * width), LOW)],
        attention_weights(width) + attention_sums(width) + BACKWARD_SCRATCH(),
        8 * 10**9, setup, finish, after,
    )


def hold(array, after):
    def kernel(*refs):
        pass

    anywhere = pl.BlockSpec(memory_space=pl.ANY)
    return pl.pallas_call(
        kernel,
        in_specs=[anywhere] * (1 + len(after)),
        out_specs=anywhere,
        out_shape=shape_of(array),
        input_output_aliases={0: 0},
    )(array, *after)


def pack_parameters(
    attn_weight, attn_bias, out_weight, ffn_in, ffn_in_bias, ffn_out, norm_gain, shifts
):
    depth, rows, width = out_weight.shape
    copies = GROUPS[1]
    hidden = ffn_in.shape[2]
    early = 4 * width + 2 * hidden + 128
    columns = 4 * width + 2 * hidden
    height = ffn_in_bias.shape[1]

    def kernel(wq_ref, ab_ref, wo_ref, wi_ref, bi_ref, wf_ref, gain_ref, shift_ref, first_ref, rest_ref, small_ref):
        def put(ref, block, at):
            block = jnp.broadcast_to(block.astype(F32)[None], (copies,) + block.shape)
            block = block.reshape(copies * block.shape[1], block.shape[2])
            ref[:, pl.ds(at, block.shape[1])] = block.astype(LOW)

        small_ref[...] = jnp.zeros(small_ref.shape, F32)
        for layer in range(depth):
            lanes = pl.ds(rows * layer, rows)
            small_ref[0:2, lanes] = ab_ref[layer].astype(F32)
            small_ref[2:4, lanes] = gain_ref[layer].astype(F32)
            small_ref[4:8, lanes] = shift_ref[layer].astype(F32)
        small_ref[0:depth, pl.ds(2 * rows, height)] = bi_ref[...].astype(F32)
        put(first_ref, wq_ref[0], 0)
        put(first_ref, small_ref[...], 3 * width)
        for layer, ref, at in ((0, first_ref, 3 * width + 128), (1, rest_ref, 3 * width)):
            if layer:
                put(ref, wq_ref[layer], 0)
            put(ref, wo_ref[layer], at)
            put(ref, wi_ref[layer], at + width)
            at += width + hidden
            down = wf_ref[layer].astype(F32)
            for step in range(hidden // width):
                put(ref, down[step * rows : (step + 1) * rows], at)
                at += width

    return pl.pallas_call(
        kernel,
        in_specs=[pl.BlockSpec(memory_space=pltpu.VMEM)] * 8,
        out_shape=[struct((copies * rows, early), LOW), struct((copies * rows, columns), LOW)],
        scratch_shapes=[vmem((rows, 128), F32)],
        compiler_params=pltpu.CompilerParams(vmem_limit_bytes=MEMORY),
    )(attn_weight, attn_bias, out_weight, ffn_in, ffn_in_bias, ffn_out, norm_gain, shifts)


def add_parts(received, after=(), passed=None, joined=None):
    extra = [] if passed is None else [passed]
    inner = [] if joined is None else [joined]
    ahead = 0 if joined is None else joined.shape[1]
    rows, lanes_in = received.shape[1:]

    def kernel(in_ref, *refs):
        out_ref = refs[len(inner) + len(extra) + len(after)]
        if inner:
            out_ref[:, pl.ds(0, ahead)] = refs[0][...]
        columns = 256
        for start in range(0, lanes_in, columns):
            size = min(columns, lanes_in - start)
            total = jnp.sum(in_ref[:, :, pl.ds(start, size)].astype(F32), 0)
            out_ref[:, pl.ds(ahead + start, size)] = total.astype(LOW)

    anywhere = pl.BlockSpec(memory_space=pl.ANY)
    near = pl.BlockSpec(memory_space=pltpu.VMEM)
    found = pl.pallas_call(
        kernel,
        in_specs=[near] * (1 + len(inner)) + [anywhere] * (len(extra) + len(after)),
        out_specs=[near] + [anywhere] * len(extra),
        out_shape=[struct((rows, ahead + lanes_in), LOW)] + [shape_of(part) for part in extra],
        input_output_aliases={1 + len(inner): 1} if extra else {},
        compiler_params=pltpu.CompilerParams(vmem_limit_bytes=MEMORY),
    )(received, *inner, *extra, *after)
    return found if extra else found[0]


def write_gradients(place, tail, front, depth, width, hidden):
    rows = GROUPS[2]
    last = front.shape[1] - 4 * width
    height = hidden // DEVICES

    def kernel(place_ref, tail_ref, front_ref, gwq_ref, gab_ref, gwo_ref, gwi_ref, gbi_ref, gwf_ref, gain_ref, shift_ref):
        spot = place_ref[0]

        def total(ref, at, columns):
            block = ref[:, pl.ds(at, columns)].astype(F32)
            return jnp.sum(block.reshape(-1, rows, columns), 0)

        def own(block, size):
            return pltpu.roll(block, block.shape[1] - spot * size, 1)

        for layer, ref, at in ((0, front_ref, last), (1, front_ref, 0)):
            gwq_ref[layer] = total(ref, at, 3 * width)
            gab_ref[layer] = own(total(ref, at + 3 * width, width), rows)[0:2, 0:rows]
        for layer, ref, at in ((0, front_ref, 4 * width), (1, tail_ref, 0)):
            gwo_ref[layer] = total(ref, at, width)
            gwi_ref[layer] = total(ref, at + width, hidden)
            for step in range(hidden // width):
                gwf_ref[layer, pl.ds(step * rows, rows)] = total(
                    ref, at + width + hidden + step * width, width
                )
            at += width + 2 * hidden
            small = own(total(ref, at, width), rows)
            gain_ref[layer] = small[2:4, 0:rows]
            shift_ref[layer] = small[4:8, 0:rows]
            line = total(ref, at + width, hidden // 8)
            line = jnp.concatenate([line[step : step + 1] for step in range(8)], 1)
            gbi_ref[pl.ds(layer, 1)] = own(line, height)[:, 0:height]

    outs = [
        struct((depth, rows, 3 * width), F32),
        struct((depth, 2, rows), F32),
        struct((depth, rows, width), F32),
        struct((depth, rows, hidden), F32),
        struct((depth, height), F32),
        struct((depth, height, width), F32),
        struct((depth, 2, rows), F32),
        struct((depth, 4, rows), F32),
    ]
    return pl.pallas_call(
        kernel,
        in_specs=[pl.BlockSpec(memory_space=pltpu.SMEM)] + [pl.BlockSpec(memory_space=pltpu.VMEM)] * 2,
        out_shape=outs,
        compiler_params=pltpu.CompilerParams(vmem_limit_bytes=MEMORY),
    )(place, tail, front)


def exchange(parts, axis):
    return lax.all_to_all(parts, axis, 0, 0, tiled=True)


def local(
    hidden_in,
    lengths,
    grad_out,
    attn_weight,
    attn_bias,
    out_weight,
    ffn_in,
    ffn_in_bias,
    ffn_out,
    norm_gain,
    shifts,
):
    depth, rows, width = out_weight.shape
    hidden = ffn_in.shape[2]
    first, second = lax.axis_size("dp"), lax.axis_size("fsdp")
    fits = (second, first, rows) == GROUPS
    urgent_size = 3 * width + 128
    if fits:
        early, later = pack_parameters(
            attn_weight, attn_bias, out_weight, ffn_in, ffn_in_bias, ffn_out, norm_gain, shifts
        )
        early = exchange(early, "dp")
        urgent = early[:, :urgent_size]
        parts = [urgent] + [
            lax.ppermute(urgent, "fsdp", [(source, source ^ step) for source in range(second)])
            for step in range(1, second)
        ]
        raw0 = lax.all_gather(early[:, urgent_size:], "fsdp")
        later = exchange(hold(later, (early,)), "dp")
        raw1 = lax.all_gather(later, "fsdp")
        place = lax.axis_index("fsdp").astype(jnp.int32).reshape(1)
    else:
        urgent, raw0, raw1 = gather_other(
            attn_weight, attn_bias, out_weight, ffn_in, ffn_in_bias, ffn_out, norm_gain, shifts
        )
        parts = [urgent[step] for step in range(urgent.shape[0])]
        place = jnp.zeros((1,), jnp.int32)

    qa0, ka0, va0, ob0, urgent = first_kernel(lengths, hidden_in, place, parts)
    n1, n2, inv, yb, gb, gp, z0 = dense_kernel(
        0, lengths, hidden_in, ob0, urgent, raw0, 0, hidden, ()
    )
    qa1, ka1, va1, ob1 = attention_kernel(1, lengths, z0, urgent, raw1, 0)
    hidden_out, dr1, dob1, sent_a = turn_kernel(
        1, lengths, z0, ob1, grad_out, urgent, raw1, 3 * width, hidden
    )
    if fits:
        tail = lax.psum_scatter(sent_a, "fsdp", scatter_dimension=0)
    dr0, dob0, sent_b = middle_kernel(
        lengths,
        (z0, dob1, ob1, qa1, ka1, va1, dr1),
        (n1, n2, inv, yb, gb, gp, ob0),
        urgent,
        raw1,
        raw0,
        hidden,
        (sent_a,),
    )
    if fits:
        tail = hold(tail, (sent_b,)).reshape(first, rows, -1)
        tail = lax.psum_scatter(tail, "dp", scatter_dimension=0)
    grad_in, sent_c = last_kernel(
        lengths, (hidden_in, dob0, ob0, qa0, ka0, va0, dr0), urgent, (sent_b,)
    )
    if fits:
        front, sent_c = add_parts(exchange(sent_b, "fsdp"), (), sent_c)
        front = add_parts(exchange(sent_c, "fsdp"), (), None, front)
        front = exchange(front, "dp")
        place = lax.axis_index(("dp", "fsdp")).astype(jnp.int32).reshape(1)
        grads = write_gradients(place, tail, front, depth, width, hidden)
    else:
        grads = scatter_other(sent_a, sent_b, sent_c, rows, width, hidden)
    return (hidden_out, grad_in, *grads)


def gather_other(
    attn_weight, attn_bias, out_weight, ffn_in, ffn_in_bias, ffn_out, norm_gain, shifts
):
    axes = ("dp", "fsdp")
    gather = lambda part, axis: lax.all_gather(part, axes, axis=axis, tiled=True)
    depth, unused, width = out_weight.shape
    hidden = ffn_in.shape[2]
    outer, inner, rows = GROUPS
    vectors = gather(jnp.concatenate([attn_bias, norm_gain, shifts], 1), 2)
    line = gather(ffn_in_bias, 1)

    def order(natural):
        return (
            natural.reshape(inner, outer, rows, -1).swapaxes(0, 1).reshape(outer, inner * rows, -1)
        )

    def stacked(part):
        part = part.reshape(DEVICES, -1, rows, width)
        return order(part.swapaxes(1, 2).reshape(width, -1))

    small = vectors.reshape(depth, 8, DEVICES, rows).transpose(2, 1, 0, 3).reshape(width, -1)
    line = line.reshape(depth, DEVICES, -1).swapaxes(0, 1)
    line = jnp.pad(line, ((0, 0), (0, 8 - depth), (0, 0))).reshape(width, -1)
    small = jnp.concatenate([small, line], 1)
    small = jnp.pad(small, ((0, 0), (0, 128 - small.shape[1])))
    wq, wo, wi, wf = (gather(part, 1) for part in (attn_weight, out_weight, ffn_in, ffn_out))
    urgent = jnp.concatenate([order(wq[0]), order(small)], 2)
    raw0 = jnp.concatenate([order(wo[0]), order(wi[0]), stacked(wf[0])], 2)
    raw1 = jnp.concatenate([order(wq[1]), order(wo[1]), order(wi[1]), stacked(wf[1])], 2)
    return urgent, raw0, raw1


def scatter_other(sent_a, sent_b, sent_c, own_rows, width, hidden):
    outer, inner, rows = GROUPS
    axes = ("dp", "fsdp")

    def natural(part):
        return part.reshape(outer, inner, rows, -1).swapaxes(0, 1).reshape(width, -1).astype(F32)

    def cut(part, sizes):
        found, at = [], 0
        for size in sizes:
            found.append(part[:, at : at + size])
            at += size
        return found

    dense = [width, hidden, hidden, width, hidden // 8]
    attention = [3 * width, width]
    wq0, ab0 = cut(natural(sent_c), attention)
    wq1, ab1, wo0, wi0, wf0, small0, bi0 = cut(natural(sent_b), attention + dense)
    wo1, wi1, wf1, small1, bi1 = cut(natural(sent_a), dense)

    def stacked(part):
        part = part.reshape(DEVICES, rows, -1, width).swapaxes(1, 2)
        return part.reshape(hidden, width)

    def spread(parts, axis):
        return lax.psum_scatter(jnp.stack(parts), axes, scatter_dimension=axis, tiled=True)

    return (
        spread([wq0, wq1], 1),
        spread([ab0[:2], ab1[:2]], 2),
        spread([wo0, wo1], 1),
        spread([wi0, wi1], 1),
        spread([bi0[:8].reshape(-1), bi1[:8].reshape(-1)], 1),
        spread([stacked(wf0), stacked(wf1)], 1),
        spread([small0[2:4], small1[2:4]], 2),
        spread([small0[4:8], small1[4:8]], 2),
    )


def solution(mesh):
    placed = (
        P(("dp", "fsdp"), None),
        P(("dp", "fsdp"), None),
        P(("dp", "fsdp"), None),
        P(None, ("dp", "fsdp"), None),
        P(None, None, ("dp", "fsdp")),
        P(None, ("dp", "fsdp"), None),
        P(None, ("dp", "fsdp"), None),
        P(None, ("dp", "fsdp")),
        P(None, ("dp", "fsdp"), None),
        P(None, None, ("dp", "fsdp")),
        P(None, None, ("dp", "fsdp")),
    )
    return jax.shard_map(
        local,
        mesh=mesh,
        in_specs=placed,
        out_specs=(
            P(("dp", "fsdp"), None),
            P(("dp", "fsdp"), None),
            P(None, ("dp", "fsdp"), None),
            P(None, None, ("dp", "fsdp")),
            P(None, ("dp", "fsdp"), None),
            P(None, ("dp", "fsdp"), None),
            P(None, ("dp", "fsdp")),
            P(None, ("dp", "fsdp"), None),
            P(None, None, ("dp", "fsdp")),
            P(None, None, ("dp", "fsdp")),
        ),
        check_vma=False,
    )
```

```python
from functools import partial

import jax
import jax.numpy as jnp
from jax import lax
from jax.experimental import pallas as pl
from jax.experimental.pallas import tpu as pltpu
from jax.sharding import PartitionSpec as P

HEADS = 4
HD = 64
SEQ = 512
PAIR = 2 * HD
FAR = -(2.0**100)
FLOOR = -1e20
EPSILON = 1e-12
PIECE = 256
SMALL = 128
GROUPS = (4, 8, 8)
DEVICES = 32
LOW = jnp.bfloat16
F32 = jnp.float32
MEMORY = 60 * 2**20


def dot_nn(left, right):
    return lax.dot_general(left, right, (((1,), (0,)), ((), ())), preferred_element_type=F32)


def dot_nt(left, right):
    return lax.dot_general(left, right, (((1,), (1,)), ((), ())), preferred_element_type=F32)


def dot_tn(left, right):
    return lax.dot_general(left, right, (((0,), (0,)), ((), ())), preferred_element_type=F32)


def pieces(total, size=PIECE):
    return [pl.ds(start, size) for start in range(0, total, size)]


def three_parts(values):
    first = values.astype(LOW).astype(F32)
    rest = values - first
    second = rest.astype(LOW).astype(F32)
    return first, second, rest - second


CURVE = (
    7.97882253e-01,
    3.63445176e-02,
    -4.47304308e-05,
    -5.04138899e-05,
    3.10523303e-06,
    -6.66676088e-08,
)
BELL = -0.5 / 0.6931471805599453


def gelu_parts(u):
    square = u * u
    near = jnp.minimum(square, 31.36)
    curve = CURVE[-1]
    for factor in CURVE[-2::-1]:
        curve = curve * near + factor
    bent = jnp.tanh(u * curve)
    half = 0.5 * u
    slope = (0.5 + 0.5 * bent) + (u * 0.3989422804014327) * jnp.exp2(square * BELL)
    return half + half * bent, slope


def lane_facts():
    lane = lax.broadcasted_iota(jnp.int32, (1, PAIR), 1)
    return lane < HD, lane & (HD - 1)


def segments(lengths_ref, row, start, rows):
    places = lax.broadcasted_iota(jnp.int32, (rows, 1), 0) + start
    bound = jnp.int32(0)
    segment = jnp.zeros((rows, 1), jnp.int32)
    last = lengths_ref.shape[1] - 1
    for entry in range(last):
        bound = bound + lengths_ref[row, entry]
        segment = segment + (places >= bound).astype(jnp.int32)
    return segment, (segment == last).astype(F32), last


def attention_forward(row, lengths_ref, x, wq_ref, bias_ref, qa_ref, ka_ref, va_ref, ob_ref, s_ref, p_ref, m_ref, pad_ref, q_ref, aug_ref):
    width = HEADS * HD
    for block in range(3):
        at = block * width
        value = dot_nn(x, wq_ref[:, at : at + width]) + bias_ref[:, at : at + width]
        for pair in range(HEADS // 2):
            q_ref[block, pair] = value[:, pair * PAIR : (pair + 1) * PAIR]
    for start in range(0, SEQ, PIECE):
        place = pl.ds(start, PIECE)
        low_half, slot = lane_facts()
        segment, pad, last = segments(lengths_ref, row, start, PIECE)
        pad_ref[place] = jnp.broadcast_to(pad, (PIECE, PAIR))
        aug_q = jnp.where(slot == segment, 1.0, 0.0)
        aug_ref[place] = aug_q
        seen = (slot == segment) & (slot != last)
        aug_k = jnp.where(seen, 0.0, jnp.where(slot <= last, FAR, jnp.where(slot <= last + 3, 1.0, 0.0)))
        for pair in range(HEADS // 2):
            q = q_ref[0, pair, place] * HD**-0.5
            k = q_ref[1, pair, place]
            v = q_ref[2, pair, place]
            q_ref[0, pair, place] = q
            qa_ref[2 * pair, place] = jnp.where(low_half, q, aug_q).astype(LOW)
            qa_ref[2 * pair + 1, place] = jnp.where(low_half, aug_q, q).astype(LOW)
            ka_ref[2 * pair, place] = jnp.where(low_half, k, aug_k).astype(LOW)
            ka_ref[2 * pair + 1, place] = jnp.where(low_half, aug_k, k).astype(LOW)
            va_ref[2 * pair, place] = jnp.where(low_half, v, 1.0).astype(LOW)
            va_ref[2 * pair + 1, place] = jnp.where(low_half, 1.0, v).astype(LOW)

    def scores(head):
        s_ref[head % 2] = dot_nt(qa_ref[head], ka_ref[head])

    def softmax(head):
        for place in pieces(SEQ):
            highest = jnp.maximum(jnp.max(s_ref[head % 2, place], -1, keepdims=True), FLOOR)
            m_ref[head % 2, place] = jnp.broadcast_to(highest, (PIECE, PAIR))
            p_ref[head % 2, place] = jnp.exp(s_ref[head % 2, place] - highest).astype(LOW)

    scores(0)
    for head in range(HEADS):
        if head + 1 < HEADS:
            scores(head + 1)
        softmax(head)
        q_ref[1, head % 2] = dot_nn(p_ref[head % 2], va_ref[head])
        if head % 2:
            pair = head // 2
            for start in range(0, SEQ, PIECE):
                place = pl.ds(start, PIECE)
                low_half, slot = lane_facts()
                even = q_ref[1, 0, place]
                odd = q_ref[1, 1, place]
                pad = pad_ref[place]
                last = lengths_ref.shape[1] - 1
                total = jnp.where(low_half, odd, even) + pad
                top = jnp.where(low_half, odd_even(m_ref, 1, place), odd_even(m_ref, 0, place))
                spread = jnp.where(pad > 0, 0.0, top + jnp.log(total))
                first, second, third = three_parts(spread)
                aug = jnp.where(
                    slot == last + 1,
                    -first,
                    jnp.where(slot == last + 2, -second, jnp.where(slot == last + 3, -third, aug_ref[place])),
                )
                q = q_ref[0, pair, place]
                qa_ref[2 * pair, place] = jnp.where(low_half, q, aug).astype(LOW)
                qa_ref[2 * pair + 1, place] = jnp.where(low_half, aug, q).astype(LOW)
                v = q_ref[2, pair, place].astype(LOW).astype(F32)
                out = jnp.where(low_half, even, odd) / pltpu.roll(total, HD, 1) + pad * v
                ob_ref[place, pl.ds(pair * PAIR, PAIR)] = out.astype(LOW)


def odd_even(ref, which, place):
    return ref[which, place]


def normal(values):
    centred = values - jnp.mean(values, -1, keepdims=True)
    inverse = lax.rsqrt(jnp.mean(centred * centred, -1, keepdims=True) + EPSILON)
    return centred * inverse, inverse


def normal_back(cotangent, unit, inverse, gains):
    scaled = cotangent * gains
    return inverse * (
        scaled
        - jnp.mean(scaled, -1, keepdims=True)
        - unit * jnp.mean(scaled * unit, -1, keepdims=True)
    )


def dense_forward(x_ref, ob_ref, wo_ref, wi_ref, wf_ref, small_ref, bi_ref, n1_ref, n2_ref, inv_ref, yb_ref, gb_ref, gp_ref, z_ref, work_ref, u_ref):
    small = lambda index: small_ref[pl.ds(index, 1)]
    work_ref[...] = dot_nn(ob_ref[...], wo_ref[...])
    for place in pieces(SEQ):
        unit, inverse = normal(x_ref[place].astype(F32) + work_ref[place] + small(4))
        n1_ref[place] = unit
        inv_ref[place, pl.ds(0, HD)] = jnp.broadcast_to(inverse, (PIECE, HD))
        y = unit * small(2) + small(5)
        yb_ref[place] = y.astype(LOW)
        work_ref[place] = y + small(6)
    columns = 256
    count = wi_ref.shape[1] // columns

    def into(step):
        u_ref[step % 2] = dot_nn(yb_ref[...], wi_ref[:, pl.ds(step * columns, columns)])

    into(0)
    for step in range(count):
        if step + 1 < count:
            into(step + 1)
        lanes = pl.ds(step * columns, columns)
        for place in pieces(SEQ, SMALL):
            g, slope = gelu_parts(u_ref[step % 2, place] + bi_ref[:, lanes])
            gb_ref[place, lanes] = g.astype(LOW)
            gp_ref[place, lanes] = slope.astype(LOW)
    work_ref[...] += dot_nn(gb_ref[...], wf_ref[...])
    for place in pieces(SEQ):
        unit, inverse = normal(work_ref[place])
        n2_ref[place] = unit
        inv_ref[place, pl.ds(HD, HD)] = jnp.broadcast_to(inverse, (PIECE, HD))
        z_ref[place] = (unit * small(3) + small(7)).astype(z_ref.dtype)


def fold(values):
    return jnp.sum(values.reshape(-1, 8, values.shape[-1]), 0)


def dense_backward(dz_ref, n1_ref, n2_ref, inv_ref, yb_ref, gb_ref, gp_ref, ob_ref, wo_ref, wi_ref, wf_ref, small_ref, dr_ref, dob_ref, gwo_ref, gwi_ref, gwf_ref, gsmall_ref, gbi_ref, low_ref, u_ref, du_ref, turned_ref):
    small = lambda index: small_ref[pl.ds(index, 1)]
    for place in pieces(SEQ):
        dz = dz_ref[place].astype(F32)
        unit = n2_ref[place]
        gsmall_ref[3] += fold(dz * unit)
        gsmall_ref[7] += fold(dz)
        dr = normal_back(dz, unit, inv_ref[place, pl.ds(HD, 1)], small(3))
        dr_ref[place] = dr
        df = dr.astype(LOW)
        low_ref[place] = df
        gsmall_ref[6] += fold(df.astype(F32))
    columns = 256
    count = wi_ref.shape[1] // columns

    def back(step):
        u_ref[step % 2] = dot_nt(low_ref[...], wf_ref[pl.ds(step * columns, columns)])

    back(0)
    turned_ref[0] = low_ref[...].T
    turned_ref[1] = yb_ref[...].T
    for step in range(count):
        if step + 1 < count:
            back(step + 1)
        lanes = pl.ds(step * columns, columns)
        gwf_ref[:, lanes] += dot_nn(turned_ref[0], gb_ref[:, lanes])
        for place in pieces(SEQ, SMALL):
            du = (u_ref[step % 2, place] * gp_ref[place, lanes].astype(F32)).astype(LOW)
            du_ref[place, lanes] = du
            gbi_ref[:, lanes] += fold(du.astype(F32))
        gwi_ref[:, lanes] += dot_nn(turned_ref[1], du_ref[:, lanes])
    u_ref[0] = dot_nt(du_ref[...], wi_ref[...])
    for place in pieces(SEQ):
        dy = dr_ref[place] + u_ref[0, place]
        unit = n1_ref[place]
        gsmall_ref[2] += fold(dy * unit)
        gsmall_ref[5] += fold(dy)
        dr = normal_back(dy, unit, inv_ref[place, pl.ds(0, 1)], small(2))
        dr_ref[place] = dr
        da = dr.astype(LOW)
        low_ref[place] = da
        gsmall_ref[4] += fold(da.astype(F32))
    gwo_ref[...] += dot_tn(ob_ref[...], low_ref[...])
    dob_ref[...] = dot_nt(low_ref[...], wo_ref[...]).astype(LOW)


def attention_backward(row, lengths_ref, x, dob_ref, ob_ref, qa_ref, ka_ref, va_ref, wq_ref, dr_ref, dx_ref, gwq_ref, gbias_ref, da_ref, p_ref, ds_ref, s_ref, dqkv_ref, dq_ref, pad_ref, kt_ref, dqt_ref):
    width = HEADS * HD
    low_half, slot = lane_facts()
    for start in range(0, SEQ, PIECE):
        place = pl.ds(start, PIECE)
        segment, pad, last = segments(lengths_ref, row, start, PIECE)
        pad_ref[place] = jnp.broadcast_to(pad, (PIECE, PAIR))
        for pair in range(HEADS // 2):
            lanes = pl.ds(pair * PAIR, PAIR)
            dob = dob_ref[place, lanes].astype(F32)
            product = dob * ob_ref[place, lanes].astype(F32)
            even = jnp.sum(jnp.where(low_half, product, 0.0), -1, keepdims=True)
            odd = jnp.sum(jnp.where(low_half, 0.0, product), -1, keepdims=True)
            first, second, third = three_parts(jnp.where(low_half, odd, even))
            aug = jnp.where(
                slot == 0, -first, jnp.where(slot == 1, -second, jnp.where(slot == 2, -third, 0.0))
            )
            da_ref[2 * pair, place] = jnp.where(low_half, dob, aug).astype(LOW)
            da_ref[2 * pair + 1, place] = jnp.where(low_half, aug, dob).astype(LOW)
    for pair in range(HEADS // 2):
        low_half, unused = lane_facts()
        keys = jnp.where(low_half, ka_ref[2 * pair].astype(F32), ka_ref[2 * pair + 1].astype(F32))
        kt_ref[pl.ds(pair * PAIR, PAIR)] = keys.T.astype(LOW)
    low_half, slot = lane_facts()

    def scores(head):
        s_ref[0, head % 2] = dot_nt(ka_ref[head], qa_ref[head])
        s_ref[1, head % 2] = dot_nt(va_ref[head], da_ref[head])

    def weigh(head):
        for place in pieces(SEQ, SMALL):
            p = jnp.exp(s_ref[0, head % 2, place])
            p_ref[head % 2, place] = p.astype(LOW)
            ds_ref[head % 2, place] = (p * s_ref[1, head % 2, place]).astype(LOW)

    scores(0)
    for head in range(HEADS):
        if head + 1 < HEADS:
            scores(head + 1)
        weigh(head)
        side = head % 2
        dq_ref[1, side] = dot_nn(ds_ref[head % 2], qa_ref[head])
        dq_ref[2, side] = dot_nn(p_ref[head % 2], da_ref[head])
        dqt_ref[pl.ds(side * HD, HD)] = dot_nn(kt_ref[pl.ds(head * HD, HD)], ds_ref[head % 2])
        if side:
            pair = head // 2
            dq_ref[0, 0] = dqt_ref[...].T
            for start in range(0, SEQ, PIECE):
                place = pl.ds(start, PIECE)
                dq = dq_ref[0, 0, place] * HD**-0.5
                dk = jnp.where(low_half, dq_ref[1, 0, place], dq_ref[1, 1, place])
                dv = jnp.where(low_half, dq_ref[2, 0, place], dq_ref[2, 1, place])
                dv = dv + pad_ref[place] * dob_ref[place, pl.ds(pair * PAIR, PAIR)].astype(F32)
                for block, value in enumerate((dq, dk, dv)):
                    lanes = pl.ds(block * width + pair * PAIR, PAIR)
                    value = value.astype(LOW)
                    dqkv_ref[place, lanes] = value
                    if block != 1:
                        into = pl.ds(pair * PAIR, PAIR)
                        gbias_ref[block // 2, :, into] += fold(value.astype(F32))
    gwq_ref[...] += dot_tn(x, dqkv_ref[...])
    dx_ref[...] = (dr_ref[...] + dot_nt(dqkv_ref[...], wq_ref[...])).astype(dx_ref.dtype)


def unpack_matrix(raw_ref, at, into_ref):
    width = into_ref.shape[0]
    for start in range(0, into_ref.shape[1], width):
        block = raw_ref[:, :, pl.ds(at + start, width)].astype(F32)
        block = block.reshape(GROUPS + (width,)).swapaxes(0, 1).reshape(width, width)
        into_ref[:, pl.ds(start, width)] = block.astype(LOW)


def unpack_stacked(raw_ref, at, into_ref):
    width = into_ref.shape[1]
    count = into_ref.shape[0] // width
    blocks = [
        raw_ref[:, :, pl.ds(at + step * width, width)].astype(F32).reshape(GROUPS + (width,))
        for step in range(count)
    ]
    outer, inner, rows = GROUPS
    for place in range(inner):
        part = jnp.stack([jnp.stack([block[f, place] for block in blocks]) for f in range(outer)])
        size = outer * count * rows
        into_ref[pl.ds(place * size, size)] = part.reshape(size, width).astype(LOW)


def counter(shape, axis):
    return lax.broadcasted_iota(jnp.int32, shape, axis)


def split_by(values, size):
    return lax.shift_right_logical(values, size.bit_length() - 1), values & (size - 1)


def sources(rows):
    outer, inner, height = GROUPS
    group, within = split_by(counter((rows, 1), 0), height)
    far, near = split_by(group, inner)
    return near * outer + far, within


def unpack_vectors(raw_ref, at, layer):
    outer, inner, rows = GROUPS
    total = outer * inner * rows
    raw = raw_ref[:, :, pl.ds(at, 128)].reshape(total, 128)
    owner, place = split_by(counter((1, total), 1), rows)
    pick = jnp.where(counter((128, 1), 0) == rows * layer + place, 1.0, 0.0).astype(LOW)
    device, unused = sources(total)
    spread = jnp.where(owner == device, dot_nn(raw, pick), 0.0)
    return jnp.sum(spread.reshape(outer * inner, rows, total), 0)


def unpack_hidden(raw_ref, at, layer, hidden):
    outer, inner, rows = GROUPS
    total = outer * inner * rows
    raw = raw_ref[:, :, pl.ds(at, 128)].reshape(total, 128)
    owner, place = split_by(counter((1, hidden), 1), hidden // (outer * inner))
    pick = jnp.where(counter((128, 1), 0) == 2 * rows + place, 1.0, 0.0).astype(LOW)
    device, within = sources(total)
    device = jnp.where(within == layer, device, -1)
    spread = jnp.where(owner == device, dot_nn(raw, pick), 0.0)
    return jnp.sum(spread, 0, keepdims=True)


def pack_matrix(sum_ref, sent_ref, at):
    width = sum_ref.shape[0]
    outer, inner, rows = GROUPS
    for start in range(0, sum_ref.shape[1], width):
        block = sum_ref[:, pl.ds(start, width)].reshape(inner, outer, rows, width)
        block = block.swapaxes(0, 1).reshape(outer, inner * rows, width)
        sent_ref[:, :, pl.ds(at + start, width)] = block.astype(LOW)


def pack_stacked(sum_ref, sent_ref, at):
    width = sum_ref.shape[0]
    outer, inner, rows = GROUPS
    count = sum_ref.shape[1] // width
    near = inner // count
    for step in range(count):
        block = sum_ref[:, pl.ds(step * width, width)].T
        block = block.reshape(near, outer, count, rows, width)
        for part in range(count):
            piece = jnp.stack([block[:, f, part] for f in range(outer)])
            piece = piece.reshape(outer, near * rows, width)
            sent_ref[:, pl.ds(step * near * rows, near * rows), pl.ds(at + part * width, width)] = (
                piece.astype(LOW)
            )


def pack_shared(block, sent_ref, at):
    outer, inner, rows = GROUPS
    columns = block.shape[1]
    block = jnp.broadcast_to(block[None], (outer * inner, rows, columns))
    sent_ref[:, :, pl.ds(at, columns)] = block.reshape(outer, inner * rows, columns).astype(LOW)


def pack_attention(gwq_ref, gbias_ref, sent_ref, at):
    pack_matrix(gwq_ref, sent_ref, at)
    width = gwq_ref.shape[0]
    line = lax.broadcasted_iota(jnp.int32, (8, width), 0)
    sums = [jnp.sum(gbias_ref[index], 0, keepdims=True) for index in range(2)]
    block = jnp.where(line == 0, sums[0], jnp.where(line == 1, sums[1], 0.0))
    pack_shared(block, sent_ref, at + 3 * width)


def pack_dense(gwo_ref, gwi_ref, gwf_ref, gsmall_ref, gbi_ref, sent_ref, at):
    width, hidden = gwi_ref.shape
    pack_matrix(gwo_ref, sent_ref, at)
    pack_matrix(gwi_ref, sent_ref, at + width)
    pack_stacked(gwf_ref, sent_ref, at + width + hidden)
    at = at + width + 2 * hidden
    pack_shared(jnp.sum(gsmall_ref[...], 1), sent_ref, at)
    line = jnp.sum(gbi_ref[...], 0, keepdims=True)
    size = hidden // 8
    block = jnp.concatenate([line[:, step * size : (step + 1) * size] for step in range(8)], 0)
    pack_shared(block, sent_ref, at + width)


def shape_of(array):
    return jax.ShapeDtypeStruct(array.shape, array.dtype)


def by_row(shape):
    if len(shape) == 2:
        return pl.BlockSpec((SEQ, shape[1]), lambda row: (row, 0))
    return pl.BlockSpec((None,) + tuple(shape[1:]), lambda row: (row,) + (0,) * (len(shape) - 1))


def whole(shape):
    return pl.BlockSpec(tuple(shape), lambda row: (0,) * len(shape))


def run_rows(
    body, lengths, rowwise, fixed, row_outs, sent, scratch, cost, setup, finish, after=(), scalars=()
):
    count = lengths.shape[0]
    cuts = [len(scalars), len(rowwise), len(fixed), len(after), len(row_outs), len(sent), len(scratch)]

    def kernel(lengths_ref, *refs):
        row = pl.program_id(0)
        groups = []
        at = 0
        for cut in cuts:
            groups.append(refs[at : at + cut])
            at += cut
        numbers, rows_in, fixed_in, unused, rows_out, sent_out, work = groups

        @pl.when(row == 0)
        def _():
            setup(numbers, fixed_in, sent_out, work)

        body(row, lengths_ref, rows_in, rows_out, work)

        if finish:

            @pl.when(row == count - 1)
            def _():
                finish(numbers, work, sent_out)

    return pl.pallas_call(
        kernel,
        grid=(count,),
        in_specs=[pl.BlockSpec(memory_space=pltpu.SMEM)] * (1 + len(scalars))
        + [by_row(array.shape) for array in rowwise]
        + [whole(array.shape) for array in fixed]
        + [pl.BlockSpec(memory_space=pl.ANY) for array in after],
        out_specs=[by_row(part.shape) for part in row_outs] + [whole(part.shape) for part in sent],
        out_shape=list(row_outs) + list(sent),
        scratch_shapes=list(scratch),
        compiler_params=pltpu.CompilerParams(
            dimension_semantics=("arbitrary",), vmem_limit_bytes=MEMORY
        ),
        cost_estimate=pl.CostEstimate(flops=cost, bytes_accessed=8 * 2**20, transcendentals=0),
    )(lengths, *scalars, *rowwise, *fixed, *after)


def struct(shape, dtype):
    return jax.ShapeDtypeStruct(tuple(shape), dtype)


FORWARD_SCRATCH = lambda: [
    pltpu.VMEM((2, SEQ, SEQ), F32),
    pltpu.VMEM((2, SEQ, SEQ), LOW),
    pltpu.VMEM((2, SEQ, PAIR), F32),
    pltpu.VMEM((SEQ, PAIR), F32),
    pltpu.VMEM((3, HEADS // 2, SEQ, PAIR), F32),
    pltpu.VMEM((SEQ, PAIR), F32),
]
BACKWARD_SCRATCH = lambda: [
    pltpu.VMEM((HEADS, SEQ, PAIR), LOW),
    pltpu.VMEM((2, SEQ, SEQ), LOW),
    pltpu.VMEM((2, SEQ, SEQ), LOW),
    pltpu.VMEM((2, 2, SEQ, SEQ), F32),
    pltpu.VMEM((SEQ, 3 * HEADS * HD), LOW),
    pltpu.VMEM((3, 2, SEQ, PAIR), F32),
    pltpu.VMEM((SEQ, PAIR), F32),
    pltpu.VMEM((HEADS * HD, SEQ), LOW),
    pltpu.VMEM((PAIR, SEQ), F32),
]


def attention_outs(rows, tokens, width):
    heads = (rows, HEADS, SEQ, PAIR)
    return [struct(heads, LOW)] * 3 + [struct((tokens, width), LOW)]


def dense_outs(tokens, width, hidden):
    return [
        struct((tokens, width), F32),
        struct((tokens, width), F32),
        struct((tokens, PAIR), F32),
        struct((tokens, width), LOW),
        struct((tokens, hidden), LOW),
        struct((tokens, hidden), LOW),
    ]


def vmem(shape, dtype):
    return pltpu.VMEM(tuple(shape), dtype)


def attention_weights(width):
    return [vmem((width, 3 * width), LOW), vmem((1, 3 * width), F32)]


def dense_weights(width, hidden):
    return [
        vmem((width, width), LOW),
        vmem((width, hidden), LOW),
        vmem((hidden, width), LOW),
        vmem((8, width), F32),
        vmem((1, hidden), F32),
    ]


def dense_sums(width, hidden):
    return [
        vmem((width, width), F32),
        vmem((width, hidden), F32),
        vmem((width, hidden), F32),
        vmem((8, 8, width), F32),
        vmem((8, hidden), F32),
    ]


def attention_sums(width):
    return [vmem((width, 3 * width), F32), vmem((2, 8, width), F32)]


def dense_work(width, hidden):
    return [
        vmem((SEQ, width), LOW),
        vmem((2, SEQ, width), F32),
        vmem((SEQ, hidden), LOW),
        vmem((2, width, SEQ), LOW),
    ]


def set_attention(layer, urgent_ref, raw_ref, at, wq_ref, bias_ref):
    width = wq_ref.shape[0]
    unpack_matrix(raw_ref, at, wq_ref)
    vectors = unpack_vectors(urgent_ref, 3 * width, layer)
    bias_ref[:, :width] = vectors[0:1]
    bias_ref[:, width : 2 * width] = jnp.zeros((1, width), F32)
    bias_ref[:, 2 * width :] = vectors[1:2]


def set_dense(layer, urgent_ref, raw_ref, at, wo_ref, wi_ref, wf_ref, small_ref, bi_ref):
    width, hidden = wi_ref.shape
    unpack_matrix(raw_ref, at, wo_ref)
    unpack_matrix(raw_ref, at + width, wi_ref)
    unpack_stacked(raw_ref, at + width + hidden, wf_ref)
    small_ref[...] = unpack_vectors(urgent_ref, 3 * width, layer)
    bi_ref[...] = unpack_hidden(urgent_ref, 3 * width, layer, hidden)


def clear(refs):
    for ref in refs:
        ref[...] = jnp.zeros(ref.shape, ref.dtype)


def first_kernel(lengths, x, place, parts):
    rows, (tokens, width) = lengths.shape[0], x.shape

    def setup(numbers, fixed, sent, work):
        for step, part in enumerate(fixed):
            sent[0][numbers[0][0] ^ step] = part[...]
        set_attention(0, sent[0], sent[0], 0, *work[:2])

    def body(row, lengths_ref, rowwise, outs, work):
        attention_forward(row, lengths_ref, rowwise[0][...], *work[:2], *outs, *work[2:])

    return run_rows(
        body, lengths, [x], list(parts), attention_outs(rows, tokens, width),
        [struct((len(parts),) + parts[0].shape, LOW)],
        attention_weights(width) + FORWARD_SCRATCH(), 4 * 10**9, setup, None, (), [place],
    )


def attention_kernel(layer, lengths, x, urgent, raw, at):
    rows, (tokens, width) = lengths.shape[0], x.shape

    def setup(numbers, fixed, sent, work):
        set_attention(layer, *fixed, at, *work[:2])

    def body(row, lengths_ref, rowwise, outs, work):
        attention_forward(row, lengths_ref, rowwise[0][...].astype(LOW), *work[:2], *outs, *work[2:])

    return run_rows(
        body, lengths, [x], [urgent, raw], attention_outs(rows, tokens, width), [],
        attention_weights(width) + FORWARD_SCRATCH(), 4 * 10**9, setup, None,
    )


def dense_kernel(layer, lengths, x, ob, urgent, raw, at, hidden, after):
    tokens, width = x.shape

    def setup(numbers, fixed, sent, work):
        set_dense(layer, *fixed, at, *work[:5])

    def body(row, lengths_ref, rowwise, outs, work):
        dense_forward(*rowwise, *work[:5], *outs, *work[5:])

    return run_rows(
        body, lengths, [x, ob], [urgent, raw],
        dense_outs(tokens, width, hidden) + [struct((tokens, width), F32)], [],
        dense_weights(width, hidden) + [vmem((SEQ, width), F32), vmem((2, SEQ, width), F32)],
        5 * 10**9, setup, None, after,
    )


def turn_kernel(layer, lengths, x, ob, cotangent, urgent, raw, at, hidden):
    tokens, width = x.shape
    columns = width + 2 * hidden + width + hidden // 8

    def setup(numbers, fixed, sent, work):
        set_dense(layer, *fixed, at, *work[:5])
        clear(work[5:10])

    def body(row, lengths_ref, rowwise, outs, work):
        x_ref, ob_ref, dz_ref = rowwise
        z_ref, dr_ref, dob_ref = outs
        weights, sums, kept = work[:5], work[5:10], work[10:16]
        work_ref, low_ref, u_ref, du_ref, turned_ref = work[16:]
        dense_forward(x_ref, ob_ref, *weights, *kept, z_ref, work_ref, u_ref)
        dense_backward(
            dz_ref, *kept, ob_ref, *weights[:4], dr_ref, dob_ref, *sums, low_ref, u_ref, du_ref,
            turned_ref,
        )

    def finish(numbers, work, sent):
        pack_dense(*work[5:10], sent[0], 0)

    kept = [vmem((SEQ,) + part.shape[1:], part.dtype) for part in dense_outs(tokens, width, hidden)]
    return run_rows(
        body, lengths, [x, ob, cotangent], [urgent, raw],
        [struct((tokens, width), LOW), struct((tokens, width), F32), struct((tokens, width), LOW)],
        [struct((4, 64, columns), LOW)],
        dense_weights(width, hidden) + dense_sums(width, hidden) + kept
        + [vmem((SEQ, width), F32)] + dense_work(width, hidden),
        10**10, setup, finish,
    )


def hand_out(place_ref, packed_ref, sent):
    for step, ref in enumerate(sent):
        ref[...] = packed_ref[place_ref[0] ^ step]


def middle_kernel(lengths, upper, lower, urgent, raw1, raw0, hidden, after, place):
    tokens, width = upper[0].shape
    columns = 4 * width + width + 2 * hidden + width + hidden // 8

    def setup(numbers, fixed, sent, work):
        urgent_ref, raw1_ref, raw0_ref = fixed
        set_attention(1, urgent_ref, raw1_ref, 0, *work[:2])
        set_dense(0, urgent_ref, raw0_ref, 0, *work[2:7])
        clear(work[7:14])

    def body(row, lengths_ref, rowwise, outs, work):
        up, low = rowwise[:7], rowwise[7:]
        dx_ref = work[15]
        attention_backward(
            row, lengths_ref, up[0][...].astype(LOW), *up[1:6], work[0], up[6], dx_ref,
            *work[7:9], *work[20:],
        )
        dense_backward(dx_ref, *low, *work[2:6], *outs, *work[9:14], *work[16:20])

    def finish(numbers, work, sent):
        pack_attention(*work[7:9], work[14], 0)
        pack_dense(*work[9:14], work[14], 4 * width)
        hand_out(numbers[0], work[14], sent)

    return run_rows(
        body, lengths, list(upper) + list(lower), [urgent, raw1, raw0],
        [struct((tokens, width), F32), struct((tokens, width), LOW)],
        [struct((64, columns), LOW)] * 4,
        attention_weights(width) + dense_weights(width, hidden)
        + attention_sums(width) + dense_sums(width, hidden)
        + [vmem((4, 64, columns), LOW), vmem((SEQ, width), F32)]
        + dense_work(width, hidden) + BACKWARD_SCRATCH(),
        15 * 10**9, setup, finish, after, [place],
    )


def last_kernel(lengths, upper, urgent, after, place):
    tokens, width = upper[0].shape

    def setup(numbers, fixed, sent, work):
        set_attention(0, fixed[0], fixed[0], 0, *work[:2])
        clear(work[2:4])

    def body(row, lengths_ref, rowwise, outs, work):
        attention_backward(
            row, lengths_ref, rowwise[0][...], *rowwise[1:6], work[0], rowwise[6], outs[0],
            *work[2:4], *work[5:],
        )

    def finish(numbers, work, sent):
        pack_attention(*work[2:4], work[4], 0)
        hand_out(numbers[0], work[4], sent)

    return run_rows(
        body, lengths, list(upper), [urgent], [struct((tokens, width), LOW)],
        [struct((64, 4 * width), LOW)] * 4,
        attention_weights(width) + attention_sums(width)
        + [vmem((4, 64, 4 * width), LOW)] + BACKWARD_SCRATCH(),
        8 * 10**9, setup, finish, after, [place],
    )


def hold(array, after):
    def kernel(*refs):
        pass

    anywhere = pl.BlockSpec(memory_space=pl.ANY)
    return pl.pallas_call(
        kernel,
        in_specs=[anywhere] * (1 + len(after)),
        out_specs=anywhere,
        out_shape=shape_of(array),
        input_output_aliases={0: 0},
    )(array, *after)


def pack_parameters(
    attn_weight, attn_bias, out_weight, ffn_in, ffn_in_bias, ffn_out, norm_gain, shifts
):
    depth, rows, width = out_weight.shape
    copies = GROUPS[1]
    hidden = ffn_in.shape[2]
    early = 4 * width + 2 * hidden + 128
    columns = 4 * width + 2 * hidden
    height = ffn_in_bias.shape[1]

    def kernel(wq_ref, ab_ref, wo_ref, wi_ref, bi_ref, wf_ref, gain_ref, shift_ref, first_ref, rest_ref, small_ref):
        def put(ref, block, at):
            block = jnp.broadcast_to(block.astype(F32)[None], (copies,) + block.shape)
            block = block.reshape(copies * block.shape[1], block.shape[2])
            ref[:, pl.ds(at, block.shape[1])] = block.astype(LOW)

        small_ref[...] = jnp.zeros(small_ref.shape, F32)
        for layer in range(depth):
            lanes = pl.ds(rows * layer, rows)
            small_ref[0:2, lanes] = ab_ref[layer].astype(F32)
            small_ref[2:4, lanes] = gain_ref[layer].astype(F32)
            small_ref[4:8, lanes] = shift_ref[layer].astype(F32)
        small_ref[0:depth, pl.ds(2 * rows, height)] = bi_ref[...].astype(F32)
        put(first_ref, wq_ref[0], 0)
        put(first_ref, small_ref[...], 3 * width)
        for layer, ref, at in ((0, first_ref, 3 * width + 128), (1, rest_ref, 3 * width)):
            if layer:
                put(ref, wq_ref[layer], 0)
            put(ref, wo_ref[layer], at)
            put(ref, wi_ref[layer], at + width)
            at += width + hidden
            down = wf_ref[layer].astype(F32)
            for step in range(hidden // width):
                put(ref, down[step * rows : (step + 1) * rows], at)
                at += width

    return pl.pallas_call(
        kernel,
        in_specs=[pl.BlockSpec(memory_space=pltpu.VMEM)] * 8,
        out_shape=[struct((copies * rows, early), LOW), struct((copies * rows, columns), LOW)],
        scratch_shapes=[vmem((rows, 128), F32)],
        compiler_params=pltpu.CompilerParams(vmem_limit_bytes=MEMORY),
    )(attn_weight, attn_bias, out_weight, ffn_in, ffn_in_bias, ffn_out, norm_gain, shifts)


def add_parts(parts, after=(), joined=None):
    inner = [] if joined is None else [joined]
    ahead = 0 if joined is None else joined.shape[1]
    rows, lanes_in = parts[0].shape
    count = len(parts)

    def kernel(*refs):
        out_ref = refs[-1]
        if inner:
            out_ref[:, pl.ds(0, ahead)] = refs[count][...]
        columns = 256
        for start in range(0, lanes_in, columns):
            size = min(columns, lanes_in - start)
            total = refs[0][:, pl.ds(start, size)].astype(F32)
            for ref in refs[1:count]:
                total = total + ref[:, pl.ds(start, size)].astype(F32)
            out_ref[:, pl.ds(ahead + start, size)] = total.astype(LOW)

    near = pl.BlockSpec(memory_space=pltpu.VMEM)
    return pl.pallas_call(
        kernel,
        in_specs=[near] * (count + len(inner)) + [pl.BlockSpec(memory_space=pl.ANY)] * len(after),
        out_specs=near,
        out_shape=struct((rows, ahead + lanes_in), LOW),
        compiler_params=pltpu.CompilerParams(vmem_limit_bytes=MEMORY),
    )(*parts, *inner, *after)


def write_gradients(place, tail, front, depth, width, hidden):
    rows = GROUPS[2]
    last = front.shape[1] - 4 * width
    height = hidden // DEVICES

    def kernel(place_ref, tail_ref, front_ref, gwq_ref, gab_ref, gwo_ref, gwi_ref, gbi_ref, gwf_ref, gain_ref, shift_ref):
        spot = place_ref[0]

        def total(ref, at, columns):
            block = ref[:, pl.ds(at, columns)].astype(F32)
            return jnp.sum(block.reshape(-1, rows, columns), 0)

        def own(block, size):
            return pltpu.roll(block, block.shape[1] - spot * size, 1)

        for layer, ref, at in ((0, front_ref, last), (1, front_ref, 0)):
            gwq_ref[layer] = total(ref, at, 3 * width)
            gab_ref[layer] = own(total(ref, at + 3 * width, width), rows)[0:2, 0:rows]
        for layer, ref, at in ((0, front_ref, 4 * width), (1, tail_ref, 0)):
            gwo_ref[layer] = total(ref, at, width)
            gwi_ref[layer] = total(ref, at + width, hidden)
            for step in range(hidden // width):
                gwf_ref[layer, pl.ds(step * rows, rows)] = total(
                    ref, at + width + hidden + step * width, width
                )
            at += width + 2 * hidden
            small = own(total(ref, at, width), rows)
            gain_ref[layer] = small[2:4, 0:rows]
            shift_ref[layer] = small[4:8, 0:rows]
            line = total(ref, at + width, hidden // 8)
            line = jnp.concatenate([line[step : step + 1] for step in range(8)], 1)
            gbi_ref[pl.ds(layer, 1)] = own(line, height)[:, 0:height]

    outs = [
        struct((depth, rows, 3 * width), F32),
        struct((depth, 2, rows), F32),
        struct((depth, rows, width), F32),
        struct((depth, rows, hidden), F32),
        struct((depth, height), F32),
        struct((depth, height, width), F32),
        struct((depth, 2, rows), F32),
        struct((depth, 4, rows), F32),
    ]
    return pl.pallas_call(
        kernel,
        in_specs=[pl.BlockSpec(memory_space=pltpu.SMEM)] + [pl.BlockSpec(memory_space=pltpu.VMEM)] * 2,
        out_shape=outs,
        compiler_params=pltpu.CompilerParams(vmem_limit_bytes=MEMORY),
    )(place, tail, front)


def exchange(parts, axis):
    return lax.all_to_all(parts, axis, 0, 0, tiled=True)


def swap(part, axis, step):
    size = lax.axis_size(axis)
    return lax.ppermute(part, axis, [(source, source ^ step) for source in range(size)])


def local(
    hidden_in,
    lengths,
    grad_out,
    attn_weight,
    attn_bias,
    out_weight,
    ffn_in,
    ffn_in_bias,
    ffn_out,
    norm_gain,
    shifts,
):
    depth, rows, width = out_weight.shape
    hidden = ffn_in.shape[2]
    first, second = lax.axis_size("dp"), lax.axis_size("fsdp")
    fits = (second, first, rows) == GROUPS
    urgent_size = 3 * width + 128
    if fits:
        early, later = pack_parameters(
            attn_weight, attn_bias, out_weight, ffn_in, ffn_in_bias, ffn_out, norm_gain, shifts
        )
        early = exchange(early, "dp")
        urgent = early[:, :urgent_size]
        parts = [urgent] + [swap(urgent, "fsdp", step) for step in range(1, second)]
        raw0 = lax.all_gather(early[:, urgent_size:], "fsdp")
        later = exchange(hold(later, (early,)), "dp")
        raw1 = lax.all_gather(hold(later, tuple(parts[1:])), "fsdp")
        place = lax.axis_index("fsdp").astype(jnp.int32).reshape(1)
    else:
        urgent, raw0, raw1 = gather_other(
            attn_weight, attn_bias, out_weight, ffn_in, ffn_in_bias, ffn_out, norm_gain, shifts
        )
        parts = [urgent[step] for step in range(urgent.shape[0])]
        place = jnp.zeros((1,), jnp.int32)

    qa0, ka0, va0, ob0, urgent = first_kernel(lengths, hidden_in, place, parts)
    n1, n2, inv, yb, gb, gp, z0 = dense_kernel(
        0, lengths, hidden_in, ob0, urgent, raw0, 0, hidden, ()
    )
    qa1, ka1, va1, ob1 = attention_kernel(1, lengths, z0, urgent, raw1, 0)
    hidden_out, dr1, dob1, sent_a = turn_kernel(
        1, lengths, z0, ob1, grad_out, urgent, raw1, 3 * width, hidden
    )
    if fits:
        tail = lax.psum_scatter(sent_a, "fsdp", scatter_dimension=0)
    dr0, dob0, *sent_b = middle_kernel(
        lengths,
        (z0, dob1, ob1, qa1, ka1, va1, dr1),
        (n1, n2, inv, yb, gb, gp, ob0),
        urgent,
        raw1,
        raw0,
        hidden,
        (sent_a,),
        place,
    )
    if fits:
        tail = exchange(hold(tail, (sent_b[0],)), "dp")
    grad_in, *sent_c = last_kernel(
        lengths, (hidden_in, dob0, ob0, qa0, ka0, va0, dr0), urgent, (sent_b[0],), place
    )
    if fits:
        got_b = [sent_b[0]] + [swap(sent_b[step], "fsdp", step) for step in range(1, second)]
        got_c = [sent_c[0]] + [swap(sent_c[step], "fsdp", step) for step in range(1, second)]
        front = add_parts(got_b, (tail,))
        front = add_parts(got_c, (), front)
        front = exchange(front, "dp")
        place = lax.axis_index(("dp", "fsdp")).astype(jnp.int32).reshape(1)
        grads = write_gradients(place, tail, front, depth, width, hidden)
    else:
        grads = scatter_other(sent_a, jnp.stack(sent_b), jnp.stack(sent_c), rows, width, hidden)
    return (hidden_out, grad_in, *grads)


def gather_other(
    attn_weight, attn_bias, out_weight, ffn_in, ffn_in_bias, ffn_out, norm_gain, shifts
):
    axes = ("dp", "fsdp")
    gather = lambda part, axis: lax.all_gather(part, axes, axis=axis, tiled=True)
    depth, unused, width = out_weight.shape
    hidden = ffn_in.shape[2]
    outer, inner, rows = GROUPS
    vectors = gather(jnp.concatenate([attn_bias, norm_gain, shifts], 1), 2)
    line = gather(ffn_in_bias, 1)

    def order(natural):
        return (
            natural.reshape(inner, outer, rows, -1).swapaxes(0, 1).reshape(outer, inner * rows, -1)
        )

    def stacked(part):
        part = part.reshape(DEVICES, -1, rows, width)
        return order(part.swapaxes(1, 2).reshape(width, -1))

    small = vectors.reshape(depth, 8, DEVICES, rows).transpose(2, 1, 0, 3).reshape(width, -1)
    line = line.reshape(depth, DEVICES, -1).swapaxes(0, 1)
    line = jnp.pad(line, ((0, 0), (0, 8 - depth), (0, 0))).reshape(width, -1)
    small = jnp.concatenate([small, line], 1)
    small = jnp.pad(small, ((0, 0), (0, 128 - small.shape[1])))
    wq, wo, wi, wf = (gather(part, 1) for part in (attn_weight, out_weight, ffn_in, ffn_out))
    urgent = jnp.concatenate([order(wq[0]), order(small)], 2)
    raw0 = jnp.concatenate([order(wo[0]), order(wi[0]), stacked(wf[0])], 2)
    raw1 = jnp.concatenate([order(wq[1]), order(wo[1]), order(wi[1]), stacked(wf[1])], 2)
    return urgent, raw0, raw1


def scatter_other(sent_a, sent_b, sent_c, own_rows, width, hidden):
    outer, inner, rows = GROUPS
    axes = ("dp", "fsdp")

    def natural(part):
        return part.reshape(outer, inner, rows, -1).swapaxes(0, 1).reshape(width, -1).astype(F32)

    def cut(part, sizes):
        found, at = [], 0
        for size in sizes:
            found.append(part[:, at : at + size])
            at += size
        return found

    dense = [width, hidden, hidden, width, hidden // 8]
    attention = [3 * width, width]
    wq0, ab0 = cut(natural(sent_c), attention)
    wq1, ab1, wo0, wi0, wf0, small0, bi0 = cut(natural(sent_b), attention + dense)
    wo1, wi1, wf1, small1, bi1 = cut(natural(sent_a), dense)

    def stacked(part):
        part = part.reshape(DEVICES, rows, -1, width).swapaxes(1, 2)
        return part.reshape(hidden, width)

    def spread(parts, axis):
        return lax.psum_scatter(jnp.stack(parts), axes, scatter_dimension=axis, tiled=True)

    return (
        spread([wq0, wq1], 1),
        spread([ab0[:2], ab1[:2]], 2),
        spread([wo0, wo1], 1),
        spread([wi0, wi1], 1),
        spread([bi0[:8].reshape(-1), bi1[:8].reshape(-1)], 1),
        spread([stacked(wf0), stacked(wf1)], 1),
        spread([small0[2:4], small1[2:4]], 2),
        spread([small0[4:8], small1[4:8]], 2),
    )


def solution(mesh):
    placed = (
        P(("dp", "fsdp"), None),
        P(("dp", "fsdp"), None),
        P(("dp", "fsdp"), None),
        P(None, ("dp", "fsdp"), None),
        P(None, None, ("dp", "fsdp")),
        P(None, ("dp", "fsdp"), None),
        P(None, ("dp", "fsdp"), None),
        P(None, ("dp", "fsdp")),
        P(None, ("dp", "fsdp"), None),
        P(None, None, ("dp", "fsdp")),
        P(None, None, ("dp", "fsdp")),
    )
    return jax.shard_map(
        local,
        mesh=mesh,
        in_specs=placed,
        out_specs=(
            P(("dp", "fsdp"), None),
            P(("dp", "fsdp"), None),
            P(None, ("dp", "fsdp"), None),
            P(None, None, ("dp", "fsdp")),
            P(None, ("dp", "fsdp"), None),
            P(None, ("dp", "fsdp"), None),
            P(None, ("dp", "fsdp")),
            P(None, ("dp", "fsdp"), None),
            P(None, None, ("dp", "fsdp")),
            P(None, None, ("dp", "fsdp")),
        ),
        check_vma=False,
    )
```

```python
from functools import partial

import jax
import jax.numpy as jnp
from jax import lax
from jax.experimental import pallas as pl
from jax.experimental.pallas import tpu as pltpu
from jax.sharding import PartitionSpec as P

HEADS = 4
HD = 64
SEQ = 512
PAIR = 2 * HD
FAR = -(2.0**100)
FLOOR = -1e20
EPSILON = 1e-12
PIECE = 256
SMALL = 128
GROUPS = (4, 8, 8)
DEVICES = 32
LOW = jnp.bfloat16
F32 = jnp.float32
MEMORY = 60 * 2**20


def dot_nn(left, right):
    return lax.dot_general(left, right, (((1,), (0,)), ((), ())), preferred_element_type=F32)


def dot_nt(left, right):
    return lax.dot_general(left, right, (((1,), (1,)), ((), ())), preferred_element_type=F32)


def dot_tn(left, right):
    return lax.dot_general(left, right, (((0,), (0,)), ((), ())), preferred_element_type=F32)


def pieces(total, size=PIECE):
    return [pl.ds(start, size) for start in range(0, total, size)]


def three_parts(values):
    first = values.astype(LOW).astype(F32)
    rest = values - first
    second = rest.astype(LOW).astype(F32)
    return first, second, rest - second


TAIL = (
    0.499999743,
    -0.398922625,
    0.249752332,
    -0.131772994,
    0.0594969557,
    -0.0222310142,
    0.00638287518,
    -0.00127118264,
    0.000151945115,
    -8.06328087e-06,
)
LOG2E = 1.4426950408889634


def gelu_parts(u):
    bell = jnp.exp2(u * u * (-0.5 * LOG2E))
    size = jnp.minimum(jnp.abs(u), 5.7)
    curve = TAIL[-1]
    for factor in TAIL[-2::-1]:
        curve = curve * size + factor
    tail = curve * bell
    cumulative = jnp.where(u > 0, 1.0 - tail, tail)
    return u * cumulative, cumulative + (u * 0.3989422804014327) * bell


def exponential(values):
    return jnp.exp2((values * LOG2E).astype(LOW))


def lane_facts():
    lane = lax.broadcasted_iota(jnp.int32, (1, PAIR), 1)
    return lane < HD, lane & (HD - 1)


def segments(lengths_ref, row, start, rows):
    places = lax.broadcasted_iota(jnp.int32, (rows, 1), 0) + start
    bound = jnp.int32(0)
    segment = jnp.zeros((rows, 1), jnp.int32)
    last = lengths_ref.shape[1] - 1
    for entry in range(last):
        bound = bound + lengths_ref[row, entry]
        segment = segment + (places >= bound).astype(jnp.int32)
    return segment, (segment == last).astype(F32), last


def attention_forward(row, lengths_ref, x, wq_ref, bias_ref, qa_ref, ka_ref, va_ref, ob_ref, s_ref, p_ref, m_ref, pad_ref, q_ref, aug_ref):
    width = HEADS * HD
    for block in range(3):
        at = block * width
        value = dot_nn(x, wq_ref[:, at : at + width]) + bias_ref[:, at : at + width]
        for pair in range(HEADS // 2):
            q_ref[block, pair] = value[:, pair * PAIR : (pair + 1) * PAIR]
    for start in range(0, SEQ, PIECE):
        place = pl.ds(start, PIECE)
        low_half, slot = lane_facts()
        segment, pad, last = segments(lengths_ref, row, start, PIECE)
        pad_ref[place] = jnp.broadcast_to(pad, (PIECE, PAIR))
        aug_q = jnp.where(slot == segment, 1.0, 0.0)
        aug_ref[place] = aug_q
        seen = (slot == segment) & (slot != last)
        aug_k = jnp.where(seen, 0.0, jnp.where(slot <= last, FAR, jnp.where(slot <= last + 3, 1.0, 0.0)))
        for pair in range(HEADS // 2):
            q = q_ref[0, pair, place] * HD**-0.5
            k = q_ref[1, pair, place]
            v = q_ref[2, pair, place]
            q_ref[0, pair, place] = q
            qa_ref[2 * pair, place] = jnp.where(low_half, q, aug_q).astype(LOW)
            qa_ref[2 * pair + 1, place] = jnp.where(low_half, aug_q, q).astype(LOW)
            ka_ref[2 * pair, place] = jnp.where(low_half, k, aug_k).astype(LOW)
            ka_ref[2 * pair + 1, place] = jnp.where(low_half, aug_k, k).astype(LOW)
            va_ref[2 * pair, place] = jnp.where(low_half, v, 1.0).astype(LOW)
            va_ref[2 * pair + 1, place] = jnp.where(low_half, 1.0, v).astype(LOW)

    def scores(head):
        s_ref[head % 2] = dot_nt(qa_ref[head], ka_ref[head])

    def softmax(head):
        for place in pieces(SEQ):
            highest = jnp.maximum(jnp.max(s_ref[head % 2, place], -1, keepdims=True), FLOOR)
            m_ref[head % 2, place] = jnp.broadcast_to(highest, (PIECE, PAIR))
            p_ref[head % 2, place] = exponential(s_ref[head % 2, place] - highest)

    scores(0)
    for head in range(HEADS):
        if head + 1 < HEADS:
            scores(head + 1)
        softmax(head)
        q_ref[1, head % 2] = dot_nn(p_ref[head % 2], va_ref[head])
        if head % 2:
            pair = head // 2
            for start in range(0, SEQ, PIECE):
                place = pl.ds(start, PIECE)
                low_half, slot = lane_facts()
                even = q_ref[1, 0, place]
                odd = q_ref[1, 1, place]
                pad = pad_ref[place]
                last = lengths_ref.shape[1] - 1
                total = jnp.where(low_half, odd, even) + pad
                top = jnp.where(low_half, odd_even(m_ref, 1, place), odd_even(m_ref, 0, place))
                spread = jnp.where(pad > 0, 0.0, top + jnp.log(total))
                first, second, third = three_parts(spread)
                aug = jnp.where(
                    slot == last + 1,
                    -first,
                    jnp.where(slot == last + 2, -second, jnp.where(slot == last + 3, -third, aug_ref[place])),
                )
                q = q_ref[0, pair, place]
                qa_ref[2 * pair, place] = jnp.where(low_half, q, aug).astype(LOW)
                qa_ref[2 * pair + 1, place] = jnp.where(low_half, aug, q).astype(LOW)
                v = q_ref[2, pair, place].astype(LOW).astype(F32)
                out = jnp.where(low_half, even, odd) / pltpu.roll(total, HD, 1) + pad * v
                ob_ref[place, pl.ds(pair * PAIR, PAIR)] = out.astype(LOW)


def odd_even(ref, which, place):
    return ref[which, place]


def normal(values):
    centred = values - jnp.mean(values, -1, keepdims=True)
    inverse = lax.rsqrt(jnp.mean(centred * centred, -1, keepdims=True) + EPSILON)
    return centred * inverse, inverse


def normal_back(cotangent, unit, inverse, gains):
    scaled = cotangent * gains
    return inverse * (
        scaled
        - jnp.mean(scaled, -1, keepdims=True)
        - unit * jnp.mean(scaled * unit, -1, keepdims=True)
    )


def dense_forward(x_ref, ob_ref, wo_ref, wi_ref, wf_ref, small_ref, bi_ref, n1_ref, n2_ref, inv_ref, yb_ref, gb_ref, gp_ref, z_ref, work_ref, u_ref):
    small = lambda index: small_ref[pl.ds(index, 1)]
    work_ref[...] = dot_nn(ob_ref[...], wo_ref[...])
    for place in pieces(SEQ):
        unit, inverse = normal(x_ref[place].astype(F32) + work_ref[place] + small(4))
        n1_ref[place] = unit
        inv_ref[place, pl.ds(0, HD)] = jnp.broadcast_to(inverse, (PIECE, HD))
        y = unit * small(2) + small(5)
        yb_ref[place] = y.astype(LOW)
        work_ref[place] = y + small(6)
    columns = 256
    count = wi_ref.shape[1] // columns

    def into(step):
        u_ref[step % 2] = dot_nn(yb_ref[...], wi_ref[:, pl.ds(step * columns, columns)])

    into(0)
    for step in range(count):
        if step + 1 < count:
            into(step + 1)
        lanes = pl.ds(step * columns, columns)
        for place in pieces(SEQ, SMALL):
            g, slope = gelu_parts(u_ref[step % 2, place] + bi_ref[:, lanes])
            gb_ref[place, lanes] = g.astype(LOW)
            gp_ref[place, lanes] = slope.astype(LOW)
    work_ref[...] += dot_nn(gb_ref[...], wf_ref[...])
    for place in pieces(SEQ):
        unit, inverse = normal(work_ref[place])
        n2_ref[place] = unit
        inv_ref[place, pl.ds(HD, HD)] = jnp.broadcast_to(inverse, (PIECE, HD))
        z_ref[place] = (unit * small(3) + small(7)).astype(z_ref.dtype)


def fold(values):
    return jnp.sum(values.reshape(-1, 8, values.shape[-1]), 0)


def dense_backward(dz_ref, n1_ref, n2_ref, inv_ref, yb_ref, gb_ref, gp_ref, ob_ref, wo_ref, wi_ref, wf_ref, small_ref, dr_ref, dob_ref, gwo_ref, gwi_ref, gwf_ref, gsmall_ref, gbi_ref, low_ref, u_ref, du_ref, turned_ref):
    small = lambda index: small_ref[pl.ds(index, 1)]
    for place in pieces(SEQ):
        dz = dz_ref[place].astype(F32)
        unit = n2_ref[place]
        gsmall_ref[3] += fold(dz * unit)
        gsmall_ref[7] += fold(dz)
        dr = normal_back(dz, unit, inv_ref[place, pl.ds(HD, 1)], small(3))
        dr_ref[place] = dr
        df = dr.astype(LOW)
        low_ref[place] = df
        gsmall_ref[6] += fold(df.astype(F32))
    columns = 256
    count = wi_ref.shape[1] // columns

    def back(step):
        u_ref[step % 2] = dot_nt(low_ref[...], wf_ref[pl.ds(step * columns, columns)])

    back(0)
    turned_ref[0] = low_ref[...].T
    turned_ref[1] = yb_ref[...].T
    for step in range(count):
        if step + 1 < count:
            back(step + 1)
        lanes = pl.ds(step * columns, columns)
        gwf_ref[:, lanes] += dot_nn(turned_ref[0], gb_ref[:, lanes])
        for place in pieces(SEQ, SMALL):
            du = (u_ref[step % 2, place] * gp_ref[place, lanes].astype(F32)).astype(LOW)
            du_ref[place, lanes] = du
            gbi_ref[:, lanes] += fold(du.astype(F32))
        gwi_ref[:, lanes] += dot_nn(turned_ref[1], du_ref[:, lanes])
    u_ref[0] = dot_nt(du_ref[...], wi_ref[...])
    for place in pieces(SEQ):
        dy = dr_ref[place] + u_ref[0, place]
        unit = n1_ref[place]
        gsmall_ref[2] += fold(dy * unit)
        gsmall_ref[5] += fold(dy)
        dr = normal_back(dy, unit, inv_ref[place, pl.ds(0, 1)], small(2))
        dr_ref[place] = dr
        da = dr.astype(LOW)
        low_ref[place] = da
        gsmall_ref[4] += fold(da.astype(F32))
    gwo_ref[...] += dot_tn(ob_ref[...], low_ref[...])
    dob_ref[...] = dot_nt(low_ref[...], wo_ref[...]).astype(LOW)


def attention_backward(row, lengths_ref, x, dob_ref, ob_ref, qa_ref, ka_ref, va_ref, wq_ref, dr_ref, dx_ref, gwq_ref, gbias_ref, da_ref, p_ref, ds_ref, s_ref, dqkv_ref, dq_ref, pad_ref, kt_ref, dqt_ref):
    width = HEADS * HD
    low_half, slot = lane_facts()
    for start in range(0, SEQ, PIECE):
        place = pl.ds(start, PIECE)
        segment, pad, last = segments(lengths_ref, row, start, PIECE)
        pad_ref[place] = jnp.broadcast_to(pad, (PIECE, PAIR))
        for pair in range(HEADS // 2):
            lanes = pl.ds(pair * PAIR, PAIR)
            dob = dob_ref[place, lanes].astype(F32)
            product = dob * ob_ref[place, lanes].astype(F32)
            even = jnp.sum(jnp.where(low_half, product, 0.0), -1, keepdims=True)
            odd = jnp.sum(jnp.where(low_half, 0.0, product), -1, keepdims=True)
            first, second, third = three_parts(jnp.where(low_half, odd, even))
            aug = jnp.where(
                slot == 0, -first, jnp.where(slot == 1, -second, jnp.where(slot == 2, -third, 0.0))
            )
            da_ref[2 * pair, place] = jnp.where(low_half, dob, aug).astype(LOW)
            da_ref[2 * pair + 1, place] = jnp.where(low_half, aug, dob).astype(LOW)
    for pair in range(HEADS // 2):
        low_half, unused = lane_facts()
        keys = jnp.where(low_half, ka_ref[2 * pair].astype(F32), ka_ref[2 * pair + 1].astype(F32))
        kt_ref[pl.ds(pair * PAIR, PAIR)] = keys.T.astype(LOW)
    low_half, slot = lane_facts()

    def scores(head):
        s_ref[0, head % 2] = dot_nt(ka_ref[head], qa_ref[head])
        s_ref[1, head % 2] = dot_nt(va_ref[head], da_ref[head])

    def weigh(head):
        for place in pieces(SEQ, SMALL):
            p = exponential(s_ref[0, head % 2, place])
            p_ref[head % 2, place] = p
            ds_ref[head % 2, place] = (p.astype(F32) * s_ref[1, head % 2, place]).astype(LOW)

    scores(0)
    for head in range(HEADS):
        if head + 1 < HEADS:
            scores(head + 1)
        weigh(head)
        side = head % 2
        dq_ref[1, side] = dot_nn(ds_ref[head % 2], qa_ref[head])
        dq_ref[2, side] = dot_nn(p_ref[head % 2], da_ref[head])
        dqt_ref[pl.ds(side * HD, HD)] = dot_nn(kt_ref[pl.ds(head * HD, HD)], ds_ref[head % 2])
        if side:
            pair = head // 2
            dq_ref[0, 0] = dqt_ref[...].T
            for start in range(0, SEQ, PIECE):
                place = pl.ds(start, PIECE)
                dq = dq_ref[0, 0, place] * HD**-0.5
                dk = jnp.where(low_half, dq_ref[1, 0, place], dq_ref[1, 1, place])
                dv = jnp.where(low_half, dq_ref[2, 0, place], dq_ref[2, 1, place])
                dv = dv + pad_ref[place] * dob_ref[place, pl.ds(pair * PAIR, PAIR)].astype(F32)
                for block, value in enumerate((dq, dk, dv)):
                    lanes = pl.ds(block * width + pair * PAIR, PAIR)
                    value = value.astype(LOW)
                    dqkv_ref[place, lanes] = value
                    if block != 1:
                        into = pl.ds(pair * PAIR, PAIR)
                        gbias_ref[block // 2, :, into] += fold(value.astype(F32))
    gwq_ref[...] += dot_tn(x, dqkv_ref[...])
    dx_ref[...] = (dr_ref[...] + dot_nt(dqkv_ref[...], wq_ref[...])).astype(dx_ref.dtype)


def unpack_matrix(raw_ref, at, into_ref):
    width = into_ref.shape[0]
    for start in range(0, into_ref.shape[1], width):
        block = raw_ref[:, :, pl.ds(at + start, width)].astype(F32)
        block = block.reshape(GROUPS + (width,)).swapaxes(0, 1).reshape(width, width)
        into_ref[:, pl.ds(start, width)] = block.astype(LOW)


def unpack_stacked(raw_ref, at, into_ref):
    width = into_ref.shape[1]
    count = into_ref.shape[0] // width
    blocks = [
        raw_ref[:, :, pl.ds(at + step * width, width)].astype(F32).reshape(GROUPS + (width,))
        for step in range(count)
    ]
    outer, inner, rows = GROUPS
    for place in range(inner):
        part = jnp.stack([jnp.stack([block[f, place] for block in blocks]) for f in range(outer)])
        size = outer * count * rows
        into_ref[pl.ds(place * size, size)] = part.reshape(size, width).astype(LOW)


def counter(shape, axis):
    return lax.broadcasted_iota(jnp.int32, shape, axis)


def split_by(values, size):
    return lax.shift_right_logical(values, size.bit_length() - 1), values & (size - 1)


def sources(rows):
    outer, inner, height = GROUPS
    group, within = split_by(counter((rows, 1), 0), height)
    far, near = split_by(group, inner)
    return near * outer + far, within


def unpack_vectors(raw_ref, at, layer):
    outer, inner, rows = GROUPS
    total = outer * inner * rows
    raw = raw_ref[:, :, pl.ds(at, 128)].reshape(total, 128)
    owner, place = split_by(counter((1, total), 1), rows)
    pick = jnp.where(counter((128, 1), 0) == rows * layer + place, 1.0, 0.0).astype(LOW)
    device, unused = sources(total)
    spread = jnp.where(owner == device, dot_nn(raw, pick), 0.0)
    return jnp.sum(spread.reshape(outer * inner, rows, total), 0)


def unpack_hidden(raw_ref, at, layer, hidden):
    outer, inner, rows = GROUPS
    total = outer * inner * rows
    raw = raw_ref[:, :, pl.ds(at, 128)].reshape(total, 128)
    owner, place = split_by(counter((1, hidden), 1), hidden // (outer * inner))
    pick = jnp.where(counter((128, 1), 0) == 2 * rows + place, 1.0, 0.0).astype(LOW)
    device, within = sources(total)
    device = jnp.where(within == layer, device, -1)
    spread = jnp.where(owner == device, dot_nn(raw, pick), 0.0)
    return jnp.sum(spread, 0, keepdims=True)


def pack_matrix(sum_ref, sent_ref, at):
    width = sum_ref.shape[0]
    outer, inner, rows = GROUPS
    for start in range(0, sum_ref.shape[1], width):
        block = sum_ref[:, pl.ds(start, width)].reshape(inner, outer, rows, width)
        block = block.swapaxes(0, 1).reshape(outer, inner * rows, width)
        sent_ref[:, :, pl.ds(at + start, width)] = block.astype(LOW)


def pack_stacked(sum_ref, sent_ref, at):
    width = sum_ref.shape[0]
    outer, inner, rows = GROUPS
    count = sum_ref.shape[1] // width
    near = inner // count
    for step in range(count):
        block = sum_ref[:, pl.ds(step * width, width)].T
        block = block.reshape(near, outer, count, rows, width)
        for part in range(count):
            piece = jnp.stack([block[:, f, part] for f in range(outer)])
            piece = piece.reshape(outer, near * rows, width)
            sent_ref[:, pl.ds(step * near * rows, near * rows), pl.ds(at + part * width, width)] = (
                piece.astype(LOW)
            )


def pack_shared(block, sent_ref, at):
    outer, inner, rows = GROUPS
    columns = block.shape[1]
    block = jnp.broadcast_to(block[None], (outer * inner, rows, columns))
    sent_ref[:, :, pl.ds(at, columns)] = block.reshape(outer, inner * rows, columns).astype(LOW)


def pack_attention(gwq_ref, gbias_ref, sent_ref, at):
    pack_matrix(gwq_ref, sent_ref, at)
    width = gwq_ref.shape[0]
    line = lax.broadcasted_iota(jnp.int32, (8, width), 0)
    sums = [jnp.sum(gbias_ref[index], 0, keepdims=True) for index in range(2)]
    block = jnp.where(line == 0, sums[0], jnp.where(line == 1, sums[1], 0.0))
    pack_shared(block, sent_ref, at + 3 * width)


def pack_dense(gwo_ref, gwi_ref, gwf_ref, gsmall_ref, gbi_ref, sent_ref, at):
    width, hidden = gwi_ref.shape
    pack_matrix(gwo_ref, sent_ref, at)
    pack_matrix(gwi_ref, sent_ref, at + width)
    pack_stacked(gwf_ref, sent_ref, at + width + hidden)
    at = at + width + 2 * hidden
    pack_shared(jnp.sum(gsmall_ref[...], 1), sent_ref, at)
    line = jnp.sum(gbi_ref[...], 0, keepdims=True)
    size = hidden // 8
    block = jnp.concatenate([line[:, step * size : (step + 1) * size] for step in range(8)], 0)
    pack_shared(block, sent_ref, at + width)


def shape_of(array):
    return jax.ShapeDtypeStruct(array.shape, array.dtype)


def by_row(shape):
    if len(shape) == 2:
        return pl.BlockSpec((SEQ, shape[1]), lambda row: (row, 0))
    return pl.BlockSpec((None,) + tuple(shape[1:]), lambda row: (row,) + (0,) * (len(shape) - 1))


def whole(shape):
    return pl.BlockSpec(tuple(shape), lambda row: (0,) * len(shape))


def run_rows(
    body, lengths, rowwise, fixed, row_outs, sent, scratch, cost, setup, finish, after=(), scalars=()
):
    count = lengths.shape[0]
    cuts = [len(scalars), len(rowwise), len(fixed), len(after), len(row_outs), len(sent), len(scratch)]

    def kernel(lengths_ref, *refs):
        row = pl.program_id(0)
        groups = []
        at = 0
        for cut in cuts:
            groups.append(refs[at : at + cut])
            at += cut
        numbers, rows_in, fixed_in, unused, rows_out, sent_out, work = groups

        @pl.when(row == 0)
        def _():
            setup(numbers, fixed_in, sent_out, work)

        body(row, lengths_ref, rows_in, rows_out, work)

        if finish:

            @pl.when(row == count - 1)
            def _():
                finish(numbers, work, sent_out)

    return pl.pallas_call(
        kernel,
        grid=(count,),
        in_specs=[pl.BlockSpec(memory_space=pltpu.SMEM)] * (1 + len(scalars))
        + [by_row(array.shape) for array in rowwise]
        + [whole(array.shape) for array in fixed]
        + [pl.BlockSpec(memory_space=pl.ANY) for array in after],
        out_specs=[by_row(part.shape) for part in row_outs] + [whole(part.shape) for part in sent],
        out_shape=list(row_outs) + list(sent),
        scratch_shapes=list(scratch),
        compiler_params=pltpu.CompilerParams(
            dimension_semantics=("arbitrary",), vmem_limit_bytes=MEMORY
        ),
        cost_estimate=pl.CostEstimate(flops=cost, bytes_accessed=8 * 2**20, transcendentals=0),
    )(lengths, *scalars, *rowwise, *fixed, *after)


def struct(shape, dtype):
    return jax.ShapeDtypeStruct(tuple(shape), dtype)


FORWARD_SCRATCH = lambda: [
    pltpu.VMEM((2, SEQ, SEQ), F32),
    pltpu.VMEM((2, SEQ, SEQ), LOW),
    pltpu.VMEM((2, SEQ, PAIR), F32),
    pltpu.VMEM((SEQ, PAIR), F32),
    pltpu.VMEM((3, HEADS // 2, SEQ, PAIR), F32),
    pltpu.VMEM((SEQ, PAIR), F32),
]
BACKWARD_SCRATCH = lambda: [
    pltpu.VMEM((HEADS, SEQ, PAIR), LOW),
    pltpu.VMEM((2, SEQ, SEQ), LOW),
    pltpu.VMEM((2, SEQ, SEQ), LOW),
    pltpu.VMEM((2, 2, SEQ, SEQ), F32),
    pltpu.VMEM((SEQ, 3 * HEADS * HD), LOW),
    pltpu.VMEM((3, 2, SEQ, PAIR), F32),
    pltpu.VMEM((SEQ, PAIR), F32),
    pltpu.VMEM((HEADS * HD, SEQ), LOW),
    pltpu.VMEM((PAIR, SEQ), F32),
]


def attention_outs(rows, tokens, width):
    heads = (rows, HEADS, SEQ, PAIR)
    return [struct(heads, LOW)] * 3 + [struct((tokens, width), LOW)]


def dense_outs(tokens, width, hidden):
    return [
        struct((tokens, width), F32),
        struct((tokens, width), F32),
        struct((tokens, PAIR), F32),
        struct((tokens, width), LOW),
        struct((tokens, hidden), LOW),
        struct((tokens, hidden), LOW),
    ]


def vmem(shape, dtype):
    return pltpu.VMEM(tuple(shape), dtype)


def attention_weights(width):
    return [vmem((width, 3 * width), LOW), vmem((1, 3 * width), F32)]


def dense_weights(width, hidden):
    return [
        vmem((width, width), LOW),
        vmem((width, hidden), LOW),
        vmem((hidden, width), LOW),
        vmem((8, width), F32),
        vmem((1, hidden), F32),
    ]


def dense_sums(width, hidden):
    return [
        vmem((width, width), F32),
        vmem((width, hidden), F32),
        vmem((width, hidden), F32),
        vmem((8, 8, width), F32),
        vmem((8, hidden), F32),
    ]


def attention_sums(width):
    return [vmem((width, 3 * width), F32), vmem((2, 8, width), F32)]


def dense_work(width, hidden):
    return [
        vmem((SEQ, width), LOW),
        vmem((2, SEQ, width), F32),
        vmem((SEQ, hidden), LOW),
        vmem((2, width, SEQ), LOW),
    ]


def set_attention(layer, urgent_ref, raw_ref, at, wq_ref, bias_ref):
    width = wq_ref.shape[0]
    unpack_matrix(raw_ref, at, wq_ref)
    vectors = unpack_vectors(urgent_ref, 3 * width, layer)
    bias_ref[:, :width] = vectors[0:1]
    bias_ref[:, width : 2 * width] = jnp.zeros((1, width), F32)
    bias_ref[:, 2 * width :] = vectors[1:2]


def set_dense(layer, urgent_ref, raw_ref, at, wo_ref, wi_ref, wf_ref, small_ref, bi_ref):
    width, hidden = wi_ref.shape
    unpack_matrix(raw_ref, at, wo_ref)
    unpack_matrix(raw_ref, at + width, wi_ref)
    unpack_stacked(raw_ref, at + width + hidden, wf_ref)
    small_ref[...] = unpack_vectors(urgent_ref, 3 * width, layer)
    bi_ref[...] = unpack_hidden(urgent_ref, 3 * width, layer, hidden)


def clear(refs):
    for ref in refs:
        ref[...] = jnp.zeros(ref.shape, ref.dtype)


def first_kernel(lengths, x, place, parts):
    rows, (tokens, width) = lengths.shape[0], x.shape

    def setup(numbers, fixed, sent, work):
        for step, part in enumerate(fixed):
            sent[0][numbers[0][0] ^ step] = part[...]
        set_attention(0, sent[0], sent[0], 0, *work[:2])

    def body(row, lengths_ref, rowwise, outs, work):
        attention_forward(row, lengths_ref, rowwise[0][...], *work[:2], *outs, *work[2:])

    return run_rows(
        body, lengths, [x], list(parts), attention_outs(rows, tokens, width),
        [struct((len(parts),) + parts[0].shape, LOW)],
        attention_weights(width) + FORWARD_SCRATCH(), 4 * 10**9, setup, None, (), [place],
    )


def attention_kernel(layer, lengths, x, urgent, raw, at):
    rows, (tokens, width) = lengths.shape[0], x.shape

    def setup(numbers, fixed, sent, work):
        set_attention(layer, *fixed, at, *work[:2])

    def body(row, lengths_ref, rowwise, outs, work):
        attention_forward(row, lengths_ref, rowwise[0][...].astype(LOW), *work[:2], *outs, *work[2:])

    return run_rows(
        body, lengths, [x], [urgent, raw], attention_outs(rows, tokens, width), [],
        attention_weights(width) + FORWARD_SCRATCH(), 4 * 10**9, setup, None,
    )


def dense_kernel(layer, lengths, x, ob, urgent, raw, at, hidden, after):
    tokens, width = x.shape

    def setup(numbers, fixed, sent, work):
        set_dense(layer, *fixed, at, *work[:5])

    def body(row, lengths_ref, rowwise, outs, work):
        dense_forward(*rowwise, *work[:5], *outs, *work[5:])

    return run_rows(
        body, lengths, [x, ob], [urgent, raw],
        dense_outs(tokens, width, hidden) + [struct((tokens, width), F32)], [],
        dense_weights(width, hidden) + [vmem((SEQ, width), F32), vmem((2, SEQ, width), F32)],
        5 * 10**9, setup, None, after,
    )


def turn_kernel(layer, lengths, x, ob, cotangent, urgent, raw, at, hidden):
    tokens, width = x.shape
    columns = width + 2 * hidden + width + hidden // 8

    def setup(numbers, fixed, sent, work):
        set_dense(layer, *fixed, at, *work[:5])
        clear(work[5:10])

    def body(row, lengths_ref, rowwise, outs, work):
        x_ref, ob_ref, dz_ref = rowwise
        z_ref, dr_ref, dob_ref = outs
        weights, sums, kept = work[:5], work[5:10], work[10:16]
        work_ref, low_ref, u_ref, du_ref, turned_ref = work[16:]
        dense_forward(x_ref, ob_ref, *weights, *kept, z_ref, work_ref, u_ref)
        dense_backward(
            dz_ref, *kept, ob_ref, *weights[:4], dr_ref, dob_ref, *sums, low_ref, u_ref, du_ref,
            turned_ref,
        )

    def finish(numbers, work, sent):
        pack_dense(*work[5:10], sent[0], 0)

    kept = [vmem((SEQ,) + part.shape[1:], part.dtype) for part in dense_outs(tokens, width, hidden)]
    return run_rows(
        body, lengths, [x, ob, cotangent], [urgent, raw],
        [struct((tokens, width), LOW), struct((tokens, width), F32), struct((tokens, width), LOW)],
        [struct((4, 64, columns), LOW)],
        dense_weights(width, hidden) + dense_sums(width, hidden) + kept
        + [vmem((SEQ, width), F32)] + dense_work(width, hidden),
        10**10, setup, finish,
    )


def hand_out(place_ref, packed_ref, sent):
    for step, ref in enumerate(sent):
        ref[...] = packed_ref[place_ref[0] ^ step]


def middle_kernel(lengths, upper, lower, urgent, raw1, raw0, hidden, after, place):
    tokens, width = upper[0].shape
    columns = 4 * width + width + 2 * hidden + width + hidden // 8

    def setup(numbers, fixed, sent, work):
        urgent_ref, raw1_ref, raw0_ref = fixed
        set_attention(1, urgent_ref, raw1_ref, 0, *work[:2])
        set_dense(0, urgent_ref, raw0_ref, 0, *work[2:7])
        clear(work[7:14])

    def body(row, lengths_ref, rowwise, outs, work):
        up, low = rowwise[:7], rowwise[7:]
        dx_ref = work[15]
        attention_backward(
            row, lengths_ref, up[0][...].astype(LOW), *up[1:6], work[0], up[6], dx_ref,
            *work[7:9], *work[20:],
        )
        dense_backward(dx_ref, *low, *work[2:6], *outs, *work[9:14], *work[16:20])

    def finish(numbers, work, sent):
        pack_attention(*work[7:9], work[14], 0)
        pack_dense(*work[9:14], work[14], 4 * width)
        hand_out(numbers[0], work[14], sent)

    return run_rows(
        body, lengths, list(upper) + list(lower), [urgent, raw1, raw0],
        [struct((tokens, width), F32), struct((tokens, width), LOW)],
        [struct((64, columns), LOW)] * 4,
        attention_weights(width) + dense_weights(width, hidden)
        + attention_sums(width) + dense_sums(width, hidden)
        + [vmem((4, 64, columns), LOW), vmem((SEQ, width), F32)]
        + dense_work(width, hidden) + BACKWARD_SCRATCH(),
        15 * 10**9, setup, finish, after, [place],
    )


def last_kernel(lengths, upper, urgent, after, place):
    tokens, width = upper[0].shape

    def setup(numbers, fixed, sent, work):
        set_attention(0, fixed[0], fixed[0], 0, *work[:2])
        clear(work[2:4])

    def body(row, lengths_ref, rowwise, outs, work):
        attention_backward(
            row, lengths_ref, rowwise[0][...], *rowwise[1:6], work[0], rowwise[6], outs[0],
            *work[2:4], *work[5:],
        )

    def finish(numbers, work, sent):
        pack_attention(*work[2:4], work[4], 0)
        hand_out(numbers[0], work[4], sent)

    return run_rows(
        body, lengths, list(upper), [urgent], [struct((tokens, width), LOW)],
        [struct((64, 4 * width), LOW)] * 4,
        attention_weights(width) + attention_sums(width)
        + [vmem((4, 64, 4 * width), LOW)] + BACKWARD_SCRATCH(),
        8 * 10**9, setup, finish, after, [place],
    )


def hold(array, after):
    def kernel(*refs):
        pass

    anywhere = pl.BlockSpec(memory_space=pl.ANY)
    return pl.pallas_call(
        kernel,
        in_specs=[anywhere] * (1 + len(after)),
        out_specs=anywhere,
        out_shape=shape_of(array),
        input_output_aliases={0: 0},
    )(array, *after)


def pack_parameters(
    attn_weight, attn_bias, out_weight, ffn_in, ffn_in_bias, ffn_out, norm_gain, shifts
):
    depth, rows, width = out_weight.shape
    copies = GROUPS[1]
    hidden = ffn_in.shape[2]
    early = 4 * width + 2 * hidden + 128
    columns = 4 * width + 2 * hidden
    height = ffn_in_bias.shape[1]

    def kernel(wq_ref, ab_ref, wo_ref, wi_ref, bi_ref, wf_ref, gain_ref, shift_ref, first_ref, rest_ref, small_ref):
        def put(ref, block, at):
            block = jnp.broadcast_to(block.astype(F32)[None], (copies,) + block.shape)
            block = block.reshape(copies * block.shape[1], block.shape[2])
            ref[:, pl.ds(at, block.shape[1])] = block.astype(LOW)

        small_ref[...] = jnp.zeros(small_ref.shape, F32)
        for layer in range(depth):
            lanes = pl.ds(rows * layer, rows)
            small_ref[0:2, lanes] = ab_ref[layer].astype(F32)
            small_ref[2:4, lanes] = gain_ref[layer].astype(F32)
            small_ref[4:8, lanes] = shift_ref[layer].astype(F32)
        small_ref[0:depth, pl.ds(2 * rows, height)] = bi_ref[...].astype(F32)
        put(first_ref, wq_ref[0], 0)
        put(first_ref, small_ref[...], 3 * width)
        for layer, ref, at in ((0, first_ref, 3 * width + 128), (1, rest_ref, 3 * width)):
            if layer:
                put(ref, wq_ref[layer], 0)
            put(ref, wo_ref[layer], at)
            put(ref, wi_ref[layer], at + width)
            at += width + hidden
            down = wf_ref[layer].astype(F32)
            for step in range(hidden // width):
                put(ref, down[step * rows : (step + 1) * rows], at)
                at += width

    return pl.pallas_call(
        kernel,
        in_specs=[pl.BlockSpec(memory_space=pltpu.VMEM)] * 8,
        out_shape=[struct((copies * rows, early), LOW), struct((copies * rows, columns), LOW)],
        scratch_shapes=[vmem((rows, 128), F32)],
        compiler_params=pltpu.CompilerParams(vmem_limit_bytes=MEMORY),
    )(attn_weight, attn_bias, out_weight, ffn_in, ffn_in_bias, ffn_out, norm_gain, shifts)


def add_parts(parts, after=(), joined=None):
    inner = [] if joined is None else [joined]
    ahead = 0 if joined is None else joined.shape[1]
    rows, lanes_in = parts[0].shape
    count = len(parts)

    def kernel(*refs):
        out_ref = refs[-1]
        if inner:
            out_ref[:, pl.ds(0, ahead)] = refs[count][...]
        columns = 256
        for start in range(0, lanes_in, columns):
            size = min(columns, lanes_in - start)
            total = refs[0][:, pl.ds(start, size)].astype(F32)
            for ref in refs[1:count]:
                total = total + ref[:, pl.ds(start, size)].astype(F32)
            out_ref[:, pl.ds(ahead + start, size)] = total.astype(LOW)

    near = pl.BlockSpec(memory_space=pltpu.VMEM)
    return pl.pallas_call(
        kernel,
        in_specs=[near] * (count + len(inner)) + [pl.BlockSpec(memory_space=pl.ANY)] * len(after),
        out_specs=near,
        out_shape=struct((rows, ahead + lanes_in), LOW),
        compiler_params=pltpu.CompilerParams(vmem_limit_bytes=MEMORY),
    )(*parts, *inner, *after)


def write_gradients(place, tail, front, depth, width, hidden):
    rows = GROUPS[2]
    last = front.shape[1] - 4 * width
    height = hidden // DEVICES

    def kernel(place_ref, tail_ref, front_ref, gwq_ref, gab_ref, gwo_ref, gwi_ref, gbi_ref, gwf_ref, gain_ref, shift_ref):
        spot = place_ref[0]

        def total(ref, at, columns):
            block = ref[:, pl.ds(at, columns)].astype(F32)
            return jnp.sum(block.reshape(-1, rows, columns), 0)

        def own(block, size):
            return pltpu.roll(block, block.shape[1] - spot * size, 1)

        for layer, ref, at in ((0, front_ref, last), (1, front_ref, 0)):
            gwq_ref[layer] = total(ref, at, 3 * width)
            gab_ref[layer] = own(total(ref, at + 3 * width, width), rows)[0:2, 0:rows]
        for layer, ref, at in ((0, front_ref, 4 * width), (1, tail_ref, 0)):
            gwo_ref[layer] = total(ref, at, width)
            gwi_ref[layer] = total(ref, at + width, hidden)
            for step in range(hidden // width):
                gwf_ref[layer, pl.ds(step * rows, rows)] = total(
                    ref, at + width + hidden + step * width, width
                )
            at += width + 2 * hidden
            small = own(total(ref, at, width), rows)
            gain_ref[layer] = small[2:4, 0:rows]
            shift_ref[layer] = small[4:8, 0:rows]
            line = total(ref, at + width, hidden // 8)
            line = jnp.concatenate([line[step : step + 1] for step in range(8)], 1)
            gbi_ref[pl.ds(layer, 1)] = own(line, height)[:, 0:height]

    outs = [
        struct((depth, rows, 3 * width), F32),
        struct((depth, 2, rows), F32),
        struct((depth, rows, width), F32),
        struct((depth, rows, hidden), F32),
        struct((depth, height), F32),
        struct((depth, height, width), F32),
        struct((depth, 2, rows), F32),
        struct((depth, 4, rows), F32),
    ]
    return pl.pallas_call(
        kernel,
        in_specs=[pl.BlockSpec(memory_space=pltpu.SMEM)] + [pl.BlockSpec(memory_space=pltpu.VMEM)] * 2,
        out_shape=outs,
        compiler_params=pltpu.CompilerParams(vmem_limit_bytes=MEMORY),
    )(place, tail, front)


def exchange(parts, axis):
    return lax.all_to_all(parts, axis, 0, 0, tiled=True)


def swap(part, axis, step):
    size = lax.axis_size(axis)
    return lax.ppermute(part, axis, [(source, source ^ step) for source in range(size)])


def local(
    hidden_in,
    lengths,
    grad_out,
    attn_weight,
    attn_bias,
    out_weight,
    ffn_in,
    ffn_in_bias,
    ffn_out,
    norm_gain,
    shifts,
):
    depth, rows, width = out_weight.shape
    hidden = ffn_in.shape[2]
    first, second = lax.axis_size("dp"), lax.axis_size("fsdp")
    fits = (second, first, rows) == GROUPS
    urgent_size = 3 * width + 128
    if fits:
        early, later = pack_parameters(
            attn_weight, attn_bias, out_weight, ffn_in, ffn_in_bias, ffn_out, norm_gain, shifts
        )
        early = exchange(early, "dp")
        urgent = early[:, :urgent_size]
        parts = [urgent] + [swap(urgent, "fsdp", step) for step in range(1, second)]
        raw0 = lax.all_gather(early[:, urgent_size:], "fsdp")
        later = exchange(hold(later, (early,)), "dp")
        raw1 = lax.all_gather(hold(later, tuple(parts[1:])), "fsdp")
        place = lax.axis_index("fsdp").astype(jnp.int32).reshape(1)
    else:
        urgent, raw0, raw1 = gather_other(
            attn_weight, attn_bias, out_weight, ffn_in, ffn_in_bias, ffn_out, norm_gain, shifts
        )
        parts = [urgent[step] for step in range(urgent.shape[0])]
        place = jnp.zeros((1,), jnp.int32)

    qa0, ka0, va0, ob0, urgent = first_kernel(lengths, hidden_in, place, parts)
    n1, n2, inv, yb, gb, gp, z0 = dense_kernel(
        0, lengths, hidden_in, ob0, urgent, raw0, 0, hidden, ()
    )
    qa1, ka1, va1, ob1 = attention_kernel(1, lengths, z0, urgent, raw1, 0)
    hidden_out, dr1, dob1, sent_a = turn_kernel(
        1, lengths, z0, ob1, grad_out, urgent, raw1, 3 * width, hidden
    )
    if fits:
        tail = lax.psum_scatter(sent_a, "fsdp", scatter_dimension=0)
    dr0, dob0, *sent_b = middle_kernel(
        lengths,
        (z0, dob1, ob1, qa1, ka1, va1, dr1),
        (n1, n2, inv, yb, gb, gp, ob0),
        urgent,
        raw1,
        raw0,
        hidden,
        (sent_a,),
        place,
    )
    if fits:
        tail = exchange(hold(tail, (sent_b[0],)), "dp")
    grad_in, *sent_c = last_kernel(
        lengths, (hidden_in, dob0, ob0, qa0, ka0, va0, dr0), urgent, (sent_b[0],), place
    )
    if fits:
        got_b = [sent_b[0]] + [swap(sent_b[step], "fsdp", step) for step in range(1, second)]
        got_c = [sent_c[0]] + [swap(sent_c[step], "fsdp", step) for step in range(1, second)]
        front = add_parts(got_b, (tail,))
        front = add_parts(got_c, (), front)
        front = exchange(front, "dp")
        place = lax.axis_index(("dp", "fsdp")).astype(jnp.int32).reshape(1)
        grads = write_gradients(place, tail, front, depth, width, hidden)
    else:
        grads = scatter_other(sent_a, jnp.stack(sent_b), jnp.stack(sent_c), rows, width, hidden)
    return (hidden_out, grad_in, *grads)


def gather_other(
    attn_weight, attn_bias, out_weight, ffn_in, ffn_in_bias, ffn_out, norm_gain, shifts
):
    axes = ("dp", "fsdp")
    gather = lambda part, axis: lax.all_gather(part, axes, axis=axis, tiled=True)
    depth, unused, width = out_weight.shape
    hidden = ffn_in.shape[2]
    outer, inner, rows = GROUPS
    vectors = gather(jnp.concatenate([attn_bias, norm_gain, shifts], 1), 2)
    line = gather(ffn_in_bias, 1)

    def order(natural):
        return (
            natural.reshape(inner, outer, rows, -1).swapaxes(0, 1).reshape(outer, inner * rows, -1)
        )

    def stacked(part):
        part = part.reshape(DEVICES, -1, rows, width)
        return order(part.swapaxes(1, 2).reshape(width, -1))

    small = vectors.reshape(depth, 8, DEVICES, rows).transpose(2, 1, 0, 3).reshape(width, -1)
    line = line.reshape(depth, DEVICES, -1).swapaxes(0, 1)
    line = jnp.pad(line, ((0, 0), (0, 8 - depth), (0, 0))).reshape(width, -1)
    small = jnp.concatenate([small, line], 1)
    small = jnp.pad(small, ((0, 0), (0, 128 - small.shape[1])))
    wq, wo, wi, wf = (gather(part, 1) for part in (attn_weight, out_weight, ffn_in, ffn_out))
    urgent = jnp.concatenate([order(wq[0]), order(small)], 2)
    raw0 = jnp.concatenate([order(wo[0]), order(wi[0]), stacked(wf[0])], 2)
    raw1 = jnp.concatenate([order(wq[1]), order(wo[1]), order(wi[1]), stacked(wf[1])], 2)
    return urgent, raw0, raw1


def scatter_other(sent_a, sent_b, sent_c, own_rows, width, hidden):
    outer, inner, rows = GROUPS
    axes = ("dp", "fsdp")

    def natural(part):
        return part.reshape(outer, inner, rows, -1).swapaxes(0, 1).reshape(width, -1).astype(F32)

    def cut(part, sizes):
        found, at = [], 0
        for size in sizes:
            found.append(part[:, at : at + size])
            at += size
        return found

    dense = [width, hidden, hidden, width, hidden // 8]
    attention = [3 * width, width]
    wq0, ab0 = cut(natural(sent_c), attention)
    wq1, ab1, wo0, wi0, wf0, small0, bi0 = cut(natural(sent_b), attention + dense)
    wo1, wi1, wf1, small1, bi1 = cut(natural(sent_a), dense)

    def stacked(part):
        part = part.reshape(DEVICES, rows, -1, width).swapaxes(1, 2)
        return part.reshape(hidden, width)

    def spread(parts, axis):
        return lax.psum_scatter(jnp.stack(parts), axes, scatter_dimension=axis, tiled=True)

    return (
        spread([wq0, wq1], 1),
        spread([ab0[:2], ab1[:2]], 2),
        spread([wo0, wo1], 1),
        spread([wi0, wi1], 1),
        spread([bi0[:8].reshape(-1), bi1[:8].reshape(-1)], 1),
        spread([stacked(wf0), stacked(wf1)], 1),
        spread([small0[2:4], small1[2:4]], 2),
        spread([small0[4:8], small1[4:8]], 2),
    )


def solution(mesh):
    placed = (
        P(("dp", "fsdp"), None),
        P(("dp", "fsdp"), None),
        P(("dp", "fsdp"), None),
        P(None, ("dp", "fsdp"), None),
        P(None, None, ("dp", "fsdp")),
        P(None, ("dp", "fsdp"), None),
        P(None, ("dp", "fsdp"), None),
        P(None, ("dp", "fsdp")),
        P(None, ("dp", "fsdp"), None),
        P(None, None, ("dp", "fsdp")),
        P(None, None, ("dp", "fsdp")),
    )
    return jax.shard_map(
        local,
        mesh=mesh,
        in_specs=placed,
        out_specs=(
            P(("dp", "fsdp"), None),
            P(("dp", "fsdp"), None),
            P(None, ("dp", "fsdp"), None),
            P(None, None, ("dp", "fsdp")),
            P(None, ("dp", "fsdp"), None),
            P(None, ("dp", "fsdp"), None),
            P(None, ("dp", "fsdp")),
            P(None, ("dp", "fsdp"), None),
            P(None, None, ("dp", "fsdp")),
            P(None, None, ("dp", "fsdp")),
        ),
        check_vma=False,
    )
```

```python
from functools import partial

import jax
import jax.numpy as jnp
from jax import lax
from jax.experimental import pallas as pl
from jax.experimental.pallas import tpu as pltpu
from jax.sharding import PartitionSpec as P

HEADS = 4
HD = 64
SEQ = 512
PAIR = 2 * HD
FAR = -(2.0**100)
FLOOR = -1e20
EPSILON = 1e-12
PIECE = 256
SMALL = 128
GROUPS = (4, 8, 8)
DEVICES = 32
LOW = jnp.bfloat16
F32 = jnp.float32
MEMORY = 60 * 2**20


def dot_nn(left, right):
    return lax.dot_general(left, right, (((1,), (0,)), ((), ())), preferred_element_type=F32)


def dot_nt(left, right):
    return lax.dot_general(left, right, (((1,), (1,)), ((), ())), preferred_element_type=F32)


def dot_tn(left, right):
    return lax.dot_general(left, right, (((0,), (0,)), ((), ())), preferred_element_type=F32)


def pieces(total, size=PIECE):
    return [pl.ds(start, size) for start in range(0, total, size)]


def three_parts(values):
    first = values.astype(LOW).astype(F32)
    rest = values - first
    second = rest.astype(LOW).astype(F32)
    return first, second, rest - second


CURVE = (
    7.97882253e-01,
    3.63445176e-02,
    -4.47304308e-05,
    -5.04138899e-05,
    3.10523303e-06,
    -6.66676088e-08,
)
BELL = -0.5 / 0.6931471805599453


def gelu_parts(u):
    square = u * u
    near = jnp.minimum(square, 31.36)
    curve = CURVE[-1]
    for factor in CURVE[-2::-1]:
        curve = curve * near + factor
    bent = jnp.tanh(u * curve)
    half = 0.5 * u
    slope = (0.5 + 0.5 * bent) + (u * 0.3989422804014327) * jnp.exp2(square * BELL)
    return half + half * bent, slope


def lane_facts():
    lane = lax.broadcasted_iota(jnp.int32, (1, PAIR), 1)
    return lane < HD, lane & (HD - 1)


def segments(lengths_ref, row, start, rows):
    places = lax.broadcasted_iota(jnp.int32, (rows, 1), 0) + start
    bound = jnp.int32(0)
    segment = jnp.zeros((rows, 1), jnp.int32)
    last = lengths_ref.shape[1] - 1
    for entry in range(last):
        bound = bound + lengths_ref[row, entry]
        segment = segment + (places >= bound).astype(jnp.int32)
    return segment, (segment == last).astype(F32), last


def attention_forward(row, lengths_ref, x, wq_ref, bias_ref, qa_ref, ka_ref, va_ref, ob_ref, s_ref, p_ref, m_ref, pad_ref, q_ref, aug_ref):
    width = HEADS * HD
    for block in range(3):
        at = block * width
        value = dot_nn(x, wq_ref[:, at : at + width]) + bias_ref[:, at : at + width]
        for pair in range(HEADS // 2):
            q_ref[block, pair] = value[:, pair * PAIR : (pair + 1) * PAIR]
    for start in range(0, SEQ, PIECE):
        place = pl.ds(start, PIECE)
        low_half, slot = lane_facts()
        segment, pad, last = segments(lengths_ref, row, start, PIECE)
        pad_ref[place] = jnp.broadcast_to(pad, (PIECE, PAIR))
        aug_q = jnp.where(slot == segment, 1.0, 0.0)
        aug_ref[place] = aug_q
        seen = (slot == segment) & (slot != last)
        aug_k = jnp.where(seen, 0.0, jnp.where(slot <= last, FAR, jnp.where(slot <= last + 3, 1.0, 0.0)))
        for pair in range(HEADS // 2):
            q = q_ref[0, pair, place] * HD**-0.5
            k = q_ref[1, pair, place]
            v = q_ref[2, pair, place]
            q_ref[0, pair, place] = q
            qa_ref[2 * pair, place] = jnp.where(low_half, q, aug_q).astype(LOW)
            qa_ref[2 * pair + 1, place] = jnp.where(low_half, aug_q, q).astype(LOW)
            ka_ref[2 * pair, place] = jnp.where(low_half, k, aug_k).astype(LOW)
            ka_ref[2 * pair + 1, place] = jnp.where(low_half, aug_k, k).astype(LOW)
            va_ref[2 * pair, place] = jnp.where(low_half, v, 1.0).astype(LOW)
            va_ref[2 * pair + 1, place] = jnp.where(low_half, 1.0, v).astype(LOW)

    def scores(head):
        s_ref[head % 2] = dot_nt(qa_ref[head], ka_ref[head])

    def softmax(head):
        for place in pieces(SEQ):
            highest = jnp.maximum(jnp.max(s_ref[head % 2, place], -1, keepdims=True), FLOOR)
            m_ref[head % 2, place] = jnp.broadcast_to(highest, (PIECE, PAIR))
            p_ref[head % 2, place] = jnp.exp(s_ref[head % 2, place] - highest).astype(LOW)

    scores(0)
    for head in range(HEADS):
        if head + 1 < HEADS:
            scores(head + 1)
        softmax(head)
        q_ref[1, head % 2] = dot_nn(p_ref[head % 2], va_ref[head])
        if head % 2:
            pair = head // 2
            for start in range(0, SEQ, PIECE):
                place = pl.ds(start, PIECE)
                low_half, slot = lane_facts()
                even = q_ref[1, 0, place]
                odd = q_ref[1, 1, place]
                pad = pad_ref[place]
                last = lengths_ref.shape[1] - 1
                total = jnp.where(low_half, odd, even) + pad
                top = jnp.where(low_half, odd_even(m_ref, 1, place), odd_even(m_ref, 0, place))
                spread = jnp.where(pad > 0, 0.0, top + jnp.log(total))
                first, second, third = three_parts(spread)
                aug = jnp.where(
                    slot == last + 1,
                    -first,
                    jnp.where(slot == last + 2, -second, jnp.where(slot == last + 3, -third, aug_ref[place])),
                )
                q = q_ref[0, pair, place]
                qa_ref[2 * pair, place] = jnp.where(low_half, q, aug).astype(LOW)
                qa_ref[2 * pair + 1, place] = jnp.where(low_half, aug, q).astype(LOW)
                v = q_ref[2, pair, place].astype(LOW).astype(F32)
                out = jnp.where(low_half, even, odd) / pltpu.roll(total, HD, 1) + pad * v
                ob_ref[place, pl.ds(pair * PAIR, PAIR)] = out.astype(LOW)


def odd_even(ref, which, place):
    return ref[which, place]


def normal(values):
    centred = values - jnp.mean(values, -1, keepdims=True)
    inverse = lax.rsqrt(jnp.mean(centred * centred, -1, keepdims=True) + EPSILON)
    return centred * inverse, inverse


def normal_back(cotangent, unit, inverse, gains):
    scaled = cotangent * gains
    return inverse * (
        scaled
        - jnp.mean(scaled, -1, keepdims=True)
        - unit * jnp.mean(scaled * unit, -1, keepdims=True)
    )


def dense_forward(x_ref, ob_ref, wo_ref, wi_ref, wf_ref, small_ref, bi_ref, n1_ref, n2_ref, inv_ref, yb_ref, gb_ref, gp_ref, z_ref, work_ref, u_ref):
    small = lambda index: small_ref[pl.ds(index, 1)]
    work_ref[...] = dot_nn(ob_ref[...], wo_ref[...])
    for place in pieces(SEQ):
        unit, inverse = normal(x_ref[place].astype(F32) + work_ref[place] + small(4))
        n1_ref[place] = unit
        inv_ref[place, pl.ds(0, HD)] = jnp.broadcast_to(inverse, (PIECE, HD))
        y = unit * small(2) + small(5)
        yb_ref[place] = y.astype(LOW)
        work_ref[place] = y + small(6)
    columns = 512
    count = wi_ref.shape[1] // columns

    def into(step):
        u_ref[step % 2] = dot_nn(yb_ref[...], wi_ref[:, pl.ds(step * columns, columns)])

    into(0)
    for step in range(count):
        if step + 1 < count:
            into(step + 1)
        lanes = pl.ds(step * columns, columns)
        for place in pieces(SEQ, SMALL):
            g, slope = gelu_parts(u_ref[step % 2, place] + bi_ref[:, lanes])
            gb_ref[place, lanes] = g.astype(LOW)
            gp_ref[place, lanes] = slope.astype(LOW)
    work_ref[...] += dot_nn(gb_ref[...], wf_ref[...])
    for place in pieces(SEQ):
        unit, inverse = normal(work_ref[place])
        n2_ref[place] = unit
        inv_ref[place, pl.ds(HD, HD)] = jnp.broadcast_to(inverse, (PIECE, HD))
        z_ref[place] = (unit * small(3) + small(7)).astype(z_ref.dtype)


def fold(values):
    return jnp.sum(values.reshape(-1, 8, values.shape[-1]), 0)


def dense_backward(dz_ref, n1_ref, n2_ref, inv_ref, yb_ref, gb_ref, gp_ref, ob_ref, wo_ref, wi_ref, wf_ref, small_ref, dr_ref, dob_ref, gwo_ref, gwi_ref, gwf_ref, gsmall_ref, gbi_ref, low_ref, u_ref, du_ref, turned_ref):
    small = lambda index: small_ref[pl.ds(index, 1)]
    for place in pieces(SEQ):
        dz = dz_ref[place].astype(F32)
        unit = n2_ref[place]
        gsmall_ref[3] += fold(dz * unit)
        gsmall_ref[7] += fold(dz)
        dr = normal_back(dz, unit, inv_ref[place, pl.ds(HD, 1)], small(3))
        dr_ref[place] = dr
        df = dr.astype(LOW)
        low_ref[place] = df
        gsmall_ref[6] += fold(df.astype(F32))
    columns = 512
    count = wi_ref.shape[1] // columns

    def back(step):
        u_ref[step % 2] = dot_nt(low_ref[...], wf_ref[pl.ds(step * columns, columns)])

    back(0)
    turned_ref[0] = low_ref[...].T
    turned_ref[1] = yb_ref[...].T
    for step in range(count):
        if step + 1 < count:
            back(step + 1)
        lanes = pl.ds(step * columns, columns)
        gwf_ref[:, lanes] += dot_nn(turned_ref[0], gb_ref[:, lanes])
        for place in pieces(SEQ, SMALL):
            du = (u_ref[step % 2, place] * gp_ref[place, lanes].astype(F32)).astype(LOW)
            du_ref[place, lanes] = du
            gbi_ref[:, lanes] += fold(du.astype(F32))
        gwi_ref[:, lanes] += dot_nn(turned_ref[1], du_ref[:, lanes])
    near = pl.ds(0, wi_ref.shape[0])
    u_ref[0, :, near] = dot_nt(du_ref[...], wi_ref[...])
    for place in pieces(SEQ):
        dy = dr_ref[place] + u_ref[0, place, near]
        unit = n1_ref[place]
        gsmall_ref[2] += fold(dy * unit)
        gsmall_ref[5] += fold(dy)
        dr = normal_back(dy, unit, inv_ref[place, pl.ds(0, 1)], small(2))
        dr_ref[place] = dr
        da = dr.astype(LOW)
        low_ref[place] = da
        gsmall_ref[4] += fold(da.astype(F32))
    gwo_ref[...] += dot_tn(ob_ref[...], low_ref[...])
    dob_ref[...] = dot_nt(low_ref[...], wo_ref[...]).astype(LOW)


def attention_backward(row, lengths_ref, x, dob_ref, ob_ref, qa_ref, ka_ref, va_ref, wq_ref, dr_ref, dx_ref, gwq_ref, gbias_ref, da_ref, p_ref, ds_ref, s_ref, dqkv_ref, dq_ref, pad_ref, kt_ref, dqt_ref):
    width = HEADS * HD
    low_half, slot = lane_facts()
    for start in range(0, SEQ, PIECE):
        place = pl.ds(start, PIECE)
        segment, pad, last = segments(lengths_ref, row, start, PIECE)
        pad_ref[place] = jnp.broadcast_to(pad, (PIECE, PAIR))
        for pair in range(HEADS // 2):
            lanes = pl.ds(pair * PAIR, PAIR)
            dob = dob_ref[place, lanes].astype(F32)
            product = dob * ob_ref[place, lanes].astype(F32)
            even = jnp.sum(jnp.where(low_half, product, 0.0), -1, keepdims=True)
            odd = jnp.sum(jnp.where(low_half, 0.0, product), -1, keepdims=True)
            first, second, third = three_parts(jnp.where(low_half, odd, even))
            aug = jnp.where(
                slot == 0, -first, jnp.where(slot == 1, -second, jnp.where(slot == 2, -third, 0.0))
            )
            da_ref[2 * pair, place] = jnp.where(low_half, dob, aug).astype(LOW)
            da_ref[2 * pair + 1, place] = jnp.where(low_half, aug, dob).astype(LOW)
    for pair in range(HEADS // 2):
        low_half, unused = lane_facts()
        keys = jnp.where(low_half, ka_ref[2 * pair].astype(F32), ka_ref[2 * pair + 1].astype(F32))
        kt_ref[pl.ds(pair * PAIR, PAIR)] = keys.T.astype(LOW)
    low_half, slot = lane_facts()

    def scores(head):
        s_ref[0, head % 2] = dot_nt(ka_ref[head], qa_ref[head])
        s_ref[1, head % 2] = dot_nt(va_ref[head], da_ref[head])

    def weigh(head):
        for place in pieces(SEQ, SMALL):
            p = jnp.exp(s_ref[0, head % 2, place])
            p_ref[head % 2, place] = p.astype(LOW)
            ds_ref[head % 2, place] = (p * s_ref[1, head % 2, place]).astype(LOW)

    scores(0)
    for head in range(HEADS):
        if head + 1 < HEADS:
            scores(head + 1)
        weigh(head)
        side = head % 2
        dq_ref[1, side] = dot_nn(ds_ref[head % 2], qa_ref[head])
        dq_ref[2, side] = dot_nn(p_ref[head % 2], da_ref[head])
        dqt_ref[pl.ds(side * HD, HD)] = dot_nn(kt_ref[pl.ds(head * HD, HD)], ds_ref[head % 2])
        if side:
            pair = head // 2
            dq_ref[0, 0] = dqt_ref[...].T
            for start in range(0, SEQ, PIECE):
                place = pl.ds(start, PIECE)
                dq = dq_ref[0, 0, place] * HD**-0.5
                dk = jnp.where(low_half, dq_ref[1, 0, place], dq_ref[1, 1, place])
                dv = jnp.where(low_half, dq_ref[2, 0, place], dq_ref[2, 1, place])
                dv = dv + pad_ref[place] * dob_ref[place, pl.ds(pair * PAIR, PAIR)].astype(F32)
                for block, value in enumerate((dq, dk, dv)):
                    lanes = pl.ds(block * width + pair * PAIR, PAIR)
                    value = value.astype(LOW)
                    dqkv_ref[place, lanes] = value
                    if block != 1:
                        into = pl.ds(pair * PAIR, PAIR)
                        gbias_ref[block // 2, :, into] += fold(value.astype(F32))
    gwq_ref[...] += dot_tn(x, dqkv_ref[...])
    dx_ref[...] = (dr_ref[...] + dot_nt(dqkv_ref[...], wq_ref[...])).astype(dx_ref.dtype)


def unpack_matrix(raw_ref, at, into_ref):
    width = into_ref.shape[0]
    for start in range(0, into_ref.shape[1], width):
        block = raw_ref[:, :, pl.ds(at + start, width)].astype(F32)
        block = block.reshape(GROUPS + (width,)).swapaxes(0, 1).reshape(width, width)
        into_ref[:, pl.ds(start, width)] = block.astype(LOW)


def unpack_stacked(raw_ref, at, into_ref):
    width = into_ref.shape[1]
    count = into_ref.shape[0] // width
    blocks = [
        raw_ref[:, :, pl.ds(at + step * width, width)].astype(F32).reshape(GROUPS + (width,))
        for step in range(count)
    ]
    outer, inner, rows = GROUPS
    for place in range(inner):
        part = jnp.stack([jnp.stack([block[f, place] for block in blocks]) for f in range(outer)])
        size = outer * count * rows
        into_ref[pl.ds(place * size, size)] = part.reshape(size, width).astype(LOW)


def counter(shape, axis):
    return lax.broadcasted_iota(jnp.int32, shape, axis)


def split_by(values, size):
    return lax.shift_right_logical(values, size.bit_length() - 1), values & (size - 1)


def sources(rows):
    outer, inner, height = GROUPS
    group, within = split_by(counter((rows, 1), 0), height)
    far, near = split_by(group, inner)
    return near * outer + far, within


def unpack_vectors(raw_ref, at, layer):
    outer, inner, rows = GROUPS
    total = outer * inner * rows
    raw = raw_ref[:, :, pl.ds(at, 128)].reshape(total, 128)
    owner, place = split_by(counter((1, total), 1), rows)
    pick = jnp.where(counter((128, 1), 0) == rows * layer + place, 1.0, 0.0).astype(LOW)
    device, unused = sources(total)
    spread = jnp.where(owner == device, dot_nn(raw, pick), 0.0)
    return jnp.sum(spread.reshape(outer * inner, rows, total), 0)


def unpack_hidden(raw_ref, at, layer, hidden):
    outer, inner, rows = GROUPS
    total = outer * inner * rows
    raw = raw_ref[:, :, pl.ds(at, 128)].reshape(total, 128)
    owner, place = split_by(counter((1, hidden), 1), hidden // (outer * inner))
    pick = jnp.where(counter((128, 1), 0) == 2 * rows + place, 1.0, 0.0).astype(LOW)
    device, within = sources(total)
    device = jnp.where(within == layer, device, -1)
    spread = jnp.where(owner == device, dot_nn(raw, pick), 0.0)
    return jnp.sum(spread, 0, keepdims=True)


def pack_matrix(sum_ref, sent_ref, at):
    width = sum_ref.shape[0]
    outer, inner, rows = GROUPS
    for start in range(0, sum_ref.shape[1], width):
        block = sum_ref[:, pl.ds(start, width)].reshape(inner, outer, rows, width)
        block = block.swapaxes(0, 1).reshape(outer, inner * rows, width)
        sent_ref[:, :, pl.ds(at + start, width)] = block.astype(LOW)


def pack_stacked(sum_ref, sent_ref, at):
    width = sum_ref.shape[0]
    outer, inner, rows = GROUPS
    count = sum_ref.shape[1] // width
    near = inner // count
    for step in range(count):
        block = sum_ref[:, pl.ds(step * width, width)].T
        block = block.reshape(near, outer, count, rows, width)
        for part in range(count):
            piece = jnp.stack([block[:, f, part] for f in range(outer)])
            piece = piece.reshape(outer, near * rows, width)
            sent_ref[:, pl.ds(step * near * rows, near * rows), pl.ds(at + part * width, width)] = (
                piece.astype(LOW)
            )


def pack_shared(block, sent_ref, at):
    outer, inner, rows = GROUPS
    columns = block.shape[1]
    block = jnp.broadcast_to(block[None], (outer * inner, rows, columns))
    sent_ref[:, :, pl.ds(at, columns)] = block.reshape(outer, inner * rows, columns).astype(LOW)


def pack_attention(gwq_ref, gbias_ref, sent_ref, at):
    pack_matrix(gwq_ref, sent_ref, at)
    width = gwq_ref.shape[0]
    line = lax.broadcasted_iota(jnp.int32, (8, width), 0)
    sums = [jnp.sum(gbias_ref[index], 0, keepdims=True) for index in range(2)]
    block = jnp.where(line == 0, sums[0], jnp.where(line == 1, sums[1], 0.0))
    pack_shared(block, sent_ref, at + 3 * width)


def pack_dense(gwo_ref, gwi_ref, gwf_ref, gsmall_ref, gbi_ref, sent_ref, at):
    width, hidden = gwi_ref.shape
    pack_matrix(gwo_ref, sent_ref, at)
    pack_matrix(gwi_ref, sent_ref, at + width)
    pack_stacked(gwf_ref, sent_ref, at + width + hidden)
    at = at + width + 2 * hidden
    pack_shared(jnp.sum(gsmall_ref[...], 1), sent_ref, at)
    line = jnp.sum(gbi_ref[...], 0, keepdims=True)
    size = hidden // 8
    block = jnp.concatenate([line[:, step * size : (step + 1) * size] for step in range(8)], 0)
    pack_shared(block, sent_ref, at + width)


def shape_of(array):
    return jax.ShapeDtypeStruct(array.shape, array.dtype)


def by_row(shape):
    if len(shape) == 2:
        return pl.BlockSpec((SEQ, shape[1]), lambda row: (row, 0))
    return pl.BlockSpec((None,) + tuple(shape[1:]), lambda row: (row,) + (0,) * (len(shape) - 1))


def whole(shape):
    return pl.BlockSpec(tuple(shape), lambda row: (0,) * len(shape))


def run_rows(
    body, lengths, rowwise, fixed, row_outs, sent, scratch, cost, setup, finish, after=(), scalars=()
):
    count = lengths.shape[0]
    cuts = [len(scalars), len(rowwise), len(fixed), len(after), len(row_outs), len(sent), len(scratch)]

    def kernel(lengths_ref, *refs):
        row = pl.program_id(0)
        groups = []
        at = 0
        for cut in cuts:
            groups.append(refs[at : at + cut])
            at += cut
        numbers, rows_in, fixed_in, unused, rows_out, sent_out, work = groups

        @pl.when(row == 0)
        def _():
            setup(numbers, fixed_in, sent_out, work)

        body(row, lengths_ref, rows_in, rows_out, work)

        if finish:

            @pl.when(row == count - 1)
            def _():
                finish(numbers, work, sent_out)

    return pl.pallas_call(
        kernel,
        grid=(count,),
        in_specs=[pl.BlockSpec(memory_space=pltpu.SMEM)] * (1 + len(scalars))
        + [by_row(array.shape) for array in rowwise]
        + [whole(array.shape) for array in fixed]
        + [pl.BlockSpec(memory_space=pl.ANY) for array in after],
        out_specs=[by_row(part.shape) for part in row_outs] + [whole(part.shape) for part in sent],
        out_shape=list(row_outs) + list(sent),
        scratch_shapes=list(scratch),
        compiler_params=pltpu.CompilerParams(
            dimension_semantics=("arbitrary",), vmem_limit_bytes=MEMORY
        ),
        cost_estimate=pl.CostEstimate(flops=cost, bytes_accessed=8 * 2**20, transcendentals=0),
    )(lengths, *scalars, *rowwise, *fixed, *after)


def struct(shape, dtype):
    return jax.ShapeDtypeStruct(tuple(shape), dtype)


FORWARD_SCRATCH = lambda: [
    pltpu.VMEM((2, SEQ, SEQ), F32),
    pltpu.VMEM((2, SEQ, SEQ), LOW),
    pltpu.VMEM((2, SEQ, PAIR), F32),
    pltpu.VMEM((SEQ, PAIR), F32),
    pltpu.VMEM((3, HEADS // 2, SEQ, PAIR), F32),
    pltpu.VMEM((SEQ, PAIR), F32),
]
BACKWARD_SCRATCH = lambda: [
    pltpu.VMEM((HEADS, SEQ, PAIR), LOW),
    pltpu.VMEM((2, SEQ, SEQ), LOW),
    pltpu.VMEM((2, SEQ, SEQ), LOW),
    pltpu.VMEM((2, 2, SEQ, SEQ), F32),
    pltpu.VMEM((SEQ, 3 * HEADS * HD), LOW),
    pltpu.VMEM((3, 2, SEQ, PAIR), F32),
    pltpu.VMEM((SEQ, PAIR), F32),
    pltpu.VMEM((HEADS * HD, SEQ), LOW),
    pltpu.VMEM((PAIR, SEQ), F32),
]


def attention_outs(rows, tokens, width):
    heads = (rows, HEADS, SEQ, PAIR)
    return [struct(heads, LOW)] * 3 + [struct((tokens, width), LOW)]


def dense_outs(tokens, width, hidden):
    return [
        struct((tokens, width), F32),
        struct((tokens, width), F32),
        struct((tokens, PAIR), F32),
        struct((tokens, width), LOW),
        struct((tokens, hidden), LOW),
        struct((tokens, hidden), LOW),
    ]


def vmem(shape, dtype):
    return pltpu.VMEM(tuple(shape), dtype)


def attention_weights(width):
    return [vmem((width, 3 * width), LOW), vmem((1, 3 * width), F32)]


def dense_weights(width, hidden):
    return [
        vmem((width, width), LOW),
        vmem((width, hidden), LOW),
        vmem((hidden, width), LOW),
        vmem((8, width), F32),
        vmem((1, hidden), F32),
    ]


def dense_sums(width, hidden):
    return [
        vmem((width, width), F32),
        vmem((width, hidden), F32),
        vmem((width, hidden), F32),
        vmem((8, 8, width), F32),
        vmem((8, hidden), F32),
    ]


def attention_sums(width):
    return [vmem((width, 3 * width), F32), vmem((2, 8, width), F32)]


def dense_work(width, hidden):
    return [
        vmem((SEQ, width), LOW),
        vmem((2, SEQ, 2 * width), F32),
        vmem((SEQ, hidden), LOW),
        vmem((2, width, SEQ), LOW),
    ]


def set_attention(layer, urgent_ref, raw_ref, at, wq_ref, bias_ref):
    width = wq_ref.shape[0]
    unpack_matrix(raw_ref, at, wq_ref)
    vectors = unpack_vectors(urgent_ref, 3 * width, layer)
    bias_ref[:, :width] = vectors[0:1]
    bias_ref[:, width : 2 * width] = jnp.zeros((1, width), F32)
    bias_ref[:, 2 * width :] = vectors[1:2]


def set_dense(layer, urgent_ref, raw_ref, at, wo_ref, wi_ref, wf_ref, small_ref, bi_ref):
    width, hidden = wi_ref.shape
    unpack_matrix(raw_ref, at, wo_ref)
    unpack_matrix(raw_ref, at + width, wi_ref)
    unpack_stacked(raw_ref, at + width + hidden, wf_ref)
    small_ref[...] = unpack_vectors(urgent_ref, 3 * width, layer)
    bi_ref[...] = unpack_hidden(urgent_ref, 3 * width, layer, hidden)


def clear(refs):
    for ref in refs:
        ref[...] = jnp.zeros(ref.shape, ref.dtype)


def first_kernel(lengths, x, place, parts):
    rows, (tokens, width) = lengths.shape[0], x.shape

    def setup(numbers, fixed, sent, work):
        for step, part in enumerate(fixed):
            sent[0][numbers[0][0] ^ step] = part[...]
        set_attention(0, sent[0], sent[0], 0, *work[:2])

    def body(row, lengths_ref, rowwise, outs, work):
        attention_forward(row, lengths_ref, rowwise[0][...], *work[:2], *outs, *work[2:])

    return run_rows(
        body, lengths, [x], list(parts), attention_outs(rows, tokens, width),
        [struct((len(parts),) + parts[0].shape, LOW)],
        attention_weights(width) + FORWARD_SCRATCH(), 4 * 10**9, setup, None, (), [place],
    )


def attention_kernel(layer, lengths, x, urgent, raw, at):
    rows, (tokens, width) = lengths.shape[0], x.shape

    def setup(numbers, fixed, sent, work):
        set_attention(layer, *fixed, at, *work[:2])

    def body(row, lengths_ref, rowwise, outs, work):
        attention_forward(row, lengths_ref, rowwise[0][...].astype(LOW), *work[:2], *outs, *work[2:])

    return run_rows(
        body, lengths, [x], [urgent, raw], attention_outs(rows, tokens, width), [],
        attention_weights(width) + FORWARD_SCRATCH(), 4 * 10**9, setup, None,
    )


def dense_kernel(layer, lengths, x, ob, urgent, raw, at, hidden, after):
    tokens, width = x.shape

    def setup(numbers, fixed, sent, work):
        set_dense(layer, *fixed, at, *work[:5])

    def body(row, lengths_ref, rowwise, outs, work):
        dense_forward(*rowwise, *work[:5], *outs, *work[5:])

    return run_rows(
        body, lengths, [x, ob], [urgent, raw],
        dense_outs(tokens, width, hidden) + [struct((tokens, width), F32)], [],
        dense_weights(width, hidden) + [vmem((SEQ, width), F32), vmem((2, SEQ, 2 * width), F32)],
        5 * 10**9, setup, None, after,
    )


def turn_kernel(layer, lengths, x, ob, cotangent, urgent, raw, at, hidden):
    tokens, width = x.shape
    columns = width + 2 * hidden + width + hidden // 8

    def setup(numbers, fixed, sent, work):
        set_dense(layer, *fixed, at, *work[:5])
        clear(work[5:10])

    def body(row, lengths_ref, rowwise, outs, work):
        x_ref, ob_ref, dz_ref = rowwise
        z_ref, dr_ref, dob_ref = outs
        weights, sums, kept = work[:5], work[5:10], work[10:16]
        work_ref, low_ref, u_ref, du_ref, turned_ref = work[16:]
        dense_forward(x_ref, ob_ref, *weights, *kept, z_ref, work_ref, u_ref)
        dense_backward(
            dz_ref, *kept, ob_ref, *weights[:4], dr_ref, dob_ref, *sums, low_ref, u_ref, du_ref,
            turned_ref,
        )

    def finish(numbers, work, sent):
        pack_dense(*work[5:10], sent[0], 0)

    kept = [vmem((SEQ,) + part.shape[1:], part.dtype) for part in dense_outs(tokens, width, hidden)]
    return run_rows(
        body, lengths, [x, ob, cotangent], [urgent, raw],
        [struct((tokens, width), LOW), struct((tokens, width), F32), struct((tokens, width), LOW)],
        [struct((4, 64, columns), LOW)],
        dense_weights(width, hidden) + dense_sums(width, hidden) + kept
        + [vmem((SEQ, width), F32)] + dense_work(width, hidden),
        10**10, setup, finish,
    )


def hand_out(place_ref, packed_ref, sent):
    for step, ref in enumerate(sent):
        ref[...] = packed_ref[place_ref[0] ^ step]


def middle_kernel(lengths, upper, lower, urgent, raw1, raw0, hidden, after, place):
    tokens, width = upper[0].shape
    columns = 4 * width + width + 2 * hidden + width + hidden // 8

    def setup(numbers, fixed, sent, work):
        urgent_ref, raw1_ref, raw0_ref = fixed
        set_attention(1, urgent_ref, raw1_ref, 0, *work[:2])
        set_dense(0, urgent_ref, raw0_ref, 0, *work[2:7])
        clear(work[7:14])

    def body(row, lengths_ref, rowwise, outs, work):
        up, low = rowwise[:7], rowwise[7:]
        dx_ref = work[15]
        attention_backward(
            row, lengths_ref, up[0][...].astype(LOW), *up[1:6], work[0], up[6], dx_ref,
            *work[7:9], *work[20:],
        )
        dense_backward(dx_ref, *low, *work[2:6], *outs, *work[9:14], *work[16:20])

    def finish(numbers, work, sent):
        pack_attention(*work[7:9], work[14], 0)
        pack_dense(*work[9:14], work[14], 4 * width)
        hand_out(numbers[0], work[14], sent)

    return run_rows(
        body, lengths, list(upper) + list(lower), [urgent, raw1, raw0],
        [struct((tokens, width), F32), struct((tokens, width), LOW)],
        [struct((64, columns), LOW)] * 4,
        attention_weights(width) + dense_weights(width, hidden)
        + attention_sums(width) + dense_sums(width, hidden)
        + [vmem((4, 64, columns), LOW), vmem((SEQ, width), F32)]
        + dense_work(width, hidden) + BACKWARD_SCRATCH(),
        15 * 10**9, setup, finish, after, [place],
    )


def last_kernel(lengths, upper, urgent, after, place):
    tokens, width = upper[0].shape

    def setup(numbers, fixed, sent, work):
        set_attention(0, fixed[0], fixed[0], 0, *work[:2])
        clear(work[2:4])

    def body(row, lengths_ref, rowwise, outs, work):
        attention_backward(
            row, lengths_ref, rowwise[0][...], *rowwise[1:6], work[0], rowwise[6], outs[0],
            *work[2:4], *work[5:],
        )

    def finish(numbers, work, sent):
        pack_attention(*work[2:4], work[4], 0)
        hand_out(numbers[0], work[4], sent)

    return run_rows(
        body, lengths, list(upper), [urgent], [struct((tokens, width), LOW)],
        [struct((64, 4 * width), LOW)] * 4,
        attention_weights(width) + attention_sums(width)
        + [vmem((4, 64, 4 * width), LOW)] + BACKWARD_SCRATCH(),
        8 * 10**9, setup, finish, after, [place],
    )


def hold(array, after):
    def kernel(*refs):
        pass

    anywhere = pl.BlockSpec(memory_space=pl.ANY)
    return pl.pallas_call(
        kernel,
        in_specs=[anywhere] * (1 + len(after)),
        out_specs=anywhere,
        out_shape=shape_of(array),
        input_output_aliases={0: 0},
    )(array, *after)


def pack_parameters(
    attn_weight, attn_bias, out_weight, ffn_in, ffn_in_bias, ffn_out, norm_gain, shifts
):
    depth, rows, width = out_weight.shape
    copies = GROUPS[1]
    hidden = ffn_in.shape[2]
    early = 4 * width + 2 * hidden + 128
    columns = 4 * width + 2 * hidden
    height = ffn_in_bias.shape[1]

    def kernel(wq_ref, ab_ref, wo_ref, wi_ref, bi_ref, wf_ref, gain_ref, shift_ref, first_ref, rest_ref, small_ref):
        def put(ref, block, at):
            block = jnp.broadcast_to(block.astype(F32)[None], (copies,) + block.shape)
            block = block.reshape(copies * block.shape[1], block.shape[2])
            ref[:, pl.ds(at, block.shape[1])] = block.astype(LOW)

        small_ref[...] = jnp.zeros(small_ref.shape, F32)
        for layer in range(depth):
            lanes = pl.ds(rows * layer, rows)
            small_ref[0:2, lanes] = ab_ref[layer].astype(F32)
            small_ref[2:4, lanes] = gain_ref[layer].astype(F32)
            small_ref[4:8, lanes] = shift_ref[layer].astype(F32)
        small_ref[0:depth, pl.ds(2 * rows, height)] = bi_ref[...].astype(F32)
        put(first_ref, wq_ref[0], 0)
        put(first_ref, small_ref[...], 3 * width)
        for layer, ref, at in ((0, first_ref, 3 * width + 128), (1, rest_ref, 3 * width)):
            if layer:
                put(ref, wq_ref[layer], 0)
            put(ref, wo_ref[layer], at)
            put(ref, wi_ref[layer], at + width)
            at += width + hidden
            down = wf_ref[layer].astype(F32)
            for step in range(hidden // width):
                put(ref, down[step * rows : (step + 1) * rows], at)
                at += width

    return pl.pallas_call(
        kernel,
        in_specs=[pl.BlockSpec(memory_space=pltpu.VMEM)] * 8,
        out_shape=[struct((copies * rows, early), LOW), struct((copies * rows, columns), LOW)],
        scratch_shapes=[vmem((rows, 128), F32)],
        compiler_params=pltpu.CompilerParams(vmem_limit_bytes=MEMORY),
    )(attn_weight, attn_bias, out_weight, ffn_in, ffn_in_bias, ffn_out, norm_gain, shifts)


def add_parts(parts, after=(), joined=None):
    inner = [] if joined is None else [joined]
    ahead = 0 if joined is None else joined.shape[1]
    rows, lanes_in = parts[0].shape
    count = len(parts)

    def kernel(*refs):
        out_ref = refs[-1]
        if inner:
            out_ref[:, pl.ds(0, ahead)] = refs[count][...]
        columns = 256
        for start in range(0, lanes_in, columns):
            size = min(columns, lanes_in - start)
            total = refs[0][:, pl.ds(start, size)].astype(F32)
            for ref in refs[1:count]:
                total = total + ref[:, pl.ds(start, size)].astype(F32)
            out_ref[:, pl.ds(ahead + start, size)] = total.astype(LOW)

    near = pl.BlockSpec(memory_space=pltpu.VMEM)
    return pl.pallas_call(
        kernel,
        in_specs=[near] * (count + len(inner)) + [pl.BlockSpec(memory_space=pl.ANY)] * len(after),
        out_specs=near,
        out_shape=struct((rows, ahead + lanes_in), LOW),
        compiler_params=pltpu.CompilerParams(vmem_limit_bytes=MEMORY),
    )(*parts, *inner, *after)


def write_gradients(place, tail, front, depth, width, hidden):
    rows = GROUPS[2]
    last = front.shape[1] - 4 * width
    height = hidden // DEVICES

    def kernel(place_ref, tail_ref, front_ref, gwq_ref, gab_ref, gwo_ref, gwi_ref, gbi_ref, gwf_ref, gain_ref, shift_ref):
        spot = place_ref[0]

        def total(ref, at, columns):
            block = ref[:, pl.ds(at, columns)].astype(F32)
            return jnp.sum(block.reshape(-1, rows, columns), 0)

        def own(block, size):
            return pltpu.roll(block, block.shape[1] - spot * size, 1)

        for layer, ref, at in ((0, front_ref, last), (1, front_ref, 0)):
            gwq_ref[layer] = total(ref, at, 3 * width)
            gab_ref[layer] = own(total(ref, at + 3 * width, width), rows)[0:2, 0:rows]
        for layer, ref, at in ((0, front_ref, 4 * width), (1, tail_ref, 0)):
            gwo_ref[layer] = total(ref, at, width)
            gwi_ref[layer] = total(ref, at + width, hidden)
            for step in range(hidden // width):
                gwf_ref[layer, pl.ds(step * rows, rows)] = total(
                    ref, at + width + hidden + step * width, width
                )
            at += width + 2 * hidden
            small = own(total(ref, at, width), rows)
            gain_ref[layer] = small[2:4, 0:rows]
            shift_ref[layer] = small[4:8, 0:rows]
            line = total(ref, at + width, hidden // 8)
            line = jnp.concatenate([line[step : step + 1] for step in range(8)], 1)
            gbi_ref[pl.ds(layer, 1)] = own(line, height)[:, 0:height]

    outs = [
        struct((depth, rows, 3 * width), F32),
        struct((depth, 2, rows), F32),
        struct((depth, rows, width), F32),
        struct((depth, rows, hidden), F32),
        struct((depth, height), F32),
        struct((depth, height, width), F32),
        struct((depth, 2, rows), F32),
        struct((depth, 4, rows), F32),
    ]
    return pl.pallas_call(
        kernel,
        in_specs=[pl.BlockSpec(memory_space=pltpu.SMEM)] + [pl.BlockSpec(memory_space=pltpu.VMEM)] * 2,
        out_shape=outs,
        compiler_params=pltpu.CompilerParams(vmem_limit_bytes=MEMORY),
    )(place, tail, front)


def exchange(parts, axis):
    return lax.all_to_all(parts, axis, 0, 0, tiled=True)


def swap(part, axis, step):
    size = lax.axis_size(axis)
    return lax.ppermute(part, axis, [(source, source ^ step) for source in range(size)])


def local(
    hidden_in,
    lengths,
    grad_out,
    attn_weight,
    attn_bias,
    out_weight,
    ffn_in,
    ffn_in_bias,
    ffn_out,
    norm_gain,
    shifts,
):
    depth, rows, width = out_weight.shape
    hidden = ffn_in.shape[2]
    first, second = lax.axis_size("dp"), lax.axis_size("fsdp")
    fits = (second, first, rows) == GROUPS
    urgent_size = 3 * width + 128
    if fits:
        early, later = pack_parameters(
            attn_weight, attn_bias, out_weight, ffn_in, ffn_in_bias, ffn_out, norm_gain, shifts
        )
        early = exchange(early, "dp")
        urgent = early[:, :urgent_size]
        parts = [urgent] + [swap(urgent, "fsdp", step) for step in range(1, second)]
        raw0 = lax.all_gather(early[:, urgent_size:], "fsdp")
        later = exchange(hold(later, (early,)), "dp")
        raw1 = lax.all_gather(hold(later, tuple(parts[1:])), "fsdp")
        place = lax.axis_index("fsdp").astype(jnp.int32).reshape(1)
    else:
        urgent, raw0, raw1 = gather_other(
            attn_weight, attn_bias, out_weight, ffn_in, ffn_in_bias, ffn_out, norm_gain, shifts
        )
        parts = [urgent[step] for step in range(urgent.shape[0])]
        place = jnp.zeros((1,), jnp.int32)

    qa0, ka0, va0, ob0, urgent = first_kernel(lengths, hidden_in, place, parts)
    n1, n2, inv, yb, gb, gp, z0 = dense_kernel(
        0, lengths, hidden_in, ob0, urgent, raw0, 0, hidden, ()
    )
    qa1, ka1, va1, ob1 = attention_kernel(1, lengths, z0, urgent, raw1, 0)
    hidden_out, dr1, dob1, sent_a = turn_kernel(
        1, lengths, z0, ob1, grad_out, urgent, raw1, 3 * width, hidden
    )
    if fits:
        tail = lax.psum_scatter(sent_a, "fsdp", scatter_dimension=0)
    dr0, dob0, *sent_b = middle_kernel(
        lengths,
        (z0, dob1, ob1, qa1, ka1, va1, dr1),
        (n1, n2, inv, yb, gb, gp, ob0),
        urgent,
        raw1,
        raw0,
        hidden,
        (sent_a,),
        place,
    )
    if fits:
        tail = exchange(hold(tail, (sent_b[0],)), "dp")
    grad_in, *sent_c = last_kernel(
        lengths, (hidden_in, dob0, ob0, qa0, ka0, va0, dr0), urgent, (sent_b[0],), place
    )
    if fits:
        got_b = [sent_b[0]] + [swap(sent_b[step], "fsdp", step) for step in range(1, second)]
        got_c = [sent_c[0]] + [swap(sent_c[step], "fsdp", step) for step in range(1, second)]
        front = add_parts(got_b, (tail,))
        front = add_parts(got_c, (), front)
        front = exchange(front, "dp")
        place = lax.axis_index(("dp", "fsdp")).astype(jnp.int32).reshape(1)
        grads = write_gradients(place, tail, front, depth, width, hidden)
    else:
        grads = scatter_other(sent_a, jnp.stack(sent_b), jnp.stack(sent_c), rows, width, hidden)
    return (hidden_out, grad_in, *grads)


def gather_other(
    attn_weight, attn_bias, out_weight, ffn_in, ffn_in_bias, ffn_out, norm_gain, shifts
):
    axes = ("dp", "fsdp")
    gather = lambda part, axis: lax.all_gather(part, axes, axis=axis, tiled=True)
    depth, unused, width = out_weight.shape
    hidden = ffn_in.shape[2]
    outer, inner, rows = GROUPS
    vectors = gather(jnp.concatenate([attn_bias, norm_gain, shifts], 1), 2)
    line = gather(ffn_in_bias, 1)

    def order(natural):
        return (
            natural.reshape(inner, outer, rows, -1).swapaxes(0, 1).reshape(outer, inner * rows, -1)
        )

    def stacked(part):
        part = part.reshape(DEVICES, -1, rows, width)
        return order(part.swapaxes(1, 2).reshape(width, -1))

    small = vectors.reshape(depth, 8, DEVICES, rows).transpose(2, 1, 0, 3).reshape(width, -1)
    line = line.reshape(depth, DEVICES, -1).swapaxes(0, 1)
    line = jnp.pad(line, ((0, 0), (0, 8 - depth), (0, 0))).reshape(width, -1)
    small = jnp.concatenate([small, line], 1)
    small = jnp.pad(small, ((0, 0), (0, 128 - small.shape[1])))
    wq, wo, wi, wf = (gather(part, 1) for part in (attn_weight, out_weight, ffn_in, ffn_out))
    urgent = jnp.concatenate([order(wq[0]), order(small)], 2)
    raw0 = jnp.concatenate([order(wo[0]), order(wi[0]), stacked(wf[0])], 2)
    raw1 = jnp.concatenate([order(wq[1]), order(wo[1]), order(wi[1]), stacked(wf[1])], 2)
    return urgent, raw0, raw1


def scatter_other(sent_a, sent_b, sent_c, own_rows, width, hidden):
    outer, inner, rows = GROUPS
    axes = ("dp", "fsdp")

    def natural(part):
        return part.reshape(outer, inner, rows, -1).swapaxes(0, 1).reshape(width, -1).astype(F32)

    def cut(part, sizes):
        found, at = [], 0
        for size in sizes:
            found.append(part[:, at : at + size])
            at += size
        return found

    dense = [width, hidden, hidden, width, hidden // 8]
    attention = [3 * width, width]
    wq0, ab0 = cut(natural(sent_c), attention)
    wq1, ab1, wo0, wi0, wf0, small0, bi0 = cut(natural(sent_b), attention + dense)
    wo1, wi1, wf1, small1, bi1 = cut(natural(sent_a), dense)

    def stacked(part):
        part = part.reshape(DEVICES, rows, -1, width).swapaxes(1, 2)
        return part.reshape(hidden, width)

    def spread(parts, axis):
        return lax.psum_scatter(jnp.stack(parts), axes, scatter_dimension=axis, tiled=True)

    return (
        spread([wq0, wq1], 1),
        spread([ab0[:2], ab1[:2]], 2),
        spread([wo0, wo1], 1),
        spread([wi0, wi1], 1),
        spread([bi0[:8].reshape(-1), bi1[:8].reshape(-1)], 1),
        spread([stacked(wf0), stacked(wf1)], 1),
        spread([small0[2:4], small1[2:4]], 2),
        spread([small0[4:8], small1[4:8]], 2),
    )


def solution(mesh):
    placed = (
        P(("dp", "fsdp"), None),
        P(("dp", "fsdp"), None),
        P(("dp", "fsdp"), None),
        P(None, ("dp", "fsdp"), None),
        P(None, None, ("dp", "fsdp")),
        P(None, ("dp", "fsdp"), None),
        P(None, ("dp", "fsdp"), None),
        P(None, ("dp", "fsdp")),
        P(None, ("dp", "fsdp"), None),
        P(None, None, ("dp", "fsdp")),
        P(None, None, ("dp", "fsdp")),
    )
    return jax.shard_map(
        local,
        mesh=mesh,
        in_specs=placed,
        out_specs=(
            P(("dp", "fsdp"), None),
            P(("dp", "fsdp"), None),
            P(None, ("dp", "fsdp"), None),
            P(None, None, ("dp", "fsdp")),
            P(None, ("dp", "fsdp"), None),
            P(None, ("dp", "fsdp"), None),
            P(None, ("dp", "fsdp")),
            P(None, ("dp", "fsdp"), None),
            P(None, None, ("dp", "fsdp")),
            P(None, None, ("dp", "fsdp")),
        ),
        check_vma=False,
    )
```

```python
from functools import partial

import jax
import jax.numpy as jnp
from jax import lax
from jax.experimental import pallas as pl
from jax.experimental.pallas import tpu as pltpu
from jax.sharding import PartitionSpec as P

HEADS = 4
HD = 64
SEQ = 512
PAIR = 2 * HD
FAR = -(2.0**100)
FLOOR = -1e20
EPSILON = 1e-12
PIECE = 256
SMALL = 128
GROUPS = (4, 8, 8)
DEVICES = 32
LOW = jnp.bfloat16
F32 = jnp.float32
MEMORY = 60 * 2**20


def dot_nn(left, right):
    return lax.dot_general(left, right, (((1,), (0,)), ((), ())), preferred_element_type=F32)


def dot_nt(left, right):
    return lax.dot_general(left, right, (((1,), (1,)), ((), ())), preferred_element_type=F32)


def dot_tn(left, right):
    return lax.dot_general(left, right, (((0,), (0,)), ((), ())), preferred_element_type=F32)


def pieces(total, size=PIECE):
    return [pl.ds(start, size) for start in range(0, total, size)]


def three_parts(values):
    first = values.astype(LOW).astype(F32)
    rest = values - first
    second = rest.astype(LOW).astype(F32)
    return first, second, rest - second


CURVE = (
    7.97882253e-01,
    3.63445176e-02,
    -4.47304308e-05,
    -5.04138899e-05,
    3.10523303e-06,
    -6.66676088e-08,
)
BELL = -0.5 / 0.6931471805599453


def gelu_parts(u):
    square = u * u
    near = jnp.minimum(square, 31.36)
    curve = CURVE[-1]
    for factor in CURVE[-2::-1]:
        curve = curve * near + factor
    bent = jnp.tanh(u * curve)
    half = 0.5 * u
    slope = (0.5 + 0.5 * bent) + (u * 0.3989422804014327) * jnp.exp2(square * BELL)
    return half + half * bent, slope


def lane_facts():
    lane = lax.broadcasted_iota(jnp.int32, (1, PAIR), 1)
    return lane < HD, lane & (HD - 1)


def segments(lengths_ref, row, start, rows):
    places = lax.broadcasted_iota(jnp.int32, (rows, 1), 0) + start
    bound = jnp.int32(0)
    segment = jnp.zeros((rows, 1), jnp.int32)
    last = lengths_ref.shape[1] - 1
    for entry in range(last):
        bound = bound + lengths_ref[row, entry]
        segment = segment + (places >= bound).astype(jnp.int32)
    return segment, (segment == last).astype(F32), last


def attention_forward(row, lengths_ref, x, wq_ref, bias_ref, qa_ref, ka_ref, va_ref, ob_ref, s_ref, p_ref, m_ref, pad_ref, q_ref, aug_ref):
    width = HEADS * HD
    for block in range(3):
        at = block * width
        value = dot_nn(x, wq_ref[:, at : at + width]) + bias_ref[:, at : at + width]
        for pair in range(HEADS // 2):
            q_ref[block, pair] = value[:, pair * PAIR : (pair + 1) * PAIR]
    for start in range(0, SEQ, PIECE):
        place = pl.ds(start, PIECE)
        low_half, slot = lane_facts()
        segment, pad, last = segments(lengths_ref, row, start, PIECE)
        pad_ref[place] = jnp.broadcast_to(pad, (PIECE, PAIR))
        aug_q = jnp.where(slot == segment, 1.0, 0.0)
        aug_ref[place] = aug_q
        seen = (slot == segment) & (slot != last)
        aug_k = jnp.where(seen, 0.0, jnp.where(slot <= last, FAR, jnp.where(slot <= last + 3, 1.0, 0.0)))
        for pair in range(HEADS // 2):
            q = q_ref[0, pair, place] * HD**-0.5
            k = q_ref[1, pair, place]
            v = q_ref[2, pair, place]
            q_ref[0, pair, place] = q
            qa_ref[2 * pair, place] = jnp.where(low_half, q, aug_q).astype(LOW)
            qa_ref[2 * pair + 1, place] = jnp.where(low_half, aug_q, q).astype(LOW)
            ka_ref[2 * pair, place] = jnp.where(low_half, k, aug_k).astype(LOW)
            ka_ref[2 * pair + 1, place] = jnp.where(low_half, aug_k, k).astype(LOW)
            va_ref[2 * pair, place] = jnp.where(low_half, v, 1.0).astype(LOW)
            va_ref[2 * pair + 1, place] = jnp.where(low_half, 1.0, v).astype(LOW)

    def scores(head):
        s_ref[head % 2] = dot_nt(qa_ref[head], ka_ref[head])

    def softmax(head):
        for place in pieces(SEQ):
            highest = jnp.maximum(jnp.max(s_ref[head % 2, place], -1, keepdims=True), FLOOR)
            m_ref[head % 2, place] = jnp.broadcast_to(highest, (PIECE, PAIR))
            p_ref[head % 2, place] = jnp.exp(s_ref[head % 2, place] - highest).astype(LOW)

    scores(0)
    for head in range(HEADS):
        if head + 1 < HEADS:
            scores(head + 1)
        softmax(head)
        q_ref[1, head % 2] = dot_nn(p_ref[head % 2], va_ref[head])
        if head % 2:
            pair = head // 2
            for start in range(0, SEQ, PIECE):
                place = pl.ds(start, PIECE)
                low_half, slot = lane_facts()
                even = q_ref[1, 0, place]
                odd = q_ref[1, 1, place]
                pad = pad_ref[place]
                last = lengths_ref.shape[1] - 1
                total = jnp.where(low_half, odd, even) + pad
                top = jnp.where(low_half, odd_even(m_ref, 1, place), odd_even(m_ref, 0, place))
                spread = jnp.where(pad > 0, 0.0, top + jnp.log(total))
                first, second, third = three_parts(spread)
                aug = jnp.where(
                    slot == last + 1,
                    -first,
                    jnp.where(slot == last + 2, -second, jnp.where(slot == last + 3, -third, aug_ref[place])),
                )
                q = q_ref[0, pair, place]
                qa_ref[2 * pair, place] = jnp.where(low_half, q, aug).astype(LOW)
                qa_ref[2 * pair + 1, place] = jnp.where(low_half, aug, q).astype(LOW)
                v = q_ref[2, pair, place].astype(LOW).astype(F32)
                out = jnp.where(low_half, even, odd) / pltpu.roll(total, HD, 1) + pad * v
                ob_ref[place, pl.ds(pair * PAIR, PAIR)] = out.astype(LOW)


def odd_even(ref, which, place):
    return ref[which, place]


def normal(values):
    centred = values - jnp.mean(values, -1, keepdims=True)
    inverse = lax.rsqrt(jnp.mean(centred * centred, -1, keepdims=True) + EPSILON)
    return centred * inverse, inverse


def normal_back(cotangent, unit, inverse, gains):
    scaled = cotangent * gains
    return inverse * (
        scaled
        - jnp.mean(scaled, -1, keepdims=True)
        - unit * jnp.mean(scaled * unit, -1, keepdims=True)
    )


def dense_forward(x_ref, ob_ref, wo_ref, wi_ref, wf_ref, small_ref, bi_ref, n1_ref, n2_ref, inv_ref, yb_ref, gb_ref, gp_ref, z_ref, work_ref, u_ref):
    small = lambda index: small_ref[pl.ds(index, 1)]
    work_ref[...] = dot_nn(ob_ref[...], wo_ref[...])
    for place in pieces(SEQ):
        unit, inverse = normal(x_ref[place].astype(F32) + work_ref[place] + small(4))
        n1_ref[place] = unit
        inv_ref[place, pl.ds(0, HD)] = jnp.broadcast_to(inverse, (PIECE, HD))
        y = unit * small(2) + small(5)
        yb_ref[place] = y.astype(LOW)
        work_ref[place] = y + small(6)
    columns = 256
    count = wi_ref.shape[1] // columns

    def into(step):
        u_ref[step % 2] = dot_nn(yb_ref[...], wi_ref[:, pl.ds(step * columns, columns)])

    into(0)
    for step in range(count):
        if step + 1 < count:
            into(step + 1)
        lanes = pl.ds(step * columns, columns)
        for place in pieces(SEQ, SMALL):
            g, slope = gelu_parts(u_ref[step % 2, place] + bi_ref[:, lanes])
            gb_ref[place, lanes] = g.astype(LOW)
            gp_ref[place, lanes] = slope.astype(LOW)
    work_ref[...] += dot_nn(gb_ref[...], wf_ref[...])
    for place in pieces(SEQ):
        unit, inverse = normal(work_ref[place])
        n2_ref[place] = unit
        inv_ref[place, pl.ds(HD, HD)] = jnp.broadcast_to(inverse, (PIECE, HD))
        z_ref[place] = (unit * small(3) + small(7)).astype(z_ref.dtype)


def fold(values):
    return jnp.sum(values.reshape(-1, 8, values.shape[-1]), 0)


def dense_backward(dz_ref, n1_ref, n2_ref, inv_ref, yb_ref, gb_ref, gp_ref, ob_ref, wo_ref, wi_ref, wf_ref, small_ref, dr_ref, dob_ref, gwo_ref, gwi_ref, gwf_ref, gsmall_ref, gbi_ref, low_ref, u_ref, du_ref, turned_ref):
    small = lambda index: small_ref[pl.ds(index, 1)]
    for place in pieces(SEQ):
        dz = dz_ref[place].astype(F32)
        unit = n2_ref[place]
        gsmall_ref[3] += fold(dz * unit)
        gsmall_ref[7] += fold(dz)
        dr = normal_back(dz, unit, inv_ref[place, pl.ds(HD, 1)], small(3))
        dr_ref[place] = dr
        df = dr.astype(LOW)
        low_ref[place] = df
        gsmall_ref[6] += fold(df.astype(F32))
    columns = 256
    count = wi_ref.shape[1] // columns

    def back(step):
        u_ref[step % 2] = dot_nt(low_ref[...], wf_ref[pl.ds(step * columns, columns)])

    back(0)
    turned_ref[0] = low_ref[...].T
    turned_ref[1] = yb_ref[...].T
    for step in range(count):
        if step + 1 < count:
            back(step + 1)
        lanes = pl.ds(step * columns, columns)
        gwf_ref[:, lanes] += dot_nn(turned_ref[0], gb_ref[:, lanes])
        for place in pieces(SEQ, SMALL):
            du = (u_ref[step % 2, place] * gp_ref[place, lanes].astype(F32)).astype(LOW)
            du_ref[place, lanes] = du
            gbi_ref[:, lanes] += fold(du.astype(F32))
        gwi_ref[:, lanes] += dot_nn(turned_ref[1], du_ref[:, lanes])
    u_ref[0] = dot_nt(du_ref[...], wi_ref[...])
    for place in pieces(SEQ):
        dy = dr_ref[place] + u_ref[0, place]
        unit = n1_ref[place]
        gsmall_ref[2] += fold(dy * unit)
        gsmall_ref[5] += fold(dy)
        dr = normal_back(dy, unit, inv_ref[place, pl.ds(0, 1)], small(2))
        dr_ref[place] = dr
        da = dr.astype(LOW)
        low_ref[place] = da
        gsmall_ref[4] += fold(da.astype(F32))
    gwo_ref[...] += dot_tn(ob_ref[...], low_ref[...])
    dob_ref[...] = dot_nt(low_ref[...], wo_ref[...]).astype(LOW)


def attention_backward(row, lengths_ref, x, dob_ref, ob_ref, qa_ref, ka_ref, va_ref, wq_ref, dr_ref, dx_ref, gwq_ref, gbias_ref, da_ref, p_ref, ds_ref, s_ref, dqkv_ref, dq_ref, pad_ref, kt_ref, dqt_ref):
    width = HEADS * HD
    low_half, slot = lane_facts()
    for start in range(0, SEQ, PIECE):
        place = pl.ds(start, PIECE)
        segment, pad, last = segments(lengths_ref, row, start, PIECE)
        pad_ref[place] = jnp.broadcast_to(pad, (PIECE, PAIR))
        for pair in range(HEADS // 2):
            lanes = pl.ds(pair * PAIR, PAIR)
            dob = dob_ref[place, lanes].astype(F32)
            product = dob * ob_ref[place, lanes].astype(F32)
            even = jnp.sum(jnp.where(low_half, product, 0.0), -1, keepdims=True)
            odd = jnp.sum(jnp.where(low_half, 0.0, product), -1, keepdims=True)
            first, second, third = three_parts(jnp.where(low_half, odd, even))
            aug = jnp.where(
                slot == 0, -first, jnp.where(slot == 1, -second, jnp.where(slot == 2, -third, 0.0))
            )
            da_ref[2 * pair, place] = jnp.where(low_half, dob, aug).astype(LOW)
            da_ref[2 * pair + 1, place] = jnp.where(low_half, aug, dob).astype(LOW)
    for pair in range(HEADS // 2):
        low_half, unused = lane_facts()
        keys = jnp.where(low_half, ka_ref[2 * pair].astype(F32), ka_ref[2 * pair + 1].astype(F32))
        kt_ref[pl.ds(pair * PAIR, PAIR)] = keys.T.astype(LOW)
    low_half, slot = lane_facts()

    def scores(head):
        s_ref[0, head % 2] = dot_nt(ka_ref[head], qa_ref[head])
        s_ref[1, head % 2] = dot_nt(va_ref[head], da_ref[head])

    def weigh(head):
        for place in pieces(SEQ, SMALL):
            p = jnp.exp(s_ref[0, head % 2, place])
            p_ref[head % 2, place] = p.astype(LOW)
            ds_ref[head % 2, place] = (p * s_ref[1, head % 2, place]).astype(LOW)

    scores(0)
    for head in range(HEADS):
        if head + 1 < HEADS:
            scores(head + 1)
        weigh(head)
        side = head % 2
        dq_ref[1, side] = dot_nn(ds_ref[head % 2], qa_ref[head])
        dq_ref[2, side] = dot_nn(p_ref[head % 2], da_ref[head])
        dqt_ref[pl.ds(side * HD, HD)] = dot_nn(kt_ref[pl.ds(head * HD, HD)], ds_ref[head % 2])
        if side:
            pair = head // 2
            dq_ref[0, 0] = dqt_ref[...].T
            for start in range(0, SEQ, PIECE):
                place = pl.ds(start, PIECE)
                dq = dq_ref[0, 0, place] * HD**-0.5
                dk = jnp.where(low_half, dq_ref[1, 0, place], dq_ref[1, 1, place])
                dv = jnp.where(low_half, dq_ref[2, 0, place], dq_ref[2, 1, place])
                dv = dv + pad_ref[place] * dob_ref[place, pl.ds(pair * PAIR, PAIR)].astype(F32)
                for block, value in enumerate((dq, dk, dv)):
                    lanes = pl.ds(block * width + pair * PAIR, PAIR)
                    value = value.astype(LOW)
                    dqkv_ref[place, lanes] = value
                    if block != 1:
                        into = pl.ds(pair * PAIR, PAIR)
                        gbias_ref[block // 2, :, into] += fold(value.astype(F32))
    gwq_ref[...] += dot_tn(x, dqkv_ref[...])
    dx_ref[...] = (dr_ref[...] + dot_nt(dqkv_ref[...], wq_ref[...])).astype(dx_ref.dtype)


def unpack_matrix(raw_ref, at, into_ref):
    width = into_ref.shape[0]
    for start in range(0, into_ref.shape[1], width):
        block = raw_ref[:, :, pl.ds(at + start, width)].astype(F32)
        block = block.reshape(GROUPS + (width,)).swapaxes(0, 1).reshape(width, width)
        into_ref[:, pl.ds(start, width)] = block.astype(LOW)


def unpack_stacked(raw_ref, at, into_ref):
    width = into_ref.shape[1]
    count = into_ref.shape[0] // width
    blocks = [
        raw_ref[:, :, pl.ds(at + step * width, width)].astype(F32).reshape(GROUPS + (width,))
        for step in range(count)
    ]
    outer, inner, rows = GROUPS
    for place in range(inner):
        part = jnp.stack([jnp.stack([block[f, place] for block in blocks]) for f in range(outer)])
        size = outer * count * rows
        into_ref[pl.ds(place * size, size)] = part.reshape(size, width).astype(LOW)


def counter(shape, axis):
    return lax.broadcasted_iota(jnp.int32, shape, axis)


def split_by(values, size):
    return lax.shift_right_logical(values, size.bit_length() - 1), values & (size - 1)


def sources(rows):
    outer, inner, height = GROUPS
    group, within = split_by(counter((rows, 1), 0), height)
    far, near = split_by(group, inner)
    return near * outer + far, within


def unpack_vectors(raw_ref, at, layer):
    outer, inner, rows = GROUPS
    total = outer * inner * rows
    raw = raw_ref[:, :, pl.ds(at, 128)].reshape(total, 128)
    owner, place = split_by(counter((1, total), 1), rows)
    pick = jnp.where(counter((128, 1), 0) == rows * layer + place, 1.0, 0.0).astype(LOW)
    device, unused = sources(total)
    spread = jnp.where(owner == device, dot_nn(raw, pick), 0.0)
    return jnp.sum(spread.reshape(outer * inner, rows, total), 0)


def unpack_hidden(raw_ref, at, layer, hidden):
    outer, inner, rows = GROUPS
    total = outer * inner * rows
    raw = raw_ref[:, :, pl.ds(at, 128)].reshape(total, 128)
    owner, place = split_by(counter((1, hidden), 1), hidden // (outer * inner))
    pick = jnp.where(counter((128, 1), 0) == 2 * rows + place, 1.0, 0.0).astype(LOW)
    device, within = sources(total)
    device = jnp.where(within == layer, device, -1)
    spread = jnp.where(owner == device, dot_nn(raw, pick), 0.0)
    return jnp.sum(spread, 0, keepdims=True)


def pack_matrix(sum_ref, sent_ref, at):
    width = sum_ref.shape[0]
    outer, inner, rows = GROUPS
    for start in range(0, sum_ref.shape[1], width):
        block = sum_ref[:, pl.ds(start, width)].reshape(inner, outer, rows, width)
        block = block.swapaxes(0, 1).reshape(outer, inner * rows, width)
        sent_ref[:, :, pl.ds(at + start, width)] = block.astype(LOW)


def pack_stacked(sum_ref, sent_ref, at):
    width = sum_ref.shape[0]
    outer, inner, rows = GROUPS
    count = sum_ref.shape[1] // width
    near = inner // count
    for step in range(count):
        block = sum_ref[:, pl.ds(step * width, width)].T
        block = block.reshape(near, outer, count, rows, width)
        for part in range(count):
            piece = jnp.stack([block[:, f, part] for f in range(outer)])
            piece = piece.reshape(outer, near * rows, width)
            sent_ref[:, pl.ds(step * near * rows, near * rows), pl.ds(at + part * width, width)] = (
                piece.astype(LOW)
            )


def pack_shared(block, sent_ref, at):
    outer, inner, rows = GROUPS
    columns = block.shape[1]
    block = jnp.broadcast_to(block[None], (outer * inner, rows, columns))
    sent_ref[:, :, pl.ds(at, columns)] = block.reshape(outer, inner * rows, columns).astype(LOW)


def pack_attention(gwq_ref, gbias_ref, sent_ref, at):
    pack_matrix(gwq_ref, sent_ref, at)
    width = gwq_ref.shape[0]
    line = lax.broadcasted_iota(jnp.int32, (8, width), 0)
    sums = [jnp.sum(gbias_ref[index], 0, keepdims=True) for index in range(2)]
    block = jnp.where(line == 0, sums[0], jnp.where(line == 1, sums[1], 0.0))
    pack_shared(block, sent_ref, at + 3 * width)


def pack_dense(gwo_ref, gwi_ref, gwf_ref, gsmall_ref, gbi_ref, sent_ref, at):
    width, hidden = gwi_ref.shape
    pack_matrix(gwo_ref, sent_ref, at)
    pack_matrix(gwi_ref, sent_ref, at + width)
    pack_stacked(gwf_ref, sent_ref, at + width + hidden)
    at = at + width + 2 * hidden
    pack_shared(jnp.sum(gsmall_ref[...], 1), sent_ref, at)
    line = jnp.sum(gbi_ref[...], 0, keepdims=True)
    size = hidden // 8
    block = jnp.concatenate([line[:, step * size : (step + 1) * size] for step in range(8)], 0)
    pack_shared(block, sent_ref, at + width)


def shape_of(array):
    return jax.ShapeDtypeStruct(array.shape, array.dtype)


def by_row(shape):
    if len(shape) == 2:
        return pl.BlockSpec((SEQ, shape[1]), lambda row: (row, 0))
    return pl.BlockSpec((None,) + tuple(shape[1:]), lambda row: (row,) + (0,) * (len(shape) - 1))


def whole(shape):
    return pl.BlockSpec(tuple(shape), lambda row: (0,) * len(shape))


def run_rows(
    body, lengths, rowwise, fixed, row_outs, sent, scratch, cost, setup, finish, after=(), scalars=()
):
    count = lengths.shape[0]
    cuts = [len(scalars), len(rowwise), len(fixed), len(after), len(row_outs), len(sent), len(scratch)]

    def kernel(lengths_ref, *refs):
        row = pl.program_id(0)
        groups = []
        at = 0
        for cut in cuts:
            groups.append(refs[at : at + cut])
            at += cut
        numbers, rows_in, fixed_in, unused, rows_out, sent_out, work = groups

        @pl.when(row == 0)
        def _():
            setup(numbers, fixed_in, sent_out, work)

        body(row, lengths_ref, rows_in, rows_out, work)

        if finish:

            @pl.when(row == count - 1)
            def _():
                finish(numbers, work, sent_out)

    return pl.pallas_call(
        kernel,
        grid=(count,),
        in_specs=[pl.BlockSpec(memory_space=pltpu.SMEM)] * (1 + len(scalars))
        + [by_row(array.shape) for array in rowwise]
        + [whole(array.shape) for array in fixed]
        + [pl.BlockSpec(memory_space=pl.ANY) for array in after],
        out_specs=[by_row(part.shape) for part in row_outs] + [whole(part.shape) for part in sent],
        out_shape=list(row_outs) + list(sent),
        scratch_shapes=list(scratch),
        compiler_params=pltpu.CompilerParams(
            dimension_semantics=("arbitrary",), vmem_limit_bytes=MEMORY
        ),
        cost_estimate=pl.CostEstimate(flops=cost, bytes_accessed=8 * 2**20, transcendentals=0),
    )(lengths, *scalars, *rowwise, *fixed, *after)


def struct(shape, dtype):
    return jax.ShapeDtypeStruct(tuple(shape), dtype)


FORWARD_SCRATCH = lambda: [
    pltpu.VMEM((2, SEQ, SEQ), F32),
    pltpu.VMEM((2, SEQ, SEQ), LOW),
    pltpu.VMEM((2, SEQ, PAIR), F32),
    pltpu.VMEM((SEQ, PAIR), F32),
    pltpu.VMEM((3, HEADS // 2, SEQ, PAIR), F32),
    pltpu.VMEM((SEQ, PAIR), F32),
]
BACKWARD_SCRATCH = lambda: [
    pltpu.VMEM((HEADS, SEQ, PAIR), LOW),
    pltpu.VMEM((2, SEQ, SEQ), LOW),
    pltpu.VMEM((2, SEQ, SEQ), LOW),
    pltpu.VMEM((2, 2, SEQ, SEQ), F32),
    pltpu.VMEM((SEQ, 3 * HEADS * HD), LOW),
    pltpu.VMEM((3, 2, SEQ, PAIR), F32),
    pltpu.VMEM((SEQ, PAIR), F32),
    pltpu.VMEM((HEADS * HD, SEQ), LOW),
    pltpu.VMEM((PAIR, SEQ), F32),
]


def attention_outs(rows, tokens, width):
    heads = (rows, HEADS, SEQ, PAIR)
    return [struct(heads, LOW)] * 3 + [struct((tokens, width), LOW)]


def dense_outs(tokens, width, hidden):
    return [
        struct((tokens, width), F32),
        struct((tokens, width), F32),
        struct((tokens, PAIR), F32),
        struct((tokens, width), LOW),
        struct((tokens, hidden), LOW),
        struct((tokens, hidden), LOW),
    ]


def vmem(shape, dtype):
    return pltpu.VMEM(tuple(shape), dtype)


def attention_weights(width):
    return [vmem((width, 3 * width), LOW), vmem((1, 3 * width), F32)]


def dense_weights(width, hidden):
    return [
        vmem((width, width), LOW),
        vmem((width, hidden), LOW),
        vmem((hidden, width), LOW),
        vmem((8, width), F32),
        vmem((1, hidden), F32),
    ]


def dense_sums(width, hidden):
    return [
        vmem((width, width), F32),
        vmem((width, hidden), F32),
        vmem((width, hidden), F32),
        vmem((8, 8, width), F32),
        vmem((8, hidden), F32),
    ]


def attention_sums(width):
    return [vmem((width, 3 * width), F32), vmem((2, 8, width), F32)]


def dense_work(width, hidden):
    return [
        vmem((SEQ, width), LOW),
        vmem((2, SEQ, width), F32),
        vmem((SEQ, hidden), LOW),
        vmem((2, width, SEQ), LOW),
    ]


def set_attention(layer, urgent_ref, raw_ref, at, wq_ref, bias_ref):
    width = wq_ref.shape[0]
    unpack_matrix(raw_ref, at, wq_ref)
    vectors = unpack_vectors(urgent_ref, 3 * width, layer)
    bias_ref[:, :width] = vectors[0:1]
    bias_ref[:, width : 2 * width] = jnp.zeros((1, width), F32)
    bias_ref[:, 2 * width :] = vectors[1:2]


def set_dense(layer, urgent_ref, raw_ref, at, wo_ref, wi_ref, wf_ref, small_ref, bi_ref):
    width, hidden = wi_ref.shape
    unpack_matrix(raw_ref, at, wo_ref)
    unpack_matrix(raw_ref, at + width, wi_ref)
    unpack_stacked(raw_ref, at + width + hidden, wf_ref)
    small_ref[...] = unpack_vectors(urgent_ref, 3 * width, layer)
    bi_ref[...] = unpack_hidden(urgent_ref, 3 * width, layer, hidden)


def clear(refs):
    for ref in refs:
        ref[...] = jnp.zeros(ref.shape, ref.dtype)


def assemble(place_ref, part_refs, into_ref):
    for step, ref in enumerate(part_refs):
        into_ref[place_ref[0] ^ step] = ref[...]


def raw_block(parts):
    return vmem((len(parts),) + parts[0].shape, LOW)


def first_kernel(lengths, x, place, parts):
    rows, (tokens, width) = lengths.shape[0], x.shape

    def setup(numbers, fixed, sent, work):
        assemble(numbers[0], fixed, sent[0])
        set_attention(0, sent[0], sent[0], 0, *work[:2])

    def body(row, lengths_ref, rowwise, outs, work):
        attention_forward(row, lengths_ref, rowwise[0][...], *work[:2], *outs, *work[2:])

    return run_rows(
        body, lengths, [x], list(parts), attention_outs(rows, tokens, width),
        [struct((len(parts),) + parts[0].shape, LOW)],
        attention_weights(width) + FORWARD_SCRATCH(), 4 * 10**9, setup, None, (), [place],
    )


def attention_kernel(layer, lengths, x, place, urgent, parts, at):
    rows, (tokens, width) = lengths.shape[0], x.shape

    def setup(numbers, fixed, sent, work):
        assemble(numbers[0], fixed[1:], work[-1])
        set_attention(layer, fixed[0], work[-1], at, *work[:2])

    def body(row, lengths_ref, rowwise, outs, work):
        attention_forward(
            row, lengths_ref, rowwise[0][...].astype(LOW), *work[:2], *outs, *work[2:-1]
        )

    return run_rows(
        body, lengths, [x], [urgent] + list(parts), attention_outs(rows, tokens, width), [],
        attention_weights(width) + FORWARD_SCRATCH() + [raw_block(parts)],
        4 * 10**9, setup, None, (), [place],
    )


def dense_kernel(layer, lengths, x, ob, place, urgent, parts, at, hidden):
    tokens, width = x.shape

    def setup(numbers, fixed, sent, work):
        assemble(numbers[0], fixed[1:], work[-1])
        set_dense(layer, fixed[0], work[-1], at, *work[:5])

    def body(row, lengths_ref, rowwise, outs, work):
        dense_forward(*rowwise, *work[:5], *outs, *work[5:-1])

    return run_rows(
        body, lengths, [x, ob], [urgent] + list(parts),
        dense_outs(tokens, width, hidden) + [struct((tokens, width), F32)], [],
        dense_weights(width, hidden)
        + [vmem((SEQ, width), F32), vmem((2, SEQ, width), F32), raw_block(parts)],
        5 * 10**9, setup, None, (), [place],
    )


def turn_kernel(layer, lengths, x, ob, cotangent, place, urgent, parts, at, hidden):
    tokens, width = x.shape
    columns = width + 2 * hidden + width + hidden // 8

    def setup(numbers, fixed, sent, work):
        assemble(numbers[0], fixed[1:], work[-1])
        set_dense(layer, fixed[0], work[-1], at, *work[:5])
        clear(work[5:10])

    def body(row, lengths_ref, rowwise, outs, work):
        x_ref, ob_ref, dz_ref = rowwise
        z_ref, dr_ref, dob_ref = outs
        weights, sums, kept = work[:5], work[5:10], work[10:16]
        work_ref, low_ref, u_ref, du_ref, turned_ref = work[16:21]
        dense_forward(x_ref, ob_ref, *weights, *kept, z_ref, work_ref, u_ref)
        dense_backward(
            dz_ref, *kept, ob_ref, *weights[:4], dr_ref, dob_ref, *sums, low_ref, u_ref, du_ref,
            turned_ref,
        )

    def finish(numbers, work, sent):
        pack_dense(*work[5:10], work[21], 0)
        hand_out(numbers[0], work[21], sent)

    kept = [vmem((SEQ,) + part.shape[1:], part.dtype) for part in dense_outs(tokens, width, hidden)]
    return run_rows(
        body, lengths, [x, ob, cotangent], [urgent] + list(parts),
        [struct((tokens, width), LOW), struct((tokens, width), F32), struct((tokens, width), LOW)],
        [struct((64, columns), LOW)] * 4,
        dense_weights(width, hidden) + dense_sums(width, hidden) + kept
        + [vmem((SEQ, width), F32)] + dense_work(width, hidden)
        + [vmem((4, 64, columns), LOW), raw_block(parts)],
        10**10, setup, finish, (), [place],
    )


def hand_out(place_ref, packed_ref, sent):
    for step, ref in enumerate(sent):
        ref[...] = packed_ref[place_ref[0] ^ step]


def middle_kernel(lengths, upper, lower, place, urgent, parts1, parts0, hidden, after):
    tokens, width = upper[0].shape
    columns = 4 * width + width + 2 * hidden + width + hidden // 8

    def setup(numbers, fixed, sent, work):
        count = len(parts1)
        assemble(numbers[0], fixed[1 : 1 + count], work[-2])
        assemble(numbers[0], fixed[1 + count :], work[-1])
        set_attention(1, fixed[0], work[-2], 0, *work[:2])
        set_dense(0, fixed[0], work[-1], 0, *work[2:7])
        clear(work[7:14])

    def body(row, lengths_ref, rowwise, outs, work):
        up, low = rowwise[:7], rowwise[7:]
        dx_ref = work[15]
        attention_backward(
            row, lengths_ref, up[0][...].astype(LOW), *up[1:6], work[0], up[6], dx_ref,
            *work[7:9], *work[20:-2],
        )
        dense_backward(dx_ref, *low, *work[2:6], *outs, *work[9:14], *work[16:20])

    def finish(numbers, work, sent):
        pack_attention(*work[7:9], work[14], 0)
        pack_dense(*work[9:14], work[14], 4 * width)
        hand_out(numbers[0], work[14], sent)

    return run_rows(
        body, lengths, list(upper) + list(lower), [urgent] + list(parts1) + list(parts0),
        [struct((tokens, width), F32), struct((tokens, width), LOW)],
        [struct((64, columns), LOW)] * 4,
        attention_weights(width) + dense_weights(width, hidden)
        + attention_sums(width) + dense_sums(width, hidden)
        + [vmem((4, 64, columns), LOW), vmem((SEQ, width), F32)]
        + dense_work(width, hidden) + BACKWARD_SCRATCH() + [raw_block(parts1), raw_block(parts0)],
        15 * 10**9, setup, finish, after, [place],
    )


def last_kernel(lengths, upper, urgent, after, place):
    tokens, width = upper[0].shape

    def setup(numbers, fixed, sent, work):
        set_attention(0, fixed[0], fixed[0], 0, *work[:2])
        clear(work[2:4])

    def body(row, lengths_ref, rowwise, outs, work):
        attention_backward(
            row, lengths_ref, rowwise[0][...], *rowwise[1:6], work[0], rowwise[6], outs[0],
            *work[2:4], *work[5:],
        )

    def finish(numbers, work, sent):
        pack_attention(*work[2:4], work[4], 0)
        hand_out(numbers[0], work[4], sent)

    return run_rows(
        body, lengths, list(upper), [urgent], [struct((tokens, width), LOW)],
        [struct((64, 4 * width), LOW)] * 4,
        attention_weights(width) + attention_sums(width)
        + [vmem((4, 64, 4 * width), LOW)] + BACKWARD_SCRATCH(),
        8 * 10**9, setup, finish, after, [place],
    )


def hold(array, after):
    def kernel(*refs):
        pass

    anywhere = pl.BlockSpec(memory_space=pl.ANY)
    return pl.pallas_call(
        kernel,
        in_specs=[anywhere] * (1 + len(after)),
        out_specs=anywhere,
        out_shape=shape_of(array),
        input_output_aliases={0: 0},
    )(array, *after)


def pack_parameters(
    attn_weight, attn_bias, out_weight, ffn_in, ffn_in_bias, ffn_out, norm_gain, shifts
):
    depth, rows, width = out_weight.shape
    copies = GROUPS[1]
    hidden = ffn_in.shape[2]
    early = 4 * width + 2 * hidden + 128
    columns = 4 * width + 2 * hidden
    height = ffn_in_bias.shape[1]

    def kernel(wq_ref, ab_ref, wo_ref, wi_ref, bi_ref, wf_ref, gain_ref, shift_ref, first_ref, rest_ref, small_ref):
        def put(ref, block, at):
            block = jnp.broadcast_to(block.astype(F32)[None], (copies,) + block.shape)
            block = block.reshape(copies * block.shape[1], block.shape[2])
            ref[:, pl.ds(at, block.shape[1])] = block.astype(LOW)

        small_ref[...] = jnp.zeros(small_ref.shape, F32)
        for layer in range(depth):
            lanes = pl.ds(rows * layer, rows)
            small_ref[0:2, lanes] = ab_ref[layer].astype(F32)
            small_ref[2:4, lanes] = gain_ref[layer].astype(F32)
            small_ref[4:8, lanes] = shift_ref[layer].astype(F32)
        small_ref[0:depth, pl.ds(2 * rows, height)] = bi_ref[...].astype(F32)
        put(first_ref, wq_ref[0], 0)
        put(first_ref, small_ref[...], 3 * width)
        for layer, ref, at in ((0, first_ref, 3 * width + 128), (1, rest_ref, 3 * width)):
            if layer:
                put(ref, wq_ref[layer], 0)
            put(ref, wo_ref[layer], at)
            put(ref, wi_ref[layer], at + width)
            at += width + hidden
            down = wf_ref[layer].astype(F32)
            for step in range(hidden // width):
                put(ref, down[step * rows : (step + 1) * rows], at)
                at += width

    return pl.pallas_call(
        kernel,
        in_specs=[pl.BlockSpec(memory_space=pltpu.VMEM)] * 8,
        out_shape=[struct((copies * rows, early), LOW), struct((copies * rows, columns), LOW)],
        scratch_shapes=[vmem((rows, 128), F32)],
        compiler_params=pltpu.CompilerParams(vmem_limit_bytes=MEMORY),
    )(attn_weight, attn_bias, out_weight, ffn_in, ffn_in_bias, ffn_out, norm_gain, shifts)


def add_parts(parts, after=(), joined=None):
    inner = [] if joined is None else [joined]
    ahead = 0 if joined is None else joined.shape[1]
    rows, lanes_in = parts[0].shape
    count = len(parts)

    def kernel(*refs):
        out_ref = refs[-1]
        if inner:
            out_ref[:, pl.ds(0, ahead)] = refs[count][...]
        columns = 256
        for start in range(0, lanes_in, columns):
            size = min(columns, lanes_in - start)
            total = refs[0][:, pl.ds(start, size)].astype(F32)
            for ref in refs[1:count]:
                total = total + ref[:, pl.ds(start, size)].astype(F32)
            out_ref[:, pl.ds(ahead + start, size)] = total.astype(LOW)

    near = pl.BlockSpec(memory_space=pltpu.VMEM)
    return pl.pallas_call(
        kernel,
        in_specs=[near] * (count + len(inner)) + [pl.BlockSpec(memory_space=pl.ANY)] * len(after),
        out_specs=near,
        out_shape=struct((rows, ahead + lanes_in), LOW),
        compiler_params=pltpu.CompilerParams(vmem_limit_bytes=MEMORY),
    )(*parts, *inner, *after)


def write_gradients(place, tail, front, depth, width, hidden):
    rows = GROUPS[2]
    last = front.shape[1] - 4 * width
    height = hidden // DEVICES

    def kernel(place_ref, tail_ref, front_ref, gwq_ref, gab_ref, gwo_ref, gwi_ref, gbi_ref, gwf_ref, gain_ref, shift_ref):
        spot = place_ref[0]

        def total(ref, at, columns):
            block = ref[:, pl.ds(at, columns)].astype(F32)
            return jnp.sum(block.reshape(-1, rows, columns), 0)

        def own(block, size):
            return pltpu.roll(block, block.shape[1] - spot * size, 1)

        for layer, ref, at in ((0, front_ref, last), (1, front_ref, 0)):
            gwq_ref[layer] = total(ref, at, 3 * width)
            gab_ref[layer] = own(total(ref, at + 3 * width, width), rows)[0:2, 0:rows]
        for layer, ref, at in ((0, front_ref, 4 * width), (1, tail_ref, 0)):
            gwo_ref[layer] = total(ref, at, width)
            gwi_ref[layer] = total(ref, at + width, hidden)
            for step in range(hidden // width):
                gwf_ref[layer, pl.ds(step * rows, rows)] = total(
                    ref, at + width + hidden + step * width, width
                )
            at += width + 2 * hidden
            small = own(total(ref, at, width), rows)
            gain_ref[layer] = small[2:4, 0:rows]
            shift_ref[layer] = small[4:8, 0:rows]
            line = total(ref, at + width, hidden // 8)
            line = jnp.concatenate([line[step : step + 1] for step in range(8)], 1)
            gbi_ref[pl.ds(layer, 1)] = own(line, height)[:, 0:height]

    outs = [
        struct((depth, rows, 3 * width), F32),
        struct((depth, 2, rows), F32),
        struct((depth, rows, width), F32),
        struct((depth, rows, hidden), F32),
        struct((depth, height), F32),
        struct((depth, height, width), F32),
        struct((depth, 2, rows), F32),
        struct((depth, 4, rows), F32),
    ]
    return pl.pallas_call(
        kernel,
        in_specs=[pl.BlockSpec(memory_space=pltpu.SMEM)] + [pl.BlockSpec(memory_space=pltpu.VMEM)] * 2,
        out_shape=outs,
        compiler_params=pltpu.CompilerParams(vmem_limit_bytes=MEMORY),
    )(place, tail, front)


def exchange(parts, axis):
    return lax.all_to_all(parts, axis, 0, 0, tiled=True)


def swap(part, axis, step):
    size = lax.axis_size(axis)
    return lax.ppermute(part, axis, [(source, source ^ step) for source in range(size)])


def local(
    hidden_in,
    lengths,
    grad_out,
    attn_weight,
    attn_bias,
    out_weight,
    ffn_in,
    ffn_in_bias,
    ffn_out,
    norm_gain,
    shifts,
):
    depth, rows, width = out_weight.shape
    hidden = ffn_in.shape[2]
    first, second = lax.axis_size("dp"), lax.axis_size("fsdp")
    fits = (second, first, rows) == GROUPS
    urgent_size = 3 * width + 128
    if fits:
        early, later = pack_parameters(
            attn_weight, attn_bias, out_weight, ffn_in, ffn_in_bias, ffn_out, norm_gain, shifts
        )
        early = exchange(early, "dp")
        partners = range(1, second)
        urgent = early[:, :urgent_size]
        urgent = [urgent] + [swap(urgent, "fsdp", step) for step in partners]
        later = exchange(hold(later, (early,)), "dp")
        raw0 = hold(early[:, urgent_size:], tuple(urgent))
        raw0 = [raw0] + [swap(raw0, "fsdp", step) for step in partners]
        place = lax.axis_index("fsdp").astype(jnp.int32).reshape(1)
    else:
        urgent, raw0, raw1 = gather_other(
            attn_weight, attn_bias, out_weight, ffn_in, ffn_in_bias, ffn_out, norm_gain, shifts
        )
        urgent, raw0, raw1 = ([part[step] for step in range(4)] for part in (urgent, raw0, raw1))
        place = jnp.zeros((1,), jnp.int32)

    qa0, ka0, va0, ob0, urgent = first_kernel(lengths, hidden_in, place, urgent)
    if fits:
        raw1 = hold(later, (ob0,))
        raw1 = [raw1] + [swap(raw1, "fsdp", step) for step in partners]
    n1, n2, inv, yb, gb, gp, z0 = dense_kernel(
        0, lengths, hidden_in, ob0, place, urgent, raw0, 0, hidden
    )
    qa1, ka1, va1, ob1 = attention_kernel(1, lengths, z0, place, urgent, raw1, 0)
    hidden_out, dr1, dob1, *sent_a = turn_kernel(
        1, lengths, z0, ob1, grad_out, place, urgent, raw1, 3 * width, hidden
    )
    dr0, dob0, *sent_b = middle_kernel(
        lengths,
        (z0, dob1, ob1, qa1, ka1, va1, dr1),
        (n1, n2, inv, yb, gb, gp, ob0),
        place,
        urgent,
        raw1,
        raw0,
        hidden,
        (sent_a[0],),
    )
    if fits:
        got_a = [sent_a[0]] + [swap(sent_a[step], "fsdp", step) for step in partners]
        tail = exchange(add_parts(got_a, (sent_b[0],)), "dp")
    grad_in, *sent_c = last_kernel(
        lengths, (hidden_in, dob0, ob0, qa0, ka0, va0, dr0), urgent, (sent_b[0],), place
    )
    if fits:
        got_b = [sent_b[0]] + [swap(sent_b[step], "fsdp", step) for step in partners]
        got_c = [sent_c[0]] + [swap(sent_c[step], "fsdp", step) for step in partners]
        front = add_parts(got_b, (tail,))
        front = add_parts(got_c, (), front)
        front = exchange(front, "dp")
        place = lax.axis_index(("dp", "fsdp")).astype(jnp.int32).reshape(1)
        grads = write_gradients(place, tail, front, depth, width, hidden)
    else:
        grads = scatter_other(
            *(jnp.stack(part) for part in (sent_a, sent_b, sent_c)), rows, width, hidden
        )
    return (hidden_out, grad_in, *grads)


def gather_other(
    attn_weight, attn_bias, out_weight, ffn_in, ffn_in_bias, ffn_out, norm_gain, shifts
):
    axes = ("dp", "fsdp")
    gather = lambda part, axis: lax.all_gather(part, axes, axis=axis, tiled=True)
    depth, unused, width = out_weight.shape
    hidden = ffn_in.shape[2]
    outer, inner, rows = GROUPS
    vectors = gather(jnp.concatenate([attn_bias, norm_gain, shifts], 1), 2)
    line = gather(ffn_in_bias, 1)

    def order(natural):
        return (
            natural.reshape(inner, outer, rows, -1).swapaxes(0, 1).reshape(outer, inner * rows, -1)
        )

    def stacked(part):
        part = part.reshape(DEVICES, -1, rows, width)
        return order(part.swapaxes(1, 2).reshape(width, -1))

    small = vectors.reshape(depth, 8, DEVICES, rows).transpose(2, 1, 0, 3).reshape(width, -1)
    line = line.reshape(depth, DEVICES, -1).swapaxes(0, 1)
    line = jnp.pad(line, ((0, 0), (0, 8 - depth), (0, 0))).reshape(width, -1)
    small = jnp.concatenate([small, line], 1)
    small = jnp.pad(small, ((0, 0), (0, 128 - small.shape[1])))
    wq, wo, wi, wf = (gather(part, 1) for part in (attn_weight, out_weight, ffn_in, ffn_out))
    urgent = jnp.concatenate([order(wq[0]), order(small)], 2)
    raw0 = jnp.concatenate([order(wo[0]), order(wi[0]), stacked(wf[0])], 2)
    raw1 = jnp.concatenate([order(wq[1]), order(wo[1]), order(wi[1]), stacked(wf[1])], 2)
    return urgent, raw0, raw1


def scatter_other(sent_a, sent_b, sent_c, own_rows, width, hidden):
    outer, inner, rows = GROUPS
    axes = ("dp", "fsdp")

    def natural(part):
        return part.reshape(outer, inner, rows, -1).swapaxes(0, 1).reshape(width, -1).astype(F32)

    def cut(part, sizes):
        found, at = [], 0
        for size in sizes:
            found.append(part[:, at : at + size])
            at += size
        return found

    dense = [width, hidden, hidden, width, hidden // 8]
    attention = [3 * width, width]
    wq0, ab0 = cut(natural(sent_c), attention)
    wq1, ab1, wo0, wi0, wf0, small0, bi0 = cut(natural(sent_b), attention + dense)
    wo1, wi1, wf1, small1, bi1 = cut(natural(sent_a), dense)

    def stacked(part):
        part = part.reshape(DEVICES, rows, -1, width).swapaxes(1, 2)
        return part.reshape(hidden, width)

    def spread(parts, axis):
        return lax.psum_scatter(jnp.stack(parts), axes, scatter_dimension=axis, tiled=True)

    return (
        spread([wq0, wq1], 1),
        spread([ab0[:2], ab1[:2]], 2),
        spread([wo0, wo1], 1),
        spread([wi0, wi1], 1),
        spread([bi0[:8].reshape(-1), bi1[:8].reshape(-1)], 1),
        spread([stacked(wf0), stacked(wf1)], 1),
        spread([small0[2:4], small1[2:4]], 2),
        spread([small0[4:8], small1[4:8]], 2),
    )


def solution(mesh):
    placed = (
        P(("dp", "fsdp"), None),
        P(("dp", "fsdp"), None),
        P(("dp", "fsdp"), None),
        P(None, ("dp", "fsdp"), None),
        P(None, None, ("dp", "fsdp")),
        P(None, ("dp", "fsdp"), None),
        P(None, ("dp", "fsdp"), None),
        P(None, ("dp", "fsdp")),
        P(None, ("dp", "fsdp"), None),
        P(None, None, ("dp", "fsdp")),
        P(None, None, ("dp", "fsdp")),
    )
    return jax.shard_map(
        local,
        mesh=mesh,
        in_specs=placed,
        out_specs=(
            P(("dp", "fsdp"), None),
            P(("dp", "fsdp"), None),
            P(None, ("dp", "fsdp"), None),
            P(None, None, ("dp", "fsdp")),
            P(None, ("dp", "fsdp"), None),
            P(None, ("dp", "fsdp"), None),
            P(None, ("dp", "fsdp")),
            P(None, ("dp", "fsdp"), None),
            P(None, None, ("dp", "fsdp")),
            P(None, None, ("dp", "fsdp")),
        ),
        check_vma=False,
    )
```

```python
from functools import partial

import jax
import jax.numpy as jnp
from jax import lax
from jax.experimental import pallas as pl
from jax.experimental.pallas import tpu as pltpu
from jax.sharding import PartitionSpec as P

HEADS = 4
HD = 64
SEQ = 512
PAIR = 2 * HD
FAR = -(2.0**100)
FLOOR = -1e20
EPSILON = 1e-12
PIECE = 256
SMALL = 128
GROUPS = (4, 8, 8)
DEVICES = 32
LOW = jnp.bfloat16
F32 = jnp.float32
MEMORY = 127 * 2**19


def dot_nn(left, right):
    return lax.dot_general(left, right, (((1,), (0,)), ((), ())), preferred_element_type=F32)


def dot_nt(left, right):
    return lax.dot_general(left, right, (((1,), (1,)), ((), ())), preferred_element_type=F32)


def dot_tn(left, right):
    return lax.dot_general(left, right, (((0,), (0,)), ((), ())), preferred_element_type=F32)


def pieces(total, size=PIECE):
    return [pl.ds(start, size) for start in range(0, total, size)]


def three_parts(values):
    first = values.astype(LOW).astype(F32)
    rest = values - first
    second = rest.astype(LOW).astype(F32)
    return first, second, rest - second


CURVE = (7.97869556e-01, 3.63928094e-02, -8.82195179e-05, -3.66000319e-05, 1.41853144e-06)
BELL = -0.5 / 0.6931471805599453


def gelu_parts(u):
    square = u * u
    curve = CURVE[-1]
    for factor in CURVE[-2::-1]:
        curve = curve * square + factor
    cumulative = 0.5 + 0.5 * jnp.tanh(u * curve)
    slope = cumulative + (u * 0.3989422804014327) * jnp.exp2(square * BELL)
    return u * cumulative, slope


def inverse_of(values):
    guess = pl.reciprocal(values, approx=True)
    return guess * (2.0 - values * guess)


def lane_facts():
    lane = lax.broadcasted_iota(jnp.int32, (1, PAIR), 1)
    return lane < HD, lane & (HD - 1)


def segments(lengths_ref, row, start, rows):
    places = lax.broadcasted_iota(jnp.int32, (rows, 1), 0) + start
    bound = jnp.int32(0)
    segment = jnp.zeros((rows, 1), jnp.int32)
    last = lengths_ref.shape[1] - 1
    for entry in range(last):
        bound = bound + lengths_ref[row, entry]
        segment = segment + (places >= bound).astype(jnp.int32)
    return segment, (segment == last).astype(F32), last


def attention_forward(row, lengths_ref, x, wq_ref, bias_ref, qa_ref, ka_ref, va_ref, ob_ref, s_ref, p_ref, m_ref, pad_ref, q_ref, aug_ref):
    width = HEADS * HD
    half = SEQ // 2
    last = lengths_ref.shape[1] - 1
    low_half, slot = lane_facts()
    for block in range(3):
        at = block * width
        value = dot_nn(x, wq_ref[:, at : at + width]) + bias_ref[:, at : at + width]
        for pair in range(HEADS // 2):
            q_ref[block, pair] = value[:, pair * PAIR : (pair + 1) * PAIR]

    def lay(step, carry):
        start = pl.multiple_of(step * SMALL, SMALL)
        place = pl.ds(start, SMALL)
        segment, pad, unused = segments(lengths_ref, row, start, SMALL)
        pad_ref[place] = jnp.broadcast_to(pad, (SMALL, PAIR))
        aug_q = jnp.where(slot == segment, 1.0, 0.0)
        aug_ref[place] = aug_q
        seen = (slot == segment) & (slot != last)
        aug_k = jnp.where(seen, 0.0, jnp.where(slot <= last, FAR, jnp.where(slot <= last + 3, 1.0, 0.0)))
        for pair in range(HEADS // 2):
            q = q_ref[0, pair, place] * HD**-0.5
            k = q_ref[1, pair, place]
            v = q_ref[2, pair, place]
            q_ref[0, pair, place] = q
            qa_ref[2 * pair, place] = jnp.where(low_half, q, aug_q).astype(LOW)
            qa_ref[2 * pair + 1, place] = jnp.where(low_half, aug_q, q).astype(LOW)
            ka_ref[2 * pair, place] = jnp.where(low_half, k, aug_k).astype(LOW)
            ka_ref[2 * pair + 1, place] = jnp.where(low_half, aug_k, k).astype(LOW)
            va_ref[2 * pair, place] = jnp.where(low_half, v, 1.0).astype(LOW)
            va_ref[2 * pair + 1, place] = jnp.where(low_half, 1.0, v).astype(LOW)
        return carry

    lax.fori_loop(0, SEQ // SMALL, lay, 0)

    def both_heads(pair, carry):
        def scores(unit):
            head = 2 * pair + unit // 2
            s_ref[unit] = dot_nt(qa_ref[head, pl.ds(unit % 2 * half, half)], ka_ref[head])

        def softmax(unit):
            side, start = unit // 2, unit % 2 * half
            for at in range(0, half, SMALL):
                place = pl.ds(at, SMALL)
                highest = jnp.maximum(jnp.max(s_ref[unit, place], -1, keepdims=True), FLOOR)
                m_ref[side, pl.ds(start + at, SMALL)] = jnp.broadcast_to(highest, (SMALL, PAIR))
                p_ref[unit, place] = jnp.exp(s_ref[unit, place] - highest).astype(LOW)

        scores(0)
        for unit in range(4):
            if unit < 3:
                scores(unit + 1)
            softmax(unit)
            side, start = unit // 2, unit % 2 * half
            q_ref[1, side, pl.ds(start, half)] = dot_nn(p_ref[unit], va_ref[2 * pair + side])
        lanes = pl.ds(pl.multiple_of(pair * PAIR, PAIR), PAIR)
        for place in pieces(SEQ, SMALL):
            even = q_ref[1, 0, place]
            odd = q_ref[1, 1, place]
            pad = pad_ref[place]
            total = jnp.where(low_half, odd, even) + pad
            top = jnp.where(low_half, m_ref[1, place], m_ref[0, place])
            spread = jnp.where(pad > 0, 0.0, top + jnp.log(total))
            first, second, third = three_parts(spread)
            aug = jnp.where(
                slot == last + 1,
                -first,
                jnp.where(slot == last + 2, -second, jnp.where(slot == last + 3, -third, aug_ref[place])),
            )
            q = q_ref[0, pair, place]
            qa_ref[2 * pair, place] = jnp.where(low_half, q, aug).astype(LOW)
            qa_ref[2 * pair + 1, place] = jnp.where(low_half, aug, q).astype(LOW)
            v = q_ref[2, pair, place].astype(LOW).astype(F32)
            share = inverse_of(pltpu.roll(total, HD, 1))
            ob_ref[place, lanes] = (jnp.where(low_half, even, odd) * share + pad * v).astype(LOW)
        return carry

    lax.fori_loop(0, HEADS // 2, both_heads, 0)


def normal(values):
    centred = values - jnp.mean(values, -1, keepdims=True)
    inverse = lax.rsqrt(jnp.mean(centred * centred, -1, keepdims=True) + EPSILON)
    return centred * inverse, inverse


def normal_back(cotangent, unit, inverse, gains):
    scaled = cotangent * gains
    return inverse * (
        scaled
        - jnp.mean(scaled, -1, keepdims=True)
        - unit * jnp.mean(scaled * unit, -1, keepdims=True)
    )


def dense_forward(x_ref, ob_ref, wo_ref, wi_ref, wf_ref, small_ref, bi_ref, n1_ref, n2_ref, inv_ref, yb_ref, gb_ref, gp_ref, z_ref, work_ref, u_ref):
    small = lambda index: small_ref[pl.ds(index, 1)]
    work_ref[...] = dot_nn(ob_ref[...], wo_ref[...])
    for place in pieces(SEQ):
        unit, inverse = normal(x_ref[place].astype(F32) + work_ref[place] + small(4))
        n1_ref[place] = unit
        inv_ref[place, pl.ds(0, HD)] = jnp.broadcast_to(inverse, (PIECE, HD))
        y = unit * small(2) + small(5)
        yb_ref[place] = y.astype(LOW)
        work_ref[place] = y + small(6)
    columns = 256
    count = wi_ref.shape[1] // columns

    def into(step):
        u_ref[step % 2] = dot_nn(yb_ref[...], wi_ref[:, pl.ds(step * columns, columns)])

    into(0)
    for step in range(count):
        if step + 1 < count:
            into(step + 1)
        lanes = pl.ds(step * columns, columns)
        for place in pieces(SEQ, SMALL):
            g, slope = gelu_parts(u_ref[step % 2, place] + bi_ref[:, lanes])
            gb_ref[place, lanes] = g.astype(LOW)
            gp_ref[place, lanes] = slope.astype(LOW)
    work_ref[...] += dot_nn(gb_ref[...], wf_ref[...])
    for place in pieces(SEQ):
        unit, inverse = normal(work_ref[place])
        n2_ref[place] = unit
        inv_ref[place, pl.ds(HD, HD)] = jnp.broadcast_to(inverse, (PIECE, HD))
        z_ref[place] = (unit * small(3) + small(7)).astype(z_ref.dtype)


def fold(values):
    return jnp.sum(values.reshape(-1, 8, values.shape[-1]), 0)


def dense_backward(dz_ref, n1_ref, n2_ref, inv_ref, yb_ref, gb_ref, gp_ref, ob_ref, wo_ref, wi_ref, wf_ref, small_ref, dr_ref, dob_ref, gwo_ref, gwi_ref, gwf_ref, gsmall_ref, gbi_ref, low_ref, u_ref, du_ref, turned_ref):
    small = lambda index: small_ref[pl.ds(index, 1)]
    for place in pieces(SEQ):
        dz = dz_ref[place].astype(F32)
        unit = n2_ref[place]
        gsmall_ref[3] += fold(dz * unit)
        gsmall_ref[7] += fold(dz)
        dr = normal_back(dz, unit, inv_ref[place, pl.ds(HD, 1)], small(3))
        dr_ref[place] = dr
        df = dr.astype(LOW)
        low_ref[place] = df
        gsmall_ref[6] += fold(df.astype(F32))
    columns = 256
    count = wi_ref.shape[1] // columns

    def back(step):
        u_ref[step % 2] = dot_nt(low_ref[...], wf_ref[pl.ds(step * columns, columns)])

    back(0)
    turned_ref[0] = low_ref[...].T
    turned_ref[1] = yb_ref[...].T
    for step in range(count):
        if step + 1 < count:
            back(step + 1)
        lanes = pl.ds(step * columns, columns)
        gwf_ref[:, lanes] += dot_nn(turned_ref[0], gb_ref[:, lanes])
        for place in pieces(SEQ, SMALL):
            du = (u_ref[step % 2, place] * gp_ref[place, lanes].astype(F32)).astype(LOW)
            du_ref[place, lanes] = du
            gbi_ref[:, lanes] += fold(du.astype(F32))
        gwi_ref[:, lanes] += dot_nn(turned_ref[1], du_ref[:, lanes])
    u_ref[0] = dot_nt(du_ref[...], wi_ref[...])
    for place in pieces(SEQ):
        dy = dr_ref[place] + u_ref[0, place]
        unit = n1_ref[place]
        gsmall_ref[2] += fold(dy * unit)
        gsmall_ref[5] += fold(dy)
        dr = normal_back(dy, unit, inv_ref[place, pl.ds(0, 1)], small(2))
        dr_ref[place] = dr
        da = dr.astype(LOW)
        low_ref[place] = da
        gsmall_ref[4] += fold(da.astype(F32))
    gwo_ref[...] += dot_tn(ob_ref[...], low_ref[...])
    dob_ref[...] = dot_nt(low_ref[...], wo_ref[...]).astype(LOW)


def attention_backward(row, lengths_ref, x, dob_ref, ob_ref, qa_ref, ka_ref, va_ref, wq_ref, dr_ref, dx_ref, gwq_ref, gbias_ref, da_ref, p_ref, ds_ref, s_ref, dqkv_ref, dq_ref, pad_ref, kt_ref, dqt_ref):
    width = HEADS * HD
    half = SEQ // 2
    low_half, slot = lane_facts()

    def lay(step, carry):
        start = pl.multiple_of(step * SMALL, SMALL)
        place = pl.ds(start, SMALL)
        segment, pad, last = segments(lengths_ref, row, start, SMALL)
        pad_ref[place] = jnp.broadcast_to(pad, (SMALL, PAIR))
        for pair in range(HEADS // 2):
            lanes = pl.ds(pair * PAIR, PAIR)
            dob = dob_ref[place, lanes].astype(F32)
            product = dob * ob_ref[place, lanes].astype(F32)
            even = jnp.sum(jnp.where(low_half, product, 0.0), -1, keepdims=True)
            odd = jnp.sum(jnp.where(low_half, 0.0, product), -1, keepdims=True)
            first, second, third = three_parts(jnp.where(low_half, odd, even))
            aug = jnp.where(
                slot == 0, -first, jnp.where(slot == 1, -second, jnp.where(slot == 2, -third, 0.0))
            )
            da_ref[2 * pair, place] = jnp.where(low_half, dob, aug).astype(LOW)
            da_ref[2 * pair + 1, place] = jnp.where(low_half, aug, dob).astype(LOW)
        return carry

    lax.fori_loop(0, SEQ // SMALL, lay, 0)

    def both_heads(pair, carry):
        keys = jnp.where(low_half, ka_ref[2 * pair].astype(F32), ka_ref[2 * pair + 1].astype(F32))
        kt_ref[...] = keys.T.astype(LOW)

        def scores(unit):
            head = 2 * pair + unit // 2
            rows = pl.ds(unit % 2 * half, half)
            s_ref[0, unit] = dot_nt(ka_ref[head, rows], qa_ref[head])
            s_ref[1, unit] = dot_nt(va_ref[head, rows], da_ref[head])

        def weigh(unit):
            for place in pieces(half, SMALL):
                p = jnp.exp(s_ref[0, unit, place])
                p_ref[unit, place] = p.astype(LOW)
                ds_ref[unit, place] = (p * s_ref[1, unit, place]).astype(LOW)

        scores(0)
        for unit in range(4):
            if unit < 3:
                scores(unit + 1)
            weigh(unit)
            side, part = unit // 2, unit % 2
            head = 2 * pair + side
            rows = pl.ds(part * half, half)
            dq_ref[1, side, rows] = dot_nn(ds_ref[unit], qa_ref[head])
            dq_ref[2, side, rows] = dot_nn(p_ref[unit], da_ref[head])
            lines = pl.ds(side * HD, HD)
            dq = dot_nn(kt_ref[lines, rows], ds_ref[unit])
            if part:
                dqt_ref[lines] += dq
            else:
                dqt_ref[lines] = dq
        dq_ref[0, 0] = dqt_ref[...].T
        into = pl.ds(pl.multiple_of(pair * PAIR, PAIR), PAIR)
        for place in pieces(SEQ, SMALL):
            dq = dq_ref[0, 0, place] * HD**-0.5
            dk = jnp.where(low_half, dq_ref[1, 0, place], dq_ref[1, 1, place])
            dv = jnp.where(low_half, dq_ref[2, 0, place], dq_ref[2, 1, place])
            dv = dv + pad_ref[place] * dob_ref[place, into].astype(F32)
            for block, value in enumerate((dq, dk, dv)):
                lanes = pl.ds(pl.multiple_of(block * width + pair * PAIR, PAIR), PAIR)
                value = value.astype(LOW)
                dqkv_ref[place, lanes] = value
                if block != 1:
                    gbias_ref[block // 2, :, into] += fold(value.astype(F32))
        return carry

    lax.fori_loop(0, HEADS // 2, both_heads, 0)
    gwq_ref[...] += dot_tn(x, dqkv_ref[...])
    dx_ref[...] = (dr_ref[...] + dot_nt(dqkv_ref[...], wq_ref[...])).astype(dx_ref.dtype)


def unpack_matrix(raw_ref, at, into_ref):
    width = into_ref.shape[0]
    for start in range(0, into_ref.shape[1], width):
        block = raw_ref[:, :, pl.ds(at + start, width)].astype(F32)
        block = block.reshape(GROUPS + (width,)).swapaxes(0, 1).reshape(width, width)
        into_ref[:, pl.ds(start, width)] = block.astype(LOW)


def unpack_stacked(raw_ref, at, into_ref):
    width = into_ref.shape[1]
    count = into_ref.shape[0] // width
    blocks = [
        raw_ref[:, :, pl.ds(at + step * width, width)].astype(F32).reshape(GROUPS + (width,))
        for step in range(count)
    ]
    outer, inner, rows = GROUPS
    for place in range(inner):
        part = jnp.stack([jnp.stack([block[f, place] for block in blocks]) for f in range(outer)])
        size = outer * count * rows
        into_ref[pl.ds(place * size, size)] = part.reshape(size, width).astype(LOW)


def counter(shape, axis):
    return lax.broadcasted_iota(jnp.int32, shape, axis)


def split_by(values, size):
    return lax.shift_right_logical(values, size.bit_length() - 1), values & (size - 1)


def sources(rows):
    outer, inner, height = GROUPS
    group, within = split_by(counter((rows, 1), 0), height)
    far, near = split_by(group, inner)
    return near * outer + far, within


def unpack_vectors(raw_ref, at, layer):
    outer, inner, rows = GROUPS
    total = outer * inner * rows
    raw = raw_ref[:, :, pl.ds(at, 128)].reshape(total, 128)
    owner, place = split_by(counter((1, total), 1), rows)
    pick = jnp.where(counter((128, 1), 0) == rows * layer + place, 1.0, 0.0).astype(LOW)
    device, unused = sources(total)
    spread = jnp.where(owner == device, dot_nn(raw, pick), 0.0)
    return jnp.sum(spread.reshape(outer * inner, rows, total), 0)


def unpack_hidden(raw_ref, at, layer, hidden):
    outer, inner, rows = GROUPS
    total = outer * inner * rows
    raw = raw_ref[:, :, pl.ds(at, 128)].reshape(total, 128)
    owner, place = split_by(counter((1, hidden), 1), hidden // (outer * inner))
    pick = jnp.where(counter((128, 1), 0) == 2 * rows + place, 1.0, 0.0).astype(LOW)
    device, within = sources(total)
    device = jnp.where(within == layer, device, -1)
    spread = jnp.where(owner == device, dot_nn(raw, pick), 0.0)
    return jnp.sum(spread, 0, keepdims=True)


def pack_matrix(sum_ref, sent_ref, at):
    width = sum_ref.shape[0]
    outer, inner, rows = GROUPS
    for start in range(0, sum_ref.shape[1], width):
        block = sum_ref[:, pl.ds(start, width)].reshape(inner, outer, rows, width)
        block = block.swapaxes(0, 1).reshape(outer, inner * rows, width)
        sent_ref[:, :, pl.ds(at + start, width)] = block.astype(LOW)


def pack_stacked(sum_ref, sent_ref, at):
    width = sum_ref.shape[0]
    outer, inner, rows = GROUPS
    count = sum_ref.shape[1] // width
    near = inner // count
    for step in range(count):
        block = sum_ref[:, pl.ds(step * width, width)].T
        block = block.reshape(near, outer, count, rows, width)
        for part in range(count):
            piece = jnp.stack([block[:, f, part] for f in range(outer)])
            piece = piece.reshape(outer, near * rows, width)
            sent_ref[:, pl.ds(step * near * rows, near * rows), pl.ds(at + part * width, width)] = (
                piece.astype(LOW)
            )


def pack_shared(block, sent_ref, at):
    outer, inner, rows = GROUPS
    columns = block.shape[1]
    block = jnp.broadcast_to(block[None], (outer * inner, rows, columns))
    sent_ref[:, :, pl.ds(at, columns)] = block.reshape(outer, inner * rows, columns).astype(LOW)


def pack_attention(gwq_ref, gbias_ref, sent_ref, at):
    pack_matrix(gwq_ref, sent_ref, at)
    width = gwq_ref.shape[0]
    line = lax.broadcasted_iota(jnp.int32, (8, width), 0)
    sums = [jnp.sum(gbias_ref[index], 0, keepdims=True) for index in range(2)]
    block = jnp.where(line == 0, sums[0], jnp.where(line == 1, sums[1], 0.0))
    pack_shared(block, sent_ref, at + 3 * width)


def pack_dense(gwo_ref, gwi_ref, gwf_ref, gsmall_ref, gbi_ref, sent_ref, at):
    width, hidden = gwi_ref.shape
    pack_matrix(gwo_ref, sent_ref, at)
    pack_matrix(gwi_ref, sent_ref, at + width)
    pack_stacked(gwf_ref, sent_ref, at + width + hidden)
    at = at + width + 2 * hidden
    pack_shared(jnp.sum(gsmall_ref[...], 1), sent_ref, at)
    line = jnp.sum(gbi_ref[...], 0, keepdims=True)
    size = hidden // 8
    block = jnp.concatenate([line[:, step * size : (step + 1) * size] for step in range(8)], 0)
    pack_shared(block, sent_ref, at + width)


def shape_of(array):
    return jax.ShapeDtypeStruct(array.shape, array.dtype)


def by_row(shape):
    if len(shape) == 2:
        return pl.BlockSpec((SEQ, shape[1]), lambda row: (row, 0))
    return pl.BlockSpec((None,) + tuple(shape[1:]), lambda row: (row,) + (0,) * (len(shape) - 1))


def whole(shape):
    return pl.BlockSpec(tuple(shape), lambda row: (0,) * len(shape))


def run_rows(
    body, lengths, rowwise, fixed, row_outs, sent, scratch, cost, setup, finish, after=(), scalars=()
):
    count = lengths.shape[0]
    cuts = [len(scalars), len(rowwise), len(fixed), len(after), len(row_outs), len(sent), len(scratch)]

    def kernel(lengths_ref, *refs):
        row = pl.program_id(0)
        groups = []
        at = 0
        for cut in cuts:
            groups.append(refs[at : at + cut])
            at += cut
        numbers, rows_in, fixed_in, unused, rows_out, sent_out, work = groups

        @pl.when(row == 0)
        def _():
            setup(numbers, fixed_in, sent_out, work)

        body(row, lengths_ref, rows_in, rows_out, work)

        if finish:

            @pl.when(row == count - 1)
            def _():
                finish(numbers, work, sent_out)

    return pl.pallas_call(
        kernel,
        grid=(count,),
        in_specs=[pl.BlockSpec(memory_space=pltpu.SMEM)] * (1 + len(scalars))
        + [by_row(array.shape) for array in rowwise]
        + [whole(array.shape) for array in fixed]
        + [pl.BlockSpec(memory_space=pl.ANY) for array in after],
        out_specs=[by_row(part.shape) for part in row_outs] + [whole(part.shape) for part in sent],
        out_shape=list(row_outs) + list(sent),
        scratch_shapes=list(scratch),
        compiler_params=pltpu.CompilerParams(
            dimension_semantics=("arbitrary",), vmem_limit_bytes=MEMORY
        ),
        cost_estimate=pl.CostEstimate(flops=cost, bytes_accessed=8 * 2**20, transcendentals=0),
    )(lengths, *scalars, *rowwise, *fixed, *after)


def struct(shape, dtype):
    return jax.ShapeDtypeStruct(tuple(shape), dtype)


FORWARD_SCRATCH = lambda: [
    pltpu.VMEM((4, SEQ // 2, SEQ), F32),
    pltpu.VMEM((4, SEQ // 2, SEQ), LOW),
    pltpu.VMEM((2, SEQ, PAIR), F32),
    pltpu.VMEM((SEQ, PAIR), F32),
    pltpu.VMEM((3, HEADS // 2, SEQ, PAIR), F32),
    pltpu.VMEM((SEQ, PAIR), F32),
]
BACKWARD_SCRATCH = lambda: [
    pltpu.VMEM((HEADS, SEQ, PAIR), LOW),
    pltpu.VMEM((4, SEQ // 2, SEQ), LOW),
    pltpu.VMEM((4, SEQ // 2, SEQ), LOW),
    pltpu.VMEM((2, 4, SEQ // 2, SEQ), F32),
    pltpu.VMEM((SEQ, 3 * HEADS * HD), LOW),
    pltpu.VMEM((3, 2, SEQ, PAIR), F32),
    pltpu.VMEM((SEQ, PAIR), F32),
    pltpu.VMEM((PAIR, SEQ), LOW),
    pltpu.VMEM((PAIR, SEQ), F32),
]


def attention_outs(rows, tokens, width):
    heads = (rows, HEADS, SEQ, PAIR)
    return [struct(heads, LOW)] * 3 + [struct((tokens, width), LOW)]


def dense_outs(tokens, width, hidden):
    return [
        struct((tokens, width), F32),
        struct((tokens, width), F32),
        struct((tokens, PAIR), F32),
        struct((tokens, width), LOW),
        struct((tokens, hidden), LOW),
        struct((tokens, hidden), LOW),
    ]


def vmem(shape, dtype):
    return pltpu.VMEM(tuple(shape), dtype)


def attention_weights(width):
    return [vmem((width, 3 * width), LOW), vmem((1, 3 * width), F32)]


def dense_weights(width, hidden):
    return [
        vmem((width, width), LOW),
        vmem((width, hidden), LOW),
        vmem((hidden, width), LOW),
        vmem((8, width), F32),
        vmem((1, hidden), F32),
    ]


def dense_sums(width, hidden):
    return [
        vmem((width, width), F32),
        vmem((width, hidden), F32),
        vmem((width, hidden), F32),
        vmem((8, 8, width), F32),
        vmem((8, hidden), F32),
    ]


def attention_sums(width):
    return [vmem((width, 3 * width), F32), vmem((2, 8, width), F32)]


def dense_work(width, hidden):
    return [
        vmem((SEQ, width), LOW),
        vmem((2, SEQ, width), F32),
        vmem((SEQ, hidden), LOW),
        vmem((2, width, SEQ), LOW),
    ]


def set_attention(layer, urgent_ref, raw_ref, at, wq_ref, bias_ref):
    width = wq_ref.shape[0]
    unpack_matrix(raw_ref, at, wq_ref)
    vectors = unpack_vectors(urgent_ref, 3 * width, layer)
    bias_ref[:, :width] = vectors[0:1]
    bias_ref[:, width : 2 * width] = jnp.zeros((1, width), F32)
    bias_ref[:, 2 * width :] = vectors[1:2]


def set_dense(layer, urgent_ref, raw_ref, at, wo_ref, wi_ref, wf_ref, small_ref, bi_ref):
    width, hidden = wi_ref.shape
    unpack_matrix(raw_ref, at, wo_ref)
    unpack_matrix(raw_ref, at + width, wi_ref)
    unpack_stacked(raw_ref, at + width + hidden, wf_ref)
    small_ref[...] = unpack_vectors(urgent_ref, 3 * width, layer)
    bi_ref[...] = unpack_hidden(urgent_ref, 3 * width, layer, hidden)


def clear(refs):
    for ref in refs:
        ref[...] = jnp.zeros(ref.shape, ref.dtype)


def assemble(place_ref, part_refs, into_ref):
    for step, ref in enumerate(part_refs):
        into_ref[place_ref[0] ^ step] = ref[...]


def raw_block(parts):
    return vmem((len(parts),) + parts[0].shape, LOW)


def first_kernel(lengths, x, place, parts):
    rows, (tokens, width) = lengths.shape[0], x.shape

    def setup(numbers, fixed, sent, work):
        assemble(numbers[0], fixed, sent[0])
        set_attention(0, sent[0], sent[0], 0, *work[:2])

    def body(row, lengths_ref, rowwise, outs, work):
        attention_forward(row, lengths_ref, rowwise[0][...], *work[:2], *outs, *work[2:])

    return run_rows(
        body, lengths, [x], list(parts), attention_outs(rows, tokens, width),
        [struct((len(parts),) + parts[0].shape, LOW)],
        attention_weights(width) + FORWARD_SCRATCH(), 4 * 10**9, setup, None, (), [place],
    )


def attention_kernel(layer, lengths, x, place, urgent, parts, at):
    rows, (tokens, width) = lengths.shape[0], x.shape

    def setup(numbers, fixed, sent, work):
        assemble(numbers[0], fixed[1:], work[-1])
        set_attention(layer, fixed[0], work[-1], at, *work[:2])

    def body(row, lengths_ref, rowwise, outs, work):
        attention_forward(
            row, lengths_ref, rowwise[0][...].astype(LOW), *work[:2], *outs, *work[2:-1]
        )

    return run_rows(
        body, lengths, [x], [urgent] + list(parts), attention_outs(rows, tokens, width), [],
        attention_weights(width) + FORWARD_SCRATCH() + [raw_block(parts)],
        4 * 10**9, setup, None, (), [place],
    )


def dense_kernel(layer, lengths, x, ob, place, urgent, parts, at, hidden):
    tokens, width = x.shape

    def setup(numbers, fixed, sent, work):
        assemble(numbers[0], fixed[1:], work[-1])
        set_dense(layer, fixed[0], work[-1], at, *work[:5])

    def body(row, lengths_ref, rowwise, outs, work):
        dense_forward(*rowwise, *work[:5], *outs, *work[5:-1])

    return run_rows(
        body, lengths, [x, ob], [urgent] + list(parts),
        dense_outs(tokens, width, hidden) + [struct((tokens, width), F32)], [],
        dense_weights(width, hidden)
        + [vmem((SEQ, width), F32), vmem((2, SEQ, width), F32), raw_block(parts)],
        5 * 10**9, setup, None, (), [place],
    )


def turn_kernel(layer, lengths, x, ob, cotangent, place, urgent, parts, at, hidden):
    tokens, width = x.shape
    columns = width + 2 * hidden + width + hidden // 8

    def setup(numbers, fixed, sent, work):
        assemble(numbers[0], fixed[1:], work[-1])
        set_dense(layer, fixed[0], work[-1], at, *work[:5])
        clear(work[5:10])

    def body(row, lengths_ref, rowwise, outs, work):
        x_ref, ob_ref, dz_ref = rowwise
        z_ref, dr_ref, dob_ref = outs
        weights, sums, kept = work[:5], work[5:10], work[10:16]
        work_ref, low_ref, u_ref, du_ref, turned_ref = work[16:21]
        dense_forward(x_ref, ob_ref, *weights, *kept, z_ref, work_ref, u_ref)
        dense_backward(
            dz_ref, *kept, ob_ref, *weights[:4], dr_ref, dob_ref, *sums, low_ref, u_ref, du_ref,
            turned_ref,
        )

    def finish(numbers, work, sent):
        pack_dense(*work[5:10], work[21], 0)
        hand_out(numbers[0], work[21], sent)

    kept = [vmem((SEQ,) + part.shape[1:], part.dtype) for part in dense_outs(tokens, width, hidden)]
    return run_rows(
        body, lengths, [x, ob, cotangent], [urgent] + list(parts),
        [struct((tokens, width), LOW), struct((tokens, width), F32), struct((tokens, width), LOW)],
        [struct((64, columns), LOW)] * 4,
        dense_weights(width, hidden) + dense_sums(width, hidden) + kept
        + [vmem((SEQ, width), F32)] + dense_work(width, hidden)
        + [vmem((4, 64, columns), LOW), raw_block(parts)],
        10**10, setup, finish, (), [place],
    )


def hand_out(place_ref, packed_ref, sent):
    for step, ref in enumerate(sent):
        ref[...] = packed_ref[place_ref[0] ^ step]


def middle_kernel(lengths, upper, lower, place, urgent, parts1, parts0, hidden, after):
    tokens, width = upper[0].shape
    columns = 4 * width + width + 2 * hidden + width + hidden // 8

    def setup(numbers, fixed, sent, work):
        count = len(parts1)
        assemble(numbers[0], fixed[1 : 1 + count], work[-2])
        assemble(numbers[0], fixed[1 + count :], work[-1])
        set_attention(1, fixed[0], work[-2], 0, *work[:2])
        set_dense(0, fixed[0], work[-1], 0, *work[2:7])
        clear(work[7:14])

    def body(row, lengths_ref, rowwise, outs, work):
        up, low = rowwise[:7], rowwise[7:]
        dx_ref = work[15]
        attention_backward(
            row, lengths_ref, up[0][...].astype(LOW), *up[1:6], work[0], up[6], dx_ref,
            *work[7:9], *work[20:-2],
        )
        dense_backward(dx_ref, *low, *work[2:6], *outs, *work[9:14], *work[16:20])

    def finish(numbers, work, sent):
        pack_attention(*work[7:9], work[14], 0)
        pack_dense(*work[9:14], work[14], 4 * width)
        hand_out(numbers[0], work[14], sent)

    return run_rows(
        body, lengths, list(upper) + list(lower), [urgent] + list(parts1) + list(parts0),
        [struct((tokens, width), F32), struct((tokens, width), LOW)],
        [struct((64, columns), LOW)] * 4,
        attention_weights(width) + dense_weights(width, hidden)
        + attention_sums(width) + dense_sums(width, hidden)
        + [vmem((4, 64, columns), LOW), vmem((SEQ, width), F32)]
        + dense_work(width, hidden) + BACKWARD_SCRATCH() + [raw_block(parts1), raw_block(parts0)],
        15 * 10**9, setup, finish, after, [place],
    )


def last_kernel(lengths, upper, urgent, after, place):
    tokens, width = upper[0].shape

    def setup(numbers, fixed, sent, work):
        set_attention(0, fixed[0], fixed[0], 0, *work[:2])
        clear(work[2:4])

    def body(row, lengths_ref, rowwise, outs, work):
        attention_backward(
            row, lengths_ref, rowwise[0][...], *rowwise[1:6], work[0], rowwise[6], outs[0],
            *work[2:4], *work[5:],
        )

    def finish(numbers, work, sent):
        pack_attention(*work[2:4], work[4], 0)
        hand_out(numbers[0], work[4], sent)

    return run_rows(
        body, lengths, list(upper), [urgent], [struct((tokens, width), LOW)],
        [struct((64, 4 * width), LOW)] * 4,
        attention_weights(width) + attention_sums(width)
        + [vmem((4, 64, 4 * width), LOW)] + BACKWARD_SCRATCH(),
        8 * 10**9, setup, finish, after, [place],
    )


def hold(array, after):
    def kernel(*refs):
        pass

    anywhere = pl.BlockSpec(memory_space=pl.ANY)
    return pl.pallas_call(
        kernel,
        in_specs=[anywhere] * (1 + len(after)),
        out_specs=anywhere,
        out_shape=shape_of(array),
        input_output_aliases={0: 0},
    )(array, *after)


def pack_parameters(
    attn_weight, attn_bias, out_weight, ffn_in, ffn_in_bias, ffn_out, norm_gain, shifts
):
    depth, rows, width = out_weight.shape
    copies = GROUPS[1]
    hidden = ffn_in.shape[2]
    early = 4 * width + 2 * hidden + 128
    columns = 4 * width + 2 * hidden
    height = ffn_in_bias.shape[1]

    def kernel(wq_ref, ab_ref, wo_ref, wi_ref, bi_ref, wf_ref, gain_ref, shift_ref, first_ref, rest_ref, small_ref):
        def put(ref, block, at):
            block = jnp.broadcast_to(block.astype(F32)[None], (copies,) + block.shape)
            block = block.reshape(copies * block.shape[1], block.shape[2])
            ref[:, pl.ds(at, block.shape[1])] = block.astype(LOW)

        small_ref[...] = jnp.zeros(small_ref.shape, F32)
        for layer in range(depth):
            lanes = pl.ds(rows * layer, rows)
            small_ref[0:2, lanes] = ab_ref[layer].astype(F32)
            small_ref[2:4, lanes] = gain_ref[layer].astype(F32)
            small_ref[4:8, lanes] = shift_ref[layer].astype(F32)
        small_ref[0:depth, pl.ds(2 * rows, height)] = bi_ref[...].astype(F32)
        put(first_ref, wq_ref[0], 0)
        put(first_ref, small_ref[...], 3 * width)
        for layer, ref, at in ((0, first_ref, 3 * width + 128), (1, rest_ref, 3 * width)):
            if layer:
                put(ref, wq_ref[layer], 0)
            put(ref, wo_ref[layer], at)
            put(ref, wi_ref[layer], at + width)
            at += width + hidden
            down = wf_ref[layer].astype(F32)
            for step in range(hidden // width):
                put(ref, down[step * rows : (step + 1) * rows], at)
                at += width

    return pl.pallas_call(
        kernel,
        in_specs=[pl.BlockSpec(memory_space=pltpu.VMEM)] * 8,
        out_shape=[struct((copies * rows, early), LOW), struct((copies * rows, columns), LOW)],
        scratch_shapes=[vmem((rows, 128), F32)],
        compiler_params=pltpu.CompilerParams(vmem_limit_bytes=MEMORY),
    )(attn_weight, attn_bias, out_weight, ffn_in, ffn_in_bias, ffn_out, norm_gain, shifts)


def add_parts(parts, after=(), joined=None):
    inner = [] if joined is None else [joined]
    ahead = 0 if joined is None else joined.shape[1]
    rows, lanes_in = parts[0].shape
    count = len(parts)

    def kernel(*refs):
        out_ref = refs[-1]
        if inner:
            out_ref[:, pl.ds(0, ahead)] = refs[count][...]
        columns = 256
        for start in range(0, lanes_in, columns):
            size = min(columns, lanes_in - start)
            total = refs[0][:, pl.ds(start, size)].astype(F32)
            for ref in refs[1:count]:
                total = total + ref[:, pl.ds(start, size)].astype(F32)
            out_ref[:, pl.ds(ahead + start, size)] = total.astype(LOW)

    near = pl.BlockSpec(memory_space=pltpu.VMEM)
    return pl.pallas_call(
        kernel,
        in_specs=[near] * (count + len(inner)) + [pl.BlockSpec(memory_space=pl.ANY)] * len(after),
        out_specs=near,
        out_shape=struct((rows, ahead + lanes_in), LOW),
        compiler_params=pltpu.CompilerParams(vmem_limit_bytes=MEMORY),
    )(*parts, *inner, *after)


def write_gradients(place, tail, front, depth, width, hidden):
    rows = GROUPS[2]
    last = front.shape[1] - 4 * width
    height = hidden // DEVICES

    def kernel(place_ref, tail_ref, front_ref, gwq_ref, gab_ref, gwo_ref, gwi_ref, gbi_ref, gwf_ref, gain_ref, shift_ref):
        spot = place_ref[0]

        def total(ref, at, columns):
            block = ref[:, pl.ds(at, columns)].astype(F32)
            return jnp.sum(block.reshape(-1, rows, columns), 0)

        def own(block, size):
            return pltpu.roll(block, block.shape[1] - spot * size, 1)

        for layer, ref, at in ((0, front_ref, last), (1, front_ref, 0)):
            gwq_ref[layer] = total(ref, at, 3 * width)
            gab_ref[layer] = own(total(ref, at + 3 * width, width), rows)[0:2, 0:rows]
        for layer, ref, at in ((0, front_ref, 4 * width), (1, tail_ref, 0)):
            gwo_ref[layer] = total(ref, at, width)
            gwi_ref[layer] = total(ref, at + width, hidden)
            for step in range(hidden // width):
                gwf_ref[layer, pl.ds(step * rows, rows)] = total(
                    ref, at + width + hidden + step * width, width
                )
            at += width + 2 * hidden
            small = own(total(ref, at, width), rows)
            gain_ref[layer] = small[2:4, 0:rows]
            shift_ref[layer] = small[4:8, 0:rows]
            line = total(ref, at + width, hidden // 8)
            line = jnp.concatenate([line[step : step + 1] for step in range(8)], 1)
            gbi_ref[pl.ds(layer, 1)] = own(line, height)[:, 0:height]

    outs = [
        struct((depth, rows, 3 * width), F32),
        struct((depth, 2, rows), F32),
        struct((depth, rows, width), F32),
        struct((depth, rows, hidden), F32),
        struct((depth, height), F32),
        struct((depth, height, width), F32),
        struct((depth, 2, rows), F32),
        struct((depth, 4, rows), F32),
    ]
    return pl.pallas_call(
        kernel,
        in_specs=[pl.BlockSpec(memory_space=pltpu.SMEM)] + [pl.BlockSpec(memory_space=pltpu.VMEM)] * 2,
        out_shape=outs,
        compiler_params=pltpu.CompilerParams(vmem_limit_bytes=MEMORY),
    )(place, tail, front)


def exchange(parts, axis):
    return lax.all_to_all(parts, axis, 0, 0, tiled=True)


def swap(part, axis, step):
    size = lax.axis_size(axis)
    return lax.ppermute(part, axis, [(source, source ^ step) for source in range(size)])


def local(
    hidden_in,
    lengths,
    grad_out,
    attn_weight,
    attn_bias,
    out_weight,
    ffn_in,
    ffn_in_bias,
    ffn_out,
    norm_gain,
    shifts,
):
    depth, rows, width = out_weight.shape
    hidden = ffn_in.shape[2]
    first, second = lax.axis_size("dp"), lax.axis_size("fsdp")
    fits = (second, first, rows) == GROUPS
    urgent_size = 3 * width + 128
    if fits:
        early, later = pack_parameters(
            attn_weight, attn_bias, out_weight, ffn_in, ffn_in_bias, ffn_out, norm_gain, shifts
        )
        early = exchange(early, "dp")
        partners = range(1, second)
        urgent = early[:, :urgent_size]
        urgent = [urgent] + [swap(urgent, "fsdp", step) for step in partners]
        later = exchange(hold(later, (early,)), "dp")
        raw0 = hold(early[:, urgent_size:], tuple(urgent))
        raw0 = [raw0] + [swap(raw0, "fsdp", step) for step in partners]
        place = lax.axis_index("fsdp").astype(jnp.int32).reshape(1)
    else:
        urgent, raw0, raw1 = gather_other(
            attn_weight, attn_bias, out_weight, ffn_in, ffn_in_bias, ffn_out, norm_gain, shifts
        )
        urgent, raw0, raw1 = ([part[step] for step in range(4)] for part in (urgent, raw0, raw1))
        place = jnp.zeros((1,), jnp.int32)

    qa0, ka0, va0, ob0, urgent = first_kernel(lengths, hidden_in, place, urgent)
    if fits:
        raw1 = hold(later, (ob0,))
        raw1 = [raw1] + [swap(raw1, "fsdp", step) for step in partners]
    n1, n2, inv, yb, gb, gp, z0 = dense_kernel(
        0, lengths, hidden_in, ob0, place, urgent, raw0, 0, hidden
    )
    qa1, ka1, va1, ob1 = attention_kernel(1, lengths, z0, place, urgent, raw1, 0)
    hidden_out, dr1, dob1, *sent_a = turn_kernel(
        1, lengths, z0, ob1, grad_out, place, urgent, raw1, 3 * width, hidden
    )
    dr0, dob0, *sent_b = middle_kernel(
        lengths,
        (z0, dob1, ob1, qa1, ka1, va1, dr1),
        (n1, n2, inv, yb, gb, gp, ob0),
        place,
        urgent,
        raw1,
        raw0,
        hidden,
        (sent_a[0],),
    )
    if fits:
        got_a = [sent_a[0]] + [swap(sent_a[step], "fsdp", step) for step in partners]
        tail = exchange(add_parts(got_a, (sent_b[0],)), "dp")
    grad_in, *sent_c = last_kernel(
        lengths, (hidden_in, dob0, ob0, qa0, ka0, va0, dr0), urgent, (sent_b[0],), place
    )
    if fits:
        got_b = [sent_b[0]] + [swap(sent_b[step], "fsdp", step) for step in partners]
        got_c = [sent_c[0]] + [swap(sent_c[step], "fsdp", step) for step in partners]
        front = add_parts(got_b, (tail,))
        front = add_parts(got_c, (), front)
        front = exchange(front, "dp")
        place = lax.axis_index(("dp", "fsdp")).astype(jnp.int32).reshape(1)
        grads = write_gradients(place, tail, front, depth, width, hidden)
    else:
        grads = scatter_other(
            *(jnp.stack(part) for part in (sent_a, sent_b, sent_c)), rows, width, hidden
        )
    return (hidden_out, grad_in, *grads)


def gather_other(
    attn_weight, attn_bias, out_weight, ffn_in, ffn_in_bias, ffn_out, norm_gain, shifts
):
    axes = ("dp", "fsdp")
    gather = lambda part, axis: lax.all_gather(part, axes, axis=axis, tiled=True)
    depth, unused, width = out_weight.shape
    hidden = ffn_in.shape[2]
    outer, inner, rows = GROUPS
    vectors = gather(jnp.concatenate([attn_bias, norm_gain, shifts], 1), 2)
    line = gather(ffn_in_bias, 1)

    def order(natural):
        return (
            natural.reshape(inner, outer, rows, -1).swapaxes(0, 1).reshape(outer, inner * rows, -1)
        )

    def stacked(part):
        part = part.reshape(DEVICES, -1, rows, width)
        return order(part.swapaxes(1, 2).reshape(width, -1))

    small = vectors.reshape(depth, 8, DEVICES, rows).transpose(2, 1, 0, 3).reshape(width, -1)
    line = line.reshape(depth, DEVICES, -1).swapaxes(0, 1)
    line = jnp.pad(line, ((0, 0), (0, 8 - depth), (0, 0))).reshape(width, -1)
    small = jnp.concatenate([small, line], 1)
    small = jnp.pad(small, ((0, 0), (0, 128 - small.shape[1])))
    wq, wo, wi, wf = (gather(part, 1) for part in (attn_weight, out_weight, ffn_in, ffn_out))
    urgent = jnp.concatenate([order(wq[0]), order(small)], 2)
    raw0 = jnp.concatenate([order(wo[0]), order(wi[0]), stacked(wf[0])], 2)
    raw1 = jnp.concatenate([order(wq[1]), order(wo[1]), order(wi[1]), stacked(wf[1])], 2)
    return urgent, raw0, raw1


def scatter_other(sent_a, sent_b, sent_c, own_rows, width, hidden):
    outer, inner, rows = GROUPS
    axes = ("dp", "fsdp")

    def natural(part):
        return part.reshape(outer, inner, rows, -1).swapaxes(0, 1).reshape(width, -1).astype(F32)

    def cut(part, sizes):
        found, at = [], 0
        for size in sizes:
            found.append(part[:, at : at + size])
            at += size
        return found

    dense = [width, hidden, hidden, width, hidden // 8]
    attention = [3 * width, width]
    wq0, ab0 = cut(natural(sent_c), attention)
    wq1, ab1, wo0, wi0, wf0, small0, bi0 = cut(natural(sent_b), attention + dense)
    wo1, wi1, wf1, small1, bi1 = cut(natural(sent_a), dense)

    def stacked(part):
        part = part.reshape(DEVICES, rows, -1, width).swapaxes(1, 2)
        return part.reshape(hidden, width)

    def spread(parts, axis):
        return lax.psum_scatter(jnp.stack(parts), axes, scatter_dimension=axis, tiled=True)

    return (
        spread([wq0, wq1], 1),
        spread([ab0[:2], ab1[:2]], 2),
        spread([wo0, wo1], 1),
        spread([wi0, wi1], 1),
        spread([bi0[:8].reshape(-1), bi1[:8].reshape(-1)], 1),
        spread([stacked(wf0), stacked(wf1)], 1),
        spread([small0[2:4], small1[2:4]], 2),
        spread([small0[4:8], small1[4:8]], 2),
    )


def solution(mesh):
    placed = (
        P(("dp", "fsdp"), None),
        P(("dp", "fsdp"), None),
        P(("dp", "fsdp"), None),
        P(None, ("dp", "fsdp"), None),
        P(None, None, ("dp", "fsdp")),
        P(None, ("dp", "fsdp"), None),
        P(None, ("dp", "fsdp"), None),
        P(None, ("dp", "fsdp")),
        P(None, ("dp", "fsdp"), None),
        P(None, None, ("dp", "fsdp")),
        P(None, None, ("dp", "fsdp")),
    )
    return jax.shard_map(
        local,
        mesh=mesh,
        in_specs=placed,
        out_specs=(
            P(("dp", "fsdp"), None),
            P(("dp", "fsdp"), None),
            P(None, ("dp", "fsdp"), None),
            P(None, None, ("dp", "fsdp")),
            P(None, ("dp", "fsdp"), None),
            P(None, ("dp", "fsdp"), None),
            P(None, ("dp", "fsdp")),
            P(None, ("dp", "fsdp"), None),
            P(None, None, ("dp", "fsdp")),
            P(None, None, ("dp", "fsdp")),
        ),
        check_vma=False,
    )
```

```python
from functools import partial

import jax
import jax.numpy as jnp
from jax import lax
from jax.experimental import pallas as pl
from jax.experimental.pallas import tpu as pltpu
from jax.sharding import PartitionSpec as P

HEADS = 4
HD = 64
SEQ = 512
PAIR = 2 * HD
FAR = -(2.0**100)
FLOOR = -1e20
EPSILON = 1e-12
PIECE = 256
SMALL = 128
GROUPS = (4, 8, 8)
DEVICES = 32
LOW = jnp.bfloat16
F32 = jnp.float32
MEMORY = 127 * 2**19


def dot_nn(left, right):
    return lax.dot_general(left, right, (((1,), (0,)), ((), ())), preferred_element_type=F32)


def dot_nt(left, right):
    return lax.dot_general(left, right, (((1,), (1,)), ((), ())), preferred_element_type=F32)


def dot_tn(left, right):
    return lax.dot_general(left, right, (((0,), (0,)), ((), ())), preferred_element_type=F32)


def pieces(total, size=PIECE):
    return [pl.ds(start, size) for start in range(0, total, size)]


def three_parts(values):
    first = values.astype(LOW).astype(F32)
    rest = values - first
    second = rest.astype(LOW).astype(F32)
    return first, second, rest - second


CURVE = (7.97869556e-01, 3.63928094e-02, -8.82195179e-05, -3.66000319e-05, 1.41853144e-06)
BELL = -0.5 / 0.6931471805599453


def gelu_parts(u):
    square = u * u
    curve = CURVE[-1]
    for factor in CURVE[-2::-1]:
        curve = curve * square + factor
    cumulative = 0.5 + 0.5 * jnp.tanh(u * curve)
    slope = cumulative + (u * 0.3989422804014327) * jnp.exp2(square * BELL)
    return u * cumulative, slope


def inverse_of(values):
    guess = pl.reciprocal(values, approx=True)
    return guess * (2.0 - values * guess)


def lane_facts():
    lane = lax.broadcasted_iota(jnp.int32, (1, PAIR), 1)
    return lane < HD, lane & (HD - 1)


def segments(lengths_ref, row, start, rows):
    places = lax.broadcasted_iota(jnp.int32, (rows, 1), 0) + start
    bound = jnp.int32(0)
    segment = jnp.zeros((rows, 1), jnp.int32)
    last = lengths_ref.shape[1] - 1
    for entry in range(last):
        bound = bound + lengths_ref[row, entry]
        segment = segment + (places >= bound).astype(jnp.int32)
    return segment, (segment == last).astype(F32), last


def attention_forward(row, lengths_ref, x, wq_ref, bias_ref, qa_ref, ka_ref, va_ref, ob_ref, s_ref, p_ref, m_ref, pad_ref, q_ref, aug_ref):
    width = HEADS * HD
    for block in range(3):
        at = block * width
        value = dot_nn(x, wq_ref[:, at : at + width]) + bias_ref[:, at : at + width]
        for pair in range(HEADS // 2):
            q_ref[block, pair] = value[:, pair * PAIR : (pair + 1) * PAIR]
        yield
    for start in range(0, SEQ, PIECE):
        place = pl.ds(start, PIECE)
        low_half, slot = lane_facts()
        segment, pad, last = segments(lengths_ref, row, start, PIECE)
        pad_ref[place] = jnp.broadcast_to(pad, (PIECE, PAIR))
        aug_q = jnp.where(slot == segment, 1.0, 0.0)
        aug_ref[place] = aug_q
        seen = (slot == segment) & (slot != last)
        aug_k = jnp.where(seen, 0.0, jnp.where(slot <= last, FAR, jnp.where(slot <= last + 3, 1.0, 0.0)))
        for pair in range(HEADS // 2):
            q = q_ref[0, pair, place] * HD**-0.5
            k = q_ref[1, pair, place]
            v = q_ref[2, pair, place]
            q_ref[0, pair, place] = q
            qa_ref[2 * pair, place] = jnp.where(low_half, q, aug_q).astype(LOW)
            qa_ref[2 * pair + 1, place] = jnp.where(low_half, aug_q, q).astype(LOW)
            ka_ref[2 * pair, place] = jnp.where(low_half, k, aug_k).astype(LOW)
            ka_ref[2 * pair + 1, place] = jnp.where(low_half, aug_k, k).astype(LOW)
            va_ref[2 * pair, place] = jnp.where(low_half, v, 1.0).astype(LOW)
            va_ref[2 * pair + 1, place] = jnp.where(low_half, 1.0, v).astype(LOW)
        yield

    def scores(head):
        s_ref[head % 2] = dot_nt(qa_ref[head], ka_ref[head])

    def softmax(head):
        for place in pieces(SEQ):
            highest = jnp.maximum(jnp.max(s_ref[head % 2, place], -1, keepdims=True), FLOOR)
            m_ref[head % 2, place] = jnp.broadcast_to(highest, (PIECE, PAIR))
            p_ref[head % 2, place] = jnp.exp(s_ref[head % 2, place] - highest).astype(LOW)

    scores(0)
    yield
    for head in range(HEADS):
        if head + 1 < HEADS:
            scores(head + 1)
            yield
        softmax(head)
        yield
        q_ref[1, head % 2] = dot_nn(p_ref[head % 2], va_ref[head])
        if head % 2:
            pair = head // 2
            for start in range(0, SEQ, PIECE):
                place = pl.ds(start, PIECE)
                low_half, slot = lane_facts()
                even = q_ref[1, 0, place]
                odd = q_ref[1, 1, place]
                pad = pad_ref[place]
                last = lengths_ref.shape[1] - 1
                total = jnp.where(low_half, odd, even) + pad
                top = jnp.where(low_half, m_ref[1, place], m_ref[0, place])
                spread = jnp.where(pad > 0, 0.0, top + jnp.log(total))
                first, second, third = three_parts(spread)
                aug = jnp.where(
                    slot == last + 1,
                    -first,
                    jnp.where(slot == last + 2, -second, jnp.where(slot == last + 3, -third, aug_ref[place])),
                )
                q = q_ref[0, pair, place]
                qa_ref[2 * pair, place] = jnp.where(low_half, q, aug).astype(LOW)
                qa_ref[2 * pair + 1, place] = jnp.where(low_half, aug, q).astype(LOW)
                v = q_ref[2, pair, place].astype(LOW).astype(F32)
                share = inverse_of(pltpu.roll(total, HD, 1))
                out = jnp.where(low_half, even, odd) * share + pad * v
                ob_ref[place, pl.ds(pair * PAIR, PAIR)] = out.astype(LOW)
            yield


def normal(values):
    centred = values - jnp.mean(values, -1, keepdims=True)
    inverse = lax.rsqrt(jnp.mean(centred * centred, -1, keepdims=True) + EPSILON)
    return centred * inverse, inverse


def normal_back(cotangent, unit, inverse, gains):
    scaled = cotangent * gains
    return inverse * (
        scaled
        - jnp.mean(scaled, -1, keepdims=True)
        - unit * jnp.mean(scaled * unit, -1, keepdims=True)
    )


def dense_forward(x_ref, ob_ref, wo_ref, wi_ref, wf_ref, small_ref, bi_ref, n1_ref, n2_ref, inv_ref, yb_ref, gb_ref, gp_ref, z_ref, work_ref, u_ref):
    small = lambda index: small_ref[pl.ds(index, 1)]
    work_ref[...] = dot_nn(ob_ref[...], wo_ref[...])
    yield
    for place in pieces(SEQ):
        unit, inverse = normal(x_ref[place].astype(F32) + work_ref[place] + small(4))
        n1_ref[place] = unit
        inv_ref[place, pl.ds(0, HD)] = jnp.broadcast_to(inverse, (PIECE, HD))
        y = unit * small(2) + small(5)
        yb_ref[place] = y.astype(LOW)
        work_ref[place] = y + small(6)
        yield
    columns = 256
    count = wi_ref.shape[1] // columns

    def into(step):
        u_ref[step % 2] = dot_nn(yb_ref[...], wi_ref[:, pl.ds(step * columns, columns)])

    into(0)
    yield
    for step in range(count):
        if step + 1 < count:
            into(step + 1)
            yield
        lanes = pl.ds(step * columns, columns)
        for place in pieces(SEQ, SMALL):
            g, slope = gelu_parts(u_ref[step % 2, place] + bi_ref[:, lanes])
            gb_ref[place, lanes] = g.astype(LOW)
            gp_ref[place, lanes] = slope.astype(LOW)
            yield
    work_ref[...] += dot_nn(gb_ref[...], wf_ref[...])
    yield
    for place in pieces(SEQ):
        unit, inverse = normal(work_ref[place])
        n2_ref[place] = unit
        inv_ref[place, pl.ds(HD, HD)] = jnp.broadcast_to(inverse, (PIECE, HD))
        z_ref[place] = (unit * small(3) + small(7)).astype(z_ref.dtype)
        yield


def fold(values):
    return jnp.sum(values.reshape(-1, 8, values.shape[-1]), 0)


def dense_backward(dz_ref, n1_ref, n2_ref, inv_ref, yb_ref, gb_ref, gp_ref, ob_ref, wo_ref, wi_ref, wf_ref, small_ref, dr_ref, dob_ref, gwo_ref, gwi_ref, gwf_ref, gsmall_ref, gbi_ref, low_ref, u_ref, du_ref, turned_ref):
    small = lambda index: small_ref[pl.ds(index, 1)]
    for place in pieces(SEQ):
        dz = dz_ref[place].astype(F32)
        unit = n2_ref[place]
        gsmall_ref[3] += fold(dz * unit)
        gsmall_ref[7] += fold(dz)
        dr = normal_back(dz, unit, inv_ref[place, pl.ds(HD, 1)], small(3))
        dr_ref[place] = dr
        df = dr.astype(LOW)
        low_ref[place] = df
        gsmall_ref[6] += fold(df.astype(F32))
        yield
    columns = 256
    count = wi_ref.shape[1] // columns

    def back(step):
        u_ref[step % 2] = dot_nt(low_ref[...], wf_ref[pl.ds(step * columns, columns)])

    back(0)
    turned_ref[0] = low_ref[...].T
    turned_ref[1] = yb_ref[...].T
    yield
    for step in range(count):
        if step + 1 < count:
            back(step + 1)
            yield
        lanes = pl.ds(step * columns, columns)
        gwf_ref[:, lanes] += dot_nn(turned_ref[0], gb_ref[:, lanes])
        yield
        for place in pieces(SEQ, SMALL):
            du = (u_ref[step % 2, place] * gp_ref[place, lanes].astype(F32)).astype(LOW)
            du_ref[place, lanes] = du
            gbi_ref[:, lanes] += fold(du.astype(F32))
        yield
        gwi_ref[:, lanes] += dot_nn(turned_ref[1], du_ref[:, lanes])
        yield
    u_ref[0] = dot_nt(du_ref[...], wi_ref[...])
    yield
    for place in pieces(SEQ):
        dy = dr_ref[place] + u_ref[0, place]
        unit = n1_ref[place]
        gsmall_ref[2] += fold(dy * unit)
        gsmall_ref[5] += fold(dy)
        dr = normal_back(dy, unit, inv_ref[place, pl.ds(0, 1)], small(2))
        dr_ref[place] = dr
        da = dr.astype(LOW)
        low_ref[place] = da
        gsmall_ref[4] += fold(da.astype(F32))
        yield
    gwo_ref[...] += dot_tn(ob_ref[...], low_ref[...])
    dob_ref[...] = dot_nt(low_ref[...], wo_ref[...]).astype(LOW)
    yield


def attention_backward(row, lengths_ref, x, dob_ref, ob_ref, qa_ref, ka_ref, va_ref, wq_ref, dr_ref, dx_ref, gwq_ref, gbias_ref, da_ref, p_ref, ds_ref, s_ref, dqkv_ref, dq_ref, pad_ref, kt_ref, dqt_ref):
    width = HEADS * HD
    low_half, slot = lane_facts()
    for start in range(0, SEQ, PIECE):
        place = pl.ds(start, PIECE)
        segment, pad, last = segments(lengths_ref, row, start, PIECE)
        pad_ref[place] = jnp.broadcast_to(pad, (PIECE, PAIR))
        for pair in range(HEADS // 2):
            lanes = pl.ds(pair * PAIR, PAIR)
            dob = dob_ref[place, lanes].astype(F32)
            product = dob * ob_ref[place, lanes].astype(F32)
            even = jnp.sum(jnp.where(low_half, product, 0.0), -1, keepdims=True)
            odd = jnp.sum(jnp.where(low_half, 0.0, product), -1, keepdims=True)
            first, second, third = three_parts(jnp.where(low_half, odd, even))
            aug = jnp.where(
                slot == 0, -first, jnp.where(slot == 1, -second, jnp.where(slot == 2, -third, 0.0))
            )
            da_ref[2 * pair, place] = jnp.where(low_half, dob, aug).astype(LOW)
            da_ref[2 * pair + 1, place] = jnp.where(low_half, aug, dob).astype(LOW)
        yield
    for pair in range(HEADS // 2):
        low_half, unused = lane_facts()
        keys = jnp.where(low_half, ka_ref[2 * pair].astype(F32), ka_ref[2 * pair + 1].astype(F32))
        kt_ref[pl.ds(pair * PAIR, PAIR)] = keys.T.astype(LOW)
    low_half, slot = lane_facts()

    def scores(head):
        s_ref[0, head % 2] = dot_nt(ka_ref[head], qa_ref[head])
        s_ref[1, head % 2] = dot_nt(va_ref[head], da_ref[head])

    def weigh(head):
        for place in pieces(SEQ, SMALL):
            p = jnp.exp(s_ref[0, head % 2, place])
            p_ref[head % 2, place] = p.astype(LOW)
            ds_ref[head % 2, place] = (p * s_ref[1, head % 2, place]).astype(LOW)

    scores(0)
    yield
    for head in range(HEADS):
        if head + 1 < HEADS:
            scores(head + 1)
            yield
        weigh(head)
        yield
        side = head % 2
        dq_ref[1, side] = dot_nn(ds_ref[head % 2], qa_ref[head])
        dq_ref[2, side] = dot_nn(p_ref[head % 2], da_ref[head])
        dqt_ref[pl.ds(side * HD, HD)] = dot_nn(kt_ref[pl.ds(head * HD, HD)], ds_ref[head % 2])
        yield
        if side:
            pair = head // 2
            dq_ref[0, 0] = dqt_ref[...].T
            for start in range(0, SEQ, PIECE):
                place = pl.ds(start, PIECE)
                dq = dq_ref[0, 0, place] * HD**-0.5
                dk = jnp.where(low_half, dq_ref[1, 0, place], dq_ref[1, 1, place])
                dv = jnp.where(low_half, dq_ref[2, 0, place], dq_ref[2, 1, place])
                dv = dv + pad_ref[place] * dob_ref[place, pl.ds(pair * PAIR, PAIR)].astype(F32)
                for block, value in enumerate((dq, dk, dv)):
                    lanes = pl.ds(block * width + pair * PAIR, PAIR)
                    value = value.astype(LOW)
                    dqkv_ref[place, lanes] = value
                    if block != 1:
                        into = pl.ds(pair * PAIR, PAIR)
                        gbias_ref[block // 2, :, into] += fold(value.astype(F32))
    yield
    gwq_ref[...] += dot_tn(x, dqkv_ref[...])
    yield
    dx_ref[...] = (dr_ref[...] + dot_nt(dqkv_ref[...], wq_ref[...])).astype(dx_ref.dtype)
    yield


def unpack_matrix(raw_ref, at, into_ref):
    width = into_ref.shape[0]
    for start in range(0, into_ref.shape[1], width):
        block = raw_ref[:, :, pl.ds(at + start, width)].astype(F32)
        block = block.reshape(GROUPS + (width,)).swapaxes(0, 1).reshape(width, width)
        into_ref[:, pl.ds(start, width)] = block.astype(LOW)


def unpack_stacked(raw_ref, at, into_ref):
    width = into_ref.shape[1]
    count = into_ref.shape[0] // width
    blocks = [
        raw_ref[:, :, pl.ds(at + step * width, width)].astype(F32).reshape(GROUPS + (width,))
        for step in range(count)
    ]
    outer, inner, rows = GROUPS
    for place in range(inner):
        part = jnp.stack([jnp.stack([block[f, place] for block in blocks]) for f in range(outer)])
        size = outer * count * rows
        into_ref[pl.ds(place * size, size)] = part.reshape(size, width).astype(LOW)


def counter(shape, axis):
    return lax.broadcasted_iota(jnp.int32, shape, axis)


def split_by(values, size):
    return lax.shift_right_logical(values, size.bit_length() - 1), values & (size - 1)


def sources(rows):
    outer, inner, height = GROUPS
    group, within = split_by(counter((rows, 1), 0), height)
    far, near = split_by(group, inner)
    return near * outer + far, within


def unpack_vectors(raw_ref, at, layer):
    outer, inner, rows = GROUPS
    total = outer * inner * rows
    raw = raw_ref[:, :, pl.ds(at, 128)].reshape(total, 128)
    owner, place = split_by(counter((1, total), 1), rows)
    pick = jnp.where(counter((128, 1), 0) == rows * layer + place, 1.0, 0.0).astype(LOW)
    device, unused = sources(total)
    spread = jnp.where(owner == device, dot_nn(raw, pick), 0.0)
    return jnp.sum(spread.reshape(outer * inner, rows, total), 0)


def unpack_hidden(raw_ref, at, layer, hidden):
    outer, inner, rows = GROUPS
    total = outer * inner * rows
    raw = raw_ref[:, :, pl.ds(at, 128)].reshape(total, 128)
    owner, place = split_by(counter((1, hidden), 1), hidden // (outer * inner))
    pick = jnp.where(counter((128, 1), 0) == 2 * rows + place, 1.0, 0.0).astype(LOW)
    device, within = sources(total)
    device = jnp.where(within == layer, device, -1)
    spread = jnp.where(owner == device, dot_nn(raw, pick), 0.0)
    return jnp.sum(spread, 0, keepdims=True)


def pack_matrix(sum_ref, sent_ref, at):
    width = sum_ref.shape[0]
    outer, inner, rows = GROUPS
    for start in range(0, sum_ref.shape[1], width):
        block = sum_ref[:, pl.ds(start, width)].reshape(inner, outer, rows, width)
        block = block.swapaxes(0, 1).reshape(outer, inner * rows, width)
        sent_ref[:, :, pl.ds(at + start, width)] = block.astype(LOW)


def pack_stacked(sum_ref, sent_ref, at):
    width = sum_ref.shape[0]
    outer, inner, rows = GROUPS
    count = sum_ref.shape[1] // width
    near = inner // count
    for step in range(count):
        block = sum_ref[:, pl.ds(step * width, width)].T
        block = block.reshape(near, outer, count, rows, width)
        for part in range(count):
            piece = jnp.stack([block[:, f, part] for f in range(outer)])
            piece = piece.reshape(outer, near * rows, width)
            sent_ref[:, pl.ds(step * near * rows, near * rows), pl.ds(at + part * width, width)] = (
                piece.astype(LOW)
            )


def pack_shared(block, sent_ref, at):
    outer, inner, rows = GROUPS
    columns = block.shape[1]
    block = jnp.broadcast_to(block[None], (outer * inner, rows, columns))
    sent_ref[:, :, pl.ds(at, columns)] = block.reshape(outer, inner * rows, columns).astype(LOW)


def pack_attention(gwq_ref, gbias_ref, sent_ref, at):
    pack_matrix(gwq_ref, sent_ref, at)
    width = gwq_ref.shape[0]
    line = lax.broadcasted_iota(jnp.int32, (8, width), 0)
    sums = [jnp.sum(gbias_ref[index], 0, keepdims=True) for index in range(2)]
    block = jnp.where(line == 0, sums[0], jnp.where(line == 1, sums[1], 0.0))
    pack_shared(block, sent_ref, at + 3 * width)


def pack_dense(gwo_ref, gwi_ref, gwf_ref, gsmall_ref, gbi_ref, sent_ref, at):
    width, hidden = gwi_ref.shape
    pack_matrix(gwo_ref, sent_ref, at)
    pack_matrix(gwi_ref, sent_ref, at + width)
    pack_stacked(gwf_ref, sent_ref, at + width + hidden)
    at = at + width + 2 * hidden
    pack_shared(jnp.sum(gsmall_ref[...], 1), sent_ref, at)
    line = jnp.sum(gbi_ref[...], 0, keepdims=True)
    size = hidden // 8
    block = jnp.concatenate([line[:, step * size : (step + 1) * size] for step in range(8)], 0)
    pack_shared(block, sent_ref, at + width)


def shape_of(array):
    return jax.ShapeDtypeStruct(array.shape, array.dtype)


def by_row(shape, group):
    if len(shape) == 2:
        return pl.BlockSpec((group * SEQ, shape[1]), lambda step: (step, 0))
    return pl.BlockSpec((group,) + tuple(shape[1:]), lambda step: (step,) + (0,) * (len(shape) - 1))


def one_row(ref, member):
    if len(ref.shape) == 2:
        return ref.at[pl.ds(member * SEQ, SEQ)]
    return ref.at[member]


def alternate(runs):
    running = []
    waiting = list(runs)
    while running or waiting:
        if waiting:
            running.append(waiting.pop(0))
        for run in list(running):
            try:
                next(run)
            except StopIteration:
                running.remove(run)


def whole(shape):
    return pl.BlockSpec(tuple(shape), lambda row: (0,) * len(shape))


def run_rows(
    body, lengths, rowwise, fixed, row_outs, sent, shared, private, cost, setup, finish, after=(),
    scalars=(), group=2
):
    count = lengths.shape[0]
    group = group if count % group == 0 else 1
    cuts = [len(scalars), len(rowwise), len(fixed), len(after), len(row_outs), len(sent)]
    cuts += [len(shared)] + [len(private)] * group

    def kernel(lengths_ref, *refs):
        step = pl.program_id(0)
        groups = []
        at = 0
        for cut in cuts:
            groups.append(refs[at : at + cut])
            at += cut
        numbers, rows_in, fixed_in, unused, rows_out, sent_out, work = groups[:7]

        @pl.when(step == 0)
        def _():
            setup(numbers, fixed_in, sent_out, work)

        alternate(
            body(
                step * group + member,
                lengths_ref,
                [one_row(ref, member) for ref in rows_in],
                [one_row(ref, member) for ref in rows_out],
                work,
                groups[7 + member],
            )
            for member in range(group)
        )

        if finish:

            @pl.when(step == count // group - 1)
            def _():
                finish(numbers, work, sent_out)

    return pl.pallas_call(
        kernel,
        grid=(count // group,),
        in_specs=[pl.BlockSpec(memory_space=pltpu.SMEM)] * (1 + len(scalars))
        + [by_row(array.shape, group) for array in rowwise]
        + [whole(array.shape) for array in fixed]
        + [pl.BlockSpec(memory_space=pl.ANY) for array in after],
        out_specs=[by_row(part.shape, group) for part in row_outs]
        + [whole(part.shape) for part in sent],
        out_shape=list(row_outs) + list(sent),
        scratch_shapes=list(shared) + list(private) * group,
        compiler_params=pltpu.CompilerParams(
            dimension_semantics=("arbitrary",), vmem_limit_bytes=MEMORY
        ),
        cost_estimate=pl.CostEstimate(flops=cost, bytes_accessed=8 * 2**20, transcendentals=0),
    )(lengths, *scalars, *rowwise, *fixed, *after)


def struct(shape, dtype):
    return jax.ShapeDtypeStruct(tuple(shape), dtype)


FORWARD_SCRATCH = lambda: [
    pltpu.VMEM((2, SEQ, SEQ), F32),
    pltpu.VMEM((2, SEQ, SEQ), LOW),
    pltpu.VMEM((2, SEQ, PAIR), F32),
    pltpu.VMEM((SEQ, PAIR), F32),
    pltpu.VMEM((3, HEADS // 2, SEQ, PAIR), F32),
    pltpu.VMEM((SEQ, PAIR), F32),
]
BACKWARD_SCRATCH = lambda: [
    pltpu.VMEM((HEADS, SEQ, PAIR), LOW),
    pltpu.VMEM((2, SEQ, SEQ), LOW),
    pltpu.VMEM((2, SEQ, SEQ), LOW),
    pltpu.VMEM((2, 2, SEQ, SEQ), F32),
    pltpu.VMEM((SEQ, 3 * HEADS * HD), LOW),
    pltpu.VMEM((3, 2, SEQ, PAIR), F32),
    pltpu.VMEM((SEQ, PAIR), F32),
    pltpu.VMEM((HEADS * HD, SEQ), LOW),
    pltpu.VMEM((PAIR, SEQ), F32),
]


def attention_outs(rows, tokens, width):
    heads = (rows, HEADS, SEQ, PAIR)
    return [struct(heads, LOW)] * 3 + [struct((tokens, width), LOW)]


def dense_outs(tokens, width, hidden):
    return [
        struct((tokens, width), F32),
        struct((tokens, width), F32),
        struct((tokens, PAIR), F32),
        struct((tokens, width), LOW),
        struct((tokens, hidden), LOW),
        struct((tokens, hidden), LOW),
    ]


def vmem(shape, dtype):
    return pltpu.VMEM(tuple(shape), dtype)


def attention_weights(width):
    return [vmem((width, 3 * width), LOW), vmem((1, 3 * width), F32)]


def dense_weights(width, hidden):
    return [
        vmem((width, width), LOW),
        vmem((width, hidden), LOW),
        vmem((hidden, width), LOW),
        vmem((8, width), F32),
        vmem((1, hidden), F32),
    ]


def dense_sums(width, hidden):
    return [
        vmem((width, width), F32),
        vmem((width, hidden), F32),
        vmem((width, hidden), F32),
        vmem((8, 8, width), F32),
        vmem((8, hidden), F32),
    ]


def attention_sums(width):
    return [vmem((width, 3 * width), F32), vmem((2, 8, width), F32)]


def dense_work(width, hidden):
    return [
        vmem((SEQ, width), LOW),
        vmem((2, SEQ, width), F32),
        vmem((SEQ, hidden), LOW),
        vmem((2, width, SEQ), LOW),
    ]


def set_attention(layer, urgent_ref, raw_ref, at, wq_ref, bias_ref):
    width = wq_ref.shape[0]
    unpack_matrix(raw_ref, at, wq_ref)
    vectors = unpack_vectors(urgent_ref, 3 * width, layer)
    bias_ref[:, :width] = vectors[0:1]
    bias_ref[:, width : 2 * width] = jnp.zeros((1, width), F32)
    bias_ref[:, 2 * width :] = vectors[1:2]


def set_dense(layer, urgent_ref, raw_ref, at, wo_ref, wi_ref, wf_ref, small_ref, bi_ref):
    width, hidden = wi_ref.shape
    unpack_matrix(raw_ref, at, wo_ref)
    unpack_matrix(raw_ref, at + width, wi_ref)
    unpack_stacked(raw_ref, at + width + hidden, wf_ref)
    small_ref[...] = unpack_vectors(urgent_ref, 3 * width, layer)
    bi_ref[...] = unpack_hidden(urgent_ref, 3 * width, layer, hidden)


def clear(refs):
    for ref in refs:
        ref[...] = jnp.zeros(ref.shape, ref.dtype)


def assemble(place_ref, part_refs, into_ref):
    for step, ref in enumerate(part_refs):
        into_ref[place_ref[0] ^ step] = ref[...]


def raw_block(parts):
    return vmem((len(parts),) + parts[0].shape, LOW)


def first_kernel(lengths, x, place, parts):
    rows, (tokens, width) = lengths.shape[0], x.shape

    def setup(numbers, fixed, sent, work):
        assemble(numbers[0], fixed, sent[0])
        set_attention(0, sent[0], sent[0], 0, *work)

    def body(row, lengths_ref, rowwise, outs, work, own):
        return attention_forward(row, lengths_ref, rowwise[0][...], *work, *outs, *own)

    return run_rows(
        body, lengths, [x], list(parts), attention_outs(rows, tokens, width),
        [struct((len(parts),) + parts[0].shape, LOW)],
        attention_weights(width), FORWARD_SCRATCH(), 4 * 10**9, setup, None, (), [place],
    )


def attention_kernel(layer, lengths, x, place, urgent, parts, at):
    rows, (tokens, width) = lengths.shape[0], x.shape

    def setup(numbers, fixed, sent, work):
        assemble(numbers[0], fixed[1:], work[2])
        set_attention(layer, fixed[0], work[2], at, *work[:2])

    def body(row, lengths_ref, rowwise, outs, work, own):
        return attention_forward(
            row, lengths_ref, rowwise[0][...].astype(LOW), *work[:2], *outs, *own
        )

    return run_rows(
        body, lengths, [x], [urgent] + list(parts), attention_outs(rows, tokens, width), [],
        attention_weights(width) + [raw_block(parts)], FORWARD_SCRATCH(),
        4 * 10**9, setup, None, (), [place],
    )


def dense_kernel(layer, lengths, x, ob, place, urgent, parts, at, hidden):
    tokens, width = x.shape

    def setup(numbers, fixed, sent, work):
        assemble(numbers[0], fixed[1:], work[5])
        set_dense(layer, fixed[0], work[5], at, *work[:5])

    def body(row, lengths_ref, rowwise, outs, work, own):
        return dense_forward(*rowwise, *work[:5], *outs, *own)

    return run_rows(
        body, lengths, [x, ob], [urgent] + list(parts),
        dense_outs(tokens, width, hidden) + [struct((tokens, width), F32)], [],
        dense_weights(width, hidden) + [raw_block(parts)],
        [vmem((SEQ, width), F32), vmem((2, SEQ, width), F32)],
        5 * 10**9, setup, None, (), [place],
    )


def turn_kernel(layer, lengths, x, ob, cotangent, place, urgent, parts, at, hidden):
    tokens, width = x.shape
    columns = width + 2 * hidden + width + hidden // 8

    def setup(numbers, fixed, sent, work):
        assemble(numbers[0], fixed[1:], work[11])
        set_dense(layer, fixed[0], work[11], at, *work[:5])
        clear(work[5:10])

    def body(row, lengths_ref, rowwise, outs, work, own):
        x_ref, ob_ref, dz_ref = rowwise
        z_ref, dr_ref, dob_ref = outs
        weights, sums = work[:5], work[5:10]
        kept, work_ref, back = own[:6], own[6], own[7:]
        yield from dense_forward(x_ref, ob_ref, *weights, *kept, z_ref, work_ref, back[1])
        yield from dense_backward(dz_ref, *kept, ob_ref, *weights[:4], dr_ref, dob_ref, *sums, *back)

    def finish(numbers, work, sent):
        pack_dense(*work[5:10], work[10], 0)
        hand_out(numbers[0], work[10], sent)

    kept = [vmem((SEQ,) + part.shape[1:], part.dtype) for part in dense_outs(tokens, width, hidden)]
    return run_rows(
        body, lengths, [x, ob, cotangent], [urgent] + list(parts),
        [struct((tokens, width), LOW), struct((tokens, width), F32), struct((tokens, width), LOW)],
        [struct((64, columns), LOW)] * 4,
        dense_weights(width, hidden) + dense_sums(width, hidden)
        + [vmem((4, 64, columns), LOW), raw_block(parts)],
        kept + [vmem((SEQ, width), F32)] + dense_work(width, hidden),
        10**10, setup, finish, (), [place],
    )


def hand_out(place_ref, packed_ref, sent):
    for step, ref in enumerate(sent):
        ref[...] = packed_ref[place_ref[0] ^ step]


def middle_kernel(lengths, upper, lower, place, urgent, parts1, parts0, hidden, after):
    tokens, width = upper[0].shape
    columns = 4 * width + width + 2 * hidden + width + hidden // 8

    def setup(numbers, fixed, sent, work):
        count = len(parts1)
        assemble(numbers[0], fixed[1 : 1 + count], work[15])
        assemble(numbers[0], fixed[1 + count :], work[16])
        set_attention(1, fixed[0], work[15], 0, *work[:2])
        set_dense(0, fixed[0], work[16], 0, *work[2:7])
        clear(work[7:14])

    def body(row, lengths_ref, rowwise, outs, work, own):
        up, low = rowwise[:7], rowwise[7:]
        dx_ref = own[0]
        yield from attention_backward(
            row, lengths_ref, up[0][...].astype(LOW), *up[1:6], work[0], up[6], dx_ref,
            *work[7:9], *own[5:],
        )
        yield from dense_backward(dx_ref, *low, *work[2:6], *outs, *work[9:14], *own[1:5])

    def finish(numbers, work, sent):
        pack_attention(*work[7:9], work[14], 0)
        pack_dense(*work[9:14], work[14], 4 * width)
        hand_out(numbers[0], work[14], sent)

    return run_rows(
        body, lengths, list(upper) + list(lower), [urgent] + list(parts1) + list(parts0),
        [struct((tokens, width), F32), struct((tokens, width), LOW)],
        [struct((64, columns), LOW)] * 4,
        attention_weights(width) + dense_weights(width, hidden)
        + attention_sums(width) + dense_sums(width, hidden)
        + [vmem((4, 64, columns), LOW), raw_block(parts1), raw_block(parts0)],
        [vmem((SEQ, width), F32)] + dense_work(width, hidden) + BACKWARD_SCRATCH(),
        15 * 10**9, setup, finish, after, [place], 1,
    )


def last_kernel(lengths, upper, urgent, after, place):
    tokens, width = upper[0].shape

    def setup(numbers, fixed, sent, work):
        set_attention(0, fixed[0], fixed[0], 0, *work[:2])
        clear(work[2:4])

    def body(row, lengths_ref, rowwise, outs, work, own):
        return attention_backward(
            row, lengths_ref, rowwise[0][...], *rowwise[1:6], work[0], rowwise[6], outs[0],
            *work[2:4], *own,
        )

    def finish(numbers, work, sent):
        pack_attention(*work[2:4], work[4], 0)
        hand_out(numbers[0], work[4], sent)

    return run_rows(
        body, lengths, list(upper), [urgent], [struct((tokens, width), LOW)],
        [struct((64, 4 * width), LOW)] * 4,
        attention_weights(width) + attention_sums(width) + [vmem((4, 64, 4 * width), LOW)],
        BACKWARD_SCRATCH(), 8 * 10**9, setup, finish, after, [place],
    )


def hold(array, after):
    def kernel(*refs):
        pass

    anywhere = pl.BlockSpec(memory_space=pl.ANY)
    return pl.pallas_call(
        kernel,
        in_specs=[anywhere] * (1 + len(after)),
        out_specs=anywhere,
        out_shape=shape_of(array),
        input_output_aliases={0: 0},
    )(array, *after)


def pack_parameters(
    attn_weight, attn_bias, out_weight, ffn_in, ffn_in_bias, ffn_out, norm_gain, shifts
):
    depth, rows, width = out_weight.shape
    copies = GROUPS[1]
    hidden = ffn_in.shape[2]
    early = 4 * width + 2 * hidden + 128
    columns = 4 * width + 2 * hidden
    height = ffn_in_bias.shape[1]

    def kernel(wq_ref, ab_ref, wo_ref, wi_ref, bi_ref, wf_ref, gain_ref, shift_ref, first_ref, rest_ref, small_ref):
        def put(ref, block, at):
            block = jnp.broadcast_to(block.astype(F32)[None], (copies,) + block.shape)
            block = block.reshape(copies * block.shape[1], block.shape[2])
            ref[:, pl.ds(at, block.shape[1])] = block.astype(LOW)

        small_ref[...] = jnp.zeros(small_ref.shape, F32)
        for layer in range(depth):
            lanes = pl.ds(rows * layer, rows)
            small_ref[0:2, lanes] = ab_ref[layer].astype(F32)
            small_ref[2:4, lanes] = gain_ref[layer].astype(F32)
            small_ref[4:8, lanes] = shift_ref[layer].astype(F32)
        small_ref[0:depth, pl.ds(2 * rows, height)] = bi_ref[...].astype(F32)
        put(first_ref, wq_ref[0], 0)
        put(first_ref, small_ref[...], 3 * width)
        for layer, ref, at in ((0, first_ref, 3 * width + 128), (1, rest_ref, 3 * width)):
            if layer:
                put(ref, wq_ref[layer], 0)
            put(ref, wo_ref[layer], at)
            put(ref, wi_ref[layer], at + width)
            at += width + hidden
            down = wf_ref[layer].astype(F32)
            for step in range(hidden // width):
                put(ref, down[step * rows : (step + 1) * rows], at)
                at += width

    return pl.pallas_call(
        kernel,
        in_specs=[pl.BlockSpec(memory_space=pltpu.VMEM)] * 8,
        out_shape=[struct((copies * rows, early), LOW), struct((copies * rows, columns), LOW)],
        scratch_shapes=[vmem((rows, 128), F32)],
        compiler_params=pltpu.CompilerParams(vmem_limit_bytes=MEMORY),
    )(attn_weight, attn_bias, out_weight, ffn_in, ffn_in_bias, ffn_out, norm_gain, shifts)


def add_parts(parts, after=(), joined=None):
    inner = [] if joined is None else [joined]
    ahead = 0 if joined is None else joined.shape[1]
    rows, lanes_in = parts[0].shape
    count = len(parts)

    def kernel(*refs):
        out_ref = refs[-1]
        if inner:
            out_ref[:, pl.ds(0, ahead)] = refs[count][...]
        columns = 256
        for start in range(0, lanes_in, columns):
            size = min(columns, lanes_in - start)
            total = refs[0][:, pl.ds(start, size)].astype(F32)
            for ref in refs[1:count]:
                total = total + ref[:, pl.ds(start, size)].astype(F32)
            out_ref[:, pl.ds(ahead + start, size)] = total.astype(LOW)

    near = pl.BlockSpec(memory_space=pltpu.VMEM)
    return pl.pallas_call(
        kernel,
        in_specs=[near] * (count + len(inner)) + [pl.BlockSpec(memory_space=pl.ANY)] * len(after),
        out_specs=near,
        out_shape=struct((rows, ahead + lanes_in), LOW),
        compiler_params=pltpu.CompilerParams(vmem_limit_bytes=MEMORY),
    )(*parts, *inner, *after)


def write_gradients(place, tail, front, depth, width, hidden):
    rows = GROUPS[2]
    last = front.shape[1] - 4 * width
    height = hidden // DEVICES

    def kernel(place_ref, tail_ref, front_ref, gwq_ref, gab_ref, gwo_ref, gwi_ref, gbi_ref, gwf_ref, gain_ref, shift_ref):
        spot = place_ref[0]

        def total(ref, at, columns):
            block = ref[:, pl.ds(at, columns)].astype(F32)
            return jnp.sum(block.reshape(-1, rows, columns), 0)

        def own(block, size):
            return pltpu.roll(block, block.shape[1] - spot * size, 1)

        for layer, ref, at in ((0, front_ref, last), (1, front_ref, 0)):
            gwq_ref[layer] = total(ref, at, 3 * width)
            gab_ref[layer] = own(total(ref, at + 3 * width, width), rows)[0:2, 0:rows]
        for layer, ref, at in ((0, front_ref, 4 * width), (1, tail_ref, 0)):
            gwo_ref[layer] = total(ref, at, width)
            gwi_ref[layer] = total(ref, at + width, hidden)
            for step in range(hidden // width):
                gwf_ref[layer, pl.ds(step * rows, rows)] = total(
                    ref, at + width + hidden + step * width, width
                )
            at += width + 2 * hidden
            small = own(total(ref, at, width), rows)
            gain_ref[layer] = small[2:4, 0:rows]
            shift_ref[layer] = small[4:8, 0:rows]
            line = total(ref, at + width, hidden // 8)
            line = jnp.concatenate([line[step : step + 1] for step in range(8)], 1)
            gbi_ref[pl.ds(layer, 1)] = own(line, height)[:, 0:height]

    outs = [
        struct((depth, rows, 3 * width), F32),
        struct((depth, 2, rows), F32),
        struct((depth, rows, width), F32),
        struct((depth, rows, hidden), F32),
        struct((depth, height), F32),
        struct((depth, height, width), F32),
        struct((depth, 2, rows), F32),
        struct((depth, 4, rows), F32),
    ]
    return pl.pallas_call(
        kernel,
        in_specs=[pl.BlockSpec(memory_space=pltpu.SMEM)] + [pl.BlockSpec(memory_space=pltpu.VMEM)] * 2,
        out_shape=outs,
        compiler_params=pltpu.CompilerParams(vmem_limit_bytes=MEMORY),
    )(place, tail, front)


def exchange(parts, axis):
    return lax.all_to_all(parts, axis, 0, 0, tiled=True)


def swap(part, axis, step):
    size = lax.axis_size(axis)
    return lax.ppermute(part, axis, [(source, source ^ step) for source in range(size)])


def local(
    hidden_in,
    lengths,
    grad_out,
    attn_weight,
    attn_bias,
    out_weight,
    ffn_in,
    ffn_in_bias,
    ffn_out,
    norm_gain,
    shifts,
):
    depth, rows, width = out_weight.shape
    hidden = ffn_in.shape[2]
    first, second = lax.axis_size("dp"), lax.axis_size("fsdp")
    fits = (second, first, rows) == GROUPS
    urgent_size = 3 * width + 128
    if fits:
        early, later = pack_parameters(
            attn_weight, attn_bias, out_weight, ffn_in, ffn_in_bias, ffn_out, norm_gain, shifts
        )
        early = exchange(early, "dp")
        partners = range(1, second)
        urgent = early[:, :urgent_size]
        urgent = [urgent] + [swap(urgent, "fsdp", step) for step in partners]
        later = exchange(hold(later, (early,)), "dp")
        raw0 = hold(early[:, urgent_size:], tuple(urgent))
        raw0 = [raw0] + [swap(raw0, "fsdp", step) for step in partners]
        place = lax.axis_index("fsdp").astype(jnp.int32).reshape(1)
    else:
        urgent, raw0, raw1 = gather_other(
            attn_weight, attn_bias, out_weight, ffn_in, ffn_in_bias, ffn_out, norm_gain, shifts
        )
        urgent, raw0, raw1 = ([part[step] for step in range(4)] for part in (urgent, raw0, raw1))
        place = jnp.zeros((1,), jnp.int32)

    qa0, ka0, va0, ob0, urgent = first_kernel(lengths, hidden_in, place, urgent)
    if fits:
        raw1 = hold(later, (ob0,))
        raw1 = [raw1] + [swap(raw1, "fsdp", step) for step in partners]
    n1, n2, inv, yb, gb, gp, z0 = dense_kernel(
        0, lengths, hidden_in, ob0, place, urgent, raw0, 0, hidden
    )
    qa1, ka1, va1, ob1 = attention_kernel(1, lengths, z0, place, urgent, raw1, 0)
    hidden_out, dr1, dob1, *sent_a = turn_kernel(
        1, lengths, z0, ob1, grad_out, place, urgent, raw1, 3 * width, hidden
    )
    dr0, dob0, *sent_b = middle_kernel(
        lengths,
        (z0, dob1, ob1, qa1, ka1, va1, dr1),
        (n1, n2, inv, yb, gb, gp, ob0),
        place,
        urgent,
        raw1,
        raw0,
        hidden,
        (sent_a[0],),
    )
    if fits:
        got_a = [sent_a[0]] + [swap(sent_a[step], "fsdp", step) for step in partners]
        tail = exchange(add_parts(got_a, (sent_b[0],)), "dp")
    grad_in, *sent_c = last_kernel(
        lengths, (hidden_in, dob0, ob0, qa0, ka0, va0, dr0), urgent, (sent_b[0],), place
    )
    if fits:
        got_b = [sent_b[0]] + [swap(sent_b[step], "fsdp", step) for step in partners]
        got_c = [sent_c[0]] + [swap(sent_c[step], "fsdp", step) for step in partners]
        front = add_parts(got_b, (tail,))
        front = add_parts(got_c, (), front)
        front = exchange(front, "dp")
        place = lax.axis_index(("dp", "fsdp")).astype(jnp.int32).reshape(1)
        grads = write_gradients(place, tail, front, depth, width, hidden)
    else:
        grads = scatter_other(
            *(jnp.stack(part) for part in (sent_a, sent_b, sent_c)), rows, width, hidden
        )
    return (hidden_out, grad_in, *grads)


def gather_other(
    attn_weight, attn_bias, out_weight, ffn_in, ffn_in_bias, ffn_out, norm_gain, shifts
):
    axes = ("dp", "fsdp")
    gather = lambda part, axis: lax.all_gather(part, axes, axis=axis, tiled=True)
    depth, unused, width = out_weight.shape
    hidden = ffn_in.shape[2]
    outer, inner, rows = GROUPS
    vectors = gather(jnp.concatenate([attn_bias, norm_gain, shifts], 1), 2)
    line = gather(ffn_in_bias, 1)

    def order(natural):
        return (
            natural.reshape(inner, outer, rows, -1).swapaxes(0, 1).reshape(outer, inner * rows, -1)
        )

    def stacked(part):
        part = part.reshape(DEVICES, -1, rows, width)
        return order(part.swapaxes(1, 2).reshape(width, -1))

    small = vectors.reshape(depth, 8, DEVICES, rows).transpose(2, 1, 0, 3).reshape(width, -1)
    line = line.reshape(depth, DEVICES, -1).swapaxes(0, 1)
    line = jnp.pad(line, ((0, 0), (0, 8 - depth), (0, 0))).reshape(width, -1)
    small = jnp.concatenate([small, line], 1)
    small = jnp.pad(small, ((0, 0), (0, 128 - small.shape[1])))
    wq, wo, wi, wf = (gather(part, 1) for part in (attn_weight, out_weight, ffn_in, ffn_out))
    urgent = jnp.concatenate([order(wq[0]), order(small)], 2)
    raw0 = jnp.concatenate([order(wo[0]), order(wi[0]), stacked(wf[0])], 2)
    raw1 = jnp.concatenate([order(wq[1]), order(wo[1]), order(wi[1]), stacked(wf[1])], 2)
    return urgent, raw0, raw1


def scatter_other(sent_a, sent_b, sent_c, own_rows, width, hidden):
    outer, inner, rows = GROUPS
    axes = ("dp", "fsdp")

    def natural(part):
        return part.reshape(outer, inner, rows, -1).swapaxes(0, 1).reshape(width, -1).astype(F32)

    def cut(part, sizes):
        found, at = [], 0
        for size in sizes:
            found.append(part[:, at : at + size])
            at += size
        return found

    dense = [width, hidden, hidden, width, hidden // 8]
    attention = [3 * width, width]
    wq0, ab0 = cut(natural(sent_c), attention)
    wq1, ab1, wo0, wi0, wf0, small0, bi0 = cut(natural(sent_b), attention + dense)
    wo1, wi1, wf1, small1, bi1 = cut(natural(sent_a), dense)

    def stacked(part):
        part = part.reshape(DEVICES, rows, -1, width).swapaxes(1, 2)
        return part.reshape(hidden, width)

    def spread(parts, axis):
        return lax.psum_scatter(jnp.stack(parts), axes, scatter_dimension=axis, tiled=True)

    return (
        spread([wq0, wq1], 1),
        spread([ab0[:2], ab1[:2]], 2),
        spread([wo0, wo1], 1),
        spread([wi0, wi1], 1),
        spread([bi0[:8].reshape(-1), bi1[:8].reshape(-1)], 1),
        spread([stacked(wf0), stacked(wf1)], 1),
        spread([small0[2:4], small1[2:4]], 2),
        spread([small0[4:8], small1[4:8]], 2),
    )


def solution(mesh):
    placed = (
        P(("dp", "fsdp"), None),
        P(("dp", "fsdp"), None),
        P(("dp", "fsdp"), None),
        P(None, ("dp", "fsdp"), None),
        P(None, None, ("dp", "fsdp")),
        P(None, ("dp", "fsdp"), None),
        P(None, ("dp", "fsdp"), None),
        P(None, ("dp", "fsdp")),
        P(None, ("dp", "fsdp"), None),
        P(None, None, ("dp", "fsdp")),
        P(None, None, ("dp", "fsdp")),
    )
    return jax.shard_map(
        local,
        mesh=mesh,
        in_specs=placed,
        out_specs=(
            P(("dp", "fsdp"), None),
            P(("dp", "fsdp"), None),
            P(None, ("dp", "fsdp"), None),
            P(None, None, ("dp", "fsdp")),
            P(None, ("dp", "fsdp"), None),
            P(None, ("dp", "fsdp"), None),
            P(None, ("dp", "fsdp")),
            P(None, ("dp", "fsdp"), None),
            P(None, None, ("dp", "fsdp")),
            P(None, None, ("dp", "fsdp")),
        ),
        check_vma=False,
    )
```

```python
from functools import partial

import jax
import jax.numpy as jnp
from jax import lax
from jax.experimental import pallas as pl
from jax.experimental.pallas import tpu as pltpu
from jax.sharding import PartitionSpec as P

HEADS = 4
HD = 64
SEQ = 512
PAIR = 2 * HD
FAR = -(2.0**100)
FLOOR = -1e20
EPSILON = 1e-12
PIECE = 256
SMALL = 128
GROUPS = (4, 8, 8)
DEVICES = 32
LOW = jnp.bfloat16
F32 = jnp.float32
MEMORY = 2**26


def dot_nn(left, right):
    return lax.dot_general(left, right, (((1,), (0,)), ((), ())), preferred_element_type=F32)


def dot_nt(left, right):
    return lax.dot_general(left, right, (((1,), (1,)), ((), ())), preferred_element_type=F32)


def dot_tn(left, right):
    return lax.dot_general(left, right, (((0,), (0,)), ((), ())), preferred_element_type=F32)


def pieces(total, size=PIECE):
    return [pl.ds(start, size) for start in range(0, total, size)]


def three_parts(values):
    first = values.astype(LOW).astype(F32)
    rest = values - first
    second = rest.astype(LOW).astype(F32)
    return first, second, rest - second


CURVE = (7.97869556e-01, 3.63928094e-02, -8.82195179e-05, -3.66000319e-05, 1.41853144e-06)
BELL = -0.5 / 0.6931471805599453


def gelu_parts(u):
    square = u * u
    curve = CURVE[-1]
    for factor in CURVE[-2::-1]:
        curve = curve * square + factor
    cumulative = 0.5 + 0.5 * jnp.tanh(u * curve)
    slope = cumulative + (u * 0.3989422804014327) * jnp.exp2(square * BELL)
    return u * cumulative, slope


def inverse_of(values):
    guess = pl.reciprocal(values, approx=True)
    return guess * (2.0 - values * guess)


def lane_facts():
    lane = lax.broadcasted_iota(jnp.int32, (1, PAIR), 1)
    return lane < HD, lane & (HD - 1)


def segments(lengths_ref, row, start, rows):
    places = lax.broadcasted_iota(jnp.int32, (rows, 1), 0) + start
    bound = jnp.int32(0)
    segment = jnp.zeros((rows, 1), jnp.int32)
    last = lengths_ref.shape[1] - 1
    for entry in range(last):
        bound = bound + lengths_ref[row, entry]
        segment = segment + (places >= bound).astype(jnp.int32)
    return segment, (segment == last).astype(F32), last


def attention_forward(row, lengths_ref, x, wq_ref, bias_ref, qa_ref, ka_ref, va_ref, ob_ref, s_ref, p_ref, m_ref, pad_ref, q_ref, aug_ref):
    width = HEADS * HD
    for block in range(3):
        at = block * width
        value = dot_nn(x, wq_ref[:, at : at + width]) + bias_ref[:, at : at + width]
        for pair in range(HEADS // 2):
            q_ref[block, pair] = value[:, pair * PAIR : (pair + 1) * PAIR]
        yield
    for start in range(0, SEQ, PIECE):
        place = pl.ds(start, PIECE)
        low_half, slot = lane_facts()
        segment, pad, last = segments(lengths_ref, row, start, PIECE)
        pad_ref[place] = jnp.broadcast_to(pad, (PIECE, PAIR))
        aug_q = jnp.where(slot == segment, 1.0, 0.0)
        aug_ref[place] = aug_q
        seen = (slot == segment) & (slot != last)
        aug_k = jnp.where(seen, 0.0, jnp.where(slot <= last, FAR, jnp.where(slot <= last + 3, 1.0, 0.0)))
        for pair in range(HEADS // 2):
            q = q_ref[0, pair, place] * HD**-0.5
            k = q_ref[1, pair, place]
            v = q_ref[2, pair, place]
            q_ref[0, pair, place] = q
            qa_ref[2 * pair, place] = jnp.where(low_half, q, aug_q).astype(LOW)
            qa_ref[2 * pair + 1, place] = jnp.where(low_half, aug_q, q).astype(LOW)
            ka_ref[2 * pair, place] = jnp.where(low_half, k, aug_k).astype(LOW)
            ka_ref[2 * pair + 1, place] = jnp.where(low_half, aug_k, k).astype(LOW)
            va_ref[2 * pair, place] = jnp.where(low_half, v, 1.0).astype(LOW)
            va_ref[2 * pair + 1, place] = jnp.where(low_half, 1.0, v).astype(LOW)
        yield

    def scores(head):
        s_ref[head % 2] = dot_nt(qa_ref[head], ka_ref[head])

    def softmax(head):
        for place in pieces(SEQ):
            highest = jnp.maximum(jnp.max(s_ref[head % 2, place], -1, keepdims=True), FLOOR)
            m_ref[head % 2, place] = jnp.broadcast_to(highest, (PIECE, PAIR))
            p_ref[head % 2, place] = jnp.exp(s_ref[head % 2, place] - highest).astype(LOW)

    scores(0)
    yield
    for head in range(HEADS):
        if head + 1 < HEADS:
            scores(head + 1)
            yield
        softmax(head)
        yield
        q_ref[1, head % 2] = dot_nn(p_ref[head % 2], va_ref[head])
        if head % 2:
            pair = head // 2
            for start in range(0, SEQ, PIECE):
                place = pl.ds(start, PIECE)
                low_half, slot = lane_facts()
                even = q_ref[1, 0, place]
                odd = q_ref[1, 1, place]
                pad = pad_ref[place]
                last = lengths_ref.shape[1] - 1
                total = jnp.where(low_half, odd, even) + pad
                top = jnp.where(low_half, m_ref[1, place], m_ref[0, place])
                spread = jnp.where(pad > 0, 0.0, top + jnp.log(total))
                first, second, third = three_parts(spread)
                aug = jnp.where(
                    slot == last + 1,
                    -first,
                    jnp.where(slot == last + 2, -second, jnp.where(slot == last + 3, -third, aug_ref[place])),
                )
                q = q_ref[0, pair, place]
                qa_ref[2 * pair, place] = jnp.where(low_half, q, aug).astype(LOW)
                qa_ref[2 * pair + 1, place] = jnp.where(low_half, aug, q).astype(LOW)
                v = q_ref[2, pair, place].astype(LOW).astype(F32)
                share = inverse_of(pltpu.roll(total, HD, 1))
                out = jnp.where(low_half, even, odd) * share + pad * v
                ob_ref[place, pl.ds(pair * PAIR, PAIR)] = out.astype(LOW)
            yield


def normal(values):
    centred = values - jnp.mean(values, -1, keepdims=True)
    inverse = lax.rsqrt(jnp.mean(centred * centred, -1, keepdims=True) + EPSILON)
    return centred * inverse, inverse


def normal_back(cotangent, unit, inverse, gains):
    scaled = cotangent * gains
    return inverse * (
        scaled
        - jnp.mean(scaled, -1, keepdims=True)
        - unit * jnp.mean(scaled * unit, -1, keepdims=True)
    )


def dense_forward(x_ref, ob_ref, wo_ref, wi_ref, wf_ref, small_ref, bi_ref, n1_ref, n2_ref, inv_ref, yb_ref, gb_ref, gp_ref, z_ref, work_ref, u_ref):
    small = lambda index: small_ref[pl.ds(index, 1)]
    work_ref[...] = dot_nn(ob_ref[...], wo_ref[...])
    yield
    for place in pieces(SEQ):
        unit, inverse = normal(x_ref[place].astype(F32) + work_ref[place] + small(4))
        n1_ref[place] = unit
        inv_ref[place, pl.ds(0, HD)] = jnp.broadcast_to(inverse, (PIECE, HD))
        y = unit * small(2) + small(5)
        yb_ref[place] = y.astype(LOW)
        work_ref[place] = y + small(6)
        yield
    columns = 256
    count = wi_ref.shape[1] // columns

    def into(step):
        u_ref[step % 2] = dot_nn(yb_ref[...], wi_ref[:, pl.ds(step * columns, columns)])

    into(0)
    yield
    for step in range(count):
        if step + 1 < count:
            into(step + 1)
            yield
        lanes = pl.ds(step * columns, columns)
        for place in pieces(SEQ, SMALL):
            g, slope = gelu_parts(u_ref[step % 2, place] + bi_ref[:, lanes])
            gb_ref[place, lanes] = g.astype(LOW)
            gp_ref[place, lanes] = slope.astype(LOW)
            yield
    work_ref[...] += dot_nn(gb_ref[...], wf_ref[...])
    yield
    for place in pieces(SEQ):
        unit, inverse = normal(work_ref[place])
        n2_ref[place] = unit
        inv_ref[place, pl.ds(HD, HD)] = jnp.broadcast_to(inverse, (PIECE, HD))
        z_ref[place] = (unit * small(3) + small(7)).astype(z_ref.dtype)
        yield


def fold(values):
    return jnp.sum(values.reshape(-1, 8, values.shape[-1]), 0)


def dense_backward(dz_ref, n1_ref, n2_ref, inv_ref, yb_ref, gb_ref, gp_ref, ob_ref, wo_ref, wi_ref, wf_ref, small_ref, dr_ref, dob_ref, gwo_ref, gwi_ref, gwf_ref, gsmall_ref, gbi_ref, low_ref, u_ref, du_ref, turned_ref):
    small = lambda index: small_ref[pl.ds(index, 1)]
    for place in pieces(SEQ):
        dz = dz_ref[place].astype(F32)
        unit = n2_ref[place]
        gsmall_ref[3] += fold(dz * unit)
        gsmall_ref[7] += fold(dz)
        dr = normal_back(dz, unit, inv_ref[place, pl.ds(HD, 1)], small(3))
        dr_ref[place] = dr
        df = dr.astype(LOW)
        low_ref[place] = df
        gsmall_ref[6] += fold(df.astype(F32))
        yield
    columns = 256
    count = wi_ref.shape[1] // columns

    def back(step):
        u_ref[step % 2] = dot_nt(low_ref[...], wf_ref[pl.ds(step * columns, columns)])

    back(0)
    turned_ref[0] = low_ref[...].T
    turned_ref[1] = yb_ref[...].T
    yield
    for step in range(count):
        if step + 1 < count:
            back(step + 1)
            yield
        lanes = pl.ds(step * columns, columns)
        gwf_ref[:, lanes] += dot_nn(turned_ref[0], gb_ref[:, lanes])
        yield
        for place in pieces(SEQ, SMALL):
            du = (u_ref[step % 2, place] * gp_ref[place, lanes].astype(F32)).astype(LOW)
            du_ref[place, lanes] = du
            gbi_ref[:, lanes] += fold(du.astype(F32))
        yield
        gwi_ref[:, lanes] += dot_nn(turned_ref[1], du_ref[:, lanes])
        yield
    u_ref[0] = dot_nt(du_ref[...], wi_ref[...])
    yield
    for place in pieces(SEQ):
        dy = dr_ref[place] + u_ref[0, place]
        unit = n1_ref[place]
        gsmall_ref[2] += fold(dy * unit)
        gsmall_ref[5] += fold(dy)
        dr = normal_back(dy, unit, inv_ref[place, pl.ds(0, 1)], small(2))
        dr_ref[place] = dr
        da = dr.astype(LOW)
        low_ref[place] = da
        gsmall_ref[4] += fold(da.astype(F32))
        yield
    gwo_ref[...] += dot_tn(ob_ref[...], low_ref[...])
    dob_ref[...] = dot_nt(low_ref[...], wo_ref[...]).astype(LOW)
    yield


def attention_backward(row, lengths_ref, x, dob_ref, ob_ref, qa_ref, ka_ref, va_ref, wq_ref, dr_ref, dx_ref, gwq_ref, gbias_ref, da_ref, p_ref, ds_ref, s_ref, dqkv_ref, dq_ref, pad_ref, kt_ref, dqt_ref):
    width = HEADS * HD
    low_half, slot = lane_facts()
    for start in range(0, SEQ, PIECE):
        place = pl.ds(start, PIECE)
        segment, pad, last = segments(lengths_ref, row, start, PIECE)
        pad_ref[place] = jnp.broadcast_to(pad, (PIECE, PAIR))
        for pair in range(HEADS // 2):
            lanes = pl.ds(pair * PAIR, PAIR)
            dob = dob_ref[place, lanes].astype(F32)
            product = dob * ob_ref[place, lanes].astype(F32)
            even = jnp.sum(jnp.where(low_half, product, 0.0), -1, keepdims=True)
            odd = jnp.sum(jnp.where(low_half, 0.0, product), -1, keepdims=True)
            first, second, third = three_parts(jnp.where(low_half, odd, even))
            aug = jnp.where(
                slot == 0, -first, jnp.where(slot == 1, -second, jnp.where(slot == 2, -third, 0.0))
            )
            da_ref[2 * pair, place] = jnp.where(low_half, dob, aug).astype(LOW)
            da_ref[2 * pair + 1, place] = jnp.where(low_half, aug, dob).astype(LOW)
        yield
    for pair in range(HEADS // 2):
        low_half, unused = lane_facts()
        keys = jnp.where(low_half, ka_ref[2 * pair].astype(F32), ka_ref[2 * pair + 1].astype(F32))
        kt_ref[pl.ds(pair * PAIR, PAIR)] = keys.T.astype(LOW)
    low_half, slot = lane_facts()

    def scores(head):
        s_ref[0, head % 2] = dot_nt(ka_ref[head], qa_ref[head])
        s_ref[1, head % 2] = dot_nt(va_ref[head], da_ref[head])

    def weigh(head):
        for place in pieces(SEQ, SMALL):
            p = jnp.exp(s_ref[0, head % 2, place])
            p_ref[head % 2, place] = p.astype(LOW)
            ds_ref[head % 2, place] = (p * s_ref[1, head % 2, place]).astype(LOW)

    scores(0)
    yield
    for head in range(HEADS):
        if head + 1 < HEADS:
            scores(head + 1)
            yield
        weigh(head)
        yield
        side = head % 2
        dq_ref[1, side] = dot_nn(ds_ref[head % 2], qa_ref[head])
        dq_ref[2, side] = dot_nn(p_ref[head % 2], da_ref[head])
        dqt_ref[pl.ds(side * HD, HD)] = dot_nn(kt_ref[pl.ds(head * HD, HD)], ds_ref[head % 2])
        yield
        if side:
            pair = head // 2
            dq_ref[0, 0] = dqt_ref[...].T
            for start in range(0, SEQ, PIECE):
                place = pl.ds(start, PIECE)
                dq = dq_ref[0, 0, place] * HD**-0.5
                dk = jnp.where(low_half, dq_ref[1, 0, place], dq_ref[1, 1, place])
                dv = jnp.where(low_half, dq_ref[2, 0, place], dq_ref[2, 1, place])
                dv = dv + pad_ref[place] * dob_ref[place, pl.ds(pair * PAIR, PAIR)].astype(F32)
                for block, value in enumerate((dq, dk, dv)):
                    lanes = pl.ds(block * width + pair * PAIR, PAIR)
                    value = value.astype(LOW)
                    dqkv_ref[place, lanes] = value
                    if block != 1:
                        into = pl.ds(pair * PAIR, PAIR)
                        gbias_ref[block // 2, :, into] += fold(value.astype(F32))
    yield
    gwq_ref[...] += dot_tn(x, dqkv_ref[...])
    yield
    dx_ref[...] = (dr_ref[...] + dot_nt(dqkv_ref[...], wq_ref[...])).astype(dx_ref.dtype)
    yield


def unpack_matrix(raw_ref, at, into_ref):
    width = into_ref.shape[0]
    for start in range(0, into_ref.shape[1], width):
        block = raw_ref[:, :, pl.ds(at + start, width)].astype(F32)
        block = block.reshape(GROUPS + (width,)).swapaxes(0, 1).reshape(width, width)
        into_ref[:, pl.ds(start, width)] = block.astype(LOW)


def unpack_stacked(raw_ref, at, into_ref):
    width = into_ref.shape[1]
    count = into_ref.shape[0] // width
    blocks = [
        raw_ref[:, :, pl.ds(at + step * width, width)].astype(F32).reshape(GROUPS + (width,))
        for step in range(count)
    ]
    outer, inner, rows = GROUPS
    for place in range(inner):
        part = jnp.stack([jnp.stack([block[f, place] for block in blocks]) for f in range(outer)])
        size = outer * count * rows
        into_ref[pl.ds(place * size, size)] = part.reshape(size, width).astype(LOW)


def counter(shape, axis):
    return lax.broadcasted_iota(jnp.int32, shape, axis)


def split_by(values, size):
    return lax.shift_right_logical(values, size.bit_length() - 1), values & (size - 1)


def sources(rows):
    outer, inner, height = GROUPS
    group, within = split_by(counter((rows, 1), 0), height)
    far, near = split_by(group, inner)
    return near * outer + far, within


def unpack_vectors(raw_ref, at, layer):
    outer, inner, rows = GROUPS
    total = outer * inner * rows
    raw = raw_ref[:, :, pl.ds(at, 128)].reshape(total, 128)
    owner, place = split_by(counter((1, total), 1), rows)
    pick = jnp.where(counter((128, 1), 0) == rows * layer + place, 1.0, 0.0).astype(LOW)
    device, unused = sources(total)
    spread = jnp.where(owner == device, dot_nn(raw, pick), 0.0)
    return jnp.sum(spread.reshape(outer * inner, rows, total), 0)


def unpack_hidden(raw_ref, at, layer, hidden):
    outer, inner, rows = GROUPS
    total = outer * inner * rows
    raw = raw_ref[:, :, pl.ds(at, 128)].reshape(total, 128)
    owner, place = split_by(counter((1, hidden), 1), hidden // (outer * inner))
    pick = jnp.where(counter((128, 1), 0) == 2 * rows + place, 1.0, 0.0).astype(LOW)
    device, within = sources(total)
    device = jnp.where(within == layer, device, -1)
    spread = jnp.where(owner == device, dot_nn(raw, pick), 0.0)
    return jnp.sum(spread, 0, keepdims=True)


def pack_matrix(sum_ref, sent_ref, at):
    width = sum_ref.shape[0]
    outer, inner, rows = GROUPS
    for start in range(0, sum_ref.shape[1], width):
        block = sum_ref[:, pl.ds(start, width)].reshape(inner, outer, rows, width)
        block = block.swapaxes(0, 1).reshape(outer, inner * rows, width)
        sent_ref[:, :, pl.ds(at + start, width)] = block.astype(LOW)


def pack_stacked(sum_ref, sent_ref, at):
    width = sum_ref.shape[0]
    outer, inner, rows = GROUPS
    count = sum_ref.shape[1] // width
    near = inner // count
    for step in range(count):
        block = sum_ref[:, pl.ds(step * width, width)].T
        block = block.reshape(near, outer, count, rows, width)
        for part in range(count):
            piece = jnp.stack([block[:, f, part] for f in range(outer)])
            piece = piece.reshape(outer, near * rows, width)
            sent_ref[:, pl.ds(step * near * rows, near * rows), pl.ds(at + part * width, width)] = (
                piece.astype(LOW)
            )


def pack_shared(block, sent_ref, at):
    outer, inner, rows = GROUPS
    columns = block.shape[1]
    block = jnp.broadcast_to(block[None], (outer * inner, rows, columns))
    sent_ref[:, :, pl.ds(at, columns)] = block.reshape(outer, inner * rows, columns).astype(LOW)


def folded(line, lanes):
    return [line[:, at : at + lanes] for at in range(0, line.shape[1], lanes)]


def pack_attention(gwq_ref, gbias_ref, sent_ref, at):
    pack_matrix(gwq_ref, sent_ref, at)
    width = gwq_ref.shape[0]
    parts = []
    for index in range(2):
        parts += folded(jnp.sum(gbias_ref[index], 0, keepdims=True), 128)
    block = jnp.concatenate(parts + [jnp.zeros((8 - len(parts), 128), F32)], 0)
    pack_shared(block, sent_ref, at + 3 * width)


def pack_dense(gwo_ref, gwi_ref, gwf_ref, gsmall_ref, gbi_ref, sent_ref, at):
    width, hidden = gwi_ref.shape
    pack_matrix(gwo_ref, sent_ref, at)
    pack_matrix(gwi_ref, sent_ref, at + width)
    pack_stacked(gwf_ref, sent_ref, at + width + hidden)
    at = at + width + 2 * hidden
    pack_shared(jnp.sum(gsmall_ref[...], 1), sent_ref, at)
    line = jnp.sum(gbi_ref[...], 0, keepdims=True)
    pack_shared(jnp.concatenate(folded(line, hidden // 8), 0), sent_ref, at + width)


def shape_of(array):
    return jax.ShapeDtypeStruct(array.shape, array.dtype)


def by_row(shape, group):
    if len(shape) == 2:
        return pl.BlockSpec((group * SEQ, shape[1]), lambda step: (step, 0))
    return pl.BlockSpec((group,) + tuple(shape[1:]), lambda step: (step,) + (0,) * (len(shape) - 1))


def one_row(ref, member):
    if len(ref.shape) == 2:
        return ref.at[pl.ds(member * SEQ, SEQ)]
    return ref.at[member]


def alternate(runs):
    running = []
    waiting = list(runs)
    while running or waiting:
        if waiting:
            running.append(waiting.pop(0))
        for run in list(running):
            try:
                next(run)
            except StopIteration:
                running.remove(run)


def whole(shape):
    return pl.BlockSpec(tuple(shape), lambda row: (0,) * len(shape))


def run_rows(
    body, lengths, rowwise, fixed, row_outs, sent, shared, private, cost, setup, finish, after=(),
    scalars=(), group=1
):
    count = lengths.shape[0]
    group = group if count % group == 0 else 1
    cuts = [len(scalars), len(rowwise), len(fixed), len(after), len(row_outs), len(sent)]
    cuts += [len(shared)] + [len(private)] * group

    def kernel(lengths_ref, *refs):
        step = pl.program_id(0)
        groups = []
        at = 0
        for cut in cuts:
            groups.append(refs[at : at + cut])
            at += cut
        numbers, rows_in, fixed_in, unused, rows_out, sent_out, work = groups[:7]

        @pl.when(step == 0)
        def _():
            setup(numbers, fixed_in, sent_out, work)

        alternate(
            body(
                step * group + member,
                lengths_ref,
                [one_row(ref, member) for ref in rows_in],
                [one_row(ref, member) for ref in rows_out],
                work,
                groups[7 + member],
            )
            for member in range(group)
        )

        if finish:

            @pl.when(step == count // group - 1)
            def _():
                finish(numbers, work, sent_out)

    return pl.pallas_call(
        kernel,
        grid=(count // group,),
        in_specs=[pl.BlockSpec(memory_space=pltpu.SMEM)] * (1 + len(scalars))
        + [by_row(array.shape, group) for array in rowwise]
        + [whole(array.shape) for array in fixed]
        + [pl.BlockSpec(memory_space=pl.ANY) for array in after],
        out_specs=[by_row(part.shape, group) for part in row_outs]
        + [whole(part.shape) for part in sent],
        out_shape=list(row_outs) + list(sent),
        scratch_shapes=list(shared) + list(private) * group,
        compiler_params=pltpu.CompilerParams(
            dimension_semantics=("arbitrary",), vmem_limit_bytes=MEMORY
        ),
        cost_estimate=pl.CostEstimate(flops=cost, bytes_accessed=8 * 2**20, transcendentals=0),
    )(lengths, *scalars, *rowwise, *fixed, *after)


def struct(shape, dtype):
    return jax.ShapeDtypeStruct(tuple(shape), dtype)


FORWARD_SCRATCH = lambda: [
    pltpu.VMEM((2, SEQ, SEQ), F32),
    pltpu.VMEM((2, SEQ, SEQ), LOW),
    pltpu.VMEM((2, SEQ, PAIR), F32),
    pltpu.VMEM((SEQ, PAIR), F32),
    pltpu.VMEM((3, HEADS // 2, SEQ, PAIR), F32),
    pltpu.VMEM((SEQ, PAIR), F32),
]
BACKWARD_SCRATCH = lambda: [
    pltpu.VMEM((HEADS, SEQ, PAIR), LOW),
    pltpu.VMEM((2, SEQ, SEQ), LOW),
    pltpu.VMEM((2, SEQ, SEQ), LOW),
    pltpu.VMEM((2, 2, SEQ, SEQ), F32),
    pltpu.VMEM((SEQ, 3 * HEADS * HD), LOW),
    pltpu.VMEM((3, 2, SEQ, PAIR), F32),
    pltpu.VMEM((SEQ, PAIR), F32),
    pltpu.VMEM((HEADS * HD, SEQ), LOW),
    pltpu.VMEM((PAIR, SEQ), F32),
]


def attention_outs(rows, tokens, width):
    heads = (rows, HEADS, SEQ, PAIR)
    return [struct(heads, LOW)] * 3 + [struct((tokens, width), LOW)]


def dense_outs(tokens, width, hidden):
    return [
        struct((tokens, width), F32),
        struct((tokens, width), F32),
        struct((tokens, PAIR), F32),
        struct((tokens, width), LOW),
        struct((tokens, hidden), LOW),
        struct((tokens, hidden), LOW),
    ]


def vmem(shape, dtype):
    return pltpu.VMEM(tuple(shape), dtype)


def attention_weights(width):
    return [vmem((width, 3 * width), LOW), vmem((1, 3 * width), F32)]


def dense_weights(width, hidden):
    return [
        vmem((width, width), LOW),
        vmem((width, hidden), LOW),
        vmem((hidden, width), LOW),
        vmem((8, width), F32),
        vmem((1, hidden), F32),
    ]


def dense_sums(width, hidden):
    return [
        vmem((width, width), F32),
        vmem((width, hidden), F32),
        vmem((width, hidden), F32),
        vmem((8, 8, width), F32),
        vmem((8, hidden), F32),
    ]


def attention_sums(width):
    return [vmem((width, 3 * width), F32), vmem((2, 8, width), F32)]


def dense_work(width, hidden):
    return [
        vmem((SEQ, width), LOW),
        vmem((2, SEQ, width), F32),
        vmem((SEQ, hidden), LOW),
        vmem((2, width, SEQ), LOW),
    ]


def set_attention(layer, urgent_ref, raw_ref, at, wq_ref, bias_ref):
    width = wq_ref.shape[0]
    unpack_matrix(raw_ref, at, wq_ref)
    vectors = unpack_vectors(urgent_ref, 3 * width, layer)
    bias_ref[:, :width] = vectors[0:1]
    bias_ref[:, width : 2 * width] = jnp.zeros((1, width), F32)
    bias_ref[:, 2 * width :] = vectors[1:2]


def set_dense(layer, urgent_ref, raw_ref, at, wo_ref, wi_ref, wf_ref, small_ref, bi_ref):
    width, hidden = wi_ref.shape
    unpack_matrix(raw_ref, at, wo_ref)
    unpack_matrix(raw_ref, at + width, wi_ref)
    unpack_stacked(raw_ref, at + width + hidden, wf_ref)
    small_ref[...] = unpack_vectors(urgent_ref, 3 * width, layer)
    bi_ref[...] = unpack_hidden(urgent_ref, 3 * width, layer, hidden)


def clear(refs):
    for ref in refs:
        ref[...] = jnp.zeros(ref.shape, ref.dtype)


def assemble(place_ref, part_refs, into_ref):
    for step, ref in enumerate(part_refs):
        into_ref[place_ref[0] ^ step] = ref[...]


def raw_block(parts):
    return vmem((len(parts),) + parts[0].shape, LOW)


def first_kernel(lengths, x, place, parts):
    rows, (tokens, width) = lengths.shape[0], x.shape

    def setup(numbers, fixed, sent, work):
        assemble(numbers[0], fixed, sent[0])
        set_attention(0, sent[0], sent[0], 0, *work)

    def body(row, lengths_ref, rowwise, outs, work, own):
        return attention_forward(row, lengths_ref, rowwise[0][...], *work, *outs, *own)

    return run_rows(
        body, lengths, [x], list(parts), attention_outs(rows, tokens, width),
        [struct((len(parts),) + parts[0].shape, LOW)],
        attention_weights(width), FORWARD_SCRATCH(), 4 * 10**9, setup, None, (), [place],
    )


def attention_kernel(layer, lengths, x, place, urgent, parts, at):
    rows, (tokens, width) = lengths.shape[0], x.shape

    def setup(numbers, fixed, sent, work):
        assemble(numbers[0], fixed[1:], work[2])
        set_attention(layer, fixed[0], work[2], at, *work[:2])

    def body(row, lengths_ref, rowwise, outs, work, own):
        return attention_forward(
            row, lengths_ref, rowwise[0][...].astype(LOW), *work[:2], *outs, *own
        )

    return run_rows(
        body, lengths, [x], [urgent] + list(parts), attention_outs(rows, tokens, width), [],
        attention_weights(width) + [raw_block(parts)], FORWARD_SCRATCH(),
        4 * 10**9, setup, None, (), [place],
    )


def dense_kernel(layer, lengths, x, ob, place, urgent, parts, at, hidden):
    tokens, width = x.shape

    def setup(numbers, fixed, sent, work):
        assemble(numbers[0], fixed[1:], work[5])
        set_dense(layer, fixed[0], work[5], at, *work[:5])

    def body(row, lengths_ref, rowwise, outs, work, own):
        return dense_forward(*rowwise, *work[:5], *outs, *own)

    return run_rows(
        body, lengths, [x, ob], [urgent] + list(parts),
        dense_outs(tokens, width, hidden) + [struct((tokens, width), F32)], [],
        dense_weights(width, hidden) + [raw_block(parts)],
        [vmem((SEQ, width), F32), vmem((2, SEQ, width), F32)],
        5 * 10**9, setup, None, (), [place],
    )


def turn_kernel(layer, lengths, x, ob, cotangent, place, urgent, parts, at, hidden):
    tokens, width = x.shape
    columns = width + 2 * hidden + width + hidden // 8

    def setup(numbers, fixed, sent, work):
        assemble(numbers[0], fixed[1:], work[11])
        set_dense(layer, fixed[0], work[11], at, *work[:5])
        clear(work[5:10])

    def body(row, lengths_ref, rowwise, outs, work, own):
        x_ref, ob_ref, dz_ref = rowwise
        z_ref, dr_ref, dob_ref = outs
        weights, sums = work[:5], work[5:10]
        kept, work_ref, back = own[:6], own[6], own[7:]
        yield from dense_forward(x_ref, ob_ref, *weights, *kept, z_ref, work_ref, back[1])
        yield from dense_backward(dz_ref, *kept, ob_ref, *weights[:4], dr_ref, dob_ref, *sums, *back)

    def finish(numbers, work, sent):
        pack_dense(*work[5:10], work[10], 0)
        hand_out(numbers[0], work[10], sent)

    kept = [vmem((SEQ,) + part.shape[1:], part.dtype) for part in dense_outs(tokens, width, hidden)]
    return run_rows(
        body, lengths, [x, ob, cotangent], [urgent] + list(parts),
        [struct((tokens, width), LOW), struct((tokens, width), F32), struct((tokens, width), LOW)],
        [struct((64, columns), LOW)] * 4,
        dense_weights(width, hidden) + dense_sums(width, hidden)
        + [vmem((4, 64, columns), LOW), raw_block(parts)],
        kept + [vmem((SEQ, width), F32)] + dense_work(width, hidden),
        10**10, setup, finish, (), [place], 2,
    )


def hand_out(place_ref, packed_ref, sent):
    for step, ref in enumerate(sent):
        ref[...] = packed_ref[place_ref[0] ^ step]


def middle_kernel(lengths, upper, lower, place, urgent, parts1, parts0, hidden, after):
    tokens, width = upper[0].shape
    columns = 3 * width + 128 + width + 2 * hidden + width + hidden // 8

    def setup(numbers, fixed, sent, work):
        count = len(parts1)
        assemble(numbers[0], fixed[1 : 1 + count], work[15])
        assemble(numbers[0], fixed[1 + count :], work[16])
        set_attention(1, fixed[0], work[15], 0, *work[:2])
        set_dense(0, fixed[0], work[16], 0, *work[2:7])
        clear(work[7:14])

    def body(row, lengths_ref, rowwise, outs, work, own):
        up, low = rowwise[:7], rowwise[7:]
        dx_ref = own[0]
        yield from attention_backward(
            row, lengths_ref, up[0][...].astype(LOW), *up[1:6], work[0], up[6], dx_ref,
            *work[7:9], *own[5:],
        )
        yield from dense_backward(dx_ref, *low, *work[2:6], *outs, *work[9:14], *own[1:5])

    def finish(numbers, work, sent):
        pack_attention(*work[7:9], work[14], 0)
        pack_dense(*work[9:14], work[14], 3 * width + 128)
        hand_out(numbers[0], work[14], sent)

    return run_rows(
        body, lengths, list(upper) + list(lower), [urgent] + list(parts1) + list(parts0),
        [struct((tokens, width), F32), struct((tokens, width), LOW)],
        [struct((64, columns), LOW)] * 4,
        attention_weights(width) + dense_weights(width, hidden)
        + attention_sums(width) + dense_sums(width, hidden)
        + [vmem((4, 64, columns), LOW), raw_block(parts1), raw_block(parts0)],
        [vmem((SEQ, width), F32)] + dense_work(width, hidden) + BACKWARD_SCRATCH(),
        15 * 10**9, setup, finish, after, [place],
    )


def last_kernel(lengths, upper, urgent, after, place):
    tokens, width = upper[0].shape

    def setup(numbers, fixed, sent, work):
        set_attention(0, fixed[0], fixed[0], 0, *work[:2])
        clear(work[2:4])

    def body(row, lengths_ref, rowwise, outs, work, own):
        return attention_backward(
            row, lengths_ref, rowwise[0][...], *rowwise[1:6], work[0], rowwise[6], outs[0],
            *work[2:4], *own,
        )

    def finish(numbers, work, sent):
        pack_attention(*work[2:4], work[4], 0)
        hand_out(numbers[0], work[4], sent)

    return run_rows(
        body, lengths, list(upper), [urgent], [struct((tokens, width), LOW)],
        [struct((64, 3 * width + 128), LOW)] * 4,
        attention_weights(width) + attention_sums(width) + [vmem((4, 64, 3 * width + 128), LOW)],
        BACKWARD_SCRATCH(), 8 * 10**9, setup, finish, after, [place], 2,
    )


def hold(array, after):
    def kernel(*refs):
        pass

    anywhere = pl.BlockSpec(memory_space=pl.ANY)
    return pl.pallas_call(
        kernel,
        in_specs=[anywhere] * (1 + len(after)),
        out_specs=anywhere,
        out_shape=shape_of(array),
        input_output_aliases={0: 0},
    )(array, *after)


def put_in_order(place, parts, cuts, after=()):
    rows, lanes = parts[0].shape
    count = len(parts)
    bounds = [0] + list(cuts) + [lanes]

    def kernel(place_ref, *refs):
        outs, order_ref = refs[count + len(after) : -1], refs[-1]
        for step, ref in enumerate(refs[:count]):
            order_ref[place_ref[0] ^ step] = ref[...].astype(F32)
        for index, ref in enumerate(outs):
            for start in range(bounds[index], bounds[index + 1], 128):
                block = order_ref[:, :, pl.ds(start, 128)].reshape(count * rows, 128)
                ref[:, pl.ds(start - bounds[index], 128)] = block.astype(LOW)

    return pl.pallas_call(
        kernel,
        in_specs=[pl.BlockSpec(memory_space=pltpu.SMEM)]
        + [pl.BlockSpec(memory_space=pltpu.VMEM)] * count
        + [pl.BlockSpec(memory_space=pl.ANY)] * len(after),
        out_shape=[
            struct((count * rows, end - start), LOW) for start, end in zip(bounds, bounds[1:])
        ],
        scratch_shapes=[vmem((count, rows, lanes), F32)],
        compiler_params=pltpu.CompilerParams(vmem_limit_bytes=MEMORY),
    )(place, *parts, *after)


def pack_parameters(
    attn_weight, attn_bias, out_weight, ffn_in, ffn_in_bias, ffn_out, norm_gain, shifts
):
    depth, rows, width = out_weight.shape
    hidden = ffn_in.shape[2]
    early = 4 * width + 2 * hidden + 128
    columns = 4 * width + 2 * hidden
    height = ffn_in_bias.shape[1]

    def kernel(wq_ref, ab_ref, wo_ref, wi_ref, bi_ref, wf_ref, gain_ref, shift_ref, first_ref, rest_ref, small_ref):
        def put(ref, block, at):
            ref[:, pl.ds(at, block.shape[1])] = block.astype(LOW)

        small_ref[...] = jnp.zeros(small_ref.shape, F32)
        for layer in range(depth):
            lanes = pl.ds(rows * layer, rows)
            small_ref[0:2, lanes] = ab_ref[layer].astype(F32)
            small_ref[2:4, lanes] = gain_ref[layer].astype(F32)
            small_ref[4:8, lanes] = shift_ref[layer].astype(F32)
        small_ref[0:depth, pl.ds(2 * rows, height)] = bi_ref[...].astype(F32)
        put(first_ref, wq_ref[0], 0)
        put(first_ref, small_ref[...], 3 * width)
        for layer, ref, at in ((0, first_ref, 3 * width + 128), (1, rest_ref, 3 * width)):
            if layer:
                put(ref, wq_ref[layer], 0)
            put(ref, wo_ref[layer], at)
            put(ref, wi_ref[layer], at + width)
            at += width + hidden
            down = wf_ref[layer].astype(F32)
            for step in range(hidden // width):
                put(ref, down[step * rows : (step + 1) * rows], at)
                at += width

    return pl.pallas_call(
        kernel,
        in_specs=[pl.BlockSpec(memory_space=pltpu.VMEM)] * 8,
        out_shape=[struct((rows, early), LOW), struct((rows, columns), LOW)],
        scratch_shapes=[vmem((rows, 128), F32)],
        compiler_params=pltpu.CompilerParams(vmem_limit_bytes=MEMORY),
    )(attn_weight, attn_bias, out_weight, ffn_in, ffn_in_bias, ffn_out, norm_gain, shifts)


def add_parts(place, parts, after=()):
    lanes = parts[0].shape[1]
    count = len(parts)
    pieces_of, rows = GROUPS[1:]

    def kernel(place_ref, *refs):
        outs, sum_ref = refs[count + len(after) : -1], refs[-1]
        for start in range(0, lanes, 128):
            near = pl.ds(start, 128)
            total = refs[0][:, near].astype(F32)
            for ref in refs[1:count]:
                total = total + ref[:, near].astype(F32)
            sum_ref[:, :, near] = total.reshape(pieces_of, rows, 128)
        for step, ref in enumerate(outs):
            ref[...] = sum_ref[place_ref[0] ^ step].astype(LOW)

    return pl.pallas_call(
        kernel,
        in_specs=[pl.BlockSpec(memory_space=pltpu.SMEM)]
        + [pl.BlockSpec(memory_space=pltpu.VMEM)] * count
        + [pl.BlockSpec(memory_space=pl.ANY)] * len(after),
        out_shape=[struct((rows, lanes), LOW)] * pieces_of,
        scratch_shapes=[vmem((pieces_of, rows, lanes), F32)],
        compiler_params=pltpu.CompilerParams(vmem_limit_bytes=MEMORY),
    )(place, *parts, *after)


def write_gradients(place, tail, middle, head, depth, width, hidden):
    rows = GROUPS[2]
    height = hidden // DEVICES
    cuts = [len(tail), len(middle), len(head)]

    def kernel(place_ref, *refs):
        tail_refs, refs = refs[: cuts[0]], refs[cuts[0] :]
        middle_refs, refs = refs[: cuts[1]], refs[cuts[1] :]
        head_refs, refs = refs[: cuts[2]], refs[cuts[2] :]
        gwq_ref, gab_ref, gwo_ref, gwi_ref, gbi_ref, gwf_ref, gain_ref, shift_ref = refs
        spot = place_ref[0]

        def total(refs, at, columns):
            found = refs[0][:, pl.ds(at, columns)].astype(F32)
            for ref in refs[1:]:
                found = found + ref[:, pl.ds(at, columns)].astype(F32)
            return found

        def own(block, size):
            return pltpu.roll(block, block.shape[1] - spot * size, 1)

        def unfolded(block, count):
            return jnp.concatenate([block[step : step + 1] for step in range(count)], 1)

        for layer, refs in ((0, head_refs), (1, middle_refs)):
            gwq_ref[layer] = total(refs, 0, 3 * width)
            block = total(refs, 3 * width, 128)
            many = width // 128
            for index in range(2):
                line = unfolded(block[index * many : (index + 1) * many], many)
                gab_ref[layer, pl.ds(index, 1)] = own(line, rows)[:, 0:rows]
        for layer, refs, at in ((0, middle_refs, 3 * width + 128), (1, tail_refs, 0)):
            gwo_ref[layer] = total(refs, at, width)
            gwi_ref[layer] = total(refs, at + width, hidden)
            for step in range(hidden // width):
                gwf_ref[layer, pl.ds(step * rows, rows)] = total(
                    refs, at + width + hidden + step * width, width
                )
            at += width + 2 * hidden
            small = own(total(refs, at, width), rows)
            gain_ref[layer] = small[2:4, 0:rows]
            shift_ref[layer] = small[4:8, 0:rows]
            line = unfolded(total(refs, at + width, hidden // 8), 8)
            gbi_ref[pl.ds(layer, 1)] = own(line, height)[:, 0:height]

    outs = [
        struct((depth, rows, 3 * width), F32),
        struct((depth, 2, rows), F32),
        struct((depth, rows, width), F32),
        struct((depth, rows, hidden), F32),
        struct((depth, height), F32),
        struct((depth, height, width), F32),
        struct((depth, 2, rows), F32),
        struct((depth, 4, rows), F32),
    ]
    return pl.pallas_call(
        kernel,
        in_specs=[pl.BlockSpec(memory_space=pltpu.SMEM)]
        + [pl.BlockSpec(memory_space=pltpu.VMEM)] * sum(cuts),
        out_shape=outs,
        compiler_params=pltpu.CompilerParams(vmem_limit_bytes=MEMORY),
    )(place, *tail, *middle, *head)


def swap(part, axis, step):
    size = lax.axis_size(axis)
    return lax.ppermute(part, axis, [(source, source ^ step) for source in range(size)])


def local(
    hidden_in,
    lengths,
    grad_out,
    attn_weight,
    attn_bias,
    out_weight,
    ffn_in,
    ffn_in_bias,
    ffn_out,
    norm_gain,
    shifts,
):
    depth, rows, width = out_weight.shape
    hidden = ffn_in.shape[2]
    first, second = lax.axis_size("dp"), lax.axis_size("fsdp")
    fits = (second, first, rows) == GROUPS
    urgent_size = 3 * width + 128
    if fits:
        early, later = pack_parameters(
            attn_weight, attn_bias, out_weight, ffn_in, ffn_in_bias, ffn_out, norm_gain, shifts
        )
        across = lax.axis_index("dp").astype(jnp.int32).reshape(1)
        place = lax.axis_index("fsdp").astype(jnp.int32).reshape(1)
        rows_of, partners = range(1, first), range(1, second)
        early = [early] + [swap(early, "dp", step) for step in rows_of]
        urgent, raw0 = put_in_order(across, early, [urgent_size])
        later = hold(later, (urgent,))
        later = [later] + [swap(later, "dp", step) for step in rows_of]
        urgent = [urgent] + [swap(urgent, "fsdp", step) for step in partners]
        raw0 = hold(raw0, tuple(urgent))
        raw0 = [raw0] + [swap(raw0, "fsdp", step) for step in partners]
    else:
        urgent, raw0, raw1 = gather_other(
            attn_weight, attn_bias, out_weight, ffn_in, ffn_in_bias, ffn_out, norm_gain, shifts
        )
        urgent, raw0, raw1 = ([part[step] for step in range(4)] for part in (urgent, raw0, raw1))
        place = jnp.zeros((1,), jnp.int32)

    qa0, ka0, va0, ob0, urgent = first_kernel(lengths, hidden_in, place, urgent)
    if fits:
        (raw1,) = put_in_order(across, later, [], (ob0,))
        raw1 = [raw1] + [swap(raw1, "fsdp", step) for step in partners]
    n1, n2, inv, yb, gb, gp, z0 = dense_kernel(
        0, lengths, hidden_in, ob0, place, urgent, raw0, 0, hidden
    )
    qa1, ka1, va1, ob1 = attention_kernel(1, lengths, z0, place, urgent, raw1, 0)
    hidden_out, dr1, dob1, *sent_a = turn_kernel(
        1, lengths, z0, ob1, grad_out, place, urgent, raw1, 3 * width, hidden
    )
    dr0, dob0, *sent_b = middle_kernel(
        lengths,
        (z0, dob1, ob1, qa1, ka1, va1, dr1),
        (n1, n2, inv, yb, gb, gp, ob0),
        place,
        urgent,
        raw1,
        raw0,
        hidden,
        (sent_a[0],),
    )
    if fits:
        got_a = [sent_a[0]] + [swap(sent_a[step], "fsdp", step) for step in partners]
        tail = add_parts(across, got_a, (sent_b[0],))
        tail = [tail[0]] + [swap(tail[step], "dp", step) for step in rows_of]
    grad_in, *sent_c = last_kernel(
        lengths, (hidden_in, dob0, ob0, qa0, ka0, va0, dr0), urgent, (sent_b[0],), place
    )
    if fits:
        got_b = [sent_b[0]] + [swap(sent_b[step], "fsdp", step) for step in partners]
        got_c = [sent_c[0]] + [swap(sent_c[step], "fsdp", step) for step in partners]
        middle = add_parts(across, got_b, (grad_in,) + tuple(tail))
        middle = [middle[0]] + [swap(middle[step], "dp", step) for step in rows_of]
        head = add_parts(across, got_c)
        head = [head[0]] + [swap(head[step], "dp", step) for step in rows_of]
        spot = lax.axis_index(("dp", "fsdp")).astype(jnp.int32).reshape(1)
        grads = write_gradients(spot, tail, middle, head, depth, width, hidden)
    else:
        grads = scatter_other(
            *(jnp.stack(part) for part in (sent_a, sent_b, sent_c)), rows, width, hidden
        )
    return (hidden_out, grad_in, *grads)


def gather_other(
    attn_weight, attn_bias, out_weight, ffn_in, ffn_in_bias, ffn_out, norm_gain, shifts
):
    axes = ("dp", "fsdp")
    gather = lambda part, axis: lax.all_gather(part, axes, axis=axis, tiled=True)
    depth, unused, width = out_weight.shape
    hidden = ffn_in.shape[2]
    outer, inner, rows = GROUPS
    vectors = gather(jnp.concatenate([attn_bias, norm_gain, shifts], 1), 2)
    line = gather(ffn_in_bias, 1)

    def order(natural):
        return (
            natural.reshape(inner, outer, rows, -1).swapaxes(0, 1).reshape(outer, inner * rows, -1)
        )

    def stacked(part):
        part = part.reshape(DEVICES, -1, rows, width)
        return order(part.swapaxes(1, 2).reshape(width, -1))

    small = vectors.reshape(depth, 8, DEVICES, rows).transpose(2, 1, 0, 3).reshape(width, -1)
    line = line.reshape(depth, DEVICES, -1).swapaxes(0, 1)
    line = jnp.pad(line, ((0, 0), (0, 8 - depth), (0, 0))).reshape(width, -1)
    small = jnp.concatenate([small, line], 1)
    small = jnp.pad(small, ((0, 0), (0, 128 - small.shape[1])))
    wq, wo, wi, wf = (gather(part, 1) for part in (attn_weight, out_weight, ffn_in, ffn_out))
    urgent = jnp.concatenate([order(wq[0]), order(small)], 2)
    raw0 = jnp.concatenate([order(wo[0]), order(wi[0]), stacked(wf[0])], 2)
    raw1 = jnp.concatenate([order(wq[1]), order(wo[1]), order(wi[1]), stacked(wf[1])], 2)
    return urgent, raw0, raw1


def scatter_other(sent_a, sent_b, sent_c, own_rows, width, hidden):
    outer, inner, rows = GROUPS
    axes = ("dp", "fsdp")

    def natural(part):
        return part.reshape(outer, inner, rows, -1).swapaxes(0, 1).reshape(width, -1).astype(F32)

    def cut(part, sizes):
        found, at = [], 0
        for size in sizes:
            found.append(part[:, at : at + size])
            at += size
        return found

    dense = [width, hidden, hidden, width, hidden // 8]
    attention = [3 * width, 128]
    wq0, ab0 = cut(natural(sent_c), attention)
    wq1, ab1, wo0, wi0, wf0, small0, bi0 = cut(natural(sent_b), attention + dense)
    wo1, wi1, wf1, small1, bi1 = cut(natural(sent_a), dense)

    def stacked(part):
        part = part.reshape(DEVICES, rows, -1, width).swapaxes(1, 2)
        return part.reshape(hidden, width)

    def spread(parts, axis):
        return lax.psum_scatter(jnp.stack(parts), axes, scatter_dimension=axis, tiled=True)

    return (
        spread([wq0, wq1], 1),
        spread([ab0[:4].reshape(2, width), ab1[:4].reshape(2, width)], 2),
        spread([wo0, wo1], 1),
        spread([wi0, wi1], 1),
        spread([bi0[:8].reshape(-1), bi1[:8].reshape(-1)], 1),
        spread([stacked(wf0), stacked(wf1)], 1),
        spread([small0[2:4], small1[2:4]], 2),
        spread([small0[4:8], small1[4:8]], 2),
    )


def solution(mesh):
    placed = (
        P(("dp", "fsdp"), None),
        P(("dp", "fsdp"), None),
        P(("dp", "fsdp"), None),
        P(None, ("dp", "fsdp"), None),
        P(None, None, ("dp", "fsdp")),
        P(None, ("dp", "fsdp"), None),
        P(None, ("dp", "fsdp"), None),
        P(None, ("dp", "fsdp")),
        P(None, ("dp", "fsdp"), None),
        P(None, None, ("dp", "fsdp")),
        P(None, None, ("dp", "fsdp")),
    )
    return jax.shard_map(
        local,
        mesh=mesh,
        in_specs=placed,
        out_specs=(
            P(("dp", "fsdp"), None),
            P(("dp", "fsdp"), None),
            P(None, ("dp", "fsdp"), None),
            P(None, None, ("dp", "fsdp")),
            P(None, ("dp", "fsdp"), None),
            P(None, ("dp", "fsdp"), None),
            P(None, ("dp", "fsdp")),
            P(None, ("dp", "fsdp"), None),
            P(None, None, ("dp", "fsdp")),
            P(None, None, ("dp", "fsdp")),
        ),
        check_vma=False,
    )
```

```python
from functools import partial

import jax
import jax.numpy as jnp
from jax import lax
from jax.experimental import pallas as pl
from jax.experimental.pallas import tpu as pltpu
from jax.sharding import PartitionSpec as P

HEADS = 4
HD = 64
SEQ = 512
PAIR = 2 * HD
FAR = -(2.0**100)
FLOOR = -1e20
EPSILON = 1e-12
PIECE = 256
SMALL = 128
GROUPS = (4, 8, 8)
DEVICES = 32
LOW = jnp.bfloat16
F32 = jnp.float32
MEMORY = 2**26


def dot_nn(left, right):
    return lax.dot_general(left, right, (((1,), (0,)), ((), ())), preferred_element_type=F32)


def dot_nt(left, right):
    return lax.dot_general(left, right, (((1,), (1,)), ((), ())), preferred_element_type=F32)


def dot_tn(left, right):
    return lax.dot_general(left, right, (((0,), (0,)), ((), ())), preferred_element_type=F32)


def pieces(total, size=PIECE):
    return [pl.ds(start, size) for start in range(0, total, size)]


def three_parts(values):
    first = values.astype(LOW).astype(F32)
    rest = values - first
    second = rest.astype(LOW).astype(F32)
    return first, second, rest - second


CURVE = (7.97869556e-01, 3.63928094e-02, -8.82195179e-05, -3.66000319e-05, 1.41853144e-06)
BELL = -0.5 / 0.6931471805599453


def gelu_parts(u):
    square = u * u
    curve = CURVE[-1]
    for factor in CURVE[-2::-1]:
        curve = curve * square + factor
    cumulative = 0.5 + 0.5 * jnp.tanh(u * curve)
    slope = cumulative + (u * 0.3989422804014327) * jnp.exp2(square * BELL)
    return u * cumulative, slope


def inverse_of(values):
    guess = pl.reciprocal(values, approx=True)
    return guess * (2.0 - values * guess)


def lane_facts():
    lane = lax.broadcasted_iota(jnp.int32, (1, PAIR), 1)
    return lane < HD, lane & (HD - 1)


def segments(lengths_ref, row, start, rows):
    places = lax.broadcasted_iota(jnp.int32, (rows, 1), 0) + start
    bound = jnp.int32(0)
    segment = jnp.zeros((rows, 1), jnp.int32)
    last = lengths_ref.shape[1] - 1
    for entry in range(last):
        bound = bound + lengths_ref[row, entry]
        segment = segment + (places >= bound).astype(jnp.int32)
    return segment, (segment == last).astype(F32), last


def attention_forward(row, lengths_ref, x, wq_ref, bias_ref, qa_ref, ka_ref, va_ref, ob_ref, s_ref, p_ref, m_ref, pad_ref, q_ref, aug_ref):
    width = HEADS * HD
    for block in range(3):
        at = block * width
        value = dot_nn(x, wq_ref[:, at : at + width]) + bias_ref[:, at : at + width]
        for pair in range(HEADS // 2):
            q_ref[block, pair] = value[:, pair * PAIR : (pair + 1) * PAIR]
        yield
    for start in range(0, SEQ, PIECE):
        place = pl.ds(start, PIECE)
        low_half, slot = lane_facts()
        segment, pad, last = segments(lengths_ref, row, start, PIECE)
        pad_ref[place] = jnp.broadcast_to(pad, (PIECE, PAIR))
        aug_q = jnp.where(slot == segment, 1.0, 0.0)
        aug_ref[place] = aug_q
        seen = (slot == segment) & (slot != last)
        aug_k = jnp.where(seen, 0.0, jnp.where(slot <= last, FAR, jnp.where(slot <= last + 3, 1.0, 0.0)))
        for pair in range(HEADS // 2):
            q = q_ref[0, pair, place] * HD**-0.5
            k = q_ref[1, pair, place]
            v = q_ref[2, pair, place]
            q_ref[0, pair, place] = q
            qa_ref[2 * pair, place] = jnp.where(low_half, q, aug_q).astype(LOW)
            qa_ref[2 * pair + 1, place] = jnp.where(low_half, aug_q, q).astype(LOW)
            ka_ref[2 * pair, place] = jnp.where(low_half, k, aug_k).astype(LOW)
            ka_ref[2 * pair + 1, place] = jnp.where(low_half, aug_k, k).astype(LOW)
            va_ref[2 * pair, place] = jnp.where(low_half, v, 1.0).astype(LOW)
            va_ref[2 * pair + 1, place] = jnp.where(low_half, 1.0, v).astype(LOW)
        yield

    def scores(head):
        s_ref[head % 2] = dot_nt(qa_ref[head], ka_ref[head])

    def softmax(head):
        for place in pieces(SEQ):
            highest = jnp.maximum(jnp.max(s_ref[head % 2, place], -1, keepdims=True), FLOOR)
            m_ref[head % 2, place] = jnp.broadcast_to(highest, (PIECE, PAIR))
            p_ref[head % 2, place] = jnp.exp(s_ref[head % 2, place] - highest).astype(LOW)

    scores(0)
    yield
    for head in range(HEADS):
        if head + 1 < HEADS:
            scores(head + 1)
            yield
        softmax(head)
        yield
        q_ref[1, head % 2] = dot_nn(p_ref[head % 2], va_ref[head])
        if head % 2:
            pair = head // 2
            for start in range(0, SEQ, PIECE):
                place = pl.ds(start, PIECE)
                low_half, slot = lane_facts()
                even = q_ref[1, 0, place]
                odd = q_ref[1, 1, place]
                pad = pad_ref[place]
                last = lengths_ref.shape[1] - 1
                total = jnp.where(low_half, odd, even) + pad
                top = jnp.where(low_half, m_ref[1, place], m_ref[0, place])
                spread = jnp.where(pad > 0, 0.0, top + jnp.log(total))
                first, second, third = three_parts(spread)
                aug = jnp.where(
                    slot == last + 1,
                    -first,
                    jnp.where(slot == last + 2, -second, jnp.where(slot == last + 3, -third, aug_ref[place])),
                )
                q = q_ref[0, pair, place]
                qa_ref[2 * pair, place] = jnp.where(low_half, q, aug).astype(LOW)
                qa_ref[2 * pair + 1, place] = jnp.where(low_half, aug, q).astype(LOW)
                v = q_ref[2, pair, place].astype(LOW).astype(F32)
                share = inverse_of(pltpu.roll(total, HD, 1))
                out = jnp.where(low_half, even, odd) * share + pad * v
                ob_ref[place, pl.ds(pair * PAIR, PAIR)] = out.astype(LOW)
            yield


def normal(values):
    centred = values - jnp.mean(values, -1, keepdims=True)
    inverse = lax.rsqrt(jnp.mean(centred * centred, -1, keepdims=True) + EPSILON)
    return centred * inverse, inverse


def normal_back(cotangent, unit, inverse, gains):
    scaled = cotangent * gains
    return inverse * (
        scaled
        - jnp.mean(scaled, -1, keepdims=True)
        - unit * jnp.mean(scaled * unit, -1, keepdims=True)
    )


def dense_forward(x_ref, ob_ref, wo_ref, wi_ref, wf_ref, small_ref, bi_ref, n1_ref, n2_ref, inv_ref, yb_ref, gb_ref, gp_ref, z_ref, work_ref, u_ref):
    small = lambda index: small_ref[pl.ds(index, 1)]
    work_ref[...] = dot_nn(ob_ref[...], wo_ref[...])
    yield
    for place in pieces(SEQ):
        unit, inverse = normal(x_ref[place].astype(F32) + work_ref[place] + small(4))
        n1_ref[place] = unit
        inv_ref[place, pl.ds(0, HD)] = jnp.broadcast_to(inverse, (PIECE, HD))
        y = unit * small(2) + small(5)
        yb_ref[place] = y.astype(LOW)
        work_ref[place] = y + small(6)
        yield
    columns = 256
    count = wi_ref.shape[1] // columns

    def into(step):
        u_ref[step % 2] = dot_nn(yb_ref[...], wi_ref[:, pl.ds(step * columns, columns)])

    into(0)
    yield
    for step in range(count):
        if step + 1 < count:
            into(step + 1)
            yield
        lanes = pl.ds(step * columns, columns)
        for place in pieces(SEQ, SMALL):
            g, slope = gelu_parts(u_ref[step % 2, place] + bi_ref[:, lanes])
            gb_ref[place, lanes] = g.astype(LOW)
            gp_ref[place, lanes] = slope.astype(LOW)
            yield
    work_ref[...] += dot_nn(gb_ref[...], wf_ref[...])
    yield
    for place in pieces(SEQ):
        unit, inverse = normal(work_ref[place])
        n2_ref[place] = unit
        inv_ref[place, pl.ds(HD, HD)] = jnp.broadcast_to(inverse, (PIECE, HD))
        z_ref[place] = (unit * small(3) + small(7)).astype(z_ref.dtype)
        yield


def fold(values):
    return jnp.sum(values.reshape(-1, 8, values.shape[-1]), 0)


def dense_backward(dz_ref, n1_ref, n2_ref, inv_ref, yb_ref, gb_ref, gp_ref, ob_ref, wo_ref, wi_ref, wf_ref, small_ref, dr_ref, dob_ref, gwo_ref, gwi_ref, gwf_ref, gsmall_ref, gbi_ref, low_ref, u_ref, du_ref, turned_ref):
    small = lambda index: small_ref[pl.ds(index, 1)]
    for place in pieces(SEQ):
        dz = dz_ref[place].astype(F32)
        unit = n2_ref[place]
        gsmall_ref[3] += fold(dz * unit)
        gsmall_ref[7] += fold(dz)
        dr = normal_back(dz, unit, inv_ref[place, pl.ds(HD, 1)], small(3))
        dr_ref[place] = dr
        df = dr.astype(LOW)
        low_ref[place] = df
        gsmall_ref[6] += fold(df.astype(F32))
        yield
    columns = 256
    count = wi_ref.shape[1] // columns

    def back(step):
        u_ref[step % 2] = dot_nt(low_ref[...], wf_ref[pl.ds(step * columns, columns)])

    back(0)
    turned_ref[0] = low_ref[...].T
    turned_ref[1] = yb_ref[...].T
    yield
    for step in range(count):
        if step + 1 < count:
            back(step + 1)
            yield
        lanes = pl.ds(step * columns, columns)
        gwf_ref[:, lanes] += dot_nn(turned_ref[0], gb_ref[:, lanes])
        yield
        for place in pieces(SEQ, SMALL):
            du = (u_ref[step % 2, place] * gp_ref[place, lanes].astype(F32)).astype(LOW)
            du_ref[place, lanes] = du
            gbi_ref[:, lanes] += fold(du.astype(F32))
        yield
        gwi_ref[:, lanes] += dot_nn(turned_ref[1], du_ref[:, lanes])
        yield
    u_ref[0] = dot_nt(du_ref[...], wi_ref[...])
    yield
    for place in pieces(SEQ):
        dy = dr_ref[place] + u_ref[0, place]
        unit = n1_ref[place]
        gsmall_ref[2] += fold(dy * unit)
        gsmall_ref[5] += fold(dy)
        dr = normal_back(dy, unit, inv_ref[place, pl.ds(0, 1)], small(2))
        dr_ref[place] = dr
        da = dr.astype(LOW)
        low_ref[place] = da
        gsmall_ref[4] += fold(da.astype(F32))
        yield
    gwo_ref[...] += dot_tn(ob_ref[...], low_ref[...])
    dob_ref[...] = dot_nt(low_ref[...], wo_ref[...]).astype(LOW)
    yield


def attention_backward(row, lengths_ref, x, dob_ref, ob_ref, qa_ref, ka_ref, va_ref, wq_ref, dr_ref, dx_ref, gwq_ref, gbias_ref, da_ref, p_ref, ds_ref, s_ref, dqkv_ref, dq_ref, pad_ref, kt_ref, dqt_ref):
    width = HEADS * HD
    low_half, slot = lane_facts()
    for start in range(0, SEQ, PIECE):
        place = pl.ds(start, PIECE)
        segment, pad, last = segments(lengths_ref, row, start, PIECE)
        pad_ref[place] = jnp.broadcast_to(pad, (PIECE, PAIR))
        for pair in range(HEADS // 2):
            lanes = pl.ds(pair * PAIR, PAIR)
            dob = dob_ref[place, lanes].astype(F32)
            product = dob * ob_ref[place, lanes].astype(F32)
            even = jnp.sum(jnp.where(low_half, product, 0.0), -1, keepdims=True)
            odd = jnp.sum(jnp.where(low_half, 0.0, product), -1, keepdims=True)
            first, second, third = three_parts(jnp.where(low_half, odd, even))
            aug = jnp.where(
                slot == 0, -first, jnp.where(slot == 1, -second, jnp.where(slot == 2, -third, 0.0))
            )
            da_ref[2 * pair, place] = jnp.where(low_half, dob, aug).astype(LOW)
            da_ref[2 * pair + 1, place] = jnp.where(low_half, aug, dob).astype(LOW)
        yield
    for pair in range(HEADS // 2):
        low_half, unused = lane_facts()
        keys = jnp.where(low_half, ka_ref[2 * pair].astype(F32), ka_ref[2 * pair + 1].astype(F32))
        kt_ref[pl.ds(pair * PAIR, PAIR)] = keys.T.astype(LOW)
    low_half, slot = lane_facts()

    def scores(head):
        s_ref[0, head % 2] = dot_nt(ka_ref[head], qa_ref[head])
        s_ref[1, head % 2] = dot_nt(va_ref[head], da_ref[head])

    def weigh(head):
        for place in pieces(SEQ, SMALL):
            p = jnp.exp(s_ref[0, head % 2, place])
            p_ref[head % 2, place] = p.astype(LOW)
            ds_ref[head % 2, place] = (p * s_ref[1, head % 2, place]).astype(LOW)

    scores(0)
    yield
    for head in range(HEADS):
        if head + 1 < HEADS:
            scores(head + 1)
            yield
        weigh(head)
        yield
        side = head % 2
        dq_ref[1, side] = dot_nn(ds_ref[head % 2], qa_ref[head])
        dq_ref[2, side] = dot_nn(p_ref[head % 2], da_ref[head])
        dqt_ref[pl.ds(side * HD, HD)] = dot_nn(kt_ref[pl.ds(head * HD, HD)], ds_ref[head % 2])
        yield
        if side:
            pair = head // 2
            dq_ref[0, 0] = dqt_ref[...].T
            for start in range(0, SEQ, PIECE):
                place = pl.ds(start, PIECE)
                dq = dq_ref[0, 0, place] * HD**-0.5
                dk = jnp.where(low_half, dq_ref[1, 0, place], dq_ref[1, 1, place])
                dv = jnp.where(low_half, dq_ref[2, 0, place], dq_ref[2, 1, place])
                dv = dv + pad_ref[place] * dob_ref[place, pl.ds(pair * PAIR, PAIR)].astype(F32)
                for block, value in enumerate((dq, dk, dv)):
                    lanes = pl.ds(block * width + pair * PAIR, PAIR)
                    value = value.astype(LOW)
                    dqkv_ref[place, lanes] = value
                    if block != 1:
                        into = pl.ds(pair * PAIR, PAIR)
                        gbias_ref[block // 2, :, into] += fold(value.astype(F32))
    yield
    gwq_ref[...] += dot_tn(x, dqkv_ref[...])
    yield
    dx_ref[...] = (dr_ref[...] + dot_nt(dqkv_ref[...], wq_ref[...])).astype(dx_ref.dtype)
    yield


def unpack_matrix(raw_ref, at, into_ref):
    width = into_ref.shape[0]
    for start in range(0, into_ref.shape[1], width):
        block = raw_ref[:, :, pl.ds(at + start, width)].astype(F32)
        block = block.reshape(GROUPS + (width,)).swapaxes(0, 1).reshape(width, width)
        into_ref[:, pl.ds(start, width)] = block.astype(LOW)


def unpack_stacked(raw_ref, at, into_ref):
    width = into_ref.shape[1]
    count = into_ref.shape[0] // width
    blocks = [
        raw_ref[:, :, pl.ds(at + step * width, width)].astype(F32).reshape(GROUPS + (width,))
        for step in range(count)
    ]
    outer, inner, rows = GROUPS
    for place in range(inner):
        part = jnp.stack([jnp.stack([block[f, place] for block in blocks]) for f in range(outer)])
        size = outer * count * rows
        into_ref[pl.ds(place * size, size)] = part.reshape(size, width).astype(LOW)


def counter(shape, axis):
    return lax.broadcasted_iota(jnp.int32, shape, axis)


def split_by(values, size):
    return lax.shift_right_logical(values, size.bit_length() - 1), values & (size - 1)


def sources(rows):
    outer, inner, height = GROUPS
    group, within = split_by(counter((rows, 1), 0), height)
    far, near = split_by(group, inner)
    return near * outer + far, within


def unpack_vectors(raw_ref, at, layer):
    outer, inner, rows = GROUPS
    total = outer * inner * rows
    raw = raw_ref[:, :, pl.ds(at, 128)].reshape(total, 128)
    owner, place = split_by(counter((1, total), 1), rows)
    pick = jnp.where(counter((128, 1), 0) == rows * layer + place, 1.0, 0.0).astype(LOW)
    device, unused = sources(total)
    spread = jnp.where(owner == device, dot_nn(raw, pick), 0.0)
    return jnp.sum(spread.reshape(outer * inner, rows, total), 0)


def unpack_hidden(raw_ref, at, layer, hidden):
    outer, inner, rows = GROUPS
    total = outer * inner * rows
    raw = raw_ref[:, :, pl.ds(at, 128)].reshape(total, 128)
    owner, place = split_by(counter((1, hidden), 1), hidden // (outer * inner))
    pick = jnp.where(counter((128, 1), 0) == 2 * rows + place, 1.0, 0.0).astype(LOW)
    device, within = sources(total)
    device = jnp.where(within == layer, device, -1)
    spread = jnp.where(owner == device, dot_nn(raw, pick), 0.0)
    return jnp.sum(spread, 0, keepdims=True)


def pack_matrix(sum_ref, sent_ref, at):
    width = sum_ref.shape[0]
    outer, inner, rows = GROUPS
    for start in range(0, sum_ref.shape[1], width):
        block = sum_ref[:, pl.ds(start, width)].reshape(inner, outer, rows, width)
        block = block.swapaxes(0, 1).reshape(outer, inner * rows, width)
        sent_ref[:, :, pl.ds(at + start, width)] = block.astype(LOW)


def pack_stacked(sum_ref, sent_ref, at):
    width = sum_ref.shape[0]
    outer, inner, rows = GROUPS
    count = sum_ref.shape[1] // width
    near = inner // count
    for step in range(count):
        block = sum_ref[:, pl.ds(step * width, width)].T
        block = block.reshape(near, outer, count, rows, width)
        for part in range(count):
            piece = jnp.stack([block[:, f, part] for f in range(outer)])
            piece = piece.reshape(outer, near * rows, width)
            sent_ref[:, pl.ds(step * near * rows, near * rows), pl.ds(at + part * width, width)] = (
                piece.astype(LOW)
            )


def pack_shared(block, sent_ref, at):
    outer, inner, rows = GROUPS
    columns = block.shape[1]
    block = jnp.broadcast_to(block[None], (outer * inner, rows, columns))
    sent_ref[:, :, pl.ds(at, columns)] = block.reshape(outer, inner * rows, columns).astype(LOW)


def folded(line, lanes):
    return [line[:, at : at + lanes] for at in range(0, line.shape[1], lanes)]


def pack_attention(gwq_ref, gbias_ref, sent_ref, at):
    pack_matrix(gwq_ref, sent_ref, at)
    width = gwq_ref.shape[0]
    parts = []
    for index in range(2):
        parts += folded(jnp.sum(gbias_ref[index], 0, keepdims=True), 128)
    block = jnp.concatenate(parts + [jnp.zeros((8 - len(parts), 128), F32)], 0)
    pack_shared(block, sent_ref, at + 3 * width)


def pack_dense(gwo_ref, gwi_ref, gwf_ref, gsmall_ref, gbi_ref, sent_ref, at):
    width, hidden = gwi_ref.shape
    pack_matrix(gwo_ref, sent_ref, at)
    pack_matrix(gwi_ref, sent_ref, at + width)
    pack_stacked(gwf_ref, sent_ref, at + width + hidden)
    at = at + width + 2 * hidden
    pack_shared(jnp.sum(gsmall_ref[...], 1), sent_ref, at)
    line = jnp.sum(gbi_ref[...], 0, keepdims=True)
    pack_shared(jnp.concatenate(folded(line, hidden // 8), 0), sent_ref, at + width)


def shape_of(array):
    return jax.ShapeDtypeStruct(array.shape, array.dtype)


def by_row(shape, group):
    if len(shape) == 2:
        return pl.BlockSpec((group * SEQ, shape[1]), lambda step: (step, 0))
    return pl.BlockSpec((group,) + tuple(shape[1:]), lambda step: (step,) + (0,) * (len(shape) - 1))


def one_row(ref, member):
    if len(ref.shape) == 2:
        return ref.at[pl.ds(member * SEQ, SEQ)]
    return ref.at[member]


def alternate(runs):
    running = []
    waiting = list(runs)
    while running or waiting:
        if waiting:
            running.append(waiting.pop(0))
        for run in list(running):
            try:
                next(run)
            except StopIteration:
                running.remove(run)


def whole(shape):
    return pl.BlockSpec(tuple(shape), lambda row: (0,) * len(shape))


def run_rows(
    body, lengths, rowwise, fixed, row_outs, sent, shared, private, cost, setup, finish, after=(),
    scalars=(), group=1
):
    count = lengths.shape[0]
    group = group if count % group == 0 else 1
    cuts = [len(scalars), len(rowwise), len(fixed), len(after), len(row_outs), len(sent)]
    cuts += [len(shared)] + [len(private)] * group

    def kernel(lengths_ref, *refs):
        step = pl.program_id(0)
        groups = []
        at = 0
        for cut in cuts:
            groups.append(refs[at : at + cut])
            at += cut
        numbers, rows_in, fixed_in, unused, rows_out, sent_out, work = groups[:7]

        @pl.when(step == 0)
        def _():
            setup(numbers, fixed_in, sent_out, work)

        alternate(
            body(
                step * group + member,
                lengths_ref,
                [one_row(ref, member) for ref in rows_in],
                [one_row(ref, member) for ref in rows_out],
                work,
                groups[7 + member],
            )
            for member in range(group)
        )

        if finish:

            @pl.when(step == count // group - 1)
            def _():
                finish(numbers, work, sent_out)

    return pl.pallas_call(
        kernel,
        grid=(count // group,),
        in_specs=[pl.BlockSpec(memory_space=pltpu.SMEM)] * (1 + len(scalars))
        + [by_row(array.shape, group) for array in rowwise]
        + [whole(array.shape) for array in fixed]
        + [pl.BlockSpec(memory_space=pl.ANY) for array in after],
        out_specs=[by_row(part.shape, group) for part in row_outs]
        + [whole(part.shape) for part in sent],
        out_shape=list(row_outs) + list(sent),
        scratch_shapes=list(shared) + list(private) * group,
        compiler_params=pltpu.CompilerParams(
            dimension_semantics=("arbitrary",), vmem_limit_bytes=MEMORY
        ),
        cost_estimate=pl.CostEstimate(flops=cost, bytes_accessed=8 * 2**20, transcendentals=0),
    )(lengths, *scalars, *rowwise, *fixed, *after)


def struct(shape, dtype):
    return jax.ShapeDtypeStruct(tuple(shape), dtype)


FORWARD_SCRATCH = lambda: [
    pltpu.VMEM((2, SEQ, SEQ), F32),
    pltpu.VMEM((2, SEQ, SEQ), LOW),
    pltpu.VMEM((2, SEQ, PAIR), F32),
    pltpu.VMEM((SEQ, PAIR), F32),
    pltpu.VMEM((3, HEADS // 2, SEQ, PAIR), F32),
    pltpu.VMEM((SEQ, PAIR), F32),
]
BACKWARD_SCRATCH = lambda: [
    pltpu.VMEM((HEADS, SEQ, PAIR), LOW),
    pltpu.VMEM((2, SEQ, SEQ), LOW),
    pltpu.VMEM((2, SEQ, SEQ), LOW),
    pltpu.VMEM((2, 2, SEQ, SEQ), F32),
    pltpu.VMEM((SEQ, 3 * HEADS * HD), LOW),
    pltpu.VMEM((3, 2, SEQ, PAIR), F32),
    pltpu.VMEM((SEQ, PAIR), F32),
    pltpu.VMEM((HEADS * HD, SEQ), LOW),
    pltpu.VMEM((PAIR, SEQ), F32),
]


def attention_outs(rows, tokens, width):
    heads = (rows, HEADS, SEQ, PAIR)
    return [struct(heads, LOW)] * 3 + [struct((tokens, width), LOW)]


def dense_outs(tokens, width, hidden):
    return [
        struct((tokens, width), F32),
        struct((tokens, width), F32),
        struct((tokens, PAIR), F32),
        struct((tokens, width), LOW),
        struct((tokens, hidden), LOW),
        struct((tokens, hidden), LOW),
    ]


def vmem(shape, dtype):
    return pltpu.VMEM(tuple(shape), dtype)


def attention_weights(width):
    return [vmem((width, 3 * width), LOW), vmem((1, 3 * width), F32)]


def dense_weights(width, hidden):
    return [
        vmem((width, width), LOW),
        vmem((width, hidden), LOW),
        vmem((hidden, width), LOW),
        vmem((8, width), F32),
        vmem((1, hidden), F32),
    ]


def dense_sums(width, hidden):
    return [
        vmem((width, width), F32),
        vmem((width, hidden), F32),
        vmem((width, hidden), F32),
        vmem((8, 8, width), F32),
        vmem((8, hidden), F32),
    ]


def attention_sums(width):
    return [vmem((width, 3 * width), F32), vmem((2, 8, width), F32)]


def dense_work(width, hidden):
    return [
        vmem((SEQ, width), LOW),
        vmem((2, SEQ, width), F32),
        vmem((SEQ, hidden), LOW),
        vmem((2, width, SEQ), LOW),
    ]


def set_attention(layer, urgent_ref, raw_ref, at, wq_ref, bias_ref):
    width = wq_ref.shape[0]
    unpack_matrix(raw_ref, at, wq_ref)
    vectors = unpack_vectors(urgent_ref, 3 * width, layer)
    bias_ref[:, :width] = vectors[0:1]
    bias_ref[:, width : 2 * width] = jnp.zeros((1, width), F32)
    bias_ref[:, 2 * width :] = vectors[1:2]


def set_dense(layer, urgent_ref, raw_ref, at, wo_ref, wi_ref, wf_ref, small_ref, bi_ref):
    width, hidden = wi_ref.shape
    unpack_matrix(raw_ref, at, wo_ref)
    unpack_matrix(raw_ref, at + width, wi_ref)
    unpack_stacked(raw_ref, at + width + hidden, wf_ref)
    small_ref[...] = unpack_vectors(urgent_ref, 3 * width, layer)
    bi_ref[...] = unpack_hidden(urgent_ref, 3 * width, layer, hidden)


def clear(refs):
    for ref in refs:
        ref[...] = jnp.zeros(ref.shape, ref.dtype)


def assemble(place_ref, part_refs, into_ref):
    for step, ref in enumerate(part_refs):
        into_ref[place_ref[0] ^ step] = ref[...]


def raw_block(parts):
    return vmem((len(parts),) + parts[0].shape, LOW)


def first_kernel(lengths, x, place, parts):
    rows, (tokens, width) = lengths.shape[0], x.shape

    def setup(numbers, fixed, sent, work):
        assemble(numbers[0], fixed, sent[0])
        set_attention(0, sent[0], sent[0], 0, *work)

    def body(row, lengths_ref, rowwise, outs, work, own):
        return attention_forward(row, lengths_ref, rowwise[0][...], *work, *outs, *own)

    return run_rows(
        body, lengths, [x], list(parts), attention_outs(rows, tokens, width),
        [struct((len(parts),) + parts[0].shape, LOW)],
        attention_weights(width), FORWARD_SCRATCH(), 4 * 10**9, setup, None, (), [place],
    )


def attention_kernel(layer, lengths, x, place, urgent, parts, at):
    rows, (tokens, width) = lengths.shape[0], x.shape

    def setup(numbers, fixed, sent, work):
        assemble(numbers[0], fixed[1:], work[2])
        set_attention(layer, fixed[0], work[2], at, *work[:2])

    def body(row, lengths_ref, rowwise, outs, work, own):
        return attention_forward(
            row, lengths_ref, rowwise[0][...].astype(LOW), *work[:2], *outs, *own
        )

    return run_rows(
        body, lengths, [x], [urgent] + list(parts), attention_outs(rows, tokens, width), [],
        attention_weights(width) + [raw_block(parts)], FORWARD_SCRATCH(),
        4 * 10**9, setup, None, (), [place],
    )


def dense_kernel(layer, lengths, x, ob, place, urgent, parts, at, hidden):
    tokens, width = x.shape

    def setup(numbers, fixed, sent, work):
        assemble(numbers[0], fixed[1:], work[5])
        set_dense(layer, fixed[0], work[5], at, *work[:5])

    def body(row, lengths_ref, rowwise, outs, work, own):
        return dense_forward(*rowwise, *work[:5], *outs, *own)

    return run_rows(
        body, lengths, [x, ob], [urgent] + list(parts),
        dense_outs(tokens, width, hidden) + [struct((tokens, width), F32)], [],
        dense_weights(width, hidden) + [raw_block(parts)],
        [vmem((SEQ, width), F32), vmem((2, SEQ, width), F32)],
        5 * 10**9, setup, None, (), [place],
    )


def turn_kernel(layer, lengths, x, ob, cotangent, place, urgent, parts, at, hidden):
    tokens, width = x.shape
    columns = width + 2 * hidden + width + hidden // 8

    def setup(numbers, fixed, sent, work):
        assemble(numbers[0], fixed[1:], work[11])
        set_dense(layer, fixed[0], work[11], at, *work[:5])
        clear(work[5:10])

    def body(row, lengths_ref, rowwise, outs, work, own):
        x_ref, ob_ref, dz_ref = rowwise
        z_ref, dr_ref, dob_ref = outs
        weights, sums = work[:5], work[5:10]
        kept, work_ref, back = own[:6], own[6], own[7:]
        yield from dense_forward(x_ref, ob_ref, *weights, *kept, z_ref, work_ref, back[1])
        yield from dense_backward(dz_ref, *kept, ob_ref, *weights[:4], dr_ref, dob_ref, *sums, *back)

    def finish(numbers, work, sent):
        pack_dense(*work[5:10], work[10], 0)
        hand_out(numbers[0], work[10], sent)

    kept = [vmem((SEQ,) + part.shape[1:], part.dtype) for part in dense_outs(tokens, width, hidden)]
    return run_rows(
        body, lengths, [x, ob, cotangent], [urgent] + list(parts),
        [struct((tokens, width), LOW), struct((tokens, width), F32), struct((tokens, width), LOW)],
        [struct((64, columns), LOW)] * 4,
        dense_weights(width, hidden) + dense_sums(width, hidden)
        + [vmem((4, 64, columns), LOW), raw_block(parts)],
        kept + [vmem((SEQ, width), F32)] + dense_work(width, hidden),
        10**10, setup, finish, (), [place], 2,
    )


def hand_out(place_ref, packed_ref, sent):
    for step, ref in enumerate(sent):
        ref[...] = packed_ref[place_ref[0] ^ step]


def middle_kernel(lengths, upper, lower, place, urgent, parts, hidden, after):
    tokens, width = upper[0].shape
    columns = 3 * width + 128 + width + 2 * hidden + width + hidden // 8

    def setup(numbers, fixed, sent, work):
        assemble(numbers[0], fixed[1:], work[15])
        set_attention(1, fixed[0], work[15], 0, *work[:2])
        set_dense(0, fixed[0], work[15], 3 * width, *work[2:7])
        clear(work[7:14])

    def body(row, lengths_ref, rowwise, outs, work, own):
        up, low = rowwise[:7], rowwise[7:]
        dx_ref = own[0]
        yield from attention_backward(
            row, lengths_ref, up[0][...].astype(LOW), *up[1:6], work[0], up[6], dx_ref,
            *work[7:9], *own[5:],
        )
        yield from dense_backward(dx_ref, *low, *work[2:6], *outs, *work[9:14], *own[1:5])

    def finish(numbers, work, sent):
        pack_attention(*work[7:9], work[14], 0)
        pack_dense(*work[9:14], work[14], 3 * width + 128)
        hand_out(numbers[0], work[14], sent)

    return run_rows(
        body, lengths, list(upper) + list(lower), [urgent] + list(parts),
        [struct((tokens, width), F32), struct((tokens, width), LOW)],
        [struct((64, columns), LOW)] * 4,
        attention_weights(width) + dense_weights(width, hidden)
        + attention_sums(width) + dense_sums(width, hidden)
        + [vmem((4, 64, columns), LOW), raw_block(parts)],
        [vmem((SEQ, width), F32)] + dense_work(width, hidden) + BACKWARD_SCRATCH(),
        15 * 10**9, setup, finish, after, [place],
    )


def last_kernel(lengths, upper, urgent, after, place):
    tokens, width = upper[0].shape

    def setup(numbers, fixed, sent, work):
        set_attention(0, fixed[0], fixed[0], 0, *work[:2])
        clear(work[2:4])

    def body(row, lengths_ref, rowwise, outs, work, own):
        return attention_backward(
            row, lengths_ref, rowwise[0][...], *rowwise[1:6], work[0], rowwise[6], outs[0],
            *work[2:4], *own,
        )

    def finish(numbers, work, sent):
        pack_attention(*work[2:4], work[4], 0)
        hand_out(numbers[0], work[4], sent)

    return run_rows(
        body, lengths, list(upper), [urgent], [struct((tokens, width), LOW)],
        [struct((64, 3 * width + 128), LOW)] * 4,
        attention_weights(width) + attention_sums(width) + [vmem((4, 64, 3 * width + 128), LOW)],
        BACKWARD_SCRATCH(), 8 * 10**9, setup, finish, after, [place], 2,
    )


def hold(array, after):
    def kernel(*refs):
        pass

    anywhere = pl.BlockSpec(memory_space=pl.ANY)
    return pl.pallas_call(
        kernel,
        in_specs=[anywhere] * (1 + len(after)),
        out_specs=anywhere,
        out_shape=shape_of(array),
        input_output_aliases={0: 0},
    )(array, *after)


def pack_parameters(
    attn_weight, attn_bias, out_weight, ffn_in, ffn_in_bias, ffn_out, norm_gain, shifts
):
    depth, rows, width = out_weight.shape
    copies = GROUPS[1]
    hidden = ffn_in.shape[2]
    dense = width + 2 * hidden
    height = ffn_in_bias.shape[1]

    def kernel(wq_ref, ab_ref, wo_ref, wi_ref, bi_ref, wf_ref, gain_ref, shift_ref, first_ref, rest_ref, small_ref):
        def put(ref, block, at):
            block = jnp.broadcast_to(block.astype(F32)[None], (copies,) + block.shape)
            block = block.reshape(copies * block.shape[1], block.shape[2])
            ref[:, pl.ds(at, block.shape[1])] = block.astype(LOW)

        small_ref[...] = jnp.zeros(small_ref.shape, F32)
        for layer in range(depth):
            lanes = pl.ds(rows * layer, rows)
            small_ref[0:2, lanes] = ab_ref[layer].astype(F32)
            small_ref[2:4, lanes] = gain_ref[layer].astype(F32)
            small_ref[4:8, lanes] = shift_ref[layer].astype(F32)
        small_ref[0:depth, pl.ds(2 * rows, height)] = bi_ref[...].astype(F32)
        put(first_ref, wq_ref[0], 0)
        put(first_ref, small_ref[...], 3 * width)
        put(first_ref, wq_ref[1], 3 * width + 128)
        for layer, ref, at in ((0, first_ref, 6 * width + 128), (1, rest_ref, 0)):
            put(ref, wo_ref[layer], at)
            put(ref, wi_ref[layer], at + width)
            at += width + hidden
            down = wf_ref[layer].astype(F32)
            for step in range(hidden // width):
                put(ref, down[step * rows : (step + 1) * rows], at)
                at += width

    return pl.pallas_call(
        kernel,
        in_specs=[pl.BlockSpec(memory_space=pltpu.VMEM)] * 8,
        out_shape=[
            struct((copies * rows, 6 * width + 128 + dense), LOW),
            struct((copies * rows, dense), LOW),
        ],
        scratch_shapes=[vmem((rows, 128), F32)],
        compiler_params=pltpu.CompilerParams(vmem_limit_bytes=MEMORY),
    )(attn_weight, attn_bias, out_weight, ffn_in, ffn_in_bias, ffn_out, norm_gain, shifts)


def add_parts(place, parts, halves, after=()):
    lanes = parts[0].shape[1]
    count = len(parts)
    many, rows = GROUPS[1:]
    outs = 2 if halves else 1

    def kernel(place_ref, *refs):
        out_refs, sum_ref = refs[count + len(after) : -1], refs[-1]
        bit = place_ref[0] & 1
        for start in range(0, lanes, 128):
            near = pl.ds(start, 128)
            total = refs[0][:, near].astype(F32)
            for ref in refs[1:count]:
                total = total + ref[:, near].astype(F32)
            if halves:
                sum_ref[:, :, near] = total.reshape(many, rows, 128)
            else:
                out_refs[0][:, near] = total.astype(LOW)
        for side, ref in enumerate(out_refs if halves else ()):
            for start in range(0, lanes, 128):
                near = pl.ds(start, 128)
                block = [sum_ref[2 * step + (bit ^ side), :, near] for step in range(many // 2)]
                ref[:, near] = jnp.concatenate(block, 0).astype(LOW)

    return pl.pallas_call(
        kernel,
        in_specs=[pl.BlockSpec(memory_space=pltpu.SMEM)]
        + [pl.BlockSpec(memory_space=pltpu.VMEM)] * count
        + [pl.BlockSpec(memory_space=pl.ANY)] * len(after),
        out_shape=[struct((many * rows // outs, lanes), LOW)] * outs,
        scratch_shapes=[vmem((many, rows, lanes), F32)],
        compiler_params=pltpu.CompilerParams(vmem_limit_bytes=MEMORY),
    )(place, *parts, *after)


def add_halves(place, pairs):
    many, rows = GROUPS[1] // 2, GROUPS[2]
    widths = [pair[0].shape[1] for pair in pairs]
    lanes = sum(widths)

    def kernel(place_ref, *refs):
        out_refs, sum_ref = refs[2 * len(pairs) : -1], refs[-1]
        at = 0
        for index, size in enumerate(widths):
            for start in range(0, size, 128):
                near = pl.ds(start, 128)
                total = refs[2 * index][:, near].astype(F32) + refs[2 * index + 1][:, near].astype(F32)
                sum_ref[:, :, pl.ds(at + start, 128)] = total.reshape(many, rows, 128)
            at += size
        far = lax.shift_right_logical(place_ref[0], 1)
        for step, ref in enumerate(out_refs):
            ref[...] = sum_ref[far ^ step].astype(LOW)

    return pl.pallas_call(
        kernel,
        in_specs=[pl.BlockSpec(memory_space=pltpu.SMEM)]
        + [pl.BlockSpec(memory_space=pltpu.VMEM)] * (2 * len(pairs)),
        out_shape=[struct((rows, lanes), LOW)] * many,
        scratch_shapes=[vmem((many, rows, lanes), F32)],
        compiler_params=pltpu.CompilerParams(vmem_limit_bytes=MEMORY),
    )(place, *(part for pair in pairs for part in pair))


def write_gradients(place, tail, front, depth, width, hidden):
    rows = GROUPS[2]
    height = hidden // DEVICES
    last = front[0].shape[1] - 3 * width - 128

    def kernel(place_ref, *refs):
        tail_refs, refs = refs[: len(tail)], refs[len(tail) :]
        front_refs, refs = refs[: len(front)], refs[len(front) :]
        gwq_ref, gab_ref, gwo_ref, gwi_ref, gbi_ref, gwf_ref, gain_ref, shift_ref = refs
        spot = place_ref[0]

        def total(refs, at, columns):
            found = 0.0
            for ref in refs:
                block = ref[:, pl.ds(at, columns)].astype(F32)
                found = found + jnp.sum(block.reshape(-1, rows, columns), 0)
            return found

        def own(block, size):
            return pltpu.roll(block, block.shape[1] - spot * size, 1)

        def unfolded(block, count):
            return jnp.concatenate([block[step : step + 1] for step in range(count)], 1)

        for layer, refs, at in ((0, front_refs, last), (1, front_refs, 0)):
            gwq_ref[layer] = total(refs, at, 3 * width)
            block = total(refs, at + 3 * width, 128)
            many = width // 128
            for index in range(2):
                line = unfolded(block[index * many : (index + 1) * many], many)
                gab_ref[layer, pl.ds(index, 1)] = own(line, rows)[:, 0:rows]
        for layer, refs, at in ((0, front_refs, 3 * width + 128), (1, tail_refs, 0)):
            gwo_ref[layer] = total(refs, at, width)
            gwi_ref[layer] = total(refs, at + width, hidden)
            for step in range(hidden // width):
                gwf_ref[layer, pl.ds(step * rows, rows)] = total(
                    refs, at + width + hidden + step * width, width
                )
            at += width + 2 * hidden
            small = own(total(refs, at, width), rows)
            gain_ref[layer] = small[2:4, 0:rows]
            shift_ref[layer] = small[4:8, 0:rows]
            line = unfolded(total(refs, at + width, hidden // 8), 8)
            gbi_ref[pl.ds(layer, 1)] = own(line, height)[:, 0:height]

    outs = [
        struct((depth, rows, 3 * width), F32),
        struct((depth, 2, rows), F32),
        struct((depth, rows, width), F32),
        struct((depth, rows, hidden), F32),
        struct((depth, height), F32),
        struct((depth, height, width), F32),
        struct((depth, 2, rows), F32),
        struct((depth, 4, rows), F32),
    ]
    return pl.pallas_call(
        kernel,
        in_specs=[pl.BlockSpec(memory_space=pltpu.SMEM)]
        + [pl.BlockSpec(memory_space=pltpu.VMEM)] * (len(tail) + len(front)),
        out_shape=outs,
        compiler_params=pltpu.CompilerParams(vmem_limit_bytes=MEMORY),
    )(place, *tail, *front)


def exchange(parts, axis):
    return lax.all_to_all(parts, axis, 0, 0, tiled=True)


def swap(part, axis, step):
    size = lax.axis_size(axis)
    return lax.ppermute(part, axis, [(source, source ^ step) for source in range(size)])


def local(
    hidden_in,
    lengths,
    grad_out,
    attn_weight,
    attn_bias,
    out_weight,
    ffn_in,
    ffn_in_bias,
    ffn_out,
    norm_gain,
    shifts,
):
    depth, rows, width = out_weight.shape
    hidden = ffn_in.shape[2]
    first, second = lax.axis_size("dp"), lax.axis_size("fsdp")
    fits = (second, first, rows) == GROUPS
    urgent_size = 3 * width + 128
    if fits:
        early, later = pack_parameters(
            attn_weight, attn_bias, out_weight, ffn_in, ffn_in_bias, ffn_out, norm_gain, shifts
        )
        across = lax.axis_index("dp").astype(jnp.int32).reshape(1)
        place = lax.axis_index("fsdp").astype(jnp.int32).reshape(1)
        partners = range(1, second)
        early = exchange(early, "dp")
        urgent = early[:, :urgent_size]
        urgent = [urgent] + [swap(urgent, "fsdp", step) for step in partners]
        later = exchange(hold(later, (early,)), "dp")
        raw0 = hold(early[:, urgent_size:], tuple(urgent))
        raw0 = [raw0] + [swap(raw0, "fsdp", step) for step in partners]
    else:
        urgent, raw0, raw1 = gather_other(
            attn_weight, attn_bias, out_weight, ffn_in, ffn_in_bias, ffn_out, norm_gain, shifts
        )
        urgent, raw0, raw1 = ([part[step] for step in range(4)] for part in (urgent, raw0, raw1))
        place = jnp.zeros((1,), jnp.int32)

    qa0, ka0, va0, ob0, urgent = first_kernel(lengths, hidden_in, place, urgent)
    if fits:
        raw1 = hold(later, (ob0,))
        raw1 = [raw1] + [swap(raw1, "fsdp", step) for step in partners]
    n1, n2, inv, yb, gb, gp, z0 = dense_kernel(
        0, lengths, hidden_in, ob0, place, urgent, raw0, 3 * width, hidden
    )
    qa1, ka1, va1, ob1 = attention_kernel(1, lengths, z0, place, urgent, raw0, 0)
    hidden_out, dr1, dob1, *sent_a = turn_kernel(
        1, lengths, z0, ob1, grad_out, place, urgent, raw1, 0, hidden
    )
    dr0, dob0, *sent_b = middle_kernel(
        lengths,
        (z0, dob1, ob1, qa1, ka1, va1, dr1),
        (n1, n2, inv, yb, gb, gp, ob0),
        place,
        urgent,
        raw0,
        hidden,
        (sent_a[0],),
    )
    if fits:
        got_a = [sent_a[0]] + [swap(sent_a[step], "fsdp", step) for step in partners]
        (tail,) = add_parts(across, got_a, False, (sent_b[0],))
        tail = exchange(tail, "dp")
    grad_in, *sent_c = last_kernel(
        lengths, (hidden_in, dob0, ob0, qa0, ka0, va0, dr0), urgent, (sent_b[0],), place
    )
    if fits:
        got_b = [sent_b[0]] + [swap(sent_b[step], "fsdp", step) for step in partners]
        got_c = [sent_c[0]] + [swap(sent_c[step], "fsdp", step) for step in partners]
        keep_b, give_b = add_parts(across, got_b, True, (grad_in, tail))
        keep_c, give_c = add_parts(across, got_c, True)
        pairs = [(keep_b, swap(give_b, "dp", 1)), (keep_c, swap(give_c, "dp", 1))]
        front = add_halves(across, pairs)
        front = [front[0]] + [swap(front[step], "dp", 2 * step) for step in range(1, first // 2)]
        spot = lax.axis_index(("dp", "fsdp")).astype(jnp.int32).reshape(1)
        grads = write_gradients(spot, [tail], front, depth, width, hidden)
    else:
        grads = scatter_other(
            *(jnp.stack(part) for part in (sent_a, sent_b, sent_c)), rows, width, hidden
        )
    return (hidden_out, grad_in, *grads)


def gather_other(
    attn_weight, attn_bias, out_weight, ffn_in, ffn_in_bias, ffn_out, norm_gain, shifts
):
    axes = ("dp", "fsdp")
    gather = lambda part, axis: lax.all_gather(part, axes, axis=axis, tiled=True)
    depth, unused, width = out_weight.shape
    hidden = ffn_in.shape[2]
    outer, inner, rows = GROUPS
    vectors = gather(jnp.concatenate([attn_bias, norm_gain, shifts], 1), 2)
    line = gather(ffn_in_bias, 1)

    def order(natural):
        return (
            natural.reshape(inner, outer, rows, -1).swapaxes(0, 1).reshape(outer, inner * rows, -1)
        )

    def stacked(part):
        part = part.reshape(DEVICES, -1, rows, width)
        return order(part.swapaxes(1, 2).reshape(width, -1))

    small = vectors.reshape(depth, 8, DEVICES, rows).transpose(2, 1, 0, 3).reshape(width, -1)
    line = line.reshape(depth, DEVICES, -1).swapaxes(0, 1)
    line = jnp.pad(line, ((0, 0), (0, 8 - depth), (0, 0))).reshape(width, -1)
    small = jnp.concatenate([small, line], 1)
    small = jnp.pad(small, ((0, 0), (0, 128 - small.shape[1])))
    wq, wo, wi, wf = (gather(part, 1) for part in (attn_weight, out_weight, ffn_in, ffn_out))
    urgent = jnp.concatenate([order(wq[0]), order(small)], 2)
    raw0 = jnp.concatenate([order(wq[1]), order(wo[0]), order(wi[0]), stacked(wf[0])], 2)
    raw1 = jnp.concatenate([order(wo[1]), order(wi[1]), stacked(wf[1])], 2)
    return urgent, raw0, raw1


def scatter_other(sent_a, sent_b, sent_c, own_rows, width, hidden):
    outer, inner, rows = GROUPS
    axes = ("dp", "fsdp")

    def natural(part):
        return part.reshape(outer, inner, rows, -1).swapaxes(0, 1).reshape(width, -1).astype(F32)

    def cut(part, sizes):
        found, at = [], 0
        for size in sizes:
            found.append(part[:, at : at + size])
            at += size
        return found

    dense = [width, hidden, hidden, width, hidden // 8]
    attention = [3 * width, 128]
    wq0, ab0 = cut(natural(sent_c), attention)
    wq1, ab1, wo0, wi0, wf0, small0, bi0 = cut(natural(sent_b), attention + dense)
    wo1, wi1, wf1, small1, bi1 = cut(natural(sent_a), dense)

    def stacked(part):
        part = part.reshape(DEVICES, rows, -1, width).swapaxes(1, 2)
        return part.reshape(hidden, width)

    def spread(parts, axis):
        return lax.psum_scatter(jnp.stack(parts), axes, scatter_dimension=axis, tiled=True)

    return (
        spread([wq0, wq1], 1),
        spread([ab0[:4].reshape(2, width), ab1[:4].reshape(2, width)], 2),
        spread([wo0, wo1], 1),
        spread([wi0, wi1], 1),
        spread([bi0[:8].reshape(-1), bi1[:8].reshape(-1)], 1),
        spread([stacked(wf0), stacked(wf1)], 1),
        spread([small0[2:4], small1[2:4]], 2),
        spread([small0[4:8], small1[4:8]], 2),
    )


def solution(mesh):
    placed = (
        P(("dp", "fsdp"), None),
        P(("dp", "fsdp"), None),
        P(("dp", "fsdp"), None),
        P(None, ("dp", "fsdp"), None),
        P(None, None, ("dp", "fsdp")),
        P(None, ("dp", "fsdp"), None),
        P(None, ("dp", "fsdp"), None),
        P(None, ("dp", "fsdp")),
        P(None, ("dp", "fsdp"), None),
        P(None, None, ("dp", "fsdp")),
        P(None, None, ("dp", "fsdp")),
    )
    return jax.shard_map(
        local,
        mesh=mesh,
        in_specs=placed,
        out_specs=(
            P(("dp", "fsdp"), None),
            P(("dp", "fsdp"), None),
            P(None, ("dp", "fsdp"), None),
            P(None, None, ("dp", "fsdp")),
            P(None, ("dp", "fsdp"), None),
            P(None, ("dp", "fsdp"), None),
            P(None, ("dp", "fsdp")),
            P(None, ("dp", "fsdp"), None),
            P(None, None, ("dp", "fsdp")),
            P(None, None, ("dp", "fsdp")),
        ),
        check_vma=False,
    )
```

```python
from functools import partial

import jax
import jax.numpy as jnp
from jax import lax
from jax.experimental import pallas as pl
from jax.experimental.pallas import tpu as pltpu
from jax.sharding import PartitionSpec as P

HEADS = 4
HD = 64
SEQ = 512
PAIR = 2 * HD
HALF = SEQ // 2
HALVES = (slice(0, HALF), slice(HALF, SEQ))
FAR = -(2.0**100)
FLOOR = -1e20
EPSILON = 1e-12
PIECE = 256
SMALL = 128
GROUPS = (4, 8, 8)
DEVICES = 32
LOW = jnp.bfloat16
F32 = jnp.float32
MEMORY = 2**26


def dot_nn(left, right):
    return lax.dot_general(left, right, (((1,), (0,)), ((), ())), preferred_element_type=F32)


def dot_nt(left, right):
    return lax.dot_general(left, right, (((1,), (1,)), ((), ())), preferred_element_type=F32)


def dot_tn(left, right):
    return lax.dot_general(left, right, (((0,), (0,)), ((), ())), preferred_element_type=F32)


def pieces(total, size=PIECE):
    return [pl.ds(start, size) for start in range(0, total, size)]


def three_parts(values):
    first = values.astype(LOW).astype(F32)
    rest = values - first
    second = rest.astype(LOW).astype(F32)
    return first, second, rest - second


CURVE = (7.97869556e-01, 3.63928094e-02, -8.82195179e-05, -3.66000319e-05, 1.41853144e-06)
BELL = -0.5 / 0.6931471805599453


def gelu_parts(u):
    square = u * u
    curve = CURVE[-1]
    for factor in CURVE[-2::-1]:
        curve = curve * square + factor
    cumulative = 0.5 + 0.5 * jnp.tanh(u * curve)
    slope = cumulative + (u * 0.3989422804014327) * jnp.exp2(square * BELL)
    return u * cumulative, slope


def inverse_of(values):
    guess = pl.reciprocal(values, approx=True)
    return guess * (2.0 - values * guess)


def lane_facts():
    lane = lax.broadcasted_iota(jnp.int32, (1, PAIR), 1)
    return lane < HD, lane & (HD - 1)


def longest_start(lengths_ref, row):
    begin, found = jnp.int32(0), jnp.int32(0)
    for entry in range(lengths_ref.shape[1]):
        size = lengths_ref[row, entry]
        found = jnp.where(size == HALF, begin, found)
        begin = begin + size
    return found


def segments(lengths_ref, row, start, rows):
    places = lax.broadcasted_iota(jnp.int32, (rows, 1), 0) + start + longest_start(lengths_ref, row)
    places = places & (SEQ - 1)
    bound = jnp.int32(0)
    segment = jnp.zeros((rows, 1), jnp.int32)
    last = lengths_ref.shape[1] - 1
    for entry in range(last):
        bound = bound + lengths_ref[row, entry]
        segment = segment + (places >= bound).astype(jnp.int32)
    return segment, (segment == last).astype(F32), last


def attention_forward(row, lengths_ref, x, wq_ref, bias_ref, qa_ref, ka_ref, va_ref, ob_ref, s_ref, p_ref, m_ref, pad_ref, q_ref, aug_ref):
    width = HEADS * HD
    for block in range(3):
        at = block * width
        value = dot_nn(x, wq_ref[:, at : at + width]) + bias_ref[:, at : at + width]
        for pair in range(HEADS // 2):
            q_ref[block, pair] = value[:, pair * PAIR : (pair + 1) * PAIR]
        yield
    for start in range(0, SEQ, PIECE):
        place = pl.ds(start, PIECE)
        low_half, slot = lane_facts()
        segment, pad, last = segments(lengths_ref, row, start, PIECE)
        pad_ref[place] = jnp.broadcast_to(pad, (PIECE, PAIR))
        aug_q = jnp.where(slot == segment, 1.0, 0.0)
        aug_ref[place] = aug_q
        seen = (slot == segment) & (slot != last)
        aug_k = jnp.where(seen, 0.0, jnp.where(slot <= last, FAR, jnp.where(slot <= last + 3, 1.0, 0.0)))
        for pair in range(HEADS // 2):
            q = q_ref[0, pair, place] * HD**-0.5
            k = q_ref[1, pair, place]
            v = q_ref[2, pair, place]
            q_ref[0, pair, place] = q
            qa_ref[2 * pair, place] = jnp.where(low_half, q, aug_q).astype(LOW)
            qa_ref[2 * pair + 1, place] = jnp.where(low_half, aug_q, q).astype(LOW)
            ka_ref[2 * pair, place] = jnp.where(low_half, k, aug_k).astype(LOW)
            ka_ref[2 * pair + 1, place] = jnp.where(low_half, aug_k, k).astype(LOW)
            va_ref[2 * pair, place] = jnp.where(low_half, v, 1.0).astype(LOW)
            va_ref[2 * pair + 1, place] = jnp.where(low_half, 1.0, v).astype(LOW)
        yield

    def scores(head):
        for half in HALVES:
            s_ref[head % 2, half] = dot_nt(qa_ref[head, half], ka_ref[head, half])

    def softmax(head):
        for place in pieces(SEQ):
            highest = jnp.maximum(jnp.max(s_ref[head % 2, place], -1, keepdims=True), FLOOR)
            m_ref[head % 2, place] = jnp.broadcast_to(highest, (PIECE, PAIR))
            p_ref[head % 2, place] = jnp.exp(s_ref[head % 2, place] - highest).astype(LOW)

    scores(0)
    yield
    for head in range(HEADS):
        if head + 1 < HEADS:
            scores(head + 1)
            yield
        softmax(head)
        yield
        for half in HALVES:
            q_ref[1, head % 2, half] = dot_nn(p_ref[head % 2, half], va_ref[head, half])
        if head % 2:
            pair = head // 2
            for start in range(0, SEQ, PIECE):
                place = pl.ds(start, PIECE)
                low_half, slot = lane_facts()
                even = q_ref[1, 0, place]
                odd = q_ref[1, 1, place]
                pad = pad_ref[place]
                last = lengths_ref.shape[1] - 1
                total = jnp.where(low_half, odd, even) + pad
                top = jnp.where(low_half, m_ref[1, place], m_ref[0, place])
                spread = jnp.where(pad > 0, 0.0, top + jnp.log(total))
                first, second, third = three_parts(spread)
                aug = jnp.where(
                    slot == last + 1,
                    -first,
                    jnp.where(slot == last + 2, -second, jnp.where(slot == last + 3, -third, aug_ref[place])),
                )
                q = q_ref[0, pair, place]
                qa_ref[2 * pair, place] = jnp.where(low_half, q, aug).astype(LOW)
                qa_ref[2 * pair + 1, place] = jnp.where(low_half, aug, q).astype(LOW)
                v = q_ref[2, pair, place].astype(LOW).astype(F32)
                share = inverse_of(pltpu.roll(total, HD, 1))
                out = jnp.where(low_half, even, odd) * share + pad * v
                ob_ref[place, pl.ds(pair * PAIR, PAIR)] = out.astype(LOW)
            yield


def normal(values):
    centred = values - jnp.mean(values, -1, keepdims=True)
    inverse = lax.rsqrt(jnp.mean(centred * centred, -1, keepdims=True) + EPSILON)
    return centred * inverse, inverse


def normal_back(cotangent, unit, inverse, gains):
    scaled = cotangent * gains
    return inverse * (
        scaled
        - jnp.mean(scaled, -1, keepdims=True)
        - unit * jnp.mean(scaled * unit, -1, keepdims=True)
    )


def dense_forward(x_ref, ob_ref, wo_ref, wi_ref, wf_ref, small_ref, bi_ref, n1_ref, n2_ref, inv_ref, yb_ref, gb_ref, gp_ref, z_ref, work_ref, u_ref):
    small = lambda index: small_ref[pl.ds(index, 1)]
    work_ref[...] = dot_nn(ob_ref[...], wo_ref[...])
    yield
    for place in pieces(SEQ):
        unit, inverse = normal(x_ref[place].astype(F32) + work_ref[place] + small(4))
        n1_ref[place] = unit
        inv_ref[place, pl.ds(0, HD)] = jnp.broadcast_to(inverse, (PIECE, HD))
        y = unit * small(2) + small(5)
        yb_ref[place] = y.astype(LOW)
        work_ref[place] = y + small(6)
        yield
    columns = 256
    count = wi_ref.shape[1] // columns

    def into(step):
        u_ref[step % 2] = dot_nn(yb_ref[...], wi_ref[:, pl.ds(step * columns, columns)])

    into(0)
    yield
    for step in range(count):
        if step + 1 < count:
            into(step + 1)
            yield
        lanes = pl.ds(step * columns, columns)
        for place in pieces(SEQ, SMALL):
            g, slope = gelu_parts(u_ref[step % 2, place] + bi_ref[:, lanes])
            gb_ref[place, lanes] = g.astype(LOW)
            gp_ref[place, lanes] = slope.astype(LOW)
            yield
    work_ref[...] += dot_nn(gb_ref[...], wf_ref[...])
    yield
    for place in pieces(SEQ):
        unit, inverse = normal(work_ref[place])
        n2_ref[place] = unit
        inv_ref[place, pl.ds(HD, HD)] = jnp.broadcast_to(inverse, (PIECE, HD))
        z_ref[place] = (unit * small(3) + small(7)).astype(z_ref.dtype)
        yield


def fold(values):
    return jnp.sum(values.reshape(-1, 8, values.shape[-1]), 0)


def dense_backward(dz_ref, n1_ref, n2_ref, inv_ref, yb_ref, gb_ref, gp_ref, ob_ref, wo_ref, wi_ref, wf_ref, small_ref, dr_ref, dob_ref, gwo_ref, gwi_ref, gwf_ref, gsmall_ref, gbi_ref, low_ref, u_ref, du_ref, turned_ref):
    small = lambda index: small_ref[pl.ds(index, 1)]
    for place in pieces(SEQ):
        dz = dz_ref[place].astype(F32)
        unit = n2_ref[place]
        gsmall_ref[3] += fold(dz * unit)
        gsmall_ref[7] += fold(dz)
        dr = normal_back(dz, unit, inv_ref[place, pl.ds(HD, 1)], small(3))
        dr_ref[place] = dr
        df = dr.astype(LOW)
        low_ref[place] = df
        gsmall_ref[6] += fold(df.astype(F32))
        yield
    columns = 256
    count = wi_ref.shape[1] // columns

    def back(step):
        u_ref[step % 2] = dot_nt(low_ref[...], wf_ref[pl.ds(step * columns, columns)])

    back(0)
    turned_ref[0] = low_ref[...].T
    turned_ref[1] = yb_ref[...].T
    yield
    for step in range(count):
        if step + 1 < count:
            back(step + 1)
            yield
        lanes = pl.ds(step * columns, columns)
        gwf_ref[:, lanes] += dot_nn(turned_ref[0], gb_ref[:, lanes])
        yield
        for place in pieces(SEQ, SMALL):
            du = (u_ref[step % 2, place] * gp_ref[place, lanes].astype(F32)).astype(LOW)
            du_ref[place, lanes] = du
            gbi_ref[:, lanes] += fold(du.astype(F32))
        yield
        gwi_ref[:, lanes] += dot_nn(turned_ref[1], du_ref[:, lanes])
        yield
    u_ref[0] = dot_nt(du_ref[...], wi_ref[...])
    yield
    for place in pieces(SEQ):
        dy = dr_ref[place] + u_ref[0, place]
        unit = n1_ref[place]
        gsmall_ref[2] += fold(dy * unit)
        gsmall_ref[5] += fold(dy)
        dr = normal_back(dy, unit, inv_ref[place, pl.ds(0, 1)], small(2))
        dr_ref[place] = dr
        da = dr.astype(LOW)
        low_ref[place] = da
        gsmall_ref[4] += fold(da.astype(F32))
        yield
    gwo_ref[...] += dot_tn(ob_ref[...], low_ref[...])
    dob_ref[...] = dot_nt(low_ref[...], wo_ref[...]).astype(LOW)
    yield


def attention_backward(row, lengths_ref, x, dob_ref, ob_ref, qa_ref, ka_ref, va_ref, wq_ref, dr_ref, dx_ref, gwq_ref, gbias_ref, da_ref, p_ref, ds_ref, s_ref, dqkv_ref, dq_ref, pad_ref, kt_ref, dqt_ref):
    width = HEADS * HD
    low_half, slot = lane_facts()
    for start in range(0, SEQ, PIECE):
        place = pl.ds(start, PIECE)
        segment, pad, last = segments(lengths_ref, row, start, PIECE)
        pad_ref[place] = jnp.broadcast_to(pad, (PIECE, PAIR))
        for pair in range(HEADS // 2):
            lanes = pl.ds(pair * PAIR, PAIR)
            dob = dob_ref[place, lanes].astype(F32)
            product = dob * ob_ref[place, lanes].astype(F32)
            even = jnp.sum(jnp.where(low_half, product, 0.0), -1, keepdims=True)
            odd = jnp.sum(jnp.where(low_half, 0.0, product), -1, keepdims=True)
            first, second, third = three_parts(jnp.where(low_half, odd, even))
            aug = jnp.where(
                slot == 0, -first, jnp.where(slot == 1, -second, jnp.where(slot == 2, -third, 0.0))
            )
            da_ref[2 * pair, place] = jnp.where(low_half, dob, aug).astype(LOW)
            da_ref[2 * pair + 1, place] = jnp.where(low_half, aug, dob).astype(LOW)
        yield
    for pair in range(HEADS // 2):
        low_half, unused = lane_facts()
        keys = jnp.where(low_half, ka_ref[2 * pair].astype(F32), ka_ref[2 * pair + 1].astype(F32))
        kt_ref[pl.ds(pair * PAIR, PAIR)] = keys.T.astype(LOW)
    low_half, slot = lane_facts()

    def scores(head):
        for half in HALVES:
            s_ref[0, head % 2, half] = dot_nt(ka_ref[head, half], qa_ref[head, half])
            s_ref[1, head % 2, half] = dot_nt(va_ref[head, half], da_ref[head, half])

    def weigh(head):
        for place in pieces(SEQ, SMALL):
            p = jnp.exp(s_ref[0, head % 2, place])
            p_ref[head % 2, place] = p.astype(LOW)
            ds_ref[head % 2, place] = (p * s_ref[1, head % 2, place]).astype(LOW)

    scores(0)
    yield
    for head in range(HEADS):
        if head + 1 < HEADS:
            scores(head + 1)
            yield
        weigh(head)
        yield
        side = head % 2
        for half in HALVES:
            dq_ref[1, side, half] = dot_nn(ds_ref[head % 2, half], qa_ref[head, half])
            dq_ref[2, side, half] = dot_nn(p_ref[head % 2, half], da_ref[head, half])
            dqt_ref[side * HD : (side + 1) * HD, half] = dot_nn(
                kt_ref[head * HD : (head + 1) * HD, half], ds_ref[head % 2, half]
            )
        yield
        if side:
            pair = head // 2
            dq_ref[0, 0] = dqt_ref[...].T
            for start in range(0, SEQ, PIECE):
                place = pl.ds(start, PIECE)
                dq = dq_ref[0, 0, place] * HD**-0.5
                dk = jnp.where(low_half, dq_ref[1, 0, place], dq_ref[1, 1, place])
                dv = jnp.where(low_half, dq_ref[2, 0, place], dq_ref[2, 1, place])
                dv = dv + pad_ref[place] * dob_ref[place, pl.ds(pair * PAIR, PAIR)].astype(F32)
                for block, value in enumerate((dq, dk, dv)):
                    lanes = pl.ds(block * width + pair * PAIR, PAIR)
                    value = value.astype(LOW)
                    dqkv_ref[place, lanes] = value
                    if block != 1:
                        into = pl.ds(pair * PAIR, PAIR)
                        gbias_ref[block // 2, :, into] += fold(value.astype(F32))
    yield
    gwq_ref[...] += dot_tn(x, dqkv_ref[...])
    yield
    dx_ref[...] = dr_ref[...] + dot_nt(dqkv_ref[...], wq_ref[...])
    yield


def unpack_matrix(raw_ref, at, into_ref):
    width = into_ref.shape[0]
    for start in range(0, into_ref.shape[1], width):
        block = raw_ref[:, :, pl.ds(at + start, width)].astype(F32)
        block = block.reshape(GROUPS + (width,)).swapaxes(0, 1).reshape(width, width)
        into_ref[:, pl.ds(start, width)] = block.astype(LOW)


def unpack_stacked(raw_ref, at, into_ref):
    width = into_ref.shape[1]
    count = into_ref.shape[0] // width
    blocks = [
        raw_ref[:, :, pl.ds(at + step * width, width)].astype(F32).reshape(GROUPS + (width,))
        for step in range(count)
    ]
    outer, inner, rows = GROUPS
    for place in range(inner):
        part = jnp.stack([jnp.stack([block[f, place] for block in blocks]) for f in range(outer)])
        size = outer * count * rows
        into_ref[pl.ds(place * size, size)] = part.reshape(size, width).astype(LOW)


def counter(shape, axis):
    return lax.broadcasted_iota(jnp.int32, shape, axis)


def split_by(values, size):
    return lax.shift_right_logical(values, size.bit_length() - 1), values & (size - 1)


def sources(rows):
    outer, inner, height = GROUPS
    group, within = split_by(counter((rows, 1), 0), height)
    far, near = split_by(group, inner)
    return near * outer + far, within


def unpack_vectors(raw_ref, at, layer):
    outer, inner, rows = GROUPS
    total = outer * inner * rows
    raw = raw_ref[:, :, pl.ds(at, 128)].reshape(total, 128)
    owner, place = split_by(counter((1, total), 1), rows)
    pick = jnp.where(counter((128, 1), 0) == rows * layer + place, 1.0, 0.0).astype(LOW)
    device, unused = sources(total)
    spread = jnp.where(owner == device, dot_nn(raw, pick), 0.0)
    return jnp.sum(spread.reshape(outer * inner, rows, total), 0)


def unpack_hidden(raw_ref, at, layer, hidden):
    outer, inner, rows = GROUPS
    total = outer * inner * rows
    raw = raw_ref[:, :, pl.ds(at, 128)].reshape(total, 128)
    owner, place = split_by(counter((1, hidden), 1), hidden // (outer * inner))
    pick = jnp.where(counter((128, 1), 0) == 2 * rows + place, 1.0, 0.0).astype(LOW)
    device, within = sources(total)
    device = jnp.where(within == layer, device, -1)
    spread = jnp.where(owner == device, dot_nn(raw, pick), 0.0)
    return jnp.sum(spread, 0, keepdims=True)


def pack_matrix(sum_ref, sent_ref, at):
    width = sum_ref.shape[0]
    outer, inner, rows = GROUPS
    for start in range(0, sum_ref.shape[1], width):
        block = sum_ref[:, pl.ds(start, width)].reshape(inner, outer, rows, width)
        block = block.swapaxes(0, 1).reshape(outer, inner * rows, width)
        sent_ref[:, :, pl.ds(at + start, width)] = block.astype(LOW)


def pack_stacked(sum_ref, sent_ref, at):
    width = sum_ref.shape[0]
    outer, inner, rows = GROUPS
    count = sum_ref.shape[1] // width
    near = inner // count
    for step in range(count):
        block = sum_ref[:, pl.ds(step * width, width)].T
        block = block.reshape(near, outer, count, rows, width)
        for part in range(count):
            piece = jnp.stack([block[:, f, part] for f in range(outer)])
            piece = piece.reshape(outer, near * rows, width)
            sent_ref[:, pl.ds(step * near * rows, near * rows), pl.ds(at + part * width, width)] = (
                piece.astype(LOW)
            )


def pack_shared(block, sent_ref, at):
    outer, inner, rows = GROUPS
    columns = block.shape[1]
    block = jnp.broadcast_to(block[None], (outer * inner, rows, columns))
    sent_ref[:, :, pl.ds(at, columns)] = block.reshape(outer, inner * rows, columns).astype(LOW)


def folded(line, lanes):
    return [line[:, at : at + lanes] for at in range(0, line.shape[1], lanes)]


def pack_attention(gwq_ref, gbias_ref, sent_ref, at):
    pack_matrix(gwq_ref, sent_ref, at)
    width = gwq_ref.shape[0]
    parts = []
    for index in range(2):
        parts += folded(jnp.sum(gbias_ref[index], 0, keepdims=True), 128)
    block = jnp.concatenate(parts + [jnp.zeros((8 - len(parts), 128), F32)], 0)
    pack_shared(block, sent_ref, at + 3 * width)


def pack_dense(gwo_ref, gwi_ref, gwf_ref, gsmall_ref, gbi_ref, sent_ref, at):
    width, hidden = gwi_ref.shape
    pack_matrix(gwo_ref, sent_ref, at)
    pack_matrix(gwi_ref, sent_ref, at + width)
    pack_stacked(gwf_ref, sent_ref, at + width + hidden)
    at = at + width + 2 * hidden
    pack_shared(jnp.sum(gsmall_ref[...], 1), sent_ref, at)
    line = jnp.sum(gbi_ref[...], 0, keepdims=True)
    pack_shared(jnp.concatenate(folded(line, hidden // 8), 0), sent_ref, at + width)


def shape_of(array):
    return jax.ShapeDtypeStruct(array.shape, array.dtype)


def by_row(shape, group):
    if len(shape) == 2:
        return pl.BlockSpec((group * SEQ, shape[1]), lambda step: (step, 0))
    return pl.BlockSpec((group,) + tuple(shape[1:]), lambda step: (step,) + (0,) * (len(shape) - 1))


def one_row(ref, member):
    if len(ref.shape) == 2:
        return ref.at[pl.ds(member * SEQ, SEQ)]
    return ref.at[member]


def alternate(runs):
    running = []
    waiting = list(runs)
    while running or waiting:
        if waiting:
            running.append(waiting.pop(0))
        for run in list(running):
            try:
                next(run)
            except StopIteration:
                running.remove(run)


def whole(shape):
    return pl.BlockSpec(tuple(shape), lambda row: (0,) * len(shape))


def run_rows(
    body, lengths, rowwise, fixed, row_outs, sent, shared, private, cost, setup, finish, after=(),
    scalars=(), group=1
):
    count = lengths.shape[0]
    group = group if count % group == 0 else 1
    cuts = [len(scalars), len(rowwise), len(fixed), len(after), len(row_outs), len(sent)]
    cuts += [len(shared)] + [len(private)] * group

    def kernel(lengths_ref, *refs):
        step = pl.program_id(0)
        groups = []
        at = 0
        for cut in cuts:
            groups.append(refs[at : at + cut])
            at += cut
        numbers, rows_in, fixed_in, unused, rows_out, sent_out, work = groups[:7]

        @pl.when(step == 0)
        def _():
            setup(numbers, fixed_in, sent_out, work)

        alternate(
            body(
                step * group + member,
                lengths_ref,
                [one_row(ref, member) for ref in rows_in],
                [one_row(ref, member) for ref in rows_out],
                work,
                groups[7 + member],
            )
            for member in range(group)
        )

        if finish:

            @pl.when(step == count // group - 1)
            def _():
                finish(numbers, work, sent_out)

    return pl.pallas_call(
        kernel,
        grid=(count // group,),
        in_specs=[pl.BlockSpec(memory_space=pltpu.SMEM)] * (1 + len(scalars))
        + [by_row(array.shape, group) for array in rowwise]
        + [whole(array.shape) for array in fixed]
        + [pl.BlockSpec(memory_space=pl.ANY) for array in after],
        out_specs=[by_row(part.shape, group) for part in row_outs]
        + [whole(part.shape) for part in sent],
        out_shape=list(row_outs) + list(sent),
        scratch_shapes=list(shared) + list(private) * group,
        compiler_params=pltpu.CompilerParams(
            dimension_semantics=("arbitrary",), vmem_limit_bytes=MEMORY
        ),
        cost_estimate=pl.CostEstimate(flops=cost, bytes_accessed=8 * 2**20, transcendentals=0),
    )(lengths, *scalars, *rowwise, *fixed, *after)


def struct(shape, dtype):
    return jax.ShapeDtypeStruct(tuple(shape), dtype)


FORWARD_SCRATCH = lambda: [
    pltpu.VMEM((2, SEQ, HALF), F32),
    pltpu.VMEM((2, SEQ, HALF), LOW),
    pltpu.VMEM((2, SEQ, PAIR), F32),
    pltpu.VMEM((SEQ, PAIR), F32),
    pltpu.VMEM((3, HEADS // 2, SEQ, PAIR), F32),
    pltpu.VMEM((SEQ, PAIR), F32),
]
BACKWARD_SCRATCH = lambda: [
    pltpu.VMEM((HEADS, SEQ, PAIR), LOW),
    pltpu.VMEM((2, SEQ, HALF), LOW),
    pltpu.VMEM((2, SEQ, HALF), LOW),
    pltpu.VMEM((2, 2, SEQ, HALF), F32),
    pltpu.VMEM((SEQ, 3 * HEADS * HD), LOW),
    pltpu.VMEM((3, 2, SEQ, PAIR), F32),
    pltpu.VMEM((SEQ, PAIR), F32),
    pltpu.VMEM((HEADS * HD, SEQ), LOW),
    pltpu.VMEM((PAIR, SEQ), F32),
]


def attention_outs(rows, tokens, width):
    heads = (rows, HEADS, SEQ, PAIR)
    return [struct(heads, LOW)] * 3 + [struct((tokens, width), LOW)]


def dense_outs(tokens, width, hidden):
    return [
        struct((tokens, width), F32),
        struct((tokens, width), F32),
        struct((tokens, PAIR), F32),
        struct((tokens, width), LOW),
        struct((tokens, hidden), LOW),
        struct((tokens, hidden), LOW),
    ]


def vmem(shape, dtype):
    return pltpu.VMEM(tuple(shape), dtype)


def attention_weights(width):
    return [vmem((width, 3 * width), LOW), vmem((1, 3 * width), F32)]


def dense_weights(width, hidden):
    return [
        vmem((width, width), LOW),
        vmem((width, hidden), LOW),
        vmem((hidden, width), LOW),
        vmem((8, width), F32),
        vmem((1, hidden), F32),
    ]


def dense_sums(width, hidden):
    return [
        vmem((width, width), F32),
        vmem((width, hidden), F32),
        vmem((width, hidden), F32),
        vmem((8, 8, width), F32),
        vmem((8, hidden), F32),
    ]


def attention_sums(width):
    return [vmem((width, 3 * width), F32), vmem((2, 8, width), F32)]


def dense_work(width, hidden):
    return [
        vmem((SEQ, width), LOW),
        vmem((2, SEQ, width), F32),
        vmem((SEQ, hidden), LOW),
        vmem((2, width, SEQ), LOW),
    ]


def set_attention(layer, urgent_ref, raw_ref, at, wq_ref, bias_ref):
    width = wq_ref.shape[0]
    unpack_matrix(raw_ref, at, wq_ref)
    vectors = unpack_vectors(urgent_ref, 3 * width, layer)
    bias_ref[:, :width] = vectors[0:1]
    bias_ref[:, width : 2 * width] = jnp.zeros((1, width), F32)
    bias_ref[:, 2 * width :] = vectors[1:2]


def set_dense(layer, urgent_ref, raw_ref, at, wo_ref, wi_ref, wf_ref, small_ref, bi_ref):
    width, hidden = wi_ref.shape
    unpack_matrix(raw_ref, at, wo_ref)
    unpack_matrix(raw_ref, at + width, wi_ref)
    unpack_stacked(raw_ref, at + width + hidden, wf_ref)
    small_ref[...] = unpack_vectors(urgent_ref, 3 * width, layer)
    bi_ref[...] = unpack_hidden(urgent_ref, 3 * width, layer, hidden)


def clear(refs):
    for ref in refs:
        ref[...] = jnp.zeros(ref.shape, ref.dtype)


def assemble(place_ref, part_refs, into_ref):
    for step, ref in enumerate(part_refs):
        into_ref[place_ref[0] ^ step] = ref[...]


def raw_block(parts):
    return vmem((len(parts),) + parts[0].shape, LOW)


def turned_back(lengths_ref, row, values):
    return pltpu.roll(values, longest_start(lengths_ref, row), 0).astype(LOW)


def rotate_kernel(lengths, arrays):
    def body(row, lengths_ref, rowwise, outs, work, own):
        back = (SEQ - longest_start(lengths_ref, row)) & (SEQ - 1)
        for source, target in zip(rowwise, outs):
            target[...] = pltpu.roll(source[...].astype(F32), back, 0).astype(LOW)
            yield

    return run_rows(
        body, lengths, list(arrays), [], [struct(array.shape, LOW) for array in arrays], [], [], [],
        10**6, lambda *refs: None, None,
    )


def first_kernel(lengths, x, place, parts):
    rows, (tokens, width) = lengths.shape[0], x.shape

    def setup(numbers, fixed, sent, work):
        assemble(numbers[0], fixed, sent[0])
        set_attention(0, sent[0], sent[0], 0, *work)

    def body(row, lengths_ref, rowwise, outs, work, own):
        return attention_forward(row, lengths_ref, rowwise[0][...], *work, *outs, *own)

    return run_rows(
        body, lengths, [x], list(parts), attention_outs(rows, tokens, width),
        [struct((len(parts),) + parts[0].shape, LOW)],
        attention_weights(width), FORWARD_SCRATCH(), 4 * 10**9, setup, None, (), [place],
    )


def attention_kernel(layer, lengths, x, place, urgent, parts, at):
    rows, (tokens, width) = lengths.shape[0], x.shape

    def setup(numbers, fixed, sent, work):
        assemble(numbers[0], fixed[1:], work[2])
        set_attention(layer, fixed[0], work[2], at, *work[:2])

    def body(row, lengths_ref, rowwise, outs, work, own):
        return attention_forward(
            row, lengths_ref, rowwise[0][...].astype(LOW), *work[:2], *outs, *own
        )

    return run_rows(
        body, lengths, [x], [urgent] + list(parts), attention_outs(rows, tokens, width), [],
        attention_weights(width) + [raw_block(parts)], FORWARD_SCRATCH(),
        4 * 10**9, setup, None, (), [place],
    )


def dense_kernel(layer, lengths, x, ob, place, urgent, parts, at, hidden):
    tokens, width = x.shape

    def setup(numbers, fixed, sent, work):
        assemble(numbers[0], fixed[1:], work[5])
        set_dense(layer, fixed[0], work[5], at, *work[:5])

    def body(row, lengths_ref, rowwise, outs, work, own):
        return dense_forward(*rowwise, *work[:5], *outs, *own)

    return run_rows(
        body, lengths, [x, ob], [urgent] + list(parts),
        dense_outs(tokens, width, hidden) + [struct((tokens, width), F32)], [],
        dense_weights(width, hidden) + [raw_block(parts)],
        [vmem((SEQ, width), F32), vmem((2, SEQ, width), F32)],
        5 * 10**9, setup, None, (), [place],
    )


def turn_kernel(layer, lengths, x, ob, cotangent, place, urgent, parts, at, hidden):
    tokens, width = x.shape
    columns = width + 2 * hidden + width + hidden // 8

    def setup(numbers, fixed, sent, work):
        assemble(numbers[0], fixed[1:], work[11])
        set_dense(layer, fixed[0], work[11], at, *work[:5])
        clear(work[5:10])

    def body(row, lengths_ref, rowwise, outs, work, own):
        x_ref, ob_ref, dz_ref = rowwise
        z_ref, dr_ref, dob_ref = outs
        weights, sums = work[:5], work[5:10]
        kept, work_ref, back = own[:6], own[6], own[7:]
        yield from dense_forward(x_ref, ob_ref, *weights, *kept, work_ref, work_ref, back[1])
        z_ref[...] = turned_back(lengths_ref, row, work_ref[...])
        yield
        yield from dense_backward(dz_ref, *kept, ob_ref, *weights[:4], dr_ref, dob_ref, *sums, *back)

    def finish(numbers, work, sent):
        pack_dense(*work[5:10], work[10], 0)
        hand_out(numbers[0], work[10], sent)

    kept = [vmem((SEQ,) + part.shape[1:], part.dtype) for part in dense_outs(tokens, width, hidden)]
    return run_rows(
        body, lengths, [x, ob, cotangent], [urgent] + list(parts),
        [struct((tokens, width), LOW), struct((tokens, width), F32), struct((tokens, width), LOW)],
        [struct((64, columns), LOW)] * 4,
        dense_weights(width, hidden) + dense_sums(width, hidden)
        + [vmem((4, 64, columns), LOW), raw_block(parts)],
        kept + [vmem((SEQ, width), F32)] + dense_work(width, hidden),
        10**10, setup, finish, (), [place], 2,
    )


def hand_out(place_ref, packed_ref, sent):
    for step, ref in enumerate(sent):
        ref[...] = packed_ref[place_ref[0] ^ step]


def middle_kernel(lengths, upper, lower, place, urgent, parts, hidden, after):
    tokens, width = upper[0].shape
    columns = 3 * width + 128 + width + 2 * hidden + width + hidden // 8

    def setup(numbers, fixed, sent, work):
        assemble(numbers[0], fixed[1:], work[15])
        set_attention(1, fixed[0], work[15], 0, *work[:2])
        set_dense(0, fixed[0], work[15], 3 * width, *work[2:7])
        clear(work[7:14])

    def body(row, lengths_ref, rowwise, outs, work, own):
        up, low = rowwise[:7], rowwise[7:]
        dx_ref = own[0]
        yield from attention_backward(
            row, lengths_ref, up[0][...].astype(LOW), *up[1:6], work[0], up[6], dx_ref,
            *work[7:9], *own[5:],
        )
        yield from dense_backward(dx_ref, *low, *work[2:6], *outs, *work[9:14], *own[1:5])

    def finish(numbers, work, sent):
        pack_attention(*work[7:9], work[14], 0)
        pack_dense(*work[9:14], work[14], 3 * width + 128)
        hand_out(numbers[0], work[14], sent)

    return run_rows(
        body, lengths, list(upper) + list(lower), [urgent] + list(parts),
        [struct((tokens, width), F32), struct((tokens, width), LOW)],
        [struct((64, columns), LOW)] * 4,
        attention_weights(width) + dense_weights(width, hidden)
        + attention_sums(width) + dense_sums(width, hidden)
        + [vmem((4, 64, columns), LOW), raw_block(parts)],
        [vmem((SEQ, width), F32)] + dense_work(width, hidden) + BACKWARD_SCRATCH(),
        15 * 10**9, setup, finish, after, [place],
    )


def last_kernel(lengths, upper, urgent, after, place):
    tokens, width = upper[0].shape

    def setup(numbers, fixed, sent, work):
        set_attention(0, fixed[0], fixed[0], 0, *work[:2])
        clear(work[2:4])

    def body(row, lengths_ref, rowwise, outs, work, own):
        yield from attention_backward(
            row, lengths_ref, rowwise[0][...], *rowwise[1:6], work[0], rowwise[6], own[0],
            *work[2:4], *own[1:],
        )
        outs[0][...] = turned_back(lengths_ref, row, own[0][...])
        yield

    def finish(numbers, work, sent):
        pack_attention(*work[2:4], work[4], 0)
        hand_out(numbers[0], work[4], sent)

    return run_rows(
        body, lengths, list(upper), [urgent], [struct((tokens, width), LOW)],
        [struct((64, 3 * width + 128), LOW)] * 4,
        attention_weights(width) + attention_sums(width) + [vmem((4, 64, 3 * width + 128), LOW)],
        [vmem((SEQ, width), F32)] + BACKWARD_SCRATCH(), 8 * 10**9, setup, finish, after, [place], 2,
    )


def hold(array, after):
    def kernel(*refs):
        pass

    anywhere = pl.BlockSpec(memory_space=pl.ANY)
    return pl.pallas_call(
        kernel,
        in_specs=[anywhere] * (1 + len(after)),
        out_specs=anywhere,
        out_shape=shape_of(array),
        input_output_aliases={0: 0},
    )(array, *after)


def pack_parameters(
    attn_weight, attn_bias, out_weight, ffn_in, ffn_in_bias, ffn_out, norm_gain, shifts
):
    depth, rows, width = out_weight.shape
    copies = GROUPS[1]
    hidden = ffn_in.shape[2]
    dense = width + 2 * hidden
    height = ffn_in_bias.shape[1]

    def kernel(wq_ref, ab_ref, wo_ref, wi_ref, bi_ref, wf_ref, gain_ref, shift_ref, first_ref, rest_ref, small_ref):
        def put(ref, block, at):
            block = jnp.broadcast_to(block.astype(F32)[None], (copies,) + block.shape)
            block = block.reshape(copies * block.shape[1], block.shape[2])
            ref[:, pl.ds(at, block.shape[1])] = block.astype(LOW)

        small_ref[...] = jnp.zeros(small_ref.shape, F32)
        for layer in range(depth):
            lanes = pl.ds(rows * layer, rows)
            small_ref[0:2, lanes] = ab_ref[layer].astype(F32)
            small_ref[2:4, lanes] = gain_ref[layer].astype(F32)
            small_ref[4:8, lanes] = shift_ref[layer].astype(F32)
        small_ref[0:depth, pl.ds(2 * rows, height)] = bi_ref[...].astype(F32)
        put(first_ref, wq_ref[0], 0)
        put(first_ref, small_ref[...], 3 * width)
        put(first_ref, wq_ref[1], 3 * width + 128)
        for layer, ref, at in ((0, first_ref, 6 * width + 128), (1, rest_ref, 0)):
            put(ref, wo_ref[layer], at)
            put(ref, wi_ref[layer], at + width)
            at += width + hidden
            down = wf_ref[layer].astype(F32)
            for step in range(hidden // width):
                put(ref, down[step * rows : (step + 1) * rows], at)
                at += width

    return pl.pallas_call(
        kernel,
        in_specs=[pl.BlockSpec(memory_space=pltpu.VMEM)] * 8,
        out_shape=[
            struct((copies * rows, 6 * width + 128 + dense), LOW),
            struct((copies * rows, dense), LOW),
        ],
        scratch_shapes=[vmem((rows, 128), F32)],
        compiler_params=pltpu.CompilerParams(vmem_limit_bytes=MEMORY),
    )(attn_weight, attn_bias, out_weight, ffn_in, ffn_in_bias, ffn_out, norm_gain, shifts)


def add_parts(place, parts, halves, after=()):
    lanes = parts[0].shape[1]
    count = len(parts)
    many, rows = GROUPS[1:]
    outs = 2 if halves else 1

    def kernel(place_ref, *refs):
        out_refs, sum_ref = refs[count + len(after) : -1], refs[-1]
        bit = place_ref[0] & 1
        for start in range(0, lanes, 128):
            near = pl.ds(start, 128)
            total = refs[0][:, near].astype(F32)
            for ref in refs[1:count]:
                total = total + ref[:, near].astype(F32)
            if halves:
                sum_ref[:, :, near] = total.reshape(many, rows, 128)
            else:
                out_refs[0][:, near] = total.astype(LOW)
        for side, ref in enumerate(out_refs if halves else ()):
            for start in range(0, lanes, 128):
                near = pl.ds(start, 128)
                block = [sum_ref[2 * step + (bit ^ side), :, near] for step in range(many // 2)]
                ref[:, near] = jnp.concatenate(block, 0).astype(LOW)

    return pl.pallas_call(
        kernel,
        in_specs=[pl.BlockSpec(memory_space=pltpu.SMEM)]
        + [pl.BlockSpec(memory_space=pltpu.VMEM)] * count
        + [pl.BlockSpec(memory_space=pl.ANY)] * len(after),
        out_shape=[struct((many * rows // outs, lanes), LOW)] * outs,
        scratch_shapes=[vmem((many, rows, lanes), F32)],
        compiler_params=pltpu.CompilerParams(vmem_limit_bytes=MEMORY),
    )(place, *parts, *after)


def add_halves(place, pairs):
    many, rows = GROUPS[1] // 2, GROUPS[2]
    widths = [pair[0].shape[1] for pair in pairs]
    lanes = sum(widths)

    def kernel(place_ref, *refs):
        out_refs, sum_ref = refs[2 * len(pairs) : -1], refs[-1]
        at = 0
        for index, size in enumerate(widths):
            for start in range(0, size, 128):
                near = pl.ds(start, 128)
                total = refs[2 * index][:, near].astype(F32) + refs[2 * index + 1][:, near].astype(F32)
                sum_ref[:, :, pl.ds(at + start, 128)] = total.reshape(many, rows, 128)
            at += size
        far = lax.shift_right_logical(place_ref[0], 1)
        for step, ref in enumerate(out_refs):
            ref[...] = sum_ref[far ^ step].astype(LOW)

    return pl.pallas_call(
        kernel,
        in_specs=[pl.BlockSpec(memory_space=pltpu.SMEM)]
        + [pl.BlockSpec(memory_space=pltpu.VMEM)] * (2 * len(pairs)),
        out_shape=[struct((rows, lanes), LOW)] * many,
        scratch_shapes=[vmem((many, rows, lanes), F32)],
        compiler_params=pltpu.CompilerParams(vmem_limit_bytes=MEMORY),
    )(place, *(part for pair in pairs for part in pair))


def write_gradients(place, tail, front, depth, width, hidden):
    rows = GROUPS[2]
    height = hidden // DEVICES
    last = front[0].shape[1] - 3 * width - 128

    def kernel(place_ref, *refs):
        tail_refs, refs = refs[: len(tail)], refs[len(tail) :]
        front_refs, refs = refs[: len(front)], refs[len(front) :]
        gwq_ref, gab_ref, gwo_ref, gwi_ref, gbi_ref, gwf_ref, gain_ref, shift_ref = refs
        spot = place_ref[0]

        def total(refs, at, columns):
            found = 0.0
            for ref in refs:
                block = ref[:, pl.ds(at, columns)].astype(F32)
                found = found + jnp.sum(block.reshape(-1, rows, columns), 0)
            return found

        def own(block, size):
            return pltpu.roll(block, block.shape[1] - spot * size, 1)

        def unfolded(block, count):
            return jnp.concatenate([block[step : step + 1] for step in range(count)], 1)

        for layer, refs, at in ((0, front_refs, last), (1, front_refs, 0)):
            gwq_ref[layer] = total(refs, at, 3 * width)
            block = total(refs, at + 3 * width, 128)
            many = width // 128
            for index in range(2):
                line = unfolded(block[index * many : (index + 1) * many], many)
                gab_ref[layer, pl.ds(index, 1)] = own(line, rows)[:, 0:rows]
        for layer, refs, at in ((0, front_refs, 3 * width + 128), (1, tail_refs, 0)):
            gwo_ref[layer] = total(refs, at, width)
            gwi_ref[layer] = total(refs, at + width, hidden)
            for step in range(hidden // width):
                gwf_ref[layer, pl.ds(step * rows, rows)] = total(
                    refs, at + width + hidden + step * width, width
                )
            at += width + 2 * hidden
            small = own(total(refs, at, width), rows)
            gain_ref[layer] = small[2:4, 0:rows]
            shift_ref[layer] = small[4:8, 0:rows]
            line = unfolded(total(refs, at + width, hidden // 8), 8)
            gbi_ref[pl.ds(layer, 1)] = own(line, height)[:, 0:height]

    outs = [
        struct((depth, rows, 3 * width), F32),
        struct((depth, 2, rows), F32),
        struct((depth, rows, width), F32),
        struct((depth, rows, hidden), F32),
        struct((depth, height), F32),
        struct((depth, height, width), F32),
        struct((depth, 2, rows), F32),
        struct((depth, 4, rows), F32),
    ]
    return pl.pallas_call(
        kernel,
        in_specs=[pl.BlockSpec(memory_space=pltpu.SMEM)]
        + [pl.BlockSpec(memory_space=pltpu.VMEM)] * (len(tail) + len(front)),
        out_shape=outs,
        compiler_params=pltpu.CompilerParams(vmem_limit_bytes=MEMORY),
    )(place, *tail, *front)


def exchange(parts, axis):
    return lax.all_to_all(parts, axis, 0, 0, tiled=True)


def swap(part, axis, step):
    size = lax.axis_size(axis)
    return lax.ppermute(part, axis, [(source, source ^ step) for source in range(size)])


def local(
    hidden_in,
    lengths,
    grad_out,
    attn_weight,
    attn_bias,
    out_weight,
    ffn_in,
    ffn_in_bias,
    ffn_out,
    norm_gain,
    shifts,
):
    depth, rows, width = out_weight.shape
    hidden = ffn_in.shape[2]
    first, second = lax.axis_size("dp"), lax.axis_size("fsdp")
    fits = (second, first, rows) == GROUPS
    urgent_size = 3 * width + 128
    if fits:
        early, later = pack_parameters(
            attn_weight, attn_bias, out_weight, ffn_in, ffn_in_bias, ffn_out, norm_gain, shifts
        )
        across = lax.axis_index("dp").astype(jnp.int32).reshape(1)
        place = lax.axis_index("fsdp").astype(jnp.int32).reshape(1)
        partners = range(1, second)
        early = exchange(early, "dp")
        urgent = early[:, :urgent_size]
        urgent = [urgent] + [swap(urgent, "fsdp", step) for step in partners]
        raw0 = hold(early[:, urgent_size:], tuple(urgent))
        raw0 = [raw0] + [swap(raw0, "fsdp", step) for step in partners]
    else:
        urgent, raw0, raw1 = gather_other(
            attn_weight, attn_bias, out_weight, ffn_in, ffn_in_bias, ffn_out, norm_gain, shifts
        )
        urgent, raw0, raw1 = ([part[step] for step in range(4)] for part in (urgent, raw0, raw1))
        place = jnp.zeros((1,), jnp.int32)

    x0, dz1 = rotate_kernel(lengths, (hidden_in, grad_out))
    qa0, ka0, va0, ob0, urgent = first_kernel(lengths, x0, place, urgent)
    if fits:
        later = exchange(hold(later, (ob0,)), "dp")
    n1, n2, inv, yb, gb, gp, z0 = dense_kernel(
        0, lengths, x0, ob0, place, urgent, raw0, 3 * width, hidden
    )
    if fits:
        raw1 = hold(later, (z0,))
        raw1 = [raw1] + [swap(raw1, "fsdp", step) for step in partners]
    qa1, ka1, va1, ob1 = attention_kernel(1, lengths, z0, place, urgent, raw0, 0)
    hidden_out, dr1, dob1, *sent_a = turn_kernel(
        1, lengths, z0, ob1, dz1, place, urgent, raw1, 0, hidden
    )
    dr0, dob0, *sent_b = middle_kernel(
        lengths,
        (z0, dob1, ob1, qa1, ka1, va1, dr1),
        (n1, n2, inv, yb, gb, gp, ob0),
        place,
        urgent,
        raw0,
        hidden,
        (sent_a[0],),
    )
    if fits:
        got_a = [sent_a[0]] + [swap(sent_a[step], "fsdp", step) for step in partners]
        (tail,) = add_parts(across, got_a, False, (sent_b[0],))
        tail = exchange(tail, "dp")
    grad_in, *sent_c = last_kernel(
        lengths, (x0, dob0, ob0, qa0, ka0, va0, dr0), urgent, (sent_b[0],), place
    )
    if fits:
        got_b = [sent_b[0]] + [swap(sent_b[step], "fsdp", step) for step in partners]
        got_c = [sent_c[0]] + [swap(sent_c[step], "fsdp", step) for step in partners]
        keep_b, give_b = add_parts(across, got_b, True, (got_c[1], tail))
        keep_c, give_c = add_parts(across, got_c, True)
        pairs = [(keep_b, swap(give_b, "dp", 1)), (keep_c, swap(give_c, "dp", 1))]
        front = add_halves(across, pairs)
        front = [front[0]] + [swap(front[step], "dp", 2 * step) for step in range(1, first // 2)]
        spot = lax.axis_index(("dp", "fsdp")).astype(jnp.int32).reshape(1)
        grads = write_gradients(spot, [tail], front, depth, width, hidden)
    else:
        grads = scatter_other(
            *(jnp.stack(part) for part in (sent_a, sent_b, sent_c)), rows, width, hidden
        )
    return (hidden_out, grad_in, *grads)


def gather_other(
    attn_weight, attn_bias, out_weight, ffn_in, ffn_in_bias, ffn_out, norm_gain, shifts
):
    axes = ("dp", "fsdp")
    gather = lambda part, axis: lax.all_gather(part, axes, axis=axis, tiled=True)
    depth, unused, width = out_weight.shape
    hidden = ffn_in.shape[2]
    outer, inner, rows = GROUPS
    vectors = gather(jnp.concatenate([attn_bias, norm_gain, shifts], 1), 2)
    line = gather(ffn_in_bias, 1)

    def order(natural):
        return (
            natural.reshape(inner, outer, rows, -1).swapaxes(0, 1).reshape(outer, inner * rows, -1)
        )

    def stacked(part):
        part = part.reshape(DEVICES, -1, rows, width)
        return order(part.swapaxes(1, 2).reshape(width, -1))

    small = vectors.reshape(depth, 8, DEVICES, rows).transpose(2, 1, 0, 3).reshape(width, -1)
    line = line.reshape(depth, DEVICES, -1).swapaxes(0, 1)
    line = jnp.pad(line, ((0, 0), (0, 8 - depth), (0, 0))).reshape(width, -1)
    small = jnp.concatenate([small, line], 1)
    small = jnp.pad(small, ((0, 0), (0, 128 - small.shape[1])))
    wq, wo, wi, wf = (gather(part, 1) for part in (attn_weight, out_weight, ffn_in, ffn_out))
    urgent = jnp.concatenate([order(wq[0]), order(small)], 2)
    raw0 = jnp.concatenate([order(wq[1]), order(wo[0]), order(wi[0]), stacked(wf[0])], 2)
    raw1 = jnp.concatenate([order(wo[1]), order(wi[1]), stacked(wf[1])], 2)
    return urgent, raw0, raw1


def scatter_other(sent_a, sent_b, sent_c, own_rows, width, hidden):
    outer, inner, rows = GROUPS
    axes = ("dp", "fsdp")

    def natural(part):
        return part.reshape(outer, inner, rows, -1).swapaxes(0, 1).reshape(width, -1).astype(F32)

    def cut(part, sizes):
        found, at = [], 0
        for size in sizes:
            found.append(part[:, at : at + size])
            at += size
        return found

    dense = [width, hidden, hidden, width, hidden // 8]
    attention = [3 * width, 128]
    wq0, ab0 = cut(natural(sent_c), attention)
    wq1, ab1, wo0, wi0, wf0, small0, bi0 = cut(natural(sent_b), attention + dense)
    wo1, wi1, wf1, small1, bi1 = cut(natural(sent_a), dense)

    def stacked(part):
        part = part.reshape(DEVICES, rows, -1, width).swapaxes(1, 2)
        return part.reshape(hidden, width)

    def spread(parts, axis):
        return lax.psum_scatter(jnp.stack(parts), axes, scatter_dimension=axis, tiled=True)

    return (
        spread([wq0, wq1], 1),
        spread([ab0[:4].reshape(2, width), ab1[:4].reshape(2, width)], 2),
        spread([wo0, wo1], 1),
        spread([wi0, wi1], 1),
        spread([bi0[:8].reshape(-1), bi1[:8].reshape(-1)], 1),
        spread([stacked(wf0), stacked(wf1)], 1),
        spread([small0[2:4], small1[2:4]], 2),
        spread([small0[4:8], small1[4:8]], 2),
    )


def solution(mesh):
    placed = (
        P(("dp", "fsdp"), None),
        P(("dp", "fsdp"), None),
        P(("dp", "fsdp"), None),
        P(None, ("dp", "fsdp"), None),
        P(None, None, ("dp", "fsdp")),
        P(None, ("dp", "fsdp"), None),
        P(None, ("dp", "fsdp"), None),
        P(None, ("dp", "fsdp")),
        P(None, ("dp", "fsdp"), None),
        P(None, None, ("dp", "fsdp")),
        P(None, None, ("dp", "fsdp")),
    )
    return jax.shard_map(
        local,
        mesh=mesh,
        in_specs=placed,
        out_specs=(
            P(("dp", "fsdp"), None),
            P(("dp", "fsdp"), None),
            P(None, ("dp", "fsdp"), None),
            P(None, None, ("dp", "fsdp")),
            P(None, ("dp", "fsdp"), None),
            P(None, ("dp", "fsdp"), None),
            P(None, ("dp", "fsdp")),
            P(None, ("dp", "fsdp"), None),
            P(None, None, ("dp", "fsdp")),
            P(None, None, ("dp", "fsdp")),
        ),
        check_vma=False,
    )
```

```python
from functools import partial

import jax
import jax.numpy as jnp
from jax import lax
from jax.experimental import pallas as pl
from jax.experimental.pallas import tpu as pltpu
from jax.sharding import PartitionSpec as P

HEADS = 4
HD = 64
SEQ = 512
PAIR = 2 * HD
EXTRA = 16
HALF = SEQ // 2
HALVES = (slice(0, HALF), slice(HALF, SEQ))
FAR = -(2.0**100)
FLOOR = -1e20
EPSILON = 1e-12
PIECE = 256
SMALL = 128
GROUPS = (4, 8, 8)
DEVICES = 32
LOW = jnp.bfloat16
F32 = jnp.float32
MEMORY = 2**26


def dot_nn(left, right):
    return lax.dot_general(left, right, (((1,), (0,)), ((), ())), preferred_element_type=F32)


def dot_nt(left, right):
    return lax.dot_general(left, right, (((1,), (1,)), ((), ())), preferred_element_type=F32)


def dot_tn(left, right):
    return lax.dot_general(left, right, (((0,), (0,)), ((), ())), preferred_element_type=F32)


def pieces(total, size=PIECE):
    return [pl.ds(start, size) for start in range(0, total, size)]


def three_parts(values):
    first = values.astype(LOW).astype(F32)
    rest = values - first
    second = rest.astype(LOW).astype(F32)
    return first, second, rest - second


CURVE = (7.97869556e-01, 3.63928094e-02, -8.82195179e-05, -3.66000319e-05, 1.41853144e-06)
BELL = -0.5 / 0.6931471805599453


def gelu_parts(u):
    square = u * u
    curve = CURVE[-1]
    for factor in CURVE[-2::-1]:
        curve = curve * square + factor
    cumulative = 0.5 + 0.5 * jnp.tanh(u * curve)
    slope = cumulative + (u * 0.3989422804014327) * jnp.exp2(square * BELL)
    return u * cumulative, slope


def inverse_of(values):
    guess = pl.reciprocal(values, approx=True)
    return guess * (2.0 - values * guess)


def longest_start(lengths_ref, row):
    begin, found = jnp.int32(0), jnp.int32(0)
    for entry in range(lengths_ref.shape[1]):
        size = lengths_ref[row, entry]
        found = jnp.where(size == HALF, begin, found)
        begin = begin + size
    return found


def segments(lengths_ref, row):
    places = lax.broadcasted_iota(jnp.int32, (1, SEQ), 1) + longest_start(lengths_ref, row)
    places = places & (SEQ - 1)
    bound = jnp.int32(0)
    segment = jnp.zeros((1, SEQ), jnp.int32)
    last = lengths_ref.shape[1] - 1
    for entry in range(last):
        bound = bound + lengths_ref[row, entry]
        segment = segment + (places >= bound).astype(jnp.int32)
    return segment, last


def head_rows(head):
    return slice(head * HD, (head + 1) * HD)


def attention_forward(row, lengths_ref, x, wt_ref, bias_ref, qa_ref, ka_ref, va_ref, ob_ref, lse_ref, s_ref, p_ref):
    width = HEADS * HD
    segment, last = segments(lengths_ref, row)
    pad = (segment == last).astype(F32)
    line = lax.broadcasted_iota(jnp.int32, (EXTRA, SEQ), 0)
    aug_q = jnp.where(line == segment, 1.0, 0.0).astype(LOW)
    seen = (line == segment) & (segment != last)
    aug_k = jnp.where(seen | (line > last), 0.0, FAR).astype(LOW)
    aug_v = jnp.where(line == 0, 1.0, 0.0).astype(LOW)
    rest = jnp.zeros((PAIR - HD - EXTRA, SEQ), LOW)
    for head in range(HEADS):
        qa_ref[head, HD : HD + EXTRA] = aug_q
        ka_ref[head, HD : HD + EXTRA] = aug_k
        va_ref[head, HD : HD + EXTRA] = aug_v
        qa_ref[head, HD + EXTRA : PAIR] = rest
        ka_ref[head, HD + EXTRA : PAIR] = rest
    for block, ref in enumerate((qa_ref, ka_ref, va_ref)):
        lines = slice(block * width, (block + 1) * width)
        bias = bias_ref[lines]
        value = dot_nt(wt_ref[lines], x) + jnp.concatenate([bias] * (SEQ // 128), 1)
        if block == 0:
            value = value * HD**-0.5
        value = value.astype(LOW)
        for head in range(HEADS):
            ref[head, 0:HD] = value[head_rows(head)]
        yield

    def scores(head):
        for half in HALVES:
            s_ref[head % 2, half] = dot_tn(ka_ref[head, :, half], qa_ref[head, :, half])

    def softmax(head):
        tops = []
        for half in HALVES:
            tops.append(jnp.maximum(jnp.max(s_ref[head % 2, half], 0, keepdims=True), FLOOR))
            p_ref[head % 2, half] = jnp.exp(s_ref[head % 2, half] - tops[-1]).astype(LOW)
        return tops

    scores(0)
    yield
    for head in range(HEADS):
        if head + 1 < HEADS:
            scores(head + 1)
            yield
        tops = softmax(head)
        yield
        for half, top in zip(HALVES, tops):
            out = dot_nn(va_ref[head, :, half], p_ref[head % 2, half])
            alone = pad[:, half]
            total = out[HD : HD + 1] + alone
            lse_ref[head : head + 1, half] = jnp.where(alone > 0, 0.0, top + jnp.log(total))
            own = alone * va_ref[head, 0:HD, half].astype(F32)
            ob_ref[head_rows(head), half] = (out[0:HD] * inverse_of(total) + own).astype(LOW)
        yield


def normal(values):
    centred = values - jnp.mean(values, -1, keepdims=True)
    inverse = lax.rsqrt(jnp.mean(centred * centred, -1, keepdims=True) + EPSILON)
    return centred * inverse, inverse


def normal_back(cotangent, unit, inverse, gains):
    scaled = cotangent * gains
    return inverse * (
        scaled
        - jnp.mean(scaled, -1, keepdims=True)
        - unit * jnp.mean(scaled * unit, -1, keepdims=True)
    )


def dense_forward(x_ref, ob_ref, wo_ref, wi_ref, wf_ref, small_ref, bi_ref, n1_ref, n2_ref, inv_ref, yb_ref, gb_ref, gp_ref, z_ref, work_ref, u_ref):
    small = lambda index: small_ref[pl.ds(index, 1)]
    work_ref[...] = dot_tn(ob_ref[...], wo_ref[...])
    yield
    for place in pieces(SEQ):
        unit, inverse = normal(x_ref[place].astype(F32) + work_ref[place] + small(4))
        n1_ref[place] = unit
        inv_ref[place, pl.ds(0, HD)] = jnp.broadcast_to(inverse, (PIECE, HD))
        y = unit * small(2) + small(5)
        yb_ref[place] = y.astype(LOW)
        work_ref[place] = y + small(6)
        yield
    columns = 256
    count = wi_ref.shape[1] // columns

    def into(step):
        u_ref[step % 2] = dot_nn(yb_ref[...], wi_ref[:, pl.ds(step * columns, columns)])

    into(0)
    yield
    for step in range(count):
        if step + 1 < count:
            into(step + 1)
            yield
        lanes = pl.ds(step * columns, columns)
        for place in pieces(SEQ, SMALL):
            g, slope = gelu_parts(u_ref[step % 2, place] + bi_ref[:, lanes])
            gb_ref[place, lanes] = g.astype(LOW)
            gp_ref[place, lanes] = slope.astype(LOW)
            yield
    work_ref[...] += dot_nn(gb_ref[...], wf_ref[...])
    yield
    for place in pieces(SEQ):
        unit, inverse = normal(work_ref[place])
        n2_ref[place] = unit
        inv_ref[place, pl.ds(HD, HD)] = jnp.broadcast_to(inverse, (PIECE, HD))
        z_ref[place] = (unit * small(3) + small(7)).astype(z_ref.dtype)
        yield


def fold(values):
    return jnp.sum(values.reshape(-1, 8, values.shape[-1]), 0)


def dense_backward(dz_ref, n1_ref, n2_ref, inv_ref, yb_ref, gb_ref, gp_ref, ob_ref, wo_ref, wi_ref, wf_ref, small_ref, dr_ref, dob_ref, gwo_ref, gwi_ref, gwf_ref, gsmall_ref, gbi_ref, low_ref, u_ref, du_ref, turned_ref):
    small = lambda index: small_ref[pl.ds(index, 1)]
    for place in pieces(SEQ):
        dz = dz_ref[place].astype(F32)
        unit = n2_ref[place]
        gsmall_ref[3] += fold(dz * unit)
        gsmall_ref[7] += fold(dz)
        dr = normal_back(dz, unit, inv_ref[place, pl.ds(HD, 1)], small(3))
        dr_ref[place] = dr
        df = dr.astype(LOW)
        low_ref[place] = df
        gsmall_ref[6] += fold(df.astype(F32))
        yield
    columns = 256
    count = wi_ref.shape[1] // columns

    def back(step):
        u_ref[step % 2] = dot_nt(low_ref[...], wf_ref[pl.ds(step * columns, columns)])

    back(0)
    turned_ref[0] = low_ref[...].T
    turned_ref[1] = yb_ref[...].T
    yield
    for step in range(count):
        if step + 1 < count:
            back(step + 1)
            yield
        lanes = pl.ds(step * columns, columns)
        gwf_ref[:, lanes] += dot_nn(turned_ref[0], gb_ref[:, lanes])
        yield
        for place in pieces(SEQ, SMALL):
            du = (u_ref[step % 2, place] * gp_ref[place, lanes].astype(F32)).astype(LOW)
            du_ref[place, lanes] = du
            gbi_ref[:, lanes] += fold(du.astype(F32))
        yield
        gwi_ref[:, lanes] += dot_nn(turned_ref[1], du_ref[:, lanes])
        yield
    u_ref[0] = dot_nt(du_ref[...], wi_ref[...])
    yield
    for place in pieces(SEQ):
        dy = dr_ref[place] + u_ref[0, place]
        unit = n1_ref[place]
        gsmall_ref[2] += fold(dy * unit)
        gsmall_ref[5] += fold(dy)
        dr = normal_back(dy, unit, inv_ref[place, pl.ds(0, 1)], small(2))
        dr_ref[place] = dr
        da = dr.astype(LOW)
        low_ref[place] = da
        gsmall_ref[4] += fold(da.astype(F32))
        yield
    gwo_ref[...] += dot_nn(ob_ref[...], low_ref[...])
    dob_ref[...] = dot_nt(wo_ref[...], low_ref[...]).astype(LOW)
    yield


def attention_backward(row, lengths_ref, x, do_ref, ob_ref, qa_ref, ka_ref, va_ref, lse_ref, wt_ref, dr_ref, dx_ref, gwq_ref, gbias_ref, p_ref, ds_ref, s_ref, dqkv_ref):
    width = HEADS * HD
    segment, last = segments(lengths_ref, row)
    pad = (segment == last).astype(F32)

    def scores(head):
        for half in HALVES:
            s_ref[0, head % 2, half] = dot_tn(ka_ref[head, :, half], qa_ref[head, :, half])
            s_ref[1, head % 2, half] = dot_tn(
                va_ref[head, 0:HD, half], do_ref[head_rows(head), half]
            )

    def weigh(head):
        product = do_ref[head_rows(head)].astype(F32) * ob_ref[head_rows(head)].astype(F32)
        centre = jnp.sum(product, 0, keepdims=True)
        for half in HALVES:
            p = jnp.exp(s_ref[0, head % 2, half] - lse_ref[head : head + 1, half])
            p_ref[head % 2, half] = p.astype(LOW)
            ds_ref[head % 2, half] = (p * (s_ref[1, head % 2, half] - centre[:, half])).astype(LOW)

    scores(0)
    yield
    for head in range(HEADS):
        if head + 1 < HEADS:
            scores(head + 1)
            yield
        weigh(head)
        yield
        for half in HALVES:
            ds, do = ds_ref[head % 2, half], do_ref[head_rows(head), half]
            dq = dot_nn(ka_ref[head, 0:HD, half], ds) * HD**-0.5
            dk = dot_nt(qa_ref[head, 0:HD, half], ds)
            dv = dot_nt(do, p_ref[head % 2, half]) + pad[:, half] * do.astype(F32)
            for block, value in enumerate((dq, dk, dv)):
                at = block * width + head * HD
                dqkv_ref[at : at + HD, half] = value.astype(LOW)
        yield
    for index, block in enumerate((0, 2)):
        value = dqkv_ref[block * width : (block + 1) * width].astype(F32)
        parts = [value[:, at : at + 128] for at in range(0, SEQ, 128)]
        gbias_ref[index] += (parts[0] + parts[1]) + (parts[2] + parts[3])
    gwq_ref[...] += dot_nn(dqkv_ref[...], x)
    yield
    dx_ref[...] = dr_ref[...] + dot_tn(dqkv_ref[...], wt_ref[...])
    yield


def unpack_matrix(raw_ref, at, into_ref):
    width = into_ref.shape[0]
    for start in range(0, into_ref.shape[1], width):
        block = raw_ref[:, :, pl.ds(at + start, width)].astype(F32)
        block = block.reshape(GROUPS + (width,)).swapaxes(0, 1).reshape(width, width)
        into_ref[:, pl.ds(start, width)] = block.astype(LOW)


def unpack_stacked(raw_ref, at, into_ref):
    width = into_ref.shape[1]
    count = into_ref.shape[0] // width
    blocks = [
        raw_ref[:, :, pl.ds(at + step * width, width)].astype(F32).reshape(GROUPS + (width,))
        for step in range(count)
    ]
    outer, inner, rows = GROUPS
    for place in range(inner):
        part = jnp.stack([jnp.stack([block[f, place] for block in blocks]) for f in range(outer)])
        size = outer * count * rows
        into_ref[pl.ds(place * size, size)] = part.reshape(size, width).astype(LOW)


def counter(shape, axis):
    return lax.broadcasted_iota(jnp.int32, shape, axis)


def split_by(values, size):
    return lax.shift_right_logical(values, size.bit_length() - 1), values & (size - 1)


def sources(rows):
    outer, inner, height = GROUPS
    group, within = split_by(counter((rows, 1), 0), height)
    far, near = split_by(group, inner)
    return near * outer + far, within


def unpack_vectors(raw_ref, at, layer):
    outer, inner, rows = GROUPS
    total = outer * inner * rows
    raw = raw_ref[:, :, pl.ds(at, 128)].reshape(total, 128)
    owner, place = split_by(counter((1, total), 1), rows)
    pick = jnp.where(counter((128, 1), 0) == rows * layer + place, 1.0, 0.0).astype(LOW)
    device, unused = sources(total)
    spread = jnp.where(owner == device, dot_nn(raw, pick), 0.0)
    return jnp.sum(spread.reshape(outer * inner, rows, total), 0)


def unpack_hidden(raw_ref, at, layer, hidden):
    outer, inner, rows = GROUPS
    total = outer * inner * rows
    raw = raw_ref[:, :, pl.ds(at, 128)].reshape(total, 128)
    owner, place = split_by(counter((1, hidden), 1), hidden // (outer * inner))
    pick = jnp.where(counter((128, 1), 0) == 2 * rows + place, 1.0, 0.0).astype(LOW)
    device, within = sources(total)
    device = jnp.where(within == layer, device, -1)
    spread = jnp.where(owner == device, dot_nn(raw, pick), 0.0)
    return jnp.sum(spread, 0, keepdims=True)


def pack_matrix(sum_ref, sent_ref, at, turned=False):
    width = sum_ref.shape[1 if turned else 0]
    outer, inner, rows = GROUPS
    for start in range(0, sum_ref.shape[0 if turned else 1], width):
        near = pl.ds(start, width)
        block = sum_ref[near].T if turned else sum_ref[:, near]
        block = block.reshape(inner, outer, rows, width)
        block = block.swapaxes(0, 1).reshape(outer, inner * rows, width)
        sent_ref[:, :, pl.ds(at + start, width)] = block.astype(LOW)


def pack_stacked(sum_ref, sent_ref, at):
    width = sum_ref.shape[0]
    outer, inner, rows = GROUPS
    count = sum_ref.shape[1] // width
    near = inner // count
    for step in range(count):
        block = sum_ref[:, pl.ds(step * width, width)].T
        block = block.reshape(near, outer, count, rows, width)
        for part in range(count):
            piece = jnp.stack([block[:, f, part] for f in range(outer)])
            piece = piece.reshape(outer, near * rows, width)
            sent_ref[:, pl.ds(step * near * rows, near * rows), pl.ds(at + part * width, width)] = (
                piece.astype(LOW)
            )


def pack_shared(block, sent_ref, at):
    outer, inner, rows = GROUPS
    columns = block.shape[1]
    block = jnp.broadcast_to(block[None], (outer * inner, rows, columns))
    sent_ref[:, :, pl.ds(at, columns)] = block.reshape(outer, inner * rows, columns).astype(LOW)


def folded(line, lanes):
    return [line[:, at : at + lanes] for at in range(0, line.shape[1], lanes)]


def pack_attention(gwq_ref, gbias_ref, sent_ref, at):
    pack_matrix(gwq_ref, sent_ref, at, True)
    width = gwq_ref.shape[1]
    parts = []
    for index in range(2):
        parts += folded(jnp.sum(gbias_ref[index].T, 0, keepdims=True), 128)
    block = jnp.concatenate(parts + [jnp.zeros((8 - len(parts), 128), F32)], 0)
    pack_shared(block, sent_ref, at + 3 * width)


def pack_dense(gwo_ref, gwi_ref, gwf_ref, gsmall_ref, gbi_ref, sent_ref, at):
    width, hidden = gwi_ref.shape
    pack_matrix(gwo_ref, sent_ref, at)
    pack_matrix(gwi_ref, sent_ref, at + width)
    pack_stacked(gwf_ref, sent_ref, at + width + hidden)
    at = at + width + 2 * hidden
    pack_shared(jnp.sum(gsmall_ref[...], 1), sent_ref, at)
    line = jnp.sum(gbi_ref[...], 0, keepdims=True)
    pack_shared(jnp.concatenate(folded(line, hidden // 8), 0), sent_ref, at + width)


def shape_of(array):
    return jax.ShapeDtypeStruct(array.shape, array.dtype)


def by_row(shape, group):
    if len(shape) == 2:
        return pl.BlockSpec((group * SEQ, shape[1]), lambda step: (step, 0))
    return pl.BlockSpec((group,) + tuple(shape[1:]), lambda step: (step,) + (0,) * (len(shape) - 1))


def one_row(ref, member):
    if len(ref.shape) == 2:
        return ref.at[pl.ds(member * SEQ, SEQ)]
    return ref.at[member]


def alternate(runs):
    running = []
    waiting = list(runs)
    while running or waiting:
        if waiting:
            running.append(waiting.pop(0))
        for run in list(running):
            try:
                next(run)
            except StopIteration:
                running.remove(run)


def whole(shape):
    return pl.BlockSpec(tuple(shape), lambda row: (0,) * len(shape))


def run_rows(
    body, lengths, rowwise, fixed, row_outs, sent, shared, private, cost, setup, finish, after=(),
    scalars=(), group=1
):
    count = lengths.shape[0]
    group = group if count % group == 0 else 1
    cuts = [len(scalars), len(rowwise), len(fixed), len(after), len(row_outs), len(sent)]
    cuts += [len(shared)] + [len(private)] * group

    def kernel(lengths_ref, *refs):
        step = pl.program_id(0)
        groups = []
        at = 0
        for cut in cuts:
            groups.append(refs[at : at + cut])
            at += cut
        numbers, rows_in, fixed_in, unused, rows_out, sent_out, work = groups[:7]

        @pl.when(step == 0)
        def _():
            setup(numbers, fixed_in, sent_out, work)

        alternate(
            body(
                step * group + member,
                lengths_ref,
                [one_row(ref, member) for ref in rows_in],
                [one_row(ref, member) for ref in rows_out],
                work,
                groups[7 + member],
            )
            for member in range(group)
        )

        if finish:

            @pl.when(step == count // group - 1)
            def _():
                finish(numbers, work, sent_out)

    return pl.pallas_call(
        kernel,
        grid=(count // group,),
        in_specs=[pl.BlockSpec(memory_space=pltpu.SMEM)] * (1 + len(scalars))
        + [by_row(array.shape, group) for array in rowwise]
        + [whole(array.shape) for array in fixed]
        + [pl.BlockSpec(memory_space=pl.ANY) for array in after],
        out_specs=[by_row(part.shape, group) for part in row_outs]
        + [whole(part.shape) for part in sent],
        out_shape=list(row_outs) + list(sent),
        scratch_shapes=list(shared) + list(private) * group,
        compiler_params=pltpu.CompilerParams(
            dimension_semantics=("arbitrary",), vmem_limit_bytes=MEMORY
        ),
        cost_estimate=pl.CostEstimate(flops=cost, bytes_accessed=8 * 2**20, transcendentals=0),
    )(lengths, *scalars, *rowwise, *fixed, *after)


def struct(shape, dtype):
    return jax.ShapeDtypeStruct(tuple(shape), dtype)


FORWARD_SCRATCH = lambda: [
    pltpu.VMEM((2, SEQ, HALF), F32),
    pltpu.VMEM((2, SEQ, HALF), LOW),
]
BACKWARD_SCRATCH = lambda: [
    pltpu.VMEM((2, SEQ, HALF), LOW),
    pltpu.VMEM((2, SEQ, HALF), LOW),
    pltpu.VMEM((2, 2, SEQ, HALF), F32),
    pltpu.VMEM((3 * HEADS * HD, SEQ), LOW),
]


def attention_outs(rows, width):
    return [
        struct((rows, HEADS, PAIR, SEQ), LOW),
        struct((rows, HEADS, PAIR, SEQ), LOW),
        struct((rows, HEADS, HD + EXTRA, SEQ), LOW),
        struct((rows, width, SEQ), LOW),
        struct((rows, 8, SEQ), F32),
    ]


def dense_outs(tokens, width, hidden):
    return [
        struct((tokens, width), F32),
        struct((tokens, width), F32),
        struct((tokens, PAIR), F32),
        struct((tokens, width), LOW),
        struct((tokens, hidden), LOW),
        struct((tokens, hidden), LOW),
    ]


def vmem(shape, dtype):
    return pltpu.VMEM(tuple(shape), dtype)


def attention_weights(width):
    return [vmem((width, 3 * width), LOW), vmem((3 * width, width), LOW), vmem((3 * width, 128), F32)]


def dense_weights(width, hidden):
    return [
        vmem((width, width), LOW),
        vmem((width, hidden), LOW),
        vmem((hidden, width), LOW),
        vmem((8, width), F32),
        vmem((1, hidden), F32),
    ]


def dense_sums(width, hidden):
    return [
        vmem((width, width), F32),
        vmem((width, hidden), F32),
        vmem((width, hidden), F32),
        vmem((8, 8, width), F32),
        vmem((8, hidden), F32),
    ]


def attention_sums(width):
    return [vmem((3 * width, width), F32), vmem((2, width, 128), F32)]


def dense_work(width, hidden):
    return [
        vmem((SEQ, width), LOW),
        vmem((2, SEQ, width), F32),
        vmem((SEQ, hidden), LOW),
        vmem((2, width, SEQ), LOW),
    ]


def set_attention(layer, urgent_ref, raw_ref, at, wq_ref, wt_ref, bias_ref):
    width = wq_ref.shape[0]
    unpack_matrix(raw_ref, at, wq_ref)
    vectors = unpack_vectors(urgent_ref, 3 * width, layer)
    for block, line in enumerate((vectors[0:1], jnp.zeros((1, width), F32), vectors[1:2])):
        lines = pl.ds(block * width, width)
        wt_ref[lines] = wq_ref[:, lines].astype(F32).T.astype(LOW)
        bias_ref[lines] = jnp.broadcast_to(line, (128, width)).T


def set_dense(layer, urgent_ref, raw_ref, at, wo_ref, wi_ref, wf_ref, small_ref, bi_ref):
    width, hidden = wi_ref.shape
    unpack_matrix(raw_ref, at, wo_ref)
    unpack_matrix(raw_ref, at + width, wi_ref)
    unpack_stacked(raw_ref, at + width + hidden, wf_ref)
    small_ref[...] = unpack_vectors(urgent_ref, 3 * width, layer)
    bi_ref[...] = unpack_hidden(urgent_ref, 3 * width, layer, hidden)


def clear(refs):
    for ref in refs:
        ref[...] = jnp.zeros(ref.shape, ref.dtype)


def assemble(place_ref, part_refs, into_ref):
    for step, ref in enumerate(part_refs):
        into_ref[place_ref[0] ^ step] = ref[...]


def raw_block(parts):
    return vmem((len(parts),) + parts[0].shape, LOW)


def turned_back(lengths_ref, row, values):
    return pltpu.roll(values, longest_start(lengths_ref, row), 0).astype(LOW)


def rotate_kernel(lengths, arrays):
    def body(row, lengths_ref, rowwise, outs, work, own):
        back = (SEQ - longest_start(lengths_ref, row)) & (SEQ - 1)
        for source, target in zip(rowwise, outs):
            target[...] = pltpu.roll(source[...].astype(F32), back, 0).astype(LOW)
            yield

    return run_rows(
        body, lengths, list(arrays), [], [struct(array.shape, LOW) for array in arrays], [], [], [],
        10**6, lambda *refs: None, None,
    )


def first_kernel(lengths, x, place, parts):
    rows, (tokens, width) = lengths.shape[0], x.shape

    def setup(numbers, fixed, sent, work):
        assemble(numbers[0], fixed, sent[0])
        set_attention(0, sent[0], sent[0], 0, *work)

    def body(row, lengths_ref, rowwise, outs, work, own):
        return attention_forward(row, lengths_ref, rowwise[0][...], *work[1:3], *outs, *own)

    return run_rows(
        body, lengths, [x], list(parts), attention_outs(rows, width),
        [struct((len(parts),) + parts[0].shape, LOW)],
        attention_weights(width), FORWARD_SCRATCH(), 4 * 10**9, setup, None, (), [place],
    )


def attention_kernel(layer, lengths, x, place, urgent, parts, at):
    rows, (tokens, width) = lengths.shape[0], x.shape

    def setup(numbers, fixed, sent, work):
        assemble(numbers[0], fixed[1:], work[3])
        set_attention(layer, fixed[0], work[3], at, *work[:3])

    def body(row, lengths_ref, rowwise, outs, work, own):
        return attention_forward(
            row, lengths_ref, rowwise[0][...].astype(LOW), *work[1:3], *outs, *own
        )

    return run_rows(
        body, lengths, [x], [urgent] + list(parts), attention_outs(rows, width), [],
        attention_weights(width) + [raw_block(parts)], FORWARD_SCRATCH(),
        4 * 10**9, setup, None, (), [place],
    )


def dense_kernel(layer, lengths, x, ob, place, urgent, parts, at, hidden):
    tokens, width = x.shape

    def setup(numbers, fixed, sent, work):
        assemble(numbers[0], fixed[1:], work[5])
        set_dense(layer, fixed[0], work[5], at, *work[:5])

    def body(row, lengths_ref, rowwise, outs, work, own):
        return dense_forward(*rowwise, *work[:5], *outs, *own)

    return run_rows(
        body, lengths, [x, ob], [urgent] + list(parts),
        dense_outs(tokens, width, hidden) + [struct((tokens, width), F32)], [],
        dense_weights(width, hidden) + [raw_block(parts)],
        [vmem((SEQ, width), F32), vmem((2, SEQ, width), F32)],
        5 * 10**9, setup, None, (), [place],
    )


def turn_kernel(layer, lengths, x, ob, cotangent, place, urgent, parts, at, hidden):
    tokens, width = x.shape
    columns = width + 2 * hidden + width + hidden // 8

    def setup(numbers, fixed, sent, work):
        assemble(numbers[0], fixed[1:], work[11])
        set_dense(layer, fixed[0], work[11], at, *work[:5])
        clear(work[5:10])

    def body(row, lengths_ref, rowwise, outs, work, own):
        x_ref, ob_ref, dz_ref = rowwise
        z_ref, dr_ref, dob_ref = outs
        weights, sums = work[:5], work[5:10]
        kept, work_ref, back = own[:6], own[6], own[7:]
        yield from dense_forward(x_ref, ob_ref, *weights, *kept, work_ref, work_ref, back[1])
        z_ref[...] = turned_back(lengths_ref, row, work_ref[...])
        yield
        yield from dense_backward(dz_ref, *kept, ob_ref, *weights[:4], dr_ref, dob_ref, *sums, *back)

    def finish(numbers, work, sent):
        pack_dense(*work[5:10], work[10], 0)
        hand_out(numbers[0], work[10], sent)

    kept = [vmem((SEQ,) + part.shape[1:], part.dtype) for part in dense_outs(tokens, width, hidden)]
    return run_rows(
        body, lengths, [x, ob, cotangent], [urgent] + list(parts),
        [struct((tokens, width), LOW), struct((tokens, width), F32), struct((tokens // SEQ, width, SEQ), LOW)],
        [struct((64, columns), LOW)] * 4,
        dense_weights(width, hidden) + dense_sums(width, hidden)
        + [vmem((4, 64, columns), LOW), raw_block(parts)],
        kept + [vmem((SEQ, width), F32)] + dense_work(width, hidden),
        10**10, setup, finish, (), [place], 2,
    )


def hand_out(place_ref, packed_ref, sent):
    for step, ref in enumerate(sent):
        ref[...] = packed_ref[place_ref[0] ^ step]


def middle_kernel(lengths, upper, lower, place, urgent, parts, hidden, after):
    tokens, width = upper[0].shape
    columns = 3 * width + 128 + width + 2 * hidden + width + hidden // 8

    def setup(numbers, fixed, sent, work):
        assemble(numbers[0], fixed[1:], work[16])
        set_attention(1, fixed[0], work[16], 0, *work[:3])
        set_dense(0, fixed[0], work[16], 3 * width, *work[3:8])
        clear(work[8:15])

    def body(row, lengths_ref, rowwise, outs, work, own):
        up, low = rowwise[:8], rowwise[8:]
        dx_ref = own[0]
        yield from attention_backward(
            row, lengths_ref, up[0][...].astype(LOW), *up[1:7], work[1], up[7], dx_ref,
            *work[8:10], *own[5:],
        )
        yield from dense_backward(dx_ref, *low, *work[3:7], *outs, *work[10:15], *own[1:5])

    def finish(numbers, work, sent):
        pack_attention(*work[8:10], work[15], 0)
        pack_dense(*work[10:15], work[15], 3 * width + 128)
        hand_out(numbers[0], work[15], sent)

    return run_rows(
        body, lengths, list(upper) + list(lower), [urgent] + list(parts),
        [struct((tokens, width), F32), struct((tokens // SEQ, width, SEQ), LOW)],
        [struct((64, columns), LOW)] * 4,
        attention_weights(width) + dense_weights(width, hidden)
        + attention_sums(width) + dense_sums(width, hidden)
        + [vmem((4, 64, columns), LOW), raw_block(parts)],
        [vmem((SEQ, width), F32)] + dense_work(width, hidden) + BACKWARD_SCRATCH(),
        15 * 10**9, setup, finish, after, [place],
    )


def last_kernel(lengths, upper, urgent, after, place):
    tokens, width = upper[0].shape

    def setup(numbers, fixed, sent, work):
        set_attention(0, fixed[0], fixed[0], 0, *work[:3])
        clear(work[3:5])

    def body(row, lengths_ref, rowwise, outs, work, own):
        yield from attention_backward(
            row, lengths_ref, rowwise[0][...], *rowwise[1:7], work[1], rowwise[7], own[0],
            *work[3:5], *own[1:],
        )
        outs[0][...] = turned_back(lengths_ref, row, own[0][...])
        yield

    def finish(numbers, work, sent):
        pack_attention(*work[3:5], work[5], 0)
        hand_out(numbers[0], work[5], sent)

    return run_rows(
        body, lengths, list(upper), [urgent], [struct((tokens, width), LOW)],
        [struct((64, 3 * width + 128), LOW)] * 4,
        attention_weights(width) + attention_sums(width) + [vmem((4, 64, 3 * width + 128), LOW)],
        [vmem((SEQ, width), F32)] + BACKWARD_SCRATCH(), 8 * 10**9, setup, finish, after, [place], 2,
    )


def hold(array, after):
    def kernel(*refs):
        pass

    anywhere = pl.BlockSpec(memory_space=pl.ANY)
    return pl.pallas_call(
        kernel,
        in_specs=[anywhere] * (1 + len(after)),
        out_specs=anywhere,
        out_shape=shape_of(array),
        input_output_aliases={0: 0},
    )(array, *after)


def pack_parameters(
    attn_weight, attn_bias, out_weight, ffn_in, ffn_in_bias, ffn_out, norm_gain, shifts
):
    depth, rows, width = out_weight.shape
    copies = GROUPS[1]
    hidden = ffn_in.shape[2]
    dense = width + 2 * hidden
    height = ffn_in_bias.shape[1]

    def kernel(wq_ref, ab_ref, wo_ref, wi_ref, bi_ref, wf_ref, gain_ref, shift_ref, first_ref, rest_ref, small_ref):
        def put(ref, block, at):
            block = jnp.broadcast_to(block.astype(F32)[None], (copies,) + block.shape)
            block = block.reshape(copies * block.shape[1], block.shape[2])
            ref[:, pl.ds(at, block.shape[1])] = block.astype(LOW)

        small_ref[...] = jnp.zeros(small_ref.shape, F32)
        for layer in range(depth):
            lanes = pl.ds(rows * layer, rows)
            small_ref[0:2, lanes] = ab_ref[layer].astype(F32)
            small_ref[2:4, lanes] = gain_ref[layer].astype(F32)
            small_ref[4:8, lanes] = shift_ref[layer].astype(F32)
        small_ref[0:depth, pl.ds(2 * rows, height)] = bi_ref[...].astype(F32)
        put(first_ref, wq_ref[0], 0)
        put(first_ref, small_ref[...], 3 * width)
        put(first_ref, wq_ref[1], 3 * width + 128)
        for layer, ref, at in ((0, first_ref, 6 * width + 128), (1, rest_ref, 0)):
            put(ref, wo_ref[layer], at)
            put(ref, wi_ref[layer], at + width)
            at += width + hidden
            down = wf_ref[layer].astype(F32)
            for step in range(hidden // width):
                put(ref, down[step * rows : (step + 1) * rows], at)
                at += width

    return pl.pallas_call(
        kernel,
        in_specs=[pl.BlockSpec(memory_space=pltpu.VMEM)] * 8,
        out_shape=[
            struct((copies * rows, 6 * width + 128 + dense), LOW),
            struct((copies * rows, dense), LOW),
        ],
        scratch_shapes=[vmem((rows, 128), F32)],
        compiler_params=pltpu.CompilerParams(vmem_limit_bytes=MEMORY),
    )(attn_weight, attn_bias, out_weight, ffn_in, ffn_in_bias, ffn_out, norm_gain, shifts)


def add_parts(place, parts, halves, after=()):
    lanes = parts[0].shape[1]
    count = len(parts)
    many, rows = GROUPS[1:]
    outs = 2 if halves else 1

    def kernel(place_ref, *refs):
        out_refs, sum_ref = refs[count + len(after) : -1], refs[-1]
        bit = place_ref[0] & 1
        for start in range(0, lanes, 128):
            near = pl.ds(start, 128)
            total = refs[0][:, near].astype(F32)
            for ref in refs[1:count]:
                total = total + ref[:, near].astype(F32)
            if halves:
                sum_ref[:, :, near] = total.reshape(many, rows, 128)
            else:
                out_refs[0][:, near] = total.astype(LOW)
        for side, ref in enumerate(out_refs if halves else ()):
            for start in range(0, lanes, 128):
                near = pl.ds(start, 128)
                block = [sum_ref[2 * step + (bit ^ side), :, near] for step in range(many // 2)]
                ref[:, near] = jnp.concatenate(block, 0).astype(LOW)

    return pl.pallas_call(
        kernel,
        in_specs=[pl.BlockSpec(memory_space=pltpu.SMEM)]
        + [pl.BlockSpec(memory_space=pltpu.VMEM)] * count
        + [pl.BlockSpec(memory_space=pl.ANY)] * len(after),
        out_shape=[struct((many * rows // outs, lanes), LOW)] * outs,
        scratch_shapes=[vmem((many, rows, lanes), F32)],
        compiler_params=pltpu.CompilerParams(vmem_limit_bytes=MEMORY),
    )(place, *parts, *after)


def add_halves(place, pairs):
    many, rows = GROUPS[1] // 2, GROUPS[2]
    widths = [pair[0].shape[1] for pair in pairs]
    lanes = sum(widths)

    def kernel(place_ref, *refs):
        out_refs, sum_ref = refs[2 * len(pairs) : -1], refs[-1]
        at = 0
        for index, size in enumerate(widths):
            for start in range(0, size, 128):
                near = pl.ds(start, 128)
                total = refs[2 * index][:, near].astype(F32) + refs[2 * index + 1][:, near].astype(F32)
                sum_ref[:, :, pl.ds(at + start, 128)] = total.reshape(many, rows, 128)
            at += size
        far = lax.shift_right_logical(place_ref[0], 1)
        for step, ref in enumerate(out_refs):
            ref[...] = sum_ref[far ^ step].astype(LOW)

    return pl.pallas_call(
        kernel,
        in_specs=[pl.BlockSpec(memory_space=pltpu.SMEM)]
        + [pl.BlockSpec(memory_space=pltpu.VMEM)] * (2 * len(pairs)),
        out_shape=[struct((rows, lanes), LOW)] * many,
        scratch_shapes=[vmem((many, rows, lanes), F32)],
        compiler_params=pltpu.CompilerParams(vmem_limit_bytes=MEMORY),
    )(place, *(part for pair in pairs for part in pair))


def write_gradients(place, tail, front, depth, width, hidden):
    rows = GROUPS[2]
    height = hidden // DEVICES
    last = front[0].shape[1] - 3 * width - 128

    def kernel(place_ref, *refs):
        tail_refs, refs = refs[: len(tail)], refs[len(tail) :]
        front_refs, refs = refs[: len(front)], refs[len(front) :]
        gwq_ref, gab_ref, gwo_ref, gwi_ref, gbi_ref, gwf_ref, gain_ref, shift_ref = refs
        spot = place_ref[0]

        def total(refs, at, columns):
            found = 0.0
            for ref in refs:
                block = ref[:, pl.ds(at, columns)].astype(F32)
                found = found + jnp.sum(block.reshape(-1, rows, columns), 0)
            return found

        def own(block, size):
            return pltpu.roll(block, block.shape[1] - spot * size, 1)

        def unfolded(block, count):
            return jnp.concatenate([block[step : step + 1] for step in range(count)], 1)

        for layer, refs, at in ((0, front_refs, last), (1, front_refs, 0)):
            gwq_ref[layer] = total(refs, at, 3 * width)
            block = total(refs, at + 3 * width, 128)
            many = width // 128
            for index in range(2):
                line = unfolded(block[index * many : (index + 1) * many], many)
                gab_ref[layer, pl.ds(index, 1)] = own(line, rows)[:, 0:rows]
        for layer, refs, at in ((0, front_refs, 3 * width + 128), (1, tail_refs, 0)):
            gwo_ref[layer] = total(refs, at, width)
            gwi_ref[layer] = total(refs, at + width, hidden)
            for step in range(hidden // width):
                gwf_ref[layer, pl.ds(step * rows, rows)] = total(
                    refs, at + width + hidden + step * width, width
                )
            at += width + 2 * hidden
            small = own(total(refs, at, width), rows)
            gain_ref[layer] = small[2:4, 0:rows]
            shift_ref[layer] = small[4:8, 0:rows]
            line = unfolded(total(refs, at + width, hidden // 8), 8)
            gbi_ref[pl.ds(layer, 1)] = own(line, height)[:, 0:height]

    outs = [
        struct((depth, rows, 3 * width), F32),
        struct((depth, 2, rows), F32),
        struct((depth, rows, width), F32),
        struct((depth, rows, hidden), F32),
        struct((depth, height), F32),
        struct((depth, height, width), F32),
        struct((depth, 2, rows), F32),
        struct((depth, 4, rows), F32),
    ]
    return pl.pallas_call(
        kernel,
        in_specs=[pl.BlockSpec(memory_space=pltpu.SMEM)]
        + [pl.BlockSpec(memory_space=pltpu.VMEM)] * (len(tail) + len(front)),
        out_shape=outs,
        compiler_params=pltpu.CompilerParams(vmem_limit_bytes=MEMORY),
    )(place, *tail, *front)


def exchange(parts, axis):
    return lax.all_to_all(parts, axis, 0, 0, tiled=True)


def swap(part, axis, step):
    size = lax.axis_size(axis)
    return lax.ppermute(part, axis, [(source, source ^ step) for source in range(size)])


def local(
    hidden_in,
    lengths,
    grad_out,
    attn_weight,
    attn_bias,
    out_weight,
    ffn_in,
    ffn_in_bias,
    ffn_out,
    norm_gain,
    shifts,
):
    depth, rows, width = out_weight.shape
    hidden = ffn_in.shape[2]
    first, second = lax.axis_size("dp"), lax.axis_size("fsdp")
    fits = (second, first, rows) == GROUPS
    urgent_size = 3 * width + 128
    if fits:
        early, later = pack_parameters(
            attn_weight, attn_bias, out_weight, ffn_in, ffn_in_bias, ffn_out, norm_gain, shifts
        )
        across = lax.axis_index("dp").astype(jnp.int32).reshape(1)
        place = lax.axis_index("fsdp").astype(jnp.int32).reshape(1)
        partners = range(1, second)
        x0, dz1 = rotate_kernel(lengths, (hidden_in, grad_out))
        early = hold(exchange(early, "dp"), (x0,))
        urgent = early[:, :urgent_size]
        urgent = [urgent] + [swap(urgent, "fsdp", step) for step in partners]
        raw0 = early[:, urgent_size:]
        raw0 = [raw0] + [swap(raw0, "fsdp", step) for step in partners]
    else:
        urgent, raw0, raw1 = gather_other(
            attn_weight, attn_bias, out_weight, ffn_in, ffn_in_bias, ffn_out, norm_gain, shifts
        )
        urgent, raw0, raw1 = ([part[step] for step in range(4)] for part in (urgent, raw0, raw1))
        place = jnp.zeros((1,), jnp.int32)
        x0, dz1 = rotate_kernel(lengths, (hidden_in, grad_out))

    qa0, ka0, va0, ob0, lse0, urgent = first_kernel(lengths, x0, place, urgent)
    if fits:
        later = exchange(hold(later, (ob0,)), "dp")
    n1, n2, inv, yb, gb, gp, z0 = dense_kernel(
        0, lengths, x0, ob0, place, urgent, raw0, 3 * width, hidden
    )
    if fits:
        raw1 = hold(later, (z0,))
        raw1 = [raw1] + [swap(raw1, "fsdp", step) for step in partners]
    qa1, ka1, va1, ob1, lse1 = attention_kernel(1, lengths, z0, place, urgent, raw0, 0)
    hidden_out, dr1, dob1, *sent_a = turn_kernel(
        1, lengths, z0, ob1, dz1, place, urgent, raw1, 0, hidden
    )
    dr0, dob0, *sent_b = middle_kernel(
        lengths,
        (z0, dob1, ob1, qa1, ka1, va1, lse1, dr1),
        (n1, n2, inv, yb, gb, gp, ob0),
        place,
        urgent,
        raw0,
        hidden,
        (sent_a[0],),
    )
    if fits:
        got_a = [sent_a[0]] + [swap(sent_a[step], "fsdp", step) for step in partners]
        (tail,) = add_parts(across, got_a, False, (sent_b[0],))
        tail = exchange(tail, "dp")
    grad_in, *sent_c = last_kernel(
        lengths, (x0, dob0, ob0, qa0, ka0, va0, lse0, dr0), urgent, (sent_b[0],), place
    )
    if fits:
        got_b = [sent_b[0]] + [swap(sent_b[step], "fsdp", step) for step in partners]
        got_c = [sent_c[0]] + [swap(sent_c[step], "fsdp", step) for step in partners]
        keep_b, give_b = add_parts(across, got_b, True, (got_c[1], tail))
        keep_c, give_c = add_parts(across, got_c, True)
        pairs = [(keep_b, swap(give_b, "dp", 1)), (keep_c, swap(give_c, "dp", 1))]
        front = add_halves(across, pairs)
        front = [front[0]] + [swap(front[step], "dp", 2 * step) for step in range(1, first // 2)]
        spot = lax.axis_index(("dp", "fsdp")).astype(jnp.int32).reshape(1)
        grads = write_gradients(spot, [tail], front, depth, width, hidden)
    else:
        grads = scatter_other(
            *(jnp.stack(part) for part in (sent_a, sent_b, sent_c)), rows, width, hidden
        )
    return (hidden_out, grad_in, *grads)


def gather_other(
    attn_weight, attn_bias, out_weight, ffn_in, ffn_in_bias, ffn_out, norm_gain, shifts
):
    axes = ("dp", "fsdp")
    gather = lambda part, axis: lax.all_gather(part, axes, axis=axis, tiled=True)
    depth, unused, width = out_weight.shape
    hidden = ffn_in.shape[2]
    outer, inner, rows = GROUPS
    vectors = gather(jnp.concatenate([attn_bias, norm_gain, shifts], 1), 2)
    line = gather(ffn_in_bias, 1)

    def order(natural):
        return (
            natural.reshape(inner, outer, rows, -1).swapaxes(0, 1).reshape(outer, inner * rows, -1)
        )

    def stacked(part):
        part = part.reshape(DEVICES, -1, rows, width)
        return order(part.swapaxes(1, 2).reshape(width, -1))

    small = vectors.reshape(depth, 8, DEVICES, rows).transpose(2, 1, 0, 3).reshape(width, -1)
    line = line.reshape(depth, DEVICES, -1).swapaxes(0, 1)
    line = jnp.pad(line, ((0, 0), (0, 8 - depth), (0, 0))).reshape(width, -1)
    small = jnp.concatenate([small, line], 1)
    small = jnp.pad(small, ((0, 0), (0, 128 - small.shape[1])))
    wq, wo, wi, wf = (gather(part, 1) for part in (attn_weight, out_weight, ffn_in, ffn_out))
    urgent = jnp.concatenate([order(wq[0]), order(small)], 2)
    raw0 = jnp.concatenate([order(wq[1]), order(wo[0]), order(wi[0]), stacked(wf[0])], 2)
    raw1 = jnp.concatenate([order(wo[1]), order(wi[1]), stacked(wf[1])], 2)
    return urgent, raw0, raw1


def scatter_other(sent_a, sent_b, sent_c, own_rows, width, hidden):
    outer, inner, rows = GROUPS
    axes = ("dp", "fsdp")

    def natural(part):
        return part.reshape(outer, inner, rows, -1).swapaxes(0, 1).reshape(width, -1).astype(F32)

    def cut(part, sizes):
        found, at = [], 0
        for size in sizes:
            found.append(part[:, at : at + size])
            at += size
        return found

    dense = [width, hidden, hidden, width, hidden // 8]
    attention = [3 * width, 128]
    wq0, ab0 = cut(natural(sent_c), attention)
    wq1, ab1, wo0, wi0, wf0, small0, bi0 = cut(natural(sent_b), attention + dense)
    wo1, wi1, wf1, small1, bi1 = cut(natural(sent_a), dense)

    def stacked(part):
        part = part.reshape(DEVICES, rows, -1, width).swapaxes(1, 2)
        return part.reshape(hidden, width)

    def spread(parts, axis):
        return lax.psum_scatter(jnp.stack(parts), axes, scatter_dimension=axis, tiled=True)

    return (
        spread([wq0, wq1], 1),
        spread([ab0[:4].reshape(2, width), ab1[:4].reshape(2, width)], 2),
        spread([wo0, wo1], 1),
        spread([wi0, wi1], 1),
        spread([bi0[:8].reshape(-1), bi1[:8].reshape(-1)], 1),
        spread([stacked(wf0), stacked(wf1)], 1),
        spread([small0[2:4], small1[2:4]], 2),
        spread([small0[4:8], small1[4:8]], 2),
    )


def solution(mesh):
    placed = (
        P(("dp", "fsdp"), None),
        P(("dp", "fsdp"), None),
        P(("dp", "fsdp"), None),
        P(None, ("dp", "fsdp"), None),
        P(None, None, ("dp", "fsdp")),
        P(None, ("dp", "fsdp"), None),
        P(None, ("dp", "fsdp"), None),
        P(None, ("dp", "fsdp")),
        P(None, ("dp", "fsdp"), None),
        P(None, None, ("dp", "fsdp")),
        P(None, None, ("dp", "fsdp")),
    )
    return jax.shard_map(
        local,
        mesh=mesh,
        in_specs=placed,
        out_specs=(
            P(("dp", "fsdp"), None),
            P(("dp", "fsdp"), None),
            P(None, ("dp", "fsdp"), None),
            P(None, None, ("dp", "fsdp")),
            P(None, ("dp", "fsdp"), None),
            P(None, ("dp", "fsdp"), None),
            P(None, ("dp", "fsdp")),
            P(None, ("dp", "fsdp"), None),
            P(None, None, ("dp", "fsdp")),
            P(None, None, ("dp", "fsdp")),
        ),
        check_vma=False,
    )
```

```python
from functools import partial

import jax
import jax.numpy as jnp
from jax import lax
from jax.experimental import pallas as pl
from jax.experimental.pallas import tpu as pltpu
from jax.sharding import PartitionSpec as P

HEADS = 4
HD = 64
SEQ = 512
PAIR = 2 * HD
EXTRA = 16
HALF = SEQ // 2
HALVES = (slice(0, HALF), slice(HALF, SEQ))
FAR = -(2.0**100)
FLOOR = -1e20
EPSILON = 1e-12
PIECE = 256
SMALL = 128
GROUPS = (4, 8, 8)
DEVICES = 32
LOW = jnp.bfloat16
F32 = jnp.float32
MEMORY = 2**26


def dot_nn(left, right):
    return lax.dot_general(left, right, (((1,), (0,)), ((), ())), preferred_element_type=F32)


def dot_nt(left, right):
    return lax.dot_general(left, right, (((1,), (1,)), ((), ())), preferred_element_type=F32)


def dot_tn(left, right):
    return lax.dot_general(left, right, (((0,), (0,)), ((), ())), preferred_element_type=F32)


def pieces(total, size=PIECE):
    return [pl.ds(start, size) for start in range(0, total, size)]


def three_parts(values):
    first = values.astype(LOW).astype(F32)
    rest = values - first
    second = rest.astype(LOW).astype(F32)
    return first, second, rest - second


CURVE = (7.97869556e-01, 3.63928094e-02, -8.82195179e-05, -3.66000319e-05, 1.41853144e-06)
BELL = -0.5 / 0.6931471805599453


def gelu_parts(u):
    square = u * u
    curve = CURVE[-1]
    for factor in CURVE[-2::-1]:
        curve = curve * square + factor
    cumulative = 0.5 + 0.5 * jnp.tanh(u * curve)
    slope = cumulative + (u * 0.3989422804014327) * jnp.exp2(square * BELL)
    return u * cumulative, slope


def inverse_of(values):
    guess = pl.reciprocal(values, approx=True)
    return guess * (2.0 - values * guess)


def longest_start(lengths_ref, row):
    begin, found = jnp.int32(0), jnp.int32(0)
    for entry in range(lengths_ref.shape[1]):
        size = lengths_ref[row, entry]
        found = jnp.where(size == HALF, begin, found)
        begin = begin + size
    return found


def segments(lengths_ref, row):
    places = lax.broadcasted_iota(jnp.int32, (1, SEQ), 1) + longest_start(lengths_ref, row)
    places = places & (SEQ - 1)
    bound = jnp.int32(0)
    segment = jnp.zeros((1, SEQ), jnp.int32)
    last = lengths_ref.shape[1] - 1
    for entry in range(last):
        bound = bound + lengths_ref[row, entry]
        segment = segment + (places >= bound).astype(jnp.int32)
    return segment, last


def head_rows(head):
    return slice(head * HD, (head + 1) * HD)


def attention_forward(row, lengths_ref, x, wt_ref, bias_ref, qa_ref, ka_ref, va_ref, ob_ref, lse_ref, s_ref, p_ref):
    width = HEADS * HD
    segment, last = segments(lengths_ref, row)
    pad = (segment == last).astype(F32)
    line = lax.broadcasted_iota(jnp.int32, (EXTRA, SEQ), 0)
    aug_q = jnp.where(line == segment, 1.0, 0.0).astype(LOW)
    seen = (line == segment) & (segment != last)
    aug_k = jnp.where(seen | (line > last), 0.0, FAR).astype(LOW)
    aug_v = jnp.where(line == 0, 1.0, 0.0).astype(LOW)
    rest = jnp.zeros((PAIR - HD - EXTRA, SEQ), LOW)
    for head in range(HEADS):
        qa_ref[head, HD : HD + EXTRA] = aug_q
        ka_ref[head, HD : HD + EXTRA] = aug_k
        va_ref[head, HD : HD + EXTRA] = aug_v
        qa_ref[head, HD + EXTRA : PAIR] = rest
        ka_ref[head, HD + EXTRA : PAIR] = rest
    for block, ref in enumerate((qa_ref, ka_ref, va_ref)):
        lines = slice(block * width, (block + 1) * width)
        bias = bias_ref[lines]
        value = dot_nt(wt_ref[lines], x) + jnp.concatenate([bias] * (SEQ // 128), 1)
        if block == 0:
            value = value * HD**-0.5
        value = value.astype(LOW)
        for head in range(HEADS):
            ref[head, 0:HD] = value[head_rows(head)]
        yield

    def scores(head):
        for half in HALVES:
            s_ref[head % 2, half] = dot_tn(ka_ref[head, :, half], qa_ref[head, :, half])

    def softmax(head):
        tops = []
        for half in HALVES:
            tops.append(jnp.maximum(jnp.max(s_ref[head % 2, half], 0, keepdims=True), FLOOR))
            p_ref[head % 2, half] = jnp.exp(s_ref[head % 2, half] - tops[-1]).astype(LOW)
        return tops

    scores(0)
    yield
    for head in range(HEADS):
        if head + 1 < HEADS:
            scores(head + 1)
            yield
        tops = softmax(head)
        yield
        for half, top in zip(HALVES, tops):
            out = dot_nn(va_ref[head, :, half], p_ref[head % 2, half])
            alone = pad[:, half]
            total = out[HD : HD + 1] + alone
            lse_ref[head : head + 1, half] = jnp.where(alone > 0, 0.0, top + jnp.log(total))
            own = alone * va_ref[head, 0:HD, half].astype(F32)
            ob_ref[head_rows(head), half] = (out[0:HD] * inverse_of(total) + own).astype(LOW)
        yield


def normal(values):
    centred = values - jnp.mean(values, -1, keepdims=True)
    inverse = lax.rsqrt(jnp.mean(centred * centred, -1, keepdims=True) + EPSILON)
    return centred * inverse, inverse


def normal_back(cotangent, unit, inverse, gains):
    scaled = cotangent * gains
    return inverse * (
        scaled
        - jnp.mean(scaled, -1, keepdims=True)
        - unit * jnp.mean(scaled * unit, -1, keepdims=True)
    )


def dense_forward(x_ref, ob_ref, wo_ref, wi_ref, wf_ref, small_ref, bi_ref, n1_ref, n2_ref, inv_ref, yb_ref, gb_ref, gp_ref, z_ref, work_ref, u_ref):
    small = lambda index: small_ref[pl.ds(index, 1)]
    work_ref[...] = dot_tn(ob_ref[...], wo_ref[...])
    yield
    for place in pieces(SEQ):
        unit, inverse = normal(x_ref[place].astype(F32) + work_ref[place] + small(4))
        n1_ref[place] = unit
        inv_ref[place, pl.ds(0, HD)] = jnp.broadcast_to(inverse, (PIECE, HD))
        y = unit * small(2) + small(5)
        yb_ref[place] = y.astype(LOW)
        work_ref[place] = y + small(6)
        yield
    columns = 256
    count = wi_ref.shape[1] // columns

    def into(step):
        u_ref[step % 2] = dot_nn(yb_ref[...], wi_ref[:, pl.ds(step * columns, columns)])

    into(0)
    yield
    for step in range(count):
        if step + 1 < count:
            into(step + 1)
            yield
        lanes = pl.ds(step * columns, columns)
        for place in pieces(SEQ, SMALL):
            g, slope = gelu_parts(u_ref[step % 2, place] + bi_ref[:, lanes])
            gb_ref[place, lanes] = g.astype(LOW)
            gp_ref[place, lanes] = slope.astype(LOW)
            yield
    work_ref[...] += dot_nn(gb_ref[...], wf_ref[...])
    yield
    for place in pieces(SEQ):
        unit, inverse = normal(work_ref[place])
        n2_ref[place] = unit
        inv_ref[place, pl.ds(HD, HD)] = jnp.broadcast_to(inverse, (PIECE, HD))
        z_ref[place] = (unit * small(3) + small(7)).astype(z_ref.dtype)
        yield


def fold(values):
    return jnp.sum(values.reshape(-1, 8, values.shape[-1]), 0)


def dense_backward(dz_ref, n1_ref, n2_ref, inv_ref, yb_ref, gb_ref, gp_ref, ob_ref, wo_ref, wi_ref, wf_ref, small_ref, dr_ref, dob_ref, gwo_ref, gwi_ref, gwf_ref, gsmall_ref, gbi_ref, low_ref, u_ref, du_ref, turned_ref):
    small = lambda index: small_ref[pl.ds(index, 1)]
    for place in pieces(SEQ):
        dz = dz_ref[place].astype(F32)
        unit = n2_ref[place]
        gsmall_ref[3] += fold(dz * unit)
        gsmall_ref[7] += fold(dz)
        dr = normal_back(dz, unit, inv_ref[place, pl.ds(HD, 1)], small(3))
        dr_ref[place] = dr
        df = dr.astype(LOW)
        low_ref[place] = df
        gsmall_ref[6] += fold(df.astype(F32))
        yield
    columns = 256
    count = wi_ref.shape[1] // columns

    def back(step):
        u_ref[step % 2] = dot_nt(low_ref[...], wf_ref[pl.ds(step * columns, columns)])

    back(0)
    turned_ref[0] = low_ref[...].T
    turned_ref[1] = yb_ref[...].T
    yield
    for step in range(count):
        if step + 1 < count:
            back(step + 1)
            yield
        lanes = pl.ds(step * columns, columns)
        gwf_ref[:, lanes] += dot_nn(turned_ref[0], gb_ref[:, lanes])
        yield
        for place in pieces(SEQ, SMALL):
            du = (u_ref[step % 2, place] * gp_ref[place, lanes].astype(F32)).astype(LOW)
            du_ref[place, lanes] = du
            gbi_ref[:, lanes] += fold(du.astype(F32))
        yield
        gwi_ref[:, lanes] += dot_nn(turned_ref[1], du_ref[:, lanes])
        yield
    u_ref[0] = dot_nt(du_ref[...], wi_ref[...])
    yield
    for place in pieces(SEQ):
        dy = dr_ref[place] + u_ref[0, place]
        unit = n1_ref[place]
        gsmall_ref[2] += fold(dy * unit)
        gsmall_ref[5] += fold(dy)
        dr = normal_back(dy, unit, inv_ref[place, pl.ds(0, 1)], small(2))
        dr_ref[place] = dr
        da = dr.astype(LOW)
        low_ref[place] = da
        gsmall_ref[4] += fold(da.astype(F32))
        yield
    gwo_ref[...] += dot_nn(ob_ref[...], low_ref[...])
    dob_ref[...] = dot_nt(wo_ref[...], low_ref[...]).astype(LOW)
    yield


def attention_backward(row, lengths_ref, x, do_ref, ob_ref, qa_ref, ka_ref, va_ref, lse_ref, wt_ref, dr_ref, dx_ref, gwq_ref, gbias_ref, p_ref, ds_ref, s_ref, dqkv_ref):
    width = HEADS * HD
    segment, last = segments(lengths_ref, row)
    pad = (segment == last).astype(F32)

    def scores(head):
        for half in HALVES:
            s_ref[0, head % 2, half] = dot_tn(ka_ref[head, :, half], qa_ref[head, :, half])
            s_ref[1, head % 2, half] = dot_tn(
                va_ref[head, 0:HD, half], do_ref[head_rows(head), half]
            )

    def weigh(head):
        product = do_ref[head_rows(head)].astype(F32) * ob_ref[head_rows(head)].astype(F32)
        centre = jnp.sum(product, 0, keepdims=True)
        for half in HALVES:
            p = jnp.exp(s_ref[0, head % 2, half] - lse_ref[head : head + 1, half])
            p_ref[head % 2, half] = p.astype(LOW)
            ds_ref[head % 2, half] = (p * (s_ref[1, head % 2, half] - centre[:, half])).astype(LOW)

    scores(0)
    yield
    for head in range(HEADS):
        if head + 1 < HEADS:
            scores(head + 1)
            yield
        weigh(head)
        yield
        for half in HALVES:
            ds, do = ds_ref[head % 2, half], do_ref[head_rows(head), half]
            dq = dot_nn(ka_ref[head, 0:HD, half], ds) * HD**-0.5
            dk = dot_nt(qa_ref[head, 0:HD, half], ds)
            dv = dot_nt(do, p_ref[head % 2, half]) + pad[:, half] * do.astype(F32)
            for block, value in enumerate((dq, dk, dv)):
                at = block * width + head * HD
                dqkv_ref[at : at + HD, half] = value.astype(LOW)
        yield
    for index, block in enumerate((0, 2)):
        value = dqkv_ref[block * width : (block + 1) * width].astype(F32)
        parts = [value[:, at : at + 128] for at in range(0, SEQ, 128)]
        gbias_ref[index] += (parts[0] + parts[1]) + (parts[2] + parts[3])
    gwq_ref[...] += dot_nn(dqkv_ref[...], x)
    yield
    dx_ref[...] = dr_ref[...] + dot_tn(dqkv_ref[...], wt_ref[...])
    yield


def unpack_matrix(raw_ref, at, into_ref):
    width = into_ref.shape[0]
    for start in range(0, into_ref.shape[1], width):
        block = raw_ref[:, :, pl.ds(at + start, width)].astype(F32)
        block = block.reshape(GROUPS + (width,)).swapaxes(0, 1).reshape(width, width)
        into_ref[:, pl.ds(start, width)] = block.astype(LOW)


def unpack_stacked(raw_ref, at, into_ref):
    width = into_ref.shape[1]
    count = into_ref.shape[0] // width
    blocks = [
        raw_ref[:, :, pl.ds(at + step * width, width)].astype(F32).reshape(GROUPS + (width,))
        for step in range(count)
    ]
    outer, inner, rows = GROUPS
    for place in range(inner):
        part = jnp.stack([jnp.stack([block[f, place] for block in blocks]) for f in range(outer)])
        size = outer * count * rows
        into_ref[pl.ds(place * size, size)] = part.reshape(size, width).astype(LOW)


def counter(shape, axis):
    return lax.broadcasted_iota(jnp.int32, shape, axis)


def split_by(values, size):
    return lax.shift_right_logical(values, size.bit_length() - 1), values & (size - 1)


def sources(rows):
    outer, inner, height = GROUPS
    group, within = split_by(counter((rows, 1), 0), height)
    far, near = split_by(group, inner)
    return near * outer + far, within


def unpack_vectors(raw_ref, at, layer):
    outer, inner, rows = GROUPS
    total = outer * inner * rows
    raw = raw_ref[:, :, pl.ds(at, 128)].reshape(total, 128)
    owner, place = split_by(counter((1, total), 1), rows)
    pick = jnp.where(counter((128, 1), 0) == rows * layer + place, 1.0, 0.0).astype(LOW)
    device, unused = sources(total)
    spread = jnp.where(owner == device, dot_nn(raw, pick), 0.0)
    return jnp.sum(spread.reshape(outer * inner, rows, total), 0)


def unpack_hidden(raw_ref, at, layer, hidden):
    outer, inner, rows = GROUPS
    total = outer * inner * rows
    raw = raw_ref[:, :, pl.ds(at, 128)].reshape(total, 128)
    owner, place = split_by(counter((1, hidden), 1), hidden // (outer * inner))
    pick = jnp.where(counter((128, 1), 0) == 2 * rows + place, 1.0, 0.0).astype(LOW)
    device, within = sources(total)
    device = jnp.where(within == layer, device, -1)
    spread = jnp.where(owner == device, dot_nn(raw, pick), 0.0)
    return jnp.sum(spread, 0, keepdims=True)


def pack_matrix(sum_ref, sent_ref, at, turned=False):
    width = sum_ref.shape[1 if turned else 0]
    outer, inner, rows = GROUPS
    for start in range(0, sum_ref.shape[0 if turned else 1], width):
        near = pl.ds(start, width)
        block = sum_ref[near].T if turned else sum_ref[:, near]
        block = block.reshape(inner, outer, rows, width)
        block = block.swapaxes(0, 1).reshape(outer, inner * rows, width)
        sent_ref[:, :, pl.ds(at + start, width)] = block.astype(LOW)


def pack_stacked(sum_ref, sent_ref, at):
    width = sum_ref.shape[0]
    outer, inner, rows = GROUPS
    count = sum_ref.shape[1] // width
    near = inner // count
    for step in range(count):
        block = sum_ref[:, pl.ds(step * width, width)].T
        block = block.reshape(near, outer, count, rows, width)
        for part in range(count):
            piece = jnp.stack([block[:, f, part] for f in range(outer)])
            piece = piece.reshape(outer, near * rows, width)
            sent_ref[:, pl.ds(step * near * rows, near * rows), pl.ds(at + part * width, width)] = (
                piece.astype(LOW)
            )


def pack_shared(block, sent_ref, at):
    outer, inner, rows = GROUPS
    columns = block.shape[1]
    block = jnp.broadcast_to(block[None], (outer * inner, rows, columns))
    sent_ref[:, :, pl.ds(at, columns)] = block.reshape(outer, inner * rows, columns).astype(LOW)


def folded(line, lanes):
    return [line[:, at : at + lanes] for at in range(0, line.shape[1], lanes)]


def pack_attention(gwq_ref, gbias_ref, sent_ref, at):
    pack_matrix(gwq_ref, sent_ref, at, True)
    width = gwq_ref.shape[1]
    parts = []
    for index in range(2):
        parts += folded(jnp.sum(gbias_ref[index].T, 0, keepdims=True), 128)
    block = jnp.concatenate(parts + [jnp.zeros((8 - len(parts), 128), F32)], 0)
    pack_shared(block, sent_ref, at + 3 * width)


def pack_dense(gwo_ref, gwi_ref, gwf_ref, gsmall_ref, gbi_ref, sent_ref, at):
    width, hidden = gwi_ref.shape
    pack_matrix(gwo_ref, sent_ref, at)
    pack_matrix(gwi_ref, sent_ref, at + width)
    pack_stacked(gwf_ref, sent_ref, at + width + hidden)
    at = at + width + 2 * hidden
    pack_shared(jnp.sum(gsmall_ref[...], 1), sent_ref, at)
    line = jnp.sum(gbi_ref[...], 0, keepdims=True)
    pack_shared(jnp.concatenate(folded(line, hidden // 8), 0), sent_ref, at + width)


def shape_of(array):
    return jax.ShapeDtypeStruct(array.shape, array.dtype)


def by_row(shape, group):
    if len(shape) == 2:
        return pl.BlockSpec((group * SEQ, shape[1]), lambda step: (step, 0))
    return pl.BlockSpec((group,) + tuple(shape[1:]), lambda step: (step,) + (0,) * (len(shape) - 1))


def one_row(ref, member):
    if len(ref.shape) == 2:
        return ref.at[pl.ds(member * SEQ, SEQ)]
    return ref.at[member]


def alternate(runs):
    running = []
    waiting = list(runs)
    while running or waiting:
        if waiting:
            running.append(waiting.pop(0))
        for run in list(running):
            try:
                next(run)
            except StopIteration:
                running.remove(run)


def whole(shape):
    return pl.BlockSpec(tuple(shape), lambda row: (0,) * len(shape))


def run_rows(
    body, lengths, rowwise, fixed, row_outs, sent, shared, private, cost, setup, finish, after=(),
    scalars=(), group=1
):
    count = lengths.shape[0]
    group = group if count % group == 0 else 1
    cuts = [len(scalars), len(rowwise), len(fixed), len(after), len(row_outs), len(sent)]
    cuts += [len(shared)] + [len(private)] * group

    def kernel(lengths_ref, *refs):
        step = pl.program_id(0)
        groups = []
        at = 0
        for cut in cuts:
            groups.append(refs[at : at + cut])
            at += cut
        numbers, rows_in, fixed_in, unused, rows_out, sent_out, work = groups[:7]

        @pl.when(step == 0)
        def _():
            setup(numbers, fixed_in, sent_out, work)

        alternate(
            body(
                step * group + member,
                lengths_ref,
                [one_row(ref, member) for ref in rows_in],
                [one_row(ref, member) for ref in rows_out],
                work,
                groups[7 + member],
            )
            for member in range(group)
        )

        if finish:

            @pl.when(step == count // group - 1)
            def _():
                finish(numbers, work, sent_out)

    return pl.pallas_call(
        kernel,
        grid=(count // group,),
        in_specs=[pl.BlockSpec(memory_space=pltpu.SMEM)] * (1 + len(scalars))
        + [by_row(array.shape, group) for array in rowwise]
        + [whole(array.shape) for array in fixed]
        + [pl.BlockSpec(memory_space=pl.ANY) for array in after],
        out_specs=[by_row(part.shape, group) for part in row_outs]
        + [whole(part.shape) for part in sent],
        out_shape=list(row_outs) + list(sent),
        scratch_shapes=list(shared) + list(private) * group,
        compiler_params=pltpu.CompilerParams(
            dimension_semantics=("arbitrary",), vmem_limit_bytes=MEMORY
        ),
        cost_estimate=pl.CostEstimate(flops=cost, bytes_accessed=8 * 2**20, transcendentals=0),
    )(lengths, *scalars, *rowwise, *fixed, *after)


def struct(shape, dtype):
    return jax.ShapeDtypeStruct(tuple(shape), dtype)


FORWARD_SCRATCH = lambda: [
    pltpu.VMEM((2, SEQ, HALF), F32),
    pltpu.VMEM((2, SEQ, HALF), LOW),
]
BACKWARD_SCRATCH = lambda: [
    pltpu.VMEM((2, SEQ, HALF), LOW),
    pltpu.VMEM((2, SEQ, HALF), LOW),
    pltpu.VMEM((2, 2, SEQ, HALF), F32),
    pltpu.VMEM((3 * HEADS * HD, SEQ), LOW),
]


def attention_outs(rows, width):
    return [
        struct((rows, HEADS, PAIR, SEQ), LOW),
        struct((rows, HEADS, PAIR, SEQ), LOW),
        struct((rows, HEADS, HD + EXTRA, SEQ), LOW),
        struct((rows, width, SEQ), LOW),
        struct((rows, 8, SEQ), F32),
    ]


def dense_outs(tokens, width, hidden):
    return [
        struct((tokens, width), F32),
        struct((tokens, width), F32),
        struct((tokens, PAIR), F32),
        struct((tokens, width), LOW),
        struct((tokens, hidden), LOW),
        struct((tokens, hidden), LOW),
    ]


def vmem(shape, dtype):
    return pltpu.VMEM(tuple(shape), dtype)


def attention_weights(width):
    return [vmem((width, 3 * width), LOW), vmem((3 * width, width), LOW), vmem((3 * width, 128), F32)]


def dense_weights(width, hidden):
    return [
        vmem((width, width), LOW),
        vmem((width, hidden), LOW),
        vmem((hidden, width), LOW),
        vmem((8, width), F32),
        vmem((1, hidden), F32),
    ]


def dense_sums(width, hidden):
    return [
        vmem((width, width), F32),
        vmem((width, hidden), F32),
        vmem((width, hidden), F32),
        vmem((8, 8, width), F32),
        vmem((8, hidden), F32),
    ]


def attention_sums(width):
    return [vmem((3 * width, width), F32), vmem((2, width, 128), F32)]


def dense_work(width, hidden):
    return [
        vmem((SEQ, width), LOW),
        vmem((2, SEQ, width), F32),
        vmem((SEQ, hidden), LOW),
        vmem((2, width, SEQ), LOW),
    ]


def set_attention(layer, urgent_ref, raw_ref, at, wq_ref, wt_ref, bias_ref):
    width = wq_ref.shape[0]
    unpack_matrix(raw_ref, at, wq_ref)
    vectors = unpack_vectors(urgent_ref, 3 * width, layer)
    for block, line in enumerate((vectors[0:1], jnp.zeros((1, width), F32), vectors[1:2])):
        lines = pl.ds(block * width, width)
        wt_ref[lines] = wq_ref[:, lines].astype(F32).T.astype(LOW)
        bias_ref[lines] = jnp.broadcast_to(line, (128, width)).T


def set_dense(layer, urgent_ref, raw_ref, at, wo_ref, wi_ref, wf_ref, small_ref, bi_ref):
    width, hidden = wi_ref.shape
    unpack_matrix(raw_ref, at, wo_ref)
    unpack_matrix(raw_ref, at + width, wi_ref)
    unpack_stacked(raw_ref, at + width + hidden, wf_ref)
    small_ref[...] = unpack_vectors(urgent_ref, 3 * width, layer)
    bi_ref[...] = unpack_hidden(urgent_ref, 3 * width, layer, hidden)


def clear(refs):
    for ref in refs:
        ref[...] = jnp.zeros(ref.shape, ref.dtype)


def assemble(place_ref, part_refs, into_ref):
    for step, ref in enumerate(part_refs):
        into_ref[place_ref[0] ^ step] = ref[...]


def raw_block(parts):
    return vmem((len(parts),) + parts[0].shape, LOW)


def turned_back(lengths_ref, row, values):
    return pltpu.roll(values, longest_start(lengths_ref, row), 0).astype(LOW)


def rotate_kernel(lengths, arrays):
    def body(row, lengths_ref, rowwise, outs, work, own):
        back = (SEQ - longest_start(lengths_ref, row)) & (SEQ - 1)
        for source, target in zip(rowwise, outs):
            target[...] = pltpu.roll(source[...].astype(F32), back, 0).astype(LOW)
            yield

    return run_rows(
        body, lengths, list(arrays), [], [struct(array.shape, LOW) for array in arrays], [], [], [],
        10**6, lambda *refs: None, None,
    )


def first_kernel(lengths, x, place, parts):
    rows, (tokens, width) = lengths.shape[0], x.shape

    def setup(numbers, fixed, sent, work):
        assemble(numbers[0], fixed, sent[0])
        set_attention(0, sent[0], sent[0], 0, *work)

    def body(row, lengths_ref, rowwise, outs, work, own):
        return attention_forward(row, lengths_ref, rowwise[0][...], *work[1:3], *outs, *own)

    return run_rows(
        body, lengths, [x], list(parts), attention_outs(rows, width),
        [struct((len(parts),) + parts[0].shape, LOW)],
        attention_weights(width), FORWARD_SCRATCH(), 4 * 10**9, setup, None, (), [place],
    )


def attention_kernel(layer, lengths, x, place, urgent, parts, at):
    rows, (tokens, width) = lengths.shape[0], x.shape

    def setup(numbers, fixed, sent, work):
        assemble(numbers[0], fixed[1:], work[3])
        set_attention(layer, fixed[0], work[3], at, *work[:3])

    def body(row, lengths_ref, rowwise, outs, work, own):
        return attention_forward(
            row, lengths_ref, rowwise[0][...].astype(LOW), *work[1:3], *outs, *own
        )

    return run_rows(
        body, lengths, [x], [urgent] + list(parts), attention_outs(rows, width), [],
        attention_weights(width) + [raw_block(parts)], FORWARD_SCRATCH(),
        4 * 10**9, setup, None, (), [place],
    )


def dense_kernel(layer, lengths, x, ob, place, urgent, parts, at, hidden):
    tokens, width = x.shape

    def setup(numbers, fixed, sent, work):
        assemble(numbers[0], fixed[1:], work[5])
        set_dense(layer, fixed[0], work[5], at, *work[:5])

    def body(row, lengths_ref, rowwise, outs, work, own):
        return dense_forward(*rowwise, *work[:5], *outs, *own)

    return run_rows(
        body, lengths, [x, ob], [urgent] + list(parts),
        dense_outs(tokens, width, hidden) + [struct((tokens, width), F32)], [],
        dense_weights(width, hidden) + [raw_block(parts)],
        [vmem((SEQ, width), F32), vmem((2, SEQ, width), F32)],
        5 * 10**9, setup, None, (), [place],
    )


def turn_kernel(layer, lengths, x, ob, cotangent, place, urgent, parts, at, hidden):
    tokens, width = x.shape
    columns = width + 2 * hidden + width + hidden // 8

    def setup(numbers, fixed, sent, work):
        assemble(numbers[0], fixed[1:], work[11])
        set_dense(layer, fixed[0], work[11], at, *work[:5])
        clear(work[5:10])

    def body(row, lengths_ref, rowwise, outs, work, own):
        x_ref, ob_ref, dz_ref = rowwise
        z_ref, dr_ref, dob_ref = outs
        weights, sums = work[:5], work[5:10]
        kept, work_ref, back = own[:6], own[6], own[7:]
        yield from dense_forward(x_ref, ob_ref, *weights, *kept, work_ref, work_ref, back[1])
        z_ref[...] = turned_back(lengths_ref, row, work_ref[...])
        yield
        yield from dense_backward(dz_ref, *kept, ob_ref, *weights[:4], dr_ref, dob_ref, *sums, *back)

    def finish(numbers, work, sent):
        pack_dense(*work[5:10], work[10], 0)
        hand_out(numbers[0], work[10], sent)

    kept = [vmem((SEQ,) + part.shape[1:], part.dtype) for part in dense_outs(tokens, width, hidden)]
    return run_rows(
        body, lengths, [x, ob, cotangent], [urgent] + list(parts),
        [struct((tokens, width), LOW), struct((tokens, width), F32), struct((tokens // SEQ, width, SEQ), LOW)],
        [struct((64, columns), LOW)] * 4,
        dense_weights(width, hidden) + dense_sums(width, hidden)
        + [vmem((4, 64, columns), LOW), raw_block(parts)],
        kept + [vmem((SEQ, width), F32)] + dense_work(width, hidden),
        10**10, setup, finish, (), [place], 2,
    )


def hand_out(place_ref, packed_ref, sent):
    for step, ref in enumerate(sent):
        ref[...] = packed_ref[place_ref[0] ^ step]


def middle_kernel(lengths, upper, lower, place, urgent, parts, hidden, after):
    tokens, width = upper[0].shape
    columns = 3 * width + 128 + width + 2 * hidden + width + hidden // 8

    def setup(numbers, fixed, sent, work):
        assemble(numbers[0], fixed[1:], work[16])
        set_attention(1, fixed[0], work[16], 0, *work[:3])
        set_dense(0, fixed[0], work[16], 3 * width, *work[3:8])
        clear(work[8:15])

    def body(row, lengths_ref, rowwise, outs, work, own):
        up, low = rowwise[:8], rowwise[8:]
        dx_ref = own[0]
        yield from attention_backward(
            row, lengths_ref, up[0][...].astype(LOW), *up[1:7], work[1], up[7], dx_ref,
            *work[8:10], *own[5:],
        )
        yield from dense_backward(dx_ref, *low, *work[3:7], *outs, *work[10:15], *own[1:5])

    def finish(numbers, work, sent):
        pack_attention(*work[8:10], work[15], 0)
        pack_dense(*work[10:15], work[15], 3 * width + 128)
        hand_out(numbers[0], work[15], sent)

    return run_rows(
        body, lengths, list(upper) + list(lower), [urgent] + list(parts),
        [struct((tokens, width), F32), struct((tokens // SEQ, width, SEQ), LOW)],
        [struct((64, columns), LOW)] * 4,
        attention_weights(width) + dense_weights(width, hidden)
        + attention_sums(width) + dense_sums(width, hidden)
        + [vmem((4, 64, columns), LOW), raw_block(parts)],
        [vmem((SEQ, width), F32)] + dense_work(width, hidden) + BACKWARD_SCRATCH(),
        15 * 10**9, setup, finish, after, [place], 2,
    )


def last_kernel(lengths, upper, urgent, after, place):
    tokens, width = upper[0].shape

    def setup(numbers, fixed, sent, work):
        set_attention(0, fixed[0], fixed[0], 0, *work[:3])
        clear(work[3:5])

    def body(row, lengths_ref, rowwise, outs, work, own):
        yield from attention_backward(
            row, lengths_ref, rowwise[0][...], *rowwise[1:7], work[1], rowwise[7], own[0],
            *work[3:5], *own[1:],
        )
        outs[0][...] = turned_back(lengths_ref, row, own[0][...])
        yield

    def finish(numbers, work, sent):
        pack_attention(*work[3:5], work[5], 0)
        hand_out(numbers[0], work[5], sent)

    return run_rows(
        body, lengths, list(upper), [urgent], [struct((tokens, width), LOW)],
        [struct((64, 3 * width + 128), LOW)] * 4,
        attention_weights(width) + attention_sums(width) + [vmem((4, 64, 3 * width + 128), LOW)],
        [vmem((SEQ, width), F32)] + BACKWARD_SCRATCH(), 8 * 10**9, setup, finish, after, [place], 2,
    )


def hold(array, after):
    def kernel(*refs):
        pass

    anywhere = pl.BlockSpec(memory_space=pl.ANY)
    return pl.pallas_call(
        kernel,
        in_specs=[anywhere] * (1 + len(after)),
        out_specs=anywhere,
        out_shape=shape_of(array),
        input_output_aliases={0: 0},
    )(array, *after)


def pack_parameters(
    attn_weight, attn_bias, out_weight, ffn_in, ffn_in_bias, ffn_out, norm_gain, shifts
):
    depth, rows, width = out_weight.shape
    copies = GROUPS[1]
    hidden = ffn_in.shape[2]
    dense = width + 2 * hidden
    height = ffn_in_bias.shape[1]

    def kernel(wq_ref, ab_ref, wo_ref, wi_ref, bi_ref, wf_ref, gain_ref, shift_ref, first_ref, rest_ref, small_ref):
        def put(ref, block, at):
            block = jnp.broadcast_to(block.astype(F32)[None], (copies,) + block.shape)
            block = block.reshape(copies * block.shape[1], block.shape[2])
            ref[:, pl.ds(at, block.shape[1])] = block.astype(LOW)

        small_ref[...] = jnp.zeros(small_ref.shape, F32)
        for layer in range(depth):
            lanes = pl.ds(rows * layer, rows)
            small_ref[0:2, lanes] = ab_ref[layer].astype(F32)
            small_ref[2:4, lanes] = gain_ref[layer].astype(F32)
            small_ref[4:8, lanes] = shift_ref[layer].astype(F32)
        small_ref[0:depth, pl.ds(2 * rows, height)] = bi_ref[...].astype(F32)
        put(first_ref, wq_ref[0], 0)
        put(first_ref, small_ref[...], 3 * width)
        put(first_ref, wq_ref[1], 3 * width + 128)
        for layer, ref, at in ((0, first_ref, 6 * width + 128), (1, rest_ref, 0)):
            put(ref, wo_ref[layer], at)
            put(ref, wi_ref[layer], at + width)
            at += width + hidden
            down = wf_ref[layer].astype(F32)
            for step in range(hidden // width):
                put(ref, down[step * rows : (step + 1) * rows], at)
                at += width

    return pl.pallas_call(
        kernel,
        in_specs=[pl.BlockSpec(memory_space=pltpu.VMEM)] * 8,
        out_shape=[
            struct((copies * rows, 6 * width + 128 + dense), LOW),
            struct((copies * rows, dense), LOW),
        ],
        scratch_shapes=[vmem((rows, 128), F32)],
        compiler_params=pltpu.CompilerParams(vmem_limit_bytes=MEMORY),
    )(attn_weight, attn_bias, out_weight, ffn_in, ffn_in_bias, ffn_out, norm_gain, shifts)


def add_parts(place, parts, halves, after=()):
    lanes = parts[0].shape[1]
    count = len(parts)
    many, rows = GROUPS[1:]
    outs = 2 if halves else 1

    def kernel(place_ref, *refs):
        out_refs, sum_ref = refs[count + len(after) : -1], refs[-1]
        bit = place_ref[0] & 1
        for start in range(0, lanes, 128):
            near = pl.ds(start, 128)
            total = refs[0][:, near].astype(F32)
            for ref in refs[1:count]:
                total = total + ref[:, near].astype(F32)
            if halves:
                sum_ref[:, :, near] = total.reshape(many, rows, 128)
            else:
                out_refs[0][:, near] = total.astype(LOW)
        for side, ref in enumerate(out_refs if halves else ()):
            for start in range(0, lanes, 128):
                near = pl.ds(start, 128)
                block = [sum_ref[2 * step + (bit ^ side), :, near] for step in range(many // 2)]
                ref[:, near] = jnp.concatenate(block, 0).astype(LOW)

    return pl.pallas_call(
        kernel,
        in_specs=[pl.BlockSpec(memory_space=pltpu.SMEM)]
        + [pl.BlockSpec(memory_space=pltpu.VMEM)] * count
        + [pl.BlockSpec(memory_space=pl.ANY)] * len(after),
        out_shape=[struct((many * rows // outs, lanes), LOW)] * outs,
        scratch_shapes=[vmem((many, rows, lanes), F32)],
        compiler_params=pltpu.CompilerParams(vmem_limit_bytes=MEMORY),
    )(place, *parts, *after)


def add_halves(place, pairs):
    many, rows = GROUPS[1] // 2, GROUPS[2]
    widths = [pair[0].shape[1] for pair in pairs]
    lanes = sum(widths)

    def kernel(place_ref, *refs):
        out_refs, sum_ref = refs[2 * len(pairs) : -1], refs[-1]
        at = 0
        for index, size in enumerate(widths):
            for start in range(0, size, 128):
                near = pl.ds(start, 128)
                total = refs[2 * index][:, near].astype(F32) + refs[2 * index + 1][:, near].astype(F32)
                sum_ref[:, :, pl.ds(at + start, 128)] = total.reshape(many, rows, 128)
            at += size
        far = lax.shift_right_logical(place_ref[0], 1)
        for step, ref in enumerate(out_refs):
            ref[...] = sum_ref[far ^ step].astype(LOW)

    return pl.pallas_call(
        kernel,
        in_specs=[pl.BlockSpec(memory_space=pltpu.SMEM)]
        + [pl.BlockSpec(memory_space=pltpu.VMEM)] * (2 * len(pairs)),
        out_shape=[struct((rows, lanes), LOW)] * many,
        scratch_shapes=[vmem((many, rows, lanes), F32)],
        compiler_params=pltpu.CompilerParams(vmem_limit_bytes=MEMORY),
    )(place, *(part for pair in pairs for part in pair))


def write_gradients(place, tail, front, depth, width, hidden):
    rows = GROUPS[2]
    height = hidden // DEVICES
    last = front[0].shape[1] - 3 * width - 128

    def kernel(place_ref, *refs):
        tail_refs, refs = refs[: len(tail)], refs[len(tail) :]
        front_refs, refs = refs[: len(front)], refs[len(front) :]
        gwq_ref, gab_ref, gwo_ref, gwi_ref, gbi_ref, gwf_ref, gain_ref, shift_ref = refs
        spot = place_ref[0]

        def total(refs, at, columns):
            found = 0.0
            for ref in refs:
                block = ref[:, pl.ds(at, columns)].astype(F32)
                found = found + jnp.sum(block.reshape(-1, rows, columns), 0)
            return found

        def own(block, size):
            return pltpu.roll(block, block.shape[1] - spot * size, 1)

        def unfolded(block, count):
            return jnp.concatenate([block[step : step + 1] for step in range(count)], 1)

        for layer, refs, at in ((0, front_refs, last), (1, front_refs, 0)):
            gwq_ref[layer] = total(refs, at, 3 * width)
            block = total(refs, at + 3 * width, 128)
            many = width // 128
            for index in range(2):
                line = unfolded(block[index * many : (index + 1) * many], many)
                gab_ref[layer, pl.ds(index, 1)] = own(line, rows)[:, 0:rows]
        for layer, refs, at in ((0, front_refs, 3 * width + 128), (1, tail_refs, 0)):
            gwo_ref[layer] = total(refs, at, width)
            gwi_ref[layer] = total(refs, at + width, hidden)
            for step in range(hidden // width):
                gwf_ref[layer, pl.ds(step * rows, rows)] = total(
                    refs, at + width + hidden + step * width, width
                )
            at += width + 2 * hidden
            small = own(total(refs, at, width), rows)
            gain_ref[layer] = small[2:4, 0:rows]
            shift_ref[layer] = small[4:8, 0:rows]
            line = unfolded(total(refs, at + width, hidden // 8), 8)
            gbi_ref[pl.ds(layer, 1)] = own(line, height)[:, 0:height]

    outs = [
        struct((depth, rows, 3 * width), F32),
        struct((depth, 2, rows), F32),
        struct((depth, rows, width), F32),
        struct((depth, rows, hidden), F32),
        struct((depth, height), F32),
        struct((depth, height, width), F32),
        struct((depth, 2, rows), F32),
        struct((depth, 4, rows), F32),
    ]
    return pl.pallas_call(
        kernel,
        in_specs=[pl.BlockSpec(memory_space=pltpu.SMEM)]
        + [pl.BlockSpec(memory_space=pltpu.VMEM)] * (len(tail) + len(front)),
        out_shape=outs,
        compiler_params=pltpu.CompilerParams(vmem_limit_bytes=MEMORY),
    )(place, *tail, *front)


def exchange(parts, axis):
    return lax.all_to_all(parts, axis, 0, 0, tiled=True)


def swap(part, axis, step):
    size = lax.axis_size(axis)
    return lax.ppermute(part, axis, [(source, source ^ step) for source in range(size)])


def local(
    hidden_in,
    lengths,
    grad_out,
    attn_weight,
    attn_bias,
    out_weight,
    ffn_in,
    ffn_in_bias,
    ffn_out,
    norm_gain,
    shifts,
):
    depth, rows, width = out_weight.shape
    hidden = ffn_in.shape[2]
    first, second = lax.axis_size("dp"), lax.axis_size("fsdp")
    fits = (second, first, rows) == GROUPS
    urgent_size = 3 * width + 128
    if fits:
        early, later = pack_parameters(
            attn_weight, attn_bias, out_weight, ffn_in, ffn_in_bias, ffn_out, norm_gain, shifts
        )
        across = lax.axis_index("dp").astype(jnp.int32).reshape(1)
        place = lax.axis_index("fsdp").astype(jnp.int32).reshape(1)
        partners = range(1, second)
        x0, dz1 = rotate_kernel(lengths, (hidden_in, grad_out))
        early = hold(exchange(early, "dp"), (x0,))
        urgent = early[:, :urgent_size]
        urgent = [urgent] + [swap(urgent, "fsdp", step) for step in partners]
        raw0 = early[:, urgent_size:]
        raw0 = [raw0, swap(raw0, "fsdp", 1), swap(raw0, "fsdp", 2)]
    else:
        urgent, raw0, raw1 = gather_other(
            attn_weight, attn_bias, out_weight, ffn_in, ffn_in_bias, ffn_out, norm_gain, shifts
        )
        urgent, raw0, raw1 = ([part[step] for step in range(4)] for part in (urgent, raw0, raw1))
        place = jnp.zeros((1,), jnp.int32)
        x0, dz1 = rotate_kernel(lengths, (hidden_in, grad_out))

    qa0, ka0, va0, ob0, lse0, urgent = first_kernel(lengths, x0, place, urgent)
    if fits:
        raw0[2] = hold(raw0[2], (ob0,))
        raw0.append(swap(raw0[2], "fsdp", 1))
        later = exchange(hold(later, (ob0,)), "dp")
    n1, n2, inv, yb, gb, gp, z0 = dense_kernel(
        0, lengths, x0, ob0, place, urgent, raw0, 3 * width, hidden
    )
    if fits:
        raw1 = hold(later, (z0,))
        raw1 = [raw1, swap(raw1, "fsdp", 1), swap(raw1, "fsdp", 2)]
    qa1, ka1, va1, ob1, lse1 = attention_kernel(1, lengths, z0, place, urgent, raw0, 0)
    if fits:
        raw1[2] = hold(raw1[2], (ob1,))
        raw1.append(swap(raw1[2], "fsdp", 1))
    hidden_out, dr1, dob1, *sent_a = turn_kernel(
        1, lengths, z0, ob1, dz1, place, urgent, raw1, 0, hidden
    )
    dr0, dob0, *sent_b = middle_kernel(
        lengths,
        (z0, dob1, ob1, qa1, ka1, va1, lse1, dr1),
        (n1, n2, inv, yb, gb, gp, ob0),
        place,
        urgent,
        raw0,
        hidden,
        (sent_a[0],),
    )
    if fits:
        got_a = [sent_a[0]] + [swap(sent_a[step], "fsdp", step) for step in partners]
        (tail,) = add_parts(across, got_a, False, (sent_b[0],))
        tail = exchange(tail, "dp")
    grad_in, *sent_c = last_kernel(
        lengths, (x0, dob0, ob0, qa0, ka0, va0, lse0, dr0), urgent, (sent_b[0],), place
    )
    if fits:
        got_b = [sent_b[0]] + [swap(sent_b[step], "fsdp", step) for step in partners]
        got_c = [sent_c[0]] + [swap(sent_c[step], "fsdp", step) for step in partners]
        keep_b, give_b = add_parts(across, got_b, True, (got_c[1], tail))
        keep_c, give_c = add_parts(across, got_c, True)
        pairs = [(keep_b, swap(give_b, "dp", 1)), (keep_c, swap(give_c, "dp", 1))]
        front = add_halves(across, pairs)
        front = [front[0]] + [swap(front[step], "dp", 2 * step) for step in range(1, first // 2)]
        spot = lax.axis_index(("dp", "fsdp")).astype(jnp.int32).reshape(1)
        grads = write_gradients(spot, [tail], front, depth, width, hidden)
    else:
        grads = scatter_other(
            *(jnp.stack(part) for part in (sent_a, sent_b, sent_c)), rows, width, hidden
        )
    return (hidden_out, grad_in, *grads)


def gather_other(
    attn_weight, attn_bias, out_weight, ffn_in, ffn_in_bias, ffn_out, norm_gain, shifts
):
    axes = ("dp", "fsdp")
    gather = lambda part, axis: lax.all_gather(part, axes, axis=axis, tiled=True)
    depth, unused, width = out_weight.shape
    hidden = ffn_in.shape[2]
    outer, inner, rows = GROUPS
    vectors = gather(jnp.concatenate([attn_bias, norm_gain, shifts], 1), 2)
    line = gather(ffn_in_bias, 1)

    def order(natural):
        return (
            natural.reshape(inner, outer, rows, -1).swapaxes(0, 1).reshape(outer, inner * rows, -1)
        )

    def stacked(part):
        part = part.reshape(DEVICES, -1, rows, width)
        return order(part.swapaxes(1, 2).reshape(width, -1))

    small = vectors.reshape(depth, 8, DEVICES, rows).transpose(2, 1, 0, 3).reshape(width, -1)
    line = line.reshape(depth, DEVICES, -1).swapaxes(0, 1)
    line = jnp.pad(line, ((0, 0), (0, 8 - depth), (0, 0))).reshape(width, -1)
    small = jnp.concatenate([small, line], 1)
    small = jnp.pad(small, ((0, 0), (0, 128 - small.shape[1])))
    wq, wo, wi, wf = (gather(part, 1) for part in (attn_weight, out_weight, ffn_in, ffn_out))
    urgent = jnp.concatenate([order(wq[0]), order(small)], 2)
    raw0 = jnp.concatenate([order(wq[1]), order(wo[0]), order(wi[0]), stacked(wf[0])], 2)
    raw1 = jnp.concatenate([order(wo[1]), order(wi[1]), stacked(wf[1])], 2)
    return urgent, raw0, raw1


def scatter_other(sent_a, sent_b, sent_c, own_rows, width, hidden):
    outer, inner, rows = GROUPS
    axes = ("dp", "fsdp")

    def natural(part):
        return part.reshape(outer, inner, rows, -1).swapaxes(0, 1).reshape(width, -1).astype(F32)

    def cut(part, sizes):
        found, at = [], 0
        for size in sizes:
            found.append(part[:, at : at + size])
            at += size
        return found

    dense = [width, hidden, hidden, width, hidden // 8]
    attention = [3 * width, 128]
    wq0, ab0 = cut(natural(sent_c), attention)
    wq1, ab1, wo0, wi0, wf0, small0, bi0 = cut(natural(sent_b), attention + dense)
    wo1, wi1, wf1, small1, bi1 = cut(natural(sent_a), dense)

    def stacked(part):
        part = part.reshape(DEVICES, rows, -1, width).swapaxes(1, 2)
        return part.reshape(hidden, width)

    def spread(parts, axis):
        return lax.psum_scatter(jnp.stack(parts), axes, scatter_dimension=axis, tiled=True)

    return (
        spread([wq0, wq1], 1),
        spread([ab0[:4].reshape(2, width), ab1[:4].reshape(2, width)], 2),
        spread([wo0, wo1], 1),
        spread([wi0, wi1], 1),
        spread([bi0[:8].reshape(-1), bi1[:8].reshape(-1)], 1),
        spread([stacked(wf0), stacked(wf1)], 1),
        spread([small0[2:4], small1[2:4]], 2),
        spread([small0[4:8], small1[4:8]], 2),
    )


def solution(mesh):
    placed = (
        P(("dp", "fsdp"), None),
        P(("dp", "fsdp"), None),
        P(("dp", "fsdp"), None),
        P(None, ("dp", "fsdp"), None),
        P(None, None, ("dp", "fsdp")),
        P(None, ("dp", "fsdp"), None),
        P(None, ("dp", "fsdp"), None),
        P(None, ("dp", "fsdp")),
        P(None, ("dp", "fsdp"), None),
        P(None, None, ("dp", "fsdp")),
        P(None, None, ("dp", "fsdp")),
    )
    return jax.shard_map(
        local,
        mesh=mesh,
        in_specs=placed,
        out_specs=(
            P(("dp", "fsdp"), None),
            P(("dp", "fsdp"), None),
            P(None, ("dp", "fsdp"), None),
            P(None, None, ("dp", "fsdp")),
            P(None, ("dp", "fsdp"), None),
            P(None, ("dp", "fsdp"), None),
            P(None, ("dp", "fsdp")),
            P(None, ("dp", "fsdp"), None),
            P(None, None, ("dp", "fsdp")),
            P(None, None, ("dp", "fsdp")),
        ),
        check_vma=False,
    )
```

```python
from functools import partial

import jax
import jax.numpy as jnp
from jax import lax
from jax.experimental import pallas as pl
from jax.experimental.pallas import tpu as pltpu
from jax.sharding import PartitionSpec as P

HEADS = 4
HD = 64
SEQ = 512
PAIR = 2 * HD
EXTRA = 16
HALF = SEQ // 2
HALVES = (slice(0, HALF), slice(HALF, SEQ))
FAR = -(2.0**100)
FLOOR = -1e20
EPSILON = 1e-12
PIECE = 256
SMALL = 128
GROUPS = (4, 8, 8)
DEVICES = 32
LOW = jnp.bfloat16
F32 = jnp.float32
MEMORY = 2**26


def dot_nn(left, right):
    return lax.dot_general(left, right, (((1,), (0,)), ((), ())), preferred_element_type=F32)


def dot_nt(left, right):
    return lax.dot_general(left, right, (((1,), (1,)), ((), ())), preferred_element_type=F32)


def dot_tn(left, right):
    return lax.dot_general(left, right, (((0,), (0,)), ((), ())), preferred_element_type=F32)


def pieces(total, size=PIECE):
    return [pl.ds(start, size) for start in range(0, total, size)]


def three_parts(values):
    first = values.astype(LOW).astype(F32)
    rest = values - first
    second = rest.astype(LOW).astype(F32)
    return first, second, rest - second


CURVE = (7.97869556e-01, 3.63928094e-02, -8.82195179e-05, -3.66000319e-05, 1.41853144e-06)
BELL = -0.5 / 0.6931471805599453


def gelu_parts(u):
    square = u * u
    curve = CURVE[-1]
    for factor in CURVE[-2::-1]:
        curve = curve * square + factor
    cumulative = 0.5 + 0.5 * jnp.tanh(u * curve)
    slope = cumulative + (u * 0.3989422804014327) * jnp.exp2(square * BELL)
    return u * cumulative, slope


def inverse_of(values):
    guess = pl.reciprocal(values, approx=True)
    return guess * (2.0 - values * guess)


def longest_start(lengths_ref, row):
    begin, found = jnp.int32(0), jnp.int32(0)
    for entry in range(lengths_ref.shape[1]):
        size = lengths_ref[row, entry]
        found = jnp.where(size == HALF, begin, found)
        begin = begin + size
    return found


def segments(lengths_ref, row):
    places = lax.broadcasted_iota(jnp.int32, (1, SEQ), 1) + longest_start(lengths_ref, row)
    places = places & (SEQ - 1)
    bound = jnp.int32(0)
    segment = jnp.zeros((1, SEQ), jnp.int32)
    last = lengths_ref.shape[1] - 1
    for entry in range(last):
        bound = bound + lengths_ref[row, entry]
        segment = segment + (places >= bound).astype(jnp.int32)
    return segment, last


def head_rows(head):
    return slice(head * HD, (head + 1) * HD)


def attention_forward(row, lengths_ref, x, wt_ref, bias_ref, qa_ref, ka_ref, va_ref, ob_ref, lse_ref, s_ref, p_ref):
    width = HEADS * HD
    segment, last = segments(lengths_ref, row)
    pad = (segment == last).astype(F32)
    line = lax.broadcasted_iota(jnp.int32, (EXTRA, SEQ), 0)
    aug_q = jnp.where(line == segment, 1.0, 0.0).astype(LOW)
    seen = (line == segment) & (segment != last)
    aug_k = jnp.where(seen | (line > last), 0.0, FAR).astype(LOW)
    aug_v = jnp.where(line == 0, 1.0, 0.0).astype(LOW)
    rest = jnp.zeros((PAIR - HD - EXTRA, SEQ), LOW)
    for head in range(HEADS):
        qa_ref[head, HD : HD + EXTRA] = aug_q
        ka_ref[head, HD : HD + EXTRA] = aug_k
        va_ref[head, HD : HD + EXTRA] = aug_v
        qa_ref[head, HD + EXTRA : PAIR] = rest
        ka_ref[head, HD + EXTRA : PAIR] = rest
    for block, ref in enumerate((qa_ref, ka_ref, va_ref)):
        lines = slice(block * width, (block + 1) * width)
        bias = bias_ref[lines]
        value = dot_nt(wt_ref[lines], x) + jnp.concatenate([bias] * (SEQ // 128), 1)
        if block == 0:
            value = value * HD**-0.5
        value = value.astype(LOW)
        for head in range(HEADS):
            ref[head, 0:HD] = value[head_rows(head)]
        yield

    def scores(head):
        for half in HALVES:
            s_ref[head % 2, half] = dot_tn(ka_ref[head, :, half], qa_ref[head, :, half])

    def softmax(head):
        tops = []
        for half in HALVES:
            tops.append(jnp.maximum(jnp.max(s_ref[head % 2, half], 0, keepdims=True), FLOOR))
            p_ref[head % 2, half] = jnp.exp(s_ref[head % 2, half] - tops[-1]).astype(LOW)
        return tops

    scores(0)
    yield
    for head in range(HEADS):
        if head + 1 < HEADS:
            scores(head + 1)
            yield
        tops = softmax(head)
        yield
        for half, top in zip(HALVES, tops):
            out = dot_nn(va_ref[head, :, half], p_ref[head % 2, half])
            alone = pad[:, half]
            total = out[HD : HD + 1] + alone
            lse_ref[head : head + 1, half] = jnp.where(alone > 0, 0.0, top + jnp.log(total))
            own = alone * va_ref[head, 0:HD, half].astype(F32)
            ob_ref[head_rows(head), half] = (out[0:HD] * inverse_of(total) + own).astype(LOW)
        yield


def normal(values):
    centred = values - jnp.mean(values, -1, keepdims=True)
    inverse = lax.rsqrt(jnp.mean(centred * centred, -1, keepdims=True) + EPSILON)
    return centred * inverse, inverse


def normal_back(cotangent, unit, inverse, gains):
    scaled = cotangent * gains
    return inverse * (
        scaled
        - jnp.mean(scaled, -1, keepdims=True)
        - unit * jnp.mean(scaled * unit, -1, keepdims=True)
    )


def dense_forward(x_ref, ob_ref, wo_ref, wi_ref, wf_ref, small_ref, bi_ref, n1_ref, n2_ref, inv_ref, yb_ref, gb_ref, gp_ref, z_ref, work_ref, u_ref):
    small = lambda index: small_ref[pl.ds(index, 1)]
    work_ref[...] = dot_tn(ob_ref[...], wo_ref[...])
    yield
    for place in pieces(SEQ):
        unit, inverse = normal(x_ref[place].astype(F32) + work_ref[place] + small(4))
        n1_ref[place] = unit
        inv_ref[place, pl.ds(0, HD)] = jnp.broadcast_to(inverse, (PIECE, HD))
        y = unit * small(2) + small(5)
        yb_ref[place] = y.astype(LOW)
        work_ref[place] = y + small(6)
        yield
    columns = 256
    count = wi_ref.shape[1] // columns

    def into(step):
        u_ref[step % 2] = dot_nn(yb_ref[...], wi_ref[:, pl.ds(step * columns, columns)])

    into(0)
    yield
    for step in range(count):
        if step + 1 < count:
            into(step + 1)
            yield
        lanes = pl.ds(step * columns, columns)
        for place in pieces(SEQ, SMALL):
            g, slope = gelu_parts(u_ref[step % 2, place] + bi_ref[:, lanes])
            gb_ref[place, lanes] = g.astype(LOW)
            gp_ref[place, lanes] = slope.astype(LOW)
            yield
    work_ref[...] += dot_nn(gb_ref[...], wf_ref[...])
    yield
    for place in pieces(SEQ):
        unit, inverse = normal(work_ref[place])
        n2_ref[place] = unit
        inv_ref[place, pl.ds(HD, HD)] = jnp.broadcast_to(inverse, (PIECE, HD))
        z_ref[place] = (unit * small(3) + small(7)).astype(z_ref.dtype)
        yield


def fold(values):
    return jnp.sum(values.reshape(-1, 8, values.shape[-1]), 0)


def dense_backward(dz_ref, n1_ref, n2_ref, inv_ref, yb_ref, gb_ref, gp_ref, ob_ref, wo_ref, wi_ref, wf_ref, small_ref, dr_ref, dob_ref, gwo_ref, gwi_ref, gwf_ref, gsmall_ref, gbi_ref, low_ref, u_ref, du_ref, turned_ref):
    small = lambda index: small_ref[pl.ds(index, 1)]
    for place in pieces(SEQ):
        dz = dz_ref[place].astype(F32)
        unit = n2_ref[place]
        gsmall_ref[3] += fold(dz * unit)
        gsmall_ref[7] += fold(dz)
        dr = normal_back(dz, unit, inv_ref[place, pl.ds(HD, 1)], small(3))
        dr_ref[place] = dr
        df = dr.astype(LOW)
        low_ref[place] = df
        gsmall_ref[6] += fold(df.astype(F32))
        yield
    columns = 256
    count = wi_ref.shape[1] // columns

    def back(step):
        u_ref[step % 2] = dot_nt(low_ref[...], wf_ref[pl.ds(step * columns, columns)])

    back(0)
    turned_ref[0] = low_ref[...].T
    turned_ref[1] = yb_ref[...].T
    yield
    for step in range(count):
        if step + 1 < count:
            back(step + 1)
            yield
        lanes = pl.ds(step * columns, columns)
        gwf_ref[:, lanes] += dot_nn(turned_ref[0], gb_ref[:, lanes])
        yield
        for place in pieces(SEQ, SMALL):
            du = (u_ref[step % 2, place] * gp_ref[place, lanes].astype(F32)).astype(LOW)
            du_ref[place, lanes] = du
            gbi_ref[:, lanes] += fold(du.astype(F32))
        yield
        gwi_ref[:, lanes] += dot_nn(turned_ref[1], du_ref[:, lanes])
        yield
    u_ref[0] = dot_nt(du_ref[...], wi_ref[...])
    yield
    for place in pieces(SEQ):
        dy = dr_ref[place] + u_ref[0, place]
        unit = n1_ref[place]
        gsmall_ref[2] += fold(dy * unit)
        gsmall_ref[5] += fold(dy)
        dr = normal_back(dy, unit, inv_ref[place, pl.ds(0, 1)], small(2))
        dr_ref[place] = dr
        da = dr.astype(LOW)
        low_ref[place] = da
        gsmall_ref[4] += fold(da.astype(F32))
        yield
    gwo_ref[...] += dot_nn(ob_ref[...], low_ref[...])
    dob_ref[...] = dot_nt(wo_ref[...], low_ref[...]).astype(LOW)
    yield


def attention_backward(row, lengths_ref, x, do_ref, ob_ref, qa_ref, ka_ref, va_ref, lse_ref, dqkv_ref, gwq_ref, gbias_ref, p_ref, ds_ref, s_ref):
    width = HEADS * HD
    segment, last = segments(lengths_ref, row)
    pad = (segment == last).astype(F32)

    def scores(head):
        for half in HALVES:
            s_ref[0, head % 2, half] = dot_tn(ka_ref[head, :, half], qa_ref[head, :, half])
            s_ref[1, head % 2, half] = dot_tn(
                va_ref[head, 0:HD, half], do_ref[head_rows(head), half]
            )

    def weigh(head):
        product = do_ref[head_rows(head)].astype(F32) * ob_ref[head_rows(head)].astype(F32)
        centre = jnp.sum(product, 0, keepdims=True)
        for half in HALVES:
            p = jnp.exp(s_ref[0, head % 2, half] - lse_ref[head : head + 1, half])
            p_ref[head % 2, half] = p.astype(LOW)
            ds_ref[head % 2, half] = (p * (s_ref[1, head % 2, half] - centre[:, half])).astype(LOW)

    scores(0)
    yield
    for head in range(HEADS):
        if head + 1 < HEADS:
            scores(head + 1)
            yield
        weigh(head)
        yield
        for half in HALVES:
            ds, do = ds_ref[head % 2, half], do_ref[head_rows(head), half]
            dq = dot_nn(ka_ref[head, 0:HD, half], ds) * HD**-0.5
            dk = dot_nt(qa_ref[head, 0:HD, half], ds)
            dv = dot_nt(do, p_ref[head % 2, half]) + pad[:, half] * do.astype(F32)
            for block, value in enumerate((dq, dk, dv)):
                at = block * width + head * HD
                dqkv_ref[at : at + HD, half] = value.astype(LOW)
        yield
    for index, block in enumerate((0, 2)):
        value = dqkv_ref[block * width : (block + 1) * width].astype(F32)
        parts = [value[:, at : at + 128] for at in range(0, SEQ, 128)]
        gbias_ref[index] += (parts[0] + parts[1]) + (parts[2] + parts[3])
    gwq_ref[...] += dot_nn(dqkv_ref[...], x)
    yield


def unpack_matrix(raw_ref, at, into_ref):
    width = into_ref.shape[0]
    for start in range(0, into_ref.shape[1], width):
        block = raw_ref[:, :, pl.ds(at + start, width)].astype(F32)
        block = block.reshape(GROUPS + (width,)).swapaxes(0, 1).reshape(width, width)
        into_ref[:, pl.ds(start, width)] = block.astype(LOW)


def unpack_stacked(raw_ref, at, into_ref):
    width = into_ref.shape[1]
    count = into_ref.shape[0] // width
    blocks = [
        raw_ref[:, :, pl.ds(at + step * width, width)].astype(F32).reshape(GROUPS + (width,))
        for step in range(count)
    ]
    outer, inner, rows = GROUPS
    for place in range(inner):
        part = jnp.stack([jnp.stack([block[f, place] for block in blocks]) for f in range(outer)])
        size = outer * count * rows
        into_ref[pl.ds(place * size, size)] = part.reshape(size, width).astype(LOW)


def counter(shape, axis):
    return lax.broadcasted_iota(jnp.int32, shape, axis)


def split_by(values, size):
    return lax.shift_right_logical(values, size.bit_length() - 1), values & (size - 1)


def sources(rows):
    outer, inner, height = GROUPS
    group, within = split_by(counter((rows, 1), 0), height)
    far, near = split_by(group, inner)
    return near * outer + far, within


def unpack_vectors(raw_ref, at, layer):
    outer, inner, rows = GROUPS
    total = outer * inner * rows
    raw = raw_ref[:, :, pl.ds(at, 128)].reshape(total, 128)
    owner, place = split_by(counter((1, total), 1), rows)
    pick = jnp.where(counter((128, 1), 0) == rows * layer + place, 1.0, 0.0).astype(LOW)
    device, unused = sources(total)
    spread = jnp.where(owner == device, dot_nn(raw, pick), 0.0)
    return jnp.sum(spread.reshape(outer * inner, rows, total), 0)


def unpack_hidden(raw_ref, at, layer, hidden):
    outer, inner, rows = GROUPS
    total = outer * inner * rows
    raw = raw_ref[:, :, pl.ds(at, 128)].reshape(total, 128)
    owner, place = split_by(counter((1, hidden), 1), hidden // (outer * inner))
    pick = jnp.where(counter((128, 1), 0) == 2 * rows + place, 1.0, 0.0).astype(LOW)
    device, within = sources(total)
    device = jnp.where(within == layer, device, -1)
    spread = jnp.where(owner == device, dot_nn(raw, pick), 0.0)
    return jnp.sum(spread, 0, keepdims=True)


def pack_matrix(sum_ref, sent_ref, at, turned=False):
    width = sum_ref.shape[1 if turned else 0]
    outer, inner, rows = GROUPS
    for start in range(0, sum_ref.shape[0 if turned else 1], width):
        near = pl.ds(start, width)
        block = sum_ref[near].T if turned else sum_ref[:, near]
        block = block.reshape(inner, outer, rows, width)
        block = block.swapaxes(0, 1).reshape(outer, inner * rows, width)
        sent_ref[:, :, pl.ds(at + start, width)] = block.astype(LOW)


def pack_stacked(sum_ref, sent_ref, at):
    width = sum_ref.shape[0]
    outer, inner, rows = GROUPS
    count = sum_ref.shape[1] // width
    near = inner // count
    for step in range(count):
        block = sum_ref[:, pl.ds(step * width, width)].T
        block = block.reshape(near, outer, count, rows, width)
        for part in range(count):
            piece = jnp.stack([block[:, f, part] for f in range(outer)])
            piece = piece.reshape(outer, near * rows, width)
            sent_ref[:, pl.ds(step * near * rows, near * rows), pl.ds(at + part * width, width)] = (
                piece.astype(LOW)
            )


def pack_shared(block, sent_ref, at):
    outer, inner, rows = GROUPS
    columns = block.shape[1]
    block = jnp.broadcast_to(block[None], (outer * inner, rows, columns))
    sent_ref[:, :, pl.ds(at, columns)] = block.reshape(outer, inner * rows, columns).astype(LOW)


def folded(line, lanes):
    return [line[:, at : at + lanes] for at in range(0, line.shape[1], lanes)]


def pack_attention(gwq_ref, gbias_ref, sent_ref, at):
    pack_matrix(gwq_ref, sent_ref, at, True)
    width = gwq_ref.shape[1]
    parts = []
    for index in range(2):
        parts += folded(jnp.sum(gbias_ref[index].T, 0, keepdims=True), 128)
    block = jnp.concatenate(parts + [jnp.zeros((8 - len(parts), 128), F32)], 0)
    pack_shared(block, sent_ref, at + 3 * width)


def pack_dense(gwo_ref, gwi_ref, gwf_ref, gsmall_ref, gbi_ref, sent_ref, at):
    width, hidden = gwi_ref.shape
    pack_matrix(gwo_ref, sent_ref, at)
    pack_matrix(gwi_ref, sent_ref, at + width)
    pack_stacked(gwf_ref, sent_ref, at + width + hidden)
    at = at + width + 2 * hidden
    pack_shared(jnp.sum(gsmall_ref[...], 1), sent_ref, at)
    line = jnp.sum(gbi_ref[...], 0, keepdims=True)
    pack_shared(jnp.concatenate(folded(line, hidden // 8), 0), sent_ref, at + width)


def shape_of(array):
    return jax.ShapeDtypeStruct(array.shape, array.dtype)


def by_row(shape, group):
    if len(shape) == 2:
        return pl.BlockSpec((group * SEQ, shape[1]), lambda step: (step, 0))
    return pl.BlockSpec((group,) + tuple(shape[1:]), lambda step: (step,) + (0,) * (len(shape) - 1))


def one_row(ref, member):
    if len(ref.shape) == 2:
        return ref.at[pl.ds(member * SEQ, SEQ)]
    return ref.at[member]


def alternate(runs):
    running = []
    waiting = list(runs)
    while running or waiting:
        if waiting:
            running.append(waiting.pop(0))
        for run in list(running):
            try:
                next(run)
            except StopIteration:
                running.remove(run)


def whole(shape):
    return pl.BlockSpec(tuple(shape), lambda row: (0,) * len(shape))


def run_rows(
    body, lengths, rowwise, fixed, row_outs, sent, shared, private, cost, setup, finish, after=(),
    scalars=(), group=1
):
    count = lengths.shape[0]
    group = group if count % group == 0 else 1
    cuts = [len(scalars), len(rowwise), len(fixed), len(after), len(row_outs), len(sent)]
    cuts += [len(shared)] + [len(private)] * group

    def kernel(lengths_ref, *refs):
        step = pl.program_id(0)
        groups = []
        at = 0
        for cut in cuts:
            groups.append(refs[at : at + cut])
            at += cut
        numbers, rows_in, fixed_in, unused, rows_out, sent_out, work = groups[:7]

        @pl.when(step == 0)
        def _():
            setup(numbers, fixed_in, sent_out, work)

        alternate(
            body(
                step * group + member,
                lengths_ref,
                [one_row(ref, member) for ref in rows_in],
                [one_row(ref, member) for ref in rows_out],
                work,
                groups[7 + member],
            )
            for member in range(group)
        )

        if finish:

            @pl.when(step == count // group - 1)
            def _():
                finish(numbers, work, sent_out)

    return pl.pallas_call(
        kernel,
        grid=(count // group,),
        in_specs=[pl.BlockSpec(memory_space=pltpu.SMEM)] * (1 + len(scalars))
        + [by_row(array.shape, group) for array in rowwise]
        + [whole(array.shape) for array in fixed]
        + [pl.BlockSpec(memory_space=pl.ANY) for array in after],
        out_specs=[by_row(part.shape, group) for part in row_outs]
        + [whole(part.shape) for part in sent],
        out_shape=list(row_outs) + list(sent),
        scratch_shapes=list(shared) + list(private) * group,
        compiler_params=pltpu.CompilerParams(
            dimension_semantics=("arbitrary",), vmem_limit_bytes=MEMORY
        ),
        cost_estimate=pl.CostEstimate(flops=cost, bytes_accessed=8 * 2**20, transcendentals=0),
    )(lengths, *scalars, *rowwise, *fixed, *after)


def struct(shape, dtype):
    return jax.ShapeDtypeStruct(tuple(shape), dtype)


FORWARD_SCRATCH = lambda: [
    pltpu.VMEM((2, SEQ, HALF), F32),
    pltpu.VMEM((2, SEQ, HALF), LOW),
]
BACKWARD_SCRATCH = lambda: [
    pltpu.VMEM((2, SEQ, HALF), LOW),
    pltpu.VMEM((2, SEQ, HALF), LOW),
    pltpu.VMEM((2, 2, SEQ, HALF), F32),
    pltpu.VMEM((3 * HEADS * HD, SEQ), LOW),
]


def attention_outs(rows, width):
    return [
        struct((rows, HEADS, PAIR, SEQ), LOW),
        struct((rows, HEADS, PAIR, SEQ), LOW),
        struct((rows, HEADS, HD + EXTRA, SEQ), LOW),
        struct((rows, width, SEQ), LOW),
        struct((rows, 8, SEQ), F32),
    ]


def dense_outs(tokens, width, hidden):
    return [
        struct((tokens, width), F32),
        struct((tokens, width), F32),
        struct((tokens, PAIR), F32),
        struct((tokens, width), LOW),
        struct((tokens, hidden), LOW),
        struct((tokens, hidden), LOW),
    ]


def vmem(shape, dtype):
    return pltpu.VMEM(tuple(shape), dtype)


def attention_weights(width):
    return [vmem((width, 3 * width), LOW), vmem((3 * width, width), LOW), vmem((3 * width, 128), F32)]


def dense_weights(width, hidden):
    return [
        vmem((width, width), LOW),
        vmem((width, hidden), LOW),
        vmem((hidden, width), LOW),
        vmem((8, width), F32),
        vmem((1, hidden), F32),
    ]


def dense_sums(width, hidden):
    return [
        vmem((width, width), F32),
        vmem((width, hidden), F32),
        vmem((width, hidden), F32),
        vmem((8, 8, width), F32),
        vmem((8, hidden), F32),
    ]


def attention_sums(width):
    return [vmem((3 * width, width), F32), vmem((2, width, 128), F32)]


def dense_work(width, hidden):
    return [
        vmem((SEQ, width), LOW),
        vmem((2, SEQ, width), F32),
        vmem((SEQ, hidden), LOW),
        vmem((2, width, SEQ), LOW),
    ]


def set_attention(layer, urgent_ref, raw_ref, at, wq_ref, wt_ref, bias_ref):
    width = wq_ref.shape[0]
    unpack_matrix(raw_ref, at, wq_ref)
    vectors = unpack_vectors(urgent_ref, 3 * width, layer)
    for block, line in enumerate((vectors[0:1], jnp.zeros((1, width), F32), vectors[1:2])):
        lines = pl.ds(block * width, width)
        wt_ref[lines] = wq_ref[:, lines].astype(F32).T.astype(LOW)
        bias_ref[lines] = jnp.broadcast_to(line, (128, width)).T


def set_dense(layer, urgent_ref, raw_ref, at, wo_ref, wi_ref, wf_ref, small_ref, bi_ref):
    width, hidden = wi_ref.shape
    unpack_matrix(raw_ref, at, wo_ref)
    unpack_matrix(raw_ref, at + width, wi_ref)
    unpack_stacked(raw_ref, at + width + hidden, wf_ref)
    small_ref[...] = unpack_vectors(urgent_ref, 3 * width, layer)
    bi_ref[...] = unpack_hidden(urgent_ref, 3 * width, layer, hidden)


def clear(refs):
    for ref in refs:
        ref[...] = jnp.zeros(ref.shape, ref.dtype)


def assemble(place_ref, part_refs, into_ref):
    for step, ref in enumerate(part_refs):
        into_ref[place_ref[0] ^ step] = ref[...]


def raw_block(parts):
    return vmem((len(parts),) + parts[0].shape, LOW)


def turned_back(lengths_ref, row, values):
    return pltpu.roll(values, longest_start(lengths_ref, row), 0).astype(LOW)


def rotate_kernel(lengths, arrays):
    def body(row, lengths_ref, rowwise, outs, work, own):
        back = (SEQ - longest_start(lengths_ref, row)) & (SEQ - 1)
        for source, target in zip(rowwise, outs):
            target[...] = pltpu.roll(source[...].astype(F32), back, 0).astype(LOW)
            yield

    return run_rows(
        body, lengths, list(arrays), [], [struct(array.shape, LOW) for array in arrays], [], [], [],
        10**6, lambda *refs: None, None,
    )


def first_kernel(lengths, x, place, parts):
    rows, (tokens, width) = lengths.shape[0], x.shape

    def setup(numbers, fixed, sent, work):
        assemble(numbers[0], fixed, sent[0])
        set_attention(0, sent[0], sent[0], 0, *work)

    def body(row, lengths_ref, rowwise, outs, work, own):
        return attention_forward(row, lengths_ref, rowwise[0][...], *work[1:3], *outs, *own)

    return run_rows(
        body, lengths, [x], list(parts), attention_outs(rows, width),
        [struct((len(parts),) + parts[0].shape, LOW)],
        attention_weights(width), FORWARD_SCRATCH(), 4 * 10**9, setup, None, (), [place],
    )


def attention_kernel(layer, lengths, x, place, urgent, parts, at):
    rows, (tokens, width) = lengths.shape[0], x.shape

    def setup(numbers, fixed, sent, work):
        assemble(numbers[0], fixed[1:], work[3])
        set_attention(layer, fixed[0], work[3], at, *work[:3])

    def body(row, lengths_ref, rowwise, outs, work, own):
        return attention_forward(
            row, lengths_ref, rowwise[0][...].astype(LOW), *work[1:3], *outs, *own
        )

    return run_rows(
        body, lengths, [x], [urgent] + list(parts), attention_outs(rows, width), [],
        attention_weights(width) + [raw_block(parts)], FORWARD_SCRATCH(),
        4 * 10**9, setup, None, (), [place],
    )


def dense_kernel(layer, lengths, x, ob, place, urgent, parts, at, hidden):
    tokens, width = x.shape

    def setup(numbers, fixed, sent, work):
        assemble(numbers[0], fixed[1:], work[5])
        set_dense(layer, fixed[0], work[5], at, *work[:5])

    def body(row, lengths_ref, rowwise, outs, work, own):
        return dense_forward(*rowwise, *work[:5], *outs, *own)

    return run_rows(
        body, lengths, [x, ob], [urgent] + list(parts),
        dense_outs(tokens, width, hidden) + [struct((tokens, width), F32)], [],
        dense_weights(width, hidden) + [raw_block(parts)],
        [vmem((SEQ, width), F32), vmem((2, SEQ, width), F32)],
        5 * 10**9, setup, None, (), [place],
    )


def turn_kernel(layer, lengths, x, ob, cotangent, place, urgent, parts, at, hidden):
    tokens, width = x.shape
    columns = width + 2 * hidden + width + hidden // 8

    def setup(numbers, fixed, sent, work):
        assemble(numbers[0], fixed[1:], work[11])
        set_dense(layer, fixed[0], work[11], at, *work[:5])
        clear(work[5:10])

    def body(row, lengths_ref, rowwise, outs, work, own):
        x_ref, ob_ref, dz_ref = rowwise
        z_ref, dr_ref, dob_ref = outs
        weights, sums = work[:5], work[5:10]
        kept, work_ref, back = own[:6], own[6], own[7:]
        yield from dense_forward(x_ref, ob_ref, *weights, *kept, z_ref, work_ref, back[1])
        yield from dense_backward(dz_ref, *kept, ob_ref, *weights[:4], dr_ref, dob_ref, *sums, *back)

    def finish(numbers, work, sent):
        pack_dense(*work[5:10], work[10], 0)
        hand_out(numbers[0], work[10], sent)

    kept = [vmem((SEQ,) + part.shape[1:], part.dtype) for part in dense_outs(tokens, width, hidden)]
    return run_rows(
        body, lengths, [x, ob, cotangent], [urgent] + list(parts),
        [struct((tokens, width), LOW), struct((tokens, width), F32), struct((tokens // SEQ, width, SEQ), LOW)],
        [struct((64, columns), LOW)] * 4,
        dense_weights(width, hidden) + dense_sums(width, hidden)
        + [vmem((4, 64, columns), LOW), raw_block(parts)],
        kept + [vmem((SEQ, width), F32)] + dense_work(width, hidden),
        10**10, setup, finish, (), [place], 2,
    )


def hand_out(place_ref, packed_ref, sent):
    for step, ref in enumerate(sent):
        ref[...] = packed_ref[place_ref[0] ^ step]


def middle_kernel(lengths, upper, lower, place, urgent, parts, hidden, after):
    tokens, width = upper[0].shape
    columns = 3 * width + 128 + width + 2 * hidden + width + hidden // 8

    def setup(numbers, fixed, sent, work):
        assemble(numbers[0], fixed[1:], work[16])
        set_attention(1, fixed[0], work[16], 0, *work[:3])
        set_dense(0, fixed[0], work[16], 3 * width, *work[3:8])
        clear(work[8:15])

    def body(row, lengths_ref, rowwise, outs, work, own):
        up, low = rowwise[:8], rowwise[8:]
        dx_ref = own[0]
        yield from attention_backward(
            row, lengths_ref, up[0][...].astype(LOW), *up[1:7], own[-1], *work[8:10], *own[5:-1]
        )
        dx_ref[...] = up[7][...] + dot_tn(own[-1][...], work[1][...])
        yield
        yield from dense_backward(dx_ref, *low, *work[3:7], *outs, *work[10:15], *own[1:5])

    def finish(numbers, work, sent):
        pack_attention(*work[8:10], work[15], 0)
        pack_dense(*work[10:15], work[15], 3 * width + 128)
        hand_out(numbers[0], work[15], sent)

    return run_rows(
        body, lengths, list(upper) + list(lower), [urgent] + list(parts),
        [struct((tokens, width), F32), struct((tokens // SEQ, width, SEQ), LOW)],
        [struct((64, columns), LOW)] * 4,
        attention_weights(width) + dense_weights(width, hidden)
        + attention_sums(width) + dense_sums(width, hidden)
        + [vmem((4, 64, columns), LOW), raw_block(parts)],
        [vmem((SEQ, width), F32)] + dense_work(width, hidden) + BACKWARD_SCRATCH(),
        15 * 10**9, setup, finish, after, [place], 2,
    )


def last_kernel(lengths, upper, after, place):
    tokens, width = upper[0].shape

    def setup(numbers, fixed, sent, work):
        clear(work[:2])

    def body(row, lengths_ref, rowwise, outs, work, own):
        return attention_backward(
            row, lengths_ref, rowwise[0][...], *rowwise[1:], outs[0], *work[:2], *own
        )

    def finish(numbers, work, sent):
        pack_attention(*work[:2], work[2], 0)
        hand_out(numbers[0], work[2], sent)

    return run_rows(
        body, lengths, list(upper), [], [struct((tokens // SEQ, 3 * width, SEQ), LOW)],
        [struct((64, 3 * width + 128), LOW)] * 4,
        attention_sums(width) + [vmem((4, 64, 3 * width + 128), LOW)],
        BACKWARD_SCRATCH()[:-1], 8 * 10**9, setup, finish, after, [place], 2,
    )


def tokens_kernel(lengths, z, dqkv, dr, urgent):
    tokens, width = dr.shape

    def setup(numbers, fixed, sent, work):
        set_attention(0, fixed[0], fixed[0], 0, *work)

    def body(row, lengths_ref, rowwise, outs, work, own):
        z_ref, dqkv_ref, dr_ref = rowwise
        outs[0][...] = turned_back(lengths_ref, row, z_ref[...].astype(F32))
        yield
        dx = dr_ref[...] + dot_tn(dqkv_ref[...], work[1][...])
        outs[1][...] = turned_back(lengths_ref, row, dx)
        yield

    return run_rows(
        body, lengths, [z, dqkv, dr], [urgent], [struct((tokens, width), LOW)] * 2, [],
        attention_weights(width), [], 10**9, setup, None,
    )


def hold(array, after):
    def kernel(*refs):
        pass

    anywhere = pl.BlockSpec(memory_space=pl.ANY)
    return pl.pallas_call(
        kernel,
        in_specs=[anywhere] * (1 + len(after)),
        out_specs=anywhere,
        out_shape=shape_of(array),
        input_output_aliases={0: 0},
    )(array, *after)


def pack_parameters(
    attn_weight, attn_bias, out_weight, ffn_in, ffn_in_bias, ffn_out, norm_gain, shifts
):
    depth, rows, width = out_weight.shape
    copies = GROUPS[1]
    hidden = ffn_in.shape[2]
    dense = width + 2 * hidden
    height = ffn_in_bias.shape[1]

    def kernel(wq_ref, ab_ref, wo_ref, wi_ref, bi_ref, wf_ref, gain_ref, shift_ref, first_ref, rest_ref, small_ref):
        def put(ref, block, at):
            block = jnp.broadcast_to(block.astype(F32)[None], (copies,) + block.shape)
            block = block.reshape(copies * block.shape[1], block.shape[2])
            ref[:, pl.ds(at, block.shape[1])] = block.astype(LOW)

        small_ref[...] = jnp.zeros(small_ref.shape, F32)
        for layer in range(depth):
            lanes = pl.ds(rows * layer, rows)
            small_ref[0:2, lanes] = ab_ref[layer].astype(F32)
            small_ref[2:4, lanes] = gain_ref[layer].astype(F32)
            small_ref[4:8, lanes] = shift_ref[layer].astype(F32)
        small_ref[0:depth, pl.ds(2 * rows, height)] = bi_ref[...].astype(F32)
        put(first_ref, wq_ref[0], 0)
        put(first_ref, small_ref[...], 3 * width)
        put(first_ref, wq_ref[1], 3 * width + 128)
        for layer, ref, at in ((0, first_ref, 6 * width + 128), (1, rest_ref, 0)):
            put(ref, wo_ref[layer], at)
            put(ref, wi_ref[layer], at + width)
            at += width + hidden
            down = wf_ref[layer].astype(F32)
            for step in range(hidden // width):
                put(ref, down[step * rows : (step + 1) * rows], at)
                at += width

    return pl.pallas_call(
        kernel,
        in_specs=[pl.BlockSpec(memory_space=pltpu.VMEM)] * 8,
        out_shape=[
            struct((copies * rows, 6 * width + 128 + dense), LOW),
            struct((copies * rows, dense), LOW),
        ],
        scratch_shapes=[vmem((rows, 128), F32)],
        compiler_params=pltpu.CompilerParams(vmem_limit_bytes=MEMORY),
    )(attn_weight, attn_bias, out_weight, ffn_in, ffn_in_bias, ffn_out, norm_gain, shifts)


def add_parts(place, parts, halves, after=()):
    lanes = parts[0].shape[1]
    count = len(parts)
    many, rows = GROUPS[1:]
    outs = 2 if halves else 1

    def kernel(place_ref, *refs):
        out_refs, sum_ref = refs[count + len(after) : -1], refs[-1]
        bit = place_ref[0] & 1
        for start in range(0, lanes, 128):
            near = pl.ds(start, 128)
            total = refs[0][:, near].astype(F32)
            for ref in refs[1:count]:
                total = total + ref[:, near].astype(F32)
            if halves:
                sum_ref[:, :, near] = total.reshape(many, rows, 128)
            else:
                out_refs[0][:, near] = total.astype(LOW)
        for side, ref in enumerate(out_refs if halves else ()):
            for start in range(0, lanes, 128):
                near = pl.ds(start, 128)
                block = [sum_ref[2 * step + (bit ^ side), :, near] for step in range(many // 2)]
                ref[:, near] = jnp.concatenate(block, 0).astype(LOW)

    return pl.pallas_call(
        kernel,
        in_specs=[pl.BlockSpec(memory_space=pltpu.SMEM)]
        + [pl.BlockSpec(memory_space=pltpu.VMEM)] * count
        + [pl.BlockSpec(memory_space=pl.ANY)] * len(after),
        out_shape=[struct((many * rows // outs, lanes), LOW)] * outs,
        scratch_shapes=[vmem((many, rows, lanes), F32)],
        compiler_params=pltpu.CompilerParams(vmem_limit_bytes=MEMORY),
    )(place, *parts, *after)


def add_halves(place, pairs):
    many, rows = GROUPS[1] // 2, GROUPS[2]
    widths = [pair[0].shape[1] for pair in pairs]
    lanes = sum(widths)

    def kernel(place_ref, *refs):
        out_refs, sum_ref = refs[2 * len(pairs) : -1], refs[-1]
        at = 0
        for index, size in enumerate(widths):
            for start in range(0, size, 128):
                near = pl.ds(start, 128)
                total = refs[2 * index][:, near].astype(F32) + refs[2 * index + 1][:, near].astype(F32)
                sum_ref[:, :, pl.ds(at + start, 128)] = total.reshape(many, rows, 128)
            at += size
        far = lax.shift_right_logical(place_ref[0], 1)
        for step, ref in enumerate(out_refs):
            ref[...] = sum_ref[far ^ step].astype(LOW)

    return pl.pallas_call(
        kernel,
        in_specs=[pl.BlockSpec(memory_space=pltpu.SMEM)]
        + [pl.BlockSpec(memory_space=pltpu.VMEM)] * (2 * len(pairs)),
        out_shape=[struct((rows, lanes), LOW)] * many,
        scratch_shapes=[vmem((many, rows, lanes), F32)],
        compiler_params=pltpu.CompilerParams(vmem_limit_bytes=MEMORY),
    )(place, *(part for pair in pairs for part in pair))


def write_gradients(place, most, head, depth, width, hidden, after):
    rows = GROUPS[2]
    height = hidden // DEVICES
    middle = width + 2 * hidden + width + hidden // 8

    def kernel(place_ref, *refs):
        most_refs, refs = refs[: len(most)], refs[len(most) :]
        head_refs, refs = refs[: len(head)], refs[len(head) + len(after) :]
        gwq_ref, gab_ref, gwo_ref, gwi_ref, gbi_ref, gwf_ref, gain_ref, shift_ref = refs
        spot = place_ref[0]

        def total(refs, at, columns):
            found = 0.0
            for ref in refs:
                block = ref[:, pl.ds(at, columns)].astype(F32)
                found = found + jnp.sum(block.reshape(-1, rows, columns), 0)
            return found

        def own(block, size):
            return pltpu.roll(block, block.shape[1] - spot * size, 1)

        def unfolded(block, count):
            return jnp.concatenate([block[step : step + 1] for step in range(count)], 1)

        for layer, refs, at in ((0, head_refs, 0), (1, most_refs, middle)):
            gwq_ref[layer] = total(refs, at, 3 * width)
            block = total(refs, at + 3 * width, 128)
            many = width // 128
            for index in range(2):
                line = unfolded(block[index * many : (index + 1) * many], many)
                gab_ref[layer, pl.ds(index, 1)] = own(line, rows)[:, 0:rows]
        for layer, refs, at in ((0, most_refs, middle + 3 * width + 128), (1, most_refs, 0)):
            gwo_ref[layer] = total(refs, at, width)
            gwi_ref[layer] = total(refs, at + width, hidden)
            for step in range(hidden // width):
                gwf_ref[layer, pl.ds(step * rows, rows)] = total(
                    refs, at + width + hidden + step * width, width
                )
            at += width + 2 * hidden
            small = own(total(refs, at, width), rows)
            gain_ref[layer] = small[2:4, 0:rows]
            shift_ref[layer] = small[4:8, 0:rows]
            line = unfolded(total(refs, at + width, hidden // 8), 8)
            gbi_ref[pl.ds(layer, 1)] = own(line, height)[:, 0:height]

    outs = [
        struct((depth, rows, 3 * width), F32),
        struct((depth, 2, rows), F32),
        struct((depth, rows, width), F32),
        struct((depth, rows, hidden), F32),
        struct((depth, height), F32),
        struct((depth, height, width), F32),
        struct((depth, 2, rows), F32),
        struct((depth, 4, rows), F32),
    ]
    return pl.pallas_call(
        kernel,
        in_specs=[pl.BlockSpec(memory_space=pltpu.SMEM)]
        + [pl.BlockSpec(memory_space=pltpu.VMEM)] * (len(most) + len(head))
        + [pl.BlockSpec(memory_space=pl.ANY)] * len(after),
        out_shape=outs,
        compiler_params=pltpu.CompilerParams(vmem_limit_bytes=MEMORY),
    )(place, *most, *head, *after)


def exchange(parts, axis):
    return lax.all_to_all(parts, axis, 0, 0, tiled=True)


def swap(part, axis, step):
    size = lax.axis_size(axis)
    return lax.ppermute(part, axis, [(source, source ^ step) for source in range(size)])


def local(
    hidden_in,
    lengths,
    grad_out,
    attn_weight,
    attn_bias,
    out_weight,
    ffn_in,
    ffn_in_bias,
    ffn_out,
    norm_gain,
    shifts,
):
    depth, rows, width = out_weight.shape
    hidden = ffn_in.shape[2]
    first, second = lax.axis_size("dp"), lax.axis_size("fsdp")
    fits = (second, first, rows) == GROUPS
    urgent_size = 3 * width + 128
    if fits:
        early, later = pack_parameters(
            attn_weight, attn_bias, out_weight, ffn_in, ffn_in_bias, ffn_out, norm_gain, shifts
        )
        across = lax.axis_index("dp").astype(jnp.int32).reshape(1)
        place = lax.axis_index("fsdp").astype(jnp.int32).reshape(1)
        partners = range(1, second)
        x0, dz1 = rotate_kernel(lengths, (hidden_in, grad_out))
        early = hold(exchange(early, "dp"), (x0,))
        urgent = early[:, :urgent_size]
        urgent = [urgent] + [swap(urgent, "fsdp", step) for step in partners]
        raw0 = early[:, urgent_size:]
        raw0 = [raw0, swap(raw0, "fsdp", 1), swap(raw0, "fsdp", 2)]
    else:
        urgent, raw0, raw1 = gather_other(
            attn_weight, attn_bias, out_weight, ffn_in, ffn_in_bias, ffn_out, norm_gain, shifts
        )
        urgent, raw0, raw1 = ([part[step] for step in range(4)] for part in (urgent, raw0, raw1))
        place = jnp.zeros((1,), jnp.int32)
        x0, dz1 = rotate_kernel(lengths, (hidden_in, grad_out))

    qa0, ka0, va0, ob0, lse0, urgent = first_kernel(lengths, x0, place, urgent)
    if fits:
        raw0[2] = hold(raw0[2], (ob0,))
        raw0.append(swap(raw0[2], "fsdp", 1))
        later = exchange(hold(later, (ob0,)), "dp")
    n1, n2, inv, yb, gb, gp, z0 = dense_kernel(
        0, lengths, x0, ob0, place, urgent, raw0, 3 * width, hidden
    )
    if fits:
        raw1 = hold(later, (z0,))
        raw1 = [raw1, swap(raw1, "fsdp", 1), swap(raw1, "fsdp", 2)]
    qa1, ka1, va1, ob1, lse1 = attention_kernel(1, lengths, z0, place, urgent, raw0, 0)
    if fits:
        raw1[2] = hold(raw1[2], (ob1,))
        raw1.append(swap(raw1[2], "fsdp", 1))
    z1, dr1, dob1, *sent_a = turn_kernel(
        1, lengths, z0, ob1, dz1, place, urgent, raw1, 0, hidden
    )
    dr0, dob0, *sent_b = middle_kernel(
        lengths,
        (z0, dob1, ob1, qa1, ka1, va1, lse1, dr1),
        (n1, n2, inv, yb, gb, gp, ob0),
        place,
        urgent,
        raw0,
        hidden,
        (sent_a[0],),
    )
    if fits:
        got_a = [sent_a[0]] + [swap(sent_a[step], "fsdp", step) for step in partners]
        keep_a, give_a = add_parts(across, got_a, True, (sent_b[0],))
        got_ax = swap(give_a, "dp", 1)
        ready = (sent_b[0], keep_a)
    else:
        ready = ()
    dqkv, *sent_c = last_kernel(
        lengths, (x0, dob0, ob0, qa0, ka0, va0, lse0), ready, place
    )
    hidden_out, grad_in = tokens_kernel(lengths, z1, dqkv, dr0, urgent)
    if fits:
        got_b = [sent_b[0]] + [swap(sent_b[step], "fsdp", step) for step in partners]
        got_c = [sent_c[0]] + [swap(sent_c[step], "fsdp", step) for step in partners]
        keep_b, give_b = add_parts(across, got_b, True, (got_c[1], got_ax))
        got_bx = swap(give_b, "dp", 1)
        keep_c, give_c = add_parts(across, got_c, True)
        got_cx = swap(give_c, "dp", 1)
        most = add_halves(across, [(keep_a, got_ax), (keep_b, got_bx)])
        most = [most[0]] + [swap(most[step], "dp", 2 * step) for step in range(1, first // 2)]
        head = add_halves(across, [(keep_c, got_cx)])
        head = [head[0]] + [swap(head[step], "dp", 2 * step) for step in range(1, first // 2)]
        spot = lax.axis_index(("dp", "fsdp")).astype(jnp.int32).reshape(1)
        grads = write_gradients(spot, most, head, depth, width, hidden, (grad_in,))
    else:
        grads = scatter_other(
            *(jnp.stack(part) for part in (sent_a, sent_b, sent_c)), rows, width, hidden
        )
    return (hidden_out, grad_in, *grads)


def gather_other(
    attn_weight, attn_bias, out_weight, ffn_in, ffn_in_bias, ffn_out, norm_gain, shifts
):
    axes = ("dp", "fsdp")
    gather = lambda part, axis: lax.all_gather(part, axes, axis=axis, tiled=True)
    depth, unused, width = out_weight.shape
    hidden = ffn_in.shape[2]
    outer, inner, rows = GROUPS
    vectors = gather(jnp.concatenate([attn_bias, norm_gain, shifts], 1), 2)
    line = gather(ffn_in_bias, 1)

    def order(natural):
        return (
            natural.reshape(inner, outer, rows, -1).swapaxes(0, 1).reshape(outer, inner * rows, -1)
        )

    def stacked(part):
        part = part.reshape(DEVICES, -1, rows, width)
        return order(part.swapaxes(1, 2).reshape(width, -1))

    small = vectors.reshape(depth, 8, DEVICES, rows).transpose(2, 1, 0, 3).reshape(width, -1)
    line = line.reshape(depth, DEVICES, -1).swapaxes(0, 1)
    line = jnp.pad(line, ((0, 0), (0, 8 - depth), (0, 0))).reshape(width, -1)
    small = jnp.concatenate([small, line], 1)
    small = jnp.pad(small, ((0, 0), (0, 128 - small.shape[1])))
    wq, wo, wi, wf = (gather(part, 1) for part in (attn_weight, out_weight, ffn_in, ffn_out))
    urgent = jnp.concatenate([order(wq[0]), order(small)], 2)
    raw0 = jnp.concatenate([order(wq[1]), order(wo[0]), order(wi[0]), stacked(wf[0])], 2)
    raw1 = jnp.concatenate([order(wo[1]), order(wi[1]), stacked(wf[1])], 2)
    return urgent, raw0, raw1


def scatter_other(sent_a, sent_b, sent_c, own_rows, width, hidden):
    outer, inner, rows = GROUPS
    axes = ("dp", "fsdp")

    def natural(part):
        return part.reshape(outer, inner, rows, -1).swapaxes(0, 1).reshape(width, -1).astype(F32)

    def cut(part, sizes):
        found, at = [], 0
        for size in sizes:
            found.append(part[:, at : at + size])
            at += size
        return found

    dense = [width, hidden, hidden, width, hidden // 8]
    attention = [3 * width, 128]
    wq0, ab0 = cut(natural(sent_c), attention)
    wq1, ab1, wo0, wi0, wf0, small0, bi0 = cut(natural(sent_b), attention + dense)
    wo1, wi1, wf1, small1, bi1 = cut(natural(sent_a), dense)

    def stacked(part):
        part = part.reshape(DEVICES, rows, -1, width).swapaxes(1, 2)
        return part.reshape(hidden, width)

    def spread(parts, axis):
        return lax.psum_scatter(jnp.stack(parts), axes, scatter_dimension=axis, tiled=True)

    return (
        spread([wq0, wq1], 1),
        spread([ab0[:4].reshape(2, width), ab1[:4].reshape(2, width)], 2),
        spread([wo0, wo1], 1),
        spread([wi0, wi1], 1),
        spread([bi0[:8].reshape(-1), bi1[:8].reshape(-1)], 1),
        spread([stacked(wf0), stacked(wf1)], 1),
        spread([small0[2:4], small1[2:4]], 2),
        spread([small0[4:8], small1[4:8]], 2),
    )


def solution(mesh):
    placed = (
        P(("dp", "fsdp"), None),
        P(("dp", "fsdp"), None),
        P(("dp", "fsdp"), None),
        P(None, ("dp", "fsdp"), None),
        P(None, None, ("dp", "fsdp")),
        P(None, ("dp", "fsdp"), None),
        P(None, ("dp", "fsdp"), None),
        P(None, ("dp", "fsdp")),
        P(None, ("dp", "fsdp"), None),
        P(None, None, ("dp", "fsdp")),
        P(None, None, ("dp", "fsdp")),
    )
    return jax.shard_map(
        local,
        mesh=mesh,
        in_specs=placed,
        out_specs=(
            P(("dp", "fsdp"), None),
            P(("dp", "fsdp"), None),
            P(None, ("dp", "fsdp"), None),
            P(None, None, ("dp", "fsdp")),
            P(None, ("dp", "fsdp"), None),
            P(None, ("dp", "fsdp"), None),
            P(None, ("dp", "fsdp")),
            P(None, ("dp", "fsdp"), None),
            P(None, None, ("dp", "fsdp")),
            P(None, None, ("dp", "fsdp")),
        ),
        check_vma=False,
    )
```

```python
from functools import partial

import jax
import jax.numpy as jnp
from jax import lax
from jax.experimental import pallas as pl
from jax.experimental.pallas import tpu as pltpu
from jax.sharding import PartitionSpec as P

HEADS = 4
HD = 64
SEQ = 512
PAIR = 2 * HD
EXTRA = 16
HALF = SEQ // 2
HALVES = (slice(0, HALF), slice(HALF, SEQ))
FAR = -(2.0**100)
FLOOR = -1e20
EPSILON = 1e-12
PIECE = 256
SMALL = 128
GROUPS = (4, 8, 8)
DEVICES = 32
LOW = jnp.bfloat16
F32 = jnp.float32
MEMORY = 2**26


def dot_nn(left, right):
    return lax.dot_general(left, right, (((1,), (0,)), ((), ())), preferred_element_type=F32)


def dot_nt(left, right):
    return lax.dot_general(left, right, (((1,), (1,)), ((), ())), preferred_element_type=F32)


def dot_tn(left, right):
    return lax.dot_general(left, right, (((0,), (0,)), ((), ())), preferred_element_type=F32)


def pieces(total, size=PIECE):
    return [pl.ds(start, size) for start in range(0, total, size)]


def three_parts(values):
    first = values.astype(LOW).astype(F32)
    rest = values - first
    second = rest.astype(LOW).astype(F32)
    return first, second, rest - second


CURVE = (7.97869556e-01, 3.63928094e-02, -8.82195179e-05, -3.66000319e-05, 1.41853144e-06)
BELL = -0.5 / 0.6931471805599453


def gelu_parts(u):
    square = u * u
    curve = CURVE[-1]
    for factor in CURVE[-2::-1]:
        curve = curve * square + factor
    cumulative = 0.5 + 0.5 * jnp.tanh(u * curve)
    slope = cumulative + (u * 0.3989422804014327) * jnp.exp2(square * BELL)
    return u * cumulative, slope


def inverse_of(values):
    guess = pl.reciprocal(values, approx=True)
    return guess * (2.0 - values * guess)


def longest_start(lengths_ref, row):
    begin, found = jnp.int32(0), jnp.int32(0)
    for entry in range(lengths_ref.shape[1]):
        size = lengths_ref[row, entry]
        found = jnp.where(size == HALF, begin, found)
        begin = begin + size
    return found


def segments(lengths_ref, row):
    places = lax.broadcasted_iota(jnp.int32, (1, SEQ), 1) + longest_start(lengths_ref, row)
    places = places & (SEQ - 1)
    bound = jnp.int32(0)
    segment = jnp.zeros((1, SEQ), jnp.int32)
    last = lengths_ref.shape[1] - 1
    for entry in range(last):
        bound = bound + lengths_ref[row, entry]
        segment = segment + (places >= bound).astype(jnp.int32)
    return segment, last


def head_rows(head):
    return slice(head * HD, (head + 1) * HD)


def attention_forward(row, lengths_ref, x, wt_ref, bias_ref, qa_ref, ka_ref, va_ref, ob_ref, lse_ref, s_ref, p_ref):
    width = HEADS * HD
    segment, last = segments(lengths_ref, row)
    pad = (segment == last).astype(F32)
    line = lax.broadcasted_iota(jnp.int32, (EXTRA, SEQ), 0)
    aug_q = jnp.where(line == segment, 1.0, 0.0).astype(LOW)
    seen = (line == segment) & (segment != last)
    aug_k = jnp.where(seen | (line > last), 0.0, FAR).astype(LOW)
    aug_v = jnp.where(line == 0, 1.0, 0.0).astype(LOW)
    rest = jnp.zeros((PAIR - HD - EXTRA, SEQ), LOW)
    for head in range(HEADS):
        qa_ref[head, HD : HD + EXTRA] = aug_q
        ka_ref[head, HD : HD + EXTRA] = aug_k
        va_ref[head, HD : HD + EXTRA] = aug_v
        qa_ref[head, HD + EXTRA : PAIR] = rest
        ka_ref[head, HD + EXTRA : PAIR] = rest
    for block, ref in enumerate((qa_ref, ka_ref, va_ref)):
        lines = slice(block * width, (block + 1) * width)
        bias = bias_ref[lines]
        value = dot_nt(wt_ref[lines], x) + jnp.concatenate([bias] * (SEQ // 128), 1)
        if block == 0:
            value = value * HD**-0.5
        value = value.astype(LOW)
        for head in range(HEADS):
            ref[head, 0:HD] = value[head_rows(head)]
        yield

    def scores(head):
        for half in HALVES:
            s_ref[head % 2, half] = dot_tn(ka_ref[head, :, half], qa_ref[head, :, half])

    def softmax(head):
        tops = []
        for half in HALVES:
            tops.append(jnp.maximum(jnp.max(s_ref[head % 2, half], 0, keepdims=True), FLOOR))
            p_ref[head % 2, half] = jnp.exp(s_ref[head % 2, half] - tops[-1]).astype(LOW)
        return tops

    scores(0)
    yield
    for head in range(HEADS):
        if head + 1 < HEADS:
            scores(head + 1)
            yield
        tops = softmax(head)
        yield
        for half, top in zip(HALVES, tops):
            out = dot_nn(va_ref[head, :, half], p_ref[head % 2, half])
            alone = pad[:, half]
            total = out[HD : HD + 1] + alone
            lse_ref[head : head + 1, half] = jnp.where(alone > 0, 0.0, top + jnp.log(total))
            own = alone * va_ref[head, 0:HD, half].astype(F32)
            ob_ref[head_rows(head), half] = (out[0:HD] * inverse_of(total) + own).astype(LOW)
        yield


def normal(values):
    centred = values - jnp.mean(values, -1, keepdims=True)
    inverse = lax.rsqrt(jnp.mean(centred * centred, -1, keepdims=True) + EPSILON)
    return centred * inverse, inverse


def normal_back(cotangent, unit, inverse, gains):
    scaled = cotangent * gains
    return inverse * (
        scaled
        - jnp.mean(scaled, -1, keepdims=True)
        - unit * jnp.mean(scaled * unit, -1, keepdims=True)
    )


def dense_forward(x_ref, ob_ref, wo_ref, wi_ref, wf_ref, small_ref, bi_ref, n1_ref, n2_ref, inv_ref, yb_ref, gb_ref, gp_ref, z_ref, work_ref, u_ref):
    small = lambda index: small_ref[pl.ds(index, 1)]
    work_ref[...] = dot_tn(ob_ref[...], wo_ref[...])
    yield
    for place in pieces(SEQ):
        unit, inverse = normal(x_ref[place].astype(F32) + work_ref[place] + small(4))
        n1_ref[place] = unit
        inv_ref[place, pl.ds(0, HD)] = jnp.broadcast_to(inverse, (PIECE, HD))
        y = unit * small(2) + small(5)
        yb_ref[place] = y.astype(LOW)
        work_ref[place] = y + small(6)
        yield
    columns = 256
    count = wi_ref.shape[1] // columns

    def into(step):
        u_ref[step % 2] = dot_nn(yb_ref[...], wi_ref[:, pl.ds(step * columns, columns)])

    into(0)
    yield
    for step in range(count):
        if step + 1 < count:
            into(step + 1)
            yield
        lanes = pl.ds(step * columns, columns)
        for place in pieces(SEQ, SMALL):
            g, slope = gelu_parts(u_ref[step % 2, place] + bi_ref[:, lanes])
            gb_ref[place, lanes] = g.astype(LOW)
            gp_ref[place, lanes] = slope.astype(LOW)
            yield
    work_ref[...] += dot_nn(gb_ref[...], wf_ref[...])
    yield
    for place in pieces(SEQ):
        unit, inverse = normal(work_ref[place])
        n2_ref[place] = unit
        inv_ref[place, pl.ds(HD, HD)] = jnp.broadcast_to(inverse, (PIECE, HD))
        z_ref[place] = (unit * small(3) + small(7)).astype(z_ref.dtype)
        yield


def fold(values):
    return jnp.sum(values.reshape(-1, 8, values.shape[-1]), 0)


def dense_backward(dz_ref, n1_ref, n2_ref, inv_ref, yb_ref, gb_ref, gp_ref, ob_ref, wo_ref, wi_ref, wf_ref, small_ref, dr_ref, dob_ref, gwo_ref, gwi_ref, gwf_ref, gsmall_ref, gbi_ref, low_ref, u_ref, du_ref, turned_ref):
    small = lambda index: small_ref[pl.ds(index, 1)]
    for place in pieces(SEQ):
        dz = dz_ref[place].astype(F32)
        unit = n2_ref[place]
        gsmall_ref[3] += fold(dz * unit)
        gsmall_ref[7] += fold(dz)
        dr = normal_back(dz, unit, inv_ref[place, pl.ds(HD, 1)], small(3))
        dr_ref[place] = dr
        df = dr.astype(LOW)
        low_ref[place] = df
        gsmall_ref[6] += fold(df.astype(F32))
        yield
    columns = 256
    count = wi_ref.shape[1] // columns

    def back(step):
        u_ref[step % 2] = dot_nt(low_ref[...], wf_ref[pl.ds(step * columns, columns)])

    back(0)
    turned_ref[0] = low_ref[...].T
    turned_ref[1] = yb_ref[...].T
    yield
    for step in range(count):
        if step + 1 < count:
            back(step + 1)
            yield
        lanes = pl.ds(step * columns, columns)
        gwf_ref[:, lanes] += dot_nn(turned_ref[0], gb_ref[:, lanes])
        yield
        for place in pieces(SEQ, SMALL):
            du = (u_ref[step % 2, place] * gp_ref[place, lanes].astype(F32)).astype(LOW)
            du_ref[place, lanes] = du
            gbi_ref[:, lanes] += fold(du.astype(F32))
        yield
        gwi_ref[:, lanes] += dot_nn(turned_ref[1], du_ref[:, lanes])
        yield
    u_ref[0] = dot_nt(du_ref[...], wi_ref[...])
    yield
    for place in pieces(SEQ):
        dy = dr_ref[place] + u_ref[0, place]
        unit = n1_ref[place]
        gsmall_ref[2] += fold(dy * unit)
        gsmall_ref[5] += fold(dy)
        dr = normal_back(dy, unit, inv_ref[place, pl.ds(0, 1)], small(2))
        dr_ref[place] = dr
        da = dr.astype(LOW)
        low_ref[place] = da
        gsmall_ref[4] += fold(da.astype(F32))
        yield
    gwo_ref[...] += dot_nn(ob_ref[...], low_ref[...])
    dob_ref[...] = dot_nt(wo_ref[...], low_ref[...]).astype(LOW)
    yield


def attention_backward(row, lengths_ref, x, do_ref, ob_ref, qa_ref, ka_ref, va_ref, lse_ref, dqkv_ref, gwq_ref, gbias_ref, p_ref, ds_ref, s_ref):
    width = HEADS * HD
    segment, last = segments(lengths_ref, row)
    pad = (segment == last).astype(F32)

    def scores(head):
        for half in HALVES:
            s_ref[0, head % 2, half] = dot_tn(ka_ref[head, :, half], qa_ref[head, :, half])
            s_ref[1, head % 2, half] = dot_tn(
                va_ref[head, 0:HD, half], do_ref[head_rows(head), half]
            )

    def weigh(head):
        product = do_ref[head_rows(head)].astype(F32) * ob_ref[head_rows(head)].astype(F32)
        centre = jnp.sum(product, 0, keepdims=True)
        for half in HALVES:
            p = jnp.exp(s_ref[0, head % 2, half] - lse_ref[head : head + 1, half])
            p_ref[head % 2, half] = p.astype(LOW)
            ds_ref[head % 2, half] = (p * (s_ref[1, head % 2, half] - centre[:, half])).astype(LOW)

    scores(0)
    yield
    for head in range(HEADS):
        if head + 1 < HEADS:
            scores(head + 1)
            yield
        weigh(head)
        yield
        for half in HALVES:
            ds, do = ds_ref[head % 2, half], do_ref[head_rows(head), half]
            dq = dot_nn(ka_ref[head, 0:HD, half], ds) * HD**-0.5
            dk = dot_nt(qa_ref[head, 0:HD, half], ds)
            dv = dot_nt(do, p_ref[head % 2, half]) + pad[:, half] * do.astype(F32)
            for block, value in enumerate((dq, dk, dv)):
                at = block * width + head * HD
                dqkv_ref[at : at + HD, half] = value.astype(LOW)
        yield
    for index, block in enumerate((0, 2)):
        value = dqkv_ref[block * width : (block + 1) * width].astype(F32)
        parts = [value[:, at : at + 128] for at in range(0, SEQ, 128)]
        gbias_ref[index] += (parts[0] + parts[1]) + (parts[2] + parts[3])
    gwq_ref[...] += dot_nn(dqkv_ref[...], x)
    yield


def unpack_matrix(raw_ref, at, into_ref):
    width = into_ref.shape[0]
    for start in range(0, into_ref.shape[1], width):
        block = raw_ref[:, :, pl.ds(at + start, width)].astype(F32)
        block = block.reshape(GROUPS + (width,)).swapaxes(0, 1).reshape(width, width)
        into_ref[:, pl.ds(start, width)] = block.astype(LOW)


def unpack_stacked(raw_ref, at, into_ref):
    width = into_ref.shape[1]
    count = into_ref.shape[0] // width
    blocks = [
        raw_ref[:, :, pl.ds(at + step * width, width)].astype(F32).reshape(GROUPS + (width,))
        for step in range(count)
    ]
    outer, inner, rows = GROUPS
    for place in range(inner):
        part = jnp.stack([jnp.stack([block[f, place] for block in blocks]) for f in range(outer)])
        size = outer * count * rows
        into_ref[pl.ds(place * size, size)] = part.reshape(size, width).astype(LOW)


def counter(shape, axis):
    return lax.broadcasted_iota(jnp.int32, shape, axis)


def split_by(values, size):
    return lax.shift_right_logical(values, size.bit_length() - 1), values & (size - 1)


def sources(rows):
    outer, inner, height = GROUPS
    group, within = split_by(counter((rows, 1), 0), height)
    far, near = split_by(group, inner)
    return near * outer + far, within


def unpack_vectors(raw_ref, at, layer):
    outer, inner, rows = GROUPS
    total = outer * inner * rows
    raw = raw_ref[:, :, pl.ds(at, 128)].reshape(total, 128)
    owner, place = split_by(counter((1, total), 1), rows)
    pick = jnp.where(counter((128, 1), 0) == rows * layer + place, 1.0, 0.0).astype(LOW)
    device, unused = sources(total)
    spread = jnp.where(owner == device, dot_nn(raw, pick), 0.0)
    return jnp.sum(spread.reshape(outer * inner, rows, total), 0)


def unpack_hidden(raw_ref, at, layer, hidden):
    outer, inner, rows = GROUPS
    total = outer * inner * rows
    raw = raw_ref[:, :, pl.ds(at, 128)].reshape(total, 128)
    owner, place = split_by(counter((1, hidden), 1), hidden // (outer * inner))
    pick = jnp.where(counter((128, 1), 0) == 2 * rows + place, 1.0, 0.0).astype(LOW)
    device, within = sources(total)
    device = jnp.where(within == layer, device, -1)
    spread = jnp.where(owner == device, dot_nn(raw, pick), 0.0)
    return jnp.sum(spread, 0, keepdims=True)


def pack_matrix(sum_ref, sent_ref, at, turned=False):
    width = sum_ref.shape[1 if turned else 0]
    outer, inner, rows = GROUPS
    for start in range(0, sum_ref.shape[0 if turned else 1], width):
        near = pl.ds(start, width)
        block = sum_ref[near].T if turned else sum_ref[:, near]
        block = block.reshape(inner, outer, rows, width)
        block = block.swapaxes(0, 1).reshape(outer, inner * rows, width)
        sent_ref[:, :, pl.ds(at + start, width)] = block.astype(LOW)


def pack_stacked(sum_ref, sent_ref, at):
    width = sum_ref.shape[0]
    outer, inner, rows = GROUPS
    count = sum_ref.shape[1] // width
    near = inner // count
    for step in range(count):
        block = sum_ref[:, pl.ds(step * width, width)].T
        block = block.reshape(near, outer, count, rows, width)
        for part in range(count):
            piece = jnp.stack([block[:, f, part] for f in range(outer)])
            piece = piece.reshape(outer, near * rows, width)
            sent_ref[:, pl.ds(step * near * rows, near * rows), pl.ds(at + part * width, width)] = (
                piece.astype(LOW)
            )


def pack_shared(block, sent_ref, at):
    outer, inner, rows = GROUPS
    columns = block.shape[1]
    block = jnp.broadcast_to(block[None], (outer * inner, rows, columns))
    sent_ref[:, :, pl.ds(at, columns)] = block.reshape(outer, inner * rows, columns).astype(LOW)


def folded(line, lanes):
    return [line[:, at : at + lanes] for at in range(0, line.shape[1], lanes)]


def pack_attention(gwq_ref, gbias_ref, sent_ref, at):
    pack_matrix(gwq_ref, sent_ref, at, True)
    width = gwq_ref.shape[1]
    parts = []
    for index in range(2):
        parts += folded(jnp.sum(gbias_ref[index].T, 0, keepdims=True), 128)
    block = jnp.concatenate(parts + [jnp.zeros((8 - len(parts), 128), F32)], 0)
    pack_shared(block, sent_ref, at + 3 * width)


def pack_dense(gwo_ref, gwi_ref, gwf_ref, gsmall_ref, gbi_ref, sent_ref, at):
    width, hidden = gwi_ref.shape
    pack_matrix(gwo_ref, sent_ref, at)
    pack_matrix(gwi_ref, sent_ref, at + width)
    pack_stacked(gwf_ref, sent_ref, at + width + hidden)
    at = at + width + 2 * hidden
    pack_shared(jnp.sum(gsmall_ref[...], 1), sent_ref, at)
    line = jnp.sum(gbi_ref[...], 0, keepdims=True)
    pack_shared(jnp.concatenate(folded(line, hidden // 8), 0), sent_ref, at + width)


def shape_of(array):
    return jax.ShapeDtypeStruct(array.shape, array.dtype)


def by_row(shape, group):
    if len(shape) == 2:
        return pl.BlockSpec((group * SEQ, shape[1]), lambda step: (step, 0))
    return pl.BlockSpec((group,) + tuple(shape[1:]), lambda step: (step,) + (0,) * (len(shape) - 1))


def one_row(ref, member):
    if len(ref.shape) == 2:
        return ref.at[pl.ds(member * SEQ, SEQ)]
    return ref.at[member]


def alternate(runs):
    running = []
    waiting = list(runs)
    while running or waiting:
        if waiting:
            running.append(waiting.pop(0))
        for run in list(running):
            try:
                next(run)
            except StopIteration:
                running.remove(run)


def whole(shape):
    return pl.BlockSpec(tuple(shape), lambda row: (0,) * len(shape))


def run_rows(
    body, lengths, rowwise, fixed, row_outs, sent, shared, private, cost, setup, finish, after=(),
    scalars=(), group=1
):
    count = lengths.shape[0]
    group = group if count % group == 0 else 1
    cuts = [len(scalars), len(rowwise), len(fixed), len(after), len(row_outs), len(sent)]
    cuts += [len(shared)] + [len(private)] * group

    def kernel(lengths_ref, *refs):
        step = pl.program_id(0)
        groups = []
        at = 0
        for cut in cuts:
            groups.append(refs[at : at + cut])
            at += cut
        numbers, rows_in, fixed_in, unused, rows_out, sent_out, work = groups[:7]

        @pl.when(step == 0)
        def _():
            setup(numbers, fixed_in, sent_out, work)

        alternate(
            body(
                step * group + member,
                lengths_ref,
                [one_row(ref, member) for ref in rows_in],
                [one_row(ref, member) for ref in rows_out],
                work,
                groups[7 + member],
            )
            for member in range(group)
        )

        if finish:

            @pl.when(step == count // group - 1)
            def _():
                finish(numbers, work, sent_out)

    return pl.pallas_call(
        kernel,
        grid=(count // group,),
        in_specs=[pl.BlockSpec(memory_space=pltpu.SMEM)] * (1 + len(scalars))
        + [by_row(array.shape, group) for array in rowwise]
        + [whole(array.shape) for array in fixed]
        + [pl.BlockSpec(memory_space=pl.ANY) for array in after],
        out_specs=[by_row(part.shape, group) for part in row_outs]
        + [whole(part.shape) for part in sent],
        out_shape=list(row_outs) + list(sent),
        scratch_shapes=list(shared) + list(private) * group,
        compiler_params=pltpu.CompilerParams(
            dimension_semantics=("arbitrary",), vmem_limit_bytes=MEMORY
        ),
        cost_estimate=pl.CostEstimate(flops=cost, bytes_accessed=8 * 2**20, transcendentals=0),
    )(lengths, *scalars, *rowwise, *fixed, *after)


def struct(shape, dtype):
    return jax.ShapeDtypeStruct(tuple(shape), dtype)


FORWARD_SCRATCH = lambda: [
    pltpu.VMEM((2, SEQ, HALF), F32),
    pltpu.VMEM((2, SEQ, HALF), LOW),
]
BACKWARD_SCRATCH = lambda: [
    pltpu.VMEM((2, SEQ, HALF), LOW),
    pltpu.VMEM((2, SEQ, HALF), LOW),
    pltpu.VMEM((2, 2, SEQ, HALF), F32),
    pltpu.VMEM((3 * HEADS * HD, SEQ), LOW),
]


def attention_outs(rows, width):
    return [
        struct((rows, HEADS, PAIR, SEQ), LOW),
        struct((rows, HEADS, PAIR, SEQ), LOW),
        struct((rows, HEADS, HD + EXTRA, SEQ), LOW),
        struct((rows, width, SEQ), LOW),
        struct((rows, 8, SEQ), F32),
    ]


def dense_outs(tokens, width, hidden):
    return [
        struct((tokens, width), F32),
        struct((tokens, width), F32),
        struct((tokens, PAIR), F32),
        struct((tokens, width), LOW),
        struct((tokens, hidden), LOW),
        struct((tokens, hidden), LOW),
    ]


def vmem(shape, dtype):
    return pltpu.VMEM(tuple(shape), dtype)


def attention_weights(width):
    return [vmem((width, 3 * width), LOW), vmem((3 * width, width), LOW), vmem((3 * width, 128), F32)]


def dense_weights(width, hidden):
    return [
        vmem((width, width), LOW),
        vmem((width, hidden), LOW),
        vmem((hidden, width), LOW),
        vmem((8, width), F32),
        vmem((1, hidden), F32),
    ]


def dense_sums(width, hidden):
    return [
        vmem((width, width), F32),
        vmem((width, hidden), F32),
        vmem((width, hidden), F32),
        vmem((8, 8, width), F32),
        vmem((8, hidden), F32),
    ]


def attention_sums(width):
    return [vmem((3 * width, width), F32), vmem((2, width, 128), F32)]


def dense_work(width, hidden):
    return [
        vmem((SEQ, width), LOW),
        vmem((2, SEQ, width), F32),
        vmem((SEQ, hidden), LOW),
        vmem((2, width, SEQ), LOW),
    ]


def set_attention(layer, urgent_ref, raw_ref, at, wq_ref, wt_ref, bias_ref):
    width = wq_ref.shape[0]
    unpack_matrix(raw_ref, at, wq_ref)
    vectors = unpack_vectors(urgent_ref, 3 * width, layer)
    for block, line in enumerate((vectors[0:1], jnp.zeros((1, width), F32), vectors[1:2])):
        lines = pl.ds(block * width, width)
        wt_ref[lines] = wq_ref[:, lines].astype(F32).T.astype(LOW)
        bias_ref[lines] = jnp.broadcast_to(line, (128, width)).T


def set_dense(layer, urgent_ref, raw_ref, at, wo_ref, wi_ref, wf_ref, small_ref, bi_ref):
    width, hidden = wi_ref.shape
    unpack_matrix(raw_ref, at, wo_ref)
    unpack_matrix(raw_ref, at + width, wi_ref)
    unpack_stacked(raw_ref, at + width + hidden, wf_ref)
    small_ref[...] = unpack_vectors(urgent_ref, 3 * width, layer)
    bi_ref[...] = unpack_hidden(urgent_ref, 3 * width, layer, hidden)


def clear(refs):
    for ref in refs:
        ref[...] = jnp.zeros(ref.shape, ref.dtype)


def assemble(place_ref, part_refs, into_ref):
    for step, ref in enumerate(part_refs):
        into_ref[place_ref[0] ^ step] = ref[...]


def raw_block(parts):
    return vmem((len(parts),) + parts[0].shape, LOW)


def turned_back(lengths_ref, row, values):
    return pltpu.roll(values, longest_start(lengths_ref, row), 0).astype(LOW)


def rotate_kernel(lengths, arrays):
    def body(row, lengths_ref, rowwise, outs, work, own):
        back = (SEQ - longest_start(lengths_ref, row)) & (SEQ - 1)
        for source, target in zip(rowwise, outs):
            target[...] = pltpu.roll(source[...].astype(F32), back, 0).astype(LOW)
            yield

    return run_rows(
        body, lengths, list(arrays), [], [struct(array.shape, LOW) for array in arrays], [], [], [],
        10**6, lambda *refs: None, None,
    )


def first_kernel(lengths, x, place, parts):
    rows, (tokens, width) = lengths.shape[0], x.shape

    def setup(numbers, fixed, sent, work):
        assemble(numbers[0], fixed, sent[0])
        set_attention(0, sent[0], sent[0], 0, *work)

    def body(row, lengths_ref, rowwise, outs, work, own):
        return attention_forward(row, lengths_ref, rowwise[0][...], *work[1:3], *outs, *own)

    return run_rows(
        body, lengths, [x], list(parts), attention_outs(rows, width),
        [struct((len(parts),) + parts[0].shape, LOW)],
        attention_weights(width), FORWARD_SCRATCH(), 4 * 10**9, setup, None, (), [place],
    )


def attention_kernel(layer, lengths, x, place, urgent, parts, at):
    rows, (tokens, width) = lengths.shape[0], x.shape

    def setup(numbers, fixed, sent, work):
        assemble(numbers[0], fixed[1:], work[3])
        set_attention(layer, fixed[0], work[3], at, *work[:3])

    def body(row, lengths_ref, rowwise, outs, work, own):
        return attention_forward(
            row, lengths_ref, rowwise[0][...].astype(LOW), *work[1:3], *outs, *own
        )

    return run_rows(
        body, lengths, [x], [urgent] + list(parts), attention_outs(rows, width), [],
        attention_weights(width) + [raw_block(parts)], FORWARD_SCRATCH(),
        4 * 10**9, setup, None, (), [place],
    )


def dense_kernel(layer, lengths, x, ob, place, urgent, parts, at, hidden):
    tokens, width = x.shape

    def setup(numbers, fixed, sent, work):
        assemble(numbers[0], fixed[1:], work[5])
        set_dense(layer, fixed[0], work[5], at, *work[:5])

    def body(row, lengths_ref, rowwise, outs, work, own):
        return dense_forward(*rowwise, *work[:5], *outs, *own)

    return run_rows(
        body, lengths, [x, ob], [urgent] + list(parts),
        dense_outs(tokens, width, hidden) + [struct((tokens, width), F32)], [],
        dense_weights(width, hidden) + [raw_block(parts)],
        [vmem((SEQ, width), F32), vmem((2, SEQ, width), F32)],
        5 * 10**9, setup, None, (), [place],
    )


def turn_kernel(layer, lengths, x, ob, cotangent, place, urgent, parts, at, hidden):
    tokens, width = x.shape
    columns = width + 2 * hidden + width + hidden // 8

    def setup(numbers, fixed, sent, work):
        assemble(numbers[0], fixed[1:], work[11])
        set_dense(layer, fixed[0], work[11], at, *work[:5])
        clear(work[5:10])

    def body(row, lengths_ref, rowwise, outs, work, own):
        x_ref, ob_ref, dz_ref = rowwise
        z_ref, dr_ref, dob_ref = outs
        weights, sums = work[:5], work[5:10]
        kept, work_ref, back = own[:6], own[6], own[7:]
        yield from dense_forward(x_ref, ob_ref, *weights, *kept, z_ref, work_ref, back[1])
        yield from dense_backward(dz_ref, *kept, ob_ref, *weights[:4], dr_ref, dob_ref, *sums, *back)

    def finish(numbers, work, sent):
        pack_dense(*work[5:10], work[10], 0)
        hand_out(numbers[0], work[10], sent)

    kept = [vmem((SEQ,) + part.shape[1:], part.dtype) for part in dense_outs(tokens, width, hidden)]
    return run_rows(
        body, lengths, [x, ob, cotangent], [urgent] + list(parts),
        [struct((tokens, width), LOW), struct((tokens, width), F32), struct((tokens // SEQ, width, SEQ), LOW)],
        [struct((64, columns), LOW)] * 4,
        dense_weights(width, hidden) + dense_sums(width, hidden)
        + [vmem((4, 64, columns), LOW), raw_block(parts)],
        kept + [vmem((SEQ, width), F32)] + dense_work(width, hidden),
        10**10, setup, finish, (), [place], 2,
    )


def hand_out(place_ref, packed_ref, sent):
    for step, ref in enumerate(sent):
        ref[...] = packed_ref[place_ref[0] ^ step]


def middle_kernel(lengths, upper, lower, place, urgent, parts, hidden, after):
    tokens, width = upper[0].shape
    columns = 3 * width + 128 + width + 2 * hidden + width + hidden // 8

    def setup(numbers, fixed, sent, work):
        assemble(numbers[0], fixed[1:], work[16])
        set_attention(1, fixed[0], work[16], 0, *work[:3])
        set_dense(0, fixed[0], work[16], 3 * width, *work[3:8])
        clear(work[8:15])

    def body(row, lengths_ref, rowwise, outs, work, own):
        up, low = rowwise[:8], rowwise[8:]
        dx_ref = own[0]
        yield from attention_backward(
            row, lengths_ref, up[0][...].astype(LOW), *up[1:7], own[-1], *work[8:10], *own[5:-1]
        )
        dx_ref[...] = up[7][...] + dot_tn(own[-1][...], work[1][...])
        yield
        yield from dense_backward(dx_ref, *low, *work[3:7], *outs, *work[10:15], *own[1:5])

    def finish(numbers, work, sent):
        pack_attention(*work[8:10], work[15], 0)
        pack_dense(*work[10:15], work[15], 3 * width + 128)
        hand_out(numbers[0], work[15], sent)

    return run_rows(
        body, lengths, list(upper) + list(lower), [urgent] + list(parts),
        [struct((tokens, width), F32), struct((tokens // SEQ, width, SEQ), LOW)],
        [struct((64, columns), LOW)] * 4,
        attention_weights(width) + dense_weights(width, hidden)
        + attention_sums(width) + dense_sums(width, hidden)
        + [vmem((4, 64, columns), LOW), raw_block(parts)],
        [vmem((SEQ, width), F32)] + dense_work(width, hidden) + BACKWARD_SCRATCH(),
        15 * 10**9, setup, finish, after, [place], 2,
    )


def last_kernel(lengths, upper, after, place):
    tokens, width = upper[0].shape

    def setup(numbers, fixed, sent, work):
        clear(work[:2])

    def body(row, lengths_ref, rowwise, outs, work, own):
        return attention_backward(
            row, lengths_ref, rowwise[0][...], *rowwise[1:], outs[0], *work[:2], *own
        )

    def finish(numbers, work, sent):
        pack_attention(*work[:2], work[2], 0)
        hand_out(numbers[0], work[2], sent)

    return run_rows(
        body, lengths, list(upper), [], [struct((tokens // SEQ, 3 * width, SEQ), LOW)],
        [struct((64, 3 * width + 128), LOW)] * 4,
        attention_sums(width) + [vmem((4, 64, 3 * width + 128), LOW)],
        BACKWARD_SCRATCH()[:-1], 8 * 10**9, setup, finish, after, [place], 2,
    )


def tokens_kernel(lengths, z, dqkv, dr, urgent):
    tokens, width = dr.shape

    def setup(numbers, fixed, sent, work):
        set_attention(0, fixed[0], fixed[0], 0, *work)

    def body(row, lengths_ref, rowwise, outs, work, own):
        z_ref, dqkv_ref, dr_ref = rowwise
        outs[0][...] = turned_back(lengths_ref, row, z_ref[...].astype(F32))
        yield
        dx = dr_ref[...] + dot_tn(dqkv_ref[...], work[1][...])
        outs[1][...] = turned_back(lengths_ref, row, dx)
        yield

    return run_rows(
        body, lengths, [z, dqkv, dr], [urgent], [struct((tokens, width), LOW)] * 2, [],
        attention_weights(width), [], 10**9, setup, None,
    )


def hold(array, after):
    def kernel(*refs):
        pass

    anywhere = pl.BlockSpec(memory_space=pl.ANY)
    return pl.pallas_call(
        kernel,
        in_specs=[anywhere] * (1 + len(after)),
        out_specs=anywhere,
        out_shape=shape_of(array),
        input_output_aliases={0: 0},
    )(array, *after)


def pack_parameters(
    attn_weight, attn_bias, out_weight, ffn_in, ffn_in_bias, ffn_out, norm_gain, shifts
):
    depth, rows, width = out_weight.shape
    copies = GROUPS[1]
    hidden = ffn_in.shape[2]
    dense = width + 2 * hidden
    height = ffn_in_bias.shape[1]

    def kernel(wq_ref, ab_ref, wo_ref, wi_ref, bi_ref, wf_ref, gain_ref, shift_ref, first_ref, rest_ref, small_ref):
        def put(ref, block, at):
            block = jnp.broadcast_to(block.astype(F32)[None], (copies,) + block.shape)
            block = block.reshape(copies * block.shape[1], block.shape[2])
            ref[:, pl.ds(at, block.shape[1])] = block.astype(LOW)

        small_ref[...] = jnp.zeros(small_ref.shape, F32)
        for layer in range(depth):
            lanes = pl.ds(rows * layer, rows)
            small_ref[0:2, lanes] = ab_ref[layer].astype(F32)
            small_ref[2:4, lanes] = gain_ref[layer].astype(F32)
            small_ref[4:8, lanes] = shift_ref[layer].astype(F32)
        small_ref[0:depth, pl.ds(2 * rows, height)] = bi_ref[...].astype(F32)
        put(first_ref, wq_ref[0], 0)
        put(first_ref, small_ref[...], 3 * width)
        put(first_ref, wq_ref[1], 3 * width + 128)
        for layer, ref, at in ((0, first_ref, 6 * width + 128), (1, rest_ref, 0)):
            put(ref, wo_ref[layer], at)
            put(ref, wi_ref[layer], at + width)
            at += width + hidden
            down = wf_ref[layer].astype(F32)
            for step in range(hidden // width):
                put(ref, down[step * rows : (step + 1) * rows], at)
                at += width

    return pl.pallas_call(
        kernel,
        in_specs=[pl.BlockSpec(memory_space=pltpu.VMEM)] * 8,
        out_shape=[
            struct((copies * rows, 6 * width + 128 + dense), LOW),
            struct((copies * rows, dense), LOW),
        ],
        scratch_shapes=[vmem((rows, 128), F32)],
        compiler_params=pltpu.CompilerParams(vmem_limit_bytes=MEMORY),
    )(attn_weight, attn_bias, out_weight, ffn_in, ffn_in_bias, ffn_out, norm_gain, shifts)


def add_parts(place, parts, halves, after=()):
    lanes = parts[0].shape[1]
    count = len(parts)
    many, rows = GROUPS[1:]
    outs = 2 if halves else 1

    def kernel(place_ref, *refs):
        out_refs, sum_ref = refs[count + len(after) : -1], refs[-1]
        bit = place_ref[0] & 1
        for start in range(0, lanes, 128):
            near = pl.ds(start, 128)
            total = refs[0][:, near].astype(F32)
            for ref in refs[1:count]:
                total = total + ref[:, near].astype(F32)
            if halves:
                sum_ref[:, :, near] = total.reshape(many, rows, 128)
            else:
                out_refs[0][:, near] = total.astype(LOW)
        for side, ref in enumerate(out_refs if halves else ()):
            for start in range(0, lanes, 128):
                near = pl.ds(start, 128)
                block = [sum_ref[2 * step + (bit ^ side), :, near] for step in range(many // 2)]
                ref[:, near] = jnp.concatenate(block, 0).astype(LOW)

    return pl.pallas_call(
        kernel,
        in_specs=[pl.BlockSpec(memory_space=pltpu.SMEM)]
        + [pl.BlockSpec(memory_space=pltpu.VMEM)] * count
        + [pl.BlockSpec(memory_space=pl.ANY)] * len(after),
        out_shape=[struct((many * rows // outs, lanes), LOW)] * outs,
        scratch_shapes=[vmem((many, rows, lanes), F32)],
        compiler_params=pltpu.CompilerParams(vmem_limit_bytes=MEMORY),
    )(place, *parts, *after)


def add_halves(place, pairs):
    many, rows = GROUPS[1] // 2, GROUPS[2]
    widths = [pair[0].shape[1] for pair in pairs]
    lanes = sum(widths)

    def kernel(place_ref, *refs):
        out_refs, sum_ref = refs[2 * len(pairs) : -1], refs[-1]
        at = 0
        for index, size in enumerate(widths):
            for start in range(0, size, 128):
                near = pl.ds(start, 128)
                total = refs[2 * index][:, near].astype(F32) + refs[2 * index + 1][:, near].astype(F32)
                sum_ref[:, :, pl.ds(at + start, 128)] = total.reshape(many, rows, 128)
            at += size
        far = lax.shift_right_logical(place_ref[0], 1)
        for step, ref in enumerate(out_refs):
            ref[...] = sum_ref[far ^ step].astype(LOW)

    return pl.pallas_call(
        kernel,
        in_specs=[pl.BlockSpec(memory_space=pltpu.SMEM)]
        + [pl.BlockSpec(memory_space=pltpu.VMEM)] * (2 * len(pairs)),
        out_shape=[struct((rows, lanes), LOW)] * many,
        scratch_shapes=[vmem((many, rows, lanes), F32)],
        compiler_params=pltpu.CompilerParams(vmem_limit_bytes=MEMORY),
    )(place, *(part for pair in pairs for part in pair))


def write_gradients(place, found, depth, width, hidden):
    rows = GROUPS[2]
    height = hidden // DEVICES
    middle = width + 2 * hidden + width + hidden // 8
    last = found[0].shape[1] - 3 * width - 128

    def kernel(place_ref, *refs):
        found_refs, refs = refs[: len(found)], refs[len(found) :]
        gwq_ref, gab_ref, gwo_ref, gwi_ref, gbi_ref, gwf_ref, gain_ref, shift_ref = refs
        spot = place_ref[0]

        def total(refs, at, columns):
            value = refs[0][:, pl.ds(at, columns)].astype(F32)
            for ref in refs[1:]:
                value = value + ref[:, pl.ds(at, columns)].astype(F32)
            return value

        def own(block, size):
            return pltpu.roll(block, block.shape[1] - spot * size, 1)

        def unfolded(block, count):
            return jnp.concatenate([block[step : step + 1] for step in range(count)], 1)

        for layer, refs, at in ((0, found_refs, last), (1, found_refs, middle)):
            gwq_ref[layer] = total(refs, at, 3 * width)
            block = total(refs, at + 3 * width, 128)
            many = width // 128
            for index in range(2):
                line = unfolded(block[index * many : (index + 1) * many], many)
                gab_ref[layer, pl.ds(index, 1)] = own(line, rows)[:, 0:rows]
        for layer, refs, at in ((0, found_refs, middle + 3 * width + 128), (1, found_refs, 0)):
            gwo_ref[layer] = total(refs, at, width)
            gwi_ref[layer] = total(refs, at + width, hidden)
            for step in range(hidden // width):
                gwf_ref[layer, pl.ds(step * rows, rows)] = total(
                    refs, at + width + hidden + step * width, width
                )
            at += width + 2 * hidden
            small = own(total(refs, at, width), rows)
            gain_ref[layer] = small[2:4, 0:rows]
            shift_ref[layer] = small[4:8, 0:rows]
            line = unfolded(total(refs, at + width, hidden // 8), 8)
            gbi_ref[pl.ds(layer, 1)] = own(line, height)[:, 0:height]

    outs = [
        struct((depth, rows, 3 * width), F32),
        struct((depth, 2, rows), F32),
        struct((depth, rows, width), F32),
        struct((depth, rows, hidden), F32),
        struct((depth, height), F32),
        struct((depth, height, width), F32),
        struct((depth, 2, rows), F32),
        struct((depth, 4, rows), F32),
    ]
    return pl.pallas_call(
        kernel,
        in_specs=[pl.BlockSpec(memory_space=pltpu.SMEM)]
        + [pl.BlockSpec(memory_space=pltpu.VMEM)] * len(found),
        out_shape=outs,
        compiler_params=pltpu.CompilerParams(vmem_limit_bytes=MEMORY),
    )(place, *found)


def exchange(parts, axis):
    return lax.all_to_all(parts, axis, 0, 0, tiled=True)


def swap(part, axis, step):
    size = lax.axis_size(axis)
    return lax.ppermute(part, axis, [(source, source ^ step) for source in range(size)])


def local(
    hidden_in,
    lengths,
    grad_out,
    attn_weight,
    attn_bias,
    out_weight,
    ffn_in,
    ffn_in_bias,
    ffn_out,
    norm_gain,
    shifts,
):
    depth, rows, width = out_weight.shape
    hidden = ffn_in.shape[2]
    first, second = lax.axis_size("dp"), lax.axis_size("fsdp")
    fits = (second, first, rows) == GROUPS
    urgent_size = 3 * width + 128
    if fits:
        early, later = pack_parameters(
            attn_weight, attn_bias, out_weight, ffn_in, ffn_in_bias, ffn_out, norm_gain, shifts
        )
        across = lax.axis_index("dp").astype(jnp.int32).reshape(1)
        place = lax.axis_index("fsdp").astype(jnp.int32).reshape(1)
        partners = range(1, second)
        x0, dz1 = rotate_kernel(lengths, (hidden_in, grad_out))
        early = hold(exchange(early, "dp"), (x0,))
        urgent = early[:, :urgent_size]
        urgent = [urgent] + [swap(urgent, "fsdp", step) for step in partners]
        raw0 = early[:, urgent_size:]
        raw0 = [raw0, swap(raw0, "fsdp", 1), swap(raw0, "fsdp", 2)]
    else:
        urgent, raw0, raw1 = gather_other(
            attn_weight, attn_bias, out_weight, ffn_in, ffn_in_bias, ffn_out, norm_gain, shifts
        )
        urgent, raw0, raw1 = ([part[step] for step in range(4)] for part in (urgent, raw0, raw1))
        place = jnp.zeros((1,), jnp.int32)
        x0, dz1 = rotate_kernel(lengths, (hidden_in, grad_out))

    qa0, ka0, va0, ob0, lse0, urgent = first_kernel(lengths, x0, place, urgent)
    if fits:
        raw0[2] = hold(raw0[2], (ob0,))
        raw0.append(swap(raw0[2], "fsdp", 1))
        later = exchange(hold(later, (ob0,)), "dp")
    n1, n2, inv, yb, gb, gp, z0 = dense_kernel(
        0, lengths, x0, ob0, place, urgent, raw0, 3 * width, hidden
    )
    if fits:
        raw1 = hold(later, (z0,))
        raw1 = [raw1, swap(raw1, "fsdp", 1), swap(raw1, "fsdp", 2)]
    qa1, ka1, va1, ob1, lse1 = attention_kernel(1, lengths, z0, place, urgent, raw0, 0)
    if fits:
        raw1[2] = hold(raw1[2], (ob1,))
        raw1.append(swap(raw1[2], "fsdp", 1))
    z1, dr1, dob1, *sent_a = turn_kernel(
        1, lengths, z0, ob1, dz1, place, urgent, raw1, 0, hidden
    )
    dr0, dob0, *sent_b = middle_kernel(
        lengths,
        (z0, dob1, ob1, qa1, ka1, va1, lse1, dr1),
        (n1, n2, inv, yb, gb, gp, ob0),
        place,
        urgent,
        raw0,
        hidden,
        (sent_a[0],),
    )
    if fits:
        got_a = [sent_a[0]] + [swap(sent_a[step], "fsdp", step) for step in partners]
        keep_a, give_a = add_parts(across, got_a, True, (sent_b[0],))
        got_ax = swap(give_a, "dp", 1)
        ready = (sent_b[0], keep_a)
    else:
        ready = ()
    dqkv, *sent_c = last_kernel(
        lengths, (x0, dob0, ob0, qa0, ka0, va0, lse0), ready, place
    )
    hidden_out, grad_in = tokens_kernel(lengths, z1, dqkv, dr0, urgent)
    if fits:
        got_b = [sent_b[0]] + [swap(sent_b[step], "fsdp", step) for step in partners]
        got_c = [sent_c[0]] + [swap(sent_c[step], "fsdp", step) for step in partners]
        keep_b, give_b = add_parts(across, got_b, True, (got_ax, grad_in))
        keep_c, give_c = add_parts(across, got_c, True)
        pairs = [(keep_a, got_ax), (keep_b, swap(give_b, "dp", 1)), (keep_c, swap(give_c, "dp", 1))]
        found = add_halves(across, pairs)
        found = [found[0]] + [swap(found[step], "dp", 2 * step) for step in range(1, first // 2)]
        spot = lax.axis_index(("dp", "fsdp")).astype(jnp.int32).reshape(1)
        grads = write_gradients(spot, found, depth, width, hidden)
    else:
        grads = scatter_other(
            *(jnp.stack(part) for part in (sent_a, sent_b, sent_c)), rows, width, hidden
        )
    return (hidden_out, grad_in, *grads)


def gather_other(
    attn_weight, attn_bias, out_weight, ffn_in, ffn_in_bias, ffn_out, norm_gain, shifts
):
    axes = ("dp", "fsdp")
    gather = lambda part, axis: lax.all_gather(part, axes, axis=axis, tiled=True)
    depth, unused, width = out_weight.shape
    hidden = ffn_in.shape[2]
    outer, inner, rows = GROUPS
    vectors = gather(jnp.concatenate([attn_bias, norm_gain, shifts], 1), 2)
    line = gather(ffn_in_bias, 1)

    def order(natural):
        return (
            natural.reshape(inner, outer, rows, -1).swapaxes(0, 1).reshape(outer, inner * rows, -1)
        )

    def stacked(part):
        part = part.reshape(DEVICES, -1, rows, width)
        return order(part.swapaxes(1, 2).reshape(width, -1))

    small = vectors.reshape(depth, 8, DEVICES, rows).transpose(2, 1, 0, 3).reshape(width, -1)
    line = line.reshape(depth, DEVICES, -1).swapaxes(0, 1)
    line = jnp.pad(line, ((0, 0), (0, 8 - depth), (0, 0))).reshape(width, -1)
    small = jnp.concatenate([small, line], 1)
    small = jnp.pad(small, ((0, 0), (0, 128 - small.shape[1])))
    wq, wo, wi, wf = (gather(part, 1) for part in (attn_weight, out_weight, ffn_in, ffn_out))
    urgent = jnp.concatenate([order(wq[0]), order(small)], 2)
    raw0 = jnp.concatenate([order(wq[1]), order(wo[0]), order(wi[0]), stacked(wf[0])], 2)
    raw1 = jnp.concatenate([order(wo[1]), order(wi[1]), stacked(wf[1])], 2)
    return urgent, raw0, raw1


def scatter_other(sent_a, sent_b, sent_c, own_rows, width, hidden):
    outer, inner, rows = GROUPS
    axes = ("dp", "fsdp")

    def natural(part):
        return part.reshape(outer, inner, rows, -1).swapaxes(0, 1).reshape(width, -1).astype(F32)

    def cut(part, sizes):
        found, at = [], 0
        for size in sizes:
            found.append(part[:, at : at + size])
            at += size
        return found

    dense = [width, hidden, hidden, width, hidden // 8]
    attention = [3 * width, 128]
    wq0, ab0 = cut(natural(sent_c), attention)
    wq1, ab1, wo0, wi0, wf0, small0, bi0 = cut(natural(sent_b), attention + dense)
    wo1, wi1, wf1, small1, bi1 = cut(natural(sent_a), dense)

    def stacked(part):
        part = part.reshape(DEVICES, rows, -1, width).swapaxes(1, 2)
        return part.reshape(hidden, width)

    def spread(parts, axis):
        return lax.psum_scatter(jnp.stack(parts), axes, scatter_dimension=axis, tiled=True)

    return (
        spread([wq0, wq1], 1),
        spread([ab0[:4].reshape(2, width), ab1[:4].reshape(2, width)], 2),
        spread([wo0, wo1], 1),
        spread([wi0, wi1], 1),
        spread([bi0[:8].reshape(-1), bi1[:8].reshape(-1)], 1),
        spread([stacked(wf0), stacked(wf1)], 1),
        spread([small0[2:4], small1[2:4]], 2),
        spread([small0[4:8], small1[4:8]], 2),
    )


def solution(mesh):
    placed = (
        P(("dp", "fsdp"), None),
        P(("dp", "fsdp"), None),
        P(("dp", "fsdp"), None),
        P(None, ("dp", "fsdp"), None),
        P(None, None, ("dp", "fsdp")),
        P(None, ("dp", "fsdp"), None),
        P(None, ("dp", "fsdp"), None),
        P(None, ("dp", "fsdp")),
        P(None, ("dp", "fsdp"), None),
        P(None, None, ("dp", "fsdp")),
        P(None, None, ("dp", "fsdp")),
    )
    return jax.shard_map(
        local,
        mesh=mesh,
        in_specs=placed,
        out_specs=(
            P(("dp", "fsdp"), None),
            P(("dp", "fsdp"), None),
            P(None, ("dp", "fsdp"), None),
            P(None, None, ("dp", "fsdp")),
            P(None, ("dp", "fsdp"), None),
            P(None, ("dp", "fsdp"), None),
            P(None, ("dp", "fsdp")),
            P(None, ("dp", "fsdp"), None),
            P(None, None, ("dp", "fsdp")),
            P(None, None, ("dp", "fsdp")),
        ),
        check_vma=False,
    )
```

```python
from functools import partial

import jax
import jax.numpy as jnp
from jax import lax
from jax.experimental import pallas as pl
from jax.experimental.pallas import tpu as pltpu
from jax.sharding import PartitionSpec as P

HEADS = 4
HD = 64
SEQ = 512
PAIR = 2 * HD
EXTRA = 16
HALF = SEQ // 2
HALVES = (slice(0, HALF), slice(HALF, SEQ))
FAR = -(2.0**100)
FLOOR = -1e20
EPSILON = 1e-12
PIECE = 256
SMALL = 128
GROUPS = (4, 8, 8)
DEVICES = 32
LOW = jnp.bfloat16
F32 = jnp.float32
MEMORY = 2**26


def dot_nn(left, right):
    return lax.dot_general(left, right, (((1,), (0,)), ((), ())), preferred_element_type=F32)


def dot_nt(left, right):
    return lax.dot_general(left, right, (((1,), (1,)), ((), ())), preferred_element_type=F32)


def dot_tn(left, right):
    return lax.dot_general(left, right, (((0,), (0,)), ((), ())), preferred_element_type=F32)


def pieces(total, size=PIECE):
    return [pl.ds(start, size) for start in range(0, total, size)]


def three_parts(values):
    first = values.astype(LOW).astype(F32)
    rest = values - first
    second = rest.astype(LOW).astype(F32)
    return first, second, rest - second


CURVE = (7.97869556e-01, 3.63928094e-02, -8.82195179e-05, -3.66000319e-05, 1.41853144e-06)
BELL = -0.5 / 0.6931471805599453


def gelu_parts(u):
    square = u * u
    curve = CURVE[-1]
    for factor in CURVE[-2::-1]:
        curve = curve * square + factor
    cumulative = 0.5 + 0.5 * jnp.tanh(u * curve)
    slope = cumulative + (u * 0.3989422804014327) * jnp.exp2(square * BELL)
    return u * cumulative, slope


def inverse_of(values):
    guess = pl.reciprocal(values, approx=True)
    return guess * (2.0 - values * guess)


def longest_start(lengths_ref, row):
    begin, found = jnp.int32(0), jnp.int32(0)
    for entry in range(lengths_ref.shape[1]):
        size = lengths_ref[row, entry]
        found = jnp.where(size == HALF, begin, found)
        begin = begin + size
    return found


def segments(lengths_ref, row):
    places = lax.broadcasted_iota(jnp.int32, (1, SEQ), 1) + longest_start(lengths_ref, row)
    places = places & (SEQ - 1)
    bound = jnp.int32(0)
    segment = jnp.zeros((1, SEQ), jnp.int32)
    last = lengths_ref.shape[1] - 1
    for entry in range(last):
        bound = bound + lengths_ref[row, entry]
        segment = segment + (places >= bound).astype(jnp.int32)
    return segment, last


def head_rows(head):
    return slice(head * HD, (head + 1) * HD)


def attention_forward(row, lengths_ref, x, wt_ref, bias_ref, qa_ref, ka_ref, va_ref, ob_ref, lse_ref, s_ref, p_ref):
    width = HEADS * HD
    segment, last = segments(lengths_ref, row)
    pad = (segment == last).astype(F32)
    line = lax.broadcasted_iota(jnp.int32, (EXTRA, SEQ), 0)
    aug_q = jnp.where(line == segment, 1.0, 0.0).astype(LOW)
    seen = (line == segment) & (segment != last)
    aug_k = jnp.where(seen | (line > last), 0.0, FAR).astype(LOW)
    aug_v = jnp.where(line == 0, 1.0, 0.0).astype(LOW)
    rest = jnp.zeros((PAIR - HD - EXTRA, SEQ), LOW)
    for head in range(HEADS):
        qa_ref[head, HD : HD + EXTRA] = aug_q
        ka_ref[head, HD : HD + EXTRA] = aug_k
        va_ref[head, HD : HD + EXTRA] = aug_v
        qa_ref[head, HD + EXTRA : PAIR] = rest
        ka_ref[head, HD + EXTRA : PAIR] = rest
    for block, ref in enumerate((qa_ref, ka_ref, va_ref)):
        lines = slice(block * width, (block + 1) * width)
        bias = bias_ref[lines]
        value = dot_nt(wt_ref[lines], x) + jnp.concatenate([bias] * (SEQ // 128), 1)
        if block == 0:
            value = value * HD**-0.5
        value = value.astype(LOW)
        for head in range(HEADS):
            ref[head, 0:HD] = value[head_rows(head)]
        yield

    def scores(head):
        for half in HALVES:
            s_ref[head % 2, half] = dot_tn(ka_ref[head, :, half], qa_ref[head, :, half])

    def softmax(head):
        tops = []
        for half in HALVES:
            tops.append(jnp.maximum(jnp.max(s_ref[head % 2, half], 0, keepdims=True), FLOOR))
            p_ref[head % 2, half] = jnp.exp(s_ref[head % 2, half] - tops[-1]).astype(LOW)
        return tops

    scores(0)
    yield
    for head in range(HEADS):
        if head + 1 < HEADS:
            scores(head + 1)
            yield
        tops = softmax(head)
        yield
        for half, top in zip(HALVES, tops):
            out = dot_nn(va_ref[head, :, half], p_ref[head % 2, half])
            alone = pad[:, half]
            total = out[HD : HD + 1] + alone
            lse_ref[head : head + 1, half] = jnp.where(alone > 0, 0.0, top + jnp.log(total))
            own = alone * va_ref[head, 0:HD, half].astype(F32)
            ob_ref[head_rows(head), half] = (out[0:HD] * inverse_of(total) + own).astype(LOW)
        yield


def normal(values):
    centred = values - jnp.mean(values, -1, keepdims=True)
    inverse = lax.rsqrt(jnp.mean(centred * centred, -1, keepdims=True) + EPSILON)
    return centred * inverse, inverse


def normal_back(cotangent, unit, inverse, gains):
    scaled = cotangent * gains
    return inverse * (
        scaled
        - jnp.mean(scaled, -1, keepdims=True)
        - unit * jnp.mean(scaled * unit, -1, keepdims=True)
    )


def dense_forward(x_ref, ob_ref, wo_ref, wi_ref, wf_ref, small_ref, bi_ref, n1_ref, n2_ref, inv_ref, yb_ref, gb_ref, gp_ref, z_ref, work_ref, u_ref):
    small = lambda index: small_ref[pl.ds(index, 1)]
    work_ref[...] = dot_tn(ob_ref[...], wo_ref[...])
    yield
    for place in pieces(SEQ):
        unit, inverse = normal(x_ref[place].astype(F32) + work_ref[place] + small(4))
        n1_ref[place] = unit
        inv_ref[place, pl.ds(0, HD)] = jnp.broadcast_to(inverse, (PIECE, HD))
        y = unit * small(2) + small(5)
        yb_ref[place] = y.astype(LOW)
        work_ref[place] = y + small(6)
        yield
    columns = 256
    count = wi_ref.shape[1] // columns

    def into(step):
        u_ref[step % 2] = dot_nn(yb_ref[...], wi_ref[:, pl.ds(step * columns, columns)])

    into(0)
    yield
    for step in range(count):
        if step + 1 < count:
            into(step + 1)
            yield
        lanes = pl.ds(step * columns, columns)
        for place in pieces(SEQ, SMALL):
            g, slope = gelu_parts(u_ref[step % 2, place] + bi_ref[:, lanes])
            gb_ref[place, lanes] = g.astype(LOW)
            gp_ref[place, lanes] = slope.astype(LOW)
            yield
    work_ref[...] += dot_nn(gb_ref[...], wf_ref[...])
    yield
    for place in pieces(SEQ):
        unit, inverse = normal(work_ref[place])
        n2_ref[place] = unit
        inv_ref[place, pl.ds(HD, HD)] = jnp.broadcast_to(inverse, (PIECE, HD))
        z_ref[place] = (unit * small(3) + small(7)).astype(z_ref.dtype)
        yield


def fold(values):
    return jnp.sum(values.reshape(-1, 8, values.shape[-1]), 0)


def dense_backward(dz_ref, n1_ref, n2_ref, inv_ref, yb_ref, gb_ref, gp_ref, ob_ref, wo_ref, wi_ref, wf_ref, small_ref, dr_ref, dob_ref, gwo_ref, gwi_ref, gwf_ref, gsmall_ref, gbi_ref, low_ref, u_ref, du_ref, turned_ref):
    small = lambda index: small_ref[pl.ds(index, 1)]
    for place in pieces(SEQ):
        dz = dz_ref[place].astype(F32)
        unit = n2_ref[place]
        gsmall_ref[3] += fold(dz * unit)
        gsmall_ref[7] += fold(dz)
        dr = normal_back(dz, unit, inv_ref[place, pl.ds(HD, 1)], small(3))
        dr_ref[place] = dr
        df = dr.astype(LOW)
        low_ref[place] = df
        gsmall_ref[6] += fold(df.astype(F32))
        yield
    columns = 256
    count = wi_ref.shape[1] // columns

    def back(step):
        u_ref[step % 2] = dot_nt(low_ref[...], wf_ref[pl.ds(step * columns, columns)])

    back(0)
    turned_ref[0] = low_ref[...].T
    turned_ref[1] = yb_ref[...].T
    yield
    for step in range(count):
        if step + 1 < count:
            back(step + 1)
            yield
        lanes = pl.ds(step * columns, columns)
        gwf_ref[:, lanes] += dot_nn(turned_ref[0], gb_ref[:, lanes])
        yield
        for place in pieces(SEQ, SMALL):
            du = (u_ref[step % 2, place] * gp_ref[place, lanes].astype(F32)).astype(LOW)
            du_ref[place, lanes] = du
            gbi_ref[:, lanes] += fold(du.astype(F32))
        yield
        gwi_ref[:, lanes] += dot_nn(turned_ref[1], du_ref[:, lanes])
        yield
    u_ref[0] = dot_nt(du_ref[...], wi_ref[...])
    yield
    for place in pieces(SEQ):
        dy = dr_ref[place] + u_ref[0, place]
        unit = n1_ref[place]
        gsmall_ref[2] += fold(dy * unit)
        gsmall_ref[5] += fold(dy)
        dr = normal_back(dy, unit, inv_ref[place, pl.ds(0, 1)], small(2))
        dr_ref[place] = dr
        da = dr.astype(LOW)
        low_ref[place] = da
        gsmall_ref[4] += fold(da.astype(F32))
        yield
    gwo_ref[...] += dot_nn(ob_ref[...], low_ref[...])
    dob_ref[...] = dot_nt(wo_ref[...], low_ref[...]).astype(LOW)
    yield


def attention_backward(row, lengths_ref, x, do_ref, ob_ref, qa_ref, ka_ref, va_ref, lse_ref, dqkv_ref, gwq_ref, gbias_ref, p_ref, ds_ref, s_ref):
    width = HEADS * HD
    segment, last = segments(lengths_ref, row)
    pad = (segment == last).astype(F32)

    def scores(head):
        for half in HALVES:
            s_ref[0, head % 2, half] = dot_tn(ka_ref[head, :, half], qa_ref[head, :, half])
            s_ref[1, head % 2, half] = dot_tn(
                va_ref[head, 0:HD, half], do_ref[head_rows(head), half]
            )

    def weigh(head):
        product = do_ref[head_rows(head)].astype(F32) * ob_ref[head_rows(head)].astype(F32)
        centre = jnp.sum(product, 0, keepdims=True)
        for half in HALVES:
            p = jnp.exp(s_ref[0, head % 2, half] - lse_ref[head : head + 1, half])
            p_ref[head % 2, half] = p.astype(LOW)
            ds_ref[head % 2, half] = (p * (s_ref[1, head % 2, half] - centre[:, half])).astype(LOW)

    scores(0)
    yield
    for head in range(HEADS):
        if head + 1 < HEADS:
            scores(head + 1)
            yield
        weigh(head)
        yield
        for half in HALVES:
            ds, do = ds_ref[head % 2, half], do_ref[head_rows(head), half]
            dq = dot_nn(ka_ref[head, 0:HD, half], ds) * HD**-0.5
            dk = dot_nt(qa_ref[head, 0:HD, half], ds)
            dv = dot_nt(do, p_ref[head % 2, half]) + pad[:, half] * do.astype(F32)
            for block, value in enumerate((dq, dk, dv)):
                at = block * width + head * HD
                dqkv_ref[at : at + HD, half] = value.astype(LOW)
        yield
    for index, block in enumerate((0, 2)):
        value = dqkv_ref[block * width : (block + 1) * width].astype(F32)
        parts = [value[:, at : at + 128] for at in range(0, SEQ, 128)]
        gbias_ref[index] += (parts[0] + parts[1]) + (parts[2] + parts[3])
    gwq_ref[...] += dot_nn(dqkv_ref[...], x)
    yield


def unpack_matrix(raw_ref, at, into_ref):
    width = into_ref.shape[0]
    for start in range(0, into_ref.shape[1], width):
        block = raw_ref[:, :, pl.ds(at + start, width)].astype(F32)
        block = block.reshape(GROUPS + (width,)).swapaxes(0, 1).reshape(width, width)
        into_ref[:, pl.ds(start, width)] = block.astype(LOW)


def unpack_stacked(raw_ref, at, into_ref):
    width = into_ref.shape[1]
    count = into_ref.shape[0] // width
    blocks = [
        raw_ref[:, :, pl.ds(at + step * width, width)].astype(F32).reshape(GROUPS + (width,))
        for step in range(count)
    ]
    outer, inner, rows = GROUPS
    for place in range(inner):
        part = jnp.stack([jnp.stack([block[f, place] for block in blocks]) for f in range(outer)])
        size = outer * count * rows
        into_ref[pl.ds(place * size, size)] = part.reshape(size, width).astype(LOW)


def counter(shape, axis):
    return lax.broadcasted_iota(jnp.int32, shape, axis)


def split_by(values, size):
    return lax.shift_right_logical(values, size.bit_length() - 1), values & (size - 1)


def sources(rows):
    outer, inner, height = GROUPS
    group, within = split_by(counter((rows, 1), 0), height)
    far, near = split_by(group, inner)
    return near * outer + far, within


def unpack_vectors(raw_ref, at, layer):
    outer, inner, rows = GROUPS
    total = outer * inner * rows
    raw = raw_ref[:, :, pl.ds(at, 128)].reshape(total, 128)
    owner, place = split_by(counter((1, total), 1), rows)
    pick = jnp.where(counter((128, 1), 0) == rows * layer + place, 1.0, 0.0).astype(LOW)
    device, unused = sources(total)
    spread = jnp.where(owner == device, dot_nn(raw, pick), 0.0)
    return jnp.sum(spread.reshape(outer * inner, rows, total), 0)


def unpack_hidden(raw_ref, at, layer, hidden):
    outer, inner, rows = GROUPS
    total = outer * inner * rows
    raw = raw_ref[:, :, pl.ds(at, 128)].reshape(total, 128)
    owner, place = split_by(counter((1, hidden), 1), hidden // (outer * inner))
    pick = jnp.where(counter((128, 1), 0) == 2 * rows + place, 1.0, 0.0).astype(LOW)
    device, within = sources(total)
    device = jnp.where(within == layer, device, -1)
    spread = jnp.where(owner == device, dot_nn(raw, pick), 0.0)
    return jnp.sum(spread, 0, keepdims=True)


def pack_matrix(sum_ref, sent_ref, at, turned=False):
    width = sum_ref.shape[1 if turned else 0]
    outer, inner, rows = GROUPS
    for start in range(0, sum_ref.shape[0 if turned else 1], width):
        near = pl.ds(start, width)
        block = sum_ref[near].T if turned else sum_ref[:, near]
        block = block.reshape(inner, outer, rows, width)
        block = block.swapaxes(0, 1).reshape(outer, inner * rows, width)
        sent_ref[:, :, pl.ds(at + start, width)] = block.astype(LOW)


def pack_stacked(sum_ref, sent_ref, at):
    width = sum_ref.shape[0]
    outer, inner, rows = GROUPS
    count = sum_ref.shape[1] // width
    near = inner // count
    for step in range(count):
        block = sum_ref[:, pl.ds(step * width, width)].T
        block = block.reshape(near, outer, count, rows, width)
        for part in range(count):
            piece = jnp.stack([block[:, f, part] for f in range(outer)])
            piece = piece.reshape(outer, near * rows, width)
            sent_ref[:, pl.ds(step * near * rows, near * rows), pl.ds(at + part * width, width)] = (
                piece.astype(LOW)
            )


def pack_shared(block, sent_ref, at):
    outer, inner, rows = GROUPS
    columns = block.shape[1]
    block = jnp.broadcast_to(block[None], (outer * inner, rows, columns))
    sent_ref[:, :, pl.ds(at, columns)] = block.reshape(outer, inner * rows, columns).astype(LOW)


def folded(line, lanes):
    return [line[:, at : at + lanes] for at in range(0, line.shape[1], lanes)]


def pack_attention(gwq_ref, gbias_ref, sent_ref, at):
    pack_matrix(gwq_ref, sent_ref, at, True)
    width = gwq_ref.shape[1]
    parts = []
    for index in range(2):
        parts += folded(jnp.sum(gbias_ref[index].T, 0, keepdims=True), 128)
    block = jnp.concatenate(parts + [jnp.zeros((8 - len(parts), 128), F32)], 0)
    pack_shared(block, sent_ref, at + 3 * width)


def pack_dense(gwo_ref, gwi_ref, gwf_ref, gsmall_ref, gbi_ref, sent_ref, at):
    width, hidden = gwi_ref.shape
    pack_matrix(gwo_ref, sent_ref, at)
    pack_matrix(gwi_ref, sent_ref, at + width)
    pack_stacked(gwf_ref, sent_ref, at + width + hidden)
    at = at + width + 2 * hidden
    pack_shared(jnp.sum(gsmall_ref[...], 1), sent_ref, at)
    line = jnp.sum(gbi_ref[...], 0, keepdims=True)
    pack_shared(jnp.concatenate(folded(line, hidden // 8), 0), sent_ref, at + width)


def shape_of(array):
    return jax.ShapeDtypeStruct(array.shape, array.dtype)


def by_row(shape, group):
    if len(shape) == 2:
        return pl.BlockSpec((group * SEQ, shape[1]), lambda step: (step, 0))
    return pl.BlockSpec((group,) + tuple(shape[1:]), lambda step: (step,) + (0,) * (len(shape) - 1))


def one_row(ref, member):
    if len(ref.shape) == 2:
        return ref.at[pl.ds(member * SEQ, SEQ)]
    return ref.at[member]


def alternate(runs):
    running = []
    waiting = list(runs)
    while running or waiting:
        if waiting:
            running.append(waiting.pop(0))
        for run in list(running):
            try:
                next(run)
            except StopIteration:
                running.remove(run)


def whole(shape):
    return pl.BlockSpec(tuple(shape), lambda row: (0,) * len(shape))


def run_rows(
    body, lengths, rowwise, fixed, row_outs, sent, shared, private, cost, setup, finish, after=(),
    scalars=(), group=1
):
    count = lengths.shape[0]
    group = group if count % group == 0 else 1
    cuts = [len(scalars), len(rowwise), len(fixed), len(after), len(row_outs), len(sent)]
    cuts += [len(shared)] + [len(private)] * group

    def kernel(lengths_ref, *refs):
        step = pl.program_id(0)
        groups = []
        at = 0
        for cut in cuts:
            groups.append(refs[at : at + cut])
            at += cut
        numbers, rows_in, fixed_in, unused, rows_out, sent_out, work = groups[:7]

        @pl.when(step == 0)
        def _():
            setup(numbers, fixed_in, sent_out, work)

        alternate(
            body(
                step * group + member,
                lengths_ref,
                [one_row(ref, member) for ref in rows_in],
                [one_row(ref, member) for ref in rows_out],
                work,
                groups[7 + member],
            )
            for member in range(group)
        )

        if finish:

            @pl.when(step == count // group - 1)
            def _():
                finish(numbers, work, sent_out)

    return pl.pallas_call(
        kernel,
        grid=(count // group,),
        in_specs=[pl.BlockSpec(memory_space=pltpu.SMEM)] * (1 + len(scalars))
        + [by_row(array.shape, group) for array in rowwise]
        + [whole(array.shape) for array in fixed]
        + [pl.BlockSpec(memory_space=pl.ANY) for array in after],
        out_specs=[by_row(part.shape, group) for part in row_outs]
        + [whole(part.shape) for part in sent],
        out_shape=list(row_outs) + list(sent),
        scratch_shapes=list(shared) + list(private) * group,
        compiler_params=pltpu.CompilerParams(
            dimension_semantics=("arbitrary",), vmem_limit_bytes=MEMORY
        ),
        cost_estimate=pl.CostEstimate(flops=cost, bytes_accessed=8 * 2**20, transcendentals=0),
    )(lengths, *scalars, *rowwise, *fixed, *after)


def struct(shape, dtype):
    return jax.ShapeDtypeStruct(tuple(shape), dtype)


FORWARD_SCRATCH = lambda: [
    pltpu.VMEM((2, SEQ, HALF), F32),
    pltpu.VMEM((2, SEQ, HALF), LOW),
]
BACKWARD_SCRATCH = lambda: [
    pltpu.VMEM((2, SEQ, HALF), LOW),
    pltpu.VMEM((2, SEQ, HALF), LOW),
    pltpu.VMEM((2, 2, SEQ, HALF), F32),
    pltpu.VMEM((3 * HEADS * HD, SEQ), LOW),
]


def attention_outs(rows, width):
    return [
        struct((rows, HEADS, PAIR, SEQ), LOW),
        struct((rows, HEADS, PAIR, SEQ), LOW),
        struct((rows, HEADS, HD + EXTRA, SEQ), LOW),
        struct((rows, width, SEQ), LOW),
        struct((rows, 8, SEQ), F32),
    ]


def dense_outs(tokens, width, hidden):
    return [
        struct((tokens, width), F32),
        struct((tokens, width), F32),
        struct((tokens, PAIR), F32),
        struct((tokens, width), LOW),
        struct((tokens, hidden), LOW),
        struct((tokens, hidden), LOW),
    ]


def vmem(shape, dtype):
    return pltpu.VMEM(tuple(shape), dtype)


def attention_weights(width):
    return [vmem((width, 3 * width), LOW), vmem((3 * width, width), LOW), vmem((3 * width, 128), F32)]


def dense_weights(width, hidden):
    return [
        vmem((width, width), LOW),
        vmem((width, hidden), LOW),
        vmem((hidden, width), LOW),
        vmem((8, width), F32),
        vmem((1, hidden), F32),
    ]


def dense_sums(width, hidden):
    return [
        vmem((width, width), F32),
        vmem((width, hidden), F32),
        vmem((width, hidden), F32),
        vmem((8, 8, width), F32),
        vmem((8, hidden), F32),
    ]


def attention_sums(width):
    return [vmem((3 * width, width), F32), vmem((2, width, 128), F32)]


def dense_work(width, hidden):
    return [
        vmem((SEQ, width), LOW),
        vmem((2, SEQ, width), F32),
        vmem((SEQ, hidden), LOW),
        vmem((2, width, SEQ), LOW),
    ]


def set_attention(layer, urgent_ref, raw_ref, at, wq_ref, wt_ref, bias_ref):
    width = wq_ref.shape[0]
    unpack_matrix(raw_ref, at, wq_ref)
    vectors = unpack_vectors(urgent_ref, 3 * width, layer)
    for block, line in enumerate((vectors[0:1], jnp.zeros((1, width), F32), vectors[1:2])):
        lines = pl.ds(block * width, width)
        wt_ref[lines] = wq_ref[:, lines].astype(F32).T.astype(LOW)
        bias_ref[lines] = jnp.broadcast_to(line, (128, width)).T


def set_dense(layer, urgent_ref, raw_ref, at, wo_ref, wi_ref, wf_ref, small_ref, bi_ref):
    width, hidden = wi_ref.shape
    unpack_matrix(raw_ref, at, wo_ref)
    unpack_matrix(raw_ref, at + width, wi_ref)
    unpack_stacked(raw_ref, at + width + hidden, wf_ref)
    small_ref[...] = unpack_vectors(urgent_ref, 3 * width, layer)
    bi_ref[...] = unpack_hidden(urgent_ref, 3 * width, layer, hidden)


def clear(refs):
    for ref in refs:
        ref[...] = jnp.zeros(ref.shape, ref.dtype)


def assemble(place_ref, part_refs, into_ref):
    for step, ref in enumerate(part_refs):
        into_ref[place_ref[0] ^ step] = ref[...]


def raw_block(parts):
    return vmem((len(parts),) + parts[0].shape, LOW)


def turned_back(lengths_ref, row, values):
    return pltpu.roll(values, longest_start(lengths_ref, row), 0).astype(LOW)


def rotate_kernel(lengths, arrays):
    def body(row, lengths_ref, rowwise, outs, work, own):
        back = (SEQ - longest_start(lengths_ref, row)) & (SEQ - 1)
        for source, target in zip(rowwise, outs):
            target[...] = pltpu.roll(source[...].astype(F32), back, 0).astype(LOW)
            yield

    return run_rows(
        body, lengths, list(arrays), [], [struct(array.shape, LOW) for array in arrays], [], [], [],
        10**6, lambda *refs: None, None,
    )


def first_kernel(lengths, x, place, parts):
    rows, (tokens, width) = lengths.shape[0], x.shape

    def setup(numbers, fixed, sent, work):
        assemble(numbers[0], fixed, sent[0])
        set_attention(0, sent[0], sent[0], 0, *work)

    def body(row, lengths_ref, rowwise, outs, work, own):
        return attention_forward(row, lengths_ref, rowwise[0][...], *work[1:3], *outs, *own)

    return run_rows(
        body, lengths, [x], list(parts), attention_outs(rows, width),
        [struct((len(parts),) + parts[0].shape, LOW)],
        attention_weights(width), FORWARD_SCRATCH(), 4 * 10**9, setup, None, (), [place],
    )


def attention_kernel(layer, lengths, x, place, urgent, parts, at):
    rows, (tokens, width) = lengths.shape[0], x.shape

    def setup(numbers, fixed, sent, work):
        assemble(numbers[0], fixed[1:], work[3])
        set_attention(layer, fixed[0], work[3], at, *work[:3])

    def body(row, lengths_ref, rowwise, outs, work, own):
        return attention_forward(
            row, lengths_ref, rowwise[0][...].astype(LOW), *work[1:3], *outs, *own
        )

    return run_rows(
        body, lengths, [x], [urgent] + list(parts), attention_outs(rows, width), [],
        attention_weights(width) + [raw_block(parts)], FORWARD_SCRATCH(),
        4 * 10**9, setup, None, (), [place],
    )


def dense_kernel(layer, lengths, x, ob, place, urgent, parts, at, hidden):
    tokens, width = x.shape

    def setup(numbers, fixed, sent, work):
        assemble(numbers[0], fixed[1:], work[5])
        set_dense(layer, fixed[0], work[5], at, *work[:5])

    def body(row, lengths_ref, rowwise, outs, work, own):
        return dense_forward(*rowwise, *work[:5], *outs, *own)

    return run_rows(
        body, lengths, [x, ob], [urgent] + list(parts),
        dense_outs(tokens, width, hidden) + [struct((tokens, width), F32)], [],
        dense_weights(width, hidden) + [raw_block(parts)],
        [vmem((SEQ, width), F32), vmem((2, SEQ, width), F32)],
        5 * 10**9, setup, None, (), [place],
    )


def turn_kernel(layer, lengths, x, ob, cotangent, place, urgent, parts, at, hidden):
    tokens, width = x.shape
    columns = width + 2 * hidden + width + hidden // 8

    def setup(numbers, fixed, sent, work):
        assemble(numbers[0], fixed[1:], work[11])
        set_dense(layer, fixed[0], work[11], at, *work[:5])
        clear(work[5:10])

    def body(row, lengths_ref, rowwise, outs, work, own):
        x_ref, ob_ref, dz_ref = rowwise
        z_ref, dr_ref, dob_ref = outs
        weights, sums = work[:5], work[5:10]
        kept, work_ref, back = own[:6], own[6], own[7:]
        yield from dense_forward(x_ref, ob_ref, *weights, *kept, z_ref, work_ref, back[1])
        yield from dense_backward(dz_ref, *kept, ob_ref, *weights[:4], dr_ref, dob_ref, *sums, *back)

    def finish(numbers, work, sent):
        pack_dense(*work[5:10], work[10], 0)
        hand_out(numbers[0], work[10], sent)

    kept = [vmem((SEQ,) + part.shape[1:], part.dtype) for part in dense_outs(tokens, width, hidden)]
    return run_rows(
        body, lengths, [x, ob, cotangent], [urgent] + list(parts),
        [struct((tokens, width), LOW), struct((tokens, width), F32), struct((tokens // SEQ, width, SEQ), LOW)],
        [struct((64, columns), LOW)] * 4,
        dense_weights(width, hidden) + dense_sums(width, hidden)
        + [vmem((4, 64, columns), LOW), raw_block(parts)],
        kept + [vmem((SEQ, width), F32)] + dense_work(width, hidden),
        10**10, setup, finish, (), [place], 2,
    )


def hand_out(place_ref, packed_ref, sent):
    for step, ref in enumerate(sent):
        ref[...] = packed_ref[place_ref[0] ^ step]


def middle_kernel(lengths, upper, lower, place, urgent, parts, hidden, after):
    tokens, width = upper[0].shape
    columns = 3 * width + 128 + width + 2 * hidden + width + hidden // 8

    def setup(numbers, fixed, sent, work):
        assemble(numbers[0], fixed[1:], work[16])
        set_attention(1, fixed[0], work[16], 0, *work[:3])
        set_dense(0, fixed[0], work[16], 3 * width, *work[3:8])
        clear(work[8:15])

    def body(row, lengths_ref, rowwise, outs, work, own):
        up, low = rowwise[:8], rowwise[8:]
        dx_ref = own[0]
        yield from attention_backward(
            row, lengths_ref, up[0][...].astype(LOW), *up[1:7], own[-1], *work[8:10], *own[5:-1]
        )
        dx_ref[...] = up[7][...] + dot_tn(own[-1][...], work[1][...])
        yield
        yield from dense_backward(dx_ref, *low, *work[3:7], *outs, *work[10:15], *own[1:5])

    def finish(numbers, work, sent):
        pack_attention(*work[8:10], work[15], 0)
        pack_dense(*work[10:15], work[15], 3 * width + 128)
        hand_out(numbers[0], work[15], sent)

    return run_rows(
        body, lengths, list(upper) + list(lower), [urgent] + list(parts),
        [struct((tokens, width), F32), struct((tokens // SEQ, width, SEQ), LOW)],
        [struct((64, columns), LOW)] * 4,
        attention_weights(width) + dense_weights(width, hidden)
        + attention_sums(width) + dense_sums(width, hidden)
        + [vmem((4, 64, columns), LOW), raw_block(parts)],
        [vmem((SEQ, width), F32)] + dense_work(width, hidden) + BACKWARD_SCRATCH(),
        15 * 10**9, setup, finish, after, [place], 2,
    )


def last_kernel(lengths, upper, after):
    tokens, width = upper[0].shape

    def setup(numbers, fixed, sent, work):
        clear(work[:2])

    def body(row, lengths_ref, rowwise, outs, work, own):
        return attention_backward(
            row, lengths_ref, rowwise[0][...], *rowwise[1:], outs[0], *work[:2], *own
        )

    def finish(numbers, work, sent):
        pack_attention(*work, sent[0], 0)

    return run_rows(
        body, lengths, list(upper), [], [struct((tokens // SEQ, 3 * width, SEQ), LOW)],
        [struct((4, 64, 3 * width + 128), LOW)],
        attention_sums(width), BACKWARD_SCRATCH()[:-1], 8 * 10**9, setup, finish, after, (), 2,
    )


def tokens_kernel(lengths, z, dqkv, dr, urgent):
    tokens, width = dr.shape

    def setup(numbers, fixed, sent, work):
        set_attention(0, fixed[0], fixed[0], 0, *work)

    def body(row, lengths_ref, rowwise, outs, work, own):
        z_ref, dqkv_ref, dr_ref = rowwise
        outs[0][...] = turned_back(lengths_ref, row, z_ref[...].astype(F32))
        yield
        dx = dr_ref[...] + dot_tn(dqkv_ref[...], work[1][...])
        outs[1][...] = turned_back(lengths_ref, row, dx)
        yield

    return run_rows(
        body, lengths, [z, dqkv, dr], [urgent], [struct((tokens, width), LOW)] * 2, [],
        attention_weights(width), [], 10**9, setup, None,
    )


def hold(array, after):
    def kernel(*refs):
        pass

    anywhere = pl.BlockSpec(memory_space=pl.ANY)
    return pl.pallas_call(
        kernel,
        in_specs=[anywhere] * (1 + len(after)),
        out_specs=anywhere,
        out_shape=shape_of(array),
        input_output_aliases={0: 0},
    )(array, *after)


def pack_parameters(
    attn_weight, attn_bias, out_weight, ffn_in, ffn_in_bias, ffn_out, norm_gain, shifts
):
    depth, rows, width = out_weight.shape
    copies = GROUPS[1]
    hidden = ffn_in.shape[2]
    dense = width + 2 * hidden
    height = ffn_in_bias.shape[1]

    def kernel(wq_ref, ab_ref, wo_ref, wi_ref, bi_ref, wf_ref, gain_ref, shift_ref, first_ref, rest_ref, small_ref):
        def put(ref, block, at):
            block = jnp.broadcast_to(block.astype(F32)[None], (copies,) + block.shape)
            block = block.reshape(copies * block.shape[1], block.shape[2])
            ref[:, pl.ds(at, block.shape[1])] = block.astype(LOW)

        small_ref[...] = jnp.zeros(small_ref.shape, F32)
        for layer in range(depth):
            lanes = pl.ds(rows * layer, rows)
            small_ref[0:2, lanes] = ab_ref[layer].astype(F32)
            small_ref[2:4, lanes] = gain_ref[layer].astype(F32)
            small_ref[4:8, lanes] = shift_ref[layer].astype(F32)
        small_ref[0:depth, pl.ds(2 * rows, height)] = bi_ref[...].astype(F32)
        put(first_ref, wq_ref[0], 0)
        put(first_ref, small_ref[...], 3 * width)
        put(first_ref, wq_ref[1], 3 * width + 128)
        for layer, ref, at in ((0, first_ref, 6 * width + 128), (1, rest_ref, 0)):
            put(ref, wo_ref[layer], at)
            put(ref, wi_ref[layer], at + width)
            at += width + hidden
            down = wf_ref[layer].astype(F32)
            for step in range(hidden // width):
                put(ref, down[step * rows : (step + 1) * rows], at)
                at += width

    return pl.pallas_call(
        kernel,
        in_specs=[pl.BlockSpec(memory_space=pltpu.VMEM)] * 8,
        out_shape=[
            struct((copies * rows, 6 * width + 128 + dense), LOW),
            struct((copies * rows, dense), LOW),
        ],
        scratch_shapes=[vmem((rows, 128), F32)],
        compiler_params=pltpu.CompilerParams(vmem_limit_bytes=MEMORY),
    )(attn_weight, attn_bias, out_weight, ffn_in, ffn_in_bias, ffn_out, norm_gain, shifts)


def add_parts(place, parts, halves, after=()):
    lanes = parts[0].shape[-1]
    count = len(parts)
    many, rows = GROUPS[1:]
    outs = 2 if halves else 1

    def kernel(place_ref, *refs):
        out_refs, sum_ref = refs[count + len(after) : -1], refs[-1]
        if len(refs[0].shape) == 3:
            in_refs = [refs[0].at[step] for step in range(refs[0].shape[0])]
        else:
            in_refs = refs[:count]
        bit = place_ref[0] & 1
        for start in range(0, lanes, 128):
            near = pl.ds(start, 128)
            total = in_refs[0][:, near].astype(F32)
            for ref in in_refs[1:]:
                total = total + ref[:, near].astype(F32)
            if halves:
                sum_ref[:, :, near] = total.reshape(many, rows, 128)
            else:
                out_refs[0][:, near] = total.astype(LOW)
        for side, ref in enumerate(out_refs if halves else ()):
            for start in range(0, lanes, 128):
                near = pl.ds(start, 128)
                block = [sum_ref[2 * step + (bit ^ side), :, near] for step in range(many // 2)]
                ref[:, near] = jnp.concatenate(block, 0).astype(LOW)

    return pl.pallas_call(
        kernel,
        in_specs=[pl.BlockSpec(memory_space=pltpu.SMEM)]
        + [pl.BlockSpec(memory_space=pltpu.VMEM)] * count
        + [pl.BlockSpec(memory_space=pl.ANY)] * len(after),
        out_shape=[struct((many * rows // outs, lanes), LOW)] * outs,
        scratch_shapes=[vmem((many, rows, lanes), F32)],
        compiler_params=pltpu.CompilerParams(vmem_limit_bytes=MEMORY),
    )(place, *parts, *after)


def add_halves(place, pairs, after=()):
    many, rows = GROUPS[1] // 2, GROUPS[2]
    widths = [pair[0].shape[1] for pair in pairs]
    lanes = sum(widths)

    def kernel(place_ref, *refs):
        out_refs, sum_ref = refs[2 * len(pairs) + len(after) : -1], refs[-1]
        at = 0
        for index, size in enumerate(widths):
            for start in range(0, size, 128):
                near = pl.ds(start, 128)
                total = refs[2 * index][:, near].astype(F32) + refs[2 * index + 1][:, near].astype(F32)
                sum_ref[:, :, pl.ds(at + start, 128)] = total.reshape(many, rows, 128)
            at += size
        far = lax.shift_right_logical(place_ref[0], 1)
        for step, ref in enumerate(out_refs):
            ref[...] = sum_ref[far ^ step].astype(LOW)

    return pl.pallas_call(
        kernel,
        in_specs=[pl.BlockSpec(memory_space=pltpu.SMEM)]
        + [pl.BlockSpec(memory_space=pltpu.VMEM)] * (2 * len(pairs))
        + [pl.BlockSpec(memory_space=pl.ANY)] * len(after),
        out_shape=[struct((rows, lanes), LOW)] * many,
        scratch_shapes=[vmem((many, rows, lanes), F32)],
        compiler_params=pltpu.CompilerParams(vmem_limit_bytes=MEMORY),
    )(place, *(part for pair in pairs for part in pair), *after)


def write_gradients(place, most, head, depth, width, hidden):
    rows = GROUPS[2]
    height = hidden // DEVICES
    middle = width + 2 * hidden + width + hidden // 8

    def kernel(place_ref, *refs):
        most_refs, refs = refs[: len(most)], refs[len(most) :]
        head_refs, refs = refs[: len(head)], refs[len(head) :]
        gwq_ref, gab_ref, gwo_ref, gwi_ref, gbi_ref, gwf_ref, gain_ref, shift_ref = refs
        spot = place_ref[0]

        def total(refs, at, columns):
            value = refs[0][:, pl.ds(at, columns)].astype(F32)
            for ref in refs[1:]:
                value = value + ref[:, pl.ds(at, columns)].astype(F32)
            return value

        def own(block, size):
            return pltpu.roll(block, block.shape[1] - spot * size, 1)

        def unfolded(block, count):
            return jnp.concatenate([block[step : step + 1] for step in range(count)], 1)

        for layer, refs, at in ((0, head_refs, 0), (1, most_refs, middle)):
            gwq_ref[layer] = total(refs, at, 3 * width)
            block = total(refs, at + 3 * width, 128)
            many = width // 128
            for index in range(2):
                line = unfolded(block[index * many : (index + 1) * many], many)
                gab_ref[layer, pl.ds(index, 1)] = own(line, rows)[:, 0:rows]
        for layer, refs, at in ((0, most_refs, middle + 3 * width + 128), (1, most_refs, 0)):
            gwo_ref[layer] = total(refs, at, width)
            gwi_ref[layer] = total(refs, at + width, hidden)
            for step in range(hidden // width):
                gwf_ref[layer, pl.ds(step * rows, rows)] = total(
                    refs, at + width + hidden + step * width, width
                )
            at += width + 2 * hidden
            small = own(total(refs, at, width), rows)
            gain_ref[layer] = small[2:4, 0:rows]
            shift_ref[layer] = small[4:8, 0:rows]
            line = unfolded(total(refs, at + width, hidden // 8), 8)
            gbi_ref[pl.ds(layer, 1)] = own(line, height)[:, 0:height]

    outs = [
        struct((depth, rows, 3 * width), F32),
        struct((depth, 2, rows), F32),
        struct((depth, rows, width), F32),
        struct((depth, rows, hidden), F32),
        struct((depth, height), F32),
        struct((depth, height, width), F32),
        struct((depth, 2, rows), F32),
        struct((depth, 4, rows), F32),
    ]
    return pl.pallas_call(
        kernel,
        in_specs=[pl.BlockSpec(memory_space=pltpu.SMEM)]
        + [pl.BlockSpec(memory_space=pltpu.VMEM)] * (len(most) + len(head)),
        out_shape=outs,
        compiler_params=pltpu.CompilerParams(vmem_limit_bytes=MEMORY),
    )(place, *most, *head)


def exchange(parts, axis):
    return lax.all_to_all(parts, axis, 0, 0, tiled=True)


def swap(part, axis, step):
    size = lax.axis_size(axis)
    return lax.ppermute(part, axis, [(source, source ^ step) for source in range(size)])


def local(
    hidden_in,
    lengths,
    grad_out,
    attn_weight,
    attn_bias,
    out_weight,
    ffn_in,
    ffn_in_bias,
    ffn_out,
    norm_gain,
    shifts,
):
    depth, rows, width = out_weight.shape
    hidden = ffn_in.shape[2]
    first, second = lax.axis_size("dp"), lax.axis_size("fsdp")
    fits = (second, first, rows) == GROUPS
    urgent_size = 3 * width + 128
    if fits:
        early, later = pack_parameters(
            attn_weight, attn_bias, out_weight, ffn_in, ffn_in_bias, ffn_out, norm_gain, shifts
        )
        across = lax.axis_index("dp").astype(jnp.int32).reshape(1)
        place = lax.axis_index("fsdp").astype(jnp.int32).reshape(1)
        partners = range(1, second)
        x0, dz1 = rotate_kernel(lengths, (hidden_in, grad_out))
        early = hold(exchange(early, "dp"), (x0,))
        urgent = early[:, :urgent_size]
        urgent = [urgent] + [swap(urgent, "fsdp", step) for step in partners]
        raw0 = early[:, urgent_size:]
        raw0 = [raw0, swap(raw0, "fsdp", 1), swap(raw0, "fsdp", 2)]
    else:
        urgent, raw0, raw1 = gather_other(
            attn_weight, attn_bias, out_weight, ffn_in, ffn_in_bias, ffn_out, norm_gain, shifts
        )
        urgent, raw0, raw1 = ([part[step] for step in range(4)] for part in (urgent, raw0, raw1))
        place = jnp.zeros((1,), jnp.int32)
        x0, dz1 = rotate_kernel(lengths, (hidden_in, grad_out))

    qa0, ka0, va0, ob0, lse0, urgent = first_kernel(lengths, x0, place, urgent)
    if fits:
        raw0[2] = hold(raw0[2], (ob0,))
        raw0.append(swap(raw0[2], "fsdp", 1))
        later = exchange(hold(later, (ob0,)), "dp")
    n1, n2, inv, yb, gb, gp, z0 = dense_kernel(
        0, lengths, x0, ob0, place, urgent, raw0, 3 * width, hidden
    )
    if fits:
        raw1 = hold(later, (z0,))
        raw1 = [raw1, swap(raw1, "fsdp", 1), swap(raw1, "fsdp", 2)]
    qa1, ka1, va1, ob1, lse1 = attention_kernel(1, lengths, z0, place, urgent, raw0, 0)
    if fits:
        raw1[2] = hold(raw1[2], (ob1,))
        raw1.append(swap(raw1[2], "fsdp", 1))
    z1, dr1, dob1, *sent_a = turn_kernel(
        1, lengths, z0, ob1, dz1, place, urgent, raw1, 0, hidden
    )
    dr0, dob0, *sent_b = middle_kernel(
        lengths,
        (z0, dob1, ob1, qa1, ka1, va1, lse1, dr1),
        (n1, n2, inv, yb, gb, gp, ob0),
        place,
        urgent,
        raw0,
        hidden,
        (sent_a[0],),
    )
    if fits:
        got_a = [sent_a[0]] + [swap(sent_a[step], "fsdp", step) for step in partners]
        keep_a, give_a = add_parts(across, got_a, True, (sent_b[0],))
        got_ax = swap(give_a, "dp", 1)
        ready = (sent_b[0], keep_a)
    else:
        ready = ()
    dqkv, sent_c = last_kernel(lengths, (x0, dob0, ob0, qa0, ka0, va0, lse0), ready)
    hidden_out, grad_in = tokens_kernel(lengths, z1, dqkv, dr0, urgent)
    if fits:
        got_b = [sent_b[0]] + [swap(sent_b[step], "fsdp", step) for step in partners]
        got_c = exchange(sent_c, "fsdp")
        keep_b, give_b = add_parts(across, got_b, True, (got_ax, grad_in))
        keep_c, give_c = add_parts(across, [got_c], True, (keep_b,))
        far = range(1, first // 2)
        most = add_halves(across, [(keep_a, got_ax), (keep_b, swap(give_b, "dp", 1))])
        head = add_halves(across, [(keep_c, swap(give_c, "dp", 1))], (most[0],))
        most = [most[0]] + [swap(most[step], "dp", 2 * step) for step in far]
        head = [head[0]] + [swap(head[step], "dp", 2 * step) for step in far]
        spot = lax.axis_index(("dp", "fsdp")).astype(jnp.int32).reshape(1)
        grads = write_gradients(spot, most, head, depth, width, hidden)
    else:
        grads = scatter_other(
            jnp.stack(sent_a), jnp.stack(sent_b), sent_c, rows, width, hidden
        )
    return (hidden_out, grad_in, *grads)


def gather_other(
    attn_weight, attn_bias, out_weight, ffn_in, ffn_in_bias, ffn_out, norm_gain, shifts
):
    axes = ("dp", "fsdp")
    gather = lambda part, axis: lax.all_gather(part, axes, axis=axis, tiled=True)
    depth, unused, width = out_weight.shape
    hidden = ffn_in.shape[2]
    outer, inner, rows = GROUPS
    vectors = gather(jnp.concatenate([attn_bias, norm_gain, shifts], 1), 2)
    line = gather(ffn_in_bias, 1)

    def order(natural):
        return (
            natural.reshape(inner, outer, rows, -1).swapaxes(0, 1).reshape(outer, inner * rows, -1)
        )

    def stacked(part):
        part = part.reshape(DEVICES, -1, rows, width)
        return order(part.swapaxes(1, 2).reshape(width, -1))

    small = vectors.reshape(depth, 8, DEVICES, rows).transpose(2, 1, 0, 3).reshape(width, -1)
    line = line.reshape(depth, DEVICES, -1).swapaxes(0, 1)
    line = jnp.pad(line, ((0, 0), (0, 8 - depth), (0, 0))).reshape(width, -1)
    small = jnp.concatenate([small, line], 1)
    small = jnp.pad(small, ((0, 0), (0, 128 - small.shape[1])))
    wq, wo, wi, wf = (gather(part, 1) for part in (attn_weight, out_weight, ffn_in, ffn_out))
    urgent = jnp.concatenate([order(wq[0]), order(small)], 2)
    raw0 = jnp.concatenate([order(wq[1]), order(wo[0]), order(wi[0]), stacked(wf[0])], 2)
    raw1 = jnp.concatenate([order(wo[1]), order(wi[1]), stacked(wf[1])], 2)
    return urgent, raw0, raw1


def scatter_other(sent_a, sent_b, sent_c, own_rows, width, hidden):
    outer, inner, rows = GROUPS
    axes = ("dp", "fsdp")

    def natural(part):
        return part.reshape(outer, inner, rows, -1).swapaxes(0, 1).reshape(width, -1).astype(F32)

    def cut(part, sizes):
        found, at = [], 0
        for size in sizes:
            found.append(part[:, at : at + size])
            at += size
        return found

    dense = [width, hidden, hidden, width, hidden // 8]
    attention = [3 * width, 128]
    wq0, ab0 = cut(natural(sent_c), attention)
    wq1, ab1, wo0, wi0, wf0, small0, bi0 = cut(natural(sent_b), attention + dense)
    wo1, wi1, wf1, small1, bi1 = cut(natural(sent_a), dense)

    def stacked(part):
        part = part.reshape(DEVICES, rows, -1, width).swapaxes(1, 2)
        return part.reshape(hidden, width)

    def spread(parts, axis):
        return lax.psum_scatter(jnp.stack(parts), axes, scatter_dimension=axis, tiled=True)

    return (
        spread([wq0, wq1], 1),
        spread([ab0[:4].reshape(2, width), ab1[:4].reshape(2, width)], 2),
        spread([wo0, wo1], 1),
        spread([wi0, wi1], 1),
        spread([bi0[:8].reshape(-1), bi1[:8].reshape(-1)], 1),
        spread([stacked(wf0), stacked(wf1)], 1),
        spread([small0[2:4], small1[2:4]], 2),
        spread([small0[4:8], small1[4:8]], 2),
    )


def solution(mesh):
    placed = (
        P(("dp", "fsdp"), None),
        P(("dp", "fsdp"), None),
        P(("dp", "fsdp"), None),
        P(None, ("dp", "fsdp"), None),
        P(None, None, ("dp", "fsdp")),
        P(None, ("dp", "fsdp"), None),
        P(None, ("dp", "fsdp"), None),
        P(None, ("dp", "fsdp")),
        P(None, ("dp", "fsdp"), None),
        P(None, None, ("dp", "fsdp")),
        P(None, None, ("dp", "fsdp")),
    )
    return jax.shard_map(
        local,
        mesh=mesh,
        in_specs=placed,
        out_specs=(
            P(("dp", "fsdp"), None),
            P(("dp", "fsdp"), None),
            P(None, ("dp", "fsdp"), None),
            P(None, None, ("dp", "fsdp")),
            P(None, ("dp", "fsdp"), None),
            P(None, ("dp", "fsdp"), None),
            P(None, ("dp", "fsdp")),
            P(None, ("dp", "fsdp"), None),
            P(None, None, ("dp", "fsdp")),
            P(None, None, ("dp", "fsdp")),
        ),
        check_vma=False,
    )
```

```python
from functools import partial

import jax
import jax.numpy as jnp
from jax import lax
from jax.experimental import pallas as pl
from jax.experimental.pallas import tpu as pltpu
from jax.sharding import PartitionSpec as P

HEADS = 4
HD = 64
SEQ = 512
PAIR = 2 * HD
EXTRA = 16
HALF = SEQ // 2
HALVES = (slice(0, HALF), slice(HALF, SEQ))
FAR = -(2.0**100)
FLOOR = -1e20
EPSILON = 1e-12
PIECE = 256
SMALL = 128
GROUPS = (4, 8, 8)
DEVICES = 32
LOW = jnp.bfloat16
F32 = jnp.float32
MEMORY = 2**26


def dot_nn(left, right):
    return lax.dot_general(left, right, (((1,), (0,)), ((), ())), preferred_element_type=F32)


def dot_nt(left, right):
    return lax.dot_general(left, right, (((1,), (1,)), ((), ())), preferred_element_type=F32)


def dot_tn(left, right):
    return lax.dot_general(left, right, (((0,), (0,)), ((), ())), preferred_element_type=F32)


def pieces(total, size=PIECE):
    return [pl.ds(start, size) for start in range(0, total, size)]


def three_parts(values):
    first = values.astype(LOW).astype(F32)
    rest = values - first
    second = rest.astype(LOW).astype(F32)
    return first, second, rest - second


BELL = -0.5 / 0.6931471805599453


def gelu_parts(u):
    cumulative = 0.5 + 0.5 * lax.erf(u * 0.7071067811865476)
    slope = cumulative + (u * 0.3989422804014327) * jnp.exp2(u * u * BELL)
    return u * cumulative, slope


def inverse_of(values):
    guess = pl.reciprocal(values, approx=True)
    return guess * (2.0 - values * guess)


def longest_start(lengths_ref, row):
    begin, found = jnp.int32(0), jnp.int32(0)
    for entry in range(lengths_ref.shape[1]):
        size = lengths_ref[row, entry]
        found = jnp.where(size == HALF, begin, found)
        begin = begin + size
    return found


def segments(lengths_ref, row):
    places = lax.broadcasted_iota(jnp.int32, (1, SEQ), 1) + longest_start(lengths_ref, row)
    places = places & (SEQ - 1)
    bound = jnp.int32(0)
    segment = jnp.zeros((1, SEQ), jnp.int32)
    last = lengths_ref.shape[1] - 1
    for entry in range(last):
        bound = bound + lengths_ref[row, entry]
        segment = segment + (places >= bound).astype(jnp.int32)
    return segment, last


def head_rows(head):
    return slice(head * HD, (head + 1) * HD)


def attention_forward(row, lengths_ref, x, wt_ref, bias_ref, qa_ref, ka_ref, va_ref, ob_ref, lse_ref, s_ref, p_ref):
    width = HEADS * HD
    segment, last = segments(lengths_ref, row)
    pad = (segment == last).astype(F32)
    line = lax.broadcasted_iota(jnp.int32, (EXTRA, SEQ), 0)
    aug_q = jnp.where(line == segment, 1.0, 0.0).astype(LOW)
    seen = (line == segment) & (segment != last)
    aug_k = jnp.where(seen | (line > last), 0.0, FAR).astype(LOW)
    aug_v = jnp.where(line == 0, 1.0, 0.0).astype(LOW)
    rest = jnp.zeros((PAIR - HD - EXTRA, SEQ), LOW)
    for head in range(HEADS):
        qa_ref[head, HD : HD + EXTRA] = aug_q
        ka_ref[head, HD : HD + EXTRA] = aug_k
        va_ref[head, HD : HD + EXTRA] = aug_v
        qa_ref[head, HD + EXTRA : PAIR] = rest
        ka_ref[head, HD + EXTRA : PAIR] = rest
    for block, ref in enumerate((qa_ref, ka_ref, va_ref)):
        lines = slice(block * width, (block + 1) * width)
        bias = bias_ref[lines]
        value = dot_nt(wt_ref[lines], x) + jnp.concatenate([bias] * (SEQ // 128), 1)
        if block == 0:
            value = value * HD**-0.5
        value = value.astype(LOW)
        for head in range(HEADS):
            ref[head, 0:HD] = value[head_rows(head)]
        yield

    def scores(head):
        for half in HALVES:
            s_ref[head % 2, half] = dot_tn(ka_ref[head, :, half], qa_ref[head, :, half])

    def softmax(head):
        tops = []
        for half in HALVES:
            tops.append(jnp.maximum(jnp.max(s_ref[head % 2, half], 0, keepdims=True), FLOOR))
            p_ref[head % 2, half] = jnp.exp(s_ref[head % 2, half] - tops[-1]).astype(LOW)
        return tops

    scores(0)
    yield
    for head in range(HEADS):
        if head + 1 < HEADS:
            scores(head + 1)
            yield
        tops = softmax(head)
        yield
        for half, top in zip(HALVES, tops):
            out = dot_nn(va_ref[head, :, half], p_ref[head % 2, half])
            alone = pad[:, half]
            total = out[HD : HD + 1] + alone
            lse_ref[head : head + 1, half] = jnp.where(alone > 0, 0.0, top + jnp.log(total))
            own = alone * va_ref[head, 0:HD, half].astype(F32)
            ob_ref[head_rows(head), half] = (out[0:HD] * inverse_of(total) + own).astype(LOW)
        yield


def normal(values):
    centred = values - jnp.mean(values, -1, keepdims=True)
    inverse = lax.rsqrt(jnp.mean(centred * centred, -1, keepdims=True) + EPSILON)
    return centred * inverse, inverse


def normal_back(cotangent, unit, inverse, gains):
    scaled = cotangent * gains
    return inverse * (
        scaled
        - jnp.mean(scaled, -1, keepdims=True)
        - unit * jnp.mean(scaled * unit, -1, keepdims=True)
    )


def dense_forward(x_ref, ob_ref, wo_ref, wi_ref, wf_ref, small_ref, bi_ref, n1_ref, n2_ref, inv_ref, yb_ref, gb_ref, gp_ref, z_ref, work_ref, u_ref):
    small = lambda index: small_ref[pl.ds(index, 1)]
    work_ref[...] = dot_tn(ob_ref[...], wo_ref[...])
    yield
    for place in pieces(SEQ):
        unit, inverse = normal(x_ref[place].astype(F32) + work_ref[place] + small(4))
        n1_ref[place] = unit
        inv_ref[place, pl.ds(0, HD)] = jnp.broadcast_to(inverse, (PIECE, HD))
        y = unit * small(2) + small(5)
        yb_ref[place] = y.astype(LOW)
        work_ref[place] = y + small(6)
        yield
    columns = 256
    count = wi_ref.shape[1] // columns

    def into(step):
        u_ref[step % 2] = dot_nn(yb_ref[...], wi_ref[:, pl.ds(step * columns, columns)])

    into(0)
    yield
    for step in range(count):
        if step + 1 < count:
            into(step + 1)
            yield
        lanes = pl.ds(step * columns, columns)
        for place in pieces(SEQ, SMALL):
            g, slope = gelu_parts(u_ref[step % 2, place] + bi_ref[:, lanes])
            gb_ref[place, lanes] = g.astype(LOW)
            gp_ref[place, lanes] = slope.astype(LOW)
            yield
    work_ref[...] += dot_nn(gb_ref[...], wf_ref[...])
    yield
    for place in pieces(SEQ):
        unit, inverse = normal(work_ref[place])
        n2_ref[place] = unit
        inv_ref[place, pl.ds(HD, HD)] = jnp.broadcast_to(inverse, (PIECE, HD))
        z_ref[place] = (unit * small(3) + small(7)).astype(z_ref.dtype)
        yield


def fold(values):
    return jnp.sum(values.reshape(-1, 8, values.shape[-1]), 0)


def dense_backward(dz_ref, n1_ref, n2_ref, inv_ref, yb_ref, gb_ref, gp_ref, ob_ref, wo_ref, wi_ref, wf_ref, small_ref, dr_ref, dob_ref, gwo_ref, gwi_ref, gwf_ref, gsmall_ref, gbi_ref, low_ref, u_ref, du_ref, turned_ref):
    small = lambda index: small_ref[pl.ds(index, 1)]
    for place in pieces(SEQ):
        dz = dz_ref[place].astype(F32)
        unit = n2_ref[place]
        gsmall_ref[3] += fold(dz * unit)
        gsmall_ref[7] += fold(dz)
        dr = normal_back(dz, unit, inv_ref[place, pl.ds(HD, 1)], small(3))
        dr_ref[place] = dr
        df = dr.astype(LOW)
        low_ref[place] = df
        gsmall_ref[6] += fold(df.astype(F32))
        yield
    columns = 256
    count = wi_ref.shape[1] // columns

    def back(step):
        u_ref[step % 2] = dot_nt(low_ref[...], wf_ref[pl.ds(step * columns, columns)])

    back(0)
    turned_ref[0, 0 : low_ref.shape[1]] = low_ref[...].T
    width = low_ref.shape[1]
    turned_ref[1, 0:width] = yb_ref[...].T
    turned_ref[1, width:] = jnp.ones((EXTRA, SEQ), LOW)
    yield
    for step in range(count):
        if step + 1 < count:
            back(step + 1)
            yield
        lanes = pl.ds(step * columns, columns)
        gwf_ref[:, lanes] += dot_nn(turned_ref[0, 0:width], gb_ref[:, lanes])
        yield
        for place in pieces(SEQ, SMALL):
            du = (u_ref[step % 2, place] * gp_ref[place, lanes].astype(F32)).astype(LOW)
            du_ref[place, lanes] = du
        yield
        product = dot_nn(turned_ref[1], du_ref[:, lanes])
        gwi_ref[:, lanes] += product[0:width]
        gbi_ref[:, lanes] += product[width : width + 8]
        yield
    u_ref[0] = dot_nt(du_ref[...], wi_ref[...])
    yield
    for place in pieces(SEQ):
        dy = dr_ref[place] + u_ref[0, place]
        unit = n1_ref[place]
        gsmall_ref[2] += fold(dy * unit)
        gsmall_ref[5] += fold(dy)
        dr = normal_back(dy, unit, inv_ref[place, pl.ds(0, 1)], small(2))
        dr_ref[place] = dr
        da = dr.astype(LOW)
        low_ref[place] = da
        gsmall_ref[4] += fold(da.astype(F32))
        yield
    gwo_ref[...] += dot_nn(ob_ref[...], low_ref[...])
    dob_ref[...] = dot_nt(wo_ref[...], low_ref[...]).astype(LOW)
    yield


def attention_backward(row, lengths_ref, x, do_ref, ob_ref, qa_ref, ka_ref, va_ref, lse_ref, dqkv_ref, gwq_ref, gbias_ref, p_ref, ds_ref, s_ref):
    width = HEADS * HD
    segment, last = segments(lengths_ref, row)
    pad = (segment == last).astype(F32)

    def scores(head):
        for half in HALVES:
            s_ref[0, head % 2, half] = dot_tn(ka_ref[head, :, half], qa_ref[head, :, half])
            s_ref[1, head % 2, half] = dot_tn(
                va_ref[head, 0:HD, half], do_ref[head_rows(head), half]
            )

    def weigh(head):
        product = do_ref[head_rows(head)].astype(F32) * ob_ref[head_rows(head)].astype(F32)
        centre = jnp.sum(product, 0, keepdims=True)
        for half in HALVES:
            p = jnp.exp(s_ref[0, head % 2, half] - lse_ref[head : head + 1, half])
            p_ref[head % 2, half] = p.astype(LOW)
            ds_ref[head % 2, half] = (p * (s_ref[1, head % 2, half] - centre[:, half])).astype(LOW)

    scores(0)
    yield
    for head in range(HEADS):
        if head + 1 < HEADS:
            scores(head + 1)
            yield
        weigh(head)
        yield
        for half in HALVES:
            ds, do = ds_ref[head % 2, half], do_ref[head_rows(head), half]
            dq = dot_nn(ka_ref[head, 0:HD, half], ds) * HD**-0.5
            dk = dot_nt(qa_ref[head, 0:HD, half], ds)
            dv = dot_nt(do, p_ref[head % 2, half]) + pad[:, half] * do.astype(F32)
            for block, value in enumerate((dq, dk, dv)):
                at = block * width + head * HD
                dqkv_ref[at : at + HD, half] = value.astype(LOW)
        yield
    for index, block in enumerate((0, 2)):
        value = dqkv_ref[block * width : (block + 1) * width].astype(F32)
        parts = [value[:, at : at + 128] for at in range(0, SEQ, 128)]
        gbias_ref[index] += (parts[0] + parts[1]) + (parts[2] + parts[3])
    gwq_ref[...] += dot_nn(dqkv_ref[...], x)
    yield


def unpack_matrix(raw_ref, at, into_ref):
    width = into_ref.shape[0]
    for start in range(0, into_ref.shape[1], width):
        block = raw_ref[:, :, pl.ds(at + start, width)].astype(F32)
        block = block.reshape(GROUPS + (width,)).swapaxes(0, 1).reshape(width, width)
        into_ref[:, pl.ds(start, width)] = block.astype(LOW)


def unpack_stacked(raw_ref, at, into_ref):
    width = into_ref.shape[1]
    count = into_ref.shape[0] // width
    blocks = [
        raw_ref[:, :, pl.ds(at + step * width, width)].astype(F32).reshape(GROUPS + (width,))
        for step in range(count)
    ]
    outer, inner, rows = GROUPS
    for place in range(inner):
        part = jnp.stack([jnp.stack([block[f, place] for block in blocks]) for f in range(outer)])
        size = outer * count * rows
        into_ref[pl.ds(place * size, size)] = part.reshape(size, width).astype(LOW)


def counter(shape, axis):
    return lax.broadcasted_iota(jnp.int32, shape, axis)


def split_by(values, size):
    return lax.shift_right_logical(values, size.bit_length() - 1), values & (size - 1)


def sources(rows):
    outer, inner, height = GROUPS
    group, within = split_by(counter((rows, 1), 0), height)
    far, near = split_by(group, inner)
    return near * outer + far, within


def unpack_vectors(raw_ref, at, layer):
    outer, inner, rows = GROUPS
    total = outer * inner * rows
    raw = raw_ref[:, :, pl.ds(at, 128)].reshape(total, 128)
    owner, place = split_by(counter((1, total), 1), rows)
    pick = jnp.where(counter((128, 1), 0) == rows * layer + place, 1.0, 0.0).astype(LOW)
    device, unused = sources(total)
    spread = jnp.where(owner == device, dot_nn(raw, pick), 0.0)
    return jnp.sum(spread.reshape(outer * inner, rows, total), 0)


def unpack_hidden(raw_ref, at, layer, hidden):
    outer, inner, rows = GROUPS
    total = outer * inner * rows
    raw = raw_ref[:, :, pl.ds(at, 128)].reshape(total, 128)
    owner, place = split_by(counter((1, hidden), 1), hidden // (outer * inner))
    pick = jnp.where(counter((128, 1), 0) == 2 * rows + place, 1.0, 0.0).astype(LOW)
    device, within = sources(total)
    device = jnp.where(within == layer, device, -1)
    spread = jnp.where(owner == device, dot_nn(raw, pick), 0.0)
    return jnp.sum(spread, 0, keepdims=True)


def pack_matrix(sum_ref, sent_ref, at, turned=False):
    width = sum_ref.shape[1 if turned else 0]
    outer, inner, rows = GROUPS
    for start in range(0, sum_ref.shape[0 if turned else 1], width):
        near = pl.ds(start, width)
        block = sum_ref[near].T if turned else sum_ref[:, near]
        block = block.reshape(inner, outer, rows, width)
        block = block.swapaxes(0, 1).reshape(outer, inner * rows, width)
        sent_ref[:, :, pl.ds(at + start, width)] = block.astype(LOW)


def pack_stacked(sum_ref, sent_ref, at):
    width = sum_ref.shape[0]
    outer, inner, rows = GROUPS
    count = sum_ref.shape[1] // width
    near = inner // count
    for step in range(count):
        block = sum_ref[:, pl.ds(step * width, width)].T
        block = block.reshape(near, outer, count, rows, width)
        for part in range(count):
            piece = jnp.stack([block[:, f, part] for f in range(outer)])
            piece = piece.reshape(outer, near * rows, width)
            sent_ref[:, pl.ds(step * near * rows, near * rows), pl.ds(at + part * width, width)] = (
                piece.astype(LOW)
            )


def pack_shared(block, sent_ref, at):
    outer, inner, rows = GROUPS
    columns = block.shape[1]
    block = jnp.broadcast_to(block[None], (outer * inner, rows, columns))
    sent_ref[:, :, pl.ds(at, columns)] = block.reshape(outer, inner * rows, columns).astype(LOW)


def folded(line, lanes):
    return [line[:, at : at + lanes] for at in range(0, line.shape[1], lanes)]


def pack_attention(gwq_ref, gbias_ref, sent_ref, at):
    pack_matrix(gwq_ref, sent_ref, at, True)
    width = gwq_ref.shape[1]
    parts = []
    for index in range(2):
        parts += folded(jnp.sum(gbias_ref[index].T, 0, keepdims=True), 128)
    block = jnp.concatenate(parts + [jnp.zeros((8 - len(parts), 128), F32)], 0)
    pack_shared(block, sent_ref, at + 3 * width)


def pack_dense(gwo_ref, gwi_ref, gwf_ref, gsmall_ref, gbi_ref, sent_ref, at):
    width, hidden = gwi_ref.shape
    pack_matrix(gwo_ref, sent_ref, at)
    pack_matrix(gwi_ref, sent_ref, at + width)
    pack_stacked(gwf_ref, sent_ref, at + width + hidden)
    at = at + width + 2 * hidden
    pack_shared(jnp.sum(gsmall_ref[...], 1), sent_ref, at)
    line = gbi_ref[0:1]
    pack_shared(jnp.concatenate(folded(line, hidden // 8), 0), sent_ref, at + width)


def shape_of(array):
    return jax.ShapeDtypeStruct(array.shape, array.dtype)


def by_row(shape, group):
    if len(shape) == 2:
        return pl.BlockSpec((group * SEQ, shape[1]), lambda step: (step, 0))
    return pl.BlockSpec((group,) + tuple(shape[1:]), lambda step: (step,) + (0,) * (len(shape) - 1))


def one_row(ref, member):
    if len(ref.shape) == 2:
        return ref.at[pl.ds(member * SEQ, SEQ)]
    return ref.at[member]


def alternate(runs):
    running = []
    waiting = list(runs)
    while running or waiting:
        if waiting:
            running.append(waiting.pop(0))
        for run in list(running):
            try:
                next(run)
            except StopIteration:
                running.remove(run)


def whole(shape):
    return pl.BlockSpec(tuple(shape), lambda row: (0,) * len(shape))


def run_rows(
    body, lengths, rowwise, fixed, row_outs, sent, shared, private, cost, setup, finish, after=(),
    scalars=(), group=1
):
    count = lengths.shape[0]
    group = group if count % group == 0 else 1
    cuts = [len(scalars), len(rowwise), len(fixed), len(after), len(row_outs), len(sent)]
    cuts += [len(shared)] + [len(private)] * group

    def kernel(lengths_ref, *refs):
        step = pl.program_id(0)
        groups = []
        at = 0
        for cut in cuts:
            groups.append(refs[at : at + cut])
            at += cut
        numbers, rows_in, fixed_in, unused, rows_out, sent_out, work = groups[:7]

        @pl.when(step == 0)
        def _():
            setup(numbers, fixed_in, sent_out, work)

        alternate(
            body(
                step * group + member,
                lengths_ref,
                [one_row(ref, member) for ref in rows_in],
                [one_row(ref, member) for ref in rows_out],
                work,
                groups[7 + member],
            )
            for member in range(group)
        )

        if finish:

            @pl.when(step == count // group - 1)
            def _():
                finish(numbers, work, sent_out)

    return pl.pallas_call(
        kernel,
        grid=(count // group,),
        in_specs=[pl.BlockSpec(memory_space=pltpu.SMEM)] * (1 + len(scalars))
        + [by_row(array.shape, group) for array in rowwise]
        + [whole(array.shape) for array in fixed]
        + [pl.BlockSpec(memory_space=pl.ANY) for array in after],
        out_specs=[by_row(part.shape, group) for part in row_outs]
        + [whole(part.shape) for part in sent],
        out_shape=list(row_outs) + list(sent),
        scratch_shapes=list(shared) + list(private) * group,
        compiler_params=pltpu.CompilerParams(
            dimension_semantics=("arbitrary",), vmem_limit_bytes=MEMORY
        ),
        cost_estimate=pl.CostEstimate(flops=cost, bytes_accessed=8 * 2**20, transcendentals=0),
    )(lengths, *scalars, *rowwise, *fixed, *after)


def struct(shape, dtype):
    return jax.ShapeDtypeStruct(tuple(shape), dtype)


FORWARD_SCRATCH = lambda: [
    pltpu.VMEM((2, SEQ, HALF), F32),
    pltpu.VMEM((2, SEQ, HALF), LOW),
]
BACKWARD_SCRATCH = lambda: [
    pltpu.VMEM((2, SEQ, HALF), LOW),
    pltpu.VMEM((2, SEQ, HALF), LOW),
    pltpu.VMEM((2, 2, SEQ, HALF), F32),
    pltpu.VMEM((3 * HEADS * HD, SEQ), LOW),
]


def attention_outs(rows, width):
    return [
        struct((rows, HEADS, PAIR, SEQ), LOW),
        struct((rows, HEADS, PAIR, SEQ), LOW),
        struct((rows, HEADS, HD + EXTRA, SEQ), LOW),
        struct((rows, width, SEQ), LOW),
        struct((rows, 8, SEQ), F32),
    ]


def dense_outs(tokens, width, hidden):
    return [
        struct((tokens, width), F32),
        struct((tokens, width), F32),
        struct((tokens, PAIR), F32),
        struct((tokens, width), LOW),
        struct((tokens, hidden), LOW),
        struct((tokens, hidden), LOW),
    ]


def vmem(shape, dtype):
    return pltpu.VMEM(tuple(shape), dtype)


def attention_weights(width):
    return [vmem((width, 3 * width), LOW), vmem((3 * width, width), LOW), vmem((3 * width, 128), F32)]


def dense_weights(width, hidden):
    return [
        vmem((width, width), LOW),
        vmem((width, hidden), LOW),
        vmem((hidden, width), LOW),
        vmem((8, width), F32),
        vmem((1, hidden), F32),
    ]


def dense_sums(width, hidden):
    return [
        vmem((width, width), F32),
        vmem((width, hidden), F32),
        vmem((width, hidden), F32),
        vmem((8, 8, width), F32),
        vmem((8, hidden), F32),
    ]


def attention_sums(width):
    return [vmem((3 * width, width), F32), vmem((2, width, 128), F32)]


def dense_work(width, hidden):
    return [
        vmem((SEQ, width), LOW),
        vmem((2, SEQ, width), F32),
        vmem((SEQ, hidden), LOW),
        vmem((2, width + EXTRA, SEQ), LOW),
    ]


def set_attention(layer, urgent_ref, raw_ref, at, wq_ref, wt_ref, bias_ref):
    width = wq_ref.shape[0]
    unpack_matrix(raw_ref, at, wq_ref)
    vectors = unpack_vectors(urgent_ref, 3 * width, layer)
    for block, line in enumerate((vectors[0:1], jnp.zeros((1, width), F32), vectors[1:2])):
        lines = pl.ds(block * width, width)
        wt_ref[lines] = wq_ref[:, lines].astype(F32).T.astype(LOW)
        bias_ref[lines] = jnp.broadcast_to(line, (128, width)).T


def set_dense(layer, urgent_ref, raw_ref, at, wo_ref, wi_ref, wf_ref, small_ref, bi_ref):
    width, hidden = wi_ref.shape
    unpack_matrix(raw_ref, at, wo_ref)
    unpack_matrix(raw_ref, at + width, wi_ref)
    unpack_stacked(raw_ref, at + width + hidden, wf_ref)
    small_ref[...] = unpack_vectors(urgent_ref, 3 * width, layer)
    bi_ref[...] = unpack_hidden(urgent_ref, 3 * width, layer, hidden)


def clear(refs):
    for ref in refs:
        ref[...] = jnp.zeros(ref.shape, ref.dtype)


def assemble(place_ref, part_refs, into_ref):
    for step, ref in enumerate(part_refs):
        into_ref[place_ref[0] ^ step] = ref[...]


def raw_block(parts):
    return vmem((len(parts),) + parts[0].shape, LOW)


def turned_back(lengths_ref, row, values):
    return pltpu.roll(values, longest_start(lengths_ref, row), 0).astype(LOW)


def rotate_kernel(lengths, arrays):
    def body(row, lengths_ref, rowwise, outs, work, own):
        back = (SEQ - longest_start(lengths_ref, row)) & (SEQ - 1)
        for source, target in zip(rowwise, outs):
            target[...] = pltpu.roll(source[...].astype(F32), back, 0).astype(LOW)
            yield

    return run_rows(
        body, lengths, list(arrays), [], [struct(array.shape, LOW) for array in arrays], [], [], [],
        10**6, lambda *refs: None, None,
    )


def first_kernel(lengths, x, place, parts):
    rows, (tokens, width) = lengths.shape[0], x.shape

    def setup(numbers, fixed, sent, work):
        assemble(numbers[0], fixed, sent[0])
        set_attention(0, sent[0], sent[0], 0, *work)

    def body(row, lengths_ref, rowwise, outs, work, own):
        return attention_forward(row, lengths_ref, rowwise[0][...], *work[1:3], *outs, *own)

    return run_rows(
        body, lengths, [x], list(parts), attention_outs(rows, width),
        [struct((len(parts),) + parts[0].shape, LOW)],
        attention_weights(width), FORWARD_SCRATCH(), 4 * 10**9, setup, None, (), [place],
    )


def attention_kernel(layer, lengths, x, place, urgent, parts, at):
    rows, (tokens, width) = lengths.shape[0], x.shape

    def setup(numbers, fixed, sent, work):
        assemble(numbers[0], fixed[1:], work[3])
        set_attention(layer, fixed[0], work[3], at, *work[:3])

    def body(row, lengths_ref, rowwise, outs, work, own):
        return attention_forward(
            row, lengths_ref, rowwise[0][...].astype(LOW), *work[1:3], *outs, *own
        )

    return run_rows(
        body, lengths, [x], [urgent] + list(parts), attention_outs(rows, width), [],
        attention_weights(width) + [raw_block(parts)], FORWARD_SCRATCH(),
        4 * 10**9, setup, None, (), [place],
    )


def dense_kernel(layer, lengths, x, ob, place, urgent, parts, at, hidden):
    tokens, width = x.shape

    def setup(numbers, fixed, sent, work):
        assemble(numbers[0], fixed[1:], work[5])
        set_dense(layer, fixed[0], work[5], at, *work[:5])

    def body(row, lengths_ref, rowwise, outs, work, own):
        return dense_forward(*rowwise, *work[:5], *outs, *own)

    return run_rows(
        body, lengths, [x, ob], [urgent] + list(parts),
        dense_outs(tokens, width, hidden) + [struct((tokens, width), F32)], [],
        dense_weights(width, hidden) + [raw_block(parts)],
        [vmem((SEQ, width), F32), vmem((2, SEQ, width), F32)],
        5 * 10**9, setup, None, (), [place],
    )


def turn_kernel(layer, lengths, x, ob, cotangent, place, urgent, parts, at, hidden):
    tokens, width = x.shape
    columns = width + 2 * hidden + width + hidden // 8

    def setup(numbers, fixed, sent, work):
        assemble(numbers[0], fixed[1:], work[11])
        set_dense(layer, fixed[0], work[11], at, *work[:5])
        clear(work[5:10])

    def body(row, lengths_ref, rowwise, outs, work, own):
        x_ref, ob_ref, dz_ref = rowwise
        z_ref, dr_ref, dob_ref = outs
        weights, sums = work[:5], work[5:10]
        kept, work_ref, back = own[:6], own[6], own[7:]
        yield from dense_forward(x_ref, ob_ref, *weights, *kept, z_ref, work_ref, back[1])
        yield from dense_backward(dz_ref, *kept, ob_ref, *weights[:4], dr_ref, dob_ref, *sums, *back)

    def finish(numbers, work, sent):
        pack_dense(*work[5:10], work[10], 0)
        hand_out(numbers[0], work[10], sent)

    kept = [vmem((SEQ,) + part.shape[1:], part.dtype) for part in dense_outs(tokens, width, hidden)]
    return run_rows(
        body, lengths, [x, ob, cotangent], [urgent] + list(parts),
        [struct((tokens, width), LOW), struct((tokens, width), F32), struct((tokens // SEQ, width, SEQ), LOW)],
        [struct((64, columns), LOW)] * 4,
        dense_weights(width, hidden) + dense_sums(width, hidden)
        + [vmem((4, 64, columns), LOW), raw_block(parts)],
        kept + [vmem((SEQ, width), F32)] + dense_work(width, hidden),
        10**10, setup, finish, (), [place], 2,
    )


def hand_out(place_ref, packed_ref, sent):
    for step, ref in enumerate(sent):
        ref[...] = packed_ref[place_ref[0] ^ step]


def middle_kernel(lengths, upper, lower, place, urgent, parts, hidden, after):
    tokens, width = upper[0].shape
    columns = 3 * width + 128 + width + 2 * hidden + width + hidden // 8

    def setup(numbers, fixed, sent, work):
        assemble(numbers[0], fixed[1:], work[16])
        set_attention(1, fixed[0], work[16], 0, *work[:3])
        set_dense(0, fixed[0], work[16], 3 * width, *work[3:8])
        clear(work[8:15])

    def body(row, lengths_ref, rowwise, outs, work, own):
        up, low = rowwise[:8], rowwise[8:]
        dx_ref = own[0]
        yield from attention_backward(
            row, lengths_ref, up[0][...].astype(LOW), *up[1:7], own[-1], *work[8:10], *own[5:-1]
        )
        dx_ref[...] = up[7][...] + dot_tn(own[-1][...], work[1][...])
        yield
        yield from dense_backward(dx_ref, *low, *work[3:7], *outs, *work[10:15], *own[1:5])

    def finish(numbers, work, sent):
        pack_attention(*work[8:10], work[15], 0)
        pack_dense(*work[10:15], work[15], 3 * width + 128)
        hand_out(numbers[0], work[15], sent)

    return run_rows(
        body, lengths, list(upper) + list(lower), [urgent] + list(parts),
        [struct((tokens, width), F32), struct((tokens // SEQ, width, SEQ), LOW)],
        [struct((64, columns), LOW)] * 4,
        attention_weights(width) + dense_weights(width, hidden)
        + attention_sums(width) + dense_sums(width, hidden)
        + [vmem((4, 64, columns), LOW), raw_block(parts)],
        [vmem((SEQ, width), F32)] + dense_work(width, hidden) + BACKWARD_SCRATCH(),
        15 * 10**9, setup, finish, after, [place], 2,
    )


def last_kernel(lengths, upper, after, place):
    tokens, width = upper[0].shape

    def setup(numbers, fixed, sent, work):
        clear(work[:2])

    def body(row, lengths_ref, rowwise, outs, work, own):
        return attention_backward(
            row, lengths_ref, rowwise[0][...], *rowwise[1:], outs[0], *work[:2], *own
        )

    def finish(numbers, work, sent):
        pack_attention(*work[:2], work[2], 0)
        hand_out(numbers[0], work[2], sent)

    return run_rows(
        body, lengths, list(upper), [], [struct((tokens // SEQ, 3 * width, SEQ), LOW)],
        [struct((64, 3 * width + 128), LOW)] * 4,
        attention_sums(width) + [vmem((4, 64, 3 * width + 128), LOW)],
        BACKWARD_SCRATCH()[:-1], 8 * 10**9, setup, finish, after, [place], 2,
    )


def tokens_kernel(lengths, z, dqkv, dr, urgent):
    tokens, width = dr.shape

    def setup(numbers, fixed, sent, work):
        set_attention(0, fixed[0], fixed[0], 0, *work)

    def body(row, lengths_ref, rowwise, outs, work, own):
        z_ref, dqkv_ref, dr_ref = rowwise
        outs[0][...] = turned_back(lengths_ref, row, z_ref[...].astype(F32))
        yield
        dx = dr_ref[...] + dot_tn(dqkv_ref[...], work[1][...])
        outs[1][...] = turned_back(lengths_ref, row, dx)
        yield

    return run_rows(
        body, lengths, [z, dqkv, dr], [urgent], [struct((tokens, width), LOW)] * 2, [],
        attention_weights(width), [], 10**9, setup, None,
    )


def hold(array, after):
    def kernel(*refs):
        pass

    anywhere = pl.BlockSpec(memory_space=pl.ANY)
    return pl.pallas_call(
        kernel,
        in_specs=[anywhere] * (1 + len(after)),
        out_specs=anywhere,
        out_shape=shape_of(array),
        input_output_aliases={0: 0},
    )(array, *after)


def pack_parameters(
    attn_weight, attn_bias, out_weight, ffn_in, ffn_in_bias, ffn_out, norm_gain, shifts
):
    depth, rows, width = out_weight.shape
    copies = GROUPS[1]
    hidden = ffn_in.shape[2]
    dense = width + 2 * hidden
    height = ffn_in_bias.shape[1]

    def kernel(wq_ref, ab_ref, wo_ref, wi_ref, bi_ref, wf_ref, gain_ref, shift_ref, first_ref, rest_ref, small_ref):
        def put(ref, block, at):
            block = jnp.broadcast_to(block.astype(F32)[None], (copies,) + block.shape)
            block = block.reshape(copies * block.shape[1], block.shape[2])
            ref[:, pl.ds(at, block.shape[1])] = block.astype(LOW)

        small_ref[...] = jnp.zeros(small_ref.shape, F32)
        for layer in range(depth):
            lanes = pl.ds(rows * layer, rows)
            small_ref[0:2, lanes] = ab_ref[layer].astype(F32)
            small_ref[2:4, lanes] = gain_ref[layer].astype(F32)
            small_ref[4:8, lanes] = shift_ref[layer].astype(F32)
        small_ref[0:depth, pl.ds(2 * rows, height)] = bi_ref[...].astype(F32)
        put(first_ref, wq_ref[0], 0)
        put(first_ref, small_ref[...], 3 * width)
        put(first_ref, wq_ref[1], 3 * width + 128)
        for layer, ref, at in ((0, first_ref, 6 * width + 128), (1, rest_ref, 0)):
            put(ref, wo_ref[layer], at)
            put(ref, wi_ref[layer], at + width)
            at += width + hidden
            down = wf_ref[layer].astype(F32)
            for step in range(hidden // width):
                put(ref, down[step * rows : (step + 1) * rows], at)
                at += width

    return pl.pallas_call(
        kernel,
        in_specs=[pl.BlockSpec(memory_space=pltpu.VMEM)] * 8,
        out_shape=[
            struct((copies * rows, 6 * width + 128 + dense), LOW),
            struct((copies * rows, dense), LOW),
        ],
        scratch_shapes=[vmem((rows, 128), F32)],
        compiler_params=pltpu.CompilerParams(vmem_limit_bytes=MEMORY),
    )(attn_weight, attn_bias, out_weight, ffn_in, ffn_in_bias, ffn_out, norm_gain, shifts)


def add_parts(place, parts, halves, after=()):
    lanes = parts[0].shape[1]
    count = len(parts)
    many, rows = GROUPS[1:]
    outs = 2 if halves else 1

    def kernel(place_ref, *refs):
        out_refs, sum_ref = refs[count + len(after) : -1], refs[-1]
        bit = place_ref[0] & 1
        for start in range(0, lanes, 128):
            near = pl.ds(start, 128)
            total = refs[0][:, near].astype(F32)
            for ref in refs[1:count]:
                total = total + ref[:, near].astype(F32)
            if halves:
                sum_ref[:, :, near] = total.reshape(many, rows, 128)
            else:
                out_refs[0][:, near] = total.astype(LOW)
        for side, ref in enumerate(out_refs if halves else ()):
            for start in range(0, lanes, 128):
                near = pl.ds(start, 128)
                block = [sum_ref[2 * step + (bit ^ side), :, near] for step in range(many // 2)]
                ref[:, near] = jnp.concatenate(block, 0).astype(LOW)

    return pl.pallas_call(
        kernel,
        in_specs=[pl.BlockSpec(memory_space=pltpu.SMEM)]
        + [pl.BlockSpec(memory_space=pltpu.VMEM)] * count
        + [pl.BlockSpec(memory_space=pl.ANY)] * len(after),
        out_shape=[struct((many * rows // outs, lanes), LOW)] * outs,
        scratch_shapes=[vmem((many, rows, lanes), F32)],
        compiler_params=pltpu.CompilerParams(vmem_limit_bytes=MEMORY),
    )(place, *parts, *after)


def add_halves(place, pairs):
    many, rows = GROUPS[1] // 2, GROUPS[2]
    widths = [pair[0].shape[1] for pair in pairs]
    lanes = sum(widths)

    def kernel(place_ref, *refs):
        out_refs, sum_ref = refs[2 * len(pairs) : -1], refs[-1]
        at = 0
        for index, size in enumerate(widths):
            for start in range(0, size, 128):
                near = pl.ds(start, 128)
                total = refs[2 * index][:, near].astype(F32) + refs[2 * index + 1][:, near].astype(F32)
                sum_ref[:, :, pl.ds(at + start, 128)] = total.reshape(many, rows, 128)
            at += size
        far = lax.shift_right_logical(place_ref[0], 1)
        for step, ref in enumerate(out_refs):
            ref[...] = sum_ref[far ^ step].astype(LOW)

    return pl.pallas_call(
        kernel,
        in_specs=[pl.BlockSpec(memory_space=pltpu.SMEM)]
        + [pl.BlockSpec(memory_space=pltpu.VMEM)] * (2 * len(pairs)),
        out_shape=[struct((rows, lanes), LOW)] * many,
        scratch_shapes=[vmem((many, rows, lanes), F32)],
        compiler_params=pltpu.CompilerParams(vmem_limit_bytes=MEMORY),
    )(place, *(part for pair in pairs for part in pair))


def write_gradients(place, found, depth, width, hidden):
    rows = GROUPS[2]
    height = hidden // DEVICES
    middle = width + 2 * hidden + width + hidden // 8
    last = found[0].shape[1] - 3 * width - 128

    def kernel(place_ref, *refs):
        found_refs, refs = refs[: len(found)], refs[len(found) :]
        gwq_ref, gab_ref, gwo_ref, gwi_ref, gbi_ref, gwf_ref, gain_ref, shift_ref = refs
        spot = place_ref[0]

        def total(refs, at, columns):
            value = refs[0][:, pl.ds(at, columns)].astype(F32)
            for ref in refs[1:]:
                value = value + ref[:, pl.ds(at, columns)].astype(F32)
            return value

        def own(block, size):
            return pltpu.roll(block, block.shape[1] - spot * size, 1)

        def unfolded(block, count):
            return jnp.concatenate([block[step : step + 1] for step in range(count)], 1)

        for layer, refs, at in ((0, found_refs, last), (1, found_refs, middle)):
            gwq_ref[layer] = total(refs, at, 3 * width)
            block = total(refs, at + 3 * width, 128)
            many = width // 128
            for index in range(2):
                line = unfolded(block[index * many : (index + 1) * many], many)
                gab_ref[layer, pl.ds(index, 1)] = own(line, rows)[:, 0:rows]
        for layer, refs, at in ((0, found_refs, middle + 3 * width + 128), (1, found_refs, 0)):
            gwo_ref[layer] = total(refs, at, width)
            gwi_ref[layer] = total(refs, at + width, hidden)
            for step in range(hidden // width):
                gwf_ref[layer, pl.ds(step * rows, rows)] = total(
                    refs, at + width + hidden + step * width, width
                )
            at += width + 2 * hidden
            small = own(total(refs, at, width), rows)
            gain_ref[layer] = small[2:4, 0:rows]
            shift_ref[layer] = small[4:8, 0:rows]
            line = unfolded(total(refs, at + width, hidden // 8), 8)
            gbi_ref[pl.ds(layer, 1)] = own(line, height)[:, 0:height]

    outs = [
        struct((depth, rows, 3 * width), F32),
        struct((depth, 2, rows), F32),
        struct((depth, rows, width), F32),
        struct((depth, rows, hidden), F32),
        struct((depth, height), F32),
        struct((depth, height, width), F32),
        struct((depth, 2, rows), F32),
        struct((depth, 4, rows), F32),
    ]
    return pl.pallas_call(
        kernel,
        in_specs=[pl.BlockSpec(memory_space=pltpu.SMEM)]
        + [pl.BlockSpec(memory_space=pltpu.VMEM)] * len(found),
        out_shape=outs,
        compiler_params=pltpu.CompilerParams(vmem_limit_bytes=MEMORY),
    )(place, *found)


def exchange(parts, axis):
    return lax.all_to_all(parts, axis, 0, 0, tiled=True)


def swap(part, axis, step):
    size = lax.axis_size(axis)
    return lax.ppermute(part, axis, [(source, source ^ step) for source in range(size)])


def local(
    hidden_in,
    lengths,
    grad_out,
    attn_weight,
    attn_bias,
    out_weight,
    ffn_in,
    ffn_in_bias,
    ffn_out,
    norm_gain,
    shifts,
):
    depth, rows, width = out_weight.shape
    hidden = ffn_in.shape[2]
    first, second = lax.axis_size("dp"), lax.axis_size("fsdp")
    fits = (second, first, rows) == GROUPS
    urgent_size = 3 * width + 128
    if fits:
        early, later = pack_parameters(
            attn_weight, attn_bias, out_weight, ffn_in, ffn_in_bias, ffn_out, norm_gain, shifts
        )
        across = lax.axis_index("dp").astype(jnp.int32).reshape(1)
        place = lax.axis_index("fsdp").astype(jnp.int32).reshape(1)
        partners = range(1, second)
        x0, dz1 = rotate_kernel(lengths, (hidden_in, grad_out))
        early = hold(exchange(early, "dp"), (x0,))
        urgent = early[:, :urgent_size]
        urgent = [urgent] + [swap(urgent, "fsdp", step) for step in partners]
        raw0 = early[:, urgent_size:]
        raw0 = [raw0, swap(raw0, "fsdp", 1), swap(raw0, "fsdp", 2)]
    else:
        urgent, raw0, raw1 = gather_other(
            attn_weight, attn_bias, out_weight, ffn_in, ffn_in_bias, ffn_out, norm_gain, shifts
        )
        urgent, raw0, raw1 = ([part[step] for step in range(4)] for part in (urgent, raw0, raw1))
        place = jnp.zeros((1,), jnp.int32)
        x0, dz1 = rotate_kernel(lengths, (hidden_in, grad_out))

    qa0, ka0, va0, ob0, lse0, urgent = first_kernel(lengths, x0, place, urgent)
    if fits:
        raw0[2] = hold(raw0[2], (ob0,))
        raw0.append(swap(raw0[2], "fsdp", 1))
        later = exchange(hold(later, (ob0,)), "dp")
    n1, n2, inv, yb, gb, gp, z0 = dense_kernel(
        0, lengths, x0, ob0, place, urgent, raw0, 3 * width, hidden
    )
    if fits:
        raw1 = hold(later, (z0,))
        raw1 = [raw1, swap(raw1, "fsdp", 1), swap(raw1, "fsdp", 2)]
    qa1, ka1, va1, ob1, lse1 = attention_kernel(1, lengths, z0, place, urgent, raw0, 0)
    if fits:
        raw1[2] = hold(raw1[2], (ob1,))
        raw1.append(swap(raw1[2], "fsdp", 1))
    z1, dr1, dob1, *sent_a = turn_kernel(
        1, lengths, z0, ob1, dz1, place, urgent, raw1, 0, hidden
    )
    dr0, dob0, *sent_b = middle_kernel(
        lengths,
        (z0, dob1, ob1, qa1, ka1, va1, lse1, dr1),
        (n1, n2, inv, yb, gb, gp, ob0),
        place,
        urgent,
        raw0,
        hidden,
        (sent_a[0],),
    )
    if fits:
        got_a = [sent_a[0]] + [swap(sent_a[step], "fsdp", step) for step in partners]
        keep_a, give_a = add_parts(across, got_a, True, (sent_b[0],))
        got_ax = swap(give_a, "dp", 1)
        ready = (sent_b[0], keep_a)
    else:
        ready = ()
    dqkv, *sent_c = last_kernel(
        lengths, (x0, dob0, ob0, qa0, ka0, va0, lse0), ready, place
    )
    hidden_out, grad_in = tokens_kernel(lengths, z1, dqkv, dr0, urgent)
    if fits:
        got_b = [sent_b[0]] + [swap(sent_b[step], "fsdp", step) for step in partners]
        got_c = [sent_c[0]] + [swap(sent_c[step], "fsdp", step) for step in partners]
        keep_b, give_b = add_parts(across, got_b, True, (got_ax, grad_in))
        keep_c, give_c = add_parts(across, got_c, True)
        pairs = [(keep_a, got_ax), (keep_b, swap(give_b, "dp", 1)), (keep_c, swap(give_c, "dp", 1))]
        found = add_halves(across, pairs)
        found = [found[0]] + [swap(found[step], "dp", 2 * step) for step in range(1, first // 2)]
        spot = lax.axis_index(("dp", "fsdp")).astype(jnp.int32).reshape(1)
        grads = write_gradients(spot, found, depth, width, hidden)
    else:
        grads = scatter_other(
            *(jnp.stack(part) for part in (sent_a, sent_b, sent_c)), rows, width, hidden
        )
    return (hidden_out, grad_in, *grads)


def gather_other(
    attn_weight, attn_bias, out_weight, ffn_in, ffn_in_bias, ffn_out, norm_gain, shifts
):
    axes = ("dp", "fsdp")
    gather = lambda part, axis: lax.all_gather(part, axes, axis=axis, tiled=True)
    depth, unused, width = out_weight.shape
    hidden = ffn_in.shape[2]
    outer, inner, rows = GROUPS
    vectors = gather(jnp.concatenate([attn_bias, norm_gain, shifts], 1), 2)
    line = gather(ffn_in_bias, 1)

    def order(natural):
        return (
            natural.reshape(inner, outer, rows, -1).swapaxes(0, 1).reshape(outer, inner * rows, -1)
        )

    def stacked(part):
        part = part.reshape(DEVICES, -1, rows, width)
        return order(part.swapaxes(1, 2).reshape(width, -1))

    small = vectors.reshape(depth, 8, DEVICES, rows).transpose(2, 1, 0, 3).reshape(width, -1)
    line = line.reshape(depth, DEVICES, -1).swapaxes(0, 1)
    line = jnp.pad(line, ((0, 0), (0, 8 - depth), (0, 0))).reshape(width, -1)
    small = jnp.concatenate([small, line], 1)
    small = jnp.pad(small, ((0, 0), (0, 128 - small.shape[1])))
    wq, wo, wi, wf = (gather(part, 1) for part in (attn_weight, out_weight, ffn_in, ffn_out))
    urgent = jnp.concatenate([order(wq[0]), order(small)], 2)
    raw0 = jnp.concatenate([order(wq[1]), order(wo[0]), order(wi[0]), stacked(wf[0])], 2)
    raw1 = jnp.concatenate([order(wo[1]), order(wi[1]), stacked(wf[1])], 2)
    return urgent, raw0, raw1


def scatter_other(sent_a, sent_b, sent_c, own_rows, width, hidden):
    outer, inner, rows = GROUPS
    axes = ("dp", "fsdp")

    def natural(part):
        return part.reshape(outer, inner, rows, -1).swapaxes(0, 1).reshape(width, -1).astype(F32)

    def cut(part, sizes):
        found, at = [], 0
        for size in sizes:
            found.append(part[:, at : at + size])
            at += size
        return found

    dense = [width, hidden, hidden, width, hidden // 8]
    attention = [3 * width, 128]
    wq0, ab0 = cut(natural(sent_c), attention)
    wq1, ab1, wo0, wi0, wf0, small0, bi0 = cut(natural(sent_b), attention + dense)
    wo1, wi1, wf1, small1, bi1 = cut(natural(sent_a), dense)

    def stacked(part):
        part = part.reshape(DEVICES, rows, -1, width).swapaxes(1, 2)
        return part.reshape(hidden, width)

    def spread(parts, axis):
        return lax.psum_scatter(jnp.stack(parts), axes, scatter_dimension=axis, tiled=True)

    return (
        spread([wq0, wq1], 1),
        spread([ab0[:4].reshape(2, width), ab1[:4].reshape(2, width)], 2),
        spread([wo0, wo1], 1),
        spread([wi0, wi1], 1),
        spread([bi0[:8].reshape(-1), bi1[:8].reshape(-1)], 1),
        spread([stacked(wf0), stacked(wf1)], 1),
        spread([small0[2:4], small1[2:4]], 2),
        spread([small0[4:8], small1[4:8]], 2),
    )


def solution(mesh):
    placed = (
        P(("dp", "fsdp"), None),
        P(("dp", "fsdp"), None),
        P(("dp", "fsdp"), None),
        P(None, ("dp", "fsdp"), None),
        P(None, None, ("dp", "fsdp")),
        P(None, ("dp", "fsdp"), None),
        P(None, ("dp", "fsdp"), None),
        P(None, ("dp", "fsdp")),
        P(None, ("dp", "fsdp"), None),
        P(None, None, ("dp", "fsdp")),
        P(None, None, ("dp", "fsdp")),
    )
    return jax.shard_map(
        local,
        mesh=mesh,
        in_specs=placed,
        out_specs=(
            P(("dp", "fsdp"), None),
            P(("dp", "fsdp"), None),
            P(None, ("dp", "fsdp"), None),
            P(None, None, ("dp", "fsdp")),
            P(None, ("dp", "fsdp"), None),
            P(None, ("dp", "fsdp"), None),
            P(None, ("dp", "fsdp")),
            P(None, ("dp", "fsdp"), None),
            P(None, None, ("dp", "fsdp")),
            P(None, None, ("dp", "fsdp")),
        ),
        check_vma=False,
    )
```

```python
from functools import partial

import jax
import jax.numpy as jnp
from jax import lax
from jax.experimental import pallas as pl
from jax.experimental.pallas import tpu as pltpu
from jax.sharding import PartitionSpec as P

HEADS = 4
HD = 64
SEQ = 512
PAIR = 2 * HD
EXTRA = 16
HALF = SEQ // 2
HALVES = (slice(0, HALF), slice(HALF, SEQ))
FAR = -(2.0**100)
FLOOR = -1e20
EPSILON = 1e-12
PIECE = 256
SMALL = 128
GROUPS = (4, 8, 8)
DEVICES = 32
LOW = jnp.bfloat16
F32 = jnp.float32
MEMORY = 2**26


def dot_nn(left, right):
    return lax.dot_general(left, right, (((1,), (0,)), ((), ())), preferred_element_type=F32)


def dot_nt(left, right):
    return lax.dot_general(left, right, (((1,), (1,)), ((), ())), preferred_element_type=F32)


def dot_tn(left, right):
    return lax.dot_general(left, right, (((0,), (0,)), ((), ())), preferred_element_type=F32)


def pieces(total, size=PIECE):
    return [pl.ds(start, size) for start in range(0, total, size)]


def three_parts(values):
    first = values.astype(LOW).astype(F32)
    rest = values - first
    second = rest.astype(LOW).astype(F32)
    return first, second, rest - second


BELL = -0.5 / 0.6931471805599453


def gelu_parts(u):
    cumulative = 0.5 + 0.5 * lax.erf(u * 0.7071067811865476)
    slope = cumulative + (u * 0.3989422804014327) * jnp.exp2(u * u * BELL)
    return u * cumulative, slope


def inverse_of(values):
    guess = pl.reciprocal(values, approx=True)
    return guess * (2.0 - values * guess)


def longest_start(lengths_ref, row):
    begin, found = jnp.int32(0), jnp.int32(0)
    for entry in range(lengths_ref.shape[1]):
        size = lengths_ref[row, entry]
        found = jnp.where(size == HALF, begin, found)
        begin = begin + size
    return found


def segments(lengths_ref, row):
    places = lax.broadcasted_iota(jnp.int32, (1, SEQ), 1) + longest_start(lengths_ref, row)
    places = places & (SEQ - 1)
    bound = jnp.int32(0)
    segment = jnp.zeros((1, SEQ), jnp.int32)
    last = lengths_ref.shape[1] - 1
    for entry in range(last):
        bound = bound + lengths_ref[row, entry]
        segment = segment + (places >= bound).astype(jnp.int32)
    return segment, last


def head_rows(head):
    return slice(head * HD, (head + 1) * HD)


def attention_forward(row, lengths_ref, x, wt_ref, bias_ref, qa_ref, ka_ref, va_ref, ob_ref, lse_ref, s_ref, p_ref):
    width = HEADS * HD
    segment, last = segments(lengths_ref, row)
    pad = (segment == last).astype(F32)
    line = lax.broadcasted_iota(jnp.int32, (EXTRA, SEQ), 0)
    aug_q = jnp.where(line == segment, 1.0, 0.0).astype(LOW)
    seen = (line == segment) & (segment != last)
    aug_k = jnp.where(seen | (line > last), 0.0, FAR).astype(LOW)
    aug_v = jnp.where(line == 0, 1.0, 0.0).astype(LOW)
    rest = jnp.zeros((PAIR - HD - EXTRA, SEQ), LOW)
    for head in range(HEADS):
        qa_ref[head, HD : HD + EXTRA] = aug_q
        ka_ref[head, HD : HD + EXTRA] = aug_k
        va_ref[head, HD : HD + EXTRA] = aug_v
        qa_ref[head, HD + EXTRA : PAIR] = rest
        ka_ref[head, HD + EXTRA : PAIR] = rest
    for block, ref in enumerate((qa_ref, ka_ref, va_ref)):
        lines = slice(block * width, (block + 1) * width)
        bias = bias_ref[lines]
        value = dot_nt(wt_ref[lines], x) + jnp.concatenate([bias] * (SEQ // 128), 1)
        if block == 0:
            value = value * HD**-0.5
        value = value.astype(LOW)
        for head in range(HEADS):
            ref[head, 0:HD] = value[head_rows(head)]
        yield

    def scores(head):
        for half in HALVES:
            s_ref[head % 2, half] = dot_tn(ka_ref[head, :, half], qa_ref[head, :, half])

    def softmax(head):
        tops = []
        for half in HALVES:
            tops.append(jnp.maximum(jnp.max(s_ref[head % 2, half], 0, keepdims=True), FLOOR))
            p_ref[head % 2, half] = jnp.exp(s_ref[head % 2, half] - tops[-1]).astype(LOW)
        return tops

    scores(0)
    yield
    for head in range(HEADS):
        if head + 1 < HEADS:
            scores(head + 1)
            yield
        tops = softmax(head)
        yield
        for half, top in zip(HALVES, tops):
            out = dot_nn(va_ref[head, :, half], p_ref[head % 2, half])
            alone = pad[:, half]
            total = out[HD : HD + 1] + alone
            lse_ref[head : head + 1, half] = jnp.where(alone > 0, 0.0, top + jnp.log(total))
            own = alone * va_ref[head, 0:HD, half].astype(F32)
            ob_ref[head_rows(head), half] = (out[0:HD] * inverse_of(total) + own).astype(LOW)
        yield


def normal(values):
    centred = values - jnp.mean(values, -1, keepdims=True)
    inverse = lax.rsqrt(jnp.mean(centred * centred, -1, keepdims=True) + EPSILON)
    return centred * inverse, inverse


def normal_back(cotangent, unit, inverse, gains):
    scaled = cotangent * gains
    return inverse * (
        scaled
        - jnp.mean(scaled, -1, keepdims=True)
        - unit * jnp.mean(scaled * unit, -1, keepdims=True)
    )


def dense_forward(x_ref, ob_ref, wo_ref, wi_ref, wf_ref, small_ref, bi_ref, n1_ref, n2_ref, inv_ref, yb_ref, gb_ref, gp_ref, z_ref, work_ref, u_ref):
    small = lambda index: small_ref[pl.ds(index, 1)]
    work_ref[...] = dot_tn(ob_ref[...], wo_ref[...])
    yield
    for place in pieces(SEQ):
        unit, inverse = normal(x_ref[place].astype(F32) + work_ref[place] + small(4))
        n1_ref[place] = unit.astype(LOW)
        inv_ref[place, pl.ds(0, HD)] = jnp.broadcast_to(inverse, (PIECE, HD))
        y = unit * small(2) + small(5)
        yb_ref[place] = y.astype(LOW)
        work_ref[place] = y + small(6)
        yield
    columns = 256
    count = wi_ref.shape[1] // columns

    def into(step):
        u_ref[step % 2] = dot_nn(yb_ref[...], wi_ref[:, pl.ds(step * columns, columns)])

    into(0)
    yield
    for step in range(count):
        if step + 1 < count:
            into(step + 1)
            yield
        lanes = pl.ds(step * columns, columns)
        for place in pieces(SEQ, SMALL):
            g, slope = gelu_parts(u_ref[step % 2, place] + bi_ref[:, lanes])
            gb_ref[place, lanes] = g.astype(LOW)
            gp_ref[place, lanes] = slope.astype(LOW)
            yield
    work_ref[...] += dot_nn(gb_ref[...], wf_ref[...])
    yield
    for place in pieces(SEQ):
        unit, inverse = normal(work_ref[place])
        n2_ref[place] = unit.astype(LOW)
        inv_ref[place, pl.ds(HD, HD)] = jnp.broadcast_to(inverse, (PIECE, HD))
        z_ref[place] = (unit * small(3) + small(7)).astype(z_ref.dtype)
        yield


def fold(values):
    return jnp.sum(values.reshape(-1, 8, values.shape[-1]), 0)


def dense_backward(dz_ref, n1_ref, n2_ref, inv_ref, yb_ref, gb_ref, gp_ref, ob_ref, wo_ref, wi_ref, wf_ref, small_ref, dr_ref, dob_ref, gwo_ref, gwi_ref, gwf_ref, gsmall_ref, gbi_ref, low_ref, u_ref, du_ref, turned_ref):
    small = lambda index: small_ref[pl.ds(index, 1)]
    for place in pieces(SEQ):
        dz = dz_ref[place].astype(F32)
        unit = n2_ref[place].astype(F32)
        gsmall_ref[3] += fold(dz * unit)
        gsmall_ref[7] += fold(dz)
        dr = normal_back(dz, unit, inv_ref[place, pl.ds(HD, 1)], small(3))
        dr_ref[place] = dr
        df = dr.astype(LOW)
        low_ref[place] = df
        gsmall_ref[6] += fold(df.astype(F32))
        yield
    columns = 256
    count = wi_ref.shape[1] // columns

    def back(step):
        u_ref[step % 2] = dot_nt(low_ref[...], wf_ref[pl.ds(step * columns, columns)])

    back(0)
    turned_ref[0, 0 : low_ref.shape[1]] = low_ref[...].T
    width = low_ref.shape[1]
    turned_ref[1, 0:width] = yb_ref[...].T
    turned_ref[1, width:] = jnp.ones((EXTRA, SEQ), LOW)
    yield
    for step in range(count):
        if step + 1 < count:
            back(step + 1)
            yield
        lanes = pl.ds(step * columns, columns)
        gwf_ref[:, lanes] += dot_nn(turned_ref[0, 0:width], gb_ref[:, lanes])
        yield
        for place in pieces(SEQ, SMALL):
            du = (u_ref[step % 2, place] * gp_ref[place, lanes].astype(F32)).astype(LOW)
            du_ref[place, lanes] = du
        yield
        product = dot_nn(turned_ref[1], du_ref[:, lanes])
        gwi_ref[:, lanes] += product[0:width]
        gbi_ref[:, lanes] += product[width : width + 8]
        yield
    u_ref[0] = dot_nt(du_ref[...], wi_ref[...])
    yield
    for place in pieces(SEQ):
        dy = dr_ref[place] + u_ref[0, place]
        unit = n1_ref[place].astype(F32)
        gsmall_ref[2] += fold(dy * unit)
        gsmall_ref[5] += fold(dy)
        dr = normal_back(dy, unit, inv_ref[place, pl.ds(0, 1)], small(2))
        dr_ref[place] = dr
        da = dr.astype(LOW)
        low_ref[place] = da
        gsmall_ref[4] += fold(da.astype(F32))
        yield
    gwo_ref[...] += dot_nn(ob_ref[...], low_ref[...])
    dob_ref[...] = dot_nt(wo_ref[...], low_ref[...]).astype(LOW)
    yield


def attention_backward(row, lengths_ref, x, do_ref, ob_ref, qa_ref, ka_ref, va_ref, lse_ref, dqkv_ref, gwq_ref, gbias_ref, p_ref, ds_ref, s_ref):
    width = HEADS * HD
    segment, last = segments(lengths_ref, row)
    pad = (segment == last).astype(F32)

    def scores(head):
        for half in HALVES:
            s_ref[0, head % 2, half] = dot_tn(ka_ref[head, :, half], qa_ref[head, :, half])
            s_ref[1, head % 2, half] = dot_tn(
                va_ref[head, 0:HD, half], do_ref[head_rows(head), half]
            )

    def weigh(head):
        product = do_ref[head_rows(head)].astype(F32) * ob_ref[head_rows(head)].astype(F32)
        centre = jnp.sum(product, 0, keepdims=True)
        for half in HALVES:
            p = jnp.exp(s_ref[0, head % 2, half] - lse_ref[head : head + 1, half])
            p_ref[head % 2, half] = p.astype(LOW)
            ds_ref[head % 2, half] = (p * (s_ref[1, head % 2, half] - centre[:, half])).astype(LOW)

    scores(0)
    yield
    for head in range(HEADS):
        if head + 1 < HEADS:
            scores(head + 1)
            yield
        weigh(head)
        yield
        for half in HALVES:
            ds, do = ds_ref[head % 2, half], do_ref[head_rows(head), half]
            dq = dot_nn(ka_ref[head, 0:HD, half], ds) * HD**-0.5
            dk = dot_nt(qa_ref[head, 0:HD, half], ds)
            dv = dot_nt(do, p_ref[head % 2, half]) + pad[:, half] * do.astype(F32)
            for block, value in enumerate((dq, dk, dv)):
                at = block * width + head * HD
                dqkv_ref[at : at + HD, half] = value.astype(LOW)
        yield
    for index, block in enumerate((0, 2)):
        value = dqkv_ref[block * width : (block + 1) * width].astype(F32)
        parts = [value[:, at : at + 128] for at in range(0, SEQ, 128)]
        gbias_ref[index] += (parts[0] + parts[1]) + (parts[2] + parts[3])
    gwq_ref[...] += dot_nn(dqkv_ref[...], x)
    yield


def unpack_matrix(raw_ref, at, into_ref):
    width = into_ref.shape[0]
    for start in range(0, into_ref.shape[1], width):
        block = raw_ref[:, :, pl.ds(at + start, width)].astype(F32)
        block = block.reshape(GROUPS + (width,)).swapaxes(0, 1).reshape(width, width)
        into_ref[:, pl.ds(start, width)] = block.astype(LOW)


def unpack_stacked(raw_ref, at, into_ref):
    width = into_ref.shape[1]
    count = into_ref.shape[0] // width
    blocks = [
        raw_ref[:, :, pl.ds(at + step * width, width)].astype(F32).reshape(GROUPS + (width,))
        for step in range(count)
    ]
    outer, inner, rows = GROUPS
    for place in range(inner):
        part = jnp.stack([jnp.stack([block[f, place] for block in blocks]) for f in range(outer)])
        size = outer * count * rows
        into_ref[pl.ds(place * size, size)] = part.reshape(size, width).astype(LOW)


def counter(shape, axis):
    return lax.broadcasted_iota(jnp.int32, shape, axis)


def split_by(values, size):
    return lax.shift_right_logical(values, size.bit_length() - 1), values & (size - 1)


def sources(rows):
    outer, inner, height = GROUPS
    group, within = split_by(counter((rows, 1), 0), height)
    far, near = split_by(group, inner)
    return near * outer + far, within


def unpack_vectors(raw_ref, at, layer):
    outer, inner, rows = GROUPS
    total = outer * inner * rows
    raw = raw_ref[:, :, pl.ds(at, 128)].reshape(total, 128)
    owner, place = split_by(counter((1, total), 1), rows)
    pick = jnp.where(counter((128, 1), 0) == rows * layer + place, 1.0, 0.0).astype(LOW)
    device, unused = sources(total)
    spread = jnp.where(owner == device, dot_nn(raw, pick), 0.0)
    return jnp.sum(spread.reshape(outer * inner, rows, total), 0)


def unpack_hidden(raw_ref, at, layer, hidden):
    outer, inner, rows = GROUPS
    total = outer * inner * rows
    raw = raw_ref[:, :, pl.ds(at, 128)].reshape(total, 128)
    owner, place = split_by(counter((1, hidden), 1), hidden // (outer * inner))
    pick = jnp.where(counter((128, 1), 0) == 2 * rows + place, 1.0, 0.0).astype(LOW)
    device, within = sources(total)
    device = jnp.where(within == layer, device, -1)
    spread = jnp.where(owner == device, dot_nn(raw, pick), 0.0)
    return jnp.sum(spread, 0, keepdims=True)


def pack_matrix(sum_ref, sent_ref, at, turned=False):
    width = sum_ref.shape[1 if turned else 0]
    outer, inner, rows = GROUPS
    for start in range(0, sum_ref.shape[0 if turned else 1], width):
        near = pl.ds(start, width)
        block = sum_ref[near].T if turned else sum_ref[:, near]
        block = block.reshape(inner, outer, rows, width)
        block = block.swapaxes(0, 1).reshape(outer, inner * rows, width)
        sent_ref[:, :, pl.ds(at + start, width)] = block.astype(LOW)


def pack_stacked(sum_ref, sent_ref, at):
    width = sum_ref.shape[0]
    outer, inner, rows = GROUPS
    count = sum_ref.shape[1] // width
    near = inner // count
    for step in range(count):
        block = sum_ref[:, pl.ds(step * width, width)].T
        block = block.reshape(near, outer, count, rows, width)
        for part in range(count):
            piece = jnp.stack([block[:, f, part] for f in range(outer)])
            piece = piece.reshape(outer, near * rows, width)
            sent_ref[:, pl.ds(step * near * rows, near * rows), pl.ds(at + part * width, width)] = (
                piece.astype(LOW)
            )


def pack_shared(block, sent_ref, at):
    outer, inner, rows = GROUPS
    columns = block.shape[1]
    block = jnp.broadcast_to(block[None], (outer * inner, rows, columns))
    sent_ref[:, :, pl.ds(at, columns)] = block.reshape(outer, inner * rows, columns).astype(LOW)


def folded(line, lanes):
    return [line[:, at : at + lanes] for at in range(0, line.shape[1], lanes)]


def pack_attention(gwq_ref, gbias_ref, sent_ref, at):
    pack_matrix(gwq_ref, sent_ref, at, True)
    width = gwq_ref.shape[1]
    parts = []
    for index in range(2):
        parts += folded(jnp.sum(gbias_ref[index].T, 0, keepdims=True), 128)
    block = jnp.concatenate(parts + [jnp.zeros((8 - len(parts), 128), F32)], 0)
    pack_shared(block, sent_ref, at + 3 * width)


def pack_dense(gwo_ref, gwi_ref, gwf_ref, gsmall_ref, gbi_ref, sent_ref, at):
    width, hidden = gwi_ref.shape
    pack_matrix(gwo_ref, sent_ref, at)
    pack_matrix(gwi_ref, sent_ref, at + width)
    pack_stacked(gwf_ref, sent_ref, at + width + hidden)
    at = at + width + 2 * hidden
    pack_shared(jnp.sum(gsmall_ref[...], 1), sent_ref, at)
    line = gbi_ref[0:1]
    pack_shared(jnp.concatenate(folded(line, hidden // 8), 0), sent_ref, at + width)


def shape_of(array):
    return jax.ShapeDtypeStruct(array.shape, array.dtype)


def by_row(shape, group):
    if len(shape) == 2:
        return pl.BlockSpec((group * SEQ, shape[1]), lambda step: (step, 0))
    return pl.BlockSpec((group,) + tuple(shape[1:]), lambda step: (step,) + (0,) * (len(shape) - 1))


def one_row(ref, member):
    if len(ref.shape) == 2:
        return ref.at[pl.ds(member * SEQ, SEQ)]
    return ref.at[member]


def alternate(runs):
    running = []
    waiting = list(runs)
    while running or waiting:
        if waiting:
            running.append(waiting.pop(0))
        for run in list(running):
            try:
                next(run)
            except StopIteration:
                running.remove(run)


def whole(shape):
    return pl.BlockSpec(tuple(shape), lambda row: (0,) * len(shape))


def run_rows(
    body, lengths, rowwise, fixed, row_outs, sent, shared, private, cost, setup, finish, after=(),
    scalars=(), group=1
):
    count = lengths.shape[0]
    group = group if count % group == 0 else 1
    cuts = [len(scalars), len(rowwise), len(fixed), len(after), len(row_outs), len(sent)]
    cuts += [len(shared)] + [len(private)] * group

    def kernel(lengths_ref, *refs):
        step = pl.program_id(0)
        groups = []
        at = 0
        for cut in cuts:
            groups.append(refs[at : at + cut])
            at += cut
        numbers, rows_in, fixed_in, unused, rows_out, sent_out, work = groups[:7]

        @pl.when(step == 0)
        def _():
            setup(numbers, fixed_in, sent_out, work)

        alternate(
            body(
                step * group + member,
                lengths_ref,
                [one_row(ref, member) for ref in rows_in],
                [one_row(ref, member) for ref in rows_out],
                work,
                groups[7 + member],
            )
            for member in range(group)
        )

        if finish:

            @pl.when(step == count // group - 1)
            def _():
                finish(numbers, work, sent_out)

    return pl.pallas_call(
        kernel,
        grid=(count // group,),
        in_specs=[pl.BlockSpec(memory_space=pltpu.SMEM)] * (1 + len(scalars))
        + [by_row(array.shape, group) for array in rowwise]
        + [whole(array.shape) for array in fixed]
        + [pl.BlockSpec(memory_space=pl.ANY) for array in after],
        out_specs=[by_row(part.shape, group) for part in row_outs]
        + [whole(part.shape) for part in sent],
        out_shape=list(row_outs) + list(sent),
        scratch_shapes=list(shared) + list(private) * group,
        compiler_params=pltpu.CompilerParams(
            dimension_semantics=("arbitrary",), vmem_limit_bytes=MEMORY
        ),
        cost_estimate=pl.CostEstimate(flops=cost, bytes_accessed=8 * 2**20, transcendentals=0),
    )(lengths, *scalars, *rowwise, *fixed, *after)


def struct(shape, dtype):
    return jax.ShapeDtypeStruct(tuple(shape), dtype)


FORWARD_SCRATCH = lambda: [
    pltpu.VMEM((2, SEQ, HALF), F32),
    pltpu.VMEM((2, SEQ, HALF), LOW),
]
BACKWARD_SCRATCH = lambda: [
    pltpu.VMEM((2, SEQ, HALF), LOW),
    pltpu.VMEM((2, SEQ, HALF), LOW),
    pltpu.VMEM((2, 2, SEQ, HALF), F32),
    pltpu.VMEM((3 * HEADS * HD, SEQ), LOW),
]


def attention_outs(rows, width):
    return [
        struct((rows, HEADS, PAIR, SEQ), LOW),
        struct((rows, HEADS, PAIR, SEQ), LOW),
        struct((rows, HEADS, HD + EXTRA, SEQ), LOW),
        struct((rows, width, SEQ), LOW),
        struct((rows, 8, SEQ), F32),
    ]


def dense_outs(tokens, width, hidden):
    return [
        struct((tokens, width), LOW),
        struct((tokens, width), LOW),
        struct((tokens, PAIR), F32),
        struct((tokens, width), LOW),
        struct((tokens, hidden), LOW),
        struct((tokens, hidden), LOW),
    ]


def vmem(shape, dtype):
    return pltpu.VMEM(tuple(shape), dtype)


def attention_weights(width):
    return [vmem((width, 3 * width), LOW), vmem((3 * width, width), LOW), vmem((3 * width, 128), F32)]


def dense_weights(width, hidden):
    return [
        vmem((width, width), LOW),
        vmem((width, hidden), LOW),
        vmem((hidden, width), LOW),
        vmem((8, width), F32),
        vmem((1, hidden), F32),
    ]


def dense_sums(width, hidden):
    return [
        vmem((width, width), F32),
        vmem((width, hidden), F32),
        vmem((width, hidden), F32),
        vmem((8, 8, width), F32),
        vmem((8, hidden), F32),
    ]


def attention_sums(width):
    return [vmem((3 * width, width), F32), vmem((2, width, 128), F32)]


def dense_work(width, hidden):
    return [
        vmem((SEQ, width), LOW),
        vmem((2, SEQ, width), F32),
        vmem((SEQ, hidden), LOW),
        vmem((2, width + EXTRA, SEQ), LOW),
    ]


def set_attention(layer, urgent_ref, raw_ref, at, wq_ref, wt_ref, bias_ref):
    width = wq_ref.shape[0]
    unpack_matrix(raw_ref, at, wq_ref)
    vectors = unpack_vectors(urgent_ref, 3 * width, layer)
    for block, line in enumerate((vectors[0:1], jnp.zeros((1, width), F32), vectors[1:2])):
        lines = pl.ds(block * width, width)
        wt_ref[lines] = wq_ref[:, lines].astype(F32).T.astype(LOW)
        bias_ref[lines] = jnp.broadcast_to(line, (128, width)).T


def set_dense(layer, urgent_ref, raw_ref, at, wo_ref, wi_ref, wf_ref, small_ref, bi_ref):
    width, hidden = wi_ref.shape
    unpack_matrix(raw_ref, at, wo_ref)
    unpack_matrix(raw_ref, at + width, wi_ref)
    unpack_stacked(raw_ref, at + width + hidden, wf_ref)
    small_ref[...] = unpack_vectors(urgent_ref, 3 * width, layer)
    bi_ref[...] = unpack_hidden(urgent_ref, 3 * width, layer, hidden)


def clear(refs):
    for ref in refs:
        ref[...] = jnp.zeros(ref.shape, ref.dtype)


def assemble(place_ref, part_refs, into_ref):
    for step, ref in enumerate(part_refs):
        into_ref[place_ref[0] ^ step] = ref[...]


def raw_block(parts):
    return vmem((len(parts),) + parts[0].shape, LOW)


def turned_back(lengths_ref, row, values):
    return pltpu.roll(values, longest_start(lengths_ref, row), 0).astype(LOW)


def rotate_kernel(lengths, arrays):
    def body(row, lengths_ref, rowwise, outs, work, own):
        back = (SEQ - longest_start(lengths_ref, row)) & (SEQ - 1)
        for source, target in zip(rowwise, outs):
            target[...] = pltpu.roll(source[...].astype(F32), back, 0).astype(LOW)
            yield

    return run_rows(
        body, lengths, list(arrays), [], [struct(array.shape, LOW) for array in arrays], [], [], [],
        10**6, lambda *refs: None, None,
    )


def first_kernel(lengths, x, place, parts):
    rows, (tokens, width) = lengths.shape[0], x.shape

    def setup(numbers, fixed, sent, work):
        assemble(numbers[0], fixed, sent[0])
        set_attention(0, sent[0], sent[0], 0, *work)

    def body(row, lengths_ref, rowwise, outs, work, own):
        return attention_forward(row, lengths_ref, rowwise[0][...], *work[1:3], *outs, *own)

    return run_rows(
        body, lengths, [x], list(parts), attention_outs(rows, width),
        [struct((len(parts),) + parts[0].shape, LOW)],
        attention_weights(width), FORWARD_SCRATCH(), 4 * 10**9, setup, None, (), [place],
    )


def attention_kernel(layer, lengths, x, place, urgent, parts, at):
    rows, (tokens, width) = lengths.shape[0], x.shape

    def setup(numbers, fixed, sent, work):
        assemble(numbers[0], fixed[1:], work[3])
        set_attention(layer, fixed[0], work[3], at, *work[:3])

    def body(row, lengths_ref, rowwise, outs, work, own):
        return attention_forward(
            row, lengths_ref, rowwise[0][...].astype(LOW), *work[1:3], *outs, *own
        )

    return run_rows(
        body, lengths, [x], [urgent] + list(parts), attention_outs(rows, width), [],
        attention_weights(width) + [raw_block(parts)], FORWARD_SCRATCH(),
        4 * 10**9, setup, None, (), [place],
    )


def dense_kernel(layer, lengths, x, ob, place, urgent, parts, at, hidden):
    tokens, width = x.shape

    def setup(numbers, fixed, sent, work):
        assemble(numbers[0], fixed[1:], work[5])
        set_dense(layer, fixed[0], work[5], at, *work[:5])

    def body(row, lengths_ref, rowwise, outs, work, own):
        return dense_forward(*rowwise, *work[:5], *outs, *own)

    return run_rows(
        body, lengths, [x, ob], [urgent] + list(parts),
        dense_outs(tokens, width, hidden) + [struct((tokens, width), F32)], [],
        dense_weights(width, hidden) + [raw_block(parts)],
        [vmem((SEQ, width), F32), vmem((2, SEQ, width), F32)],
        5 * 10**9, setup, None, (), [place],
    )


def turn_kernel(layer, lengths, x, ob, cotangent, place, urgent, parts, at, hidden):
    tokens, width = x.shape
    columns = width + 2 * hidden + width + hidden // 8

    def setup(numbers, fixed, sent, work):
        assemble(numbers[0], fixed[1:], work[11])
        set_dense(layer, fixed[0], work[11], at, *work[:5])
        clear(work[5:10])

    def body(row, lengths_ref, rowwise, outs, work, own):
        x_ref, ob_ref, dz_ref = rowwise
        z_ref, dr_ref, dob_ref = outs
        weights, sums = work[:5], work[5:10]
        kept, work_ref, back = own[:6], own[6], own[7:]
        yield from dense_forward(x_ref, ob_ref, *weights, *kept, z_ref, work_ref, back[1])
        yield from dense_backward(dz_ref, *kept, ob_ref, *weights[:4], dr_ref, dob_ref, *sums, *back)

    def finish(numbers, work, sent):
        pack_dense(*work[5:10], work[10], 0)
        hand_out(numbers[0], work[10], sent)

    kept = [vmem((SEQ,) + part.shape[1:], part.dtype) for part in dense_outs(tokens, width, hidden)]
    return run_rows(
        body, lengths, [x, ob, cotangent], [urgent] + list(parts),
        [struct((tokens, width), LOW), struct((tokens, width), F32), struct((tokens // SEQ, width, SEQ), LOW)],
        [struct((64, columns), LOW)] * 4,
        dense_weights(width, hidden) + dense_sums(width, hidden)
        + [vmem((4, 64, columns), LOW), raw_block(parts)],
        kept + [vmem((SEQ, width), F32)] + dense_work(width, hidden),
        10**10, setup, finish, (), [place], 2,
    )


def hand_out(place_ref, packed_ref, sent):
    for step, ref in enumerate(sent):
        ref[...] = packed_ref[place_ref[0] ^ step]


def middle_kernel(lengths, upper, lower, place, urgent, parts, hidden, after):
    tokens, width = upper[0].shape
    columns = 3 * width + 128 + width + 2 * hidden + width + hidden // 8

    def setup(numbers, fixed, sent, work):
        assemble(numbers[0], fixed[1:], work[16])
        set_attention(1, fixed[0], work[16], 0, *work[:3])
        set_dense(0, fixed[0], work[16], 3 * width, *work[3:8])
        clear(work[8:15])

    def body(row, lengths_ref, rowwise, outs, work, own):
        up, low = rowwise[:8], rowwise[8:]
        dx_ref = own[0]
        yield from attention_backward(
            row, lengths_ref, up[0][...].astype(LOW), *up[1:7], own[-1], *work[8:10], *own[5:-1]
        )
        dx_ref[...] = up[7][...] + dot_tn(own[-1][...], work[1][...])
        yield
        yield from dense_backward(dx_ref, *low, *work[3:7], *outs, *work[10:15], *own[1:5])

    def finish(numbers, work, sent):
        pack_attention(*work[8:10], work[15], 0)
        pack_dense(*work[10:15], work[15], 3 * width + 128)
        hand_out(numbers[0], work[15], sent)

    return run_rows(
        body, lengths, list(upper) + list(lower), [urgent] + list(parts),
        [struct((tokens, width), F32), struct((tokens // SEQ, width, SEQ), LOW)],
        [struct((64, columns), LOW)] * 4,
        attention_weights(width) + dense_weights(width, hidden)
        + attention_sums(width) + dense_sums(width, hidden)
        + [vmem((4, 64, columns), LOW), raw_block(parts)],
        [vmem((SEQ, width), F32)] + dense_work(width, hidden) + BACKWARD_SCRATCH(),
        15 * 10**9, setup, finish, after, [place], 2,
    )


def last_kernel(lengths, upper, after, place):
    tokens, width = upper[0].shape

    def setup(numbers, fixed, sent, work):
        clear(work[:2])

    def body(row, lengths_ref, rowwise, outs, work, own):
        return attention_backward(
            row, lengths_ref, rowwise[0][...], *rowwise[1:], outs[0], *work[:2], *own
        )

    def finish(numbers, work, sent):
        pack_attention(*work[:2], work[2], 0)
        hand_out(numbers[0], work[2], sent)

    return run_rows(
        body, lengths, list(upper), [], [struct((tokens // SEQ, 3 * width, SEQ), LOW)],
        [struct((64, 3 * width + 128), LOW)] * 4,
        attention_sums(width) + [vmem((4, 64, 3 * width + 128), LOW)],
        BACKWARD_SCRATCH()[:-1], 8 * 10**9, setup, finish, after, [place], 2,
    )


def tokens_kernel(lengths, z, dqkv, dr, urgent):
    tokens, width = dr.shape

    def setup(numbers, fixed, sent, work):
        set_attention(0, fixed[0], fixed[0], 0, *work)

    def body(row, lengths_ref, rowwise, outs, work, own):
        z_ref, dqkv_ref, dr_ref = rowwise
        outs[0][...] = turned_back(lengths_ref, row, z_ref[...].astype(F32))
        yield
        dx = dr_ref[...] + dot_tn(dqkv_ref[...], work[1][...])
        outs[1][...] = turned_back(lengths_ref, row, dx)
        yield

    return run_rows(
        body, lengths, [z, dqkv, dr], [urgent], [struct((tokens, width), LOW)] * 2, [],
        attention_weights(width), [], 10**9, setup, None,
    )


def hold(array, after):
    def kernel(*refs):
        pass

    anywhere = pl.BlockSpec(memory_space=pl.ANY)
    return pl.pallas_call(
        kernel,
        in_specs=[anywhere] * (1 + len(after)),
        out_specs=anywhere,
        out_shape=shape_of(array),
        input_output_aliases={0: 0},
    )(array, *after)


def pack_parameters(
    attn_weight, attn_bias, out_weight, ffn_in, ffn_in_bias, ffn_out, norm_gain, shifts
):
    depth, rows, width = out_weight.shape
    copies = GROUPS[1]
    hidden = ffn_in.shape[2]
    dense = width + 2 * hidden
    height = ffn_in_bias.shape[1]

    def kernel(wq_ref, ab_ref, wo_ref, wi_ref, bi_ref, wf_ref, gain_ref, shift_ref, first_ref, rest_ref, small_ref):
        def put(ref, block, at):
            block = jnp.broadcast_to(block.astype(F32)[None], (copies,) + block.shape)
            block = block.reshape(copies * block.shape[1], block.shape[2])
            ref[:, pl.ds(at, block.shape[1])] = block.astype(LOW)

        small_ref[...] = jnp.zeros(small_ref.shape, F32)
        for layer in range(depth):
            lanes = pl.ds(rows * layer, rows)
            small_ref[0:2, lanes] = ab_ref[layer].astype(F32)
            small_ref[2:4, lanes] = gain_ref[layer].astype(F32)
            small_ref[4:8, lanes] = shift_ref[layer].astype(F32)
        small_ref[0:depth, pl.ds(2 * rows, height)] = bi_ref[...].astype(F32)
        put(first_ref, wq_ref[0], 0)
        put(first_ref, small_ref[...], 3 * width)
        put(first_ref, wq_ref[1], 3 * width + 128)
        for layer, ref, at in ((0, first_ref, 6 * width + 128), (1, rest_ref, 0)):
            put(ref, wo_ref[layer], at)
            put(ref, wi_ref[layer], at + width)
            at += width + hidden
            down = wf_ref[layer].astype(F32)
            for step in range(hidden // width):
                put(ref, down[step * rows : (step + 1) * rows], at)
                at += width

    return pl.pallas_call(
        kernel,
        in_specs=[pl.BlockSpec(memory_space=pltpu.VMEM)] * 8,
        out_shape=[
            struct((copies * rows, 6 * width + 128 + dense), LOW),
            struct((copies * rows, dense), LOW),
        ],
        scratch_shapes=[vmem((rows, 128), F32)],
        compiler_params=pltpu.CompilerParams(vmem_limit_bytes=MEMORY),
    )(attn_weight, attn_bias, out_weight, ffn_in, ffn_in_bias, ffn_out, norm_gain, shifts)


def add_parts(place, parts, halves, after=()):
    lanes = parts[0].shape[1]
    count = len(parts)
    many, rows = GROUPS[1:]
    outs = 2 if halves else 1

    def kernel(place_ref, *refs):
        out_refs, sum_ref = refs[count + len(after) : -1], refs[-1]
        bit = place_ref[0] & 1
        for start in range(0, lanes, 128):
            near = pl.ds(start, 128)
            total = refs[0][:, near].astype(F32)
            for ref in refs[1:count]:
                total = total + ref[:, near].astype(F32)
            if halves:
                sum_ref[:, :, near] = total.reshape(many, rows, 128)
            else:
                out_refs[0][:, near] = total.astype(LOW)
        for side, ref in enumerate(out_refs if halves else ()):
            for start in range(0, lanes, 128):
                near = pl.ds(start, 128)
                block = [sum_ref[2 * step + (bit ^ side), :, near] for step in range(many // 2)]
                ref[:, near] = jnp.concatenate(block, 0).astype(LOW)

    return pl.pallas_call(
        kernel,
        in_specs=[pl.BlockSpec(memory_space=pltpu.SMEM)]
        + [pl.BlockSpec(memory_space=pltpu.VMEM)] * count
        + [pl.BlockSpec(memory_space=pl.ANY)] * len(after),
        out_shape=[struct((many * rows // outs, lanes), LOW)] * outs,
        scratch_shapes=[vmem((many, rows, lanes), F32)],
        compiler_params=pltpu.CompilerParams(vmem_limit_bytes=MEMORY),
    )(place, *parts, *after)


def add_halves(place, pairs, after=()):
    many, rows = GROUPS[1] // 2, GROUPS[2]
    widths = [pair[0].shape[1] for pair in pairs]
    lanes = sum(widths)

    def kernel(place_ref, *refs):
        out_refs, sum_ref = refs[2 * len(pairs) + len(after) : -1], refs[-1]
        at = 0
        for index, size in enumerate(widths):
            for start in range(0, size, 128):
                near = pl.ds(start, 128)
                total = refs[2 * index][:, near].astype(F32) + refs[2 * index + 1][:, near].astype(F32)
                sum_ref[:, :, pl.ds(at + start, 128)] = total.reshape(many, rows, 128)
            at += size
        far = lax.shift_right_logical(place_ref[0], 1)
        for step, ref in enumerate(out_refs):
            ref[...] = sum_ref[far ^ step].astype(LOW)

    return pl.pallas_call(
        kernel,
        in_specs=[pl.BlockSpec(memory_space=pltpu.SMEM)]
        + [pl.BlockSpec(memory_space=pltpu.VMEM)] * (2 * len(pairs))
        + [pl.BlockSpec(memory_space=pl.ANY)] * len(after),
        out_shape=[struct((rows, lanes), LOW)] * many,
        scratch_shapes=[vmem((many, rows, lanes), F32)],
        compiler_params=pltpu.CompilerParams(vmem_limit_bytes=MEMORY),
    )(place, *(part for pair in pairs for part in pair), *after)


def write_gradients(place, outer, inner, depth, width, hidden):
    rows = GROUPS[2]
    height = hidden // DEVICES
    middle = width + 2 * hidden + width + hidden // 8

    def kernel(place_ref, *refs):
        outer_refs, refs = refs[: len(outer)], refs[len(outer) :]
        inner_refs, refs = refs[: len(inner)], refs[len(inner) :]
        gwq_ref, gab_ref, gwo_ref, gwi_ref, gbi_ref, gwf_ref, gain_ref, shift_ref = refs
        spot = place_ref[0]

        def total(refs, at, columns):
            value = refs[0][:, pl.ds(at, columns)].astype(F32)
            for ref in refs[1:]:
                value = value + ref[:, pl.ds(at, columns)].astype(F32)
            return value

        def own(block, size):
            return pltpu.roll(block, block.shape[1] - spot * size, 1)

        def unfolded(block, count):
            return jnp.concatenate([block[step : step + 1] for step in range(count)], 1)

        for layer, refs, at in ((0, outer_refs, middle), (1, inner_refs, 0)):
            gwq_ref[layer] = total(refs, at, 3 * width)
            block = total(refs, at + 3 * width, 128)
            many = width // 128
            for index in range(2):
                line = unfolded(block[index * many : (index + 1) * many], many)
                gab_ref[layer, pl.ds(index, 1)] = own(line, rows)[:, 0:rows]
        for layer, refs, at in ((0, inner_refs, 3 * width + 128), (1, outer_refs, 0)):
            gwo_ref[layer] = total(refs, at, width)
            gwi_ref[layer] = total(refs, at + width, hidden)
            for step in range(hidden // width):
                gwf_ref[layer, pl.ds(step * rows, rows)] = total(
                    refs, at + width + hidden + step * width, width
                )
            at += width + 2 * hidden
            small = own(total(refs, at, width), rows)
            gain_ref[layer] = small[2:4, 0:rows]
            shift_ref[layer] = small[4:8, 0:rows]
            line = unfolded(total(refs, at + width, hidden // 8), 8)
            gbi_ref[pl.ds(layer, 1)] = own(line, height)[:, 0:height]

    outs = [
        struct((depth, rows, 3 * width), F32),
        struct((depth, 2, rows), F32),
        struct((depth, rows, width), F32),
        struct((depth, rows, hidden), F32),
        struct((depth, height), F32),
        struct((depth, height, width), F32),
        struct((depth, 2, rows), F32),
        struct((depth, 4, rows), F32),
    ]
    return pl.pallas_call(
        kernel,
        in_specs=[pl.BlockSpec(memory_space=pltpu.SMEM)]
        + [pl.BlockSpec(memory_space=pltpu.VMEM)] * (len(outer) + len(inner)),
        out_shape=outs,
        compiler_params=pltpu.CompilerParams(vmem_limit_bytes=MEMORY),
    )(place, *outer, *inner)


def exchange(parts, axis):
    return lax.all_to_all(parts, axis, 0, 0, tiled=True)


def swap(part, axis, step):
    size = lax.axis_size(axis)
    return lax.ppermute(part, axis, [(source, source ^ step) for source in range(size)])


def local(
    hidden_in,
    lengths,
    grad_out,
    attn_weight,
    attn_bias,
    out_weight,
    ffn_in,
    ffn_in_bias,
    ffn_out,
    norm_gain,
    shifts,
):
    depth, rows, width = out_weight.shape
    hidden = ffn_in.shape[2]
    first, second = lax.axis_size("dp"), lax.axis_size("fsdp")
    fits = (second, first, rows) == GROUPS
    urgent_size = 3 * width + 128
    if fits:
        early, later = pack_parameters(
            attn_weight, attn_bias, out_weight, ffn_in, ffn_in_bias, ffn_out, norm_gain, shifts
        )
        across = lax.axis_index("dp").astype(jnp.int32).reshape(1)
        place = lax.axis_index("fsdp").astype(jnp.int32).reshape(1)
        partners = range(1, second)
        x0, dz1 = rotate_kernel(lengths, (hidden_in, grad_out))
        early = hold(exchange(early, "dp"), (x0,))
        urgent = early[:, :urgent_size]
        urgent = [urgent] + [swap(urgent, "fsdp", step) for step in partners]
        raw0 = early[:, urgent_size:]
        raw0 = [raw0, swap(raw0, "fsdp", 1), swap(raw0, "fsdp", 2)]
    else:
        urgent, raw0, raw1 = gather_other(
            attn_weight, attn_bias, out_weight, ffn_in, ffn_in_bias, ffn_out, norm_gain, shifts
        )
        urgent, raw0, raw1 = ([part[step] for step in range(4)] for part in (urgent, raw0, raw1))
        place = jnp.zeros((1,), jnp.int32)
        x0, dz1 = rotate_kernel(lengths, (hidden_in, grad_out))

    qa0, ka0, va0, ob0, lse0, urgent = first_kernel(lengths, x0, place, urgent)
    if fits:
        raw0[2] = hold(raw0[2], (ob0,))
        raw0.append(swap(raw0[2], "fsdp", 1))
        later = exchange(hold(later, (ob0,)), "dp")
    n1, n2, inv, yb, gb, gp, z0 = dense_kernel(
        0, lengths, x0, ob0, place, urgent, raw0, 3 * width, hidden
    )
    if fits:
        raw1 = hold(later, (z0,))
        raw1 = [raw1, swap(raw1, "fsdp", 1), swap(raw1, "fsdp", 2)]
    qa1, ka1, va1, ob1, lse1 = attention_kernel(1, lengths, z0, place, urgent, raw0, 0)
    if fits:
        raw1[2] = hold(raw1[2], (ob1,))
        raw1.append(swap(raw1[2], "fsdp", 1))
    z1, dr1, dob1, *sent_a = turn_kernel(
        1, lengths, z0, ob1, dz1, place, urgent, raw1, 0, hidden
    )
    dr0, dob0, *sent_b = middle_kernel(
        lengths,
        (z0, dob1, ob1, qa1, ka1, va1, lse1, dr1),
        (n1, n2, inv, yb, gb, gp, ob0),
        place,
        urgent,
        raw0,
        hidden,
        (sent_a[0],),
    )
    if fits:
        got_a = [sent_a[0]] + [swap(sent_a[step], "fsdp", step) for step in partners]
        keep_a, give_a = add_parts(across, got_a, True, (sent_b[0],))
        got_ax = swap(give_a, "dp", 1)
        ready = (sent_b[0], keep_a)
    else:
        ready = ()
    dqkv, *sent_c = last_kernel(
        lengths, (x0, dob0, ob0, qa0, ka0, va0, lse0), ready, place
    )
    hidden_out, grad_in = tokens_kernel(lengths, z1, dqkv, dr0, urgent)
    if fits:
        got_b = [sent_b[0]] + [swap(sent_b[step], "fsdp", step) for step in partners]
        got_c = [sent_c[0]] + [swap(sent_c[step], "fsdp", step) for step in partners]
        keep_c, give_c = add_parts(across, got_c, True, (grad_in,))
        got_cx = swap(give_c, "dp", 1)
        keep_b, give_b = add_parts(across, got_b, True, (keep_c,))
        got_bx = swap(give_b, "dp", 1)
        far = range(1, first // 2)
        outer = add_halves(across, [(keep_a, got_ax), (keep_c, got_cx)], (keep_b,))
        inner = add_halves(across, [(keep_b, got_bx)], (outer[0],))
        outer = [outer[0]] + [swap(outer[step], "dp", 2 * step) for step in far]
        inner = [inner[0]] + [swap(inner[step], "dp", 2 * step) for step in far]
        spot = lax.axis_index(("dp", "fsdp")).astype(jnp.int32).reshape(1)
        grads = write_gradients(spot, outer, inner, depth, width, hidden)
    else:
        grads = scatter_other(
            *(jnp.stack(part) for part in (sent_a, sent_b, sent_c)), rows, width, hidden
        )
    return (hidden_out, grad_in, *grads)


def gather_other(
    attn_weight, attn_bias, out_weight, ffn_in, ffn_in_bias, ffn_out, norm_gain, shifts
):
    axes = ("dp", "fsdp")
    gather = lambda part, axis: lax.all_gather(part, axes, axis=axis, tiled=True)
    depth, unused, width = out_weight.shape
    hidden = ffn_in.shape[2]
    outer, inner, rows = GROUPS
    vectors = gather(jnp.concatenate([attn_bias, norm_gain, shifts], 1), 2)
    line = gather(ffn_in_bias, 1)

    def order(natural):
        return (
            natural.reshape(inner, outer, rows, -1).swapaxes(0, 1).reshape(outer, inner * rows, -1)
        )

    def stacked(part):
        part = part.reshape(DEVICES, -1, rows, width)
        return order(part.swapaxes(1, 2).reshape(width, -1))

    small = vectors.reshape(depth, 8, DEVICES, rows).transpose(2, 1, 0, 3).reshape(width, -1)
    line = line.reshape(depth, DEVICES, -1).swapaxes(0, 1)
    line = jnp.pad(line, ((0, 0), (0, 8 - depth), (0, 0))).reshape(width, -1)
    small = jnp.concatenate([small, line], 1)
    small = jnp.pad(small, ((0, 0), (0, 128 - small.shape[1])))
    wq, wo, wi, wf = (gather(part, 1) for part in (attn_weight, out_weight, ffn_in, ffn_out))
    urgent = jnp.concatenate([order(wq[0]), order(small)], 2)
    raw0 = jnp.concatenate([order(wq[1]), order(wo[0]), order(wi[0]), stacked(wf[0])], 2)
    raw1 = jnp.concatenate([order(wo[1]), order(wi[1]), stacked(wf[1])], 2)
    return urgent, raw0, raw1


def scatter_other(sent_a, sent_b, sent_c, own_rows, width, hidden):
    outer, inner, rows = GROUPS
    axes = ("dp", "fsdp")

    def natural(part):
        return part.reshape(outer, inner, rows, -1).swapaxes(0, 1).reshape(width, -1).astype(F32)

    def cut(part, sizes):
        found, at = [], 0
        for size in sizes:
            found.append(part[:, at : at + size])
            at += size
        return found

    dense = [width, hidden, hidden, width, hidden // 8]
    attention = [3 * width, 128]
    wq0, ab0 = cut(natural(sent_c), attention)
    wq1, ab1, wo0, wi0, wf0, small0, bi0 = cut(natural(sent_b), attention + dense)
    wo1, wi1, wf1, small1, bi1 = cut(natural(sent_a), dense)

    def stacked(part):
        part = part.reshape(DEVICES, rows, -1, width).swapaxes(1, 2)
        return part.reshape(hidden, width)

    def spread(parts, axis):
        return lax.psum_scatter(jnp.stack(parts), axes, scatter_dimension=axis, tiled=True)

    return (
        spread([wq0, wq1], 1),
        spread([ab0[:4].reshape(2, width), ab1[:4].reshape(2, width)], 2),
        spread([wo0, wo1], 1),
        spread([wi0, wi1], 1),
        spread([bi0[:8].reshape(-1), bi1[:8].reshape(-1)], 1),
        spread([stacked(wf0), stacked(wf1)], 1),
        spread([small0[2:4], small1[2:4]], 2),
        spread([small0[4:8], small1[4:8]], 2),
    )


def solution(mesh):
    placed = (
        P(("dp", "fsdp"), None),
        P(("dp", "fsdp"), None),
        P(("dp", "fsdp"), None),
        P(None, ("dp", "fsdp"), None),
        P(None, None, ("dp", "fsdp")),
        P(None, ("dp", "fsdp"), None),
        P(None, ("dp", "fsdp"), None),
        P(None, ("dp", "fsdp")),
        P(None, ("dp", "fsdp"), None),
        P(None, None, ("dp", "fsdp")),
        P(None, None, ("dp", "fsdp")),
    )
    return jax.shard_map(
        local,
        mesh=mesh,
        in_specs=placed,
        out_specs=(
            P(("dp", "fsdp"), None),
            P(("dp", "fsdp"), None),
            P(None, ("dp", "fsdp"), None),
            P(None, None, ("dp", "fsdp")),
            P(None, ("dp", "fsdp"), None),
            P(None, ("dp", "fsdp"), None),
            P(None, ("dp", "fsdp")),
            P(None, ("dp", "fsdp"), None),
            P(None, None, ("dp", "fsdp")),
            P(None, None, ("dp", "fsdp")),
        ),
        check_vma=False,
    )
```

```python
from functools import partial

import jax
import jax.numpy as jnp
from jax import lax
from jax.experimental import pallas as pl
from jax.experimental.pallas import tpu as pltpu
from jax.sharding import PartitionSpec as P

HEADS = 4
HD = 64
SEQ = 512
PAIR = 2 * HD
EXTRA = 16
HALF = SEQ // 2
HALVES = (slice(0, HALF), slice(HALF, SEQ))
FAR = -(2.0**100)
FLOOR = -1e20
EPSILON = 1e-12
PIECE = 256
SMALL = 128
GROUPS = (4, 8, 8)
DEVICES = 32
LOW = jnp.bfloat16
F32 = jnp.float32
MEMORY = 2**26


def dot_nn(left, right):
    return lax.dot_general(left, right, (((1,), (0,)), ((), ())), preferred_element_type=F32)


def dot_nt(left, right):
    return lax.dot_general(left, right, (((1,), (1,)), ((), ())), preferred_element_type=F32)


def dot_tn(left, right):
    return lax.dot_general(left, right, (((0,), (0,)), ((), ())), preferred_element_type=F32)


def pieces(total, size=PIECE):
    return [pl.ds(start, size) for start in range(0, total, size)]


def three_parts(values):
    first = values.astype(LOW).astype(F32)
    rest = values - first
    second = rest.astype(LOW).astype(F32)
    return first, second, rest - second


BELL = -0.5 / 0.6931471805599453


def gelu_parts(u):
    cumulative = 0.5 + 0.5 * lax.erf(u * 0.7071067811865476)
    slope = cumulative + (u * 0.3989422804014327) * jnp.exp2(u * u * BELL)
    return u * cumulative, slope


def inverse_of(values):
    guess = pl.reciprocal(values, approx=True)
    return guess * (2.0 - values * guess)


def longest_start(lengths_ref, row):
    begin, found = jnp.int32(0), jnp.int32(0)
    for entry in range(lengths_ref.shape[1]):
        size = lengths_ref[row, entry]
        found = jnp.where(size == HALF, begin, found)
        begin = begin + size
    return found


def segments(lengths_ref, row):
    places = lax.broadcasted_iota(jnp.int32, (1, SEQ), 1) + longest_start(lengths_ref, row)
    places = places & (SEQ - 1)
    bound = jnp.int32(0)
    segment = jnp.zeros((1, SEQ), jnp.int32)
    last = lengths_ref.shape[1] - 1
    for entry in range(last):
        bound = bound + lengths_ref[row, entry]
        segment = segment + (places >= bound).astype(jnp.int32)
    return segment, last


def head_rows(head):
    return slice(head * HD, (head + 1) * HD)


def attention_forward(row, lengths_ref, x, wt_ref, bias_ref, qa_ref, ka_ref, va_ref, ob_ref, lse_ref, s_ref, p_ref):
    width = HEADS * HD
    segment, last = segments(lengths_ref, row)
    pad = (segment == last).astype(F32)
    line = lax.broadcasted_iota(jnp.int32, (EXTRA, SEQ), 0)
    aug_q = jnp.where(line == segment, 1.0, 0.0).astype(LOW)
    seen = (line == segment) & (segment != last)
    aug_k = jnp.where(seen | (line > last), 0.0, FAR).astype(LOW)
    aug_v = jnp.where(line == 0, 1.0, 0.0).astype(LOW)
    rest = jnp.zeros((PAIR - HD - EXTRA, SEQ), LOW)
    for head in range(HEADS):
        qa_ref[head, HD : HD + EXTRA] = aug_q
        ka_ref[head, HD : HD + EXTRA] = aug_k
        va_ref[head, HD : HD + EXTRA] = aug_v
        qa_ref[head, HD + EXTRA : PAIR] = rest
        ka_ref[head, HD + EXTRA : PAIR] = rest
    for block, ref in enumerate((qa_ref, ka_ref, va_ref)):
        lines = slice(block * width, (block + 1) * width)
        bias = bias_ref[lines]
        value = dot_nt(wt_ref[lines], x) + jnp.concatenate([bias] * (SEQ // 128), 1)
        if block == 0:
            value = value * HD**-0.5
        value = value.astype(LOW)
        for head in range(HEADS):
            ref[head, 0:HD] = value[head_rows(head)]
        yield

    def scores(head):
        for half in HALVES:
            s_ref[head % 2, half] = dot_tn(ka_ref[head, :, half], qa_ref[head, :, half])

    def softmax(head):
        tops = []
        for half in HALVES:
            tops.append(jnp.maximum(jnp.max(s_ref[head % 2, half], 0, keepdims=True), FLOOR))
            p_ref[head % 2, half] = jnp.exp(s_ref[head % 2, half] - tops[-1]).astype(LOW)
        return tops

    scores(0)
    yield
    for head in range(HEADS):
        if head + 1 < HEADS:
            scores(head + 1)
            yield
        tops = softmax(head)
        yield
        for half, top in zip(HALVES, tops):
            out = dot_nn(va_ref[head, :, half], p_ref[head % 2, half])
            alone = pad[:, half]
            total = out[HD : HD + 1] + alone
            lse_ref[head : head + 1, half] = jnp.where(alone > 0, 0.0, top + jnp.log(total))
            own = alone * va_ref[head, 0:HD, half].astype(F32)
            ob_ref[head_rows(head), half] = (out[0:HD] * inverse_of(total) + own).astype(LOW)
        yield


def normal(values):
    centred = values - jnp.mean(values, -1, keepdims=True)
    inverse = lax.rsqrt(jnp.mean(centred * centred, -1, keepdims=True) + EPSILON)
    return centred * inverse, inverse


def normal_back(cotangent, unit, inverse, gains):
    scaled = cotangent * gains
    return inverse * (
        scaled
        - jnp.mean(scaled, -1, keepdims=True)
        - unit * jnp.mean(scaled * unit, -1, keepdims=True)
    )


def dense_forward(x_ref, ob_ref, wo_ref, wi_ref, wf_ref, small_ref, bi_ref, n1_ref, n2_ref, inv_ref, yb_ref, gb_ref, gp_ref, z_ref, work_ref, u_ref):
    small = lambda index: small_ref[pl.ds(index, 1)]
    work_ref[...] = dot_tn(ob_ref[...], wo_ref[...])
    yield
    for place in pieces(SEQ):
        unit, inverse = normal(x_ref[place].astype(F32) + work_ref[place] + small(4))
        n1_ref[place] = unit
        inv_ref[place, pl.ds(0, HD)] = jnp.broadcast_to(inverse, (PIECE, HD))
        y = unit * small(2) + small(5)
        yb_ref[place] = y.astype(LOW)
        work_ref[place] = y + small(6)
        yield
    columns = 256
    count = wi_ref.shape[1] // columns

    def into(step):
        u_ref[step % 2] = dot_nn(yb_ref[...], wi_ref[:, pl.ds(step * columns, columns)])

    into(0)
    yield
    for step in range(count):
        if step + 1 < count:
            into(step + 1)
            yield
        lanes = pl.ds(step * columns, columns)
        for place in pieces(SEQ, SMALL):
            g, slope = gelu_parts(u_ref[step % 2, place] + bi_ref[:, lanes])
            gb_ref[place, lanes] = g.astype(LOW)
            gp_ref[place, lanes] = slope.astype(LOW)
            yield
    work_ref[...] += dot_nn(gb_ref[...], wf_ref[...])
    yield
    for place in pieces(SEQ):
        unit, inverse = normal(work_ref[place])
        n2_ref[place] = unit
        inv_ref[place, pl.ds(HD, HD)] = jnp.broadcast_to(inverse, (PIECE, HD))
        z_ref[place] = (unit * small(3) + small(7)).astype(z_ref.dtype)
        yield


def fold(values):
    return jnp.sum(values.reshape(-1, 8, values.shape[-1]), 0)


def dense_backward(dz_ref, n1_ref, n2_ref, inv_ref, yb_ref, gb_ref, gp_ref, ob_ref, wo_ref, wi_ref, wf_ref, small_ref, dr_ref, dob_ref, gwo_ref, gwi_ref, gwf_ref, gsmall_ref, gbi_ref, low_ref, u_ref, du_ref, turned_ref):
    small = lambda index: small_ref[pl.ds(index, 1)]
    for place in pieces(SEQ):
        dz = dz_ref[place].astype(F32)
        unit = n2_ref[place]
        gsmall_ref[3] += fold(dz * unit)
        gsmall_ref[7] += fold(dz)
        dr = normal_back(dz, unit, inv_ref[place, pl.ds(HD, 1)], small(3))
        dr_ref[place] = dr
        df = dr.astype(LOW)
        low_ref[place] = df
        gsmall_ref[6] += fold(df.astype(F32))
        yield
    columns = 256
    count = wi_ref.shape[1] // columns

    def back(step):
        u_ref[step % 2] = dot_nt(low_ref[...], wf_ref[pl.ds(step * columns, columns)])

    back(0)
    turned_ref[0, 0 : low_ref.shape[1]] = low_ref[...].T
    width = low_ref.shape[1]
    turned_ref[1, 0:width] = yb_ref[...].T
    turned_ref[1, width:] = jnp.ones((EXTRA, SEQ), LOW)
    yield
    for step in range(count):
        if step + 1 < count:
            back(step + 1)
            yield
        lanes = pl.ds(step * columns, columns)
        gwf_ref[:, lanes] += dot_nn(turned_ref[0, 0:width], gb_ref[:, lanes])
        yield
        for place in pieces(SEQ, SMALL):
            du = (u_ref[step % 2, place] * gp_ref[place, lanes].astype(F32)).astype(LOW)
            du_ref[place, lanes] = du
        yield
        product = dot_nn(turned_ref[1], du_ref[:, lanes])
        gwi_ref[:, lanes] += product[0:width]
        gbi_ref[:, lanes] += product[width : width + 8]
        yield
    u_ref[0] = dot_nt(du_ref[...], wi_ref[...])
    yield
    for place in pieces(SEQ):
        dy = dr_ref[place] + u_ref[0, place]
        unit = n1_ref[place]
        gsmall_ref[2] += fold(dy * unit)
        gsmall_ref[5] += fold(dy)
        dr = normal_back(dy, unit, inv_ref[place, pl.ds(0, 1)], small(2))
        dr_ref[place] = dr
        da = dr.astype(LOW)
        low_ref[place] = da
        gsmall_ref[4] += fold(da.astype(F32))
        yield
    gwo_ref[...] += dot_nn(ob_ref[...], low_ref[...])
    dob_ref[...] = dot_nt(wo_ref[...], low_ref[...]).astype(LOW)
    yield


def attention_backward(row, lengths_ref, x, do_ref, ob_ref, qa_ref, ka_ref, va_ref, lse_ref, dqkv_ref, gwq_ref, gbias_ref, p_ref, ds_ref, s_ref):
    width = HEADS * HD
    segment, last = segments(lengths_ref, row)
    pad = (segment == last).astype(F32)

    def scores(head):
        for half in HALVES:
            s_ref[0, head % 2, half] = dot_tn(ka_ref[head, :, half], qa_ref[head, :, half])
            s_ref[1, head % 2, half] = dot_tn(
                va_ref[head, 0:HD, half], do_ref[head_rows(head), half]
            )

    def weigh(head):
        product = do_ref[head_rows(head)].astype(F32) * ob_ref[head_rows(head)].astype(F32)
        centre = jnp.sum(product, 0, keepdims=True)
        for half in HALVES:
            p = jnp.exp(s_ref[0, head % 2, half] - lse_ref[head : head + 1, half])
            p_ref[head % 2, half] = p.astype(LOW)
            ds_ref[head % 2, half] = (p * (s_ref[1, head % 2, half] - centre[:, half])).astype(LOW)

    scores(0)
    yield
    for head in range(HEADS):
        if head + 1 < HEADS:
            scores(head + 1)
            yield
        weigh(head)
        yield
        for half in HALVES:
            ds, do = ds_ref[head % 2, half], do_ref[head_rows(head), half]
            dq = dot_nn(ka_ref[head, 0:HD, half], ds) * HD**-0.5
            dk = dot_nt(qa_ref[head, 0:HD, half], ds)
            dv = dot_nt(do, p_ref[head % 2, half]) + pad[:, half] * do.astype(F32)
            for block, value in enumerate((dq, dk, dv)):
                at = block * width + head * HD
                dqkv_ref[at : at + HD, half] = value.astype(LOW)
        yield
    for index, block in enumerate((0, 2)):
        value = dqkv_ref[block * width : (block + 1) * width].astype(F32)
        parts = [value[:, at : at + 128] for at in range(0, SEQ, 128)]
        gbias_ref[index] += (parts[0] + parts[1]) + (parts[2] + parts[3])
    gwq_ref[...] += dot_nn(dqkv_ref[...], x)
    yield


def unpack_matrix(raw_ref, at, into_ref):
    width = into_ref.shape[0]
    for start in range(0, into_ref.shape[1], width):
        block = raw_ref[:, :, pl.ds(at + start, width)].astype(F32)
        block = block.reshape(GROUPS + (width,)).swapaxes(0, 1).reshape(width, width)
        into_ref[:, pl.ds(start, width)] = block.astype(LOW)


def unpack_stacked(raw_ref, at, into_ref):
    width = into_ref.shape[1]
    count = into_ref.shape[0] // width
    blocks = [
        raw_ref[:, :, pl.ds(at + step * width, width)].astype(F32).reshape(GROUPS + (width,))
        for step in range(count)
    ]
    outer, inner, rows = GROUPS
    for place in range(inner):
        part = jnp.stack([jnp.stack([block[f, place] for block in blocks]) for f in range(outer)])
        size = outer * count * rows
        into_ref[pl.ds(place * size, size)] = part.reshape(size, width).astype(LOW)


def counter(shape, axis):
    return lax.broadcasted_iota(jnp.int32, shape, axis)


def split_by(values, size):
    return lax.shift_right_logical(values, size.bit_length() - 1), values & (size - 1)


def sources(rows):
    outer, inner, height = GROUPS
    group, within = split_by(counter((rows, 1), 0), height)
    far, near = split_by(group, inner)
    return near * outer + far, within


def unpack_vectors(raw_ref, at, layer):
    outer, inner, rows = GROUPS
    total = outer * inner * rows
    raw = raw_ref[:, :, pl.ds(at, 128)].reshape(total, 128)
    owner, place = split_by(counter((1, total), 1), rows)
    pick = jnp.where(counter((128, 1), 0) == rows * layer + place, 1.0, 0.0).astype(LOW)
    device, unused = sources(total)
    spread = jnp.where(owner == device, dot_nn(raw, pick), 0.0)
    return jnp.sum(spread.reshape(outer * inner, rows, total), 0)


def unpack_hidden(raw_ref, at, layer, hidden):
    outer, inner, rows = GROUPS
    total = outer * inner * rows
    raw = raw_ref[:, :, pl.ds(at, 128)].reshape(total, 128)
    owner, place = split_by(counter((1, hidden), 1), hidden // (outer * inner))
    pick = jnp.where(counter((128, 1), 0) == 2 * rows + place, 1.0, 0.0).astype(LOW)
    device, within = sources(total)
    device = jnp.where(within == layer, device, -1)
    spread = jnp.where(owner == device, dot_nn(raw, pick), 0.0)
    return jnp.sum(spread, 0, keepdims=True)


def pack_matrix(sum_ref, sent_ref, at, turned=False):
    width = sum_ref.shape[1 if turned else 0]
    outer, inner, rows = GROUPS
    for start in range(0, sum_ref.shape[0 if turned else 1], width):
        near = pl.ds(start, width)
        block = sum_ref[near].T if turned else sum_ref[:, near]
        block = block.reshape(inner, outer, rows, width)
        block = block.swapaxes(0, 1).reshape(outer, inner * rows, width)
        sent_ref[:, :, pl.ds(at + start, width)] = block.astype(LOW)


def pack_stacked(sum_ref, sent_ref, at):
    width = sum_ref.shape[0]
    outer, inner, rows = GROUPS
    count = sum_ref.shape[1] // width
    near = inner // count
    for step in range(count):
        block = sum_ref[:, pl.ds(step * width, width)].T
        block = block.reshape(near, outer, count, rows, width)
        for part in range(count):
            piece = jnp.stack([block[:, f, part] for f in range(outer)])
            piece = piece.reshape(outer, near * rows, width)
            sent_ref[:, pl.ds(step * near * rows, near * rows), pl.ds(at + part * width, width)] = (
                piece.astype(LOW)
            )


def pack_shared(block, sent_ref, at):
    outer, inner, rows = GROUPS
    columns = block.shape[1]
    block = jnp.broadcast_to(block[None], (outer * inner, rows, columns))
    sent_ref[:, :, pl.ds(at, columns)] = block.reshape(outer, inner * rows, columns).astype(LOW)


def folded(line, lanes):
    return [line[:, at : at + lanes] for at in range(0, line.shape[1], lanes)]


def pack_attention(gwq_ref, gbias_ref, sent_ref, at):
    pack_matrix(gwq_ref, sent_ref, at, True)
    width = gwq_ref.shape[1]
    parts = []
    for index in range(2):
        parts += folded(jnp.sum(gbias_ref[index].T, 0, keepdims=True), 128)
    block = jnp.concatenate(parts + [jnp.zeros((8 - len(parts), 128), F32)], 0)
    pack_shared(block, sent_ref, at + 3 * width)


def pack_dense(gwo_ref, gwi_ref, gwf_ref, gsmall_ref, gbi_ref, sent_ref, at):
    width, hidden = gwi_ref.shape
    pack_matrix(gwo_ref, sent_ref, at)
    pack_matrix(gwi_ref, sent_ref, at + width)
    pack_stacked(gwf_ref, sent_ref, at + width + hidden)
    at = at + width + 2 * hidden
    pack_shared(jnp.sum(gsmall_ref[...], 1), sent_ref, at)
    line = gbi_ref[0:1]
    pack_shared(jnp.concatenate(folded(line, hidden // 8), 0), sent_ref, at + width)


def shape_of(array):
    return jax.ShapeDtypeStruct(array.shape, array.dtype)


def by_row(shape, group):
    if len(shape) == 2:
        return pl.BlockSpec((group * SEQ, shape[1]), lambda step: (step, 0))
    return pl.BlockSpec((group,) + tuple(shape[1:]), lambda step: (step,) + (0,) * (len(shape) - 1))


def one_row(ref, member):
    if len(ref.shape) == 2:
        return ref.at[pl.ds(member * SEQ, SEQ)]
    return ref.at[member]


def alternate(runs):
    running = []
    waiting = list(runs)
    while running or waiting:
        if waiting:
            running.append(waiting.pop(0))
        for run in list(running):
            try:
                next(run)
            except StopIteration:
                running.remove(run)


def whole(shape):
    return pl.BlockSpec(tuple(shape), lambda row: (0,) * len(shape))


def run_rows(
    body, lengths, rowwise, fixed, row_outs, sent, shared, private, cost, setup, finish, after=(),
    scalars=(), group=1
):
    count = lengths.shape[0]
    group = group if count % group == 0 else 1
    cuts = [len(scalars), len(rowwise), len(fixed), len(after), len(row_outs), len(sent)]
    cuts += [len(shared)] + [len(private)] * group

    def kernel(lengths_ref, *refs):
        step = pl.program_id(0)
        groups = []
        at = 0
        for cut in cuts:
            groups.append(refs[at : at + cut])
            at += cut
        numbers, rows_in, fixed_in, unused, rows_out, sent_out, work = groups[:7]

        @pl.when(step == 0)
        def _():
            setup(numbers, fixed_in, sent_out, work)

        alternate(
            body(
                step * group + member,
                lengths_ref,
                [one_row(ref, member) for ref in rows_in],
                [one_row(ref, member) for ref in rows_out],
                work,
                groups[7 + member],
            )
            for member in range(group)
        )

        if finish:

            @pl.when(step == count // group - 1)
            def _():
                finish(numbers, work, sent_out)

    return pl.pallas_call(
        kernel,
        grid=(count // group,),
        in_specs=[pl.BlockSpec(memory_space=pltpu.SMEM)] * (1 + len(scalars))
        + [by_row(array.shape, group) for array in rowwise]
        + [whole(array.shape) for array in fixed]
        + [pl.BlockSpec(memory_space=pl.ANY) for array in after],
        out_specs=[by_row(part.shape, group) for part in row_outs]
        + [whole(part.shape) for part in sent],
        out_shape=list(row_outs) + list(sent),
        scratch_shapes=list(shared) + list(private) * group,
        compiler_params=pltpu.CompilerParams(
            dimension_semantics=("arbitrary",), vmem_limit_bytes=MEMORY
        ),
        cost_estimate=pl.CostEstimate(flops=cost, bytes_accessed=8 * 2**20, transcendentals=0),
    )(lengths, *scalars, *rowwise, *fixed, *after)


def struct(shape, dtype):
    return jax.ShapeDtypeStruct(tuple(shape), dtype)


FORWARD_SCRATCH = lambda: [
    pltpu.VMEM((2, SEQ, HALF), F32),
    pltpu.VMEM((2, SEQ, HALF), LOW),
]
BACKWARD_SCRATCH = lambda: [
    pltpu.VMEM((2, SEQ, HALF), LOW),
    pltpu.VMEM((2, SEQ, HALF), LOW),
    pltpu.VMEM((2, 2, SEQ, HALF), F32),
    pltpu.VMEM((3 * HEADS * HD, SEQ), LOW),
]


def attention_outs(rows, width):
    return [
        struct((rows, HEADS, PAIR, SEQ), LOW),
        struct((rows, HEADS, PAIR, SEQ), LOW),
        struct((rows, HEADS, HD + EXTRA, SEQ), LOW),
        struct((rows, width, SEQ), LOW),
        struct((rows, 8, SEQ), F32),
    ]


def dense_outs(tokens, width, hidden):
    return [
        struct((tokens, width), F32),
        struct((tokens, width), F32),
        struct((tokens, PAIR), F32),
        struct((tokens, width), LOW),
        struct((tokens, hidden), LOW),
        struct((tokens, hidden), LOW),
    ]


def vmem(shape, dtype):
    return pltpu.VMEM(tuple(shape), dtype)


def attention_weights(width):
    return [vmem((width, 3 * width), LOW), vmem((3 * width, width), LOW), vmem((3 * width, 128), F32)]


def dense_weights(width, hidden):
    return [
        vmem((width, width), LOW),
        vmem((width, hidden), LOW),
        vmem((hidden, width), LOW),
        vmem((8, width), F32),
        vmem((1, hidden), F32),
    ]


def dense_sums(width, hidden):
    return [
        vmem((width, width), F32),
        vmem((width, hidden), F32),
        vmem((width, hidden), F32),
        vmem((8, 8, width), F32),
        vmem((8, hidden), F32),
    ]


def attention_sums(width):
    return [vmem((3 * width, width), F32), vmem((2, width, 128), F32)]


def dense_work(width, hidden):
    return [
        vmem((SEQ, width), LOW),
        vmem((2, SEQ, width), F32),
        vmem((SEQ, hidden), LOW),
        vmem((2, width + EXTRA, SEQ), LOW),
    ]


def set_attention(layer, urgent_ref, raw_ref, at, wq_ref, wt_ref, bias_ref):
    width = wq_ref.shape[0]
    unpack_matrix(raw_ref, at, wq_ref)
    vectors = unpack_vectors(urgent_ref, 3 * width, layer)
    for block, line in enumerate((vectors[0:1], jnp.zeros((1, width), F32), vectors[1:2])):
        lines = pl.ds(block * width, width)
        wt_ref[lines] = wq_ref[:, lines].astype(F32).T.astype(LOW)
        bias_ref[lines] = jnp.broadcast_to(line, (128, width)).T


def set_dense(layer, urgent_ref, raw_ref, at, wo_ref, wi_ref, wf_ref, small_ref, bi_ref):
    width, hidden = wi_ref.shape
    unpack_matrix(raw_ref, at, wo_ref)
    unpack_matrix(raw_ref, at + width, wi_ref)
    unpack_stacked(raw_ref, at + width + hidden, wf_ref)
    small_ref[...] = unpack_vectors(urgent_ref, 3 * width, layer)
    bi_ref[...] = unpack_hidden(urgent_ref, 3 * width, layer, hidden)


def clear(refs):
    for ref in refs:
        ref[...] = jnp.zeros(ref.shape, ref.dtype)


def assemble(place_ref, part_refs, into_ref):
    for step, ref in enumerate(part_refs):
        into_ref[place_ref[0] ^ step] = ref[...]


def raw_block(parts):
    return vmem((len(parts),) + parts[0].shape, LOW)


def turned_back(lengths_ref, row, values):
    return pltpu.roll(values, longest_start(lengths_ref, row), 0).astype(LOW)


def rotate_kernel(lengths, arrays):
    def body(row, lengths_ref, rowwise, outs, work, own):
        back = (SEQ - longest_start(lengths_ref, row)) & (SEQ - 1)
        for source, target in zip(rowwise, outs):
            target[...] = pltpu.roll(source[...].astype(F32), back, 0).astype(LOW)
            yield

    return run_rows(
        body, lengths, list(arrays), [], [struct(array.shape, LOW) for array in arrays], [], [], [],
        10**6, lambda *refs: None, None,
    )


def first_kernel(lengths, x, place, parts):
    rows, (tokens, width) = lengths.shape[0], x.shape

    def setup(numbers, fixed, sent, work):
        assemble(numbers[0], fixed, sent[0])
        set_attention(0, sent[0], sent[0], 0, *work)

    def body(row, lengths_ref, rowwise, outs, work, own):
        return attention_forward(row, lengths_ref, rowwise[0][...], *work[1:3], *outs, *own)

    return run_rows(
        body, lengths, [x], list(parts), attention_outs(rows, width),
        [struct((len(parts),) + parts[0].shape, LOW)],
        attention_weights(width), FORWARD_SCRATCH(), 4 * 10**9, setup, None, (), [place],
    )


def attention_kernel(layer, lengths, x, place, urgent, parts, at):
    rows, (tokens, width) = lengths.shape[0], x.shape

    def setup(numbers, fixed, sent, work):
        assemble(numbers[0], fixed[1:], work[3])
        set_attention(layer, fixed[0], work[3], at, *work[:3])

    def body(row, lengths_ref, rowwise, outs, work, own):
        return attention_forward(
            row, lengths_ref, rowwise[0][...].astype(LOW), *work[1:3], *outs, *own
        )

    return run_rows(
        body, lengths, [x], [urgent] + list(parts), attention_outs(rows, width), [],
        attention_weights(width) + [raw_block(parts)], FORWARD_SCRATCH(),
        4 * 10**9, setup, None, (), [place],
    )


def dense_kernel(layer, lengths, x, ob, place, urgent, parts, at, hidden):
    tokens, width = x.shape

    def setup(numbers, fixed, sent, work):
        assemble(numbers[0], fixed[1:], work[5])
        set_dense(layer, fixed[0], work[5], at, *work[:5])

    def body(row, lengths_ref, rowwise, outs, work, own):
        return dense_forward(*rowwise, *work[:5], *outs, *own)

    return run_rows(
        body, lengths, [x, ob], [urgent] + list(parts),
        dense_outs(tokens, width, hidden) + [struct((tokens, width), F32)], [],
        dense_weights(width, hidden) + [raw_block(parts)],
        [vmem((SEQ, width), F32), vmem((2, SEQ, width), F32)],
        5 * 10**9, setup, None, (), [place],
    )


def turn_kernel(layer, lengths, x, ob, cotangent, place, urgent, parts, at, hidden):
    tokens, width = x.shape
    columns = width + 2 * hidden + width + hidden // 8

    def setup(numbers, fixed, sent, work):
        assemble(numbers[0], fixed[1:], work[11])
        set_dense(layer, fixed[0], work[11], at, *work[:5])
        clear(work[5:10])

    def body(row, lengths_ref, rowwise, outs, work, own):
        x_ref, ob_ref, dz_ref = rowwise
        z_ref, dr_ref, dob_ref = outs
        weights, sums = work[:5], work[5:10]
        kept, work_ref, back = own[:6], own[6], own[7:]
        yield from dense_forward(x_ref, ob_ref, *weights, *kept, z_ref, work_ref, back[1])
        yield from dense_backward(dz_ref, *kept, ob_ref, *weights[:4], dr_ref, dob_ref, *sums, *back)

    def finish(numbers, work, sent):
        pack_dense(*work[5:10], work[10], 0)
        hand_out(numbers[0], work[10], sent)

    kept = [vmem((SEQ,) + part.shape[1:], part.dtype) for part in dense_outs(tokens, width, hidden)]
    return run_rows(
        body, lengths, [x, ob, cotangent], [urgent] + list(parts),
        [struct((tokens, width), LOW), struct((tokens, width), F32), struct((tokens // SEQ, width, SEQ), LOW)],
        [struct((64, columns), LOW)] * 4,
        dense_weights(width, hidden) + dense_sums(width, hidden)
        + [vmem((4, 64, columns), LOW), raw_block(parts)],
        kept + [vmem((SEQ, width), F32)] + dense_work(width, hidden),
        10**10, setup, finish, (), [place], 2,
    )


def hand_out(place_ref, packed_ref, sent):
    for step, ref in enumerate(sent):
        ref[...] = packed_ref[place_ref[0] ^ step]


def middle_kernel(lengths, upper, lower, place, urgent, parts, hidden, after):
    tokens, width = upper[0].shape
    columns = 3 * width + 128 + width + 2 * hidden + width + hidden // 8

    def setup(numbers, fixed, sent, work):
        assemble(numbers[0], fixed[1:], work[16])
        set_attention(1, fixed[0], work[16], 0, *work[:3])
        set_dense(0, fixed[0], work[16], 3 * width, *work[3:8])
        clear(work[8:15])

    def body(row, lengths_ref, rowwise, outs, work, own):
        up, low = rowwise[:8], rowwise[8:]
        dx_ref = own[0]
        yield from attention_backward(
            row, lengths_ref, up[0][...].astype(LOW), *up[1:7], own[-1], *work[8:10], *own[5:-1]
        )
        dx_ref[...] = up[7][...] + dot_tn(own[-1][...], work[1][...])
        yield
        yield from dense_backward(dx_ref, *low, *work[3:7], *outs, *work[10:15], *own[1:5])

    def finish(numbers, work, sent):
        pack_attention(*work[8:10], work[15], 0)
        pack_dense(*work[10:15], work[15], 3 * width + 128)
        hand_out(numbers[0], work[15], sent)

    return run_rows(
        body, lengths, list(upper) + list(lower), [urgent] + list(parts),
        [struct((tokens, width), F32), struct((tokens // SEQ, width, SEQ), LOW)],
        [struct((64, columns), LOW)] * 4,
        attention_weights(width) + dense_weights(width, hidden)
        + attention_sums(width) + dense_sums(width, hidden)
        + [vmem((4, 64, columns), LOW), raw_block(parts)],
        [vmem((SEQ, width), F32)] + dense_work(width, hidden) + BACKWARD_SCRATCH(),
        15 * 10**9, setup, finish, after, [place], 2,
    )


def last_kernel(lengths, upper, after, place):
    tokens, width = upper[0].shape

    def setup(numbers, fixed, sent, work):
        clear(work[:2])

    def body(row, lengths_ref, rowwise, outs, work, own):
        return attention_backward(
            row, lengths_ref, rowwise[0][...], *rowwise[1:], outs[0], *work[:2], *own
        )

    def finish(numbers, work, sent):
        pack_attention(*work[:2], work[2], 0)
        hand_out(numbers[0], work[2], sent)

    return run_rows(
        body, lengths, list(upper), [], [struct((tokens // SEQ, 3 * width, SEQ), LOW)],
        [struct((64, 3 * width + 128), LOW)] * 4,
        attention_sums(width) + [vmem((4, 64, 3 * width + 128), LOW)],
        BACKWARD_SCRATCH()[:-1], 8 * 10**9, setup, finish, after, [place], 2,
    )


def outward_kernel(lengths, z):
    def body(row, lengths_ref, rowwise, outs, work, own):
        outs[0][...] = turned_back(lengths_ref, row, rowwise[0][...].astype(F32))
        yield

    (found,) = run_rows(
        body, lengths, [z], [], [struct(z.shape, LOW)], [], [], [], 3 * 10**9,
        lambda *refs: None, None,
    )
    return found


def inward_kernel(lengths, dqkv, dr, urgent, after):
    tokens, width = dr.shape

    def setup(numbers, fixed, sent, work):
        set_attention(0, fixed[0], fixed[0], 0, *work)

    def body(row, lengths_ref, rowwise, outs, work, own):
        dqkv_ref, dr_ref = rowwise
        dx = dr_ref[...] + dot_tn(dqkv_ref[...], work[1][...])
        outs[0][...] = turned_back(lengths_ref, row, dx)
        yield

    (found,) = run_rows(
        body, lengths, [dqkv, dr], [urgent], [struct((tokens, width), LOW)], [],
        attention_weights(width), [], 10**10, setup, None, after,
    )
    return found


def hold(array, after):
    def kernel(*refs):
        pass

    anywhere = pl.BlockSpec(memory_space=pl.ANY)
    return pl.pallas_call(
        kernel,
        in_specs=[anywhere] * (1 + len(after)),
        out_specs=anywhere,
        out_shape=shape_of(array),
        input_output_aliases={0: 0},
    )(array, *after)


def pack_parameters(
    attn_weight, attn_bias, out_weight, ffn_in, ffn_in_bias, ffn_out, norm_gain, shifts
):
    depth, rows, width = out_weight.shape
    copies = GROUPS[1]
    hidden = ffn_in.shape[2]
    dense = width + 2 * hidden
    height = ffn_in_bias.shape[1]

    def kernel(wq_ref, ab_ref, wo_ref, wi_ref, bi_ref, wf_ref, gain_ref, shift_ref, first_ref, rest_ref, small_ref):
        def put(ref, block, at):
            block = jnp.broadcast_to(block.astype(F32)[None], (copies,) + block.shape)
            block = block.reshape(copies * block.shape[1], block.shape[2])
            ref[:, pl.ds(at, block.shape[1])] = block.astype(LOW)

        small_ref[...] = jnp.zeros(small_ref.shape, F32)
        for layer in range(depth):
            lanes = pl.ds(rows * layer, rows)
            small_ref[0:2, lanes] = ab_ref[layer].astype(F32)
            small_ref[2:4, lanes] = gain_ref[layer].astype(F32)
            small_ref[4:8, lanes] = shift_ref[layer].astype(F32)
        small_ref[0:depth, pl.ds(2 * rows, height)] = bi_ref[...].astype(F32)
        put(first_ref, wq_ref[0], 0)
        put(first_ref, small_ref[...], 3 * width)
        put(first_ref, wq_ref[1], 3 * width + 128)
        for layer, ref, at in ((0, first_ref, 6 * width + 128), (1, rest_ref, 0)):
            put(ref, wo_ref[layer], at)
            put(ref, wi_ref[layer], at + width)
            at += width + hidden
            down = wf_ref[layer].astype(F32)
            for step in range(hidden // width):
                put(ref, down[step * rows : (step + 1) * rows], at)
                at += width

    return pl.pallas_call(
        kernel,
        in_specs=[pl.BlockSpec(memory_space=pltpu.VMEM)] * 8,
        out_shape=[
            struct((copies * rows, 6 * width + 128 + dense), LOW),
            struct((copies * rows, dense), LOW),
        ],
        scratch_shapes=[vmem((rows, 128), F32)],
        compiler_params=pltpu.CompilerParams(vmem_limit_bytes=MEMORY),
    )(attn_weight, attn_bias, out_weight, ffn_in, ffn_in_bias, ffn_out, norm_gain, shifts)


def add_parts(place, parts, halves, after=()):
    lanes = parts[0].shape[1]
    count = len(parts)
    many, rows = GROUPS[1:]
    outs = 2 if halves else 1

    def kernel(place_ref, *refs):
        out_refs, sum_ref = refs[count + len(after) : -1], refs[-1]
        bit = place_ref[0] & 1
        for start in range(0, lanes, 128):
            near = pl.ds(start, 128)
            total = refs[0][:, near].astype(F32)
            for ref in refs[1:count]:
                total = total + ref[:, near].astype(F32)
            if halves:
                sum_ref[:, :, near] = total.reshape(many, rows, 128)
            else:
                out_refs[0][:, near] = total.astype(LOW)
        for side, ref in enumerate(out_refs if halves else ()):
            for start in range(0, lanes, 128):
                near = pl.ds(start, 128)
                block = [sum_ref[2 * step + (bit ^ side), :, near] for step in range(many // 2)]
                ref[:, near] = jnp.concatenate(block, 0).astype(LOW)

    return pl.pallas_call(
        kernel,
        in_specs=[pl.BlockSpec(memory_space=pltpu.SMEM)]
        + [pl.BlockSpec(memory_space=pltpu.VMEM)] * count
        + [pl.BlockSpec(memory_space=pl.ANY)] * len(after),
        out_shape=[struct((many * rows // outs, lanes), LOW)] * outs,
        scratch_shapes=[vmem((many, rows, lanes), F32)],
        compiler_params=pltpu.CompilerParams(vmem_limit_bytes=MEMORY),
    )(place, *parts, *after)


def add_halves(place, pairs, after=()):
    many, rows = GROUPS[1] // 2, GROUPS[2]
    widths = [pair[0].shape[1] for pair in pairs]
    lanes = sum(widths)

    def kernel(place_ref, *refs):
        out_refs, sum_ref = refs[2 * len(pairs) + len(after) : -1], refs[-1]
        at = 0
        for index, size in enumerate(widths):
            for start in range(0, size, 128):
                near = pl.ds(start, 128)
                total = refs[2 * index][:, near].astype(F32) + refs[2 * index + 1][:, near].astype(F32)
                sum_ref[:, :, pl.ds(at + start, 128)] = total.reshape(many, rows, 128)
            at += size
        far = lax.shift_right_logical(place_ref[0], 1)
        for step, ref in enumerate(out_refs):
            ref[...] = sum_ref[far ^ step].astype(LOW)

    return pl.pallas_call(
        kernel,
        in_specs=[pl.BlockSpec(memory_space=pltpu.SMEM)]
        + [pl.BlockSpec(memory_space=pltpu.VMEM)] * (2 * len(pairs))
        + [pl.BlockSpec(memory_space=pl.ANY)] * len(after),
        out_shape=[struct((rows, lanes), LOW)] * many,
        scratch_shapes=[vmem((many, rows, lanes), F32)],
        compiler_params=pltpu.CompilerParams(vmem_limit_bytes=MEMORY),
    )(place, *(part for pair in pairs for part in pair), *after)


def write_gradients(place, found, depth, width, hidden):
    rows = GROUPS[2]
    height = hidden // DEVICES
    middle = width + 2 * hidden + width + hidden // 8
    last = found[0].shape[1] - 3 * width - 128

    def kernel(place_ref, *refs):
        found_refs, refs = refs[: len(found)], refs[len(found) :]
        gwq_ref, gab_ref, gwo_ref, gwi_ref, gbi_ref, gwf_ref, gain_ref, shift_ref = refs
        spot = place_ref[0]

        def total(refs, at, columns):
            value = refs[0][:, pl.ds(at, columns)].astype(F32)
            for ref in refs[1:]:
                value = value + ref[:, pl.ds(at, columns)].astype(F32)
            return value

        def own(block, size):
            return pltpu.roll(block, block.shape[1] - spot * size, 1)

        def unfolded(block, count):
            return jnp.concatenate([block[step : step + 1] for step in range(count)], 1)

        for layer, refs, at in ((0, found_refs, last), (1, found_refs, middle)):
            gwq_ref[layer] = total(refs, at, 3 * width)
            block = total(refs, at + 3 * width, 128)
            many = width // 128
            for index in range(2):
                line = unfolded(block[index * many : (index + 1) * many], many)
                gab_ref[layer, pl.ds(index, 1)] = own(line, rows)[:, 0:rows]
        for layer, refs, at in ((0, found_refs, middle + 3 * width + 128), (1, found_refs, 0)):
            gwo_ref[layer] = total(refs, at, width)
            gwi_ref[layer] = total(refs, at + width, hidden)
            for step in range(hidden // width):
                gwf_ref[layer, pl.ds(step * rows, rows)] = total(
                    refs, at + width + hidden + step * width, width
                )
            at += width + 2 * hidden
            small = own(total(refs, at, width), rows)
            gain_ref[layer] = small[2:4, 0:rows]
            shift_ref[layer] = small[4:8, 0:rows]
            line = unfolded(total(refs, at + width, hidden // 8), 8)
            gbi_ref[pl.ds(layer, 1)] = own(line, height)[:, 0:height]

    outs = [
        struct((depth, rows, 3 * width), F32),
        struct((depth, 2, rows), F32),
        struct((depth, rows, width), F32),
        struct((depth, rows, hidden), F32),
        struct((depth, height), F32),
        struct((depth, height, width), F32),
        struct((depth, 2, rows), F32),
        struct((depth, 4, rows), F32),
    ]
    return pl.pallas_call(
        kernel,
        in_specs=[pl.BlockSpec(memory_space=pltpu.SMEM)]
        + [pl.BlockSpec(memory_space=pltpu.VMEM)] * len(found),
        out_shape=outs,
        compiler_params=pltpu.CompilerParams(vmem_limit_bytes=MEMORY),
    )(place, *found)


def exchange(parts, axis):
    return lax.all_to_all(parts, axis, 0, 0, tiled=True)


def swap(part, axis, step):
    size = lax.axis_size(axis)
    return lax.ppermute(part, axis, [(source, source ^ step) for source in range(size)])


def local(
    hidden_in,
    lengths,
    grad_out,
    attn_weight,
    attn_bias,
    out_weight,
    ffn_in,
    ffn_in_bias,
    ffn_out,
    norm_gain,
    shifts,
):
    depth, rows, width = out_weight.shape
    hidden = ffn_in.shape[2]
    first, second = lax.axis_size("dp"), lax.axis_size("fsdp")
    fits = (second, first, rows) == GROUPS
    urgent_size = 3 * width + 128
    if fits:
        early, later = pack_parameters(
            attn_weight, attn_bias, out_weight, ffn_in, ffn_in_bias, ffn_out, norm_gain, shifts
        )
        across = lax.axis_index("dp").astype(jnp.int32).reshape(1)
        place = lax.axis_index("fsdp").astype(jnp.int32).reshape(1)
        partners = range(1, second)
        x0, dz1 = rotate_kernel(lengths, (hidden_in, grad_out))
        early = hold(exchange(early, "dp"), (x0,))
        urgent = early[:, :urgent_size]
        urgent = [urgent] + [swap(urgent, "fsdp", step) for step in partners]
        raw0 = early[:, urgent_size:]
        raw0 = [raw0, swap(raw0, "fsdp", 1), swap(raw0, "fsdp", 2)]
    else:
        urgent, raw0, raw1 = gather_other(
            attn_weight, attn_bias, out_weight, ffn_in, ffn_in_bias, ffn_out, norm_gain, shifts
        )
        urgent, raw0, raw1 = ([part[step] for step in range(4)] for part in (urgent, raw0, raw1))
        place = jnp.zeros((1,), jnp.int32)
        x0, dz1 = rotate_kernel(lengths, (hidden_in, grad_out))

    qa0, ka0, va0, ob0, lse0, urgent = first_kernel(lengths, x0, place, urgent)
    if fits:
        raw0[2] = hold(raw0[2], (ob0,))
        raw0.append(swap(raw0[2], "fsdp", 1))
        later = exchange(hold(later, (ob0,)), "dp")
    n1, n2, inv, yb, gb, gp, z0 = dense_kernel(
        0, lengths, x0, ob0, place, urgent, raw0, 3 * width, hidden
    )
    if fits:
        raw1 = hold(later, (z0,))
        raw1 = [raw1, swap(raw1, "fsdp", 1), swap(raw1, "fsdp", 2)]
    qa1, ka1, va1, ob1, lse1 = attention_kernel(1, lengths, z0, place, urgent, raw0, 0)
    if fits:
        raw1[2] = hold(raw1[2], (ob1,))
        raw1.append(swap(raw1[2], "fsdp", 1))
    z1, dr1, dob1, *sent_a = turn_kernel(
        1, lengths, z0, ob1, dz1, place, urgent, raw1, 0, hidden
    )
    dr0, dob0, *sent_b = middle_kernel(
        lengths,
        (z0, dob1, ob1, qa1, ka1, va1, lse1, dr1),
        (n1, n2, inv, yb, gb, gp, ob0),
        place,
        urgent,
        raw0,
        hidden,
        (sent_a[0],),
    )
    if fits:
        got_a = [sent_a[0]] + [swap(sent_a[step], "fsdp", step) for step in partners]
        keep_a, give_a = add_parts(across, got_a, True, (sent_b[0],))
        got_ax = swap(give_a, "dp", 1)
        ready = (sent_b[0], keep_a)
    else:
        ready = ()
    dqkv, *sent_c = last_kernel(
        lengths, (x0, dob0, ob0, qa0, ka0, va0, lse0), ready, place
    )
    hidden_out = outward_kernel(lengths, z1)
    if fits:
        got_b = [sent_b[0]] + [swap(sent_b[step], "fsdp", step) for step in partners]
        got_c = [sent_c[0]] + [swap(sent_c[step], "fsdp", step) for step in partners]
        keep_b, give_b = add_parts(across, got_b, True, (got_ax, hidden_out))
        keep_c, give_c = add_parts(across, got_c, True, (keep_b,))
        grad_in = inward_kernel(lengths, dqkv, dr0, urgent, (keep_c,))
        pairs = [(keep_a, got_ax), (keep_b, swap(give_b, "dp", 1)), (keep_c, swap(give_c, "dp", 1))]
        found = add_halves(across, pairs, (grad_in,))
        found = [found[0]] + [swap(found[step], "dp", 2 * step) for step in range(1, first // 2)]
        spot = lax.axis_index(("dp", "fsdp")).astype(jnp.int32).reshape(1)
        grads = write_gradients(spot, found, depth, width, hidden)
    else:
        grad_in = inward_kernel(lengths, dqkv, dr0, urgent, ())
        grads = scatter_other(
            *(jnp.stack(part) for part in (sent_a, sent_b, sent_c)), rows, width, hidden
        )
    return (hidden_out, grad_in, *grads)


def gather_other(
    attn_weight, attn_bias, out_weight, ffn_in, ffn_in_bias, ffn_out, norm_gain, shifts
):
    axes = ("dp", "fsdp")
    gather = lambda part, axis: lax.all_gather(part, axes, axis=axis, tiled=True)
    depth, unused, width = out_weight.shape
    hidden = ffn_in.shape[2]
    outer, inner, rows = GROUPS
    vectors = gather(jnp.concatenate([attn_bias, norm_gain, shifts], 1), 2)
    line = gather(ffn_in_bias, 1)

    def order(natural):
        return (
            natural.reshape(inner, outer, rows, -1).swapaxes(0, 1).reshape(outer, inner * rows, -1)
        )

    def stacked(part):
        part = part.reshape(DEVICES, -1, rows, width)
        return order(part.swapaxes(1, 2).reshape(width, -1))

    small = vectors.reshape(depth, 8, DEVICES, rows).transpose(2, 1, 0, 3).reshape(width, -1)
    line = line.reshape(depth, DEVICES, -1).swapaxes(0, 1)
    line = jnp.pad(line, ((0, 0), (0, 8 - depth), (0, 0))).reshape(width, -1)
    small = jnp.concatenate([small, line], 1)
    small = jnp.pad(small, ((0, 0), (0, 128 - small.shape[1])))
    wq, wo, wi, wf = (gather(part, 1) for part in (attn_weight, out_weight, ffn_in, ffn_out))
    urgent = jnp.concatenate([order(wq[0]), order(small)], 2)
    raw0 = jnp.concatenate([order(wq[1]), order(wo[0]), order(wi[0]), stacked(wf[0])], 2)
    raw1 = jnp.concatenate([order(wo[1]), order(wi[1]), stacked(wf[1])], 2)
    return urgent, raw0, raw1


def scatter_other(sent_a, sent_b, sent_c, own_rows, width, hidden):
    outer, inner, rows = GROUPS
    axes = ("dp", "fsdp")

    def natural(part):
        return part.reshape(outer, inner, rows, -1).swapaxes(0, 1).reshape(width, -1).astype(F32)

    def cut(part, sizes):
        found, at = [], 0
        for size in sizes:
            found.append(part[:, at : at + size])
            at += size
        return found

    dense = [width, hidden, hidden, width, hidden // 8]
    attention = [3 * width, 128]
    wq0, ab0 = cut(natural(sent_c), attention)
    wq1, ab1, wo0, wi0, wf0, small0, bi0 = cut(natural(sent_b), attention + dense)
    wo1, wi1, wf1, small1, bi1 = cut(natural(sent_a), dense)

    def stacked(part):
        part = part.reshape(DEVICES, rows, -1, width).swapaxes(1, 2)
        return part.reshape(hidden, width)

    def spread(parts, axis):
        return lax.psum_scatter(jnp.stack(parts), axes, scatter_dimension=axis, tiled=True)

    return (
        spread([wq0, wq1], 1),
        spread([ab0[:4].reshape(2, width), ab1[:4].reshape(2, width)], 2),
        spread([wo0, wo1], 1),
        spread([wi0, wi1], 1),
        spread([bi0[:8].reshape(-1), bi1[:8].reshape(-1)], 1),
        spread([stacked(wf0), stacked(wf1)], 1),
        spread([small0[2:4], small1[2:4]], 2),
        spread([small0[4:8], small1[4:8]], 2),
    )


def solution(mesh):
    placed = (
        P(("dp", "fsdp"), None),
        P(("dp", "fsdp"), None),
        P(("dp", "fsdp"), None),
        P(None, ("dp", "fsdp"), None),
        P(None, None, ("dp", "fsdp")),
        P(None, ("dp", "fsdp"), None),
        P(None, ("dp", "fsdp"), None),
        P(None, ("dp", "fsdp")),
        P(None, ("dp", "fsdp"), None),
        P(None, None, ("dp", "fsdp")),
        P(None, None, ("dp", "fsdp")),
    )
    return jax.shard_map(
        local,
        mesh=mesh,
        in_specs=placed,
        out_specs=(
            P(("dp", "fsdp"), None),
            P(("dp", "fsdp"), None),
            P(None, ("dp", "fsdp"), None),
            P(None, None, ("dp", "fsdp")),
            P(None, ("dp", "fsdp"), None),
            P(None, ("dp", "fsdp"), None),
            P(None, ("dp", "fsdp")),
            P(None, ("dp", "fsdp"), None),
            P(None, None, ("dp", "fsdp")),
            P(None, None, ("dp", "fsdp")),
        ),
        check_vma=False,
    )
```

```python
from functools import partial

import jax
import jax.numpy as jnp
from jax import lax
from jax.experimental import pallas as pl
from jax.experimental.pallas import tpu as pltpu
from jax.sharding import PartitionSpec as P

HEADS = 4
HD = 64
SEQ = 512
PAIR = 2 * HD
EXTRA = 16
HALF = SEQ // 2
HALVES = (slice(0, HALF), slice(HALF, SEQ))
FAR = -(2.0**100)
FLOOR = -1e20
EPSILON = 1e-12
PIECE = 256
SMALL = 128
GROUPS = (4, 8, 8)
DEVICES = 32
LOW = jnp.bfloat16
F32 = jnp.float32
MEMORY = 2**26


def dot_nn(left, right):
    return lax.dot_general(left, right, (((1,), (0,)), ((), ())), preferred_element_type=F32)


def dot_nt(left, right):
    return lax.dot_general(left, right, (((1,), (1,)), ((), ())), preferred_element_type=F32)


def dot_tn(left, right):
    return lax.dot_general(left, right, (((0,), (0,)), ((), ())), preferred_element_type=F32)


def pieces(total, size=PIECE):
    return [pl.ds(start, size) for start in range(0, total, size)]


def three_parts(values):
    first = values.astype(LOW).astype(F32)
    rest = values - first
    second = rest.astype(LOW).astype(F32)
    return first, second, rest - second


BELL = -0.5 / 0.6931471805599453


def gelu_parts(u):
    cumulative = 0.5 + 0.5 * lax.erf(u * 0.7071067811865476)
    slope = cumulative + (u * 0.3989422804014327) * jnp.exp2(u * u * BELL)
    return u * cumulative, slope


def inverse_of(values):
    guess = pl.reciprocal(values, approx=True)
    return guess * (2.0 - values * guess)


def longest_start(lengths_ref, row):
    begin, found = jnp.int32(0), jnp.int32(0)
    for entry in range(lengths_ref.shape[1]):
        size = lengths_ref[row, entry]
        found = jnp.where(size == HALF, begin, found)
        begin = begin + size
    return found


def segments(lengths_ref, row):
    places = lax.broadcasted_iota(jnp.int32, (1, SEQ), 1) + longest_start(lengths_ref, row)
    places = places & (SEQ - 1)
    bound = jnp.int32(0)
    segment = jnp.zeros((1, SEQ), jnp.int32)
    last = lengths_ref.shape[1] - 1
    for entry in range(last):
        bound = bound + lengths_ref[row, entry]
        segment = segment + (places >= bound).astype(jnp.int32)
    return segment, last


def head_rows(head):
    return slice(head * HD, (head + 1) * HD)


def attention_forward(row, lengths_ref, x, wt_ref, bias_ref, qa_ref, ka_ref, va_ref, ob_ref, lse_ref, s_ref, p_ref):
    width = HEADS * HD
    segment, last = segments(lengths_ref, row)
    pad = (segment == last).astype(F32)
    line = lax.broadcasted_iota(jnp.int32, (EXTRA, SEQ), 0)
    aug_q = jnp.where(line == segment, 1.0, 0.0).astype(LOW)
    seen = (line == segment) & (segment != last)
    aug_k = jnp.where(seen | (line > last), 0.0, FAR).astype(LOW)
    aug_v = jnp.where(line == 0, 1.0, 0.0).astype(LOW)
    rest = jnp.zeros((PAIR - HD - EXTRA, SEQ), LOW)
    for head in range(HEADS):
        qa_ref[head, HD : HD + EXTRA] = aug_q
        ka_ref[head, HD : HD + EXTRA] = aug_k
        va_ref[head, HD : HD + EXTRA] = aug_v
        qa_ref[head, HD + EXTRA : PAIR] = rest
        ka_ref[head, HD + EXTRA : PAIR] = rest
    for block, ref in enumerate((qa_ref, ka_ref, va_ref)):
        lines = slice(block * width, (block + 1) * width)
        bias = bias_ref[lines]
        value = dot_nt(wt_ref[lines], x) + jnp.concatenate([bias] * (SEQ // 128), 1)
        if block == 0:
            value = value * HD**-0.5
        value = value.astype(LOW)
        for head in range(HEADS):
            ref[head, 0:HD] = value[head_rows(head)]
        yield

    def scores(head):
        for half in HALVES:
            s_ref[head % 2, half] = dot_tn(ka_ref[head, :, half], qa_ref[head, :, half])

    def softmax(head):
        tops = []
        for half in HALVES:
            tops.append(jnp.maximum(jnp.max(s_ref[head % 2, half], 0, keepdims=True), FLOOR))
            p_ref[head % 2, half] = jnp.exp(s_ref[head % 2, half] - tops[-1]).astype(LOW)
        return tops

    scores(0)
    yield
    for head in range(HEADS):
        if head + 1 < HEADS:
            scores(head + 1)
            yield
        tops = softmax(head)
        yield
        for half, top in zip(HALVES, tops):
            out = dot_nn(va_ref[head, :, half], p_ref[head % 2, half])
            alone = pad[:, half]
            total = out[HD : HD + 1] + alone
            lse_ref[head : head + 1, half] = jnp.where(alone > 0, 0.0, top + jnp.log(total))
            own = alone * va_ref[head, 0:HD, half].astype(F32)
            ob_ref[head_rows(head), half] = (out[0:HD] * inverse_of(total) + own).astype(LOW)
        yield


def normal(values):
    centred = values - jnp.mean(values, -1, keepdims=True)
    inverse = lax.rsqrt(jnp.mean(centred * centred, -1, keepdims=True) + EPSILON)
    return centred * inverse, inverse


def normal_back(cotangent, unit, inverse, gains):
    scaled = cotangent * gains
    return inverse * (
        scaled
        - jnp.mean(scaled, -1, keepdims=True)
        - unit * jnp.mean(scaled * unit, -1, keepdims=True)
    )


def dense_forward(x_ref, ob_ref, wo_ref, wi_ref, wf_ref, small_ref, bi_ref, n1_ref, n2_ref, inv_ref, yb_ref, gb_ref, gp_ref, z_ref, work_ref, u_ref):
    small = lambda index: small_ref[pl.ds(index, 1)]
    work_ref[...] = dot_tn(ob_ref[...], wo_ref[...])
    yield
    for place in pieces(SEQ):
        unit, inverse = normal(x_ref[place].astype(F32) + work_ref[place] + small(4))
        n1_ref[place] = unit
        inv_ref[place, pl.ds(0, HD)] = jnp.broadcast_to(inverse, (PIECE, HD))
        y = unit * small(2) + small(5)
        yb_ref[place] = y.astype(LOW)
        work_ref[place] = y + small(6)
        yield
    columns = 256
    count = wi_ref.shape[1] // columns

    def into(step):
        u_ref[step % 2] = dot_nn(yb_ref[...], wi_ref[:, pl.ds(step * columns, columns)])

    into(0)
    yield
    for step in range(count):
        if step + 1 < count:
            into(step + 1)
            yield
        lanes = pl.ds(step * columns, columns)
        for place in pieces(SEQ, SMALL):
            g, slope = gelu_parts(u_ref[step % 2, place] + bi_ref[:, lanes])
            gb_ref[place, lanes] = g.astype(LOW)
            gp_ref[place, lanes] = slope.astype(LOW)
            yield
    work_ref[...] += dot_nn(gb_ref[...], wf_ref[...])
    yield
    for place in pieces(SEQ):
        unit, inverse = normal(work_ref[place])
        n2_ref[place] = unit
        inv_ref[place, pl.ds(HD, HD)] = jnp.broadcast_to(inverse, (PIECE, HD))
        z_ref[place] = (unit * small(3) + small(7)).astype(z_ref.dtype)
        yield


def fold(values):
    return jnp.sum(values.reshape(-1, 8, values.shape[-1]), 0)


def dense_backward(dz_ref, n1_ref, n2_ref, inv_ref, yb_ref, gb_ref, gp_ref, ob_ref, wo_ref, wi_ref, wf_ref, small_ref, dr_ref, dob_ref, gwo_ref, gwi_ref, gwf_ref, gsmall_ref, gbi_ref, low_ref, u_ref, du_ref, turned_ref):
    small = lambda index: small_ref[pl.ds(index, 1)]
    for place in pieces(SEQ):
        dz = dz_ref[place].astype(F32)
        unit = n2_ref[place]
        gsmall_ref[3] += fold(dz * unit)
        gsmall_ref[7] += fold(dz)
        dr = normal_back(dz, unit, inv_ref[place, pl.ds(HD, 1)], small(3))
        dr_ref[place] = dr
        df = dr.astype(LOW)
        low_ref[place] = df
        gsmall_ref[6] += fold(df.astype(F32))
        yield
    columns = 256
    count = wi_ref.shape[1] // columns

    def back(step):
        u_ref[step % 2] = dot_nt(low_ref[...], wf_ref[pl.ds(step * columns, columns)])

    back(0)
    turned_ref[0, 0 : low_ref.shape[1]] = low_ref[...].T
    width = low_ref.shape[1]
    turned_ref[1, 0:width] = yb_ref[...].T
    turned_ref[1, width:] = jnp.ones((EXTRA, SEQ), LOW)
    yield
    for step in range(count):
        if step + 1 < count:
            back(step + 1)
            yield
        lanes = pl.ds(step * columns, columns)
        gwf_ref[:, lanes] += dot_nn(turned_ref[0, 0:width], gb_ref[:, lanes])
        yield
        for place in pieces(SEQ, SMALL):
            du = (u_ref[step % 2, place] * gp_ref[place, lanes].astype(F32)).astype(LOW)
            du_ref[place, lanes] = du
        yield
        product = dot_nn(turned_ref[1], du_ref[:, lanes])
        gwi_ref[:, lanes] += product[0:width]
        gbi_ref[:, lanes] += product[width : width + 8]
        yield
    u_ref[0] = dot_nt(du_ref[...], wi_ref[...])
    yield
    for place in pieces(SEQ):
        dy = dr_ref[place] + u_ref[0, place]
        unit = n1_ref[place]
        gsmall_ref[2] += fold(dy * unit)
        gsmall_ref[5] += fold(dy)
        dr = normal_back(dy, unit, inv_ref[place, pl.ds(0, 1)], small(2))
        dr_ref[place] = dr
        da = dr.astype(LOW)
        low_ref[place] = da
        gsmall_ref[4] += fold(da.astype(F32))
        yield
    gwo_ref[...] += dot_nn(ob_ref[...], low_ref[...])
    dob_ref[...] = dot_nt(wo_ref[...], low_ref[...]).astype(LOW)
    yield


def attention_backward(row, lengths_ref, x, do_ref, ob_ref, qa_ref, ka_ref, va_ref, lse_ref, dqkv_ref, gwq_ref, gbias_ref, p_ref, ds_ref, s_ref):
    width = HEADS * HD
    segment, last = segments(lengths_ref, row)
    pad = (segment == last).astype(F32)

    def scores(head):
        for half in HALVES:
            s_ref[0, head % 2, half] = dot_tn(ka_ref[head, :, half], qa_ref[head, :, half])
            s_ref[1, head % 2, half] = dot_tn(
                va_ref[head, 0:HD, half], do_ref[head_rows(head), half]
            )

    def weigh(head):
        product = do_ref[head_rows(head)].astype(F32) * ob_ref[head_rows(head)].astype(F32)
        centre = jnp.sum(product, 0, keepdims=True)
        for half in HALVES:
            p = jnp.exp(s_ref[0, head % 2, half] - lse_ref[head : head + 1, half])
            p_ref[head % 2, half] = p.astype(LOW)
            ds_ref[head % 2, half] = (p * (s_ref[1, head % 2, half] - centre[:, half])).astype(LOW)

    scores(0)
    yield
    for head in range(HEADS):
        if head + 1 < HEADS:
            scores(head + 1)
            yield
        weigh(head)
        yield
        for half in HALVES:
            ds, do = ds_ref[head % 2, half], do_ref[head_rows(head), half]
            dq = dot_nn(ka_ref[head, 0:HD, half], ds) * HD**-0.5
            dk = dot_nt(qa_ref[head, 0:HD, half], ds)
            dv = dot_nt(do, p_ref[head % 2, half]) + pad[:, half] * do.astype(F32)
            for block, value in enumerate((dq, dk, dv)):
                at = block * width + head * HD
                dqkv_ref[at : at + HD, half] = value.astype(LOW)
        yield
    for index, block in enumerate((0, 2)):
        value = dqkv_ref[block * width : (block + 1) * width].astype(F32)
        parts = [value[:, at : at + 128] for at in range(0, SEQ, 128)]
        gbias_ref[index] += (parts[0] + parts[1]) + (parts[2] + parts[3])
    gwq_ref[...] += dot_nn(dqkv_ref[...], x)
    yield


def unpack_matrix(raw_ref, at, into_ref):
    width = into_ref.shape[0]
    for start in range(0, into_ref.shape[1], width):
        block = raw_ref[:, :, pl.ds(at + start, width)].astype(F32)
        block = block.reshape(GROUPS + (width,)).swapaxes(0, 1).reshape(width, width)
        into_ref[:, pl.ds(start, width)] = block.astype(LOW)


def unpack_stacked(raw_ref, at, into_ref):
    width = into_ref.shape[1]
    count = into_ref.shape[0] // width
    blocks = [
        raw_ref[:, :, pl.ds(at + step * width, width)].astype(F32).reshape(GROUPS + (width,))
        for step in range(count)
    ]
    outer, inner, rows = GROUPS
    for place in range(inner):
        part = jnp.stack([jnp.stack([block[f, place] for block in blocks]) for f in range(outer)])
        size = outer * count * rows
        into_ref[pl.ds(place * size, size)] = part.reshape(size, width).astype(LOW)


def counter(shape, axis):
    return lax.broadcasted_iota(jnp.int32, shape, axis)


def split_by(values, size):
    return lax.shift_right_logical(values, size.bit_length() - 1), values & (size - 1)


def sources(rows):
    outer, inner, height = GROUPS
    group, within = split_by(counter((rows, 1), 0), height)
    far, near = split_by(group, inner)
    return near * outer + far, within


def unpack_vectors(raw_ref, at, layer):
    outer, inner, rows = GROUPS
    total = outer * inner * rows
    raw = raw_ref[:, :, pl.ds(at, 128)].reshape(total, 128)
    owner, place = split_by(counter((1, total), 1), rows)
    pick = jnp.where(counter((128, 1), 0) == rows * layer + place, 1.0, 0.0).astype(LOW)
    device, unused = sources(total)
    spread = jnp.where(owner == device, dot_nn(raw, pick), 0.0)
    return jnp.sum(spread.reshape(outer * inner, rows, total), 0)


def unpack_hidden(raw_ref, at, layer, hidden):
    outer, inner, rows = GROUPS
    total = outer * inner * rows
    raw = raw_ref[:, :, pl.ds(at, 128)].reshape(total, 128)
    owner, place = split_by(counter((1, hidden), 1), hidden // (outer * inner))
    pick = jnp.where(counter((128, 1), 0) == 2 * rows + place, 1.0, 0.0).astype(LOW)
    device, within = sources(total)
    device = jnp.where(within == layer, device, -1)
    spread = jnp.where(owner == device, dot_nn(raw, pick), 0.0)
    return jnp.sum(spread, 0, keepdims=True)


def pack_matrix(sum_ref, sent_ref, at, turned=False):
    width = sum_ref.shape[1 if turned else 0]
    outer, inner, rows = GROUPS
    for start in range(0, sum_ref.shape[0 if turned else 1], width):
        near = pl.ds(start, width)
        block = sum_ref[near].T if turned else sum_ref[:, near]
        block = block.reshape(inner, outer, rows, width)
        block = block.swapaxes(0, 1).reshape(outer, inner * rows, width)
        sent_ref[:, :, pl.ds(at + start, width)] = block.astype(LOW)


def pack_stacked(sum_ref, sent_ref, at):
    width = sum_ref.shape[0]
    outer, inner, rows = GROUPS
    count = sum_ref.shape[1] // width
    near = inner // count
    for step in range(count):
        block = sum_ref[:, pl.ds(step * width, width)].T
        block = block.reshape(near, outer, count, rows, width)
        for part in range(count):
            piece = jnp.stack([block[:, f, part] for f in range(outer)])
            piece = piece.reshape(outer, near * rows, width)
            sent_ref[:, pl.ds(step * near * rows, near * rows), pl.ds(at + part * width, width)] = (
                piece.astype(LOW)
            )


def pack_vectors(block, line, sent_ref, at):
    outer, inner, rows = GROUPS
    total = outer * inner * rows
    device, within = sources(total)
    owner, unused = split_by(counter((1, total), 1), rows)
    spread = jnp.broadcast_to(block[None], (outer * inner, rows, total)).reshape(total, total)
    spread = jnp.where(owner == device, spread, 0.0).astype(LOW)
    unused, place = split_by(counter((total, 1), 0), rows)
    found = dot_nn(spread, jnp.where(counter((1, 128), 1) == place, 1.0, 0.0).astype(LOW))
    if line is not None:
        hidden = line.shape[1]
        height = hidden // (outer * inner)
        owner, unused = split_by(counter((1, hidden), 1), height)
        spread = jnp.where(owner == jnp.where(within == 0, device, -1), line, 0.0).astype(LOW)
        unused, place = split_by(counter((hidden, 1), 0), height)
        pick = jnp.where(counter((1, 128), 1) == 2 * rows + place, 1.0, 0.0).astype(LOW)
        found = found + dot_nn(spread, pick)
    sent_ref[:, :, pl.ds(at, 128)] = found.reshape(outer, inner * rows, 128).astype(LOW)


def bias_rows(gbias_ref):
    width = gbias_ref.shape[1]
    parts = [jnp.sum(gbias_ref[index].T, 0, keepdims=True) for index in range(2)]
    return jnp.concatenate(parts + [jnp.zeros((6, width), F32)], 0)


def pack_dense(gwo_ref, gwi_ref, gwf_ref, gsmall_ref, gbi_ref, block, sent_ref, at):
    width, hidden = gwi_ref.shape
    pack_matrix(gwo_ref, sent_ref, at)
    pack_matrix(gwi_ref, sent_ref, at + width)
    pack_stacked(gwf_ref, sent_ref, at + width + hidden)
    block = jnp.sum(gsmall_ref[...], 1) + block
    pack_vectors(block, gbi_ref[0:1], sent_ref, at + width + 2 * hidden)


def shape_of(array):
    return jax.ShapeDtypeStruct(array.shape, array.dtype)


def by_row(shape, group):
    if len(shape) == 2:
        return pl.BlockSpec((group * SEQ, shape[1]), lambda step: (step, 0))
    return pl.BlockSpec((group,) + tuple(shape[1:]), lambda step: (step,) + (0,) * (len(shape) - 1))


def one_row(ref, member):
    if len(ref.shape) == 2:
        return ref.at[pl.ds(member * SEQ, SEQ)]
    return ref.at[member]


def alternate(runs):
    running = []
    waiting = list(runs)
    while running or waiting:
        if waiting:
            running.append(waiting.pop(0))
        for run in list(running):
            try:
                next(run)
            except StopIteration:
                running.remove(run)


def whole(shape):
    return pl.BlockSpec(tuple(shape), lambda row: (0,) * len(shape))


def run_rows(
    body, lengths, rowwise, fixed, row_outs, sent, shared, private, cost, setup, finish, after=(),
    scalars=(), group=1
):
    count = lengths.shape[0]
    group = group if count % group == 0 else 1
    cuts = [len(scalars), len(rowwise), len(fixed), len(after), len(row_outs), len(sent)]
    cuts += [len(shared)] + [len(private)] * group

    def kernel(lengths_ref, *refs):
        step = pl.program_id(0)
        groups = []
        at = 0
        for cut in cuts:
            groups.append(refs[at : at + cut])
            at += cut
        numbers, rows_in, fixed_in, unused, rows_out, sent_out, work = groups[:7]

        @pl.when(step == 0)
        def _():
            setup(numbers, fixed_in, sent_out, work)

        alternate(
            body(
                step * group + member,
                lengths_ref,
                [one_row(ref, member) for ref in rows_in],
                [one_row(ref, member) for ref in rows_out],
                work,
                groups[7 + member],
            )
            for member in range(group)
        )

        if finish:

            @pl.when(step == count // group - 1)
            def _():
                finish(numbers, work, sent_out)

    return pl.pallas_call(
        kernel,
        grid=(count // group,),
        in_specs=[pl.BlockSpec(memory_space=pltpu.SMEM)] * (1 + len(scalars))
        + [by_row(array.shape, group) for array in rowwise]
        + [whole(array.shape) for array in fixed]
        + [pl.BlockSpec(memory_space=pl.ANY) for array in after],
        out_specs=[by_row(part.shape, group) for part in row_outs]
        + [whole(part.shape) for part in sent],
        out_shape=list(row_outs) + list(sent),
        scratch_shapes=list(shared) + list(private) * group,
        compiler_params=pltpu.CompilerParams(
            dimension_semantics=("arbitrary",), vmem_limit_bytes=MEMORY
        ),
        cost_estimate=pl.CostEstimate(flops=cost, bytes_accessed=8 * 2**20, transcendentals=0),
    )(lengths, *scalars, *rowwise, *fixed, *after)


def struct(shape, dtype):
    return jax.ShapeDtypeStruct(tuple(shape), dtype)


FORWARD_SCRATCH = lambda: [
    pltpu.VMEM((2, SEQ, HALF), F32),
    pltpu.VMEM((2, SEQ, HALF), LOW),
]
BACKWARD_SCRATCH = lambda: [
    pltpu.VMEM((2, SEQ, HALF), LOW),
    pltpu.VMEM((2, SEQ, HALF), LOW),
    pltpu.VMEM((2, 2, SEQ, HALF), F32),
    pltpu.VMEM((3 * HEADS * HD, SEQ), LOW),
]


def attention_outs(rows, width):
    return [
        struct((rows, HEADS, PAIR, SEQ), LOW),
        struct((rows, HEADS, PAIR, SEQ), LOW),
        struct((rows, HEADS, HD + EXTRA, SEQ), LOW),
        struct((rows, width, SEQ), LOW),
        struct((rows, 8, SEQ), F32),
    ]


def dense_outs(tokens, width, hidden):
    return [
        struct((tokens, width), F32),
        struct((tokens, width), F32),
        struct((tokens, PAIR), F32),
        struct((tokens, width), LOW),
        struct((tokens, hidden), LOW),
        struct((tokens, hidden), LOW),
    ]


def vmem(shape, dtype):
    return pltpu.VMEM(tuple(shape), dtype)


def attention_weights(width):
    return [vmem((width, 3 * width), LOW), vmem((3 * width, width), LOW), vmem((3 * width, 128), F32)]


def dense_weights(width, hidden):
    return [
        vmem((width, width), LOW),
        vmem((width, hidden), LOW),
        vmem((hidden, width), LOW),
        vmem((8, width), F32),
        vmem((1, hidden), F32),
    ]


def dense_sums(width, hidden):
    return [
        vmem((width, width), F32),
        vmem((width, hidden), F32),
        vmem((width, hidden), F32),
        vmem((8, 8, width), F32),
        vmem((8, hidden), F32),
    ]


def attention_sums(width):
    return [vmem((3 * width, width), F32), vmem((2, width, 128), F32)]


def dense_work(width, hidden):
    return [
        vmem((SEQ, width), LOW),
        vmem((2, SEQ, width), F32),
        vmem((SEQ, hidden), LOW),
        vmem((2, width + EXTRA, SEQ), LOW),
    ]


def set_attention(layer, urgent_ref, raw_ref, at, wq_ref, wt_ref, bias_ref):
    width = wq_ref.shape[0]
    unpack_matrix(raw_ref, at, wq_ref)
    vectors = unpack_vectors(urgent_ref, 3 * width, layer)
    for block, line in enumerate((vectors[0:1], jnp.zeros((1, width), F32), vectors[1:2])):
        lines = pl.ds(block * width, width)
        wt_ref[lines] = wq_ref[:, lines].astype(F32).T.astype(LOW)
        bias_ref[lines] = jnp.broadcast_to(line, (128, width)).T


def set_dense(layer, urgent_ref, raw_ref, at, wo_ref, wi_ref, wf_ref, small_ref, bi_ref):
    width, hidden = wi_ref.shape
    unpack_matrix(raw_ref, at, wo_ref)
    unpack_matrix(raw_ref, at + width, wi_ref)
    unpack_stacked(raw_ref, at + width + hidden, wf_ref)
    small_ref[...] = unpack_vectors(urgent_ref, 3 * width, layer)
    bi_ref[...] = unpack_hidden(urgent_ref, 3 * width, layer, hidden)


def clear(refs):
    for ref in refs:
        ref[...] = jnp.zeros(ref.shape, ref.dtype)


def assemble(place_ref, part_refs, into_ref):
    for step, ref in enumerate(part_refs):
        into_ref[place_ref[0] ^ step] = ref[...]


def raw_block(parts):
    return vmem((len(parts),) + parts[0].shape, LOW)


def turned_back(lengths_ref, row, values):
    return pltpu.roll(values, longest_start(lengths_ref, row), 0).astype(LOW)


def rotate_kernel(lengths, arrays):
    def body(row, lengths_ref, rowwise, outs, work, own):
        back = (SEQ - longest_start(lengths_ref, row)) & (SEQ - 1)
        for source, target in zip(rowwise, outs):
            target[...] = pltpu.roll(source[...].astype(F32), back, 0).astype(LOW)
            yield

    return run_rows(
        body, lengths, list(arrays), [], [struct(array.shape, LOW) for array in arrays], [], [], [],
        10**6, lambda *refs: None, None,
    )


def first_kernel(lengths, x, place, parts):
    rows, (tokens, width) = lengths.shape[0], x.shape

    def setup(numbers, fixed, sent, work):
        assemble(numbers[0], fixed, sent[0])
        set_attention(0, sent[0], sent[0], 0, *work)

    def body(row, lengths_ref, rowwise, outs, work, own):
        return attention_forward(row, lengths_ref, rowwise[0][...], *work[1:3], *outs, *own)

    return run_rows(
        body, lengths, [x], list(parts), attention_outs(rows, width),
        [struct((len(parts),) + parts[0].shape, LOW)],
        attention_weights(width), FORWARD_SCRATCH(), 4 * 10**9, setup, None, (), [place],
    )


def attention_kernel(layer, lengths, x, place, urgent, parts, at):
    rows, (tokens, width) = lengths.shape[0], x.shape

    def setup(numbers, fixed, sent, work):
        assemble(numbers[0], fixed[1:], work[3])
        set_attention(layer, fixed[0], work[3], at, *work[:3])

    def body(row, lengths_ref, rowwise, outs, work, own):
        return attention_forward(
            row, lengths_ref, rowwise[0][...].astype(LOW), *work[1:3], *outs, *own
        )

    return run_rows(
        body, lengths, [x], [urgent] + list(parts), attention_outs(rows, width), [],
        attention_weights(width) + [raw_block(parts)], FORWARD_SCRATCH(),
        4 * 10**9, setup, None, (), [place],
    )


def dense_kernel(layer, lengths, x, ob, place, urgent, parts, at, hidden):
    tokens, width = x.shape

    def setup(numbers, fixed, sent, work):
        assemble(numbers[0], fixed[1:], work[5])
        set_dense(layer, fixed[0], work[5], at, *work[:5])

    def body(row, lengths_ref, rowwise, outs, work, own):
        return dense_forward(*rowwise, *work[:5], *outs, *own)

    return run_rows(
        body, lengths, [x, ob], [urgent] + list(parts),
        dense_outs(tokens, width, hidden) + [struct((tokens, width), F32)], [],
        dense_weights(width, hidden) + [raw_block(parts)],
        [vmem((SEQ, width), F32), vmem((2, SEQ, width), F32)],
        5 * 10**9, setup, None, (), [place],
    )


def turn_kernel(layer, lengths, x, ob, cotangent, place, urgent, parts, at, hidden):
    tokens, width = x.shape
    columns = width + 2 * hidden + 128

    def setup(numbers, fixed, sent, work):
        assemble(numbers[0], fixed[1:], work[11])
        set_dense(layer, fixed[0], work[11], at, *work[:5])
        clear(work[5:10])

    def body(row, lengths_ref, rowwise, outs, work, own):
        x_ref, ob_ref, dz_ref = rowwise
        z_ref, dr_ref, dob_ref = outs
        weights, sums = work[:5], work[5:10]
        kept, work_ref, back = own[:6], own[6], own[7:]
        yield from dense_forward(x_ref, ob_ref, *weights, *kept, z_ref, work_ref, back[1])
        yield from dense_backward(dz_ref, *kept, ob_ref, *weights[:4], dr_ref, dob_ref, *sums, *back)

    def finish(numbers, work, sent):
        pack_dense(*work[5:10], 0.0, work[10], 0)
        hand_out(numbers[0], work[10], sent)

    kept = [vmem((SEQ,) + part.shape[1:], part.dtype) for part in dense_outs(tokens, width, hidden)]
    return run_rows(
        body, lengths, [x, ob, cotangent], [urgent] + list(parts),
        [struct((tokens, width), LOW), struct((tokens, width), F32), struct((tokens // SEQ, width, SEQ), LOW)],
        [struct((64, columns), LOW)] * 4,
        dense_weights(width, hidden) + dense_sums(width, hidden)
        + [vmem((4, 64, columns), LOW), raw_block(parts)],
        kept + [vmem((SEQ, width), F32)] + dense_work(width, hidden),
        10**10, setup, finish, (), [place], 2,
    )


def hand_out(place_ref, packed_ref, sent):
    for step, ref in enumerate(sent):
        ref[...] = packed_ref[place_ref[0] ^ step]


def middle_kernel(lengths, upper, lower, place, urgent, parts, hidden, after):
    tokens, width = upper[0].shape
    columns = 4 * width + 2 * hidden + 128

    def setup(numbers, fixed, sent, work):
        assemble(numbers[0], fixed[1:], work[16])
        set_attention(1, fixed[0], work[16], 0, *work[:3])
        set_dense(0, fixed[0], work[16], 3 * width, *work[3:8])
        clear(work[8:15])

    def body(row, lengths_ref, rowwise, outs, work, own):
        up, low = rowwise[:8], rowwise[8:]
        dx_ref = own[0]
        yield from attention_backward(
            row, lengths_ref, up[0][...].astype(LOW), *up[1:7], own[-1], *work[8:10], *own[5:-1]
        )
        dx_ref[...] = up[7][...] + dot_tn(own[-1][...], work[1][...])
        yield
        yield from dense_backward(dx_ref, *low, *work[3:7], *outs, *work[10:15], *own[1:5])

    def finish(numbers, work, sent):
        pack_matrix(work[8], work[15], 0, True)
        pack_dense(*work[10:15], bias_rows(work[9]), work[15], 3 * width)
        hand_out(numbers[0], work[15], sent)

    return run_rows(
        body, lengths, list(upper) + list(lower), [urgent] + list(parts),
        [struct((tokens, width), F32), struct((tokens // SEQ, width, SEQ), LOW)],
        [struct((64, columns), LOW)] * 4,
        attention_weights(width) + dense_weights(width, hidden)
        + attention_sums(width) + dense_sums(width, hidden)
        + [vmem((4, 64, columns), LOW), raw_block(parts)],
        [vmem((SEQ, width), F32)] + dense_work(width, hidden) + BACKWARD_SCRATCH(),
        15 * 10**9, setup, finish, after, [place], 2,
    )


def last_kernel(lengths, upper, after, place):
    tokens, width = upper[0].shape

    def setup(numbers, fixed, sent, work):
        clear(work[:2])

    def body(row, lengths_ref, rowwise, outs, work, own):
        return attention_backward(
            row, lengths_ref, rowwise[0][...], *rowwise[1:], outs[0], *work[:2], *own
        )

    def finish(numbers, work, sent):
        pack_matrix(work[0], work[2], 0, True)
        pack_vectors(bias_rows(work[1]), None, work[2], 3 * width)
        hand_out(numbers[0], work[2], sent)

    return run_rows(
        body, lengths, list(upper), [], [struct((tokens // SEQ, 3 * width, SEQ), LOW)],
        [struct((64, 3 * width + 128), LOW)] * 4,
        attention_sums(width) + [vmem((4, 64, 3 * width + 128), LOW)],
        BACKWARD_SCRATCH()[:-1], 8 * 10**9, setup, finish, after, [place], 2,
    )


def outward_kernel(lengths, z):
    def body(row, lengths_ref, rowwise, outs, work, own):
        outs[0][...] = turned_back(lengths_ref, row, rowwise[0][...].astype(F32))
        yield

    (found,) = run_rows(
        body, lengths, [z], [], [struct(z.shape, LOW)], [], [], [], 3 * 10**9,
        lambda *refs: None, None,
    )
    return found


def inward_kernel(lengths, dqkv, dr, urgent, after):
    tokens, width = dr.shape

    def setup(numbers, fixed, sent, work):
        set_attention(0, fixed[0], fixed[0], 0, *work)

    def body(row, lengths_ref, rowwise, outs, work, own):
        dqkv_ref, dr_ref = rowwise
        dx = dr_ref[...] + dot_tn(dqkv_ref[...], work[1][...])
        outs[0][...] = turned_back(lengths_ref, row, dx)
        yield

    (found,) = run_rows(
        body, lengths, [dqkv, dr], [urgent], [struct((tokens, width), LOW)], [],
        attention_weights(width), [], 10**10, setup, None, after,
    )
    return found


def hold(array, after):
    def kernel(*refs):
        pass

    anywhere = pl.BlockSpec(memory_space=pl.ANY)
    return pl.pallas_call(
        kernel,
        in_specs=[anywhere] * (1 + len(after)),
        out_specs=anywhere,
        out_shape=shape_of(array),
        input_output_aliases={0: 0},
    )(array, *after)


def pack_parameters(
    attn_weight, attn_bias, out_weight, ffn_in, ffn_in_bias, ffn_out, norm_gain, shifts
):
    depth, rows, width = out_weight.shape
    copies = GROUPS[1]
    hidden = ffn_in.shape[2]
    dense = width + 2 * hidden
    height = ffn_in_bias.shape[1]

    def kernel(wq_ref, ab_ref, wo_ref, wi_ref, bi_ref, wf_ref, gain_ref, shift_ref, first_ref, rest_ref, small_ref):
        def put(ref, block, at):
            block = jnp.broadcast_to(block.astype(F32)[None], (copies,) + block.shape)
            block = block.reshape(copies * block.shape[1], block.shape[2])
            ref[:, pl.ds(at, block.shape[1])] = block.astype(LOW)

        small_ref[...] = jnp.zeros(small_ref.shape, F32)
        for layer in range(depth):
            lanes = pl.ds(rows * layer, rows)
            small_ref[0:2, lanes] = ab_ref[layer].astype(F32)
            small_ref[2:4, lanes] = gain_ref[layer].astype(F32)
            small_ref[4:8, lanes] = shift_ref[layer].astype(F32)
        small_ref[0:depth, pl.ds(2 * rows, height)] = bi_ref[...].astype(F32)
        put(first_ref, wq_ref[0], 0)
        put(first_ref, small_ref[...], 3 * width)
        put(first_ref, wq_ref[1], 3 * width + 128)
        for layer, ref, at in ((0, first_ref, 6 * width + 128), (1, rest_ref, 0)):
            put(ref, wo_ref[layer], at)
            put(ref, wi_ref[layer], at + width)
            at += width + hidden
            down = wf_ref[layer].astype(F32)
            for step in range(hidden // width):
                put(ref, down[step * rows : (step + 1) * rows], at)
                at += width

    return pl.pallas_call(
        kernel,
        in_specs=[pl.BlockSpec(memory_space=pltpu.VMEM)] * 8,
        out_shape=[
            struct((copies * rows, 6 * width + 128 + dense), LOW),
            struct((copies * rows, dense), LOW),
        ],
        scratch_shapes=[vmem((rows, 128), F32)],
        compiler_params=pltpu.CompilerParams(vmem_limit_bytes=MEMORY),
    )(attn_weight, attn_bias, out_weight, ffn_in, ffn_in_bias, ffn_out, norm_gain, shifts)


def add_parts(place, parts, halves, after=()):
    lanes = parts[0].shape[1]
    count = len(parts)
    many, rows = GROUPS[1:]
    outs = 2 if halves else 1

    def kernel(place_ref, *refs):
        out_refs, sum_ref = refs[count + len(after) : -1], refs[-1]
        bit = place_ref[0] & 1
        for start in range(0, lanes, 128):
            near = pl.ds(start, 128)
            total = refs[0][:, near].astype(F32)
            for ref in refs[1:count]:
                total = total + ref[:, near].astype(F32)
            if halves:
                sum_ref[:, :, near] = total.reshape(many, rows, 128)
            else:
                out_refs[0][:, near] = total.astype(LOW)
        for side, ref in enumerate(out_refs if halves else ()):
            for start in range(0, lanes, 128):
                near = pl.ds(start, 128)
                block = [sum_ref[2 * step + (bit ^ side), :, near] for step in range(many // 2)]
                ref[:, near] = jnp.concatenate(block, 0).astype(LOW)

    return pl.pallas_call(
        kernel,
        in_specs=[pl.BlockSpec(memory_space=pltpu.SMEM)]
        + [pl.BlockSpec(memory_space=pltpu.VMEM)] * count
        + [pl.BlockSpec(memory_space=pl.ANY)] * len(after),
        out_shape=[struct((many * rows // outs, lanes), LOW)] * outs,
        scratch_shapes=[vmem((many, rows, lanes), F32)],
        compiler_params=pltpu.CompilerParams(vmem_limit_bytes=MEMORY),
    )(place, *parts, *after)


def add_halves(place, pairs, after=()):
    many, rows = GROUPS[1] // 2, GROUPS[2]
    widths = [pair[0].shape[1] for pair in pairs]
    lanes = sum(widths)

    def kernel(place_ref, *refs):
        out_refs, sum_ref = refs[2 * len(pairs) + len(after) : -1], refs[-1]
        at = 0
        for index, size in enumerate(widths):
            for start in range(0, size, 128):
                near = pl.ds(start, 128)
                total = refs[2 * index][:, near].astype(F32) + refs[2 * index + 1][:, near].astype(F32)
                sum_ref[:, :, pl.ds(at + start, 128)] = total.reshape(many, rows, 128)
            at += size
        far = lax.shift_right_logical(place_ref[0], 1)
        for step, ref in enumerate(out_refs):
            ref[...] = sum_ref[far ^ step].astype(LOW)

    return pl.pallas_call(
        kernel,
        in_specs=[pl.BlockSpec(memory_space=pltpu.SMEM)]
        + [pl.BlockSpec(memory_space=pltpu.VMEM)] * (2 * len(pairs))
        + [pl.BlockSpec(memory_space=pl.ANY)] * len(after),
        out_shape=[struct((rows, lanes), LOW)] * many,
        scratch_shapes=[vmem((many, rows, lanes), F32)],
        compiler_params=pltpu.CompilerParams(vmem_limit_bytes=MEMORY),
    )(place, *(part for pair in pairs for part in pair), *after)


def write_gradients(found, depth, width, hidden, after):
    rows = GROUPS[2]
    height = hidden // DEVICES
    dense = width + 2 * hidden

    def kernel(*refs):
        found_refs, refs = refs[: len(found)], refs[len(found) + len(after) :]
        gwq_ref, gab_ref, gwo_ref, gwi_ref, gbi_ref, gwf_ref, gain_ref, shift_ref = refs

        def total(at, columns):
            value = found_refs[0][:, pl.ds(at, columns)].astype(F32)
            for ref in found_refs[1:]:
                value = value + ref[:, pl.ds(at, columns)].astype(F32)
            return value

        first, second = dense + 128, 2 * dense + 3 * width + 256
        blocks = [total(at, 128) for at in (dense, first + 3 * width + dense, second + 3 * width)]
        for layer, at, block in ((0, second, blocks[2]), (1, first, blocks[1])):
            gwq_ref[layer] = total(at, 3 * width)
            gab_ref[layer] = block[0:2, 0:rows]
        for layer, at, block in ((0, first + 3 * width, blocks[1]), (1, 0, blocks[0])):
            gwo_ref[layer] = total(at, width)
            gwi_ref[layer] = total(at + width, hidden)
            for step in range(hidden // width):
                gwf_ref[layer, pl.ds(step * rows, rows)] = total(
                    at + width + hidden + step * width, width
                )
            gain_ref[layer] = block[2:4, 0:rows]
            shift_ref[layer] = block[4:8, 0:rows]
            gbi_ref[pl.ds(layer, 1)] = pltpu.roll(block, 128 - 2 * rows, 1)[0:1, 0:height]

    outs = [
        struct((depth, rows, 3 * width), F32),
        struct((depth, 2, rows), F32),
        struct((depth, rows, width), F32),
        struct((depth, rows, hidden), F32),
        struct((depth, height), F32),
        struct((depth, height, width), F32),
        struct((depth, 2, rows), F32),
        struct((depth, 4, rows), F32),
    ]
    return pl.pallas_call(
        kernel,
        in_specs=[pl.BlockSpec(memory_space=pltpu.VMEM)] * len(found)
        + [pl.BlockSpec(memory_space=pl.ANY)] * len(after),
        out_shape=outs,
        compiler_params=pltpu.CompilerParams(vmem_limit_bytes=MEMORY),
    )(*found, *after)


def exchange(parts, axis):
    return lax.all_to_all(parts, axis, 0, 0, tiled=True)


def swap(part, axis, step):
    size = lax.axis_size(axis)
    return lax.ppermute(part, axis, [(source, source ^ step) for source in range(size)])


def local(
    hidden_in,
    lengths,
    grad_out,
    attn_weight,
    attn_bias,
    out_weight,
    ffn_in,
    ffn_in_bias,
    ffn_out,
    norm_gain,
    shifts,
):
    depth, rows, width = out_weight.shape
    hidden = ffn_in.shape[2]
    first, second = lax.axis_size("dp"), lax.axis_size("fsdp")
    fits = (second, first, rows) == GROUPS
    urgent_size = 3 * width + 128
    if fits:
        early, later = pack_parameters(
            attn_weight, attn_bias, out_weight, ffn_in, ffn_in_bias, ffn_out, norm_gain, shifts
        )
        across = lax.axis_index("dp").astype(jnp.int32).reshape(1)
        place = lax.axis_index("fsdp").astype(jnp.int32).reshape(1)
        partners = range(1, second)
        x0, dz1 = rotate_kernel(lengths, (hidden_in, grad_out))
        early = hold(exchange(early, "dp"), (x0,))
        urgent = early[:, :urgent_size]
        urgent = [urgent] + [swap(urgent, "fsdp", step) for step in partners]
        raw0 = early[:, urgent_size:]
        raw0 = [raw0, swap(raw0, "fsdp", 1), swap(raw0, "fsdp", 2)]
    else:
        urgent, raw0, raw1 = gather_other(
            attn_weight, attn_bias, out_weight, ffn_in, ffn_in_bias, ffn_out, norm_gain, shifts
        )
        urgent, raw0, raw1 = ([part[step] for step in range(4)] for part in (urgent, raw0, raw1))
        place = jnp.zeros((1,), jnp.int32)
        x0, dz1 = rotate_kernel(lengths, (hidden_in, grad_out))

    qa0, ka0, va0, ob0, lse0, urgent = first_kernel(lengths, x0, place, urgent)
    if fits:
        raw0[2] = hold(raw0[2], (ob0,))
        raw0.append(swap(raw0[2], "fsdp", 1))
        later = exchange(hold(later, (ob0,)), "dp")
    n1, n2, inv, yb, gb, gp, z0 = dense_kernel(
        0, lengths, x0, ob0, place, urgent, raw0, 3 * width, hidden
    )
    if fits:
        raw1 = hold(later, (z0,))
        raw1 = [raw1, swap(raw1, "fsdp", 1), swap(raw1, "fsdp", 2)]
    qa1, ka1, va1, ob1, lse1 = attention_kernel(1, lengths, z0, place, urgent, raw0, 0)
    if fits:
        raw1[2] = hold(raw1[2], (ob1,))
        raw1.append(swap(raw1[2], "fsdp", 1))
    z1, dr1, dob1, *sent_a = turn_kernel(
        1, lengths, z0, ob1, dz1, place, urgent, raw1, 0, hidden
    )
    dr0, dob0, *sent_b = middle_kernel(
        lengths,
        (z0, dob1, ob1, qa1, ka1, va1, lse1, dr1),
        (n1, n2, inv, yb, gb, gp, ob0),
        place,
        urgent,
        raw0,
        hidden,
        (sent_a[0],),
    )
    if fits:
        got_a = [sent_a[0]] + [swap(sent_a[step], "fsdp", step) for step in partners]
        keep_a, give_a = add_parts(across, got_a, True, (sent_b[0],))
        got_ax = swap(give_a, "dp", 1)
        ready = (sent_b[0], keep_a)
    else:
        ready = ()
    dqkv, *sent_c = last_kernel(
        lengths, (x0, dob0, ob0, qa0, ka0, va0, lse0), ready, place
    )
    hidden_out = outward_kernel(lengths, z1)
    if fits:
        got_b = [sent_b[0]] + [swap(sent_b[step], "fsdp", step) for step in partners]
        got_c = [sent_c[0]] + [swap(sent_c[step], "fsdp", step) for step in partners]
        keep_b, give_b = add_parts(across, got_b, True, (got_ax, hidden_out))
        keep_c, give_c = add_parts(across, got_c, True, (keep_b,))
        pairs = [(keep_a, got_ax), (keep_b, swap(give_b, "dp", 1)), (keep_c, swap(give_c, "dp", 1))]
        found = add_halves(across, pairs)
        grad_in = inward_kernel(lengths, dqkv, dr0, urgent, (found[0],))
        found = [found[0]] + [swap(found[step], "dp", 2 * step) for step in range(1, first // 2)]
        grads = write_gradients(found, depth, width, hidden, (grad_in,))
    else:
        grad_in = inward_kernel(lengths, dqkv, dr0, urgent, ())
        grads = scatter_other(
            *(jnp.stack(part) for part in (sent_a, sent_b, sent_c)), rows, width, hidden
        )
    return (hidden_out, grad_in, *grads)


def gather_other(
    attn_weight, attn_bias, out_weight, ffn_in, ffn_in_bias, ffn_out, norm_gain, shifts
):
    axes = ("dp", "fsdp")
    gather = lambda part, axis: lax.all_gather(part, axes, axis=axis, tiled=True)
    depth, unused, width = out_weight.shape
    hidden = ffn_in.shape[2]
    outer, inner, rows = GROUPS
    vectors = gather(jnp.concatenate([attn_bias, norm_gain, shifts], 1), 2)
    line = gather(ffn_in_bias, 1)

    def order(natural):
        return (
            natural.reshape(inner, outer, rows, -1).swapaxes(0, 1).reshape(outer, inner * rows, -1)
        )

    def stacked(part):
        part = part.reshape(DEVICES, -1, rows, width)
        return order(part.swapaxes(1, 2).reshape(width, -1))

    small = vectors.reshape(depth, 8, DEVICES, rows).transpose(2, 1, 0, 3).reshape(width, -1)
    line = line.reshape(depth, DEVICES, -1).swapaxes(0, 1)
    line = jnp.pad(line, ((0, 0), (0, 8 - depth), (0, 0))).reshape(width, -1)
    small = jnp.concatenate([small, line], 1)
    small = jnp.pad(small, ((0, 0), (0, 128 - small.shape[1])))
    wq, wo, wi, wf = (gather(part, 1) for part in (attn_weight, out_weight, ffn_in, ffn_out))
    urgent = jnp.concatenate([order(wq[0]), order(small)], 2)
    raw0 = jnp.concatenate([order(wq[1]), order(wo[0]), order(wi[0]), stacked(wf[0])], 2)
    raw1 = jnp.concatenate([order(wo[1]), order(wi[1]), stacked(wf[1])], 2)
    return urgent, raw0, raw1


def scatter_other(sent_a, sent_b, sent_c, own_rows, width, hidden):
    outer, inner, rows = GROUPS
    axes = ("dp", "fsdp")

    def natural(part):
        return part.reshape(outer, inner, rows, -1).swapaxes(0, 1).reshape(width, -1).astype(F32)

    def cut(part, sizes):
        found, at = [], 0
        for size in sizes:
            found.append(part[:, at : at + size])
            at += size
        return found

    dense = [width, hidden, hidden, 128]
    wq0, block_c = cut(natural(sent_c), [3 * width, 128])
    wq1, wo0, wi0, wf0, block_b = cut(natural(sent_b), [3 * width] + dense)
    wo1, wi1, wf1, block_a = cut(natural(sent_a), dense)

    def vectors(block):
        block = block.reshape(DEVICES, rows, 128)
        return block[:, :, :rows].swapaxes(0, 1).reshape(rows, width)

    def line(block):
        block = block.reshape(DEVICES, rows, 128)
        return block[:, 0, 2 * rows : 2 * rows + hidden // DEVICES].reshape(-1)

    def stacked(part):
        part = part.reshape(DEVICES, rows, -1, width).swapaxes(1, 2)
        return part.reshape(hidden, width)

    def spread(parts, axis):
        return lax.psum_scatter(jnp.stack(parts), axes, scatter_dimension=axis, tiled=True)

    return (
        spread([wq0, wq1], 1),
        spread([vectors(block_c)[0:2], vectors(block_b)[0:2]], 2),
        spread([wo0, wo1], 1),
        spread([wi0, wi1], 1),
        spread([line(block_b), line(block_a)], 1),
        spread([stacked(wf0), stacked(wf1)], 1),
        spread([vectors(block_b)[2:4], vectors(block_a)[2:4]], 2),
        spread([vectors(block_b)[4:8], vectors(block_a)[4:8]], 2),
    )


def solution(mesh):
    placed = (
        P(("dp", "fsdp"), None),
        P(("dp", "fsdp"), None),
        P(("dp", "fsdp"), None),
        P(None, ("dp", "fsdp"), None),
        P(None, None, ("dp", "fsdp")),
        P(None, ("dp", "fsdp"), None),
        P(None, ("dp", "fsdp"), None),
        P(None, ("dp", "fsdp")),
        P(None, ("dp", "fsdp"), None),
        P(None, None, ("dp", "fsdp")),
        P(None, None, ("dp", "fsdp")),
    )
    return jax.shard_map(
        local,
        mesh=mesh,
        in_specs=placed,
        out_specs=(
            P(("dp", "fsdp"), None),
            P(("dp", "fsdp"), None),
            P(None, ("dp", "fsdp"), None),
            P(None, None, ("dp", "fsdp")),
            P(None, ("dp", "fsdp"), None),
            P(None, ("dp", "fsdp"), None),
            P(None, ("dp", "fsdp")),
            P(None, ("dp", "fsdp"), None),
            P(None, None, ("dp", "fsdp")),
            P(None, None, ("dp", "fsdp")),
        ),
        check_vma=False,
    )
```

```python
from functools import partial

import jax
import jax.numpy as jnp
from jax import lax
from jax.experimental import pallas as pl
from jax.experimental.pallas import tpu as pltpu
from jax.sharding import PartitionSpec as P

HEADS = 4
HD = 64
SEQ = 512
PAIR = 2 * HD
EXTRA = 16
HALF = SEQ // 2
HALVES = (slice(0, HALF), slice(HALF, SEQ))
FAR = -(2.0**100)
FLOOR = -1e20
EPSILON = 1e-12
PIECE = 256
SMALL = 128
GROUPS = (4, 8, 8)
DEVICES = 32
LOW = jnp.bfloat16
F32 = jnp.float32
MEMORY = 2**26


def dot_nn(left, right):
    return lax.dot_general(left, right, (((1,), (0,)), ((), ())), preferred_element_type=F32)


def dot_nt(left, right):
    return lax.dot_general(left, right, (((1,), (1,)), ((), ())), preferred_element_type=F32)


def dot_tn(left, right):
    return lax.dot_general(left, right, (((0,), (0,)), ((), ())), preferred_element_type=F32)


def pieces(total, size=PIECE):
    return [pl.ds(start, size) for start in range(0, total, size)]


def three_parts(values):
    first = values.astype(LOW).astype(F32)
    rest = values - first
    second = rest.astype(LOW).astype(F32)
    return first, second, rest - second


BELL = -0.5 / 0.6931471805599453


def gelu_parts(u):
    cumulative = 0.5 + 0.5 * lax.erf(u * 0.7071067811865476)
    slope = cumulative + (u * 0.3989422804014327) * jnp.exp2(u * u * BELL)
    return u * cumulative, slope


def inverse_of(values):
    guess = pl.reciprocal(values, approx=True)
    return guess * (2.0 - values * guess)


def longest_start(lengths_ref, row):
    begin, found = jnp.int32(0), jnp.int32(0)
    for entry in range(lengths_ref.shape[1]):
        size = lengths_ref[row, entry]
        found = jnp.where(size == HALF, begin, found)
        begin = begin + size
    return found


def segments(lengths_ref, row):
    places = lax.broadcasted_iota(jnp.int32, (1, SEQ), 1) + longest_start(lengths_ref, row)
    places = places & (SEQ - 1)
    bound = jnp.int32(0)
    segment = jnp.zeros((1, SEQ), jnp.int32)
    last = lengths_ref.shape[1] - 1
    for entry in range(last):
        bound = bound + lengths_ref[row, entry]
        segment = segment + (places >= bound).astype(jnp.int32)
    return segment, last


def head_rows(head):
    return slice(head * HD, (head + 1) * HD)


def attention_forward(row, lengths_ref, x, wt_ref, bias_ref, qa_ref, ka_ref, va_ref, ob_ref, lse_ref, s_ref, p_ref):
    width = HEADS * HD
    segment, last = segments(lengths_ref, row)
    pad = (segment == last).astype(F32)
    line = lax.broadcasted_iota(jnp.int32, (EXTRA, SEQ), 0)
    aug_q = jnp.where(line == segment, 1.0, 0.0).astype(LOW)
    seen = (line == segment) & (segment != last)
    aug_k = jnp.where(seen | (line > last), 0.0, FAR).astype(LOW)
    aug_v = jnp.where(line == 0, 1.0, 0.0).astype(LOW)
    rest = jnp.zeros((PAIR - HD - EXTRA, SEQ), LOW)
    for head in range(HEADS):
        qa_ref[head, HD : HD + EXTRA] = aug_q
        ka_ref[head, HD : HD + EXTRA] = aug_k
        va_ref[head, HD : HD + EXTRA] = aug_v
        qa_ref[head, HD + EXTRA : PAIR] = rest
        ka_ref[head, HD + EXTRA : PAIR] = rest
    for block, ref in enumerate((qa_ref, ka_ref, va_ref)):
        lines = slice(block * width, (block + 1) * width)
        bias = bias_ref[lines]
        value = dot_nt(wt_ref[lines], x) + jnp.concatenate([bias] * (SEQ // 128), 1)
        if block == 0:
            value = value * HD**-0.5
        value = value.astype(LOW)
        for head in range(HEADS):
            ref[head, 0:HD] = value[head_rows(head)]
        yield

    def scores(head):
        for half in HALVES:
            s_ref[head % 2, half] = dot_tn(ka_ref[head, :, half], qa_ref[head, :, half])

    def softmax(head):
        tops = []
        for half in HALVES:
            tops.append(jnp.maximum(jnp.max(s_ref[head % 2, half], 0, keepdims=True), FLOOR))
            p_ref[head % 2, half] = jnp.exp(s_ref[head % 2, half] - tops[-1]).astype(LOW)
        return tops

    scores(0)
    yield
    for head in range(HEADS):
        if head + 1 < HEADS:
            scores(head + 1)
            yield
        tops = softmax(head)
        yield
        for half, top in zip(HALVES, tops):
            out = dot_nn(va_ref[head, :, half], p_ref[head % 2, half])
            alone = pad[:, half]
            total = out[HD : HD + 1] + alone
            lse_ref[head : head + 1, half] = jnp.where(alone > 0, 0.0, top + jnp.log(total))
            own = alone * va_ref[head, 0:HD, half].astype(F32)
            ob_ref[head_rows(head), half] = (out[0:HD] * inverse_of(total) + own).astype(LOW)
        yield


def normal(values):
    centred = values - jnp.mean(values, -1, keepdims=True)
    inverse = lax.rsqrt(jnp.mean(centred * centred, -1, keepdims=True) + EPSILON)
    return centred * inverse, inverse


def normal_back(cotangent, unit, inverse, gains):
    scaled = cotangent * gains
    return inverse * (
        scaled
        - jnp.mean(scaled, -1, keepdims=True)
        - unit * jnp.mean(scaled * unit, -1, keepdims=True)
    )


def dense_forward(x_ref, ob_ref, wo_ref, wi_ref, wf_ref, small_ref, bi_ref, n1_ref, n2_ref, inv_ref, yb_ref, gb_ref, gp_ref, z_ref, work_ref, u_ref):
    small = lambda index: small_ref[pl.ds(index, 1)]
    work_ref[...] = dot_tn(ob_ref[...], wo_ref[...])
    yield
    for place in pieces(SEQ):
        unit, inverse = normal(x_ref[place].astype(F32) + work_ref[place] + small(4))
        n1_ref[place] = unit
        inv_ref[place, pl.ds(0, HD)] = jnp.broadcast_to(inverse, (PIECE, HD))
        y = unit * small(2) + small(5)
        yb_ref[place] = y.astype(LOW)
        work_ref[place] = y + small(6)
        yield
    columns = 256
    count = wi_ref.shape[1] // columns

    def into(step):
        u_ref[step % 2] = dot_nn(yb_ref[...], wi_ref[:, pl.ds(step * columns, columns)])

    into(0)
    yield
    for step in range(count):
        if step + 1 < count:
            into(step + 1)
            yield
        lanes = pl.ds(step * columns, columns)
        for place in pieces(SEQ, SMALL):
            g, slope = gelu_parts(u_ref[step % 2, place] + bi_ref[:, lanes])
            gb_ref[place, lanes] = g.astype(LOW)
            gp_ref[place, lanes] = slope.astype(LOW)
            yield
    work_ref[...] += dot_nn(gb_ref[...], wf_ref[...])
    yield
    for place in pieces(SEQ):
        unit, inverse = normal(work_ref[place])
        n2_ref[place] = unit
        inv_ref[place, pl.ds(HD, HD)] = jnp.broadcast_to(inverse, (PIECE, HD))
        z_ref[place] = (unit * small(3) + small(7)).astype(z_ref.dtype)
        yield


def fold(values):
    return jnp.sum(values.reshape(-1, 8, values.shape[-1]), 0)


def dense_backward(dz_ref, n1_ref, n2_ref, inv_ref, yb_ref, gb_ref, gp_ref, ob_ref, wo_ref, wi_ref, wf_ref, small_ref, dr_ref, dob_ref, gwo_ref, gwi_ref, gwf_ref, gsmall_ref, gbi_ref, low_ref, u_ref, du_ref, turned_ref):
    small = lambda index: small_ref[pl.ds(index, 1)]
    for place in pieces(SEQ):
        dz = dz_ref[place].astype(F32)
        unit = n2_ref[place]
        gsmall_ref[3] += fold(dz * unit)
        gsmall_ref[7] += fold(dz)
        dr = normal_back(dz, unit, inv_ref[place, pl.ds(HD, 1)], small(3))
        dr_ref[place] = dr
        df = dr.astype(LOW)
        low_ref[place] = df
        gsmall_ref[6] += fold(df.astype(F32))
        yield
    columns = 256
    count = wi_ref.shape[1] // columns

    def back(step):
        u_ref[step % 2] = dot_nt(low_ref[...], wf_ref[pl.ds(step * columns, columns)])

    back(0)
    turned_ref[0, 0 : low_ref.shape[1]] = low_ref[...].T
    width = low_ref.shape[1]
    turned_ref[1, 0:width] = yb_ref[...].T
    turned_ref[1, width:] = jnp.ones((EXTRA, SEQ), LOW)
    yield
    for step in range(count):
        if step + 1 < count:
            back(step + 1)
            yield
        lanes = pl.ds(step * columns, columns)
        gwf_ref[:, lanes] += dot_nn(turned_ref[0, 0:width], gb_ref[:, lanes])
        yield
        for place in pieces(SEQ, SMALL):
            du = (u_ref[step % 2, place] * gp_ref[place, lanes].astype(F32)).astype(LOW)
            du_ref[place, lanes] = du
        yield
        product = dot_nn(turned_ref[1], du_ref[:, lanes])
        gwi_ref[:, lanes] += product[0:width]
        gbi_ref[:, lanes] += product[width : width + 8]
        yield
    u_ref[0] = dot_nt(du_ref[...], wi_ref[...])
    yield
    for place in pieces(SEQ):
        dy = dr_ref[place] + u_ref[0, place]
        unit = n1_ref[place]
        gsmall_ref[2] += fold(dy * unit)
        gsmall_ref[5] += fold(dy)
        dr = normal_back(dy, unit, inv_ref[place, pl.ds(0, 1)], small(2))
        dr_ref[place] = dr
        da = dr.astype(LOW)
        low_ref[place] = da
        gsmall_ref[4] += fold(da.astype(F32))
        yield
    gwo_ref[...] += dot_nn(ob_ref[...], low_ref[...])
    dob_ref[...] = dot_nt(wo_ref[...], low_ref[...]).astype(LOW)
    yield


def attention_backward(row, lengths_ref, x, do_ref, ob_ref, qa_ref, ka_ref, va_ref, lse_ref, dqkv_ref, gwq_ref, gbias_ref, p_ref, ds_ref, s_ref):
    width = HEADS * HD
    segment, last = segments(lengths_ref, row)
    pad = (segment == last).astype(F32)

    def scores(head):
        for half in HALVES:
            s_ref[0, head % 2, half] = dot_tn(ka_ref[head, :, half], qa_ref[head, :, half])
            s_ref[1, head % 2, half] = dot_tn(
                va_ref[head, 0:HD, half], do_ref[head_rows(head), half]
            )

    def weigh(head):
        product = do_ref[head_rows(head)].astype(F32) * ob_ref[head_rows(head)].astype(F32)
        centre = jnp.sum(product, 0, keepdims=True)
        for half in HALVES:
            p = jnp.exp(s_ref[0, head % 2, half] - lse_ref[head : head + 1, half])
            p_ref[head % 2, half] = p.astype(LOW)
            ds_ref[head % 2, half] = (p * (s_ref[1, head % 2, half] - centre[:, half])).astype(LOW)

    scores(0)
    yield
    for head in range(HEADS):
        if head + 1 < HEADS:
            scores(head + 1)
            yield
        weigh(head)
        yield
        for half in HALVES:
            ds, do = ds_ref[head % 2, half], do_ref[head_rows(head), half]
            dq = dot_nn(ka_ref[head, 0:HD, half], ds) * HD**-0.5
            dk = dot_nt(qa_ref[head, 0:HD, half], ds)
            dv = dot_nt(do, p_ref[head % 2, half]) + pad[:, half] * do.astype(F32)
            for block, value in enumerate((dq, dk, dv)):
                at = block * width + head * HD
                dqkv_ref[at : at + HD, half] = value.astype(LOW)
        yield
    for index, block in enumerate((0, 2)):
        value = dqkv_ref[block * width : (block + 1) * width].astype(F32)
        parts = [value[:, at : at + 128] for at in range(0, SEQ, 128)]
        gbias_ref[index] += (parts[0] + parts[1]) + (parts[2] + parts[3])
    gwq_ref[...] += dot_nn(dqkv_ref[...], x)
    yield


def unpack_matrix(raw_ref, at, into_ref):
    width = into_ref.shape[0]
    for start in range(0, into_ref.shape[1], width):
        block = raw_ref[:, :, pl.ds(at + start, width)].astype(F32)
        block = block.reshape(GROUPS + (width,)).swapaxes(0, 1).reshape(width, width)
        into_ref[:, pl.ds(start, width)] = block.astype(LOW)


def unpack_stacked(raw_ref, at, into_ref):
    width = into_ref.shape[1]
    count = into_ref.shape[0] // width
    blocks = [
        raw_ref[:, :, pl.ds(at + step * width, width)].astype(F32).reshape(GROUPS + (width,))
        for step in range(count)
    ]
    outer, inner, rows = GROUPS
    for place in range(inner):
        part = jnp.stack([jnp.stack([block[f, place] for block in blocks]) for f in range(outer)])
        size = outer * count * rows
        into_ref[pl.ds(place * size, size)] = part.reshape(size, width).astype(LOW)


def counter(shape, axis):
    return lax.broadcasted_iota(jnp.int32, shape, axis)


def split_by(values, size):
    return lax.shift_right_logical(values, size.bit_length() - 1), values & (size - 1)


def sources(rows):
    outer, inner, height = GROUPS
    group, within = split_by(counter((rows, 1), 0), height)
    far, near = split_by(group, inner)
    return near * outer + far, within


def unpack_vectors(raw_ref, at, layer):
    outer, inner, rows = GROUPS
    total = outer * inner * rows
    raw = raw_ref[:, :, pl.ds(at, 128)].reshape(total, 128)
    owner, place = split_by(counter((1, total), 1), rows)
    pick = jnp.where(counter((128, 1), 0) == rows * layer + place, 1.0, 0.0).astype(LOW)
    device, unused = sources(total)
    spread = jnp.where(owner == device, dot_nn(raw, pick), 0.0)
    return jnp.sum(spread.reshape(outer * inner, rows, total), 0)


def unpack_hidden(raw_ref, at, layer, hidden):
    outer, inner, rows = GROUPS
    total = outer * inner * rows
    raw = raw_ref[:, :, pl.ds(at, 128)].reshape(total, 128)
    owner, place = split_by(counter((1, hidden), 1), hidden // (outer * inner))
    pick = jnp.where(counter((128, 1), 0) == 2 * rows + place, 1.0, 0.0).astype(LOW)
    device, within = sources(total)
    device = jnp.where(within == layer, device, -1)
    spread = jnp.where(owner == device, dot_nn(raw, pick), 0.0)
    return jnp.sum(spread, 0, keepdims=True)


def pack_matrix(sum_ref, sent_ref, at, turned=False):
    width = sum_ref.shape[1 if turned else 0]
    outer, inner, rows = GROUPS
    for start in range(0, sum_ref.shape[0 if turned else 1], width):
        near = pl.ds(start, width)
        block = sum_ref[near].T if turned else sum_ref[:, near]
        block = block.reshape(inner, outer, rows, width)
        block = block.swapaxes(0, 1).reshape(outer, inner * rows, width)
        sent_ref[:, :, pl.ds(at + start, width)] = block.astype(LOW)


def pack_stacked(sum_ref, sent_ref, at):
    width = sum_ref.shape[0]
    outer, inner, rows = GROUPS
    count = sum_ref.shape[1] // width
    near = inner // count
    for step in range(count):
        block = sum_ref[:, pl.ds(step * width, width)].T
        block = block.reshape(near, outer, count, rows, width)
        for part in range(count):
            piece = jnp.stack([block[:, f, part] for f in range(outer)])
            piece = piece.reshape(outer, near * rows, width)
            sent_ref[:, pl.ds(step * near * rows, near * rows), pl.ds(at + part * width, width)] = (
                piece.astype(LOW)
            )


def pack_vectors(block, line, sent_ref, at):
    outer, inner, rows = GROUPS
    total = outer * inner * rows
    device, within = sources(total)
    owner, unused = split_by(counter((1, total), 1), rows)
    spread = jnp.broadcast_to(block[None], (outer * inner, rows, total)).reshape(total, total)
    spread = jnp.where(owner == device, spread, 0.0).astype(LOW)
    unused, place = split_by(counter((total, 1), 0), rows)
    found = dot_nn(spread, jnp.where(counter((1, 128), 1) == place, 1.0, 0.0).astype(LOW))
    if line is not None:
        hidden = line.shape[1]
        height = hidden // (outer * inner)
        owner, unused = split_by(counter((1, hidden), 1), height)
        spread = jnp.where(owner == jnp.where(within == 0, device, -1), line, 0.0).astype(LOW)
        unused, place = split_by(counter((hidden, 1), 0), height)
        pick = jnp.where(counter((1, 128), 1) == 2 * rows + place, 1.0, 0.0).astype(LOW)
        found = found + dot_nn(spread, pick)
    sent_ref[:, :, pl.ds(at, 128)] = found.reshape(outer, inner * rows, 128).astype(LOW)


def bias_rows(gbias_ref):
    width = gbias_ref.shape[1]
    parts = [jnp.sum(gbias_ref[index].T, 0, keepdims=True) for index in range(2)]
    return jnp.concatenate(parts + [jnp.zeros((6, width), F32)], 0)


def pack_dense(gwo_ref, gwi_ref, gwf_ref, gsmall_ref, gbi_ref, block, sent_ref, at):
    width, hidden = gwi_ref.shape
    pack_matrix(gwo_ref, sent_ref, at)
    pack_matrix(gwi_ref, sent_ref, at + width)
    pack_stacked(gwf_ref, sent_ref, at + width + hidden)
    block = jnp.sum(gsmall_ref[...], 1) + block
    pack_vectors(block, gbi_ref[0:1], sent_ref, at + width + 2 * hidden)


def shape_of(array):
    return jax.ShapeDtypeStruct(array.shape, array.dtype)


def by_row(shape, group):
    if len(shape) == 2:
        return pl.BlockSpec((group * SEQ, shape[1]), lambda step: (step, 0))
    return pl.BlockSpec((group,) + tuple(shape[1:]), lambda step: (step,) + (0,) * (len(shape) - 1))


def one_row(ref, member):
    if len(ref.shape) == 2:
        return ref.at[pl.ds(member * SEQ, SEQ)]
    return ref.at[member]


def alternate(runs):
    running = []
    waiting = list(runs)
    while running or waiting:
        if waiting:
            running.append(waiting.pop(0))
        for run in list(running):
            try:
                next(run)
            except StopIteration:
                running.remove(run)


def whole(shape):
    return pl.BlockSpec(tuple(shape), lambda row: (0,) * len(shape))


def run_rows(
    body, lengths, rowwise, fixed, row_outs, sent, shared, private, cost, setup, finish, after=(),
    scalars=(), group=1
):
    count = lengths.shape[0]
    group = group if count % group == 0 else 1
    cuts = [len(scalars), len(rowwise), len(fixed), len(after), len(row_outs), len(sent)]
    cuts += [len(shared)] + [len(private)] * group

    def kernel(lengths_ref, *refs):
        step = pl.program_id(0)
        groups = []
        at = 0
        for cut in cuts:
            groups.append(refs[at : at + cut])
            at += cut
        numbers, rows_in, fixed_in, unused, rows_out, sent_out, work = groups[:7]

        @pl.when(step == 0)
        def _():
            setup(numbers, fixed_in, sent_out, work)

        alternate(
            body(
                step * group + member,
                lengths_ref,
                [one_row(ref, member) for ref in rows_in],
                [one_row(ref, member) for ref in rows_out],
                work,
                groups[7 + member],
            )
            for member in range(group)
        )

        if finish:

            @pl.when(step == count // group - 1)
            def _():
                finish(numbers, work, sent_out)

    return pl.pallas_call(
        kernel,
        grid=(count // group,),
        in_specs=[pl.BlockSpec(memory_space=pltpu.SMEM)] * (1 + len(scalars))
        + [by_row(array.shape, group) for array in rowwise]
        + [whole(array.shape) for array in fixed]
        + [pl.BlockSpec(memory_space=pl.ANY) for array in after],
        out_specs=[by_row(part.shape, group) for part in row_outs]
        + [whole(part.shape) for part in sent],
        out_shape=list(row_outs) + list(sent),
        scratch_shapes=list(shared) + list(private) * group,
        compiler_params=pltpu.CompilerParams(
            dimension_semantics=("arbitrary",), vmem_limit_bytes=MEMORY
        ),
        cost_estimate=pl.CostEstimate(flops=cost, bytes_accessed=8 * 2**20, transcendentals=0),
    )(lengths, *scalars, *rowwise, *fixed, *after)


def struct(shape, dtype):
    return jax.ShapeDtypeStruct(tuple(shape), dtype)


FORWARD_SCRATCH = lambda: [
    pltpu.VMEM((2, SEQ, HALF), F32),
    pltpu.VMEM((2, SEQ, HALF), LOW),
]
BACKWARD_SCRATCH = lambda: [
    pltpu.VMEM((2, SEQ, HALF), LOW),
    pltpu.VMEM((2, SEQ, HALF), LOW),
    pltpu.VMEM((2, 2, SEQ, HALF), F32),
    pltpu.VMEM((3 * HEADS * HD, SEQ), LOW),
]


def attention_outs(rows, width):
    return [
        struct((rows, HEADS, PAIR, SEQ), LOW),
        struct((rows, HEADS, PAIR, SEQ), LOW),
        struct((rows, HEADS, HD + EXTRA, SEQ), LOW),
        struct((rows, width, SEQ), LOW),
        struct((rows, 8, SEQ), F32),
    ]


def dense_outs(tokens, width, hidden):
    return [
        struct((tokens, width), F32),
        struct((tokens, width), F32),
        struct((tokens, PAIR), F32),
        struct((tokens, width), LOW),
        struct((tokens, hidden), LOW),
        struct((tokens, hidden), LOW),
    ]


def vmem(shape, dtype):
    return pltpu.VMEM(tuple(shape), dtype)


def attention_weights(width):
    return [vmem((width, 3 * width), LOW), vmem((3 * width, width), LOW), vmem((3 * width, 128), F32)]


def dense_weights(width, hidden):
    return [
        vmem((width, width), LOW),
        vmem((width, hidden), LOW),
        vmem((hidden, width), LOW),
        vmem((8, width), F32),
        vmem((1, hidden), F32),
    ]


def dense_sums(width, hidden):
    return [
        vmem((width, width), F32),
        vmem((width, hidden), F32),
        vmem((width, hidden), F32),
        vmem((8, 8, width), F32),
        vmem((8, hidden), F32),
    ]


def attention_sums(width):
    return [vmem((3 * width, width), F32), vmem((2, width, 128), F32)]


def dense_work(width, hidden):
    return [
        vmem((SEQ, width), LOW),
        vmem((2, SEQ, width), F32),
        vmem((SEQ, hidden), LOW),
        vmem((2, width + EXTRA, SEQ), LOW),
    ]


def set_attention(layer, urgent_ref, raw_ref, at, wq_ref, wt_ref, bias_ref):
    width = wq_ref.shape[0]
    unpack_matrix(raw_ref, at, wq_ref)
    vectors = unpack_vectors(urgent_ref, 3 * width, layer)
    for block, line in enumerate((vectors[0:1], jnp.zeros((1, width), F32), vectors[1:2])):
        lines = pl.ds(block * width, width)
        wt_ref[lines] = wq_ref[:, lines].astype(F32).T.astype(LOW)
        bias_ref[lines] = jnp.broadcast_to(line, (128, width)).T


def set_dense(layer, urgent_ref, raw_ref, at, wo_ref, wi_ref, wf_ref, small_ref, bi_ref):
    width, hidden = wi_ref.shape
    unpack_matrix(raw_ref, at, wo_ref)
    unpack_matrix(raw_ref, at + width, wi_ref)
    unpack_stacked(raw_ref, at + width + hidden, wf_ref)
    small_ref[...] = unpack_vectors(urgent_ref, 3 * width, layer)
    bi_ref[...] = unpack_hidden(urgent_ref, 3 * width, layer, hidden)


def clear(refs):
    for ref in refs:
        ref[...] = jnp.zeros(ref.shape, ref.dtype)


def assemble(place_ref, part_refs, into_ref):
    for step, ref in enumerate(part_refs):
        into_ref[place_ref[0] ^ step] = ref[...]


def raw_block(parts):
    return vmem((len(parts),) + parts[0].shape, LOW)


def turned_back(lengths_ref, row, values):
    return pltpu.roll(values, longest_start(lengths_ref, row), 0).astype(LOW)


def rotate_kernel(lengths, arrays):
    def body(row, lengths_ref, rowwise, outs, work, own):
        back = (SEQ - longest_start(lengths_ref, row)) & (SEQ - 1)
        for source, target in zip(rowwise, outs):
            target[...] = pltpu.roll(source[...].astype(F32), back, 0).astype(LOW)
            yield

    return run_rows(
        body, lengths, list(arrays), [], [struct(array.shape, LOW) for array in arrays], [], [], [],
        10**6, lambda *refs: None, None,
    )


def first_kernel(lengths, x, place, parts):
    rows, (tokens, width) = lengths.shape[0], x.shape

    def setup(numbers, fixed, sent, work):
        assemble(numbers[0], fixed, sent[0])
        set_attention(0, sent[0], sent[0], 0, *work)

    def body(row, lengths_ref, rowwise, outs, work, own):
        return attention_forward(row, lengths_ref, rowwise[0][...], *work[1:3], *outs, *own)

    return run_rows(
        body, lengths, [x], list(parts), attention_outs(rows, width),
        [struct((len(parts),) + parts[0].shape, LOW)],
        attention_weights(width), FORWARD_SCRATCH(), 4 * 10**9, setup, None, (), [place],
    )


def attention_kernel(layer, lengths, x, place, urgent, parts, at):
    rows, (tokens, width) = lengths.shape[0], x.shape

    def setup(numbers, fixed, sent, work):
        assemble(numbers[0], fixed[1:], work[3])
        set_attention(layer, fixed[0], work[3], at, *work[:3])

    def body(row, lengths_ref, rowwise, outs, work, own):
        return attention_forward(
            row, lengths_ref, rowwise[0][...].astype(LOW), *work[1:3], *outs, *own
        )

    return run_rows(
        body, lengths, [x], [urgent] + list(parts), attention_outs(rows, width), [],
        attention_weights(width) + [raw_block(parts)], FORWARD_SCRATCH(),
        4 * 10**9, setup, None, (), [place],
    )


def dense_kernel(layer, lengths, x, ob, place, urgent, parts, at, hidden):
    tokens, width = x.shape

    def setup(numbers, fixed, sent, work):
        assemble(numbers[0], fixed[1:], work[5])
        set_dense(layer, fixed[0], work[5], at, *work[:5])

    def body(row, lengths_ref, rowwise, outs, work, own):
        return dense_forward(*rowwise, *work[:5], *outs, *own)

    return run_rows(
        body, lengths, [x, ob], [urgent] + list(parts),
        dense_outs(tokens, width, hidden) + [struct((tokens, width), F32)], [],
        dense_weights(width, hidden) + [raw_block(parts)],
        [vmem((SEQ, width), F32), vmem((2, SEQ, width), F32)],
        5 * 10**9, setup, None, (), [place],
    )


def turn_kernel(layer, lengths, x, ob, cotangent, place, urgent, parts, at, hidden):
    tokens, width = x.shape
    columns = width + 2 * hidden + 128

    def setup(numbers, fixed, sent, work):
        assemble(numbers[0], fixed[1:], work[11])
        set_dense(layer, fixed[0], work[11], at, *work[:5])
        clear(work[5:10])

    def body(row, lengths_ref, rowwise, outs, work, own):
        x_ref, ob_ref, dz_ref = rowwise
        z_ref, dr_ref, dob_ref = outs
        weights, sums = work[:5], work[5:10]
        kept, work_ref, back = own[:6], own[6], own[7:]
        yield from dense_forward(x_ref, ob_ref, *weights, *kept, z_ref, work_ref, back[1])
        yield from dense_backward(dz_ref, *kept, ob_ref, *weights[:4], dr_ref, dob_ref, *sums, *back)

    def finish(numbers, work, sent):
        pack_dense(*work[5:10], 0.0, work[10], 0)
        hand_out(numbers[0], work[10], sent)

    kept = [vmem((SEQ,) + part.shape[1:], part.dtype) for part in dense_outs(tokens, width, hidden)]
    return run_rows(
        body, lengths, [x, ob, cotangent], [urgent] + list(parts),
        [struct((tokens, width), LOW), struct((tokens, width), F32), struct((tokens // SEQ, width, SEQ), LOW)],
        [struct((64, columns), LOW)] * 4,
        dense_weights(width, hidden) + dense_sums(width, hidden)
        + [vmem((4, 64, columns), LOW), raw_block(parts)],
        kept + [vmem((SEQ, width), F32)] + dense_work(width, hidden),
        10**10, setup, finish, (), [place], 2,
    )


def hand_out(place_ref, packed_ref, sent):
    for step, ref in enumerate(sent):
        ref[...] = packed_ref[place_ref[0] ^ step]


def middle_kernel(lengths, upper, lower, place, urgent, parts, hidden, after):
    tokens, width = upper[0].shape
    columns = 4 * width + 2 * hidden + 128

    def setup(numbers, fixed, sent, work):
        assemble(numbers[0], fixed[1:], work[16])
        set_attention(1, fixed[0], work[16], 0, *work[:3])
        set_dense(0, fixed[0], work[16], 3 * width, *work[3:8])
        clear(work[8:15])

    def body(row, lengths_ref, rowwise, outs, work, own):
        up, low = rowwise[:8], rowwise[8:]
        dx_ref = own[0]
        yield from attention_backward(
            row, lengths_ref, up[0][...].astype(LOW), *up[1:7], own[-1], *work[8:10], *own[5:-1]
        )
        dx_ref[...] = up[7][...] + dot_tn(own[-1][...], work[1][...])
        yield
        yield from dense_backward(dx_ref, *low, *work[3:7], *outs, *work[10:15], *own[1:5])

    def finish(numbers, work, sent):
        pack_matrix(work[8], work[15], 0, True)
        pack_dense(*work[10:15], bias_rows(work[9]), work[15], 3 * width)
        hand_out(numbers[0], work[15], sent)

    return run_rows(
        body, lengths, list(upper) + list(lower), [urgent] + list(parts),
        [struct((tokens, width), F32), struct((tokens // SEQ, width, SEQ), LOW)],
        [struct((64, columns), LOW)] * 4,
        attention_weights(width) + dense_weights(width, hidden)
        + attention_sums(width) + dense_sums(width, hidden)
        + [vmem((4, 64, columns), LOW), raw_block(parts)],
        [vmem((SEQ, width), F32)] + dense_work(width, hidden) + BACKWARD_SCRATCH(),
        15 * 10**9, setup, finish, after, [place], 2,
    )


def last_kernel(lengths, upper, after, place):
    tokens, width = upper[0].shape

    def setup(numbers, fixed, sent, work):
        clear(work[:2])

    def body(row, lengths_ref, rowwise, outs, work, own):
        return attention_backward(
            row, lengths_ref, rowwise[0][...], *rowwise[1:], outs[0], *work[:2], *own
        )

    def finish(numbers, work, sent):
        pack_matrix(work[0], work[2], 0, True)
        pack_vectors(bias_rows(work[1]), None, work[2], 3 * width)
        hand_out(numbers[0], work[2], sent)

    return run_rows(
        body, lengths, list(upper), [], [struct((tokens // SEQ, 3 * width, SEQ), LOW)],
        [struct((64, 3 * width + 128), LOW)] * 4,
        attention_sums(width) + [vmem((4, 64, 3 * width + 128), LOW)],
        BACKWARD_SCRATCH()[:-1], 8 * 10**9, setup, finish, after, [place], 2,
    )


def outward_kernel(lengths, z, after):
    def body(row, lengths_ref, rowwise, outs, work, own):
        outs[0][...] = turned_back(lengths_ref, row, rowwise[0][...].astype(F32))
        yield

    (found,) = run_rows(
        body, lengths, [z], [], [struct(z.shape, LOW)], [], [], [], 3 * 10**9,
        lambda *refs: None, None, after,
    )
    return found


def inward_kernel(lengths, dqkv, dr, urgent, after):
    tokens, width = dr.shape

    def setup(numbers, fixed, sent, work):
        set_attention(0, fixed[0], fixed[0], 0, *work)

    def body(row, lengths_ref, rowwise, outs, work, own):
        dqkv_ref, dr_ref = rowwise
        dx = dr_ref[...] + dot_tn(dqkv_ref[...], work[1][...])
        outs[0][...] = turned_back(lengths_ref, row, dx)
        yield

    (found,) = run_rows(
        body, lengths, [dqkv, dr], [urgent], [struct((tokens, width), LOW)], [],
        attention_weights(width), [], 10**10, setup, None, after,
    )
    return found


def hold(array, after):
    def kernel(*refs):
        pass

    anywhere = pl.BlockSpec(memory_space=pl.ANY)
    return pl.pallas_call(
        kernel,
        in_specs=[anywhere] * (1 + len(after)),
        out_specs=anywhere,
        out_shape=shape_of(array),
        input_output_aliases={0: 0},
    )(array, *after)


def pack_parameters(
    attn_weight, attn_bias, out_weight, ffn_in, ffn_in_bias, ffn_out, norm_gain, shifts
):
    depth, rows, width = out_weight.shape
    copies = GROUPS[1]
    hidden = ffn_in.shape[2]
    dense = width + 2 * hidden
    height = ffn_in_bias.shape[1]

    def kernel(wq_ref, ab_ref, wo_ref, wi_ref, bi_ref, wf_ref, gain_ref, shift_ref, first_ref, rest_ref, small_ref):
        def put(ref, block, at):
            block = jnp.broadcast_to(block.astype(F32)[None], (copies,) + block.shape)
            block = block.reshape(copies * block.shape[1], block.shape[2])
            ref[:, pl.ds(at, block.shape[1])] = block.astype(LOW)

        small_ref[...] = jnp.zeros(small_ref.shape, F32)
        for layer in range(depth):
            lanes = pl.ds(rows * layer, rows)
            small_ref[0:2, lanes] = ab_ref[layer].astype(F32)
            small_ref[2:4, lanes] = gain_ref[layer].astype(F32)
            small_ref[4:8, lanes] = shift_ref[layer].astype(F32)
        small_ref[0:depth, pl.ds(2 * rows, height)] = bi_ref[...].astype(F32)
        put(first_ref, wq_ref[0], 0)
        put(first_ref, small_ref[...], 3 * width)
        put(first_ref, wq_ref[1], 3 * width + 128)
        for layer, ref, at in ((0, first_ref, 6 * width + 128), (1, rest_ref, 0)):
            put(ref, wo_ref[layer], at)
            put(ref, wi_ref[layer], at + width)
            at += width + hidden
            down = wf_ref[layer].astype(F32)
            for step in range(hidden // width):
                put(ref, down[step * rows : (step + 1) * rows], at)
                at += width

    return pl.pallas_call(
        kernel,
        in_specs=[pl.BlockSpec(memory_space=pltpu.VMEM)] * 8,
        out_shape=[
            struct((copies * rows, 6 * width + 128 + dense), LOW),
            struct((copies * rows, dense), LOW),
        ],
        scratch_shapes=[vmem((rows, 128), F32)],
        compiler_params=pltpu.CompilerParams(vmem_limit_bytes=MEMORY),
    )(attn_weight, attn_bias, out_weight, ffn_in, ffn_in_bias, ffn_out, norm_gain, shifts)


def add_parts(place, parts, halves, after=()):
    lanes = parts[0].shape[1]
    count = len(parts)
    many, rows = GROUPS[1:]
    outs = 2 if halves else 1

    def kernel(place_ref, *refs):
        out_refs, sum_ref = refs[count + len(after) : -1], refs[-1]
        bit = place_ref[0] & 1
        for start in range(0, lanes, 128):
            near = pl.ds(start, 128)
            total = refs[0][:, near].astype(F32)
            for ref in refs[1:count]:
                total = total + ref[:, near].astype(F32)
            if halves:
                sum_ref[:, :, near] = total.reshape(many, rows, 128)
            else:
                out_refs[0][:, near] = total.astype(LOW)
        for side, ref in enumerate(out_refs if halves else ()):
            for start in range(0, lanes, 128):
                near = pl.ds(start, 128)
                block = [sum_ref[2 * step + (bit ^ side), :, near] for step in range(many // 2)]
                ref[:, near] = jnp.concatenate(block, 0).astype(LOW)

    return pl.pallas_call(
        kernel,
        in_specs=[pl.BlockSpec(memory_space=pltpu.SMEM)]
        + [pl.BlockSpec(memory_space=pltpu.VMEM)] * count
        + [pl.BlockSpec(memory_space=pl.ANY)] * len(after),
        out_shape=[struct((many * rows // outs, lanes), LOW)] * outs,
        scratch_shapes=[vmem((many, rows, lanes), F32)],
        compiler_params=pltpu.CompilerParams(vmem_limit_bytes=MEMORY),
    )(place, *parts, *after)


def add_halves(place, pairs, after=()):
    many, rows = GROUPS[1] // 2, GROUPS[2]
    widths = [pair[0].shape[1] for pair in pairs]
    lanes = sum(widths)

    def kernel(place_ref, *refs):
        out_refs, sum_ref = refs[2 * len(pairs) + len(after) : -1], refs[-1]
        at = 0
        for index, size in enumerate(widths):
            for start in range(0, size, 128):
                near = pl.ds(start, 128)
                total = refs[2 * index][:, near].astype(F32) + refs[2 * index + 1][:, near].astype(F32)
                sum_ref[:, :, pl.ds(at + start, 128)] = total.reshape(many, rows, 128)
            at += size
        far = lax.shift_right_logical(place_ref[0], 1)
        for step, ref in enumerate(out_refs):
            ref[...] = sum_ref[far ^ step].astype(LOW)

    return pl.pallas_call(
        kernel,
        in_specs=[pl.BlockSpec(memory_space=pltpu.SMEM)]
        + [pl.BlockSpec(memory_space=pltpu.VMEM)] * (2 * len(pairs))
        + [pl.BlockSpec(memory_space=pl.ANY)] * len(after),
        out_shape=[struct((rows, lanes), LOW)] * many,
        scratch_shapes=[vmem((many, rows, lanes), F32)],
        compiler_params=pltpu.CompilerParams(vmem_limit_bytes=MEMORY),
    )(place, *(part for pair in pairs for part in pair), *after)


def write_gradients(found, depth, width, hidden, after):
    rows = GROUPS[2]
    height = hidden // DEVICES
    dense = width + 2 * hidden

    def kernel(*refs):
        found_refs, refs = refs[: len(found)], refs[len(found) + len(after) :]
        gwq_ref, gab_ref, gwo_ref, gwi_ref, gbi_ref, gwf_ref, gain_ref, shift_ref = refs

        def total(at, columns):
            value = found_refs[0][:, pl.ds(at, columns)].astype(F32)
            for ref in found_refs[1:]:
                value = value + ref[:, pl.ds(at, columns)].astype(F32)
            return value

        first, second = dense + 128, 2 * dense + 3 * width + 256
        blocks = [total(at, 128) for at in (dense, first + 3 * width + dense, second + 3 * width)]
        for layer, at, block in ((0, second, blocks[2]), (1, first, blocks[1])):
            gwq_ref[layer] = total(at, 3 * width)
            gab_ref[layer] = block[0:2, 0:rows]
        for layer, at, block in ((0, first + 3 * width, blocks[1]), (1, 0, blocks[0])):
            gwo_ref[layer] = total(at, width)
            gwi_ref[layer] = total(at + width, hidden)
            for step in range(hidden // width):
                gwf_ref[layer, pl.ds(step * rows, rows)] = total(
                    at + width + hidden + step * width, width
                )
            gain_ref[layer] = block[2:4, 0:rows]
            shift_ref[layer] = block[4:8, 0:rows]
            gbi_ref[pl.ds(layer, 1)] = pltpu.roll(block, 128 - 2 * rows, 1)[0:1, 0:height]

    outs = [
        struct((depth, rows, 3 * width), F32),
        struct((depth, 2, rows), F32),
        struct((depth, rows, width), F32),
        struct((depth, rows, hidden), F32),
        struct((depth, height), F32),
        struct((depth, height, width), F32),
        struct((depth, 2, rows), F32),
        struct((depth, 4, rows), F32),
    ]
    return pl.pallas_call(
        kernel,
        in_specs=[pl.BlockSpec(memory_space=pltpu.VMEM)] * len(found)
        + [pl.BlockSpec(memory_space=pl.ANY)] * len(after),
        out_shape=outs,
        compiler_params=pltpu.CompilerParams(vmem_limit_bytes=MEMORY),
    )(*found, *after)


def exchange(parts, axis):
    return lax.all_to_all(parts, axis, 0, 0, tiled=True)


def swap(part, axis, step):
    size = lax.axis_size(axis)
    return lax.ppermute(part, axis, [(source, source ^ step) for source in range(size)])


def local(
    hidden_in,
    lengths,
    grad_out,
    attn_weight,
    attn_bias,
    out_weight,
    ffn_in,
    ffn_in_bias,
    ffn_out,
    norm_gain,
    shifts,
):
    depth, rows, width = out_weight.shape
    hidden = ffn_in.shape[2]
    first, second = lax.axis_size("dp"), lax.axis_size("fsdp")
    fits = (second, first, rows) == GROUPS
    urgent_size = 3 * width + 128
    if fits:
        early, later = pack_parameters(
            attn_weight, attn_bias, out_weight, ffn_in, ffn_in_bias, ffn_out, norm_gain, shifts
        )
        across = lax.axis_index("dp").astype(jnp.int32).reshape(1)
        place = lax.axis_index("fsdp").astype(jnp.int32).reshape(1)
        partners = range(1, second)
        x0, dz1 = rotate_kernel(lengths, (hidden_in, grad_out))
        early = hold(exchange(early, "dp"), (x0,))
        urgent = early[:, :urgent_size]
        urgent = [urgent] + [swap(urgent, "fsdp", step) for step in partners]
        raw0 = early[:, urgent_size:]
        raw0 = [raw0, swap(raw0, "fsdp", 1), swap(raw0, "fsdp", 2)]
    else:
        urgent, raw0, raw1 = gather_other(
            attn_weight, attn_bias, out_weight, ffn_in, ffn_in_bias, ffn_out, norm_gain, shifts
        )
        urgent, raw0, raw1 = ([part[step] for step in range(4)] for part in (urgent, raw0, raw1))
        place = jnp.zeros((1,), jnp.int32)
        x0, dz1 = rotate_kernel(lengths, (hidden_in, grad_out))

    qa0, ka0, va0, ob0, lse0, urgent = first_kernel(lengths, x0, place, urgent)
    if fits:
        raw0[2] = hold(raw0[2], (ob0,))
        raw0.append(swap(raw0[2], "fsdp", 1))
        later = exchange(hold(later, (ob0,)), "dp")
    n1, n2, inv, yb, gb, gp, z0 = dense_kernel(
        0, lengths, x0, ob0, place, urgent, raw0, 3 * width, hidden
    )
    if fits:
        raw1 = hold(later, (z0,))
        raw1 = [raw1, swap(raw1, "fsdp", 1), swap(raw1, "fsdp", 2)]
    qa1, ka1, va1, ob1, lse1 = attention_kernel(1, lengths, z0, place, urgent, raw0, 0)
    if fits:
        raw1[2] = hold(raw1[2], (ob1,))
        raw1.append(swap(raw1[2], "fsdp", 1))
    z1, dr1, dob1, *sent_a = turn_kernel(
        1, lengths, z0, ob1, dz1, place, urgent, raw1, 0, hidden
    )
    dr0, dob0, *sent_b = middle_kernel(
        lengths,
        (z0, dob1, ob1, qa1, ka1, va1, lse1, dr1),
        (n1, n2, inv, yb, gb, gp, ob0),
        place,
        urgent,
        raw0,
        hidden,
        (sent_a[0],),
    )
    if fits:
        got_a = [sent_a[0]] + [swap(sent_a[step], "fsdp", step) for step in partners]
        keep_a, give_a = add_parts(across, got_a, True, (sent_b[0],))
        got_ax = swap(give_a, "dp", 1)
        ready = (sent_b[0], keep_a)
    else:
        ready = ()
    dqkv, *sent_c = last_kernel(
        lengths, (x0, dob0, ob0, qa0, ka0, va0, lse0), ready, place
    )
    hidden_out = outward_kernel(lengths, z1, (sent_c[0],))
    if fits:
        got_b = [sent_b[0]] + [swap(sent_b[step], "fsdp", step) for step in partners]
        got_c = [sent_c[0]] + [swap(sent_c[step], "fsdp", step) for step in partners]
        keep_b, give_b = add_parts(across, got_b, True, (got_ax, hidden_out))
        keep_c, give_c = add_parts(across, got_c, True, (keep_b,))
        pairs = [(keep_a, got_ax), (keep_b, swap(give_b, "dp", 1)), (keep_c, swap(give_c, "dp", 1))]
        found = add_halves(across, pairs)
        grad_in = inward_kernel(lengths, dqkv, dr0, urgent, (found[0],))
        found = [found[0]] + [swap(found[step], "dp", 2 * step) for step in range(1, first // 2)]
        grads = write_gradients(found, depth, width, hidden, (grad_in,))
    else:
        grad_in = inward_kernel(lengths, dqkv, dr0, urgent, ())
        grads = scatter_other(
            *(jnp.stack(part) for part in (sent_a, sent_b, sent_c)), rows, width, hidden
        )
    return (hidden_out, grad_in, *grads)


def gather_other(
    attn_weight, attn_bias, out_weight, ffn_in, ffn_in_bias, ffn_out, norm_gain, shifts
):
    axes = ("dp", "fsdp")
    gather = lambda part, axis: lax.all_gather(part, axes, axis=axis, tiled=True)
    depth, unused, width = out_weight.shape
    hidden = ffn_in.shape[2]
    outer, inner, rows = GROUPS
    vectors = gather(jnp.concatenate([attn_bias, norm_gain, shifts], 1), 2)
    line = gather(ffn_in_bias, 1)

    def order(natural):
        return (
            natural.reshape(inner, outer, rows, -1).swapaxes(0, 1).reshape(outer, inner * rows, -1)
        )

    def stacked(part):
        part = part.reshape(DEVICES, -1, rows, width)
        return order(part.swapaxes(1, 2).reshape(width, -1))

    small = vectors.reshape(depth, 8, DEVICES, rows).transpose(2, 1, 0, 3).reshape(width, -1)
    line = line.reshape(depth, DEVICES, -1).swapaxes(0, 1)
    line = jnp.pad(line, ((0, 0), (0, 8 - depth), (0, 0))).reshape(width, -1)
    small = jnp.concatenate([small, line], 1)
    small = jnp.pad(small, ((0, 0), (0, 128 - small.shape[1])))
    wq, wo, wi, wf = (gather(part, 1) for part in (attn_weight, out_weight, ffn_in, ffn_out))
    urgent = jnp.concatenate([order(wq[0]), order(small)], 2)
    raw0 = jnp.concatenate([order(wq[1]), order(wo[0]), order(wi[0]), stacked(wf[0])], 2)
    raw1 = jnp.concatenate([order(wo[1]), order(wi[1]), stacked(wf[1])], 2)
    return urgent, raw0, raw1


def scatter_other(sent_a, sent_b, sent_c, own_rows, width, hidden):
    outer, inner, rows = GROUPS
    axes = ("dp", "fsdp")

    def natural(part):
        return part.reshape(outer, inner, rows, -1).swapaxes(0, 1).reshape(width, -1).astype(F32)

    def cut(part, sizes):
        found, at = [], 0
        for size in sizes:
            found.append(part[:, at : at + size])
            at += size
        return found

    dense = [width, hidden, hidden, 128]
    wq0, block_c = cut(natural(sent_c), [3 * width, 128])
    wq1, wo0, wi0, wf0, block_b = cut(natural(sent_b), [3 * width] + dense)
    wo1, wi1, wf1, block_a = cut(natural(sent_a), dense)

    def vectors(block):
        block = block.reshape(DEVICES, rows, 128)
        return block[:, :, :rows].swapaxes(0, 1).reshape(rows, width)

    def line(block):
        block = block.reshape(DEVICES, rows, 128)
        return block[:, 0, 2 * rows : 2 * rows + hidden // DEVICES].reshape(-1)

    def stacked(part):
        part = part.reshape(DEVICES, rows, -1, width).swapaxes(1, 2)
        return part.reshape(hidden, width)

    def spread(parts, axis):
        return lax.psum_scatter(jnp.stack(parts), axes, scatter_dimension=axis, tiled=True)

    return (
        spread([wq0, wq1], 1),
        spread([vectors(block_c)[0:2], vectors(block_b)[0:2]], 2),
        spread([wo0, wo1], 1),
        spread([wi0, wi1], 1),
        spread([line(block_b), line(block_a)], 1),
        spread([stacked(wf0), stacked(wf1)], 1),
        spread([vectors(block_b)[2:4], vectors(block_a)[2:4]], 2),
        spread([vectors(block_b)[4:8], vectors(block_a)[4:8]], 2),
    )


def solution(mesh):
    placed = (
        P(("dp", "fsdp"), None),
        P(("dp", "fsdp"), None),
        P(("dp", "fsdp"), None),
        P(None, ("dp", "fsdp"), None),
        P(None, None, ("dp", "fsdp")),
        P(None, ("dp", "fsdp"), None),
        P(None, ("dp", "fsdp"), None),
        P(None, ("dp", "fsdp")),
        P(None, ("dp", "fsdp"), None),
        P(None, None, ("dp", "fsdp")),
        P(None, None, ("dp", "fsdp")),
    )
    return jax.shard_map(
        local,
        mesh=mesh,
        in_specs=placed,
        out_specs=(
            P(("dp", "fsdp"), None),
            P(("dp", "fsdp"), None),
            P(None, ("dp", "fsdp"), None),
            P(None, None, ("dp", "fsdp")),
            P(None, ("dp", "fsdp"), None),
            P(None, ("dp", "fsdp"), None),
            P(None, ("dp", "fsdp")),
            P(None, ("dp", "fsdp"), None),
            P(None, None, ("dp", "fsdp")),
            P(None, None, ("dp", "fsdp")),
        ),
        check_vma=False,
    )
```

```python
from functools import partial

import jax
import jax.numpy as jnp
from jax import lax
from jax.experimental import pallas as pl
from jax.experimental.pallas import tpu as pltpu
from jax.sharding import PartitionSpec as P

HEADS = 4
HD = 64
SEQ = 512
PAIR = 2 * HD
EXTRA = 16
HALF = SEQ // 2
HALVES = (slice(0, HALF), slice(HALF, SEQ))
FAR = -(2.0**100)
FLOOR = -1e20
EPSILON = 1e-12
PIECE = 256
SMALL = 128
GROUPS = (4, 8, 8)
DEVICES = 32
LOW = jnp.bfloat16
F32 = jnp.float32
MEMORY = 2**26


def dot_nn(left, right):
    return lax.dot_general(left, right, (((1,), (0,)), ((), ())), preferred_element_type=F32)


def dot_nt(left, right):
    return lax.dot_general(left, right, (((1,), (1,)), ((), ())), preferred_element_type=F32)


def dot_tn(left, right):
    return lax.dot_general(left, right, (((0,), (0,)), ((), ())), preferred_element_type=F32)


def pieces(total, size=PIECE):
    return [pl.ds(start, size) for start in range(0, total, size)]


def three_parts(values):
    first = values.astype(LOW).astype(F32)
    rest = values - first
    second = rest.astype(LOW).astype(F32)
    return first, second, rest - second


BELL = -0.5 / 0.6931471805599453


def gelu_parts(u):
    cumulative = 0.5 + 0.5 * lax.erf(u * 0.7071067811865476)
    slope = cumulative + (u * 0.3989422804014327) * jnp.exp2(u * u * BELL)
    return u * cumulative, slope


def inverse_of(values):
    guess = pl.reciprocal(values, approx=True)
    return guess * (2.0 - values * guess)


def longest_start(lengths_ref, row):
    begin, found = jnp.int32(0), jnp.int32(0)
    for entry in range(lengths_ref.shape[1]):
        size = lengths_ref[row, entry]
        found = jnp.where(size == HALF, begin, found)
        begin = begin + size
    return found


def segments(lengths_ref, row):
    places = lax.broadcasted_iota(jnp.int32, (1, SEQ), 1) + longest_start(lengths_ref, row)
    places = places & (SEQ - 1)
    bound = jnp.int32(0)
    segment = jnp.zeros((1, SEQ), jnp.int32)
    last = lengths_ref.shape[1] - 1
    for entry in range(last):
        bound = bound + lengths_ref[row, entry]
        segment = segment + (places >= bound).astype(jnp.int32)
    return segment, last


def head_rows(head):
    return slice(head * HD, (head + 1) * HD)


def attention_forward(row, lengths_ref, x, wt_ref, bias_ref, qa_ref, ka_ref, va_ref, ob_ref, lse_ref, s_ref, p_ref):
    width = HEADS * HD
    segment, last = segments(lengths_ref, row)
    pad = (segment == last).astype(F32)
    line = lax.broadcasted_iota(jnp.int32, (EXTRA, SEQ), 0)
    aug_q = jnp.where(line == segment, 1.0, 0.0).astype(LOW)
    seen = (line == segment) & (segment != last)
    aug_k = jnp.where(seen | (line > last), 0.0, FAR).astype(LOW)
    aug_v = jnp.where(line == 0, 1.0, 0.0).astype(LOW)
    rest = jnp.zeros((PAIR - HD - EXTRA, SEQ), LOW)
    for head in range(HEADS):
        qa_ref[head, HD : HD + EXTRA] = aug_q
        ka_ref[head, HD : HD + EXTRA] = aug_k
        va_ref[head, HD : HD + EXTRA] = aug_v
        qa_ref[head, HD + EXTRA : PAIR] = rest
        ka_ref[head, HD + EXTRA : PAIR] = rest
    for block, ref in enumerate((qa_ref, ka_ref, va_ref)):
        lines = slice(block * width, (block + 1) * width)
        bias = bias_ref[lines]
        value = dot_nt(wt_ref[lines], x) + jnp.concatenate([bias] * (SEQ // 128), 1)
        if block == 0:
            value = value * HD**-0.5
        value = value.astype(LOW)
        for head in range(HEADS):
            ref[head, 0:HD] = value[head_rows(head)]
        yield

    def scores(head):
        for half in HALVES:
            s_ref[head % 2, half] = dot_tn(ka_ref[head, :, half], qa_ref[head, :, half])

    def softmax(head):
        tops = []
        for half in HALVES:
            tops.append(jnp.maximum(jnp.max(s_ref[head % 2, half], 0, keepdims=True), FLOOR))
            p_ref[head % 2, half] = jnp.exp(s_ref[head % 2, half] - tops[-1]).astype(LOW)
        return tops

    scores(0)
    yield
    for head in range(HEADS):
        if head + 1 < HEADS:
            scores(head + 1)
            yield
        tops = softmax(head)
        yield
        for half, top in zip(HALVES, tops):
            out = dot_nn(va_ref[head, :, half], p_ref[head % 2, half])
            alone = pad[:, half]
            total = out[HD : HD + 1] + alone
            lse_ref[head : head + 1, half] = jnp.where(alone > 0, 0.0, top + jnp.log(total))
            own = alone * va_ref[head, 0:HD, half].astype(F32)
            ob_ref[head_rows(head), half] = (out[0:HD] * inverse_of(total) + own).astype(LOW)
        yield


def normal(values):
    centred = values - jnp.mean(values, -1, keepdims=True)
    inverse = lax.rsqrt(jnp.mean(centred * centred, -1, keepdims=True) + EPSILON)
    return centred * inverse, inverse


def normal_back(cotangent, unit, inverse, gains):
    scaled = cotangent * gains
    return inverse * (
        scaled
        - jnp.mean(scaled, -1, keepdims=True)
        - unit * jnp.mean(scaled * unit, -1, keepdims=True)
    )


def dense_forward(x_ref, ob_ref, wo_ref, wi_ref, wf_ref, small_ref, bi_ref, n1_ref, n2_ref, inv_ref, yb_ref, gb_ref, gp_ref, z_ref, work_ref, u_ref):
    small = lambda index: small_ref[pl.ds(index, 1)]
    work_ref[...] = dot_tn(ob_ref[...], wo_ref[...])
    yield
    for place in pieces(SEQ):
        unit, inverse = normal(x_ref[place].astype(F32) + work_ref[place] + small(4))
        n1_ref[place] = unit
        inv_ref[place, pl.ds(0, HD)] = jnp.broadcast_to(inverse, (PIECE, HD))
        y = unit * small(2) + small(5)
        yb_ref[place] = y.astype(LOW)
        work_ref[place] = y + small(6)
        yield
    columns = 256
    count = wi_ref.shape[1] // columns

    def into(step):
        u_ref[step % 2] = dot_nn(yb_ref[...], wi_ref[:, pl.ds(step * columns, columns)])

    into(0)
    yield
    for step in range(count):
        if step + 1 < count:
            into(step + 1)
            yield
        lanes = pl.ds(step * columns, columns)
        for place in pieces(SEQ, SMALL):
            g, slope = gelu_parts(u_ref[step % 2, place] + bi_ref[:, lanes])
            gb_ref[place, lanes] = g.astype(LOW)
            gp_ref[place, lanes] = slope.astype(LOW)
            yield
    work_ref[...] += dot_nn(gb_ref[...], wf_ref[...])
    yield
    for place in pieces(SEQ):
        unit, inverse = normal(work_ref[place])
        n2_ref[place] = unit
        inv_ref[place, pl.ds(HD, HD)] = jnp.broadcast_to(inverse, (PIECE, HD))
        z_ref[place] = (unit * small(3) + small(7)).astype(z_ref.dtype)
        yield


def fold(values):
    return jnp.sum(values.reshape(-1, 8, values.shape[-1]), 0)


def dense_backward(dz_ref, n1_ref, n2_ref, inv_ref, yb_ref, gb_ref, gp_ref, ob_ref, wo_ref, wi_ref, wf_ref, small_ref, dr_ref, dob_ref, gwo_ref, gwi_ref, gwf_ref, gsmall_ref, gbi_ref, low_ref, u_ref, du_ref, turned_ref):
    small = lambda index: small_ref[pl.ds(index, 1)]
    for place in pieces(SEQ):
        dz = dz_ref[place].astype(F32)
        unit = n2_ref[place]
        gsmall_ref[3] += fold(dz * unit)
        gsmall_ref[7] += fold(dz)
        dr = normal_back(dz, unit, inv_ref[place, pl.ds(HD, 1)], small(3))
        dr_ref[place] = dr
        df = dr.astype(LOW)
        low_ref[place] = df
        gsmall_ref[6] += fold(df.astype(F32))
        yield
    columns = 256
    count = wi_ref.shape[1] // columns

    def back(step):
        u_ref[step % 2] = dot_nt(low_ref[...], wf_ref[pl.ds(step * columns, columns)])

    back(0)
    turned_ref[0, 0 : low_ref.shape[1]] = low_ref[...].T
    width = low_ref.shape[1]
    turned_ref[1, 0:width] = yb_ref[...].T
    turned_ref[1, width:] = jnp.ones((EXTRA, SEQ), LOW)
    yield
    for step in range(count):
        if step + 1 < count:
            back(step + 1)
            yield
        lanes = pl.ds(step * columns, columns)
        gwf_ref[:, lanes] += dot_nn(turned_ref[0, 0:width], gb_ref[:, lanes])
        yield
        for place in pieces(SEQ, SMALL):
            du = (u_ref[step % 2, place] * gp_ref[place, lanes].astype(F32)).astype(LOW)
            du_ref[place, lanes] = du
        yield
        product = dot_nn(turned_ref[1], du_ref[:, lanes])
        gwi_ref[:, lanes] += product[0:width]
        gbi_ref[:, lanes] += product[width : width + 8]
        yield
    u_ref[0] = dot_nt(du_ref[...], wi_ref[...])
    yield
    for place in pieces(SEQ):
        dy = dr_ref[place] + u_ref[0, place]
        unit = n1_ref[place]
        gsmall_ref[2] += fold(dy * unit)
        gsmall_ref[5] += fold(dy)
        dr = normal_back(dy, unit, inv_ref[place, pl.ds(0, 1)], small(2))
        dr_ref[place] = dr
        da = dr.astype(LOW)
        low_ref[place] = da
        gsmall_ref[4] += fold(da.astype(F32))
        yield
    gwo_ref[...] += dot_nn(ob_ref[...], low_ref[...])
    dob_ref[...] = dot_nt(wo_ref[...], low_ref[...]).astype(LOW)
    yield


def attention_backward(row, lengths_ref, x, do_ref, ob_ref, qa_ref, ka_ref, va_ref, lse_ref, dqkv_ref, gwq_ref, gbias_ref, p_ref, ds_ref, s_ref):
    width = HEADS * HD
    segment, last = segments(lengths_ref, row)
    pad = (segment == last).astype(F32)

    def scores(head):
        for half in HALVES:
            s_ref[0, head % 2, half] = dot_tn(ka_ref[head, :, half], qa_ref[head, :, half])
            s_ref[1, head % 2, half] = dot_tn(
                va_ref[head, 0:HD, half], do_ref[head_rows(head), half]
            )

    def weigh(head):
        product = do_ref[head_rows(head)].astype(F32) * ob_ref[head_rows(head)].astype(F32)
        centre = jnp.sum(product, 0, keepdims=True)
        for half in HALVES:
            p = jnp.exp(s_ref[0, head % 2, half] - lse_ref[head : head + 1, half])
            p_ref[head % 2, half] = p.astype(LOW)
            ds_ref[head % 2, half] = (p * (s_ref[1, head % 2, half] - centre[:, half])).astype(LOW)

    scores(0)
    yield
    for head in range(HEADS):
        if head + 1 < HEADS:
            scores(head + 1)
            yield
        weigh(head)
        yield
        for half in HALVES:
            ds, do = ds_ref[head % 2, half], do_ref[head_rows(head), half]
            dq = dot_nn(ka_ref[head, 0:HD, half], ds) * HD**-0.5
            dk = dot_nt(qa_ref[head, 0:HD, half], ds)
            dv = dot_nt(do, p_ref[head % 2, half]) + pad[:, half] * do.astype(F32)
            for block, value in enumerate((dq, dk, dv)):
                at = block * width + head * HD
                dqkv_ref[at : at + HD, half] = value.astype(LOW)
        yield
    for index, block in enumerate((0, 2)):
        value = dqkv_ref[block * width : (block + 1) * width].astype(F32)
        parts = [value[:, at : at + 128] for at in range(0, SEQ, 128)]
        gbias_ref[index] += (parts[0] + parts[1]) + (parts[2] + parts[3])
    gwq_ref[...] += dot_nn(dqkv_ref[...], x)
    yield


def unpack_matrix(raw_ref, at, into_ref):
    width = into_ref.shape[0]
    for start in range(0, into_ref.shape[1], width):
        block = raw_ref[:, :, pl.ds(at + start, width)].astype(F32)
        block = block.reshape(GROUPS + (width,)).swapaxes(0, 1).reshape(width, width)
        into_ref[:, pl.ds(start, width)] = block.astype(LOW)


def unpack_stacked(raw_ref, at, into_ref):
    width = into_ref.shape[1]
    count = into_ref.shape[0] // width
    blocks = [
        raw_ref[:, :, pl.ds(at + step * width, width)].astype(F32).reshape(GROUPS + (width,))
        for step in range(count)
    ]
    outer, inner, rows = GROUPS
    for place in range(inner):
        part = jnp.stack([jnp.stack([block[f, place] for block in blocks]) for f in range(outer)])
        size = outer * count * rows
        into_ref[pl.ds(place * size, size)] = part.reshape(size, width).astype(LOW)


def counter(shape, axis):
    return lax.broadcasted_iota(jnp.int32, shape, axis)


def split_by(values, size):
    return lax.shift_right_logical(values, size.bit_length() - 1), values & (size - 1)


def sources(rows):
    outer, inner, height = GROUPS
    group, within = split_by(counter((rows, 1), 0), height)
    far, near = split_by(group, inner)
    return near * outer + far, within


def unpack_vectors(raw_ref, at, layer):
    outer, inner, rows = GROUPS
    total = outer * inner * rows
    raw = raw_ref[:, :, pl.ds(at, 128)].reshape(total, 128)
    owner, place = split_by(counter((1, total), 1), rows)
    pick = jnp.where(counter((128, 1), 0) == rows * layer + place, 1.0, 0.0).astype(LOW)
    device, unused = sources(total)
    spread = jnp.where(owner == device, dot_nn(raw, pick), 0.0)
    return jnp.sum(spread.reshape(outer * inner, rows, total), 0)


def unpack_hidden(raw_ref, at, layer, hidden):
    outer, inner, rows = GROUPS
    total = outer * inner * rows
    raw = raw_ref[:, :, pl.ds(at, 128)].reshape(total, 128)
    owner, place = split_by(counter((1, hidden), 1), hidden // (outer * inner))
    pick = jnp.where(counter((128, 1), 0) == 2 * rows + place, 1.0, 0.0).astype(LOW)
    device, within = sources(total)
    device = jnp.where(within == layer, device, -1)
    spread = jnp.where(owner == device, dot_nn(raw, pick), 0.0)
    return jnp.sum(spread, 0, keepdims=True)


def pack_matrix(sum_ref, sent_ref, at, turned=False):
    width = sum_ref.shape[1 if turned else 0]
    outer, inner, rows = GROUPS
    for start in range(0, sum_ref.shape[0 if turned else 1], width):
        near = pl.ds(start, width)
        block = sum_ref[near].T if turned else sum_ref[:, near]
        block = block.reshape(inner, outer, rows, width)
        block = block.swapaxes(0, 1).reshape(outer, inner * rows, width)
        sent_ref[:, :, pl.ds(at + start, width)] = block.astype(LOW)


def pack_stacked(sum_ref, sent_ref, at):
    width = sum_ref.shape[0]
    outer, inner, rows = GROUPS
    count = sum_ref.shape[1] // width
    near = inner // count
    for step in range(count):
        block = sum_ref[:, pl.ds(step * width, width)].T
        block = block.reshape(near, outer, count, rows, width)
        for part in range(count):
            piece = jnp.stack([block[:, f, part] for f in range(outer)])
            piece = piece.reshape(outer, near * rows, width)
            sent_ref[:, pl.ds(step * near * rows, near * rows), pl.ds(at + part * width, width)] = (
                piece.astype(LOW)
            )


def pack_vectors(block, line, sent_ref, at):
    outer, inner, rows = GROUPS
    total = outer * inner * rows
    device, within = sources(total)
    owner, unused = split_by(counter((1, total), 1), rows)
    spread = jnp.broadcast_to(block[None], (outer * inner, rows, total)).reshape(total, total)
    spread = jnp.where(owner == device, spread, 0.0).astype(LOW)
    unused, place = split_by(counter((total, 1), 0), rows)
    found = dot_nn(spread, jnp.where(counter((1, 128), 1) == place, 1.0, 0.0).astype(LOW))
    if line is not None:
        hidden = line.shape[1]
        height = hidden // (outer * inner)
        owner, unused = split_by(counter((1, hidden), 1), height)
        spread = jnp.where(owner == jnp.where(within == 0, device, -1), line, 0.0).astype(LOW)
        unused, place = split_by(counter((hidden, 1), 0), height)
        pick = jnp.where(counter((1, 128), 1) == 2 * rows + place, 1.0, 0.0).astype(LOW)
        found = found + dot_nn(spread, pick)
    sent_ref[:, :, pl.ds(at, 128)] = found.reshape(outer, inner * rows, 128).astype(LOW)


def bias_rows(gbias_ref):
    width = gbias_ref.shape[1]
    parts = [jnp.sum(gbias_ref[index].T, 0, keepdims=True) for index in range(2)]
    return jnp.concatenate(parts + [jnp.zeros((6, width), F32)], 0)


def pack_dense(gwo_ref, gwi_ref, gwf_ref, gsmall_ref, gbi_ref, block, sent_ref, at):
    width, hidden = gwi_ref.shape
    pack_matrix(gwo_ref, sent_ref, at)
    pack_matrix(gwi_ref, sent_ref, at + width)
    pack_stacked(gwf_ref, sent_ref, at + width + hidden)
    block = jnp.sum(gsmall_ref[...], 1) + block
    pack_vectors(block, gbi_ref[0:1], sent_ref, at + width + 2 * hidden)


def shape_of(array):
    return jax.ShapeDtypeStruct(array.shape, array.dtype)


def by_row(shape, group):
    if len(shape) == 2:
        return pl.BlockSpec((group * SEQ, shape[1]), lambda step: (step, 0))
    return pl.BlockSpec((group,) + tuple(shape[1:]), lambda step: (step,) + (0,) * (len(shape) - 1))


def one_row(ref, member):
    if len(ref.shape) == 2:
        return ref.at[pl.ds(member * SEQ, SEQ)]
    return ref.at[member]


def alternate(runs):
    running = []
    waiting = list(runs)
    while running or waiting:
        if waiting:
            running.append(waiting.pop(0))
        for run in list(running):
            try:
                next(run)
            except StopIteration:
                running.remove(run)


def whole(shape):
    return pl.BlockSpec(tuple(shape), lambda row: (0,) * len(shape))


def run_rows(
    body, lengths, rowwise, fixed, row_outs, sent, shared, private, cost, setup, finish, after=(),
    scalars=(), group=1
):
    count = lengths.shape[0]
    group = group if count % group == 0 else 1
    cuts = [len(scalars), len(rowwise), len(fixed), len(after), len(row_outs), len(sent)]
    cuts += [len(shared)] + [len(private)] * group

    def kernel(lengths_ref, *refs):
        step = pl.program_id(0)
        groups = []
        at = 0
        for cut in cuts:
            groups.append(refs[at : at + cut])
            at += cut
        numbers, rows_in, fixed_in, unused, rows_out, sent_out, work = groups[:7]

        @pl.when(step == 0)
        def _():
            setup(numbers, fixed_in, sent_out, work)

        alternate(
            body(
                step * group + member,
                lengths_ref,
                [one_row(ref, member) for ref in rows_in],
                [one_row(ref, member) for ref in rows_out],
                work,
                groups[7 + member],
            )
            for member in range(group)
        )

        if finish:

            @pl.when(step == count // group - 1)
            def _():
                finish(numbers, work, sent_out)

    return pl.pallas_call(
        kernel,
        grid=(count // group,),
        in_specs=[pl.BlockSpec(memory_space=pltpu.SMEM)] * (1 + len(scalars))
        + [by_row(array.shape, group) for array in rowwise]
        + [whole(array.shape) for array in fixed]
        + [pl.BlockSpec(memory_space=pl.ANY) for array in after],
        out_specs=[by_row(part.shape, group) for part in row_outs]
        + [whole(part.shape) for part in sent],
        out_shape=list(row_outs) + list(sent),
        scratch_shapes=list(shared) + list(private) * group,
        compiler_params=pltpu.CompilerParams(
            dimension_semantics=("arbitrary",), vmem_limit_bytes=MEMORY
        ),
        cost_estimate=pl.CostEstimate(flops=cost, bytes_accessed=8 * 2**20, transcendentals=0),
    )(lengths, *scalars, *rowwise, *fixed, *after)


def struct(shape, dtype):
    return jax.ShapeDtypeStruct(tuple(shape), dtype)


FORWARD_SCRATCH = lambda: [
    pltpu.VMEM((2, SEQ, HALF), F32),
    pltpu.VMEM((2, SEQ, HALF), LOW),
]
BACKWARD_SCRATCH = lambda: [
    pltpu.VMEM((2, SEQ, HALF), LOW),
    pltpu.VMEM((2, SEQ, HALF), LOW),
    pltpu.VMEM((2, 2, SEQ, HALF), F32),
    pltpu.VMEM((3 * HEADS * HD, SEQ), LOW),
]


def attention_outs(rows, width):
    return [
        struct((rows, HEADS, PAIR, SEQ), LOW),
        struct((rows, HEADS, PAIR, SEQ), LOW),
        struct((rows, HEADS, HD + EXTRA, SEQ), LOW),
        struct((rows, width, SEQ), LOW),
        struct((rows, 8, SEQ), F32),
    ]


def dense_outs(tokens, width, hidden):
    return [
        struct((tokens, width), F32),
        struct((tokens, width), F32),
        struct((tokens, PAIR), F32),
        struct((tokens, width), LOW),
        struct((tokens, hidden), LOW),
        struct((tokens, hidden), LOW),
    ]


def vmem(shape, dtype):
    return pltpu.VMEM(tuple(shape), dtype)


def attention_weights(width):
    return [vmem((width, 3 * width), LOW), vmem((3 * width, width), LOW), vmem((3 * width, 128), F32)]


def dense_weights(width, hidden):
    return [
        vmem((width, width), LOW),
        vmem((width, hidden), LOW),
        vmem((hidden, width), LOW),
        vmem((8, width), F32),
        vmem((1, hidden), F32),
    ]


def dense_sums(width, hidden):
    return [
        vmem((width, width), F32),
        vmem((width, hidden), F32),
        vmem((width, hidden), F32),
        vmem((8, 8, width), F32),
        vmem((8, hidden), F32),
    ]


def attention_sums(width):
    return [vmem((3 * width, width), F32), vmem((2, width, 128), F32)]


def dense_work(width, hidden):
    return [
        vmem((SEQ, width), LOW),
        vmem((2, SEQ, width), F32),
        vmem((SEQ, hidden), LOW),
        vmem((2, width + EXTRA, SEQ), LOW),
    ]


def set_attention(layer, urgent_ref, raw_ref, at, wq_ref, wt_ref, bias_ref):
    width = wq_ref.shape[0]
    unpack_matrix(raw_ref, at, wq_ref)
    vectors = unpack_vectors(urgent_ref, 3 * width, layer)
    for block, line in enumerate((vectors[0:1], jnp.zeros((1, width), F32), vectors[1:2])):
        lines = pl.ds(block * width, width)
        wt_ref[lines] = wq_ref[:, lines].astype(F32).T.astype(LOW)
        bias_ref[lines] = jnp.broadcast_to(line, (128, width)).T


def set_dense(layer, urgent_ref, raw_ref, at, wo_ref, wi_ref, wf_ref, small_ref, bi_ref):
    width, hidden = wi_ref.shape
    unpack_matrix(raw_ref, at, wo_ref)
    unpack_matrix(raw_ref, at + width, wi_ref)
    unpack_stacked(raw_ref, at + width + hidden, wf_ref)
    small_ref[...] = unpack_vectors(urgent_ref, 3 * width, layer)
    bi_ref[...] = unpack_hidden(urgent_ref, 3 * width, layer, hidden)


def clear(refs):
    for ref in refs:
        ref[...] = jnp.zeros(ref.shape, ref.dtype)


def assemble(place_ref, part_refs, into_ref):
    for step, ref in enumerate(part_refs):
        into_ref[place_ref[0] ^ step] = ref[...]


def raw_block(parts):
    return vmem((len(parts),) + parts[0].shape, LOW)


def turned_back(lengths_ref, row, values):
    return pltpu.roll(values, longest_start(lengths_ref, row), 0).astype(LOW)


def rotate_kernel(lengths, arrays):
    def body(row, lengths_ref, rowwise, outs, work, own):
        back = (SEQ - longest_start(lengths_ref, row)) & (SEQ - 1)
        for source, target in zip(rowwise, outs):
            target[...] = pltpu.roll(source[...].astype(F32), back, 0).astype(LOW)
            yield

    return run_rows(
        body, lengths, list(arrays), [], [struct(array.shape, LOW) for array in arrays], [], [], [],
        10**6, lambda *refs: None, None,
    )


def first_kernel(lengths, x, place, parts):
    rows, (tokens, width) = lengths.shape[0], x.shape

    def setup(numbers, fixed, sent, work):
        assemble(numbers[0], fixed, sent[0])
        set_attention(0, sent[0], sent[0], 0, *work)

    def body(row, lengths_ref, rowwise, outs, work, own):
        return attention_forward(row, lengths_ref, rowwise[0][...], *work[1:3], *outs, *own)

    return run_rows(
        body, lengths, [x], list(parts), attention_outs(rows, width),
        [struct((len(parts),) + parts[0].shape, LOW)],
        attention_weights(width), FORWARD_SCRATCH(), 4 * 10**9, setup, None, (), [place],
    )


def attention_kernel(layer, lengths, x, place, urgent, parts, at):
    rows, (tokens, width) = lengths.shape[0], x.shape

    def setup(numbers, fixed, sent, work):
        assemble(numbers[0], fixed[1:], work[3])
        set_attention(layer, fixed[0], work[3], at, *work[:3])

    def body(row, lengths_ref, rowwise, outs, work, own):
        return attention_forward(
            row, lengths_ref, rowwise[0][...].astype(LOW), *work[1:3], *outs, *own
        )

    return run_rows(
        body, lengths, [x], [urgent] + list(parts), attention_outs(rows, width), [],
        attention_weights(width) + [raw_block(parts)], FORWARD_SCRATCH(),
        4 * 10**9, setup, None, (), [place],
    )


def dense_kernel(layer, lengths, x, ob, place, urgent, parts, at, hidden):
    tokens, width = x.shape

    def setup(numbers, fixed, sent, work):
        assemble(numbers[0], fixed[1:], work[5])
        set_dense(layer, fixed[0], work[5], at, *work[:5])

    def body(row, lengths_ref, rowwise, outs, work, own):
        return dense_forward(*rowwise, *work[:5], *outs, *own)

    return run_rows(
        body, lengths, [x, ob], [urgent] + list(parts),
        dense_outs(tokens, width, hidden) + [struct((tokens, width), F32)], [],
        dense_weights(width, hidden) + [raw_block(parts)],
        [vmem((SEQ, width), F32), vmem((2, SEQ, width), F32)],
        5 * 10**9, setup, None, (), [place],
    )


def turn_kernel(layer, lengths, x, ob, cotangent, place, urgent, parts, at, hidden):
    tokens, width = x.shape
    columns = width + 2 * hidden + 128

    def setup(numbers, fixed, sent, work):
        assemble(numbers[0], fixed[1:], work[11])
        set_dense(layer, fixed[0], work[11], at, *work[:5])
        clear(work[5:10])

    def body(row, lengths_ref, rowwise, outs, work, own):
        x_ref, ob_ref, dz_ref = rowwise
        z_ref, dr_ref, dob_ref = outs
        weights, sums = work[:5], work[5:10]
        kept, work_ref, back = own[:6], own[6], own[7:]
        yield from dense_forward(x_ref, ob_ref, *weights, *kept, z_ref, work_ref, back[1])
        yield from dense_backward(dz_ref, *kept, ob_ref, *weights[:4], dr_ref, dob_ref, *sums, *back)

    def finish(numbers, work, sent):
        pack_dense(*work[5:10], 0.0, work[10], 0)
        hand_out(numbers[0], work[10], sent)

    kept = [vmem((SEQ,) + part.shape[1:], part.dtype) for part in dense_outs(tokens, width, hidden)]
    return run_rows(
        body, lengths, [x, ob, cotangent], [urgent] + list(parts),
        [struct((tokens, width), LOW), struct((tokens, width), F32), struct((tokens // SEQ, width, SEQ), LOW)],
        [struct((64, columns), LOW)] * 4,
        dense_weights(width, hidden) + dense_sums(width, hidden)
        + [vmem((4, 64, columns), LOW), raw_block(parts)],
        kept + [vmem((SEQ, width), F32)] + dense_work(width, hidden),
        10**10, setup, finish, (), [place], 2,
    )


def hand_out(place_ref, packed_ref, sent):
    for step, ref in enumerate(sent):
        ref[...] = packed_ref[place_ref[0] ^ step]


def middle_kernel(lengths, upper, lower, place, urgent, parts, hidden, after):
    tokens, width = upper[0].shape
    columns = 4 * width + 2 * hidden + 128

    def setup(numbers, fixed, sent, work):
        assemble(numbers[0], fixed[1:], work[16])
        set_attention(1, fixed[0], work[16], 0, *work[:3])
        set_dense(0, fixed[0], work[16], 3 * width, *work[3:8])
        clear(work[8:15])

    def body(row, lengths_ref, rowwise, outs, work, own):
        up, low = rowwise[:8], rowwise[8:]
        dx_ref = own[0]
        yield from attention_backward(
            row, lengths_ref, up[0][...].astype(LOW), *up[1:7], own[-1], *work[8:10], *own[5:-1]
        )
        dx_ref[...] = up[7][...] + dot_tn(own[-1][...], work[1][...])
        yield
        yield from dense_backward(dx_ref, *low, *work[3:7], *outs, *work[10:15], *own[1:5])

    def finish(numbers, work, sent):
        pack_matrix(work[8], work[15], 0, True)
        pack_dense(*work[10:15], bias_rows(work[9]), work[15], 3 * width)
        hand_out(numbers[0], work[15], sent)

    return run_rows(
        body, lengths, list(upper) + list(lower), [urgent] + list(parts),
        [struct((tokens, width), F32), struct((tokens // SEQ, width, SEQ), LOW)],
        [struct((64, columns), LOW)] * 4,
        attention_weights(width) + dense_weights(width, hidden)
        + attention_sums(width) + dense_sums(width, hidden)
        + [vmem((4, 64, columns), LOW), raw_block(parts)],
        [vmem((SEQ, width), F32)] + dense_work(width, hidden) + BACKWARD_SCRATCH(),
        15 * 10**9, setup, finish, after, [place], 2,
    )


def last_kernel(lengths, upper, after, place):
    tokens, width = upper[0].shape

    def setup(numbers, fixed, sent, work):
        clear(work[:2])

    def body(row, lengths_ref, rowwise, outs, work, own):
        return attention_backward(
            row, lengths_ref, rowwise[0][...], *rowwise[1:], outs[0], *work[:2], *own
        )

    def finish(numbers, work, sent):
        pack_matrix(work[0], work[2], 0, True)
        pack_vectors(bias_rows(work[1]), None, work[2], 3 * width)
        hand_out(numbers[0], work[2], sent)

    return run_rows(
        body, lengths, list(upper), [], [struct((tokens // SEQ, 3 * width, SEQ), LOW)],
        [struct((64, 3 * width + 128), LOW)] * 4,
        attention_sums(width) + [vmem((4, 64, 3 * width + 128), LOW)],
        BACKWARD_SCRATCH()[:-1], 8 * 10**9, setup, finish, after, [place], 2,
    )


def outward_kernel(lengths, z, after):
    def body(row, lengths_ref, rowwise, outs, work, own):
        outs[0][...] = turned_back(lengths_ref, row, rowwise[0][...].astype(F32))
        yield

    (found,) = run_rows(
        body, lengths, [z], [], [struct(z.shape, LOW)], [], [], [], 3 * 10**9,
        lambda *refs: None, None, after,
    )
    return found


def inward_kernel(lengths, dqkv, dr, urgent, after):
    tokens, width = dr.shape

    def setup(numbers, fixed, sent, work):
        set_attention(0, fixed[0], fixed[0], 0, *work)

    def body(row, lengths_ref, rowwise, outs, work, own):
        dqkv_ref, dr_ref = rowwise
        dx = dr_ref[...] + dot_tn(dqkv_ref[...], work[1][...])
        outs[0][...] = turned_back(lengths_ref, row, dx)
        yield

    (found,) = run_rows(
        body, lengths, [dqkv, dr], [urgent], [struct((tokens, width), LOW)], [],
        attention_weights(width), [], 10**10, setup, None, after,
    )
    return found


def hold(array, after):
    def kernel(*refs):
        pass

    anywhere = pl.BlockSpec(memory_space=pl.ANY)
    return pl.pallas_call(
        kernel,
        in_specs=[anywhere] * (1 + len(after)),
        out_specs=anywhere,
        out_shape=shape_of(array),
        input_output_aliases={0: 0},
    )(array, *after)


def pack_parameters(
    attn_weight, attn_bias, out_weight, ffn_in, ffn_in_bias, ffn_out, norm_gain, shifts
):
    depth, rows, width = out_weight.shape
    copies = GROUPS[1]
    hidden = ffn_in.shape[2]
    dense = width + 2 * hidden
    height = ffn_in_bias.shape[1]

    def kernel(wq_ref, ab_ref, wo_ref, wi_ref, bi_ref, wf_ref, gain_ref, shift_ref, first_ref, rest_ref, small_ref):
        def put(ref, block, at):
            block = jnp.broadcast_to(block.astype(F32)[None], (copies,) + block.shape)
            block = block.reshape(copies * block.shape[1], block.shape[2])
            ref[:, pl.ds(at, block.shape[1])] = block.astype(LOW)

        small_ref[...] = jnp.zeros(small_ref.shape, F32)
        for layer in range(depth):
            lanes = pl.ds(rows * layer, rows)
            small_ref[0:2, lanes] = ab_ref[layer].astype(F32)
            small_ref[2:4, lanes] = gain_ref[layer].astype(F32)
            small_ref[4:8, lanes] = shift_ref[layer].astype(F32)
        small_ref[0:depth, pl.ds(2 * rows, height)] = bi_ref[...].astype(F32)
        put(first_ref, wq_ref[0], 0)
        put(first_ref, small_ref[...], 3 * width)
        put(first_ref, wq_ref[1], 3 * width + 128)
        for layer, ref, at in ((0, first_ref, 6 * width + 128), (1, rest_ref, 0)):
            put(ref, wo_ref[layer], at)
            put(ref, wi_ref[layer], at + width)
            at += width + hidden
            down = wf_ref[layer].astype(F32)
            for step in range(hidden // width):
                put(ref, down[step * rows : (step + 1) * rows], at)
                at += width

    return pl.pallas_call(
        kernel,
        in_specs=[pl.BlockSpec(memory_space=pltpu.VMEM)] * 8,
        out_shape=[
            struct((copies * rows, 6 * width + 128 + dense), LOW),
            struct((copies * rows, dense), LOW),
        ],
        scratch_shapes=[vmem((rows, 128), F32)],
        compiler_params=pltpu.CompilerParams(vmem_limit_bytes=MEMORY),
    )(attn_weight, attn_bias, out_weight, ffn_in, ffn_in_bias, ffn_out, norm_gain, shifts)


def add_parts(place, parts, halves, after=()):
    lanes = parts[0].shape[1]
    count = len(parts)
    many, rows = GROUPS[1:]
    outs = 2 if halves else 1

    def kernel(place_ref, *refs):
        out_refs, sum_ref = refs[count + len(after) : -1], refs[-1]
        bit = place_ref[0] & 1
        for start in range(0, lanes, 128):
            near = pl.ds(start, 128)
            total = refs[0][:, near].astype(F32)
            for ref in refs[1:count]:
                total = total + ref[:, near].astype(F32)
            if halves:
                sum_ref[:, :, near] = total.reshape(many, rows, 128)
            else:
                out_refs[0][:, near] = total.astype(LOW)
        for side, ref in enumerate(out_refs if halves else ()):
            for start in range(0, lanes, 128):
                near = pl.ds(start, 128)
                block = [sum_ref[2 * step + (bit ^ side), :, near] for step in range(many // 2)]
                ref[:, near] = jnp.concatenate(block, 0).astype(LOW)

    return pl.pallas_call(
        kernel,
        in_specs=[pl.BlockSpec(memory_space=pltpu.SMEM)]
        + [pl.BlockSpec(memory_space=pltpu.VMEM)] * count
        + [pl.BlockSpec(memory_space=pl.ANY)] * len(after),
        out_shape=[struct((many * rows // outs, lanes), LOW)] * outs,
        scratch_shapes=[vmem((many, rows, lanes), F32)],
        compiler_params=pltpu.CompilerParams(vmem_limit_bytes=MEMORY),
    )(place, *parts, *after)


def add_halves(place, pairs, after=()):
    many, rows = GROUPS[1] // 2, GROUPS[2]
    widths = [pair[0].shape[1] for pair in pairs]
    lanes = sum(widths)

    def kernel(place_ref, *refs):
        out_refs, sum_ref = refs[2 * len(pairs) + len(after) : -1], refs[-1]
        at = 0
        for index, size in enumerate(widths):
            for start in range(0, size, 128):
                near = pl.ds(start, 128)
                total = refs[2 * index][:, near].astype(F32) + refs[2 * index + 1][:, near].astype(F32)
                sum_ref[:, :, pl.ds(at + start, 128)] = total.reshape(many, rows, 128)
            at += size
        far = lax.shift_right_logical(place_ref[0], 1)
        for step, ref in enumerate(out_refs):
            ref[...] = sum_ref[far ^ step].astype(LOW)

    return pl.pallas_call(
        kernel,
        in_specs=[pl.BlockSpec(memory_space=pltpu.SMEM)]
        + [pl.BlockSpec(memory_space=pltpu.VMEM)] * (2 * len(pairs))
        + [pl.BlockSpec(memory_space=pl.ANY)] * len(after),
        out_shape=[struct((rows, lanes), LOW)] * many,
        scratch_shapes=[vmem((many, rows, lanes), F32)],
        compiler_params=pltpu.CompilerParams(vmem_limit_bytes=MEMORY),
    )(place, *(part for pair in pairs for part in pair), *after)


def write_gradients(found, depth, width, hidden, after):
    rows = GROUPS[2]
    height = hidden // DEVICES
    dense = width + 2 * hidden

    def kernel(*refs):
        found_refs, refs = refs[: len(found)], refs[len(found) + len(after) :]
        gwq_ref, gab_ref, gwo_ref, gwi_ref, gbi_ref, gwf_ref, gain_ref, shift_ref = refs

        def total(at, columns):
            value = found_refs[0][:, pl.ds(at, columns)].astype(F32)
            for ref in found_refs[1:]:
                value = value + ref[:, pl.ds(at, columns)].astype(F32)
            return value

        first, second = dense + 128, 2 * dense + 3 * width + 256
        blocks = [total(at, 128) for at in (dense, first + 3 * width + dense, second + 3 * width)]
        for layer, at, block in ((0, second, blocks[2]), (1, first, blocks[1])):
            gwq_ref[layer] = total(at, 3 * width)
            gab_ref[layer] = block[0:2, 0:rows]
        for layer, at, block in ((0, first + 3 * width, blocks[1]), (1, 0, blocks[0])):
            gwo_ref[layer] = total(at, width)
            gwi_ref[layer] = total(at + width, hidden)
            for step in range(hidden // width):
                gwf_ref[layer, pl.ds(step * rows, rows)] = total(
                    at + width + hidden + step * width, width
                )
            gain_ref[layer] = block[2:4, 0:rows]
            shift_ref[layer] = block[4:8, 0:rows]
            gbi_ref[pl.ds(layer, 1)] = pltpu.roll(block, 128 - 2 * rows, 1)[0:1, 0:height]

    outs = [
        struct((depth, rows, 3 * width), F32),
        struct((depth, 2, rows), F32),
        struct((depth, rows, width), F32),
        struct((depth, rows, hidden), F32),
        struct((depth, height), F32),
        struct((depth, height, width), F32),
        struct((depth, 2, rows), F32),
        struct((depth, 4, rows), F32),
    ]
    return pl.pallas_call(
        kernel,
        in_specs=[pl.BlockSpec(memory_space=pltpu.VMEM)] * len(found)
        + [pl.BlockSpec(memory_space=pl.ANY)] * len(after),
        out_shape=outs,
        compiler_params=pltpu.CompilerParams(vmem_limit_bytes=MEMORY),
    )(*found, *after)


def exchange(parts, axis):
    return lax.all_to_all(parts, axis, 0, 0, tiled=True)


def swap(part, axis, step):
    size = lax.axis_size(axis)
    return lax.ppermute(part, axis, [(source, source ^ step) for source in range(size)])


def local(
    hidden_in,
    lengths,
    grad_out,
    attn_weight,
    attn_bias,
    out_weight,
    ffn_in,
    ffn_in_bias,
    ffn_out,
    norm_gain,
    shifts,
):
    depth, rows, width = out_weight.shape
    hidden = ffn_in.shape[2]
    first, second = lax.axis_size("dp"), lax.axis_size("fsdp")
    fits = (second, first, rows) == GROUPS
    urgent_size = 3 * width + 128
    if fits:
        early, later = pack_parameters(
            attn_weight, attn_bias, out_weight, ffn_in, ffn_in_bias, ffn_out, norm_gain, shifts
        )
        across = lax.axis_index("dp").astype(jnp.int32).reshape(1)
        place = lax.axis_index("fsdp").astype(jnp.int32).reshape(1)
        partners = range(1, second)
        x0, dz1 = rotate_kernel(lengths, (hidden_in, grad_out))
        early = hold(exchange(early, "dp"), (x0,))
        urgent = early[:, :urgent_size]
        urgent = [urgent] + [swap(urgent, "fsdp", step) for step in partners]
        raw0 = early[:, urgent_size:]
        raw0 = [raw0, swap(raw0, "fsdp", 1), swap(raw0, "fsdp", 2)]
    else:
        urgent, raw0, raw1 = gather_other(
            attn_weight, attn_bias, out_weight, ffn_in, ffn_in_bias, ffn_out, norm_gain, shifts
        )
        urgent, raw0, raw1 = ([part[step] for step in range(4)] for part in (urgent, raw0, raw1))
        place = jnp.zeros((1,), jnp.int32)
        x0, dz1 = rotate_kernel(lengths, (hidden_in, grad_out))

    qa0, ka0, va0, ob0, lse0, urgent = first_kernel(lengths, x0, place, urgent)
    if fits:
        raw0[2] = hold(raw0[2], (ob0,))
        raw0.append(swap(raw0[2], "fsdp", 1))
        later = exchange(hold(later, (ob0,)), "dp")
    n1, n2, inv, yb, gb, gp, z0 = dense_kernel(
        0, lengths, x0, ob0, place, urgent, raw0, 3 * width, hidden
    )
    if fits:
        raw1 = hold(later, (z0,))
        raw1 = [raw1, swap(raw1, "fsdp", 1), swap(raw1, "fsdp", 2)]
    qa1, ka1, va1, ob1, lse1 = attention_kernel(1, lengths, z0, place, urgent, raw0, 0)
    if fits:
        raw1[2] = hold(raw1[2], (ob1,))
        raw1.append(swap(raw1[2], "fsdp", 1))
    z1, dr1, dob1, *sent_a = turn_kernel(
        1, lengths, z0, ob1, dz1, place, urgent, raw1, 0, hidden
    )
    dr0, dob0, *sent_b = middle_kernel(
        lengths,
        (z0, dob1, ob1, qa1, ka1, va1, lse1, dr1),
        (n1, n2, inv, yb, gb, gp, ob0),
        place,
        urgent,
        raw0,
        hidden,
        (sent_a[0],),
    )
    if fits:
        got_a = [sent_a[0]] + [swap(sent_a[step], "fsdp", step) for step in partners]
        keep_a, give_a = add_parts(across, got_a, True, (sent_b[0],))
        got_ax = swap(give_a, "dp", 1)
        ready = (sent_b[0], keep_a)
    else:
        ready = ()
    dqkv, *sent_c = last_kernel(
        lengths, (x0, dob0, ob0, qa0, ka0, va0, lse0), ready, place
    )
    if fits:
        got_b = [sent_b[0]] + [swap(sent_b[step], "fsdp", step) for step in partners]
        got_c = [sent_c[0]] + [swap(sent_c[step], "fsdp", step) for step in partners]
        keep_b, give_b = add_parts(across, got_b, True, (got_ax, dqkv))
        keep_c, give_c = add_parts(across, got_c, True, (keep_b,))
        grad_in = inward_kernel(lengths, dqkv, dr0, urgent, (keep_c,))
        pairs = [(keep_a, got_ax), (keep_b, swap(give_b, "dp", 1)), (keep_c, swap(give_c, "dp", 1))]
        found = add_halves(across, pairs, (grad_in,))
        hidden_out = outward_kernel(lengths, z1, (found[0],))
        found = [found[0]] + [swap(found[step], "dp", 2 * step) for step in range(1, first // 2)]
        grads = write_gradients(found, depth, width, hidden, (hidden_out,))
    else:
        grad_in = inward_kernel(lengths, dqkv, dr0, urgent, ())
        hidden_out = outward_kernel(lengths, z1, ())
        grads = scatter_other(
            *(jnp.stack(part) for part in (sent_a, sent_b, sent_c)), rows, width, hidden
        )
    return (hidden_out, grad_in, *grads)


def gather_other(
    attn_weight, attn_bias, out_weight, ffn_in, ffn_in_bias, ffn_out, norm_gain, shifts
):
    axes = ("dp", "fsdp")
    gather = lambda part, axis: lax.all_gather(part, axes, axis=axis, tiled=True)
    depth, unused, width = out_weight.shape
    hidden = ffn_in.shape[2]
    outer, inner, rows = GROUPS
    vectors = gather(jnp.concatenate([attn_bias, norm_gain, shifts], 1), 2)
    line = gather(ffn_in_bias, 1)

    def order(natural):
        return (
            natural.reshape(inner, outer, rows, -1).swapaxes(0, 1).reshape(outer, inner * rows, -1)
        )

    def stacked(part):
        part = part.reshape(DEVICES, -1, rows, width)
        return order(part.swapaxes(1, 2).reshape(width, -1))

    small = vectors.reshape(depth, 8, DEVICES, rows).transpose(2, 1, 0, 3).reshape(width, -1)
    line = line.reshape(depth, DEVICES, -1).swapaxes(0, 1)
    line = jnp.pad(line, ((0, 0), (0, 8 - depth), (0, 0))).reshape(width, -1)
    small = jnp.concatenate([small, line], 1)
    small = jnp.pad(small, ((0, 0), (0, 128 - small.shape[1])))
    wq, wo, wi, wf = (gather(part, 1) for part in (attn_weight, out_weight, ffn_in, ffn_out))
    urgent = jnp.concatenate([order(wq[0]), order(small)], 2)
    raw0 = jnp.concatenate([order(wq[1]), order(wo[0]), order(wi[0]), stacked(wf[0])], 2)
    raw1 = jnp.concatenate([order(wo[1]), order(wi[1]), stacked(wf[1])], 2)
    return urgent, raw0, raw1


def scatter_other(sent_a, sent_b, sent_c, own_rows, width, hidden):
    outer, inner, rows = GROUPS
    axes = ("dp", "fsdp")

    def natural(part):
        return part.reshape(outer, inner, rows, -1).swapaxes(0, 1).reshape(width, -1).astype(F32)

    def cut(part, sizes):
        found, at = [], 0
        for size in sizes:
            found.append(part[:, at : at + size])
            at += size
        return found

    dense = [width, hidden, hidden, 128]
    wq0, block_c = cut(natural(sent_c), [3 * width, 128])
    wq1, wo0, wi0, wf0, block_b = cut(natural(sent_b), [3 * width] + dense)
    wo1, wi1, wf1, block_a = cut(natural(sent_a), dense)

    def vectors(block):
        block = block.reshape(DEVICES, rows, 128)
        return block[:, :, :rows].swapaxes(0, 1).reshape(rows, width)

    def line(block):
        block = block.reshape(DEVICES, rows, 128)
        return block[:, 0, 2 * rows : 2 * rows + hidden // DEVICES].reshape(-1)

    def stacked(part):
        part = part.reshape(DEVICES, rows, -1, width).swapaxes(1, 2)
        return part.reshape(hidden, width)

    def spread(parts, axis):
        return lax.psum_scatter(jnp.stack(parts), axes, scatter_dimension=axis, tiled=True)

    return (
        spread([wq0, wq1], 1),
        spread([vectors(block_c)[0:2], vectors(block_b)[0:2]], 2),
        spread([wo0, wo1], 1),
        spread([wi0, wi1], 1),
        spread([line(block_b), line(block_a)], 1),
        spread([stacked(wf0), stacked(wf1)], 1),
        spread([vectors(block_b)[2:4], vectors(block_a)[2:4]], 2),
        spread([vectors(block_b)[4:8], vectors(block_a)[4:8]], 2),
    )


def solution(mesh):
    placed = (
        P(("dp", "fsdp"), None),
        P(("dp", "fsdp"), None),
        P(("dp", "fsdp"), None),
        P(None, ("dp", "fsdp"), None),
        P(None, None, ("dp", "fsdp")),
        P(None, ("dp", "fsdp"), None),
        P(None, ("dp", "fsdp"), None),
        P(None, ("dp", "fsdp")),
        P(None, ("dp", "fsdp"), None),
        P(None, None, ("dp", "fsdp")),
        P(None, None, ("dp", "fsdp")),
    )
    return jax.shard_map(
        local,
        mesh=mesh,
        in_specs=placed,
        out_specs=(
            P(("dp", "fsdp"), None),
            P(("dp", "fsdp"), None),
            P(None, ("dp", "fsdp"), None),
            P(None, None, ("dp", "fsdp")),
            P(None, ("dp", "fsdp"), None),
            P(None, ("dp", "fsdp"), None),
            P(None, ("dp", "fsdp")),
            P(None, ("dp", "fsdp"), None),
            P(None, None, ("dp", "fsdp")),
            P(None, None, ("dp", "fsdp")),
        ),
        check_vma=False,
    )
```

```python
from functools import partial

import jax
import jax.numpy as jnp
from jax import lax
from jax.experimental import pallas as pl
from jax.experimental.pallas import tpu as pltpu
from jax.sharding import PartitionSpec as P

HEADS = 4
HD = 64
SEQ = 512
PAIR = 2 * HD
EXTRA = 16
HALF = SEQ // 2
HALVES = (slice(0, HALF), slice(HALF, SEQ))
FAR = -(2.0**100)
FLOOR = -1e20
EPSILON = 1e-12
PIECE = 256
SMALL = 128
GROUPS = (4, 8, 8)
DEVICES = 32
LOW = jnp.bfloat16
F32 = jnp.float32
MEMORY = 2**26


def dot_nn(left, right):
    return lax.dot_general(left, right, (((1,), (0,)), ((), ())), preferred_element_type=F32)


def dot_nt(left, right):
    return lax.dot_general(left, right, (((1,), (1,)), ((), ())), preferred_element_type=F32)


def dot_tn(left, right):
    return lax.dot_general(left, right, (((0,), (0,)), ((), ())), preferred_element_type=F32)


def pieces(total, size=PIECE):
    return [pl.ds(start, size) for start in range(0, total, size)]


def three_parts(values):
    first = values.astype(LOW).astype(F32)
    rest = values - first
    second = rest.astype(LOW).astype(F32)
    return first, second, rest - second


BELL = -0.5 / 0.6931471805599453


def gelu_parts(u):
    cumulative = 0.5 + 0.5 * lax.erf(u * 0.7071067811865476)
    slope = cumulative + (u * 0.3989422804014327) * jnp.exp2(u * u * BELL)
    return u * cumulative, slope


def inverse_of(values):
    guess = pl.reciprocal(values, approx=True)
    return guess * (2.0 - values * guess)


def longest_start(lengths_ref, row):
    begin, found = jnp.int32(0), jnp.int32(0)
    for entry in range(lengths_ref.shape[1]):
        size = lengths_ref[row, entry]
        found = jnp.where(size == HALF, begin, found)
        begin = begin + size
    return found


def segments(lengths_ref, row):
    places = lax.broadcasted_iota(jnp.int32, (1, SEQ), 1) + longest_start(lengths_ref, row)
    places = places & (SEQ - 1)
    bound = jnp.int32(0)
    segment = jnp.zeros((1, SEQ), jnp.int32)
    last = lengths_ref.shape[1] - 1
    for entry in range(last):
        bound = bound + lengths_ref[row, entry]
        segment = segment + (places >= bound).astype(jnp.int32)
    return segment, last


def head_rows(head):
    return slice(head * HD, (head + 1) * HD)


def attention_forward(row, lengths_ref, x, wt_ref, bias_ref, qa_ref, ka_ref, va_ref, ob_ref, lse_ref, s_ref, p_ref):
    width = HEADS * HD
    segment, last = segments(lengths_ref, row)
    pad = (segment == last).astype(F32)
    line = lax.broadcasted_iota(jnp.int32, (EXTRA, SEQ), 0)
    aug_q = jnp.where(line == segment, 1.0, 0.0).astype(LOW)
    seen = (line == segment) & (segment != last)
    aug_k = jnp.where(seen | (line > last), 0.0, FAR).astype(LOW)
    aug_v = jnp.where(line == 0, 1.0, 0.0).astype(LOW)
    rest = jnp.zeros((PAIR - HD - EXTRA, SEQ), LOW)
    for head in range(HEADS):
        qa_ref[head, HD : HD + EXTRA] = aug_q
        ka_ref[head, HD : HD + EXTRA] = aug_k
        va_ref[head, HD : HD + EXTRA] = aug_v
        qa_ref[head, HD + EXTRA : PAIR] = rest
        ka_ref[head, HD + EXTRA : PAIR] = rest
    for block, ref in enumerate((qa_ref, ka_ref, va_ref)):
        lines = slice(block * width, (block + 1) * width)
        bias = bias_ref[lines]
        value = dot_nt(wt_ref[lines], x) + jnp.concatenate([bias] * (SEQ // 128), 1)
        if block == 0:
            value = value * HD**-0.5
        value = value.astype(LOW)
        for head in range(HEADS):
            ref[head, 0:HD] = value[head_rows(head)]
        yield

    def scores(head):
        for half in HALVES:
            s_ref[head % 2, half] = dot_tn(ka_ref[head, :, half], qa_ref[head, :, half])

    def softmax(head):
        tops = []
        for half in HALVES:
            tops.append(jnp.maximum(jnp.max(s_ref[head % 2, half], 0, keepdims=True), FLOOR))
            p_ref[head % 2, half] = jnp.exp(s_ref[head % 2, half] - tops[-1]).astype(LOW)
        return tops

    scores(0)
    yield
    for head in range(HEADS):
        if head + 1 < HEADS:
            scores(head + 1)
            yield
        tops = softmax(head)
        yield
        for half, top in zip(HALVES, tops):
            out = dot_nn(va_ref[head, :, half], p_ref[head % 2, half])
            alone = pad[:, half]
            total = out[HD : HD + 1] + alone
            lse_ref[head : head + 1, half] = jnp.where(alone > 0, 0.0, top + jnp.log(total))
            own = alone * va_ref[head, 0:HD, half].astype(F32)
            ob_ref[head_rows(head), half] = (out[0:HD] * inverse_of(total) + own).astype(LOW)
        yield


def normal(values):
    centred = values - jnp.mean(values, -1, keepdims=True)
    inverse = lax.rsqrt(jnp.mean(centred * centred, -1, keepdims=True) + EPSILON)
    return centred * inverse, inverse


def normal_back(cotangent, unit, inverse, gains):
    scaled = cotangent * gains
    return inverse * (
        scaled
        - jnp.mean(scaled, -1, keepdims=True)
        - unit * jnp.mean(scaled * unit, -1, keepdims=True)
    )


def dense_forward(x_ref, ob_ref, wo_ref, wi_ref, wf_ref, small_ref, bi_ref, n1_ref, n2_ref, inv_ref, yb_ref, gb_ref, gp_ref, z_ref, work_ref, u_ref):
    small = lambda index: small_ref[pl.ds(index, 1)]
    work_ref[...] = dot_tn(ob_ref[...], wo_ref[...])
    yield
    for place in pieces(SEQ):
        unit, inverse = normal(x_ref[place].astype(F32) + work_ref[place] + small(4))
        n1_ref[place] = unit
        inv_ref[place, pl.ds(0, HD)] = jnp.broadcast_to(inverse, (PIECE, HD))
        y = unit * small(2) + small(5)
        yb_ref[place] = y.astype(LOW)
        work_ref[place] = y + small(6)
        yield
    columns = 256
    count = wi_ref.shape[1] // columns

    def into(step):
        u_ref[step % 2] = dot_nn(yb_ref[...], wi_ref[:, pl.ds(step * columns, columns)])

    into(0)
    yield
    for step in range(count):
        if step + 1 < count:
            into(step + 1)
            yield
        lanes = pl.ds(step * columns, columns)
        for place in pieces(SEQ, SMALL):
            g, slope = gelu_parts(u_ref[step % 2, place] + bi_ref[:, lanes])
            gb_ref[place, lanes] = g.astype(LOW)
            gp_ref[place, lanes] = slope.astype(LOW)
            yield
    work_ref[...] += dot_nn(gb_ref[...], wf_ref[...])
    yield
    for place in pieces(SEQ):
        unit, inverse = normal(work_ref[place])
        n2_ref[place] = unit
        inv_ref[place, pl.ds(HD, HD)] = jnp.broadcast_to(inverse, (PIECE, HD))
        z_ref[place] = (unit * small(3) + small(7)).astype(z_ref.dtype)
        yield


def fold(values):
    return jnp.sum(values.reshape(-1, 8, values.shape[-1]), 0)


def dense_backward(dz_ref, n1_ref, n2_ref, inv_ref, yb_ref, gb_ref, gp_ref, ob_ref, wo_ref, wi_ref, wf_ref, small_ref, dr_ref, dob_ref, gwo_ref, gwi_ref, gwf_ref, gsmall_ref, gbi_ref, low_ref, u_ref, du_ref, turned_ref):
    small = lambda index: small_ref[pl.ds(index, 1)]
    for place in pieces(SEQ):
        dz = dz_ref[place].astype(F32)
        unit = n2_ref[place]
        gsmall_ref[3] += fold(dz * unit)
        gsmall_ref[7] += fold(dz)
        dr = normal_back(dz, unit, inv_ref[place, pl.ds(HD, 1)], small(3))
        dr_ref[place] = dr
        df = dr.astype(LOW)
        low_ref[place] = df
        gsmall_ref[6] += fold(df.astype(F32))
        yield
    columns = 256
    count = wi_ref.shape[1] // columns

    def back(step):
        u_ref[step % 2] = dot_nt(low_ref[...], wf_ref[pl.ds(step * columns, columns)])

    back(0)
    turned_ref[0, 0 : low_ref.shape[1]] = low_ref[...].T
    width = low_ref.shape[1]
    turned_ref[1, 0:width] = yb_ref[...].T
    turned_ref[1, width:] = jnp.ones((EXTRA, SEQ), LOW)
    yield
    for step in range(count):
        if step + 1 < count:
            back(step + 1)
            yield
        lanes = pl.ds(step * columns, columns)
        gwf_ref[:, lanes] += dot_nn(turned_ref[0, 0:width], gb_ref[:, lanes])
        yield
        for place in pieces(SEQ, SMALL):
            du = (u_ref[step % 2, place] * gp_ref[place, lanes].astype(F32)).astype(LOW)
            du_ref[place, lanes] = du
        yield
        product = dot_nn(turned_ref[1], du_ref[:, lanes])
        gwi_ref[:, lanes] += product[0:width]
        gbi_ref[:, lanes] += product[width : width + 8]
        yield
    u_ref[0] = dot_nt(du_ref[...], wi_ref[...])
    yield
    for place in pieces(SEQ):
        dy = dr_ref[place] + u_ref[0, place]
        unit = n1_ref[place]
        gsmall_ref[2] += fold(dy * unit)
        gsmall_ref[5] += fold(dy)
        dr = normal_back(dy, unit, inv_ref[place, pl.ds(0, 1)], small(2))
        dr_ref[place] = dr
        da = dr.astype(LOW)
        low_ref[place] = da
        gsmall_ref[4] += fold(da.astype(F32))
        yield
    gwo_ref[...] += dot_nn(ob_ref[...], low_ref[...])
    dob_ref[...] = dot_nt(wo_ref[...], low_ref[...]).astype(LOW)
    yield


def attention_backward(row, lengths_ref, x, do_ref, ob_ref, qa_ref, ka_ref, va_ref, lse_ref, dqkv_ref, gwq_ref, gbias_ref, p_ref, ds_ref, s_ref):
    width = HEADS * HD
    segment, last = segments(lengths_ref, row)
    pad = (segment == last).astype(F32)

    def scores(head):
        for half in HALVES:
            s_ref[0, head % 2, half] = dot_tn(ka_ref[head, :, half], qa_ref[head, :, half])
            s_ref[1, head % 2, half] = dot_tn(
                va_ref[head, 0:HD, half], do_ref[head_rows(head), half]
            )

    def weigh(head):
        product = do_ref[head_rows(head)].astype(F32) * ob_ref[head_rows(head)].astype(F32)
        centre = jnp.sum(product, 0, keepdims=True)
        for half in HALVES:
            p = jnp.exp(s_ref[0, head % 2, half] - lse_ref[head : head + 1, half])
            p_ref[head % 2, half] = p.astype(LOW)
            ds_ref[head % 2, half] = (p * (s_ref[1, head % 2, half] - centre[:, half])).astype(LOW)

    scores(0)
    yield
    for head in range(HEADS):
        if head + 1 < HEADS:
            scores(head + 1)
            yield
        weigh(head)
        yield
        for half in HALVES:
            ds, do = ds_ref[head % 2, half], do_ref[head_rows(head), half]
            dq = dot_nn(ka_ref[head, 0:HD, half], ds) * HD**-0.5
            dk = dot_nt(qa_ref[head, 0:HD, half], ds)
            dv = dot_nt(do, p_ref[head % 2, half]) + pad[:, half] * do.astype(F32)
            for block, value in enumerate((dq, dk, dv)):
                at = block * width + head * HD
                dqkv_ref[at : at + HD, half] = value.astype(LOW)
        yield
    for index, block in enumerate((0, 2)):
        value = dqkv_ref[block * width : (block + 1) * width].astype(F32)
        parts = [value[:, at : at + 128] for at in range(0, SEQ, 128)]
        gbias_ref[index] += (parts[0] + parts[1]) + (parts[2] + parts[3])
    gwq_ref[...] += dot_nn(dqkv_ref[...], x)
    yield


def unpack_matrix(raw_ref, at, into_ref):
    width = into_ref.shape[0]
    for start in range(0, into_ref.shape[1], width):
        block = raw_ref[:, :, pl.ds(at + start, width)].astype(F32)
        block = block.reshape(GROUPS + (width,)).swapaxes(0, 1).reshape(width, width)
        into_ref[:, pl.ds(start, width)] = block.astype(LOW)


def unpack_stacked(raw_ref, at, into_ref):
    width = into_ref.shape[1]
    count = into_ref.shape[0] // width
    blocks = [
        raw_ref[:, :, pl.ds(at + step * width, width)].astype(F32).reshape(GROUPS + (width,))
        for step in range(count)
    ]
    outer, inner, rows = GROUPS
    for place in range(inner):
        part = jnp.stack([jnp.stack([block[f, place] for block in blocks]) for f in range(outer)])
        size = outer * count * rows
        into_ref[pl.ds(place * size, size)] = part.reshape(size, width).astype(LOW)


def counter(shape, axis):
    return lax.broadcasted_iota(jnp.int32, shape, axis)


def split_by(values, size):
    return lax.shift_right_logical(values, size.bit_length() - 1), values & (size - 1)


def sources(rows):
    outer, inner, height = GROUPS
    group, within = split_by(counter((rows, 1), 0), height)
    far, near = split_by(group, inner)
    return near * outer + far, within


def unpack_vectors(raw_ref, at, layer):
    outer, inner, rows = GROUPS
    total = outer * inner * rows
    raw = raw_ref[:, :, pl.ds(at, 128)].reshape(total, 128)
    owner, place = split_by(counter((1, total), 1), rows)
    pick = jnp.where(counter((128, 1), 0) == rows * layer + place, 1.0, 0.0).astype(LOW)
    device, unused = sources(total)
    spread = jnp.where(owner == device, dot_nn(raw, pick), 0.0)
    return jnp.sum(spread.reshape(outer * inner, rows, total), 0)


def unpack_hidden(raw_ref, at, layer, hidden):
    outer, inner, rows = GROUPS
    total = outer * inner * rows
    raw = raw_ref[:, :, pl.ds(at, 128)].reshape(total, 128)
    owner, place = split_by(counter((1, hidden), 1), hidden // (outer * inner))
    pick = jnp.where(counter((128, 1), 0) == 2 * rows + place, 1.0, 0.0).astype(LOW)
    device, within = sources(total)
    device = jnp.where(within == layer, device, -1)
    spread = jnp.where(owner == device, dot_nn(raw, pick), 0.0)
    return jnp.sum(spread, 0, keepdims=True)


def pack_matrix(sum_ref, sent_ref, at, turned=False):
    width = sum_ref.shape[1 if turned else 0]
    outer, inner, rows = GROUPS
    for start in range(0, sum_ref.shape[0 if turned else 1], width):
        near = pl.ds(start, width)
        block = sum_ref[near].T if turned else sum_ref[:, near]
        block = block.reshape(inner, outer, rows, width)
        block = block.swapaxes(0, 1).reshape(outer, inner * rows, width)
        sent_ref[:, :, pl.ds(at + start, width)] = block.astype(LOW)


def pack_stacked(sum_ref, sent_ref, at):
    width = sum_ref.shape[0]
    outer, inner, rows = GROUPS
    count = sum_ref.shape[1] // width
    near = inner // count
    for step in range(count):
        block = sum_ref[:, pl.ds(step * width, width)].T
        block = block.reshape(near, outer, count, rows, width)
        for part in range(count):
            piece = jnp.stack([block[:, f, part] for f in range(outer)])
            piece = piece.reshape(outer, near * rows, width)
            sent_ref[:, pl.ds(step * near * rows, near * rows), pl.ds(at + part * width, width)] = (
                piece.astype(LOW)
            )


def pack_vectors(block, line, sent_ref, at):
    outer, inner, rows = GROUPS
    total = outer * inner * rows
    device, within = sources(total)
    owner, unused = split_by(counter((1, total), 1), rows)
    spread = jnp.broadcast_to(block[None], (outer * inner, rows, total)).reshape(total, total)
    spread = jnp.where(owner == device, spread, 0.0).astype(LOW)
    unused, place = split_by(counter((total, 1), 0), rows)
    found = dot_nn(spread, jnp.where(counter((1, 128), 1) == place, 1.0, 0.0).astype(LOW))
    if line is not None:
        hidden = line.shape[1]
        height = hidden // (outer * inner)
        owner, unused = split_by(counter((1, hidden), 1), height)
        spread = jnp.where(owner == jnp.where(within == 0, device, -1), line, 0.0).astype(LOW)
        unused, place = split_by(counter((hidden, 1), 0), height)
        pick = jnp.where(counter((1, 128), 1) == 2 * rows + place, 1.0, 0.0).astype(LOW)
        found = found + dot_nn(spread, pick)
    sent_ref[:, :, pl.ds(at, 128)] = found.reshape(outer, inner * rows, 128).astype(LOW)


def bias_rows(gbias_ref):
    width = gbias_ref.shape[1]
    parts = [jnp.sum(gbias_ref[index].T, 0, keepdims=True) for index in range(2)]
    return jnp.concatenate(parts + [jnp.zeros((6, width), F32)], 0)


def pack_dense(gwo_ref, gwi_ref, gwf_ref, gsmall_ref, gbi_ref, block, sent_ref, at):
    width, hidden = gwi_ref.shape
    pack_matrix(gwo_ref, sent_ref, at)
    pack_matrix(gwi_ref, sent_ref, at + width)
    pack_stacked(gwf_ref, sent_ref, at + width + hidden)
    block = jnp.sum(gsmall_ref[...], 1) + block
    pack_vectors(block, gbi_ref[0:1], sent_ref, at + width + 2 * hidden)


def shape_of(array):
    return jax.ShapeDtypeStruct(array.shape, array.dtype)


def by_row(shape, group):
    if len(shape) == 2:
        return pl.BlockSpec((group * SEQ, shape[1]), lambda step: (step, 0))
    return pl.BlockSpec((group,) + tuple(shape[1:]), lambda step: (step,) + (0,) * (len(shape) - 1))


def one_row(ref, member):
    if len(ref.shape) == 2:
        return ref.at[pl.ds(member * SEQ, SEQ)]
    return ref.at[member]


def alternate(runs):
    running = []
    waiting = list(runs)
    while running or waiting:
        if waiting:
            running.append(waiting.pop(0))
        for run in list(running):
            try:
                next(run)
            except StopIteration:
                running.remove(run)


def whole(shape):
    return pl.BlockSpec(tuple(shape), lambda row: (0,) * len(shape))


def run_rows(
    body, lengths, rowwise, fixed, row_outs, sent, shared, private, cost, setup, finish, after=(),
    scalars=(), group=1, late=()
):
    count = lengths.shape[0]
    group = group if count % group == 0 else 1
    cuts = [len(scalars), len(rowwise), len(fixed), len(after), len(late), len(row_outs), len(sent)]
    cuts += [len(shared)] + [len(private)] * group + [len(late), 1 if late else 0]
    late_blocks = [
        (group * SEQ, part.shape[1]) if len(part.shape) == 2 else (group,) + tuple(part.shape[1:])
        for part in late
    ]

    def kernel(lengths_ref, *refs):
        step = pl.program_id(0)
        groups = []
        at = 0
        for cut in cuts:
            groups.append(refs[at : at + cut])
            at += cut
        numbers, rows_in, fixed_in, unused, late_in, rows_out, sent_out, work = groups[:8]
        late_refs = groups[8 + group]
        copies = [
            pltpu.make_async_copy(
                source.at[pl.ds(step * block[0], block[0])], target, groups[-1][0].at[index]
            )
            for index, (source, target, block) in enumerate(zip(late_in, late_refs, late_blocks))
        ]
        for copy in copies:
            copy.start()
        waiting = list(copies)

        def wait():
            while waiting:
                waiting.pop().wait()

        @pl.when(step == 0)
        def _():
            setup(numbers, fixed_in, sent_out, work)

        alternate(
            body(
                step * group + member,
                lengths_ref,
                [one_row(ref, member) for ref in rows_in],
                [one_row(ref, member) for ref in rows_out],
                work,
                groups[8 + member],
                *([[one_row(ref, member) for ref in late_refs], wait] if late else []),
            )
            for member in range(group)
        )

        if finish:

            @pl.when(step == count // group - 1)
            def _():
                finish(numbers, work, sent_out)

    return pl.pallas_call(
        kernel,
        grid=(count // group,),
        in_specs=[pl.BlockSpec(memory_space=pltpu.SMEM)] * (1 + len(scalars))
        + [by_row(array.shape, group) for array in rowwise]
        + [whole(array.shape) for array in fixed]
        + [pl.BlockSpec(memory_space=pl.ANY) for array in (*after, *late)],
        out_specs=[by_row(part.shape, group) for part in row_outs]
        + [whole(part.shape) for part in sent],
        out_shape=list(row_outs) + list(sent),
        scratch_shapes=list(shared)
        + list(private) * group
        + [vmem(block, part.dtype) for block, part in zip(late_blocks, late)]
        + ([pltpu.SemaphoreType.DMA((len(late),))] if late else []),
        compiler_params=pltpu.CompilerParams(
            dimension_semantics=("arbitrary",), vmem_limit_bytes=MEMORY
        ),
        cost_estimate=pl.CostEstimate(flops=cost, bytes_accessed=8 * 2**20, transcendentals=0),
    )(lengths, *scalars, *rowwise, *fixed, *after, *late)


def struct(shape, dtype):
    return jax.ShapeDtypeStruct(tuple(shape), dtype)


FORWARD_SCRATCH = lambda: [
    pltpu.VMEM((2, SEQ, HALF), F32),
    pltpu.VMEM((2, SEQ, HALF), LOW),
]
BACKWARD_SCRATCH = lambda: [
    pltpu.VMEM((2, SEQ, HALF), LOW),
    pltpu.VMEM((2, SEQ, HALF), LOW),
    pltpu.VMEM((2, 2, SEQ, HALF), F32),
    pltpu.VMEM((3 * HEADS * HD, SEQ), LOW),
]


def attention_outs(rows, width):
    return [
        struct((rows, HEADS, PAIR, SEQ), LOW),
        struct((rows, HEADS, PAIR, SEQ), LOW),
        struct((rows, HEADS, HD + EXTRA, SEQ), LOW),
        struct((rows, width, SEQ), LOW),
        struct((rows, 8, SEQ), F32),
    ]


def dense_outs(tokens, width, hidden):
    return [
        struct((tokens, width), F32),
        struct((tokens, width), F32),
        struct((tokens, PAIR), F32),
        struct((tokens, width), LOW),
        struct((tokens, hidden), LOW),
        struct((tokens, hidden), LOW),
    ]


def vmem(shape, dtype):
    return pltpu.VMEM(tuple(shape), dtype)


def attention_weights(width):
    return [vmem((width, 3 * width), LOW), vmem((3 * width, width), LOW), vmem((3 * width, 128), F32)]


def dense_weights(width, hidden):
    return [
        vmem((width, width), LOW),
        vmem((width, hidden), LOW),
        vmem((hidden, width), LOW),
        vmem((8, width), F32),
        vmem((1, hidden), F32),
    ]


def dense_sums(width, hidden):
    return [
        vmem((width, width), F32),
        vmem((width, hidden), F32),
        vmem((width, hidden), F32),
        vmem((8, 8, width), F32),
        vmem((8, hidden), F32),
    ]


def attention_sums(width):
    return [vmem((3 * width, width), F32), vmem((2, width, 128), F32)]


def dense_work(width, hidden):
    return [
        vmem((SEQ, width), LOW),
        vmem((2, SEQ, width), F32),
        vmem((SEQ, hidden), LOW),
        vmem((2, width + EXTRA, SEQ), LOW),
    ]


def set_attention(layer, urgent_ref, raw_ref, at, wq_ref, wt_ref, bias_ref):
    width = wq_ref.shape[0]
    unpack_matrix(raw_ref, at, wq_ref)
    vectors = unpack_vectors(urgent_ref, 3 * width, layer)
    for block, line in enumerate((vectors[0:1], jnp.zeros((1, width), F32), vectors[1:2])):
        lines = pl.ds(block * width, width)
        wt_ref[lines] = wq_ref[:, lines].astype(F32).T.astype(LOW)
        bias_ref[lines] = jnp.broadcast_to(line, (128, width)).T


def set_dense(layer, urgent_ref, raw_ref, at, wo_ref, wi_ref, wf_ref, small_ref, bi_ref):
    width, hidden = wi_ref.shape
    unpack_matrix(raw_ref, at, wo_ref)
    unpack_matrix(raw_ref, at + width, wi_ref)
    unpack_stacked(raw_ref, at + width + hidden, wf_ref)
    small_ref[...] = unpack_vectors(urgent_ref, 3 * width, layer)
    bi_ref[...] = unpack_hidden(urgent_ref, 3 * width, layer, hidden)


def clear(refs):
    for ref in refs:
        ref[...] = jnp.zeros(ref.shape, ref.dtype)


def assemble(place_ref, part_refs, into_ref):
    for step, ref in enumerate(part_refs):
        into_ref[place_ref[0] ^ step] = ref[...]


def raw_block(parts):
    return vmem((len(parts),) + parts[0].shape, LOW)


def turned_back(lengths_ref, row, values):
    return pltpu.roll(values, longest_start(lengths_ref, row), 0).astype(LOW)


def rotate_kernel(lengths, arrays):
    def body(row, lengths_ref, rowwise, outs, work, own):
        back = (SEQ - longest_start(lengths_ref, row)) & (SEQ - 1)
        for source, target in zip(rowwise, outs):
            target[...] = pltpu.roll(source[...].astype(F32), back, 0).astype(LOW)
            yield

    return run_rows(
        body, lengths, list(arrays), [], [struct(array.shape, LOW) for array in arrays], [], [], [],
        10**6, lambda *refs: None, None,
    )


def first_kernel(lengths, x, place, parts):
    rows, (tokens, width) = lengths.shape[0], x.shape

    def setup(numbers, fixed, sent, work):
        assemble(numbers[0], fixed, sent[0])
        set_attention(0, sent[0], sent[0], 0, *work)

    def body(row, lengths_ref, rowwise, outs, work, own):
        return attention_forward(row, lengths_ref, rowwise[0][...], *work[1:3], *outs, *own)

    return run_rows(
        body, lengths, [x], list(parts), attention_outs(rows, width),
        [struct((len(parts),) + parts[0].shape, LOW)],
        attention_weights(width), FORWARD_SCRATCH(), 4 * 10**9, setup, None, (), [place],
    )


def attention_kernel(layer, lengths, x, place, urgent, parts, at):
    rows, (tokens, width) = lengths.shape[0], x.shape

    def setup(numbers, fixed, sent, work):
        assemble(numbers[0], fixed[1:], work[3])
        set_attention(layer, fixed[0], work[3], at, *work[:3])

    def body(row, lengths_ref, rowwise, outs, work, own):
        return attention_forward(
            row, lengths_ref, rowwise[0][...].astype(LOW), *work[1:3], *outs, *own
        )

    return run_rows(
        body, lengths, [x], [urgent] + list(parts), attention_outs(rows, width), [],
        attention_weights(width) + [raw_block(parts)], FORWARD_SCRATCH(),
        4 * 10**9, setup, None, (), [place],
    )


def dense_kernel(layer, lengths, x, ob, place, urgent, parts, at, hidden):
    tokens, width = x.shape

    def setup(numbers, fixed, sent, work):
        assemble(numbers[0], fixed[1:], work[5])
        set_dense(layer, fixed[0], work[5], at, *work[:5])

    def body(row, lengths_ref, rowwise, outs, work, own):
        return dense_forward(*rowwise, *work[:5], *outs, *own)

    return run_rows(
        body, lengths, [x, ob], [urgent] + list(parts),
        dense_outs(tokens, width, hidden) + [struct((tokens, width), F32)], [],
        dense_weights(width, hidden) + [raw_block(parts)],
        [vmem((SEQ, width), F32), vmem((2, SEQ, width), F32)],
        5 * 10**9, setup, None, (), [place],
    )


def turn_kernel(layer, lengths, x, ob, cotangent, place, urgent, parts, at, hidden):
    tokens, width = x.shape
    columns = width + 2 * hidden + 128

    def setup(numbers, fixed, sent, work):
        assemble(numbers[0], fixed[1:], work[11])
        set_dense(layer, fixed[0], work[11], at, *work[:5])
        clear(work[5:10])

    def body(row, lengths_ref, rowwise, outs, work, own):
        x_ref, ob_ref, dz_ref = rowwise
        z_ref, dr_ref, dob_ref = outs
        weights, sums = work[:5], work[5:10]
        kept, work_ref, back = own[:6], own[6], own[7:]
        yield from dense_forward(x_ref, ob_ref, *weights, *kept, z_ref, work_ref, back[1])
        yield from dense_backward(dz_ref, *kept, ob_ref, *weights[:4], dr_ref, dob_ref, *sums, *back)

    def finish(numbers, work, sent):
        pack_dense(*work[5:10], 0.0, work[10], 0)
        hand_out(numbers[0], work[10], sent)

    kept = [vmem((SEQ,) + part.shape[1:], part.dtype) for part in dense_outs(tokens, width, hidden)]
    return run_rows(
        body, lengths, [x, ob, cotangent], [urgent] + list(parts),
        [struct((tokens, width), LOW), struct((tokens, width), F32), struct((tokens // SEQ, width, SEQ), LOW)],
        [struct((64, columns), LOW)] * 4,
        dense_weights(width, hidden) + dense_sums(width, hidden)
        + [vmem((4, 64, columns), LOW), raw_block(parts)],
        kept + [vmem((SEQ, width), F32)] + dense_work(width, hidden),
        10**10, setup, finish, (), [place], 2,
    )


def hand_out(place_ref, packed_ref, sent):
    for step, ref in enumerate(sent):
        ref[...] = packed_ref[place_ref[0] ^ step]


def middle_kernel(lengths, upper, lower, place, urgent, parts, hidden, after):
    tokens, width = upper[0].shape
    columns = 4 * width + 2 * hidden + 128

    def setup(numbers, fixed, sent, work):
        assemble(numbers[0], fixed[1:], work[16])
        set_attention(1, fixed[0], work[16], 0, *work[:3])
        set_dense(0, fixed[0], work[16], 3 * width, *work[3:8])
        clear(work[8:15])

    def body(row, lengths_ref, up, outs, work, own, low, wait):
        dx_ref = own[0]
        yield from attention_backward(
            row, lengths_ref, up[0][...].astype(LOW), *up[1:7], own[-1], *work[8:10], *own[5:-1]
        )
        dx_ref[...] = up[7][...] + dot_tn(own[-1][...], work[1][...])
        yield
        wait()
        yield from dense_backward(dx_ref, *low, *work[3:7], *outs, *work[10:15], *own[1:5])

    def finish(numbers, work, sent):
        pack_matrix(work[8], work[15], 0, True)
        pack_dense(*work[10:15], bias_rows(work[9]), work[15], 3 * width)
        hand_out(numbers[0], work[15], sent)

    return run_rows(
        body, lengths, list(upper), [urgent] + list(parts),
        [struct((tokens, width), F32), struct((tokens // SEQ, width, SEQ), LOW)],
        [struct((64, columns), LOW)] * 4,
        attention_weights(width) + dense_weights(width, hidden)
        + attention_sums(width) + dense_sums(width, hidden)
        + [vmem((4, 64, columns), LOW), raw_block(parts)],
        [vmem((SEQ, width), F32)] + dense_work(width, hidden) + BACKWARD_SCRATCH(),
        15 * 10**9, setup, finish, after, [place], 2, list(lower),
    )


def last_kernel(lengths, upper, after, place):
    tokens, width = upper[0].shape

    def setup(numbers, fixed, sent, work):
        clear(work[:2])

    def body(row, lengths_ref, rowwise, outs, work, own):
        return attention_backward(
            row, lengths_ref, rowwise[0][...], *rowwise[1:], outs[0], *work[:2], *own
        )

    def finish(numbers, work, sent):
        pack_matrix(work[0], work[2], 0, True)
        pack_vectors(bias_rows(work[1]), None, work[2], 3 * width)
        hand_out(numbers[0], work[2], sent)

    return run_rows(
        body, lengths, list(upper), [], [struct((tokens // SEQ, 3 * width, SEQ), LOW)],
        [struct((64, 3 * width + 128), LOW)] * 4,
        attention_sums(width) + [vmem((4, 64, 3 * width + 128), LOW)],
        BACKWARD_SCRATCH()[:-1], 8 * 10**9, setup, finish, after, [place], 2,
    )


def outward_kernel(lengths, z, after):
    def body(row, lengths_ref, rowwise, outs, work, own):
        outs[0][...] = turned_back(lengths_ref, row, rowwise[0][...].astype(F32))
        yield

    (found,) = run_rows(
        body, lengths, [z], [], [struct(z.shape, LOW)], [], [], [], 3 * 10**9,
        lambda *refs: None, None, after,
    )
    return found


def inward_kernel(lengths, dqkv, dr, urgent, after):
    tokens, width = dr.shape

    def setup(numbers, fixed, sent, work):
        set_attention(0, fixed[0], fixed[0], 0, *work)

    def body(row, lengths_ref, rowwise, outs, work, own):
        dqkv_ref, dr_ref = rowwise
        dx = dr_ref[...] + dot_tn(dqkv_ref[...], work[1][...])
        outs[0][...] = turned_back(lengths_ref, row, dx)
        yield

    (found,) = run_rows(
        body, lengths, [dqkv, dr], [urgent], [struct((tokens, width), LOW)], [],
        attention_weights(width), [], 5 * 10**9, setup, None, after,
    )
    return found


def hold(array, after):
    def kernel(*refs):
        pass

    anywhere = pl.BlockSpec(memory_space=pl.ANY)
    return pl.pallas_call(
        kernel,
        in_specs=[anywhere] * (1 + len(after)),
        out_specs=anywhere,
        out_shape=shape_of(array),
        input_output_aliases={0: 0},
    )(array, *after)


def pack_parameters(
    attn_weight, attn_bias, out_weight, ffn_in, ffn_in_bias, ffn_out, norm_gain, shifts
):
    depth, rows, width = out_weight.shape
    copies = GROUPS[1]
    hidden = ffn_in.shape[2]
    dense = width + 2 * hidden
    height = ffn_in_bias.shape[1]

    def kernel(wq_ref, ab_ref, wo_ref, wi_ref, bi_ref, wf_ref, gain_ref, shift_ref, first_ref, rest_ref, small_ref):
        def put(ref, block, at):
            block = jnp.broadcast_to(block.astype(F32)[None], (copies,) + block.shape)
            block = block.reshape(copies * block.shape[1], block.shape[2])
            ref[:, pl.ds(at, block.shape[1])] = block.astype(LOW)

        small_ref[...] = jnp.zeros(small_ref.shape, F32)
        for layer in range(depth):
            lanes = pl.ds(rows * layer, rows)
            small_ref[0:2, lanes] = ab_ref[layer].astype(F32)
            small_ref[2:4, lanes] = gain_ref[layer].astype(F32)
            small_ref[4:8, lanes] = shift_ref[layer].astype(F32)
        small_ref[0:depth, pl.ds(2 * rows, height)] = bi_ref[...].astype(F32)
        put(first_ref, wq_ref[0], 0)
        put(first_ref, small_ref[...], 3 * width)
        put(first_ref, wq_ref[1], 3 * width + 128)
        for layer, ref, at in ((0, first_ref, 6 * width + 128), (1, rest_ref, 0)):
            put(ref, wo_ref[layer], at)
            put(ref, wi_ref[layer], at + width)
            at += width + hidden
            down = wf_ref[layer].astype(F32)
            for step in range(hidden // width):
                put(ref, down[step * rows : (step + 1) * rows], at)
                at += width

    return pl.pallas_call(
        kernel,
        in_specs=[pl.BlockSpec(memory_space=pltpu.VMEM)] * 8,
        out_shape=[
            struct((copies * rows, 6 * width + 128 + dense), LOW),
            struct((copies * rows, dense), LOW),
        ],
        scratch_shapes=[vmem((rows, 128), F32)],
        compiler_params=pltpu.CompilerParams(vmem_limit_bytes=MEMORY),
    )(attn_weight, attn_bias, out_weight, ffn_in, ffn_in_bias, ffn_out, norm_gain, shifts)


def add_parts(place, parts, halves, after=()):
    lanes = parts[0].shape[1]
    count = len(parts)
    many, rows = GROUPS[1:]
    outs = 2 if halves else 1

    def kernel(place_ref, *refs):
        out_refs, sum_ref = refs[count + len(after) : -1], refs[-1]
        bit = place_ref[0] & 1
        for start in range(0, lanes, 128):
            near = pl.ds(start, 128)
            total = refs[0][:, near].astype(F32)
            for ref in refs[1:count]:
                total = total + ref[:, near].astype(F32)
            if halves:
                sum_ref[:, :, near] = total.reshape(many, rows, 128)
            else:
                out_refs[0][:, near] = total.astype(LOW)
        for side, ref in enumerate(out_refs if halves else ()):
            for start in range(0, lanes, 128):
                near = pl.ds(start, 128)
                block = [sum_ref[2 * step + (bit ^ side), :, near] for step in range(many // 2)]
                ref[:, near] = jnp.concatenate(block, 0).astype(LOW)

    return pl.pallas_call(
        kernel,
        in_specs=[pl.BlockSpec(memory_space=pltpu.SMEM)]
        + [pl.BlockSpec(memory_space=pltpu.VMEM)] * count
        + [pl.BlockSpec(memory_space=pl.ANY)] * len(after),
        out_shape=[struct((many * rows // outs, lanes), LOW)] * outs,
        scratch_shapes=[vmem((many, rows, lanes), F32)],
        compiler_params=pltpu.CompilerParams(vmem_limit_bytes=MEMORY),
    )(place, *parts, *after)


def add_halves(place, pairs, after=()):
    many, rows = GROUPS[1] // 2, GROUPS[2]
    widths = [pair[0].shape[1] for pair in pairs]
    lanes = sum(widths)

    def kernel(place_ref, *refs):
        out_refs, sum_ref = refs[2 * len(pairs) + len(after) : -1], refs[-1]
        at = 0
        for index, size in enumerate(widths):
            for start in range(0, size, 128):
                near = pl.ds(start, 128)
                total = refs[2 * index][:, near].astype(F32) + refs[2 * index + 1][:, near].astype(F32)
                sum_ref[:, :, pl.ds(at + start, 128)] = total.reshape(many, rows, 128)
            at += size
        far = lax.shift_right_logical(place_ref[0], 1)
        for step, ref in enumerate(out_refs):
            ref[...] = sum_ref[far ^ step].astype(LOW)

    return pl.pallas_call(
        kernel,
        in_specs=[pl.BlockSpec(memory_space=pltpu.SMEM)]
        + [pl.BlockSpec(memory_space=pltpu.VMEM)] * (2 * len(pairs))
        + [pl.BlockSpec(memory_space=pl.ANY)] * len(after),
        out_shape=[struct((rows, lanes), LOW)] * many,
        scratch_shapes=[vmem((many, rows, lanes), F32)],
        compiler_params=pltpu.CompilerParams(vmem_limit_bytes=MEMORY),
    )(place, *(part for pair in pairs for part in pair), *after)


def write_gradients(found, depth, width, hidden, after):
    rows = GROUPS[2]
    height = hidden // DEVICES
    dense = width + 2 * hidden

    def kernel(*refs):
        found_refs, refs = refs[: len(found)], refs[len(found) + len(after) :]
        gwq_ref, gab_ref, gwo_ref, gwi_ref, gbi_ref, gwf_ref, gain_ref, shift_ref = refs

        def total(at, columns):
            value = found_refs[0][:, pl.ds(at, columns)].astype(F32)
            for ref in found_refs[1:]:
                value = value + ref[:, pl.ds(at, columns)].astype(F32)
            return value

        first, second = dense + 128, 2 * dense + 3 * width + 256
        blocks = [total(at, 128) for at in (dense, first + 3 * width + dense, second + 3 * width)]
        for layer, at, block in ((0, second, blocks[2]), (1, first, blocks[1])):
            gwq_ref[layer] = total(at, 3 * width)
            gab_ref[layer] = block[0:2, 0:rows]
        for layer, at, block in ((0, first + 3 * width, blocks[1]), (1, 0, blocks[0])):
            gwo_ref[layer] = total(at, width)
            gwi_ref[layer] = total(at + width, hidden)
            for step in range(hidden // width):
                gwf_ref[layer, pl.ds(step * rows, rows)] = total(
                    at + width + hidden + step * width, width
                )
            gain_ref[layer] = block[2:4, 0:rows]
            shift_ref[layer] = block[4:8, 0:rows]
            gbi_ref[pl.ds(layer, 1)] = pltpu.roll(block, 128 - 2 * rows, 1)[0:1, 0:height]

    outs = [
        struct((depth, rows, 3 * width), F32),
        struct((depth, 2, rows), F32),
        struct((depth, rows, width), F32),
        struct((depth, rows, hidden), F32),
        struct((depth, height), F32),
        struct((depth, height, width), F32),
        struct((depth, 2, rows), F32),
        struct((depth, 4, rows), F32),
    ]
    return pl.pallas_call(
        kernel,
        in_specs=[pl.BlockSpec(memory_space=pltpu.VMEM)] * len(found)
        + [pl.BlockSpec(memory_space=pl.ANY)] * len(after),
        out_shape=outs,
        compiler_params=pltpu.CompilerParams(vmem_limit_bytes=MEMORY),
    )(*found, *after)


def exchange(parts, axis):
    return lax.all_to_all(parts, axis, 0, 0, tiled=True)


def swap(part, axis, step):
    size = lax.axis_size(axis)
    return lax.ppermute(part, axis, [(source, source ^ step) for source in range(size)])


def local(
    hidden_in,
    lengths,
    grad_out,
    attn_weight,
    attn_bias,
    out_weight,
    ffn_in,
    ffn_in_bias,
    ffn_out,
    norm_gain,
    shifts,
):
    depth, rows, width = out_weight.shape
    hidden = ffn_in.shape[2]
    first, second = lax.axis_size("dp"), lax.axis_size("fsdp")
    fits = (second, first, rows) == GROUPS
    urgent_size = 3 * width + 128
    if fits:
        early, later = pack_parameters(
            attn_weight, attn_bias, out_weight, ffn_in, ffn_in_bias, ffn_out, norm_gain, shifts
        )
        across = lax.axis_index("dp").astype(jnp.int32).reshape(1)
        place = lax.axis_index("fsdp").astype(jnp.int32).reshape(1)
        partners = range(1, second)
        x0, dz1 = rotate_kernel(lengths, (hidden_in, grad_out))
        early = hold(exchange(early, "dp"), (x0,))
        urgent = early[:, :urgent_size]
        urgent = [urgent] + [swap(urgent, "fsdp", step) for step in partners]
        raw0 = early[:, urgent_size:]
        raw0 = [raw0, swap(raw0, "fsdp", 1), swap(raw0, "fsdp", 2)]
    else:
        urgent, raw0, raw1 = gather_other(
            attn_weight, attn_bias, out_weight, ffn_in, ffn_in_bias, ffn_out, norm_gain, shifts
        )
        urgent, raw0, raw1 = ([part[step] for step in range(4)] for part in (urgent, raw0, raw1))
        place = jnp.zeros((1,), jnp.int32)
        x0, dz1 = rotate_kernel(lengths, (hidden_in, grad_out))

    qa0, ka0, va0, ob0, lse0, urgent = first_kernel(lengths, x0, place, urgent)
    if fits:
        raw0[2] = hold(raw0[2], (ob0,))
        raw0.append(swap(raw0[2], "fsdp", 1))
        later = exchange(hold(later, (ob0,)), "dp")
    n1, n2, inv, yb, gb, gp, z0 = dense_kernel(
        0, lengths, x0, ob0, place, urgent, raw0, 3 * width, hidden
    )
    if fits:
        raw1 = hold(later, (z0,))
        raw1 = [raw1, swap(raw1, "fsdp", 1), swap(raw1, "fsdp", 2)]
    qa1, ka1, va1, ob1, lse1 = attention_kernel(1, lengths, z0, place, urgent, raw0, 0)
    if fits:
        raw1[2] = hold(raw1[2], (ob1,))
        raw1.append(swap(raw1[2], "fsdp", 1))
    z1, dr1, dob1, *sent_a = turn_kernel(
        1, lengths, z0, ob1, dz1, place, urgent, raw1, 0, hidden
    )
    dr0, dob0, *sent_b = middle_kernel(
        lengths,
        (z0, dob1, ob1, qa1, ka1, va1, lse1, dr1),
        (n1, n2, inv, yb, gb, gp, ob0),
        place,
        urgent,
        raw0,
        hidden,
        (sent_a[0],),
    )
    if fits:
        got_a = [sent_a[0]] + [swap(sent_a[step], "fsdp", step) for step in partners]
        keep_a, give_a = add_parts(across, got_a, True, (sent_b[0],))
        got_ax = swap(give_a, "dp", 1)
        ready = (sent_b[0], keep_a)
    else:
        ready = ()
    dqkv, *sent_c = last_kernel(
        lengths, (x0, dob0, ob0, qa0, ka0, va0, lse0), ready, place
    )
    if fits:
        got_b = [sent_b[0]] + [swap(sent_b[step], "fsdp", step) for step in partners]
        got_c = [sent_c[0]] + [swap(sent_c[step], "fsdp", step) for step in partners]
        keep_b, give_b = add_parts(across, got_b, True, (got_ax, dqkv))
        keep_c, give_c = add_parts(across, got_c, True, (keep_b,))
        grad_in = inward_kernel(lengths, dqkv, dr0, urgent, (keep_c,))
        pairs = [(keep_a, got_ax), (keep_b, swap(give_b, "dp", 1)), (keep_c, swap(give_c, "dp", 1))]
        found = add_halves(across, pairs, (grad_in,))
        hidden_out = outward_kernel(lengths, z1, (found[0],))
        found = [found[0]] + [swap(found[step], "dp", 2 * step) for step in range(1, first // 2)]
        grads = write_gradients(found, depth, width, hidden, (hidden_out,))
    else:
        grad_in = inward_kernel(lengths, dqkv, dr0, urgent, ())
        hidden_out = outward_kernel(lengths, z1, ())
        grads = scatter_other(
            *(jnp.stack(part) for part in (sent_a, sent_b, sent_c)), rows, width, hidden
        )
    return (hidden_out, grad_in, *grads)


def gather_other(
    attn_weight, attn_bias, out_weight, ffn_in, ffn_in_bias, ffn_out, norm_gain, shifts
):
    axes = ("dp", "fsdp")
    gather = lambda part, axis: lax.all_gather(part, axes, axis=axis, tiled=True)
    depth, unused, width = out_weight.shape
    hidden = ffn_in.shape[2]
    outer, inner, rows = GROUPS
    vectors = gather(jnp.concatenate([attn_bias, norm_gain, shifts], 1), 2)
    line = gather(ffn_in_bias, 1)

    def order(natural):
        return (
            natural.reshape(inner, outer, rows, -1).swapaxes(0, 1).reshape(outer, inner * rows, -1)
        )

    def stacked(part):
        part = part.reshape(DEVICES, -1, rows, width)
        return order(part.swapaxes(1, 2).reshape(width, -1))

    small = vectors.reshape(depth, 8, DEVICES, rows).transpose(2, 1, 0, 3).reshape(width, -1)
    line = line.reshape(depth, DEVICES, -1).swapaxes(0, 1)
    line = jnp.pad(line, ((0, 0), (0, 8 - depth), (0, 0))).reshape(width, -1)
    small = jnp.concatenate([small, line], 1)
    small = jnp.pad(small, ((0, 0), (0, 128 - small.shape[1])))
    wq, wo, wi, wf = (gather(part, 1) for part in (attn_weight, out_weight, ffn_in, ffn_out))
    urgent = jnp.concatenate([order(wq[0]), order(small)], 2)
    raw0 = jnp.concatenate([order(wq[1]), order(wo[0]), order(wi[0]), stacked(wf[0])], 2)
    raw1 = jnp.concatenate([order(wo[1]), order(wi[1]), stacked(wf[1])], 2)
    return urgent, raw0, raw1


def scatter_other(sent_a, sent_b, sent_c, own_rows, width, hidden):
    outer, inner, rows = GROUPS
    axes = ("dp", "fsdp")

    def natural(part):
        return part.reshape(outer, inner, rows, -1).swapaxes(0, 1).reshape(width, -1).astype(F32)

    def cut(part, sizes):
        found, at = [], 0
        for size in sizes:
            found.append(part[:, at : at + size])
            at += size
        return found

    dense = [width, hidden, hidden, 128]
    wq0, block_c = cut(natural(sent_c), [3 * width, 128])
    wq1, wo0, wi0, wf0, block_b = cut(natural(sent_b), [3 * width] + dense)
    wo1, wi1, wf1, block_a = cut(natural(sent_a), dense)

    def vectors(block):
        block = block.reshape(DEVICES, rows, 128)
        return block[:, :, :rows].swapaxes(0, 1).reshape(rows, width)

    def line(block):
        block = block.reshape(DEVICES, rows, 128)
        return block[:, 0, 2 * rows : 2 * rows + hidden // DEVICES].reshape(-1)

    def stacked(part):
        part = part.reshape(DEVICES, rows, -1, width).swapaxes(1, 2)
        return part.reshape(hidden, width)

    def spread(parts, axis):
        return lax.psum_scatter(jnp.stack(parts), axes, scatter_dimension=axis, tiled=True)

    return (
        spread([wq0, wq1], 1),
        spread([vectors(block_c)[0:2], vectors(block_b)[0:2]], 2),
        spread([wo0, wo1], 1),
        spread([wi0, wi1], 1),
        spread([line(block_b), line(block_a)], 1),
        spread([stacked(wf0), stacked(wf1)], 1),
        spread([vectors(block_b)[2:4], vectors(block_a)[2:4]], 2),
        spread([vectors(block_b)[4:8], vectors(block_a)[4:8]], 2),
    )


def solution(mesh):
    placed = (
        P(("dp", "fsdp"), None),
        P(("dp", "fsdp"), None),
        P(("dp", "fsdp"), None),
        P(None, ("dp", "fsdp"), None),
        P(None, None, ("dp", "fsdp")),
        P(None, ("dp", "fsdp"), None),
        P(None, ("dp", "fsdp"), None),
        P(None, ("dp", "fsdp")),
        P(None, ("dp", "fsdp"), None),
        P(None, None, ("dp", "fsdp")),
        P(None, None, ("dp", "fsdp")),
    )
    return jax.shard_map(
        local,
        mesh=mesh,
        in_specs=placed,
        out_specs=(
            P(("dp", "fsdp"), None),
            P(("dp", "fsdp"), None),
            P(None, ("dp", "fsdp"), None),
            P(None, None, ("dp", "fsdp")),
            P(None, ("dp", "fsdp"), None),
            P(None, ("dp", "fsdp"), None),
            P(None, ("dp", "fsdp")),
            P(None, ("dp", "fsdp"), None),
            P(None, None, ("dp", "fsdp")),
            P(None, None, ("dp", "fsdp")),
        ),
        check_vma=False,
    )
```

```python
from functools import partial

import jax
import jax.numpy as jnp
from jax import lax
from jax.experimental import pallas as pl
from jax.experimental.pallas import tpu as pltpu
from jax.sharding import PartitionSpec as P

HEADS = 4
HD = 64
SEQ = 512
PAIR = 2 * HD
EXTRA = 16
HALF = SEQ // 2
HALVES = (slice(0, HALF), slice(HALF, SEQ))
FAR = -(2.0**100)
FLOOR = -1e20
EPSILON = 1e-12
PIECE = 256
SMALL = 128
GROUPS = (4, 8, 8)
DEVICES = 32
LOW = jnp.bfloat16
F32 = jnp.float32
MEMORY = 2**26


def dot_nn(left, right):
    return lax.dot_general(left, right, (((1,), (0,)), ((), ())), preferred_element_type=F32)


def dot_nt(left, right):
    return lax.dot_general(left, right, (((1,), (1,)), ((), ())), preferred_element_type=F32)


def dot_tn(left, right):
    return lax.dot_general(left, right, (((0,), (0,)), ((), ())), preferred_element_type=F32)


def pieces(total, size=PIECE):
    return [pl.ds(start, size) for start in range(0, total, size)]


def three_parts(values):
    first = values.astype(LOW).astype(F32)
    rest = values - first
    second = rest.astype(LOW).astype(F32)
    return first, second, rest - second


BELL = -0.5 / 0.6931471805599453


def gelu_parts(u):
    cumulative = 0.5 + 0.5 * lax.erf(u * 0.7071067811865476)
    slope = cumulative + (u * 0.3989422804014327) * jnp.exp2(u * u * BELL)
    return u * cumulative, slope


def inverse_of(values):
    guess = pl.reciprocal(values, approx=True)
    return guess * (2.0 - values * guess)


def longest_start(lengths_ref, row):
    begin, found = jnp.int32(0), jnp.int32(0)
    for entry in range(lengths_ref.shape[1]):
        size = lengths_ref[row, entry]
        found = jnp.where(size == HALF, begin, found)
        begin = begin + size
    return found


def segments(lengths_ref, row):
    places = lax.broadcasted_iota(jnp.int32, (1, SEQ), 1) + longest_start(lengths_ref, row)
    places = places & (SEQ - 1)
    bound = jnp.int32(0)
    segment = jnp.zeros((1, SEQ), jnp.int32)
    last = lengths_ref.shape[1] - 1
    for entry in range(last):
        bound = bound + lengths_ref[row, entry]
        segment = segment + (places >= bound).astype(jnp.int32)
    return segment, last


def head_rows(head):
    return slice(head * HD, (head + 1) * HD)


def attention_forward(row, lengths_ref, x, wt_ref, bias_ref, qa_ref, ka_ref, va_ref, ob_ref, lse_ref, s_ref, p_ref):
    width = HEADS * HD
    segment, last = segments(lengths_ref, row)
    pad = (segment == last).astype(F32)
    line = lax.broadcasted_iota(jnp.int32, (EXTRA, SEQ), 0)
    aug_q = jnp.where(line == segment, 1.0, 0.0).astype(LOW)
    seen = (line == segment) & (segment != last)
    aug_k = jnp.where(seen | (line > last), 0.0, FAR).astype(LOW)
    aug_v = jnp.where(line == 0, 1.0, 0.0).astype(LOW)
    rest = jnp.zeros((PAIR - HD - EXTRA, SEQ), LOW)
    for head in range(HEADS):
        qa_ref[head, HD : HD + EXTRA] = aug_q
        ka_ref[head, HD : HD + EXTRA] = aug_k
        va_ref[head, HD : HD + EXTRA] = aug_v
        qa_ref[head, HD + EXTRA : PAIR] = rest
        ka_ref[head, HD + EXTRA : PAIR] = rest
    for block, ref in enumerate((qa_ref, ka_ref, va_ref)):
        lines = slice(block * width, (block + 1) * width)
        bias = bias_ref[lines]
        value = dot_nt(wt_ref[lines], x) + jnp.concatenate([bias] * (SEQ // 128), 1)
        if block == 0:
            value = value * HD**-0.5
        value = value.astype(LOW)
        for head in range(HEADS):
            ref[head, 0:HD] = value[head_rows(head)]
        yield

    def scores(head):
        for half in HALVES:
            s_ref[head % 2, half] = dot_tn(ka_ref[head, :, half], qa_ref[head, :, half])

    def softmax(head):
        tops = []
        for half in HALVES:
            tops.append(jnp.maximum(jnp.max(s_ref[head % 2, half], 0, keepdims=True), FLOOR))
            p_ref[head % 2, half] = jnp.exp(s_ref[head % 2, half] - tops[-1]).astype(LOW)
        return tops

    scores(0)
    yield
    for head in range(HEADS):
        if head + 1 < HEADS:
            scores(head + 1)
            yield
        tops = softmax(head)
        yield
        for half, top in zip(HALVES, tops):
            out = dot_nn(va_ref[head, :, half], p_ref[head % 2, half])
            alone = pad[:, half]
            total = out[HD : HD + 1] + alone
            lse_ref[head : head + 1, half] = jnp.where(alone > 0, 0.0, top + jnp.log(total))
            own = alone * va_ref[head, 0:HD, half].astype(F32)
            ob_ref[head_rows(head), half] = (out[0:HD] * inverse_of(total) + own).astype(LOW)
        yield


def normal(values):
    centred = values - jnp.mean(values, -1, keepdims=True)
    inverse = lax.rsqrt(jnp.mean(centred * centred, -1, keepdims=True) + EPSILON)
    return centred * inverse, inverse


def normal_back(cotangent, unit, inverse, gains):
    scaled = cotangent * gains
    return inverse * (
        scaled
        - jnp.mean(scaled, -1, keepdims=True)
        - unit * jnp.mean(scaled * unit, -1, keepdims=True)
    )


def dense_forward(x_ref, ob_ref, wo_ref, wi_ref, wf_ref, small_ref, bi_ref, n1_ref, n2_ref, inv_ref, yb_ref, gb_ref, gp_ref, z_ref, work_ref, u_ref):
    small = lambda index: small_ref[pl.ds(index, 1)]
    work_ref[...] = dot_tn(ob_ref[...], wo_ref[...])
    yield
    for place in pieces(SEQ):
        unit, inverse = normal(x_ref[place].astype(F32) + work_ref[place] + small(4))
        n1_ref[place] = unit
        inv_ref[place, pl.ds(0, HD)] = jnp.broadcast_to(inverse, (PIECE, HD))
        y = unit * small(2) + small(5)
        yb_ref[place] = y.astype(LOW)
        work_ref[place] = y + small(6)
        yield
    columns = 256
    count = wi_ref.shape[1] // columns

    def into(step):
        u_ref[step % 2] = dot_nn(yb_ref[...], wi_ref[:, pl.ds(step * columns, columns)])

    into(0)
    yield
    for step in range(count):
        if step + 1 < count:
            into(step + 1)
            yield
        lanes = pl.ds(step * columns, columns)
        for place in pieces(SEQ, SMALL):
            g, slope = gelu_parts(u_ref[step % 2, place] + bi_ref[:, lanes])
            gb_ref[place, lanes] = g.astype(LOW)
            gp_ref[place, lanes] = slope.astype(LOW)
            yield
    work_ref[...] += dot_nn(gb_ref[...], wf_ref[...])
    yield
    for place in pieces(SEQ):
        unit, inverse = normal(work_ref[place])
        n2_ref[place] = unit
        inv_ref[place, pl.ds(HD, HD)] = jnp.broadcast_to(inverse, (PIECE, HD))
        z_ref[place] = (unit * small(3) + small(7)).astype(z_ref.dtype)
        yield


def fold(values):
    return jnp.sum(values.reshape(-1, 8, values.shape[-1]), 0)


def dense_backward(dz_ref, n1_ref, n2_ref, inv_ref, yb_ref, gb_ref, gp_ref, ob_ref, wo_ref, wi_ref, wf_ref, small_ref, dr_ref, dob_ref, gwo_ref, gwi_ref, gwf_ref, gsmall_ref, gbi_ref, low_ref, u_ref, du_ref, turned_ref):
    small = lambda index: small_ref[pl.ds(index, 1)]
    for place in pieces(SEQ):
        dz = dz_ref[place].astype(F32)
        unit = n2_ref[place]
        gsmall_ref[3] += fold(dz * unit)
        gsmall_ref[7] += fold(dz)
        dr = normal_back(dz, unit, inv_ref[place, pl.ds(HD, 1)], small(3))
        dr_ref[place] = dr
        df = dr.astype(LOW)
        low_ref[place] = df
        gsmall_ref[6] += fold(df.astype(F32))
        yield
    columns = 256
    count = wi_ref.shape[1] // columns

    def back(step):
        u_ref[step % 2] = dot_nt(low_ref[...], wf_ref[pl.ds(step * columns, columns)])

    back(0)
    turned_ref[0, 0 : low_ref.shape[1]] = low_ref[...].T
    width = low_ref.shape[1]
    turned_ref[1, 0:width] = yb_ref[...].T
    turned_ref[1, width:] = jnp.ones((EXTRA, SEQ), LOW)
    yield
    for step in range(count):
        if step + 1 < count:
            back(step + 1)
            yield
        lanes = pl.ds(step * columns, columns)
        gwf_ref[:, lanes] += dot_nn(turned_ref[0, 0:width], gb_ref[:, lanes])
        yield
        for place in pieces(SEQ, SMALL):
            du = (u_ref[step % 2, place] * gp_ref[place, lanes].astype(F32)).astype(LOW)
            du_ref[place, lanes] = du
        yield
        product = dot_nn(turned_ref[1], du_ref[:, lanes])
        gwi_ref[:, lanes] += product[0:width]
        gbi_ref[:, lanes] += product[width : width + 8]
        yield
    u_ref[0] = dot_nt(du_ref[...], wi_ref[...])
    yield
    for place in pieces(SEQ):
        dy = dr_ref[place] + u_ref[0, place]
        unit = n1_ref[place]
        gsmall_ref[2] += fold(dy * unit)
        gsmall_ref[5] += fold(dy)
        dr = normal_back(dy, unit, inv_ref[place, pl.ds(0, 1)], small(2))
        dr_ref[place] = dr
        da = dr.astype(LOW)
        low_ref[place] = da
        gsmall_ref[4] += fold(da.astype(F32))
        yield
    gwo_ref[...] += dot_nn(ob_ref[...], low_ref[...])
    dob_ref[...] = dot_nt(wo_ref[...], low_ref[...]).astype(LOW)
    yield


def attention_backward(row, lengths_ref, x, do_ref, ob_ref, qa_ref, ka_ref, va_ref, lse_ref, dqkv_ref, gwq_ref, gbias_ref, p_ref, ds_ref, s_ref):
    width = HEADS * HD
    segment, last = segments(lengths_ref, row)
    pad = (segment == last).astype(F32)

    def scores(head):
        for half in HALVES:
            s_ref[0, head % 2, half] = dot_tn(ka_ref[head, :, half], qa_ref[head, :, half])
            s_ref[1, head % 2, half] = dot_tn(
                va_ref[head, 0:HD, half], do_ref[head_rows(head), half]
            )

    def weigh(head):
        product = do_ref[head_rows(head)].astype(F32) * ob_ref[head_rows(head)].astype(F32)
        centre = jnp.sum(product, 0, keepdims=True)
        for half in HALVES:
            p = jnp.exp(s_ref[0, head % 2, half] - lse_ref[head : head + 1, half])
            p_ref[head % 2, half] = p.astype(LOW)
            ds_ref[head % 2, half] = (p * (s_ref[1, head % 2, half] - centre[:, half])).astype(LOW)

    scores(0)
    yield
    for head in range(HEADS):
        if head + 1 < HEADS:
            scores(head + 1)
            yield
        weigh(head)
        yield
        for half in HALVES:
            ds, do = ds_ref[head % 2, half], do_ref[head_rows(head), half]
            dq = dot_nn(ka_ref[head, 0:HD, half], ds) * HD**-0.5
            dk = dot_nt(qa_ref[head, 0:HD, half], ds)
            dv = dot_nt(do, p_ref[head % 2, half]) + pad[:, half] * do.astype(F32)
            for block, value in enumerate((dq, dk, dv)):
                at = block * width + head * HD
                dqkv_ref[at : at + HD, half] = value.astype(LOW)
        yield
    for index, block in enumerate((0, 2)):
        value = dqkv_ref[block * width : (block + 1) * width].astype(F32)
        parts = [value[:, at : at + 128] for at in range(0, SEQ, 128)]
        gbias_ref[index] += (parts[0] + parts[1]) + (parts[2] + parts[3])
    gwq_ref[...] += dot_nn(dqkv_ref[...], x)
    yield


def unpack_matrix(raw_ref, at, into_ref):
    width = into_ref.shape[0]
    for start in range(0, into_ref.shape[1], width):
        block = raw_ref[:, :, pl.ds(at + start, width)].astype(F32)
        block = block.reshape(GROUPS + (width,)).swapaxes(0, 1).reshape(width, width)
        into_ref[:, pl.ds(start, width)] = block.astype(LOW)


def unpack_stacked(raw_ref, at, into_ref):
    width = into_ref.shape[1]
    count = into_ref.shape[0] // width
    blocks = [
        raw_ref[:, :, pl.ds(at + step * width, width)].astype(F32).reshape(GROUPS + (width,))
        for step in range(count)
    ]
    outer, inner, rows = GROUPS
    for place in range(inner):
        part = jnp.stack([jnp.stack([block[f, place] for block in blocks]) for f in range(outer)])
        size = outer * count * rows
        into_ref[pl.ds(place * size, size)] = part.reshape(size, width).astype(LOW)


def counter(shape, axis):
    return lax.broadcasted_iota(jnp.int32, shape, axis)


def split_by(values, size):
    return lax.shift_right_logical(values, size.bit_length() - 1), values & (size - 1)


def sources(rows):
    outer, inner, height = GROUPS
    group, within = split_by(counter((rows, 1), 0), height)
    far, near = split_by(group, inner)
    return near * outer + far, within


def unpack_vectors(raw_ref, at, layer):
    outer, inner, rows = GROUPS
    total = outer * inner * rows
    raw = raw_ref[:, :, pl.ds(at, 128)].reshape(total, 128)
    owner, place = split_by(counter((1, total), 1), rows)
    pick = jnp.where(counter((128, 1), 0) == rows * layer + place, 1.0, 0.0).astype(LOW)
    device, unused = sources(total)
    spread = jnp.where(owner == device, dot_nn(raw, pick), 0.0)
    return jnp.sum(spread.reshape(outer * inner, rows, total), 0)


def unpack_hidden(raw_ref, at, layer, hidden):
    outer, inner, rows = GROUPS
    total = outer * inner * rows
    raw = raw_ref[:, :, pl.ds(at, 128)].reshape(total, 128)
    owner, place = split_by(counter((1, hidden), 1), hidden // (outer * inner))
    pick = jnp.where(counter((128, 1), 0) == 2 * rows + place, 1.0, 0.0).astype(LOW)
    device, within = sources(total)
    device = jnp.where(within == layer, device, -1)
    spread = jnp.where(owner == device, dot_nn(raw, pick), 0.0)
    return jnp.sum(spread, 0, keepdims=True)


def pack_matrix(sum_ref, sent_ref, at, turned=False):
    width = sum_ref.shape[1 if turned else 0]
    outer, inner, rows = GROUPS
    for start in range(0, sum_ref.shape[0 if turned else 1], width):
        near = pl.ds(start, width)
        block = sum_ref[near].T if turned else sum_ref[:, near]
        block = block.reshape(inner, outer, rows, width)
        block = block.swapaxes(0, 1).reshape(outer, inner * rows, width)
        sent_ref[:, :, pl.ds(at + start, width)] = block.astype(LOW)


def pack_stacked(sum_ref, sent_ref, at):
    width = sum_ref.shape[0]
    outer, inner, rows = GROUPS
    count = sum_ref.shape[1] // width
    near = inner // count
    for step in range(count):
        block = sum_ref[:, pl.ds(step * width, width)].T
        block = block.reshape(near, outer, count, rows, width)
        for part in range(count):
            piece = jnp.stack([block[:, f, part] for f in range(outer)])
            piece = piece.reshape(outer, near * rows, width)
            sent_ref[:, pl.ds(step * near * rows, near * rows), pl.ds(at + part * width, width)] = (
                piece.astype(LOW)
            )


def pack_vectors(block, line, sent_ref, at):
    outer, inner, rows = GROUPS
    total = outer * inner * rows
    device, within = sources(total)
    owner, unused = split_by(counter((1, total), 1), rows)
    spread = jnp.broadcast_to(block[None], (outer * inner, rows, total)).reshape(total, total)
    spread = jnp.where(owner == device, spread, 0.0).astype(LOW)
    unused, place = split_by(counter((total, 1), 0), rows)
    found = dot_nn(spread, jnp.where(counter((1, 128), 1) == place, 1.0, 0.0).astype(LOW))
    if line is not None:
        hidden = line.shape[1]
        height = hidden // (outer * inner)
        owner, unused = split_by(counter((1, hidden), 1), height)
        spread = jnp.where(owner == jnp.where(within == 0, device, -1), line, 0.0).astype(LOW)
        unused, place = split_by(counter((hidden, 1), 0), height)
        pick = jnp.where(counter((1, 128), 1) == 2 * rows + place, 1.0, 0.0).astype(LOW)
        found = found + dot_nn(spread, pick)
    sent_ref[:, :, pl.ds(at, 128)] = found.reshape(outer, inner * rows, 128).astype(LOW)


def bias_rows(gbias_ref):
    width = gbias_ref.shape[1]
    parts = [jnp.sum(gbias_ref[index].T, 0, keepdims=True) for index in range(2)]
    return jnp.concatenate(parts + [jnp.zeros((6, width), F32)], 0)


def pack_dense(gwo_ref, gwi_ref, gwf_ref, gsmall_ref, gbi_ref, block, sent_ref, at):
    width, hidden = gwi_ref.shape
    pack_matrix(gwo_ref, sent_ref, at)
    pack_matrix(gwi_ref, sent_ref, at + width)
    pack_stacked(gwf_ref, sent_ref, at + width + hidden)
    block = jnp.sum(gsmall_ref[...], 1) + block
    pack_vectors(block, gbi_ref[0:1], sent_ref, at + width + 2 * hidden)


def shape_of(array):
    return jax.ShapeDtypeStruct(array.shape, array.dtype)


def by_row(shape, group):
    if len(shape) == 2:
        return pl.BlockSpec((group * SEQ, shape[1]), lambda step: (step, 0))
    return pl.BlockSpec((group,) + tuple(shape[1:]), lambda step: (step,) + (0,) * (len(shape) - 1))


def one_row(ref, member):
    if len(ref.shape) == 2:
        return ref.at[pl.ds(member * SEQ, SEQ)]
    return ref.at[member]


def alternate(runs):
    running = []
    waiting = list(runs)
    while running or waiting:
        if waiting:
            running.append(waiting.pop(0))
        for run in list(running):
            try:
                next(run)
            except StopIteration:
                running.remove(run)


def whole(shape):
    return pl.BlockSpec(tuple(shape), lambda row: (0,) * len(shape))


def run_rows(
    body, lengths, rowwise, fixed, row_outs, sent, shared, private, cost, setup, finish, after=(),
    scalars=(), group=1, moved=8
):
    count = lengths.shape[0]
    group = group if count % group == 0 else 1
    cuts = [len(scalars), len(rowwise), len(fixed), len(after), len(row_outs), len(sent)]
    cuts += [len(shared)] + [len(private)] * group

    def kernel(lengths_ref, *refs):
        step = pl.program_id(0)
        groups = []
        at = 0
        for cut in cuts:
            groups.append(refs[at : at + cut])
            at += cut
        numbers, rows_in, fixed_in, unused, rows_out, sent_out, work = groups[:7]

        @pl.when(step == 0)
        def _():
            setup(numbers, fixed_in, sent_out, work)

        alternate(
            body(
                step * group + member,
                lengths_ref,
                [one_row(ref, member) for ref in rows_in],
                [one_row(ref, member) for ref in rows_out],
                work,
                groups[7 + member],
            )
            for member in range(group)
        )

        if finish:

            @pl.when(step == count // group - 1)
            def _():
                finish(numbers, work, sent_out)

    return pl.pallas_call(
        kernel,
        grid=(count // group,),
        in_specs=[pl.BlockSpec(memory_space=pltpu.SMEM)] * (1 + len(scalars))
        + [by_row(array.shape, group) for array in rowwise]
        + [whole(array.shape) for array in fixed]
        + [pl.BlockSpec(memory_space=pl.ANY) for array in after],
        out_specs=[by_row(part.shape, group) for part in row_outs]
        + [whole(part.shape) for part in sent],
        out_shape=list(row_outs) + list(sent),
        scratch_shapes=list(shared) + list(private) * group,
        compiler_params=pltpu.CompilerParams(
            dimension_semantics=("arbitrary",), vmem_limit_bytes=MEMORY
        ),
        cost_estimate=pl.CostEstimate(
            flops=cost, bytes_accessed=moved * 2**20, transcendentals=0
        ),
    )(lengths, *scalars, *rowwise, *fixed, *after)


def struct(shape, dtype):
    return jax.ShapeDtypeStruct(tuple(shape), dtype)


FORWARD_SCRATCH = lambda: [
    pltpu.VMEM((2, SEQ, HALF), F32),
    pltpu.VMEM((2, SEQ, HALF), LOW),
]
BACKWARD_SCRATCH = lambda: [
    pltpu.VMEM((2, SEQ, HALF), LOW),
    pltpu.VMEM((2, SEQ, HALF), LOW),
    pltpu.VMEM((2, 2, SEQ, HALF), F32),
    pltpu.VMEM((3 * HEADS * HD, SEQ), LOW),
]


def attention_outs(rows, width):
    return [
        struct((rows, HEADS, PAIR, SEQ), LOW),
        struct((rows, HEADS, PAIR, SEQ), LOW),
        struct((rows, HEADS, HD + EXTRA, SEQ), LOW),
        struct((rows, width, SEQ), LOW),
        struct((rows, 8, SEQ), F32),
    ]


def dense_outs(tokens, width, hidden):
    return [
        struct((tokens, width), F32),
        struct((tokens, width), F32),
        struct((tokens, PAIR), F32),
        struct((tokens, width), LOW),
        struct((tokens, hidden), LOW),
        struct((tokens, hidden), LOW),
    ]


def vmem(shape, dtype):
    return pltpu.VMEM(tuple(shape), dtype)


def attention_weights(width):
    return [vmem((width, 3 * width), LOW), vmem((3 * width, width), LOW), vmem((3 * width, 128), F32)]


def dense_weights(width, hidden):
    return [
        vmem((width, width), LOW),
        vmem((width, hidden), LOW),
        vmem((hidden, width), LOW),
        vmem((8, width), F32),
        vmem((1, hidden), F32),
    ]


def dense_sums(width, hidden):
    return [
        vmem((width, width), F32),
        vmem((width, hidden), F32),
        vmem((width, hidden), F32),
        vmem((8, 8, width), F32),
        vmem((8, hidden), F32),
    ]


def attention_sums(width):
    return [vmem((3 * width, width), F32), vmem((2, width, 128), F32)]


def dense_work(width, hidden):
    return [
        vmem((SEQ, width), LOW),
        vmem((2, SEQ, width), F32),
        vmem((SEQ, hidden), LOW),
        vmem((2, width + EXTRA, SEQ), LOW),
    ]


def set_attention(layer, urgent_ref, raw_ref, at, wq_ref, wt_ref, bias_ref):
    width = wq_ref.shape[0]
    unpack_matrix(raw_ref, at, wq_ref)
    vectors = unpack_vectors(urgent_ref, 3 * width, layer)
    for block, line in enumerate((vectors[0:1], jnp.zeros((1, width), F32), vectors[1:2])):
        lines = pl.ds(block * width, width)
        wt_ref[lines] = wq_ref[:, lines].astype(F32).T.astype(LOW)
        bias_ref[lines] = jnp.broadcast_to(line, (128, width)).T


def set_dense(layer, urgent_ref, raw_ref, at, wo_ref, wi_ref, wf_ref, small_ref, bi_ref):
    width, hidden = wi_ref.shape
    unpack_matrix(raw_ref, at, wo_ref)
    unpack_matrix(raw_ref, at + width, wi_ref)
    unpack_stacked(raw_ref, at + width + hidden, wf_ref)
    small_ref[...] = unpack_vectors(urgent_ref, 3 * width, layer)
    bi_ref[...] = unpack_hidden(urgent_ref, 3 * width, layer, hidden)


def clear(refs):
    for ref in refs:
        ref[...] = jnp.zeros(ref.shape, ref.dtype)


def assemble(place_ref, part_refs, into_ref):
    for step, ref in enumerate(part_refs):
        into_ref[place_ref[0] ^ step] = ref[...]


def raw_block(parts):
    return vmem((len(parts),) + parts[0].shape, LOW)


def turned_back(lengths_ref, row, values):
    return pltpu.roll(values, longest_start(lengths_ref, row), 0).astype(LOW)


def rotate_kernel(lengths, arrays):
    def body(row, lengths_ref, rowwise, outs, work, own):
        back = (SEQ - longest_start(lengths_ref, row)) & (SEQ - 1)
        for source, target in zip(rowwise, outs):
            target[...] = pltpu.roll(source[...].astype(F32), back, 0).astype(LOW)
            yield

    return run_rows(
        body, lengths, list(arrays), [], [struct(array.shape, LOW) for array in arrays], [], [], [],
        10**6, lambda *refs: None, None,
    )


def first_kernel(lengths, x, place, parts):
    rows, (tokens, width) = lengths.shape[0], x.shape

    def setup(numbers, fixed, sent, work):
        assemble(numbers[0], fixed, sent[0])
        set_attention(0, sent[0], sent[0], 0, *work)

    def body(row, lengths_ref, rowwise, outs, work, own):
        return attention_forward(row, lengths_ref, rowwise[0][...], *work[1:3], *outs, *own)

    return run_rows(
        body, lengths, [x], list(parts), attention_outs(rows, width),
        [struct((len(parts),) + parts[0].shape, LOW)],
        attention_weights(width), FORWARD_SCRATCH(), 4 * 10**9, setup, None, (), [place],
    )


def attention_kernel(layer, lengths, x, place, urgent, parts, at):
    rows, (tokens, width) = lengths.shape[0], x.shape

    def setup(numbers, fixed, sent, work):
        assemble(numbers[0], fixed[1:], work[3])
        set_attention(layer, fixed[0], work[3], at, *work[:3])

    def body(row, lengths_ref, rowwise, outs, work, own):
        return attention_forward(
            row, lengths_ref, rowwise[0][...].astype(LOW), *work[1:3], *outs, *own
        )

    return run_rows(
        body, lengths, [x], [urgent] + list(parts), attention_outs(rows, width), [],
        attention_weights(width) + [raw_block(parts)], FORWARD_SCRATCH(),
        4 * 10**9, setup, None, (), [place],
    )


def dense_kernel(layer, lengths, x, ob, place, urgent, parts, at, hidden):
    tokens, width = x.shape

    def setup(numbers, fixed, sent, work):
        assemble(numbers[0], fixed[1:], work[5])
        set_dense(layer, fixed[0], work[5], at, *work[:5])

    def body(row, lengths_ref, rowwise, outs, work, own):
        return dense_forward(*rowwise, *work[:5], *outs, *own)

    return run_rows(
        body, lengths, [x, ob], [urgent] + list(parts),
        dense_outs(tokens, width, hidden) + [struct((tokens, width), F32)], [],
        dense_weights(width, hidden) + [raw_block(parts)],
        [vmem((SEQ, width), F32), vmem((2, SEQ, width), F32)],
        5 * 10**9, setup, None, (), [place],
    )


def turn_kernel(layer, lengths, x, ob, cotangent, place, urgent, parts, at, hidden):
    tokens, width = x.shape
    columns = width + 2 * hidden + 128

    def setup(numbers, fixed, sent, work):
        assemble(numbers[0], fixed[1:], work[11])
        set_dense(layer, fixed[0], work[11], at, *work[:5])
        clear(work[5:10])

    def body(row, lengths_ref, rowwise, outs, work, own):
        x_ref, ob_ref, dz_ref = rowwise
        z_ref, dr_ref, dob_ref = outs
        weights, sums = work[:5], work[5:10]
        kept, work_ref, back = own[:6], own[6], own[7:]
        yield from dense_forward(x_ref, ob_ref, *weights, *kept, z_ref, work_ref, back[1])
        yield from dense_backward(dz_ref, *kept, ob_ref, *weights[:4], dr_ref, dob_ref, *sums, *back)

    def finish(numbers, work, sent):
        pack_dense(*work[5:10], 0.0, work[10], 0)
        hand_out(numbers[0], work[10], sent)

    kept = [vmem((SEQ,) + part.shape[1:], part.dtype) for part in dense_outs(tokens, width, hidden)]
    return run_rows(
        body, lengths, [x, ob, cotangent], [urgent] + list(parts),
        [struct((tokens, width), LOW), struct((tokens, width), F32), struct((tokens // SEQ, width, SEQ), LOW)],
        [struct((64, columns), LOW)] * 4,
        dense_weights(width, hidden) + dense_sums(width, hidden)
        + [vmem((4, 64, columns), LOW), raw_block(parts)],
        kept + [vmem((SEQ, width), F32)] + dense_work(width, hidden),
        10**10, setup, finish, (), [place], 2,
    )


def hand_out(place_ref, packed_ref, sent):
    for step, ref in enumerate(sent):
        ref[...] = packed_ref[place_ref[0] ^ step]


def middle_kernel(lengths, upper, lower, place, urgent, parts, hidden, after):
    tokens, width = upper[0].shape
    columns = 4 * width + 2 * hidden + 128

    def setup(numbers, fixed, sent, work):
        assemble(numbers[0], fixed[1:], work[16])
        set_attention(1, fixed[0], work[16], 0, *work[:3])
        set_dense(0, fixed[0], work[16], 3 * width, *work[3:8])
        clear(work[8:15])

    def body(row, lengths_ref, rowwise, outs, work, own):
        up, low = rowwise[:8], rowwise[8:]
        dx_ref = own[0]
        yield from attention_backward(
            row, lengths_ref, up[0][...].astype(LOW), *up[1:7], own[-1], *work[8:10], *own[5:-1]
        )
        dx_ref[...] = up[7][...] + dot_tn(own[-1][...], work[1][...])
        yield
        yield from dense_backward(dx_ref, *low, *work[3:7], *outs, *work[10:15], *own[1:5])

    def finish(numbers, work, sent):
        pack_matrix(work[8], work[15], 0, True)
        pack_dense(*work[10:15], bias_rows(work[9]), work[15], 3 * width)
        hand_out(numbers[0], work[15], sent)

    return run_rows(
        body, lengths, list(upper) + list(lower), [urgent] + list(parts),
        [struct((tokens, width), F32), struct((tokens // SEQ, width, SEQ), LOW)],
        [struct((64, columns), LOW)] * 4,
        attention_weights(width) + dense_weights(width, hidden)
        + attention_sums(width) + dense_sums(width, hidden)
        + [vmem((4, 64, columns), LOW), raw_block(parts)],
        [vmem((SEQ, width), F32)] + dense_work(width, hidden) + BACKWARD_SCRATCH(),
        15 * 10**9, setup, finish, after, [place], 2,
    )


def last_kernel(lengths, upper, after, place):
    tokens, width = upper[0].shape

    def setup(numbers, fixed, sent, work):
        clear(work[:2])

    def body(row, lengths_ref, rowwise, outs, work, own):
        return attention_backward(
            row, lengths_ref, rowwise[0][...], *rowwise[1:], outs[0], *work[:2], *own
        )

    def finish(numbers, work, sent):
        pack_matrix(work[0], work[2], 0, True)
        pack_vectors(bias_rows(work[1]), None, work[2], 3 * width)
        hand_out(numbers[0], work[2], sent)

    return run_rows(
        body, lengths, list(upper), [], [struct((tokens // SEQ, 3 * width, SEQ), LOW)],
        [struct((64, 3 * width + 128), LOW)] * 4,
        attention_sums(width) + [vmem((4, 64, 3 * width + 128), LOW)],
        BACKWARD_SCRATCH()[:-1], 8 * 10**9, setup, finish, after, [place], 2,
    )


def outward_kernel(lengths, z, after):
    def body(row, lengths_ref, rowwise, outs, work, own):
        outs[0][...] = turned_back(lengths_ref, row, rowwise[0][...].astype(F32))
        yield

    (found,) = run_rows(
        body, lengths, [z], [], [struct(z.shape, LOW)], [], [], [], 3 * 10**9,
        lambda *refs: None, None, after,
    )
    return found


def inward_kernel(lengths, dqkv, dr, urgent, after):
    tokens, width = dr.shape

    def setup(numbers, fixed, sent, work):
        set_attention(0, fixed[0], fixed[0], 0, *work)

    def body(row, lengths_ref, rowwise, outs, work, own):
        dqkv_ref, dr_ref = rowwise
        dx = dr_ref[...] + dot_tn(dqkv_ref[...], work[1][...])
        outs[0][...] = turned_back(lengths_ref, row, dx)
        yield

    (found,) = run_rows(
        body, lengths, [dqkv, dr], [urgent], [struct((tokens, width), LOW)], [],
        attention_weights(width), [], 10**9, setup, None, after, moved=6,
    )
    return found


def hold(array, after):
    def kernel(*refs):
        pass

    anywhere = pl.BlockSpec(memory_space=pl.ANY)
    return pl.pallas_call(
        kernel,
        in_specs=[anywhere] * (1 + len(after)),
        out_specs=anywhere,
        out_shape=shape_of(array),
        input_output_aliases={0: 0},
    )(array, *after)


def pack_parameters(
    attn_weight, attn_bias, out_weight, ffn_in, ffn_in_bias, ffn_out, norm_gain, shifts
):
    depth, rows, width = out_weight.shape
    copies = GROUPS[1]
    hidden = ffn_in.shape[2]
    dense = width + 2 * hidden
    height = ffn_in_bias.shape[1]

    def kernel(wq_ref, ab_ref, wo_ref, wi_ref, bi_ref, wf_ref, gain_ref, shift_ref, first_ref, rest_ref, small_ref):
        def put(ref, block, at):
            block = jnp.broadcast_to(block.astype(F32)[None], (copies,) + block.shape)
            block = block.reshape(copies * block.shape[1], block.shape[2])
            ref[:, pl.ds(at, block.shape[1])] = block.astype(LOW)

        small_ref[...] = jnp.zeros(small_ref.shape, F32)
        for layer in range(depth):
            lanes = pl.ds(rows * layer, rows)
            small_ref[0:2, lanes] = ab_ref[layer].astype(F32)
            small_ref[2:4, lanes] = gain_ref[layer].astype(F32)
            small_ref[4:8, lanes] = shift_ref[layer].astype(F32)
        small_ref[0:depth, pl.ds(2 * rows, height)] = bi_ref[...].astype(F32)
        put(first_ref, wq_ref[0], 0)
        put(first_ref, small_ref[...], 3 * width)
        put(first_ref, wq_ref[1], 3 * width + 128)
        for layer, ref, at in ((0, first_ref, 6 * width + 128), (1, rest_ref, 0)):
            put(ref, wo_ref[layer], at)
            put(ref, wi_ref[layer], at + width)
            at += width + hidden
            down = wf_ref[layer].astype(F32)
            for step in range(hidden // width):
                put(ref, down[step * rows : (step + 1) * rows], at)
                at += width

    return pl.pallas_call(
        kernel,
        in_specs=[pl.BlockSpec(memory_space=pltpu.VMEM)] * 8,
        out_shape=[
            struct((copies * rows, 6 * width + 128 + dense), LOW),
            struct((copies * rows, dense), LOW),
        ],
        scratch_shapes=[vmem((rows, 128), F32)],
        compiler_params=pltpu.CompilerParams(vmem_limit_bytes=MEMORY),
    )(attn_weight, attn_bias, out_weight, ffn_in, ffn_in_bias, ffn_out, norm_gain, shifts)


def add_parts(place, parts, halves, after=()):
    lanes = parts[0].shape[1]
    count = len(parts)
    many, rows = GROUPS[1:]
    outs = 2 if halves else 1

    def kernel(place_ref, *refs):
        out_refs, sum_ref = refs[count + len(after) : -1], refs[-1]
        bit = place_ref[0] & 1
        for start in range(0, lanes, 128):
            near = pl.ds(start, 128)
            total = refs[0][:, near].astype(F32)
            for ref in refs[1:count]:
                total = total + ref[:, near].astype(F32)
            if halves:
                sum_ref[:, :, near] = total.reshape(many, rows, 128)
            else:
                out_refs[0][:, near] = total.astype(LOW)
        for side, ref in enumerate(out_refs if halves else ()):
            for start in range(0, lanes, 128):
                near = pl.ds(start, 128)
                block = [sum_ref[2 * step + (bit ^ side), :, near] for step in range(many // 2)]
                ref[:, near] = jnp.concatenate(block, 0).astype(LOW)

    return pl.pallas_call(
        kernel,
        in_specs=[pl.BlockSpec(memory_space=pltpu.SMEM)]
        + [pl.BlockSpec(memory_space=pltpu.VMEM)] * count
        + [pl.BlockSpec(memory_space=pl.ANY)] * len(after),
        out_shape=[struct((many * rows // outs, lanes), LOW)] * outs,
        scratch_shapes=[vmem((many, rows, lanes), F32)],
        compiler_params=pltpu.CompilerParams(vmem_limit_bytes=MEMORY),
    )(place, *parts, *after)


def add_halves(place, pairs, after=()):
    many, rows = GROUPS[1] // 2, GROUPS[2]
    widths = [pair[0].shape[1] for pair in pairs]
    lanes = sum(widths)

    def kernel(place_ref, *refs):
        out_refs, sum_ref = refs[2 * len(pairs) + len(after) : -1], refs[-1]
        at = 0
        for index, size in enumerate(widths):
            for start in range(0, size, 128):
                near = pl.ds(start, 128)
                total = refs[2 * index][:, near].astype(F32) + refs[2 * index + 1][:, near].astype(F32)
                sum_ref[:, :, pl.ds(at + start, 128)] = total.reshape(many, rows, 128)
            at += size
        far = lax.shift_right_logical(place_ref[0], 1)
        for step, ref in enumerate(out_refs):
            ref[...] = sum_ref[far ^ step].astype(LOW)

    return pl.pallas_call(
        kernel,
        in_specs=[pl.BlockSpec(memory_space=pltpu.SMEM)]
        + [pl.BlockSpec(memory_space=pltpu.VMEM)] * (2 * len(pairs))
        + [pl.BlockSpec(memory_space=pl.ANY)] * len(after),
        out_shape=[struct((rows, lanes), LOW)] * many,
        scratch_shapes=[vmem((many, rows, lanes), F32)],
        compiler_params=pltpu.CompilerParams(vmem_limit_bytes=MEMORY),
    )(place, *(part for pair in pairs for part in pair), *after)


def write_gradients(found, depth, width, hidden, after):
    rows = GROUPS[2]
    height = hidden // DEVICES
    dense = width + 2 * hidden

    def kernel(*refs):
        found_refs, refs = refs[: len(found)], refs[len(found) + len(after) :]
        gwq_ref, gab_ref, gwo_ref, gwi_ref, gbi_ref, gwf_ref, gain_ref, shift_ref = refs

        def total(at, columns):
            value = found_refs[0][:, pl.ds(at, columns)].astype(F32)
            for ref in found_refs[1:]:
                value = value + ref[:, pl.ds(at, columns)].astype(F32)
            return value

        first, second = dense + 128, 2 * dense + 3 * width + 256
        blocks = [total(at, 128) for at in (dense, first + 3 * width + dense, second + 3 * width)]
        for layer, at, block in ((0, second, blocks[2]), (1, first, blocks[1])):
            gwq_ref[layer] = total(at, 3 * width)
            gab_ref[layer] = block[0:2, 0:rows]
        for layer, at, block in ((0, first + 3 * width, blocks[1]), (1, 0, blocks[0])):
            gwo_ref[layer] = total(at, width)
            gwi_ref[layer] = total(at + width, hidden)
            for step in range(hidden // width):
                gwf_ref[layer, pl.ds(step * rows, rows)] = total(
                    at + width + hidden + step * width, width
                )
            gain_ref[layer] = block[2:4, 0:rows]
            shift_ref[layer] = block[4:8, 0:rows]
            gbi_ref[pl.ds(layer, 1)] = pltpu.roll(block, 128 - 2 * rows, 1)[0:1, 0:height]

    outs = [
        struct((depth, rows, 3 * width), F32),
        struct((depth, 2, rows), F32),
        struct((depth, rows, width), F32),
        struct((depth, rows, hidden), F32),
        struct((depth, height), F32),
        struct((depth, height, width), F32),
        struct((depth, 2, rows), F32),
        struct((depth, 4, rows), F32),
    ]
    return pl.pallas_call(
        kernel,
        in_specs=[pl.BlockSpec(memory_space=pltpu.VMEM)] * len(found)
        + [pl.BlockSpec(memory_space=pl.ANY)] * len(after),
        out_shape=outs,
        compiler_params=pltpu.CompilerParams(vmem_limit_bytes=MEMORY),
    )(*found, *after)


def exchange(parts, axis):
    return lax.all_to_all(parts, axis, 0, 0, tiled=True)


def swap(part, axis, step):
    size = lax.axis_size(axis)
    return lax.ppermute(part, axis, [(source, source ^ step) for source in range(size)])


def local(
    hidden_in,
    lengths,
    grad_out,
    attn_weight,
    attn_bias,
    out_weight,
    ffn_in,
    ffn_in_bias,
    ffn_out,
    norm_gain,
    shifts,
):
    depth, rows, width = out_weight.shape
    hidden = ffn_in.shape[2]
    first, second = lax.axis_size("dp"), lax.axis_size("fsdp")
    fits = (second, first, rows) == GROUPS
    urgent_size = 3 * width + 128
    if fits:
        early, later = pack_parameters(
            attn_weight, attn_bias, out_weight, ffn_in, ffn_in_bias, ffn_out, norm_gain, shifts
        )
        across = lax.axis_index("dp").astype(jnp.int32).reshape(1)
        place = lax.axis_index("fsdp").astype(jnp.int32).reshape(1)
        partners = range(1, second)
        x0, dz1 = rotate_kernel(lengths, (hidden_in, grad_out))
        early = hold(exchange(early, "dp"), (x0,))
        urgent = early[:, :urgent_size]
        urgent = [urgent] + [swap(urgent, "fsdp", step) for step in partners]
        raw0 = early[:, urgent_size:]
        raw0 = [raw0, swap(raw0, "fsdp", 1), swap(raw0, "fsdp", 2)]
    else:
        urgent, raw0, raw1 = gather_other(
            attn_weight, attn_bias, out_weight, ffn_in, ffn_in_bias, ffn_out, norm_gain, shifts
        )
        urgent, raw0, raw1 = ([part[step] for step in range(4)] for part in (urgent, raw0, raw1))
        place = jnp.zeros((1,), jnp.int32)
        x0, dz1 = rotate_kernel(lengths, (hidden_in, grad_out))

    qa0, ka0, va0, ob0, lse0, urgent = first_kernel(lengths, x0, place, urgent)
    if fits:
        raw0[2] = hold(raw0[2], (ob0,))
        raw0.append(swap(raw0[2], "fsdp", 1))
        later = exchange(hold(later, (ob0,)), "dp")
    n1, n2, inv, yb, gb, gp, z0 = dense_kernel(
        0, lengths, x0, ob0, place, urgent, raw0, 3 * width, hidden
    )
    if fits:
        raw1 = hold(later, (z0,))
        raw1 = [raw1, swap(raw1, "fsdp", 1), swap(raw1, "fsdp", 2)]
    qa1, ka1, va1, ob1, lse1 = attention_kernel(1, lengths, z0, place, urgent, raw0, 0)
    if fits:
        raw1[2] = hold(raw1[2], (ob1,))
        raw1.append(swap(raw1[2], "fsdp", 1))
    z1, dr1, dob1, *sent_a = turn_kernel(
        1, lengths, z0, ob1, dz1, place, urgent, raw1, 0, hidden
    )
    dr0, dob0, *sent_b = middle_kernel(
        lengths,
        (z0, dob1, ob1, qa1, ka1, va1, lse1, dr1),
        (n1, n2, inv, yb, gb, gp, ob0),
        place,
        urgent,
        raw0,
        hidden,
        (sent_a[0],),
    )
    if fits:
        got_a = [sent_a[0]] + [swap(sent_a[step], "fsdp", step) for step in partners]
        keep_a, give_a = add_parts(across, got_a, True, (sent_b[0],))
        got_ax = swap(give_a, "dp", 1)
        ready = (sent_b[0], keep_a)
    else:
        ready = ()
    dqkv, *sent_c = last_kernel(
        lengths, (x0, dob0, ob0, qa0, ka0, va0, lse0), ready, place
    )
    if fits:
        got_b = [sent_b[0]] + [swap(sent_b[step], "fsdp", step) for step in partners]
        got_c = [sent_c[0]] + [swap(sent_c[step], "fsdp", step) for step in partners]
        keep_b, give_b = add_parts(across, got_b, True, (got_ax, dqkv))
        keep_c, give_c = add_parts(across, got_c, True, (keep_b,))
        grad_in = inward_kernel(lengths, dqkv, dr0, urgent, (keep_c,))
        pairs = [(keep_a, got_ax), (keep_b, swap(give_b, "dp", 1)), (keep_c, swap(give_c, "dp", 1))]
        found = add_halves(across, pairs, (grad_in,))
        hidden_out = outward_kernel(lengths, z1, (found[0],))
        found = [found[0]] + [swap(found[step], "dp", 2 * step) for step in range(1, first // 2)]
        grads = write_gradients(found, depth, width, hidden, (hidden_out,))
    else:
        grad_in = inward_kernel(lengths, dqkv, dr0, urgent, ())
        hidden_out = outward_kernel(lengths, z1, ())
        grads = scatter_other(
            *(jnp.stack(part) for part in (sent_a, sent_b, sent_c)), rows, width, hidden
        )
    return (hidden_out, grad_in, *grads)


def gather_other(
    attn_weight, attn_bias, out_weight, ffn_in, ffn_in_bias, ffn_out, norm_gain, shifts
):
    axes = ("dp", "fsdp")
    gather = lambda part, axis: lax.all_gather(part, axes, axis=axis, tiled=True)
    depth, unused, width = out_weight.shape
    hidden = ffn_in.shape[2]
    outer, inner, rows = GROUPS
    vectors = gather(jnp.concatenate([attn_bias, norm_gain, shifts], 1), 2)
    line = gather(ffn_in_bias, 1)

    def order(natural):
        return (
            natural.reshape(inner, outer, rows, -1).swapaxes(0, 1).reshape(outer, inner * rows, -1)
        )

    def stacked(part):
        part = part.reshape(DEVICES, -1, rows, width)
        return order(part.swapaxes(1, 2).reshape(width, -1))

    small = vectors.reshape(depth, 8, DEVICES, rows).transpose(2, 1, 0, 3).reshape(width, -1)
    line = line.reshape(depth, DEVICES, -1).swapaxes(0, 1)
    line = jnp.pad(line, ((0, 0), (0, 8 - depth), (0, 0))).reshape(width, -1)
    small = jnp.concatenate([small, line], 1)
    small = jnp.pad(small, ((0, 0), (0, 128 - small.shape[1])))
    wq, wo, wi, wf = (gather(part, 1) for part in (attn_weight, out_weight, ffn_in, ffn_out))
    urgent = jnp.concatenate([order(wq[0]), order(small)], 2)
    raw0 = jnp.concatenate([order(wq[1]), order(wo[0]), order(wi[0]), stacked(wf[0])], 2)
    raw1 = jnp.concatenate([order(wo[1]), order(wi[1]), stacked(wf[1])], 2)
    return urgent, raw0, raw1


def scatter_other(sent_a, sent_b, sent_c, own_rows, width, hidden):
    outer, inner, rows = GROUPS
    axes = ("dp", "fsdp")

    def natural(part):
        return part.reshape(outer, inner, rows, -1).swapaxes(0, 1).reshape(width, -1).astype(F32)

    def cut(part, sizes):
        found, at = [], 0
        for size in sizes:
            found.append(part[:, at : at + size])
            at += size
        return found

    dense = [width, hidden, hidden, 128]
    wq0, block_c = cut(natural(sent_c), [3 * width, 128])
    wq1, wo0, wi0, wf0, block_b = cut(natural(sent_b), [3 * width] + dense)
    wo1, wi1, wf1, block_a = cut(natural(sent_a), dense)

    def vectors(block):
        block = block.reshape(DEVICES, rows, 128)
        return block[:, :, :rows].swapaxes(0, 1).reshape(rows, width)

    def line(block):
        block = block.reshape(DEVICES, rows, 128)
        return block[:, 0, 2 * rows : 2 * rows + hidden // DEVICES].reshape(-1)

    def stacked(part):
        part = part.reshape(DEVICES, rows, -1, width).swapaxes(1, 2)
        return part.reshape(hidden, width)

    def spread(parts, axis):
        return lax.psum_scatter(jnp.stack(parts), axes, scatter_dimension=axis, tiled=True)

    return (
        spread([wq0, wq1], 1),
        spread([vectors(block_c)[0:2], vectors(block_b)[0:2]], 2),
        spread([wo0, wo1], 1),
        spread([wi0, wi1], 1),
        spread([line(block_b), line(block_a)], 1),
        spread([stacked(wf0), stacked(wf1)], 1),
        spread([vectors(block_b)[2:4], vectors(block_a)[2:4]], 2),
        spread([vectors(block_b)[4:8], vectors(block_a)[4:8]], 2),
    )


def solution(mesh):
    placed = (
        P(("dp", "fsdp"), None),
        P(("dp", "fsdp"), None),
        P(("dp", "fsdp"), None),
        P(None, ("dp", "fsdp"), None),
        P(None, None, ("dp", "fsdp")),
        P(None, ("dp", "fsdp"), None),
        P(None, ("dp", "fsdp"), None),
        P(None, ("dp", "fsdp")),
        P(None, ("dp", "fsdp"), None),
        P(None, None, ("dp", "fsdp")),
        P(None, None, ("dp", "fsdp")),
    )
    return jax.shard_map(
        local,
        mesh=mesh,
        in_specs=placed,
        out_specs=(
            P(("dp", "fsdp"), None),
            P(("dp", "fsdp"), None),
            P(None, ("dp", "fsdp"), None),
            P(None, None, ("dp", "fsdp")),
            P(None, ("dp", "fsdp"), None),
            P(None, ("dp", "fsdp"), None),
            P(None, ("dp", "fsdp")),
            P(None, ("dp", "fsdp"), None),
            P(None, None, ("dp", "fsdp")),
            P(None, None, ("dp", "fsdp")),
        ),
        check_vma=False,
    )
```

```python
from functools import partial

import jax
import jax.numpy as jnp
from jax import lax
from jax.experimental import pallas as pl
from jax.experimental.pallas import tpu as pltpu
from jax.sharding import PartitionSpec as P

HEADS = 4
HD = 64
SEQ = 512
PAIR = 2 * HD
EXTRA = 16
HALF = SEQ // 2
HALVES = (slice(0, HALF), slice(HALF, SEQ))
FAR = -(2.0**100)
FLOOR = -1e20
EPSILON = 1e-12
PIECE = 256
SMALL = 64
GROUPS = (4, 8, 8)
DEVICES = 32
LOW = jnp.bfloat16
F32 = jnp.float32
MEMORY = 2**26


def dot_nn(left, right):
    return lax.dot_general(left, right, (((1,), (0,)), ((), ())), preferred_element_type=F32)


def dot_nt(left, right):
    return lax.dot_general(left, right, (((1,), (1,)), ((), ())), preferred_element_type=F32)


def dot_tn(left, right):
    return lax.dot_general(left, right, (((0,), (0,)), ((), ())), preferred_element_type=F32)


def pieces(total, size=PIECE):
    return [pl.ds(start, size) for start in range(0, total, size)]


def three_parts(values):
    first = values.astype(LOW).astype(F32)
    rest = values - first
    second = rest.astype(LOW).astype(F32)
    return first, second, rest - second


BELL = -0.5 / 0.6931471805599453


def gelu_parts(u):
    cumulative = 0.5 + 0.5 * lax.erf(u * 0.7071067811865476)
    slope = cumulative + (u * 0.3989422804014327) * jnp.exp2(u * u * BELL)
    return u * cumulative, slope


def inverse_of(values):
    guess = pl.reciprocal(values, approx=True)
    return guess * (2.0 - values * guess)


def longest_start(lengths_ref, row):
    begin, found = jnp.int32(0), jnp.int32(0)
    for entry in range(lengths_ref.shape[1]):
        size = lengths_ref[row, entry]
        found = jnp.where(size == HALF, begin, found)
        begin = begin + size
    return found


def segments(lengths_ref, row):
    places = lax.broadcasted_iota(jnp.int32, (1, SEQ), 1) + longest_start(lengths_ref, row)
    places = places & (SEQ - 1)
    bound = jnp.int32(0)
    segment = jnp.zeros((1, SEQ), jnp.int32)
    last = lengths_ref.shape[1] - 1
    for entry in range(last):
        bound = bound + lengths_ref[row, entry]
        segment = segment + (places >= bound).astype(jnp.int32)
    return segment, last


def head_rows(head):
    return slice(head * HD, (head + 1) * HD)


def attention_forward(row, lengths_ref, x, wt_ref, bias_ref, qa_ref, ka_ref, va_ref, ob_ref, lse_ref, s_ref, p_ref):
    width = HEADS * HD
    segment, last = segments(lengths_ref, row)
    pad = (segment == last).astype(F32)
    line = lax.broadcasted_iota(jnp.int32, (EXTRA, SEQ), 0)
    aug_q = jnp.where(line == segment, 1.0, 0.0).astype(LOW)
    seen = (line == segment) & (segment != last)
    aug_k = jnp.where(seen | (line > last), 0.0, FAR).astype(LOW)
    aug_v = jnp.where(line == 0, 1.0, 0.0).astype(LOW)
    rest = jnp.zeros((PAIR - HD - EXTRA, SEQ), LOW)
    for head in range(HEADS):
        qa_ref[head, HD : HD + EXTRA] = aug_q
        ka_ref[head, HD : HD + EXTRA] = aug_k
        va_ref[head, HD : HD + EXTRA] = aug_v
        qa_ref[head, HD + EXTRA : PAIR] = rest
        ka_ref[head, HD + EXTRA : PAIR] = rest
    for block, ref in enumerate((qa_ref, ka_ref, va_ref)):
        lines = slice(block * width, (block + 1) * width)
        bias = bias_ref[lines]
        value = dot_nt(wt_ref[lines], x) + jnp.concatenate([bias] * (SEQ // 128), 1)
        if block == 0:
            value = value * HD**-0.5
        value = value.astype(LOW)
        for head in range(HEADS):
            ref[head, 0:HD] = value[head_rows(head)]
        yield

    def scores(head):
        for half in HALVES:
            s_ref[head % 2, half] = dot_tn(ka_ref[head, :, half], qa_ref[head, :, half])

    def softmax(head):
        tops = []
        for half in HALVES:
            tops.append(jnp.maximum(jnp.max(s_ref[head % 2, half], 0, keepdims=True), FLOOR))
            p_ref[head % 2, half] = jnp.exp(s_ref[head % 2, half] - tops[-1]).astype(LOW)
        return tops

    scores(0)
    yield
    for head in range(HEADS):
        if head + 1 < HEADS:
            scores(head + 1)
            yield
        tops = softmax(head)
        yield
        for half, top in zip(HALVES, tops):
            out = dot_nn(va_ref[head, :, half], p_ref[head % 2, half])
            alone = pad[:, half]
            total = out[HD : HD + 1] + alone
            lse_ref[head : head + 1, half] = jnp.where(alone > 0, 0.0, top + jnp.log(total))
            own = alone * va_ref[head, 0:HD, half].astype(F32)
            ob_ref[head_rows(head), half] = (out[0:HD] * inverse_of(total) + own).astype(LOW)
        yield


def normal(values):
    centred = values - jnp.mean(values, -1, keepdims=True)
    inverse = lax.rsqrt(jnp.mean(centred * centred, -1, keepdims=True) + EPSILON)
    return centred * inverse, inverse


def normal_back(cotangent, unit, inverse, gains):
    scaled = cotangent * gains
    return inverse * (
        scaled
        - jnp.mean(scaled, -1, keepdims=True)
        - unit * jnp.mean(scaled * unit, -1, keepdims=True)
    )


def dense_forward(x_ref, ob_ref, wo_ref, wi_ref, wf_ref, small_ref, bi_ref, n1_ref, n2_ref, inv_ref, yb_ref, gb_ref, gp_ref, z_ref, work_ref, u_ref):
    small = lambda index: small_ref[pl.ds(index, 1)]
    work_ref[...] = dot_tn(ob_ref[...], wo_ref[...])
    yield
    for place in pieces(SEQ):
        unit, inverse = normal(x_ref[place].astype(F32) + work_ref[place] + small(4))
        n1_ref[place] = unit
        inv_ref[place, pl.ds(0, HD)] = jnp.broadcast_to(inverse, (PIECE, HD))
        y = unit * small(2) + small(5)
        yb_ref[place] = y.astype(LOW)
        work_ref[place] = y + small(6)
        yield
    columns = 256
    count = wi_ref.shape[1] // columns

    def into(step):
        u_ref[step % 2] = dot_nn(yb_ref[...], wi_ref[:, pl.ds(step * columns, columns)])

    into(0)
    yield
    for step in range(count):
        if step + 1 < count:
            into(step + 1)
            yield
        lanes = pl.ds(step * columns, columns)
        for place in pieces(SEQ, SMALL):
            g, slope = gelu_parts(u_ref[step % 2, place] + bi_ref[:, lanes])
            gb_ref[place, lanes] = g.astype(LOW)
            gp_ref[place, lanes] = slope.astype(LOW)
            yield
    work_ref[...] += dot_nn(gb_ref[...], wf_ref[...])
    yield
    for place in pieces(SEQ):
        unit, inverse = normal(work_ref[place])
        n2_ref[place] = unit
        inv_ref[place, pl.ds(HD, HD)] = jnp.broadcast_to(inverse, (PIECE, HD))
        z_ref[place] = (unit * small(3) + small(7)).astype(z_ref.dtype)
        yield


def fold(values):
    return jnp.sum(values.reshape(-1, 8, values.shape[-1]), 0)


def dense_backward(dz_ref, n1_ref, n2_ref, inv_ref, yb_ref, gb_ref, gp_ref, ob_ref, wo_ref, wi_ref, wf_ref, small_ref, dr_ref, dob_ref, gwo_ref, gwi_ref, gwf_ref, gsmall_ref, gbi_ref, low_ref, u_ref, du_ref, turned_ref):
    small = lambda index: small_ref[pl.ds(index, 1)]
    for place in pieces(SEQ):
        dz = dz_ref[place].astype(F32)
        unit = n2_ref[place]
        gsmall_ref[3] += fold(dz * unit)
        gsmall_ref[7] += fold(dz)
        dr = normal_back(dz, unit, inv_ref[place, pl.ds(HD, 1)], small(3))
        dr_ref[place] = dr
        df = dr.astype(LOW)
        low_ref[place] = df
        gsmall_ref[6] += fold(df.astype(F32))
        yield
    columns = 256
    count = wi_ref.shape[1] // columns

    def back(step):
        u_ref[step % 2] = dot_nt(low_ref[...], wf_ref[pl.ds(step * columns, columns)])

    back(0)
    turned_ref[0, 0 : low_ref.shape[1]] = low_ref[...].T
    width = low_ref.shape[1]
    turned_ref[1, 0:width] = yb_ref[...].T
    turned_ref[1, width:] = jnp.ones((EXTRA, SEQ), LOW)
    yield
    for step in range(count):
        if step + 1 < count:
            back(step + 1)
            yield
        lanes = pl.ds(step * columns, columns)
        gwf_ref[:, lanes] += dot_nn(turned_ref[0, 0:width], gb_ref[:, lanes])
        yield
        for place in pieces(SEQ, SMALL):
            du = (u_ref[step % 2, place] * gp_ref[place, lanes].astype(F32)).astype(LOW)
            du_ref[place, lanes] = du
        yield
        product = dot_nn(turned_ref[1], du_ref[:, lanes])
        gwi_ref[:, lanes] += product[0:width]
        gbi_ref[:, lanes] += product[width : width + 8]
        yield
    u_ref[0] = dot_nt(du_ref[...], wi_ref[...])
    yield
    for place in pieces(SEQ):
        dy = dr_ref[place] + u_ref[0, place]
        unit = n1_ref[place]
        gsmall_ref[2] += fold(dy * unit)
        gsmall_ref[5] += fold(dy)
        dr = normal_back(dy, unit, inv_ref[place, pl.ds(0, 1)], small(2))
        dr_ref[place] = dr
        da = dr.astype(LOW)
        low_ref[place] = da
        gsmall_ref[4] += fold(da.astype(F32))
        yield
    gwo_ref[...] += dot_nn(ob_ref[...], low_ref[...])
    dob_ref[...] = dot_nt(wo_ref[...], low_ref[...]).astype(LOW)
    yield


def attention_backward(row, lengths_ref, x, do_ref, ob_ref, qa_ref, ka_ref, va_ref, lse_ref, dqkv_ref, gwq_ref, gbias_ref, p_ref, ds_ref, s_ref):
    width = HEADS * HD
    segment, last = segments(lengths_ref, row)
    pad = (segment == last).astype(F32)

    def scores(head):
        for half in HALVES:
            s_ref[0, head % 2, half] = dot_tn(ka_ref[head, :, half], qa_ref[head, :, half])
            s_ref[1, head % 2, half] = dot_tn(
                va_ref[head, 0:HD, half], do_ref[head_rows(head), half]
            )

    def weigh(head):
        product = do_ref[head_rows(head)].astype(F32) * ob_ref[head_rows(head)].astype(F32)
        centre = jnp.sum(product, 0, keepdims=True)
        for half in HALVES:
            p = jnp.exp(s_ref[0, head % 2, half] - lse_ref[head : head + 1, half])
            p_ref[head % 2, half] = p.astype(LOW)
            ds_ref[head % 2, half] = (p * (s_ref[1, head % 2, half] - centre[:, half])).astype(LOW)

    scores(0)
    yield
    for head in range(HEADS):
        if head + 1 < HEADS:
            scores(head + 1)
            yield
        weigh(head)
        yield
        for half in HALVES:
            ds, do = ds_ref[head % 2, half], do_ref[head_rows(head), half]
            dq = dot_nn(ka_ref[head, 0:HD, half], ds) * HD**-0.5
            dk = dot_nt(qa_ref[head, 0:HD, half], ds)
            dv = dot_nt(do, p_ref[head % 2, half]) + pad[:, half] * do.astype(F32)
            for block, value in enumerate((dq, dk, dv)):
                at = block * width + head * HD
                dqkv_ref[at : at + HD, half] = value.astype(LOW)
        yield
    for index, block in enumerate((0, 2)):
        value = dqkv_ref[block * width : (block + 1) * width].astype(F32)
        parts = [value[:, at : at + 128] for at in range(0, SEQ, 128)]
        gbias_ref[index] += (parts[0] + parts[1]) + (parts[2] + parts[3])
    gwq_ref[...] += dot_nn(dqkv_ref[...], x)
    yield


def unpack_matrix(raw_ref, at, into_ref):
    width = into_ref.shape[0]
    for start in range(0, into_ref.shape[1], width):
        block = raw_ref[:, :, pl.ds(at + start, width)].astype(F32)
        block = block.reshape(GROUPS + (width,)).swapaxes(0, 1).reshape(width, width)
        into_ref[:, pl.ds(start, width)] = block.astype(LOW)


def unpack_stacked(raw_ref, at, into_ref):
    width = into_ref.shape[1]
    count = into_ref.shape[0] // width
    blocks = [
        raw_ref[:, :, pl.ds(at + step * width, width)].astype(F32).reshape(GROUPS + (width,))
        for step in range(count)
    ]
    outer, inner, rows = GROUPS
    for place in range(inner):
        part = jnp.stack([jnp.stack([block[f, place] for block in blocks]) for f in range(outer)])
        size = outer * count * rows
        into_ref[pl.ds(place * size, size)] = part.reshape(size, width).astype(LOW)


def counter(shape, axis):
    return lax.broadcasted_iota(jnp.int32, shape, axis)


def split_by(values, size):
    return lax.shift_right_logical(values, size.bit_length() - 1), values & (size - 1)


def sources(rows):
    outer, inner, height = GROUPS
    group, within = split_by(counter((rows, 1), 0), height)
    far, near = split_by(group, inner)
    return near * outer + far, within


def unpack_vectors(raw_ref, at, layer):
    outer, inner, rows = GROUPS
    total = outer * inner * rows
    raw = raw_ref[:, :, pl.ds(at, 128)].reshape(total, 128)
    owner, place = split_by(counter((1, total), 1), rows)
    pick = jnp.where(counter((128, 1), 0) == rows * layer + place, 1.0, 0.0).astype(LOW)
    device, unused = sources(total)
    spread = jnp.where(owner == device, dot_nn(raw, pick), 0.0)
    return jnp.sum(spread.reshape(outer * inner, rows, total), 0)


def unpack_hidden(raw_ref, at, layer, hidden):
    outer, inner, rows = GROUPS
    total = outer * inner * rows
    raw = raw_ref[:, :, pl.ds(at, 128)].reshape(total, 128)
    owner, place = split_by(counter((1, hidden), 1), hidden // (outer * inner))
    pick = jnp.where(counter((128, 1), 0) == 2 * rows + place, 1.0, 0.0).astype(LOW)
    device, within = sources(total)
    device = jnp.where(within == layer, device, -1)
    spread = jnp.where(owner == device, dot_nn(raw, pick), 0.0)
    return jnp.sum(spread, 0, keepdims=True)


def pack_matrix(sum_ref, sent_ref, at, turned=False):
    width = sum_ref.shape[1 if turned else 0]
    outer, inner, rows = GROUPS
    for start in range(0, sum_ref.shape[0 if turned else 1], width):
        near = pl.ds(start, width)
        block = sum_ref[near].T if turned else sum_ref[:, near]
        block = block.reshape(inner, outer, rows, width)
        block = block.swapaxes(0, 1).reshape(outer, inner * rows, width)
        sent_ref[:, :, pl.ds(at + start, width)] = block.astype(LOW)


def pack_stacked(sum_ref, sent_ref, at):
    width = sum_ref.shape[0]
    outer, inner, rows = GROUPS
    count = sum_ref.shape[1] // width
    near = inner // count
    for step in range(count):
        block = sum_ref[:, pl.ds(step * width, width)].T
        block = block.reshape(near, outer, count, rows, width)
        for part in range(count):
            piece = jnp.stack([block[:, f, part] for f in range(outer)])
            piece = piece.reshape(outer, near * rows, width)
            sent_ref[:, pl.ds(step * near * rows, near * rows), pl.ds(at + part * width, width)] = (
                piece.astype(LOW)
            )


def pack_vectors(block, line, sent_ref, at):
    outer, inner, rows = GROUPS
    total = outer * inner * rows
    device, within = sources(total)
    owner, unused = split_by(counter((1, total), 1), rows)
    spread = jnp.broadcast_to(block[None], (outer * inner, rows, total)).reshape(total, total)
    spread = jnp.where(owner == device, spread, 0.0).astype(LOW)
    unused, place = split_by(counter((total, 1), 0), rows)
    found = dot_nn(spread, jnp.where(counter((1, 128), 1) == place, 1.0, 0.0).astype(LOW))
    if line is not None:
        hidden = line.shape[1]
        height = hidden // (outer * inner)
        owner, unused = split_by(counter((1, hidden), 1), height)
        spread = jnp.where(owner == jnp.where(within == 0, device, -1), line, 0.0).astype(LOW)
        unused, place = split_by(counter((hidden, 1), 0), height)
        pick = jnp.where(counter((1, 128), 1) == 2 * rows + place, 1.0, 0.0).astype(LOW)
        found = found + dot_nn(spread, pick)
    sent_ref[:, :, pl.ds(at, 128)] = found.reshape(outer, inner * rows, 128).astype(LOW)


def bias_rows(gbias_ref):
    width = gbias_ref.shape[1]
    parts = [jnp.sum(gbias_ref[index].T, 0, keepdims=True) for index in range(2)]
    return jnp.concatenate(parts + [jnp.zeros((6, width), F32)], 0)


def pack_dense(gwo_ref, gwi_ref, gwf_ref, gsmall_ref, gbi_ref, block, sent_ref, at):
    width, hidden = gwi_ref.shape
    pack_matrix(gwo_ref, sent_ref, at)
    pack_matrix(gwi_ref, sent_ref, at + width)
    pack_stacked(gwf_ref, sent_ref, at + width + hidden)
    block = jnp.sum(gsmall_ref[...], 1) + block
    pack_vectors(block, gbi_ref[0:1], sent_ref, at + width + 2 * hidden)


def shape_of(array):
    return jax.ShapeDtypeStruct(array.shape, array.dtype)


def by_row(shape, group):
    if len(shape) == 2:
        return pl.BlockSpec((group * SEQ, shape[1]), lambda step: (step, 0))
    return pl.BlockSpec((group,) + tuple(shape[1:]), lambda step: (step,) + (0,) * (len(shape) - 1))


def one_row(ref, member):
    if len(ref.shape) == 2:
        return ref.at[pl.ds(member * SEQ, SEQ)]
    return ref.at[member]


def alternate(runs):
    running = []
    waiting = list(runs)
    while running or waiting:
        if waiting:
            running.append(waiting.pop(0))
        for run in list(running):
            try:
                next(run)
            except StopIteration:
                running.remove(run)


def whole(shape):
    return pl.BlockSpec(tuple(shape), lambda row: (0,) * len(shape))


def run_rows(
    body, lengths, rowwise, fixed, row_outs, sent, shared, private, cost, setup, finish, after=(),
    scalars=(), group=1, moved=8
):
    count = lengths.shape[0]
    group = group if count % group == 0 else 1
    cuts = [len(scalars), len(rowwise), len(fixed), len(after), len(row_outs), len(sent)]
    cuts += [len(shared)] + [len(private)] * group

    def kernel(lengths_ref, *refs):
        step = pl.program_id(0)
        groups = []
        at = 0
        for cut in cuts:
            groups.append(refs[at : at + cut])
            at += cut
        numbers, rows_in, fixed_in, unused, rows_out, sent_out, work = groups[:7]

        @pl.when(step == 0)
        def _():
            setup(numbers, fixed_in, sent_out, work)

        alternate(
            body(
                step * group + member,
                lengths_ref,
                [one_row(ref, member) for ref in rows_in],
                [one_row(ref, member) for ref in rows_out],
                work,
                groups[7 + member],
            )
            for member in range(group)
        )

        if finish:

            @pl.when(step == count // group - 1)
            def _():
                finish(numbers, work, sent_out)

    return pl.pallas_call(
        kernel,
        grid=(count // group,),
        in_specs=[pl.BlockSpec(memory_space=pltpu.SMEM)] * (1 + len(scalars))
        + [by_row(array.shape, group) for array in rowwise]
        + [whole(array.shape) for array in fixed]
        + [pl.BlockSpec(memory_space=pl.ANY) for array in after],
        out_specs=[by_row(part.shape, group) for part in row_outs]
        + [whole(part.shape) for part in sent],
        out_shape=list(row_outs) + list(sent),
        scratch_shapes=list(shared) + list(private) * group,
        compiler_params=pltpu.CompilerParams(
            dimension_semantics=("arbitrary",), vmem_limit_bytes=MEMORY
        ),
        cost_estimate=pl.CostEstimate(
            flops=cost, bytes_accessed=moved * 2**20, transcendentals=0
        ),
    )(lengths, *scalars, *rowwise, *fixed, *after)


def struct(shape, dtype):
    return jax.ShapeDtypeStruct(tuple(shape), dtype)


FORWARD_SCRATCH = lambda: [
    pltpu.VMEM((2, SEQ, HALF), F32),
    pltpu.VMEM((2, SEQ, HALF), LOW),
]
BACKWARD_SCRATCH = lambda: [
    pltpu.VMEM((2, SEQ, HALF), LOW),
    pltpu.VMEM((2, SEQ, HALF), LOW),
    pltpu.VMEM((2, 2, SEQ, HALF), F32),
    pltpu.VMEM((3 * HEADS * HD, SEQ), LOW),
]


def attention_outs(rows, width):
    return [
        struct((rows, HEADS, PAIR, SEQ), LOW),
        struct((rows, HEADS, PAIR, SEQ), LOW),
        struct((rows, HEADS, HD + EXTRA, SEQ), LOW),
        struct((rows, width, SEQ), LOW),
        struct((rows, 8, SEQ), F32),
    ]


def dense_outs(tokens, width, hidden):
    return [
        struct((tokens, width), F32),
        struct((tokens, width), F32),
        struct((tokens, PAIR), F32),
        struct((tokens, width), LOW),
        struct((tokens, hidden), LOW),
        struct((tokens, hidden), LOW),
    ]


def vmem(shape, dtype):
    return pltpu.VMEM(tuple(shape), dtype)


def attention_weights(width):
    return [vmem((width, 3 * width), LOW), vmem((3 * width, width), LOW), vmem((3 * width, 128), F32)]


def dense_weights(width, hidden):
    return [
        vmem((width, width), LOW),
        vmem((width, hidden), LOW),
        vmem((hidden, width), LOW),
        vmem((8, width), F32),
        vmem((1, hidden), F32),
    ]


def dense_sums(width, hidden):
    return [
        vmem((width, width), F32),
        vmem((width, hidden), F32),
        vmem((width, hidden), F32),
        vmem((8, 8, width), F32),
        vmem((8, hidden), F32),
    ]


def attention_sums(width):
    return [vmem((3 * width, width), F32), vmem((2, width, 128), F32)]


def dense_work(width, hidden):
    return [
        vmem((SEQ, width), LOW),
        vmem((2, SEQ, width), F32),
        vmem((SEQ, hidden), LOW),
        vmem((2, width + EXTRA, SEQ), LOW),
    ]


def set_attention(layer, urgent_ref, raw_ref, at, wq_ref, wt_ref, bias_ref):
    width = wq_ref.shape[0]
    unpack_matrix(raw_ref, at, wq_ref)
    vectors = unpack_vectors(urgent_ref, 3 * width, layer)
    for block, line in enumerate((vectors[0:1], jnp.zeros((1, width), F32), vectors[1:2])):
        lines = pl.ds(block * width, width)
        wt_ref[lines] = wq_ref[:, lines].astype(F32).T.astype(LOW)
        bias_ref[lines] = jnp.broadcast_to(line, (128, width)).T


def set_dense(layer, urgent_ref, raw_ref, at, wo_ref, wi_ref, wf_ref, small_ref, bi_ref):
    width, hidden = wi_ref.shape
    unpack_matrix(raw_ref, at, wo_ref)
    unpack_matrix(raw_ref, at + width, wi_ref)
    unpack_stacked(raw_ref, at + width + hidden, wf_ref)
    small_ref[...] = unpack_vectors(urgent_ref, 3 * width, layer)
    bi_ref[...] = unpack_hidden(urgent_ref, 3 * width, layer, hidden)


def clear(refs):
    for ref in refs:
        ref[...] = jnp.zeros(ref.shape, ref.dtype)


def assemble(place_ref, part_refs, into_ref):
    for step, ref in enumerate(part_refs):
        into_ref[place_ref[0] ^ step] = ref[...]


def raw_block(parts):
    return vmem((len(parts),) + parts[0].shape, LOW)


def turned_back(lengths_ref, row, values):
    return pltpu.roll(values, longest_start(lengths_ref, row), 0).astype(LOW)


def rotate_kernel(lengths, arrays):
    def body(row, lengths_ref, rowwise, outs, work, own):
        back = (SEQ - longest_start(lengths_ref, row)) & (SEQ - 1)
        for source, target in zip(rowwise, outs):
            target[...] = pltpu.roll(source[...].astype(F32), back, 0).astype(LOW)
            yield

    return run_rows(
        body, lengths, list(arrays), [], [struct(array.shape, LOW) for array in arrays], [], [], [],
        10**6, lambda *refs: None, None,
    )


def first_kernel(lengths, x, place, parts):
    rows, (tokens, width) = lengths.shape[0], x.shape

    def setup(numbers, fixed, sent, work):
        assemble(numbers[0], fixed, sent[0])
        set_attention(0, sent[0], sent[0], 0, *work)

    def body(row, lengths_ref, rowwise, outs, work, own):
        return attention_forward(row, lengths_ref, rowwise[0][...], *work[1:3], *outs, *own)

    return run_rows(
        body, lengths, [x], list(parts), attention_outs(rows, width),
        [struct((len(parts),) + parts[0].shape, LOW)],
        attention_weights(width), FORWARD_SCRATCH(), 4 * 10**9, setup, None, (), [place],
    )


def attention_kernel(layer, lengths, x, place, urgent, parts, at):
    rows, (tokens, width) = lengths.shape[0], x.shape

    def setup(numbers, fixed, sent, work):
        assemble(numbers[0], fixed[1:], work[3])
        set_attention(layer, fixed[0], work[3], at, *work[:3])

    def body(row, lengths_ref, rowwise, outs, work, own):
        return attention_forward(
            row, lengths_ref, rowwise[0][...].astype(LOW), *work[1:3], *outs, *own
        )

    return run_rows(
        body, lengths, [x], [urgent] + list(parts), attention_outs(rows, width), [],
        attention_weights(width) + [raw_block(parts)], FORWARD_SCRATCH(),
        4 * 10**9, setup, None, (), [place],
    )


def dense_kernel(layer, lengths, x, ob, place, urgent, parts, at, hidden):
    tokens, width = x.shape

    def setup(numbers, fixed, sent, work):
        assemble(numbers[0], fixed[1:], work[5])
        set_dense(layer, fixed[0], work[5], at, *work[:5])

    def body(row, lengths_ref, rowwise, outs, work, own):
        return dense_forward(*rowwise, *work[:5], *outs, *own)

    return run_rows(
        body, lengths, [x, ob], [urgent] + list(parts),
        dense_outs(tokens, width, hidden) + [struct((tokens, width), F32)], [],
        dense_weights(width, hidden) + [raw_block(parts)],
        [vmem((SEQ, width), F32), vmem((2, SEQ, width), F32)],
        5 * 10**9, setup, None, (), [place],
    )


def turn_kernel(layer, lengths, x, ob, cotangent, place, urgent, parts, at, hidden):
    tokens, width = x.shape
    columns = width + 2 * hidden + 128

    def setup(numbers, fixed, sent, work):
        assemble(numbers[0], fixed[1:], work[11])
        set_dense(layer, fixed[0], work[11], at, *work[:5])
        clear(work[5:10])

    def body(row, lengths_ref, rowwise, outs, work, own):
        x_ref, ob_ref, dz_ref = rowwise
        z_ref, dr_ref, dob_ref = outs
        weights, sums = work[:5], work[5:10]
        kept, work_ref, back = own[:6], own[6], own[7:]
        yield from dense_forward(x_ref, ob_ref, *weights, *kept, z_ref, work_ref, back[1])
        yield from dense_backward(dz_ref, *kept, ob_ref, *weights[:4], dr_ref, dob_ref, *sums, *back)

    def finish(numbers, work, sent):
        pack_dense(*work[5:10], 0.0, work[10], 0)
        hand_out(numbers[0], work[10], sent)

    kept = [vmem((SEQ,) + part.shape[1:], part.dtype) for part in dense_outs(tokens, width, hidden)]
    return run_rows(
        body, lengths, [x, ob, cotangent], [urgent] + list(parts),
        [struct((tokens, width), LOW), struct((tokens, width), F32), struct((tokens // SEQ, width, SEQ), LOW)],
        [struct((64, columns), LOW)] * 4,
        dense_weights(width, hidden) + dense_sums(width, hidden)
        + [vmem((4, 64, columns), LOW), raw_block(parts)],
        kept + [vmem((SEQ, width), F32)] + dense_work(width, hidden),
        10**10, setup, finish, (), [place], 2,
    )


def hand_out(place_ref, packed_ref, sent):
    for step, ref in enumerate(sent):
        ref[...] = packed_ref[place_ref[0] ^ step]


def middle_kernel(lengths, upper, lower, place, urgent, parts, hidden, after):
    tokens, width = upper[0].shape
    columns = 4 * width + 2 * hidden + 128

    def setup(numbers, fixed, sent, work):
        assemble(numbers[0], fixed[1:], work[16])
        set_attention(1, fixed[0], work[16], 0, *work[:3])
        set_dense(0, fixed[0], work[16], 3 * width, *work[3:8])
        clear(work[8:15])

    def body(row, lengths_ref, rowwise, outs, work, own):
        up, low = rowwise[:8], rowwise[8:]
        dx_ref = own[0]
        yield from attention_backward(
            row, lengths_ref, up[0][...].astype(LOW), *up[1:7], own[-1], *work[8:10], *own[5:-1]
        )
        dx_ref[...] = up[7][...] + dot_tn(own[-1][...], work[1][...])
        yield
        yield from dense_backward(dx_ref, *low, *work[3:7], *outs, *work[10:15], *own[1:5])

    def finish(numbers, work, sent):
        pack_matrix(work[8], work[15], 0, True)
        pack_dense(*work[10:15], bias_rows(work[9]), work[15], 3 * width)
        hand_out(numbers[0], work[15], sent)

    return run_rows(
        body, lengths, list(upper) + list(lower), [urgent] + list(parts),
        [struct((tokens, width), F32), struct((tokens // SEQ, width, SEQ), LOW)],
        [struct((64, columns), LOW)] * 4,
        attention_weights(width) + dense_weights(width, hidden)
        + attention_sums(width) + dense_sums(width, hidden)
        + [vmem((4, 64, columns), LOW), raw_block(parts)],
        [vmem((SEQ, width), F32)] + dense_work(width, hidden) + BACKWARD_SCRATCH(),
        15 * 10**9, setup, finish, after, [place], 2,
    )


def last_kernel(lengths, upper, after, place):
    tokens, width = upper[0].shape

    def setup(numbers, fixed, sent, work):
        clear(work[:2])

    def body(row, lengths_ref, rowwise, outs, work, own):
        return attention_backward(
            row, lengths_ref, rowwise[0][...], *rowwise[1:], outs[0], *work[:2], *own
        )

    def finish(numbers, work, sent):
        pack_matrix(work[0], work[2], 0, True)
        pack_vectors(bias_rows(work[1]), None, work[2], 3 * width)
        hand_out(numbers[0], work[2], sent)

    return run_rows(
        body, lengths, list(upper), [], [struct((tokens // SEQ, 3 * width, SEQ), LOW)],
        [struct((64, 3 * width + 128), LOW)] * 4,
        attention_sums(width) + [vmem((4, 64, 3 * width + 128), LOW)],
        BACKWARD_SCRATCH()[:-1], 8 * 10**9, setup, finish, after, [place], 2,
    )


def outward_kernel(lengths, z, after):
    def body(row, lengths_ref, rowwise, outs, work, own):
        outs[0][...] = turned_back(lengths_ref, row, rowwise[0][...].astype(F32))
        yield

    (found,) = run_rows(
        body, lengths, [z], [], [struct(z.shape, LOW)], [], [], [], 3 * 10**9,
        lambda *refs: None, None, after,
    )
    return found


def inward_kernel(lengths, dqkv, dr, urgent, after):
    tokens, width = dr.shape

    def setup(numbers, fixed, sent, work):
        set_attention(0, fixed[0], fixed[0], 0, *work)

    def body(row, lengths_ref, rowwise, outs, work, own):
        dqkv_ref, dr_ref = rowwise
        dx = dr_ref[...] + dot_tn(dqkv_ref[...], work[1][...])
        outs[0][...] = turned_back(lengths_ref, row, dx)
        yield

    (found,) = run_rows(
        body, lengths, [dqkv, dr], [urgent], [struct((tokens, width), LOW)], [],
        attention_weights(width), [], 10**9, setup, None, after, moved=6,
    )
    return found


def hold(array, after):
    def kernel(*refs):
        pass

    anywhere = pl.BlockSpec(memory_space=pl.ANY)
    return pl.pallas_call(
        kernel,
        in_specs=[anywhere] * (1 + len(after)),
        out_specs=anywhere,
        out_shape=shape_of(array),
        input_output_aliases={0: 0},
    )(array, *after)


def pack_parameters(
    attn_weight, attn_bias, out_weight, ffn_in, ffn_in_bias, ffn_out, norm_gain, shifts
):
    depth, rows, width = out_weight.shape
    copies = GROUPS[1]
    hidden = ffn_in.shape[2]
    dense = width + 2 * hidden
    height = ffn_in_bias.shape[1]

    def kernel(wq_ref, ab_ref, wo_ref, wi_ref, bi_ref, wf_ref, gain_ref, shift_ref, first_ref, rest_ref, small_ref):
        def put(ref, block, at):
            block = jnp.broadcast_to(block.astype(F32)[None], (copies,) + block.shape)
            block = block.reshape(copies * block.shape[1], block.shape[2])
            ref[:, pl.ds(at, block.shape[1])] = block.astype(LOW)

        small_ref[...] = jnp.zeros(small_ref.shape, F32)
        for layer in range(depth):
            lanes = pl.ds(rows * layer, rows)
            small_ref[0:2, lanes] = ab_ref[layer].astype(F32)
            small_ref[2:4, lanes] = gain_ref[layer].astype(F32)
            small_ref[4:8, lanes] = shift_ref[layer].astype(F32)
        small_ref[0:depth, pl.ds(2 * rows, height)] = bi_ref[...].astype(F32)
        put(first_ref, wq_ref[0], 0)
        put(first_ref, small_ref[...], 3 * width)
        put(first_ref, wq_ref[1], 3 * width + 128)
        for layer, ref, at in ((0, first_ref, 6 * width + 128), (1, rest_ref, 0)):
            put(ref, wo_ref[layer], at)
            put(ref, wi_ref[layer], at + width)
            at += width + hidden
            down = wf_ref[layer].astype(F32)
            for step in range(hidden // width):
                put(ref, down[step * rows : (step + 1) * rows], at)
                at += width

    return pl.pallas_call(
        kernel,
        in_specs=[pl.BlockSpec(memory_space=pltpu.VMEM)] * 8,
        out_shape=[
            struct((copies * rows, 6 * width + 128 + dense), LOW),
            struct((copies * rows, dense), LOW),
        ],
        scratch_shapes=[vmem((rows, 128), F32)],
        compiler_params=pltpu.CompilerParams(vmem_limit_bytes=MEMORY),
    )(attn_weight, attn_bias, out_weight, ffn_in, ffn_in_bias, ffn_out, norm_gain, shifts)


def add_parts(place, parts, halves, after=()):
    lanes = parts[0].shape[1]
    count = len(parts)
    many, rows = GROUPS[1:]
    outs = 2 if halves else 1

    def kernel(place_ref, *refs):
        out_refs, sum_ref = refs[count + len(after) : -1], refs[-1]
        bit = place_ref[0] & 1
        for start in range(0, lanes, 128):
            near = pl.ds(start, 128)
            total = refs[0][:, near].astype(F32)
            for ref in refs[1:count]:
                total = total + ref[:, near].astype(F32)
            if halves:
                sum_ref[:, :, near] = total.reshape(many, rows, 128)
            else:
                out_refs[0][:, near] = total.astype(LOW)
        for side, ref in enumerate(out_refs if halves else ()):
            for start in range(0, lanes, 128):
                near = pl.ds(start, 128)
                block = [sum_ref[2 * step + (bit ^ side), :, near] for step in range(many // 2)]
                ref[:, near] = jnp.concatenate(block, 0).astype(LOW)

    return pl.pallas_call(
        kernel,
        in_specs=[pl.BlockSpec(memory_space=pltpu.SMEM)]
        + [pl.BlockSpec(memory_space=pltpu.VMEM)] * count
        + [pl.BlockSpec(memory_space=pl.ANY)] * len(after),
        out_shape=[struct((many * rows // outs, lanes), LOW)] * outs,
        scratch_shapes=[vmem((many, rows, lanes), F32)],
        compiler_params=pltpu.CompilerParams(vmem_limit_bytes=MEMORY),
    )(place, *parts, *after)


def add_halves(place, pairs, after=()):
    many, rows = GROUPS[1] // 2, GROUPS[2]
    widths = [pair[0].shape[1] for pair in pairs]
    lanes = sum(widths)

    def kernel(place_ref, *refs):
        out_refs, sum_ref = refs[2 * len(pairs) + len(after) : -1], refs[-1]
        at = 0
        for index, size in enumerate(widths):
            for start in range(0, size, 128):
                near = pl.ds(start, 128)
                total = refs[2 * index][:, near].astype(F32) + refs[2 * index + 1][:, near].astype(F32)
                sum_ref[:, :, pl.ds(at + start, 128)] = total.reshape(many, rows, 128)
            at += size
        far = lax.shift_right_logical(place_ref[0], 1)
        for step, ref in enumerate(out_refs):
            ref[...] = sum_ref[far ^ step].astype(LOW)

    return pl.pallas_call(
        kernel,
        in_specs=[pl.BlockSpec(memory_space=pltpu.SMEM)]
        + [pl.BlockSpec(memory_space=pltpu.VMEM)] * (2 * len(pairs))
        + [pl.BlockSpec(memory_space=pl.ANY)] * len(after),
        out_shape=[struct((rows, lanes), LOW)] * many,
        scratch_shapes=[vmem((many, rows, lanes), F32)],
        compiler_params=pltpu.CompilerParams(vmem_limit_bytes=MEMORY),
    )(place, *(part for pair in pairs for part in pair), *after)


def write_gradients(found, depth, width, hidden, after):
    rows = GROUPS[2]
    height = hidden // DEVICES
    dense = width + 2 * hidden

    def kernel(*refs):
        found_refs, refs = refs[: len(found)], refs[len(found) + len(after) :]
        gwq_ref, gab_ref, gwo_ref, gwi_ref, gbi_ref, gwf_ref, gain_ref, shift_ref = refs

        def total(at, columns):
            value = found_refs[0][:, pl.ds(at, columns)].astype(F32)
            for ref in found_refs[1:]:
                value = value + ref[:, pl.ds(at, columns)].astype(F32)
            return value

        first, second = dense + 128, 2 * dense + 3 * width + 256
        blocks = [total(at, 128) for at in (dense, first + 3 * width + dense, second + 3 * width)]
        for layer, at, block in ((0, second, blocks[2]), (1, first, blocks[1])):
            gwq_ref[layer] = total(at, 3 * width)
            gab_ref[layer] = block[0:2, 0:rows]
        for layer, at, block in ((0, first + 3 * width, blocks[1]), (1, 0, blocks[0])):
            gwo_ref[layer] = total(at, width)
            gwi_ref[layer] = total(at + width, hidden)
            for step in range(hidden // width):
                gwf_ref[layer, pl.ds(step * rows, rows)] = total(
                    at + width + hidden + step * width, width
                )
            gain_ref[layer] = block[2:4, 0:rows]
            shift_ref[layer] = block[4:8, 0:rows]
            gbi_ref[pl.ds(layer, 1)] = pltpu.roll(block, 128 - 2 * rows, 1)[0:1, 0:height]

    outs = [
        struct((depth, rows, 3 * width), F32),
        struct((depth, 2, rows), F32),
        struct((depth, rows, width), F32),
        struct((depth, rows, hidden), F32),
        struct((depth, height), F32),
        struct((depth, height, width), F32),
        struct((depth, 2, rows), F32),
        struct((depth, 4, rows), F32),
    ]
    return pl.pallas_call(
        kernel,
        in_specs=[pl.BlockSpec(memory_space=pltpu.VMEM)] * len(found)
        + [pl.BlockSpec(memory_space=pl.ANY)] * len(after),
        out_shape=outs,
        compiler_params=pltpu.CompilerParams(vmem_limit_bytes=MEMORY),
    )(*found, *after)


def exchange(parts, axis):
    return lax.all_to_all(parts, axis, 0, 0, tiled=True)


def swap(part, axis, step):
    size = lax.axis_size(axis)
    return lax.ppermute(part, axis, [(source, source ^ step) for source in range(size)])


def local(
    hidden_in,
    lengths,
    grad_out,
    attn_weight,
    attn_bias,
    out_weight,
    ffn_in,
    ffn_in_bias,
    ffn_out,
    norm_gain,
    shifts,
):
    depth, rows, width = out_weight.shape
    hidden = ffn_in.shape[2]
    first, second = lax.axis_size("dp"), lax.axis_size("fsdp")
    fits = (second, first, rows) == GROUPS
    urgent_size = 3 * width + 128
    if fits:
        early, later = pack_parameters(
            attn_weight, attn_bias, out_weight, ffn_in, ffn_in_bias, ffn_out, norm_gain, shifts
        )
        across = lax.axis_index("dp").astype(jnp.int32).reshape(1)
        place = lax.axis_index("fsdp").astype(jnp.int32).reshape(1)
        partners = range(1, second)
        x0, dz1 = rotate_kernel(lengths, (hidden_in, grad_out))
        early = hold(exchange(early, "dp"), (x0,))
        urgent = early[:, :urgent_size]
        urgent = [urgent] + [swap(urgent, "fsdp", step) for step in partners]
        raw0 = early[:, urgent_size:]
        raw0 = [raw0, swap(raw0, "fsdp", 1), swap(raw0, "fsdp", 2)]
    else:
        urgent, raw0, raw1 = gather_other(
            attn_weight, attn_bias, out_weight, ffn_in, ffn_in_bias, ffn_out, norm_gain, shifts
        )
        urgent, raw0, raw1 = ([part[step] for step in range(4)] for part in (urgent, raw0, raw1))
        place = jnp.zeros((1,), jnp.int32)
        x0, dz1 = rotate_kernel(lengths, (hidden_in, grad_out))

    qa0, ka0, va0, ob0, lse0, urgent = first_kernel(lengths, x0, place, urgent)
    if fits:
        raw0[2] = hold(raw0[2], (ob0,))
        raw0.append(swap(raw0[2], "fsdp", 1))
        later = exchange(hold(later, (ob0,)), "dp")
    n1, n2, inv, yb, gb, gp, z0 = dense_kernel(
        0, lengths, x0, ob0, place, urgent, raw0, 3 * width, hidden
    )
    if fits:
        raw1 = hold(later, (z0,))
        raw1 = [raw1, swap(raw1, "fsdp", 1), swap(raw1, "fsdp", 2)]
    qa1, ka1, va1, ob1, lse1 = attention_kernel(1, lengths, z0, place, urgent, raw0, 0)
    if fits:
        raw1[2] = hold(raw1[2], (ob1,))
        raw1.append(swap(raw1[2], "fsdp", 1))
    z1, dr1, dob1, *sent_a = turn_kernel(
        1, lengths, z0, ob1, dz1, place, urgent, raw1, 0, hidden
    )
    dr0, dob0, *sent_b = middle_kernel(
        lengths,
        (z0, dob1, ob1, qa1, ka1, va1, lse1, dr1),
        (n1, n2, inv, yb, gb, gp, ob0),
        place,
        urgent,
        raw0,
        hidden,
        (sent_a[0],),
    )
    if fits:
        got_a = [sent_a[0]] + [swap(sent_a[step], "fsdp", step) for step in partners]
        keep_a, give_a = add_parts(across, got_a, True, (sent_b[0],))
        got_ax = swap(give_a, "dp", 1)
        ready = (sent_b[0], keep_a)
    else:
        ready = ()
    dqkv, *sent_c = last_kernel(
        lengths, (x0, dob0, ob0, qa0, ka0, va0, lse0), ready, place
    )
    if fits:
        got_b = [sent_b[0]] + [swap(sent_b[step], "fsdp", step) for step in partners]
        got_c = [sent_c[0]] + [swap(sent_c[step], "fsdp", step) for step in partners]
        keep_b, give_b = add_parts(across, got_b, True, (got_ax, dqkv))
        keep_c, give_c = add_parts(across, got_c, True, (keep_b,))
        grad_in = inward_kernel(lengths, dqkv, dr0, urgent, (keep_c,))
        pairs = [(keep_a, got_ax), (keep_b, swap(give_b, "dp", 1)), (keep_c, swap(give_c, "dp", 1))]
        found = add_halves(across, pairs, (grad_in,))
        hidden_out = outward_kernel(lengths, z1, (found[0],))
        found = [found[0]] + [swap(found[step], "dp", 2 * step) for step in range(1, first // 2)]
        grads = write_gradients(found, depth, width, hidden, (hidden_out,))
    else:
        grad_in = inward_kernel(lengths, dqkv, dr0, urgent, ())
        hidden_out = outward_kernel(lengths, z1, ())
        grads = scatter_other(
            *(jnp.stack(part) for part in (sent_a, sent_b, sent_c)), rows, width, hidden
        )
    return (hidden_out, grad_in, *grads)


def gather_other(
    attn_weight, attn_bias, out_weight, ffn_in, ffn_in_bias, ffn_out, norm_gain, shifts
):
    axes = ("dp", "fsdp")
    gather = lambda part, axis: lax.all_gather(part, axes, axis=axis, tiled=True)
    depth, unused, width = out_weight.shape
    hidden = ffn_in.shape[2]
    outer, inner, rows = GROUPS
    vectors = gather(jnp.concatenate([attn_bias, norm_gain, shifts], 1), 2)
    line = gather(ffn_in_bias, 1)

    def order(natural):
        return (
            natural.reshape(inner, outer, rows, -1).swapaxes(0, 1).reshape(outer, inner * rows, -1)
        )

    def stacked(part):
        part = part.reshape(DEVICES, -1, rows, width)
        return order(part.swapaxes(1, 2).reshape(width, -1))

    small = vectors.reshape(depth, 8, DEVICES, rows).transpose(2, 1, 0, 3).reshape(width, -1)
    line = line.reshape(depth, DEVICES, -1).swapaxes(0, 1)
    line = jnp.pad(line, ((0, 0), (0, 8 - depth), (0, 0))).reshape(width, -1)
    small = jnp.concatenate([small, line], 1)
    small = jnp.pad(small, ((0, 0), (0, 128 - small.shape[1])))
    wq, wo, wi, wf = (gather(part, 1) for part in (attn_weight, out_weight, ffn_in, ffn_out))
    urgent = jnp.concatenate([order(wq[0]), order(small)], 2)
    raw0 = jnp.concatenate([order(wq[1]), order(wo[0]), order(wi[0]), stacked(wf[0])], 2)
    raw1 = jnp.concatenate([order(wo[1]), order(wi[1]), stacked(wf[1])], 2)
    return urgent, raw0, raw1


def scatter_other(sent_a, sent_b, sent_c, own_rows, width, hidden):
    outer, inner, rows = GROUPS
    axes = ("dp", "fsdp")

    def natural(part):
        return part.reshape(outer, inner, rows, -1).swapaxes(0, 1).reshape(width, -1).astype(F32)

    def cut(part, sizes):
        found, at = [], 0
        for size in sizes:
            found.append(part[:, at : at + size])
            at += size
        return found

    dense = [width, hidden, hidden, 128]
    wq0, block_c = cut(natural(sent_c), [3 * width, 128])
    wq1, wo0, wi0, wf0, block_b = cut(natural(sent_b), [3 * width] + dense)
    wo1, wi1, wf1, block_a = cut(natural(sent_a), dense)

    def vectors(block):
        block = block.reshape(DEVICES, rows, 128)
        return block[:, :, :rows].swapaxes(0, 1).reshape(rows, width)

    def line(block):
        block = block.reshape(DEVICES, rows, 128)
        return block[:, 0, 2 * rows : 2 * rows + hidden // DEVICES].reshape(-1)

    def stacked(part):
        part = part.reshape(DEVICES, rows, -1, width).swapaxes(1, 2)
        return part.reshape(hidden, width)

    def spread(parts, axis):
        return lax.psum_scatter(jnp.stack(parts), axes, scatter_dimension=axis, tiled=True)

    return (
        spread([wq0, wq1], 1),
        spread([vectors(block_c)[0:2], vectors(block_b)[0:2]], 2),
        spread([wo0, wo1], 1),
        spread([wi0, wi1], 1),
        spread([line(block_b), line(block_a)], 1),
        spread([stacked(wf0), stacked(wf1)], 1),
        spread([vectors(block_b)[2:4], vectors(block_a)[2:4]], 2),
        spread([vectors(block_b)[4:8], vectors(block_a)[4:8]], 2),
    )


def solution(mesh):
    placed = (
        P(("dp", "fsdp"), None),
        P(("dp", "fsdp"), None),
        P(("dp", "fsdp"), None),
        P(None, ("dp", "fsdp"), None),
        P(None, None, ("dp", "fsdp")),
        P(None, ("dp", "fsdp"), None),
        P(None, ("dp", "fsdp"), None),
        P(None, ("dp", "fsdp")),
        P(None, ("dp", "fsdp"), None),
        P(None, None, ("dp", "fsdp")),
        P(None, None, ("dp", "fsdp")),
    )
    return jax.shard_map(
        local,
        mesh=mesh,
        in_specs=placed,
        out_specs=(
            P(("dp", "fsdp"), None),
            P(("dp", "fsdp"), None),
            P(None, ("dp", "fsdp"), None),
            P(None, None, ("dp", "fsdp")),
            P(None, ("dp", "fsdp"), None),
            P(None, ("dp", "fsdp"), None),
            P(None, ("dp", "fsdp")),
            P(None, ("dp", "fsdp"), None),
            P(None, None, ("dp", "fsdp")),
            P(None, None, ("dp", "fsdp")),
        ),
        check_vma=False,
    )
```
